32 devices in a mesh: section: 4 (over y, x), batch: 8 (over z, core).
Axes of the slice: x: 2, y: 2, z: 4, core: 2. Of those that a mesh axis runs over, the one named last changes fastest.
Arguments:
- latents: bfloat16 [8192, 1024], P('batch'), may hold values from -400 to 400
- points: bfloat16 [4096, 1024], P('batch'), may hold values from -6 to 6
- neighbours: int32 [32, 256], P('batch'), may hold values from 0 to 511
- lengths: int32 [32], P('batch'), may hold values from 64 to 256, as said below
- cross_proj: bfloat16 [1024, 3, 1024], P('batch'), may hold values from -0.1875 to 0.1875
- cross_out: bfloat16 [1024, 1024], P('batch'), may hold values from -0.75 to 0.75
- cross_gains: bfloat16 [2, 1024], P(None, 'batch'), may hold values from 0.099609375 to 1.8984375
- self_proj: bfloat16 [1024, 3, 1024], P('batch'), may hold values from -0.1875 to 0.1875
- self_out: bfloat16 [1024, 1024], P('batch'), may hold values from -0.75 to 0.75
- self_gain: bfloat16 [1024], P('batch'), may hold values from 0.099609375 to 1.8984375
- mlp_gain: bfloat16 [2, 1024], P(None, 'batch'), may hold values from 0.099609375 to 1.8984375
- mlp_in: bfloat16 [2, 1024, 4096], P(None, 'batch'), may hold values from -0.1875 to 0.1875
- mlp_in_bias: bfloat16 [2, 4096], P(None, 'batch'), may hold values from -3 to 3
- mlp_down: bfloat16 [2, 1024, 4096], P(None, 'batch'), may hold values from -0.1875 to 0.1875
- mlp_out_bias: bfloat16 [2, 1024], P(None, 'batch'), may hold values from -2 to 2
- cotangent: bfloat16 [8192, 1024], P('batch'), may hold values from -6 to 6
Outputs:
- latents_out: bfloat16 [8192, 1024], P('batch')
- latents_grad: float32 [8192, 1024], P('batch')
- points_grad: float32 [4096, 1024], P('batch')
- cross_proj_grad: float32 [1024, 3, 1024], P('batch')
- cross_out_grad: float32 [1024, 1024], P('batch')
- cross_gains_grad: float32 [2, 1024], P(None, 'batch')
- self_proj_grad: float32 [1024, 3, 1024], P('batch')
- self_out_grad: float32 [1024, 1024], P('batch')
- self_gain_grad: float32 [1024], P('batch')
- mlp_gain_grad: float32 [2, 1024], P(None, 'batch')
- mlp_in_grad: float32 [2, 1024, 4096], P(None, 'batch')
- mlp_in_bias_grad: float32 [2, 4096], P(None, 'batch')
- mlp_down_grad: float32 [2, 1024, 4096], P(None, 'batch')
- mlp_out_bias_grad: float32 [2, 1024], P(None, 'batch')
- norm_mean: float32 [], replicated
The draws below stay inside these ranges and needn't reach their ends.
Inputs may be any that keep to these rules, and one draw needn't show every extreme that they name: Entry neighbours[g, j] names one of the 512 point rows of the block of 4 consecutive groups that holds g; entries may repeat. `lengths`: the value 256 occurs in every draw.
All inputs are finite; a program needn't handle non-finite values.
Results may differ from the reference program's by a relative error of at most 0.02.
Values may be sent and summed in bfloat16 or wider, within the bound.
A program may use at most 832 MiB of HBM per device.

```python
import math
import jax
import jax.numpy as jnp
from jax import lax

D = 1024
FF = 4096
HD = 128
LAT = 256
NEIGH = 256
PTS_DEV = 512
GROUPS = 32
TOKENS = 8192
POINTS = 4096
N_BATCH = 8


def draw_latents(key, part):
    key = jax.random.fold_in(key, 7)
    key_base, key_rows, key_cols = jax.random.split(key, 3)
    row_ids = (jnp.arange(TOKENS) // LAT).astype(jnp.float32) / max(GROUPS - 1, 1)
    row_scale = jnp.exp(jax.random.uniform(key_rows, (TOKENS,), jnp.float32, math.log(0.4), math.log(4.0)))
    col_scale = jnp.exp(jax.random.uniform(key_cols, (D,), jnp.float32, math.log(0.5), math.log(1.6)))
    ramp_up = 3.0 ** row_ids
    base_vals = jax.random.normal(key_base, (TOKENS, D), jnp.float32)
    values = base_vals * row_scale[:, None] * col_scale[None, :] * ramp_up[:, None]
    return values.astype(jnp.bfloat16)


def draw_lengths(key, part):
    key = jax.random.fold_in(key, 5)
    key_counts, key_spot = jax.random.split(key, 2)
    counts = jax.random.randint(key_counts, (GROUPS,), NEIGH // 4, NEIGH + 1)
    spot_at = jax.random.randint(key_spot, (), 0, GROUPS)
    counts = counts.at[spot_at].set(NEIGH)
    counts = counts.at[(spot_at + 1) % GROUPS].set(NEIGH // 4)
    return counts.astype(jnp.int32)


def with_ends(array, own_key, low, high):
    index_at = [jax.random.randint(jax.random.fold_in(own_key, axis), (), 0, length) for axis, length in enumerate(array.shape)]
    widest = array.shape.index(max(array.shape))
    neighbour = index_at[:widest] + [(index_at[widest] + 1) % array.shape[widest]] + index_at[widest + 1:]
    return array.at[tuple(index_at)].set(low).at[tuple(neighbour)].set(high)


def spiked(drawn, own_key, source, target, blocks, factor):
    owner, partner = [(jnp.arange(drawn.shape[axis_at]) // (drawn.shape[axis_at] // blocks)).reshape([-1 if axis == axis_at else 1 for axis in range(drawn.ndim)]) for axis_at in (source, target)]
    chosen = jax.random.permutation(own_key, blocks)[partner]
    strong = (owner == chosen) | (owner == (partner + blocks // 2) % blocks)
    return jnp.where(strong, factor * drawn, drawn)


def block_scale(key, dims, cuts, least, top_value):
    gain, own = 1.0, jax.random.fold_in(key, 6)
    for dim, parts in cuts:
        heights = jnp.exp(jax.random.uniform(jax.random.fold_in(own, dim), (parts,), jnp.float32, least / len(cuts), top_value / len(cuts)))
        gain = gain * jnp.repeat(heights, dims[dim] // parts).reshape([-1 if axis == dim else 1 for axis in range(len(dims))])
    return gain


def bell_draw(own_key, shape, scale, bound, cuts=(), kind=jnp.bfloat16):
    entries = scale * jax.random.normal(own_key, shape, jnp.float32)
    if cuts:
        entries = entries * block_scale(own_key, shape, cuts, -0.22, 0.18)
    return jnp.clip(entries, -bound, bound).astype(kind)


def noise_with(key, shape, scale, reach, shards, heavy, held_as=jnp.bfloat16):
    array = scale * jax.random.normal(key, shape, jnp.float32)
    if shards:
        array = array * block_scale(key, shape, shards, -0.22, 0.18)
    return jnp.clip(spiked(array, jax.random.fold_in(key, 3), *heavy), -reach, reach).astype(held_as)


def setup_inputs(seed: int = 0) -> dict:
    streams_of = jax.random.split(jax.random.key(seed), 17)
    latents = draw_latents(jax.random.fold_in(streams_of[16], 71), 0)
    points = bell_draw(streams_of[1], (POINTS, D), 1.0, 6.0, ((0, 8),))
    neighbours = with_ends(jax.random.randint(streams_of[2], (GROUPS, NEIGH), 0, PTS_DEV), jax.random.fold_in(streams_of[2], 1), 0, PTS_DEV - 1).astype(jnp.int32)
    lengths = draw_lengths(jax.random.fold_in(streams_of[16], 71), 0)
    cross_proj = bell_draw(streams_of[4], (D, 3, D), D ** -0.5, 0.1875, ((0, 8),))
    cross_out = bell_draw(streams_of[5], (D, D), (D // 16) ** -0.5, 0.75, ((0, 8),))
    cross_gains = jnp.clip(1.0 + 0.18 * jax.random.normal(streams_of[6], (2, D), jnp.float32), 0.099609375, 1.8984375).astype(jnp.bfloat16)
    self_proj = bell_draw(streams_of[7], (D, 3, D), D ** -0.5, 0.1875, ((0, 8),))
    self_out = bell_draw(streams_of[8], (D, D), (D // 16) ** -0.5, 0.75, ((0, 8),))
    self_gain = jnp.clip(1.0 + 0.18 * jax.random.normal(streams_of[9], (D,), jnp.float32), 0.099609375, 1.8984375).astype(jnp.bfloat16)
    mlp_gain = jnp.clip(1.0 + 0.18 * jax.random.normal(streams_of[10], (2, D), jnp.float32), 0.099609375, 1.8984375).astype(jnp.bfloat16)
    mlp_in = bell_draw(streams_of[11], (2, D, FF), D ** -0.5, 0.1875, ((1, 8),))
    mlp_in_bias = bell_draw(streams_of[12], (2, FF), 0.5, 3.0, ((1, 8),))
    mlp_down = bell_draw(streams_of[13], (2, D, FF), (FF // 4) ** -0.5, 0.1875, ((1, 8),))
    mlp_out_bias = bell_draw(streams_of[14], (2, D), 0.3, 2.0, ((1, 8),))
    cotangent = noise_with(streams_of[15], (TOKENS, D), 1.0, 6.0, ((0, 8),), (0, 1, 8, 2.0))
    return {"latents": latents, "points": points, "neighbours": neighbours, "lengths": lengths, "cross_proj": cross_proj, "cross_out": cross_out, "cross_gains": cross_gains, "self_proj": self_proj, "self_out": self_out, "self_gain": self_gain, "mlp_gain": mlp_gain, "mlp_in": mlp_in, "mlp_in_bias": mlp_in_bias, "mlp_down": mlp_down, "mlp_out_bias": mlp_out_bias, "cotangent": cotangent}


@jax.custom_vjp
def low(v):
    return lax.optimization_barrier(v.astype(jnp.bfloat16)).astype(jnp.float32)

@jax.custom_vjp
def low_back(v):
    return v

def low_keep(v):
    return (low(v), None)

def low_pass(kept, grad):
    return (grad,)

def back_keep(v):
    return (v, None)

def back_low(kept, grad):
    return (low(grad),)
low.defvjp(low_keep, low_pass)
low_back.defvjp(back_keep, back_low)
PRECISION = lax.Precision.HIGHEST
EPSILON = 1e-05
MASKED = -1e+30

def layer_norm(values, gain_vec):
    centred = values - lax.optimization_barrier(jnp.mean(values, axis=-1, keepdims=True))
    return centred * lax.rsqrt(lax.optimization_barrier(jnp.mean(centred * centred, axis=-1, keepdims=True)) + EPSILON) * gain_vec

def section_out(values):
    return low(low_back(values))

def attend(inputs, source, valid_keys, gain_q, gain_kv, projection, out_proj):
    groups = source.shape[0]
    head_count = D // HD
    queries_in = low(layer_norm(inputs, gain_q))
    keys_in = low(layer_norm(source, gain_kv))
    queries = low(low_back(jnp.dot(queries_in, projection[:, 0], precision=PRECISION)))
    key_rows = low(low_back(jnp.einsum('gnd,de->gne', keys_in, projection[:, 1], precision=PRECISION)))
    value_rows = low(low_back(jnp.einsum('gnd,de->gne', keys_in, projection[:, 2], precision=PRECISION)))
    query_heads = queries.reshape(groups, LAT, head_count, HD)
    key_heads = key_rows.reshape(groups, NEIGH, head_count, HD)
    value_heads = value_rows.reshape(groups, NEIGH, head_count, HD)
    scores = jnp.einsum('glhc,gnhc->ghln', query_heads, key_heads, precision=PRECISION) * (1.0 / math.sqrt(HD))
    scores = low_back(scores)
    if valid_keys is not None:
        scores = jnp.where(valid_keys[:, None, None, :], scores, MASKED)
    soft_full = jax.nn.softmax(scores, axis=-1)
    mixture = jnp.einsum('ghln,gnhc->glhc', low(soft_full), value_heads, precision=PRECISION)
    mixture = low(low_back(mixture.reshape(groups * LAT, D)))
    return inputs + jnp.dot(mixture, out_proj, precision=PRECISION)

def feed(inputs, gain_vec, w_in, b_in, w_down, b_out):
    lowered = low(layer_norm(inputs, gain_vec))
    pre_act = low_back(jnp.dot(lowered, w_in, precision=PRECISION) + b_in)
    active = low(jax.nn.gelu(pre_act))
    return inputs + lax.dot_general(active, w_down, (((1,), (1,)), ((), ())), precision=PRECISION) + b_out

def two_layers(params, block_in):
    lat_rows, point_rows, neighbour_rows, length_rows = block_in
    cross_proj, cross_out, cross_gains, self_proj, self_out, self_gain, mlp_gain, mlp_in, mlp_in_bias, mlp_down, mlp_out_bias = params
    source = jnp.take(point_rows, neighbour_rows, axis=0)
    valid_keys = jnp.arange(NEIGH).astype(jnp.int32)[None, :] < length_rows.astype(jnp.int32)[:, None]
    hidden = section_out(attend(lat_rows, source, valid_keys, cross_gains[0], cross_gains[1], cross_proj, cross_out))
    hidden = section_out(feed(hidden, mlp_gain[0], mlp_in[0], mlp_in_bias[0], mlp_down[0], mlp_out_bias[0]))
    hidden = section_out(attend(hidden, hidden.reshape(-1, LAT, D), None, self_gain, self_gain, self_proj, self_out))
    return section_out(feed(hidden, mlp_gain[1], mlp_in[1], mlp_in_bias[1], mlp_down[1], mlp_out_bias[1]))

def forward(lat_rows, point_rows, neighbours, lengths, params):
    blocks = (lat_rows.reshape(N_BATCH, -1, D), point_rows.reshape(N_BATCH, -1, D), neighbours.reshape(N_BATCH, -1, NEIGH), lengths.reshape(N_BATCH, -1))

    def one_block(carry_in, block_in):
        return (carry_in, jax.checkpoint(two_layers)(params, block_in))
    carry_out, outputs = lax.scan(one_block, jnp.zeros((), jnp.float32), blocks)
    return outputs.reshape(-1, D)

def reference(latents, points, neighbours, lengths, cross_proj, cross_out, cross_gains, self_proj, self_out, self_gain, mlp_gain, mlp_in, mlp_in_bias, mlp_down, mlp_out_bias, cotangent):
    params = tuple((weight.astype(jnp.float32) for weight in (cross_proj, cross_out, cross_gains, self_proj, self_out, self_gain, mlp_gain, mlp_in, mlp_in_bias, mlp_down, mlp_out_bias)))

    def objective(lat_rows, point_rows, weights):
        outputs = forward(lat_rows, point_rows, neighbours, lengths, weights)
        grouped = outputs.reshape(GROUPS, -1)
        group_norms = jnp.sqrt(lax.optimization_barrier(jnp.mean(grouped * grouped, axis=1)) + EPSILON)
        norm_mean = jnp.mean(group_norms)
        penalty = 0.5 * (GROUPS * LAT * D) * norm_mean * norm_mean
        return (outputs, penalty, norm_mean)
    (outputs, penalty, norm_mean), pullback = jax.vjp(objective, latents.astype(jnp.float32), points.astype(jnp.float32), params)
    lat_grad, point_grad, weight_grads = pullback((cotangent.astype(jnp.float32), jnp.ones_like(penalty), jnp.zeros_like(norm_mean)))
    cross_proj_grad, cross_out_grad, cross_gains_grad, self_proj_grad, self_out_grad, self_gain_grad, mlp_gain_grad, mlp_in_grad, mlp_in_bias_grad, mlp_down_grad, mlp_out_bias_grad = weight_grads
    return (outputs.astype(jnp.bfloat16), lat_grad, point_grad, cross_proj_grad, cross_out_grad, cross_gains_grad, self_proj_grad, self_out_grad, self_gain_grad, mlp_gain_grad, mlp_in_grad, mlp_in_bias_grad, mlp_down_grad, mlp_out_bias_grad, norm_mean)
```

```python
import math

import jax
import jax.numpy as jnp
from jax import lax
from jax.sharding import PartitionSpec as P

HD = 128
EPSILON = 1e-05
MASKED = -1e30
BF = jnp.bfloat16
F32 = jnp.float32
ALL = ("batch", "section")


def mm(a, b):
    return jnp.dot(a, b, preferred_element_type=F32)


def mm_rows(a, b):
    return lax.dot_general(a, b, (((0,), (0,)), ((), ())), preferred_element_type=F32)


def mm_cols(a, b):
    return lax.dot_general(a, b, (((1,), (1,)), ((), ())), preferred_element_type=F32)


def unit_rows(values):
    centred = values - jnp.mean(values, axis=-1, keepdims=True)
    inverse = lax.rsqrt(jnp.mean(centred * centred, axis=-1, keepdims=True) + EPSILON)
    return centred * inverse, inverse


def norm_back(gradient, unit, inverse, gain):
    scaled = gradient * gain
    inner = (
        scaled
        - jnp.mean(scaled, axis=-1, keepdims=True)
        - unit * jnp.mean(scaled * unit, axis=-1, keepdims=True)
    )
    return inverse * inner, jnp.sum(gradient * unit, axis=0)


def heads_of(rows):
    return rows.reshape(rows.shape[0], -1, HD)


def attend(inputs, source, valid, gain_q, gain_kv, proj, out):
    unit_x, inv_x = unit_rows(inputs)
    queries_in = (unit_x * gain_q).astype(BF)
    unit_s, inv_s = unit_rows(source)
    keys_in = (unit_s * gain_kv).astype(BF)
    width = inputs.shape[1]
    q = mm(queries_in, proj[:, :width]).astype(BF)
    kv = mm(keys_in, proj[:, width:]).astype(BF)
    k, v = kv[:, :width], kv[:, width:]
    scores = jnp.einsum(
        "lhc,nhc->hln", heads_of(q), heads_of(k), preferred_element_type=F32
    ) * (1.0 / math.sqrt(HD))
    if valid is not None:
        scores = jnp.where(valid[None, None, :], scores, MASKED)
    grown = jnp.exp(scores - jnp.max(scores, axis=-1, keepdims=True))
    soft = grown / jnp.sum(grown, axis=-1, keepdims=True)
    mixture = jnp.einsum("hln,nhc->lhc", soft.astype(BF), heads_of(v), preferred_element_type=F32)
    mixture = mixture.reshape(inputs.shape).astype(BF)
    result = (inputs + mm(mixture, out)).astype(BF)
    return result, (unit_x, inv_x, queries_in, unit_s, inv_s, keys_in, q, k, v, soft, mixture)


def attend_back(gradient, kept, gain_q, gain_kv, proj, out):
    unit_x, inv_x, queries_in, unit_s, inv_s, keys_in, q, k, v, soft, mixture = kept
    width = gradient.shape[1]
    scale = 1.0 / math.sqrt(HD)
    grad_mix = mm_cols(gradient, out).astype(BF)
    out_grad = mm_rows(mixture, gradient).astype(BF)
    grad_soft = jnp.einsum(
        "lhc,nhc->hln", heads_of(grad_mix), heads_of(v), preferred_element_type=F32
    )
    inner = jnp.sum(soft * grad_soft, axis=-1, keepdims=True)
    grad_scores = (soft * (grad_soft - inner)).astype(BF)
    dq = jnp.einsum("hln,nhc->lhc", grad_scores, heads_of(k), preferred_element_type=F32) * scale
    dk = jnp.einsum("hln,lhc->nhc", grad_scores, heads_of(q), preferred_element_type=F32) * scale
    dv = jnp.einsum(
        "hln,lhc->nhc", soft.astype(BF), heads_of(grad_mix), preferred_element_type=F32
    )
    dq = dq.reshape(gradient.shape).astype(BF)
    dk = dk.reshape(-1, width).astype(BF)
    dv = dv.reshape(-1, width).astype(BF)
    dkv = jnp.concatenate([dk, dv], axis=1)
    grad_x, gain_q_grad = norm_back(mm_cols(dq, proj[:, :width]), unit_x, inv_x, gain_q)
    grad_s, gain_kv_grad = norm_back(mm_cols(dkv, proj[:, width:]), unit_s, inv_s, gain_kv)
    proj_grad = jnp.concatenate(
        [mm_rows(queries_in, dq).astype(BF), mm_rows(keys_in, dkv).astype(BF)], axis=1
    )
    return grad_x, grad_s, gain_q_grad, gain_kv_grad, proj_grad, out_grad


def feed(inputs, gain, w_in, b_in, w_down, b_out):
    unit, inverse = unit_rows(inputs)
    lowered = (unit * gain).astype(BF)
    pre_act = mm(lowered, w_in) + b_in
    active = jax.nn.gelu(pre_act).astype(BF)
    result = (inputs + mm_cols(active, w_down) + b_out).astype(BF)
    return result, (unit, inverse, lowered, pre_act, active)


def feed_back(gradient, kept, gain, w_in, w_down):
    unit, inverse, lowered, pre_act, active = kept
    grad_act = mm(gradient, w_down)
    grad_pre = jax.vjp(jax.nn.gelu, pre_act)[1](grad_act)[0].astype(BF)
    grad_x, gain_grad = norm_back(mm_cols(grad_pre, w_in), unit, inverse, gain)
    down_grad = mm_rows(gradient, active).astype(BF)
    in_grad = mm_rows(lowered, grad_pre).astype(BF)
    bias_grad = jnp.sum(grad_pre.astype(F32), axis=0)
    out_grad = jnp.sum(gradient.astype(F32), axis=0)
    return grad_x, gain_grad, in_grad, bias_grad, down_grad, out_grad


def per_device(
    latents,
    points,
    neighbours,
    lengths,
    cross_proj,
    cross_out,
    cross_gains,
    self_proj,
    self_out,
    self_gain,
    mlp_gain,
    mlp_in,
    mlp_in_bias,
    mlp_down,
    mlp_out_bias,
    cotangent,
):
    sections = lax.axis_size("section")
    section_at = lax.axis_index("section")
    width = latents.shape[1]
    hidden = mlp_in.shape[2]
    groups_dev = neighbours.shape[0]
    rows = latents.shape[0] // sections
    shard = cross_out.shape[0]
    piece = shard // sections
    groups_all = groups_dev * lax.axis_size("batch")

    def gathered(block):
        own = lax.dynamic_slice_in_dim(block, section_at * piece, piece, 0)
        return lax.all_gather(own, ALL, axis=0, tiled=True)

    vectors = jnp.concatenate(
        [
            cross_gains.reshape(-1),
            self_gain,
            mlp_gain.reshape(-1),
            mlp_out_bias.reshape(-1),
            mlp_in_bias.reshape(-1),
        ]
    ).reshape(-1, shard)
    spread = lax.all_gather(vectors, "batch", axis=0, tiled=False).astype(F32)

    def vector(first, count):
        return spread[:, first : first + count].reshape(-1)

    gains_cross = (vector(0, 1), vector(1, 1))
    gain_self = vector(2, 1)
    gains_mlp = (vector(3, 1), vector(4, 1))
    biases_out = (vector(5, 1), vector(6, 1))
    per_bias = hidden // width
    biases_in = (vector(7, per_bias), vector(7 + per_bias, per_bias))

    proj_c = gathered(cross_proj.reshape(shard, 3 * width))
    out_c = gathered(cross_out)
    in_0 = gathered(mlp_in[0])
    down_0 = gathered(mlp_down[0])
    proj_s = gathered(self_proj.reshape(shard, 3 * width))
    out_s = gathered(self_out)
    in_1 = gathered(mlp_in[1])
    down_1 = gathered(mlp_down[1])

    mine = lax.dynamic_slice_in_dim(latents, section_at * rows, rows, 0).astype(F32)
    cot = lax.dynamic_slice_in_dim(cotangent, section_at * rows, rows, 0).astype(F32)
    listed = lax.dynamic_index_in_dim(neighbours, section_at, 0, keepdims=False)
    length = lax.dynamic_index_in_dim(lengths, section_at, 0, keepdims=False)
    valid = jnp.arange(listed.shape[0], dtype=jnp.int32) < length
    picks = listed[:, None] == jnp.arange(points.shape[0], dtype=jnp.int32)[None, :]
    picks = picks.astype(BF)
    source = mm(picks, points)

    u1, kept_c = attend(mine, source, valid, gains_cross[0], gains_cross[1], proj_c, out_c)
    u2, kept_0 = feed(u1.astype(F32), gains_mlp[0], in_0, biases_in[0], down_0, biases_out[0])
    u2 = u2.astype(F32)
    u3, kept_s = attend(u2, u2, None, gain_self, gain_self, proj_s, out_s)
    u4, kept_1 = feed(u3.astype(F32), gains_mlp[1], in_1, biases_in[1], down_1, biases_out[1])
    final = u4.astype(F32)
    group_norm = jnp.sqrt(jnp.mean(final * final) + EPSILON)
    norm_mean = lax.psum(group_norm, ALL) / groups_all

    def settled(grad):
        part = lax.psum_scatter(grad, ALL, scatter_dimension=0, tiled=True)
        return lax.all_gather(part, "section", axis=0, tiled=True).astype(F32)

    g4 = (cot + (norm_mean / group_norm) * final).astype(BF)
    dx, gain_1_grad, in_1_grad, bias_1_grad, down_1_grad, ob_1_grad = feed_back(
        g4, kept_1, gains_mlp[1], in_1, down_1
    )
    in_1_grad, down_1_grad = settled(in_1_grad), settled(down_1_grad)
    g3 = (g4.astype(F32) + dx).astype(BF)
    dx, ds, gq, gkv, proj_s_grad, out_s_grad = attend_back(
        g3, kept_s, gain_self, gain_self, proj_s, out_s
    )
    proj_s_grad, out_s_grad = settled(proj_s_grad), settled(out_s_grad)
    gain_s_grad = gq + gkv
    g2 = (g3.astype(F32) + dx + ds).astype(BF)
    dx, gain_0_grad, in_0_grad, bias_0_grad, down_0_grad, ob_0_grad = feed_back(
        g2, kept_0, gains_mlp[0], in_0, down_0
    )
    in_0_grad, down_0_grad = settled(in_0_grad), settled(down_0_grad)
    g1 = (g2.astype(F32) + dx).astype(BF)
    dx, ds, cq_grad, ckv_grad, proj_c_grad, out_c_grad = attend_back(
        g1, kept_c, gains_cross[0], gains_cross[1], proj_c, out_c
    )
    proj_c_grad, out_c_grad = settled(proj_c_grad), settled(out_c_grad)
    g0 = (g1.astype(F32) + dx).astype(BF)
    high = ds.astype(BF)
    low = (ds - high.astype(F32)).astype(BF)
    point_part = mm_rows(picks, high) + mm_rows(picks, low)
    points_grad = lax.psum(point_part.astype(BF), "section").astype(F32)
    latents_out = lax.all_gather(u4, "section", axis=0, tiled=True)
    latents_grad = lax.all_gather(g0, "section", axis=0, tiled=True).astype(F32)

    small = jnp.concatenate(
        [
            cq_grad,
            ckv_grad,
            gain_s_grad,
            gain_0_grad,
            gain_1_grad,
            ob_0_grad,
            ob_1_grad,
            bias_0_grad,
            bias_1_grad,
        ]
    ).reshape(-1, width)
    small = lax.psum(small, ALL)
    batch_at = lax.axis_index("batch")

    def own(first, count):
        flat = small[first : first + count].reshape(-1)
        size = flat.shape[0] // lax.axis_size("batch")
        return lax.dynamic_slice_in_dim(flat, batch_at * size, size, 0)

    return (
        latents_out,
        latents_grad,
        points_grad,
        proj_c_grad.reshape(shard, 3, width),
        out_c_grad,
        jnp.stack([own(0, 1), own(1, 1)]),
        proj_s_grad.reshape(shard, 3, width),
        out_s_grad,
        own(2, 1),
        jnp.stack([own(3, 1), own(4, 1)]),
        jnp.stack([in_0_grad, in_1_grad]),
        jnp.stack([own(7, per_bias), own(7 + per_bias, per_bias)]),
        jnp.stack([down_0_grad, down_1_grad]),
        jnp.stack([own(5, 1), own(6, 1)]),
        norm_mean,
    )


def solution(mesh):
    rows = P("batch", None)
    cols = P(None, "batch")
    block = P("batch", None, None)
    pair = P(None, "batch", None)
    return jax.shard_map(
        per_device,
        mesh=mesh,
        in_specs=(
            rows,
            rows,
            rows,
            P("batch"),
            block,
            rows,
            cols,
            block,
            rows,
            P("batch"),
            cols,
            pair,
            cols,
            pair,
            cols,
            rows,
        ),
        out_specs=(
            rows,
            rows,
            rows,
            block,
            rows,
            cols,
            block,
            rows,
            P("batch"),
            cols,
            pair,
            cols,
            pair,
            cols,
            P(),
        ),
        check_vma=False,
    )
```

```python
import functools
import math

import jax
import jax.numpy as jnp
from jax import lax
from jax.experimental import pallas as pl
from jax.experimental.pallas import tpu as pltpu
from jax.sharding import PartitionSpec as P

HD = 128
EPSILON = 1e-05
MASKED = -1e30
BF = jnp.bfloat16
F32 = jnp.float32
ALL = ("batch", "section")
MESH = pl.DeviceIdType.MESH
GATHER_WIDTH = 2048
AHEAD = 3


def mm(a, b):
    return jnp.dot(a, b, preferred_element_type=F32)


def mm_rows(a, b):
    return lax.dot_general(a, b, (((0,), (0,)), ((), ())), preferred_element_type=F32)


def mm_cols(a, b):
    return lax.dot_general(a, b, (((1,), (1,)), ((), ())), preferred_element_type=F32)


def unit_rows(values):
    centred = values - jnp.mean(values, axis=-1, keepdims=True)
    inverse = lax.rsqrt(jnp.mean(centred * centred, axis=-1, keepdims=True) + EPSILON)
    return centred * inverse, inverse


def norm_back(gradient, unit, inverse, gain):
    scaled = gradient * gain
    inner = (
        scaled
        - jnp.mean(scaled, axis=-1, keepdims=True)
        - unit * jnp.mean(scaled * unit, axis=-1, keepdims=True)
    )
    return inverse * inner, jnp.sum(gradient * unit, axis=0)


def heads_of(rows):
    return rows.reshape(rows.shape[0], -1, HD)


def attend(inputs, source, valid, gain_q, gain_kv, proj, out):
    unit_x, inv_x = unit_rows(inputs)
    queries_in = (unit_x * gain_q).astype(BF)
    unit_s, inv_s = unit_rows(source)
    keys_in = (unit_s * gain_kv).astype(BF)
    width = inputs.shape[1]
    q = mm(queries_in, proj[:, :width]).astype(BF)
    kv = mm(keys_in, proj[:, width:]).astype(BF)
    k, v = kv[:, :width], kv[:, width:]
    scores = jnp.einsum(
        "lhc,nhc->hln", heads_of(q), heads_of(k), preferred_element_type=F32
    ) * (1.0 / math.sqrt(HD))
    if valid is not None:
        scores = jnp.where(valid[None, None, :], scores, MASKED)
    grown = jnp.exp(scores - jnp.max(scores, axis=-1, keepdims=True))
    soft = grown / jnp.sum(grown, axis=-1, keepdims=True)
    mixture = jnp.einsum("hln,nhc->lhc", soft.astype(BF), heads_of(v), preferred_element_type=F32)
    mixture = mixture.reshape(inputs.shape).astype(BF)
    result = (inputs + mm(mixture, out)).astype(BF)
    return result, (unit_x, inv_x, queries_in, unit_s, inv_s, keys_in, q, k, v, soft, mixture)


def attend_back(gradient, kept, gain_q, gain_kv, proj, out):
    unit_x, inv_x, queries_in, unit_s, inv_s, keys_in, q, k, v, soft, mixture = kept
    width = gradient.shape[1]
    scale = 1.0 / math.sqrt(HD)
    grad_mix = mm_cols(gradient, out).astype(BF)
    out_grad = mm_rows(mixture, gradient).astype(BF)
    grad_soft = jnp.einsum(
        "lhc,nhc->hln", heads_of(grad_mix), heads_of(v), preferred_element_type=F32
    )
    inner = jnp.sum(soft * grad_soft, axis=-1, keepdims=True)
    grad_scores = (soft * (grad_soft - inner)).astype(BF)
    dq = jnp.einsum("hln,nhc->lhc", grad_scores, heads_of(k), preferred_element_type=F32) * scale
    dk = jnp.einsum("hln,lhc->nhc", grad_scores, heads_of(q), preferred_element_type=F32) * scale
    dv = jnp.einsum(
        "hln,lhc->nhc", soft.astype(BF), heads_of(grad_mix), preferred_element_type=F32
    )
    dq = dq.reshape(gradient.shape).astype(BF)
    dk = dk.reshape(-1, width).astype(BF)
    dv = dv.reshape(-1, width).astype(BF)
    dkv = jnp.concatenate([dk, dv], axis=1)
    grad_x, gain_q_grad = norm_back(mm_cols(dq, proj[:, :width]), unit_x, inv_x, gain_q)
    grad_s, gain_kv_grad = norm_back(mm_cols(dkv, proj[:, width:]), unit_s, inv_s, gain_kv)
    proj_grad = jnp.concatenate(
        [mm_rows(queries_in, dq).astype(BF), mm_rows(keys_in, dkv).astype(BF)], axis=1
    )
    return grad_x, grad_s, gain_q_grad, gain_kv_grad, proj_grad, out_grad


def feed(inputs, gain, w_in, b_in, w_down, b_out):
    unit, inverse = unit_rows(inputs)
    lowered = (unit * gain).astype(BF)
    pre_act = mm(lowered, w_in) + b_in
    active = jax.nn.gelu(pre_act).astype(BF)
    result = (inputs + mm_cols(active, w_down) + b_out).astype(BF)
    return result, (unit, inverse, lowered, pre_act, active)


def feed_back(gradient, kept, gain, w_in, w_down):
    unit, inverse, lowered, pre_act, active = kept
    grad_act = mm(gradient, w_down)
    grad_pre = jax.vjp(jax.nn.gelu, pre_act)[1](grad_act)[0].astype(BF)
    grad_x, gain_grad = norm_back(mm_cols(grad_pre, w_in), unit, inverse, gain)
    down_grad = mm_rows(gradient, active).astype(BF)
    in_grad = mm_rows(lowered, grad_pre).astype(BF)
    bias_grad = jnp.sum(grad_pre.astype(F32), axis=0)
    out_grad = jnp.sum(gradient.astype(F32), axis=0)
    return grad_x, gain_grad, in_grad, bias_grad, down_grad, out_grad


def gather_kernel(widths, *refs):
    count = len(widths)
    ins, outs = refs[:count], refs[count : 2 * count]
    (own_sem, send, recv, kin_send, kin_recv) = refs[2 * count :]
    section_at = lax.axis_index("section")
    batch_at = lax.axis_index("batch")
    line = lax.axis_size("batch") // 2
    core = lax.rem(batch_at, 2)
    spot = batch_at // 2
    beside = section_at + 1 - 2 * lax.rem(section_at, 2)
    above = lax.rem(section_at + 2, 4)
    across = lax.rem(beside + 2, 4)
    sibling = batch_at + 1 - 2 * core
    shard = ins[0].shape[0]

    def down_line(step):
        return lax.rem(spot + step, line) * 2 + core

    def up_line(step):
        return lax.rem(spot + line - step, line) * 2 + core

    peers = [(beside, batch_at), (above, batch_at), (section_at, sibling)]
    peers += [(section_at, down_line(step)) for step in range(1, line)]
    barrier = pltpu.get_barrier_semaphore()
    for peer in peers:
        pl.semaphore_signal(barrier, inc=1, device_id=peer, device_id_type=MESH)
    pl.semaphore_wait(barrier, len(peers))

    items = [
        (index, start, min(GATHER_WIDTH, width - start))
        for index, width in enumerate(widths)
        for start in range(0, width, GATHER_WIDTH)
    ]

    def spread(ref, owner, first, size):
        return ref.at[pl.ds(pl.multiple_of(owner * shard, shard), shard), pl.ds(first, size)]

    def part(item, quarter):
        _, start, size = items[item]
        return pl.multiple_of(start + quarter * (size // 4), 128), size // 4

    def line_copy(item, step):
        index = items[item][0]
        first, size = part(item, section_at)
        return pltpu.make_async_remote_copy(
            ins[index].at[:, pl.ds(first, size)],
            spread(outs[index], batch_at, first, size),
            send.at[0, item, step],
            recv.at[0, item, step],
            device_id=(section_at, down_line(step)),
            device_id_type=MESH,
        )

    def plane_copy(item, step, way, quarter, low, size, peer):
        index = items[item][0]
        ref = spread(outs[index], up_line(step), low, size)
        return pltpu.make_async_remote_copy(
            ref,
            ref,
            send.at[way, item, step],
            recv.at[way, item, step],
            device_id=(peer, batch_at),
            device_id_type=MESH,
        )

    def near(item, step):
        first, size = part(item, section_at)
        return [
            plane_copy(item, step, 1, section_at, first, size, beside),
            plane_copy(item, step, 2, section_at, first, size, above),
        ]

    def far(item, step):
        size = items[item][2] // 8
        by_y, _ = part(item, beside)
        by_x, _ = part(item, above)
        by_x = pl.multiple_of(by_x + size, 128)
        return [
            plane_copy(item, step, 3, beside, by_y, size, above),
            plane_copy(item, step, 4, above, by_x, size, beside),
        ]

    def kin(item, step):
        index, start, size = items[item]
        if step == 0:
            source = ins[index].at[:, pl.ds(start, size)]
        else:
            source = spread(outs[index], up_line(step), start, size)
        return pltpu.make_async_remote_copy(
            source,
            spread(outs[index], up_line(step), start, size),
            kin_send.at[item, step],
            kin_recv.at[item, step],
            device_id=(section_at, sibling),
            device_id_type=MESH,
        )

    def own(item):
        index, start, size = items[item]
        return pltpu.make_async_copy(
            ins[index].at[:, pl.ds(start, size)],
            spread(outs[index], batch_at, start, size),
            own_sem.at[item],
        )

    steps = range(1, line)
    total = len(items)
    started = []

    def launch(copies):
        for copy in copies:
            copy.start()
        started.extend(copies)

    for item in range(min(AHEAD, total)):
        launch([line_copy(item, step) for step in steps])
    for moment in range(total + 2):
        if moment + AHEAD < total:
            launch([line_copy(moment + AHEAD, step) for step in steps])
        if moment < total:
            for step in steps:
                line_copy(moment, step).wait_recv()
                launch(near(moment, step))
            own(moment).start()
            launch([kin(moment, 0)])
        if 0 <= moment - 1 < total:
            for step in steps:
                for copy, onward in zip(near(moment - 1, step), far(moment - 1, step)):
                    copy.wait_recv()
                    launch([onward])
        if 0 <= moment - 2 < total:
            for step in steps:
                for copy in far(moment - 2, step):
                    copy.wait_recv()
                launch([kin(moment - 2, step)])
    for item in range(total):
        own(item).wait()
        for step in range(line):
            kin(item, step).wait_recv()
    for copy in started:
        copy.wait_send()


def gather_all(blocks):
    widths = tuple(block.shape[1] for block in blocks)
    line = lax.axis_size("batch") // 2
    total = sum(-(-width // GATHER_WIDTH) for width in widths)
    full = blocks[0].shape[0] * line * 2
    anywhere = pl.BlockSpec(memory_space=pl.ANY)
    return pl.pallas_call(
        functools.partial(gather_kernel, widths),
        out_shape=[jax.ShapeDtypeStruct((full, width), BF) for width in widths],
        in_specs=[anywhere] * len(blocks),
        out_specs=[anywhere] * len(blocks),
        scratch_shapes=[
            pltpu.SemaphoreType.DMA((total,)),
            pltpu.SemaphoreType.DMA((5, total, line)),
            pltpu.SemaphoreType.DMA((5, total, line)),
            pltpu.SemaphoreType.DMA((total, line)),
            pltpu.SemaphoreType.DMA((total, line)),
        ],
        compiler_params=pltpu.CompilerParams(collective_id=1, has_side_effects=True),
    )(*blocks)


def per_device(
    latents,
    points,
    neighbours,
    lengths,
    cross_proj,
    cross_out,
    cross_gains,
    self_proj,
    self_out,
    self_gain,
    mlp_gain,
    mlp_in,
    mlp_in_bias,
    mlp_down,
    mlp_out_bias,
    cotangent,
):
    sections = lax.axis_size("section")
    section_at = lax.axis_index("section")
    width = latents.shape[1]
    hidden = mlp_in.shape[2]
    groups_dev = neighbours.shape[0]
    rows = latents.shape[0] // sections
    shard = cross_out.shape[0]
    piece = shard // sections
    groups_all = groups_dev * lax.axis_size("batch")

    def gathered(block):
        own = lax.dynamic_slice_in_dim(block, section_at * piece, piece, 0)
        return lax.all_gather(own, ALL, axis=0, tiled=True)

    vectors = jnp.concatenate(
        [
            cross_gains.reshape(-1),
            self_gain,
            mlp_gain.reshape(-1),
            mlp_out_bias.reshape(-1),
            mlp_in_bias.reshape(-1),
        ]
    ).reshape(-1, shard)
    spread = lax.all_gather(vectors, "batch", axis=0, tiled=False).astype(F32)

    def vector(first, count):
        return spread[:, first : first + count].reshape(-1)

    gains_cross = (vector(0, 1), vector(1, 1))
    gain_self = vector(2, 1)
    gains_mlp = (vector(3, 1), vector(4, 1))
    biases_out = (vector(5, 1), vector(6, 1))
    per_bias = hidden // width
    biases_in = (vector(7, per_bias), vector(7 + per_bias, per_bias))

    blocks = [
        cross_proj.reshape(shard, 3 * width),
        cross_out,
        mlp_in[0],
        mlp_down[0],
        self_proj.reshape(shard, 3 * width),
        self_out,
        mlp_in[1],
        mlp_down[1],
    ]
    small_slice = lax.axis_size("batch") == 8
    full = gather_all(blocks) if small_slice else [gathered(block) for block in blocks]
    proj_c, out_c, in_0, down_0, proj_s, out_s, in_1, down_1 = full

    mine = lax.dynamic_slice_in_dim(latents, section_at * rows, rows, 0).astype(F32)
    cot = lax.dynamic_slice_in_dim(cotangent, section_at * rows, rows, 0).astype(F32)
    listed = lax.dynamic_index_in_dim(neighbours, section_at, 0, keepdims=False)
    length = lax.dynamic_index_in_dim(lengths, section_at, 0, keepdims=False)
    valid = jnp.arange(listed.shape[0], dtype=jnp.int32) < length
    picks = listed[:, None] == jnp.arange(points.shape[0], dtype=jnp.int32)[None, :]
    picks = picks.astype(BF)
    source = mm(picks, points)

    u1, kept_c = attend(mine, source, valid, gains_cross[0], gains_cross[1], proj_c, out_c)
    u2, kept_0 = feed(u1.astype(F32), gains_mlp[0], in_0, biases_in[0], down_0, biases_out[0])
    u2 = u2.astype(F32)
    u3, kept_s = attend(u2, u2, None, gain_self, gain_self, proj_s, out_s)
    u4, kept_1 = feed(u3.astype(F32), gains_mlp[1], in_1, biases_in[1], down_1, biases_out[1])
    final = u4.astype(F32)
    group_norm = jnp.sqrt(jnp.mean(final * final) + EPSILON)
    norm_mean = lax.psum(group_norm, ALL) / groups_all

    def settled(grad):
        part = lax.psum_scatter(grad, ALL, scatter_dimension=0, tiled=True)
        return lax.all_gather(part, "section", axis=0, tiled=True).astype(F32)

    g4 = (cot + (norm_mean / group_norm) * final).astype(BF)
    dx, gain_1_grad, in_1_grad, bias_1_grad, down_1_grad, ob_1_grad = feed_back(
        g4, kept_1, gains_mlp[1], in_1, down_1
    )
    in_1_grad, down_1_grad = settled(in_1_grad), settled(down_1_grad)
    g3 = (g4.astype(F32) + dx).astype(BF)
    dx, ds, gq, gkv, proj_s_grad, out_s_grad = attend_back(
        g3, kept_s, gain_self, gain_self, proj_s, out_s
    )
    proj_s_grad, out_s_grad = settled(proj_s_grad), settled(out_s_grad)
    gain_s_grad = gq + gkv
    g2 = (g3.astype(F32) + dx + ds).astype(BF)
    dx, gain_0_grad, in_0_grad, bias_0_grad, down_0_grad, ob_0_grad = feed_back(
        g2, kept_0, gains_mlp[0], in_0, down_0
    )
    in_0_grad, down_0_grad = settled(in_0_grad), settled(down_0_grad)
    g1 = (g2.astype(F32) + dx).astype(BF)
    dx, ds, cq_grad, ckv_grad, proj_c_grad, out_c_grad = attend_back(
        g1, kept_c, gains_cross[0], gains_cross[1], proj_c, out_c
    )
    proj_c_grad, out_c_grad = settled(proj_c_grad), settled(out_c_grad)
    g0 = (g1.astype(F32) + dx).astype(BF)
    high = ds.astype(BF)
    low = (ds - high.astype(F32)).astype(BF)
    point_part = mm_rows(picks, high) + mm_rows(picks, low)
    points_grad = lax.psum(point_part.astype(BF), "section").astype(F32)
    latents_out = lax.all_gather(u4, "section", axis=0, tiled=True)
    latents_grad = lax.all_gather(g0, "section", axis=0, tiled=True).astype(F32)

    small = jnp.concatenate(
        [
            cq_grad,
            ckv_grad,
            gain_s_grad,
            gain_0_grad,
            gain_1_grad,
            ob_0_grad,
            ob_1_grad,
            bias_0_grad,
            bias_1_grad,
        ]
    ).reshape(-1, width)
    small = lax.psum(small, ALL)
    batch_at = lax.axis_index("batch")

    def own(first, count):
        flat = small[first : first + count].reshape(-1)
        size = flat.shape[0] // lax.axis_size("batch")
        return lax.dynamic_slice_in_dim(flat, batch_at * size, size, 0)

    return (
        latents_out,
        latents_grad,
        points_grad,
        proj_c_grad.reshape(shard, 3, width),
        out_c_grad,
        jnp.stack([own(0, 1), own(1, 1)]),
        proj_s_grad.reshape(shard, 3, width),
        out_s_grad,
        own(2, 1),
        jnp.stack([own(3, 1), own(4, 1)]),
        jnp.stack([in_0_grad, in_1_grad]),
        jnp.stack([own(7, per_bias), own(7 + per_bias, per_bias)]),
        jnp.stack([down_0_grad, down_1_grad]),
        jnp.stack([own(5, 1), own(6, 1)]),
        norm_mean,
    )


def solution(mesh):
    rows = P("batch", None)
    cols = P(None, "batch")
    block = P("batch", None, None)
    pair = P(None, "batch", None)
    return jax.shard_map(
        per_device,
        mesh=mesh,
        in_specs=(
            rows,
            rows,
            rows,
            P("batch"),
            block,
            rows,
            cols,
            block,
            rows,
            P("batch"),
            cols,
            pair,
            cols,
            pair,
            cols,
            rows,
        ),
        out_specs=(
            rows,
            rows,
            rows,
            block,
            rows,
            cols,
            block,
            rows,
            P("batch"),
            cols,
            pair,
            cols,
            pair,
            cols,
            P(),
        ),
        check_vma=False,
    )
```

```python
import functools
import math

import jax
import jax.numpy as jnp
from jax import lax
from jax.experimental import pallas as pl
from jax.experimental.pallas import tpu as pltpu
from jax.sharding import PartitionSpec as P

HD = 128
EPSILON = 1e-05
MASKED = -1e30
BF = jnp.bfloat16
F32 = jnp.float32
ALL = ("batch", "section")
MESH = pl.DeviceIdType.MESH
GATHER_WIDTH = 2048
AHEAD = 3


def mm(a, b):
    return jnp.dot(a, b, preferred_element_type=F32)


def mm_rows(a, b):
    return lax.dot_general(a, b, (((0,), (0,)), ((), ())), preferred_element_type=F32)


def mm_cols(a, b):
    return lax.dot_general(a, b, (((1,), (1,)), ((), ())), preferred_element_type=F32)


def unit_rows(values):
    centred = values - jnp.mean(values, axis=-1, keepdims=True)
    inverse = lax.rsqrt(jnp.mean(centred * centred, axis=-1, keepdims=True) + EPSILON)
    return centred * inverse, inverse


def norm_back(gradient, unit, inverse, gain):
    scaled = gradient * gain
    inner = (
        scaled
        - jnp.mean(scaled, axis=-1, keepdims=True)
        - unit * jnp.mean(scaled * unit, axis=-1, keepdims=True)
    )
    return inverse * inner, jnp.sum(gradient * unit, axis=0)


def heads_of(rows):
    return rows.reshape(rows.shape[0], -1, HD)


def attend(inputs, source, valid, gain_q, gain_kv, proj, out):
    unit_x, inv_x = unit_rows(inputs)
    queries_in = (unit_x * gain_q).astype(BF)
    unit_s, inv_s = unit_rows(source)
    keys_in = (unit_s * gain_kv).astype(BF)
    width = inputs.shape[1]
    q = mm(queries_in, proj[:, :width]).astype(BF)
    kv = mm(keys_in, proj[:, width:]).astype(BF)
    k, v = kv[:, :width], kv[:, width:]
    scores = jnp.einsum(
        "lhc,nhc->hln", heads_of(q), heads_of(k), preferred_element_type=F32
    ) * (1.0 / math.sqrt(HD))
    if valid is not None:
        scores = jnp.where(valid[None, None, :], scores, MASKED)
    grown = jnp.exp(scores - jnp.max(scores, axis=-1, keepdims=True))
    soft = grown / jnp.sum(grown, axis=-1, keepdims=True)
    mixture = jnp.einsum("hln,nhc->lhc", soft.astype(BF), heads_of(v), preferred_element_type=F32)
    mixture = mixture.reshape(inputs.shape).astype(BF)
    result = (inputs + mm(mixture, out)).astype(BF)
    return result, (unit_x, inv_x, queries_in, unit_s, inv_s, keys_in, q, k, v, soft, mixture)


def attend_back(gradient, kept, gain_q, gain_kv, proj, out):
    unit_x, inv_x, queries_in, unit_s, inv_s, keys_in, q, k, v, soft, mixture = kept
    width = gradient.shape[1]
    scale = 1.0 / math.sqrt(HD)
    grad_mix = mm_cols(gradient, out).astype(BF)
    grad_soft = jnp.einsum(
        "lhc,nhc->hln", heads_of(grad_mix), heads_of(v), preferred_element_type=F32
    )
    inner = jnp.sum(soft * grad_soft, axis=-1, keepdims=True)
    grad_scores = (soft * (grad_soft - inner)).astype(BF)
    dq = jnp.einsum("hln,nhc->lhc", grad_scores, heads_of(k), preferred_element_type=F32) * scale
    dk = jnp.einsum("hln,lhc->nhc", grad_scores, heads_of(q), preferred_element_type=F32) * scale
    dv = jnp.einsum(
        "hln,lhc->nhc", soft.astype(BF), heads_of(grad_mix), preferred_element_type=F32
    )
    dq = dq.reshape(gradient.shape).astype(BF)
    dk = dk.reshape(-1, width).astype(BF)
    dv = dv.reshape(-1, width).astype(BF)
    dkv = jnp.concatenate([dk, dv], axis=1)
    grad_x, gain_q_grad = norm_back(mm_cols(dq, proj[:, :width]), unit_x, inv_x, gain_q)
    grad_s, gain_kv_grad = norm_back(mm_cols(dkv, proj[:, width:]), unit_s, inv_s, gain_kv)
    pairs = ((queries_in, dq), (keys_in, dkv), (mixture, gradient))
    return grad_x, grad_s, gain_q_grad, gain_kv_grad, pairs


def feed(inputs, gain, w_in, b_in, w_down, b_out):
    unit, inverse = unit_rows(inputs)
    lowered = (unit * gain).astype(BF)
    pre_act = mm(lowered, w_in) + b_in
    active = jax.nn.gelu(pre_act).astype(BF)
    result = (inputs + mm_cols(active, w_down) + b_out).astype(BF)
    return result, (unit, inverse, lowered, pre_act, active)


def feed_back(gradient, kept, gain, w_in, w_down):
    unit, inverse, lowered, pre_act, active = kept
    grad_act = mm(gradient, w_down)
    grad_pre = jax.vjp(jax.nn.gelu, pre_act)[1](grad_act)[0].astype(BF)
    grad_x, gain_grad = norm_back(mm_cols(grad_pre, w_in), unit, inverse, gain)
    bias_grad = jnp.sum(grad_pre.astype(F32), axis=0)
    out_grad = jnp.sum(gradient.astype(F32), axis=0)
    return grad_x, gain_grad, bias_grad, out_grad, ((lowered, grad_pre), (gradient, active))


def gather_kernel(widths, *refs):
    count = len(widths)
    ins, outs = refs[:count], refs[count : 2 * count]
    (own_sem, send, recv, kin_send, kin_recv) = refs[2 * count :]
    section_at = lax.axis_index("section")
    batch_at = lax.axis_index("batch")
    line = lax.axis_size("batch") // 2
    core = lax.rem(batch_at, 2)
    spot = batch_at // 2
    beside = section_at + 1 - 2 * lax.rem(section_at, 2)
    above = lax.rem(section_at + 2, 4)
    across = lax.rem(beside + 2, 4)
    sibling = batch_at + 1 - 2 * core
    shard = ins[0].shape[0]

    def down_line(step):
        return lax.rem(spot + step, line) * 2 + core

    def up_line(step):
        return lax.rem(spot + line - step, line) * 2 + core

    peers = [(beside, batch_at), (above, batch_at), (section_at, sibling)]
    peers += [(section_at, down_line(step)) for step in range(1, line)]
    barrier = pltpu.get_barrier_semaphore()
    for peer in peers:
        pl.semaphore_signal(barrier, inc=1, device_id=peer, device_id_type=MESH)
    pl.semaphore_wait(barrier, len(peers))

    items = [
        (index, start, min(GATHER_WIDTH, width - start))
        for index, width in enumerate(widths)
        for start in range(0, width, GATHER_WIDTH)
    ]

    def spread(ref, owner, first, size):
        return ref.at[pl.ds(pl.multiple_of(owner * shard, shard), shard), pl.ds(first, size)]

    def part(item, quarter):
        _, start, size = items[item]
        return pl.multiple_of(start + quarter * (size // 4), 128), size // 4

    def line_copy(item, step):
        index = items[item][0]
        first, size = part(item, section_at)
        return pltpu.make_async_remote_copy(
            ins[index].at[:, pl.ds(first, size)],
            spread(outs[index], batch_at, first, size),
            send.at[0, item, step],
            recv.at[0, item, step],
            device_id=(section_at, down_line(step)),
            device_id_type=MESH,
        )

    def plane_copy(item, step, way, quarter, low, size, peer):
        index = items[item][0]
        ref = spread(outs[index], up_line(step), low, size)
        return pltpu.make_async_remote_copy(
            ref,
            ref,
            send.at[way, item, step],
            recv.at[way, item, step],
            device_id=(peer, batch_at),
            device_id_type=MESH,
        )

    def near(item, step):
        first, size = part(item, section_at)
        return [
            plane_copy(item, step, 1, section_at, first, size, beside),
            plane_copy(item, step, 2, section_at, first, size, above),
        ]

    def far(item, step):
        size = items[item][2] // 8
        by_y, _ = part(item, beside)
        by_x, _ = part(item, above)
        by_x = pl.multiple_of(by_x + size, 128)
        return [
            plane_copy(item, step, 3, beside, by_y, size, above),
            plane_copy(item, step, 4, above, by_x, size, beside),
        ]

    def kin(item, step):
        index, start, size = items[item]
        if step == 0:
            source = ins[index].at[:, pl.ds(start, size)]
        else:
            source = spread(outs[index], up_line(step), start, size)
        return pltpu.make_async_remote_copy(
            source,
            spread(outs[index], up_line(step), start, size),
            kin_send.at[item, step],
            kin_recv.at[item, step],
            device_id=(section_at, sibling),
            device_id_type=MESH,
        )

    def own(item):
        index, start, size = items[item]
        return pltpu.make_async_copy(
            ins[index].at[:, pl.ds(start, size)],
            spread(outs[index], batch_at, start, size),
            own_sem.at[item],
        )

    steps = range(1, line)
    total = len(items)
    started = []

    def launch(copies):
        for copy in copies:
            copy.start()
        started.extend(copies)

    for item in range(min(AHEAD, total)):
        launch([line_copy(item, step) for step in steps])
    for moment in range(total + 2):
        if moment + AHEAD < total:
            launch([line_copy(moment + AHEAD, step) for step in steps])
        if moment < total:
            for step in steps:
                line_copy(moment, step).wait_recv()
                launch(near(moment, step))
            own(moment).start()
            launch([kin(moment, 0)])
        if 0 <= moment - 1 < total:
            for step in steps:
                for copy, onward in zip(near(moment - 1, step), far(moment - 1, step)):
                    copy.wait_recv()
                    launch([onward])
        if 0 <= moment - 2 < total:
            for step in steps:
                for copy in far(moment - 2, step):
                    copy.wait_recv()
                launch([kin(moment - 2, step)])
    for item in range(total):
        own(item).wait()
        for step in range(line):
            kin(item, step).wait_recv()
    for copy in started:
        copy.wait_send()


def gather_all(blocks):
    widths = tuple(block.shape[1] for block in blocks)
    line = lax.axis_size("batch") // 2
    total = sum(-(-width // GATHER_WIDTH) for width in widths)
    full = blocks[0].shape[0] * line * 2
    anywhere = pl.BlockSpec(memory_space=pl.ANY)
    return pl.pallas_call(
        functools.partial(gather_kernel, widths),
        out_shape=[jax.ShapeDtypeStruct((full, width), BF) for width in widths],
        in_specs=[anywhere] * len(blocks),
        out_specs=[anywhere] * len(blocks),
        scratch_shapes=[
            pltpu.SemaphoreType.DMA((total,)),
            pltpu.SemaphoreType.DMA((5, total, line)),
            pltpu.SemaphoreType.DMA((5, total, line)),
            pltpu.SemaphoreType.DMA((total, line)),
            pltpu.SemaphoreType.DMA((total, line)),
        ],
        compiler_params=pltpu.CompilerParams(collective_id=1, has_side_effects=True),
    )(*blocks)


JOBS = (4096, 4096, 1024, 2048, 1024) * 2
ITEMS = (
    ((0, 0), (0, 1024)),
    ((0, 2048), (0, 3072)),
    ((1, 0), (1, 1024)),
    ((1, 2048), (1, 3072)),
    ((3, 0), (3, 1024)),
    ((2, 0), (4, 0)),
    ((5, 0), (5, 1024)),
    ((5, 2048), (5, 3072)),
    ((6, 0), (6, 1024)),
    ((6, 2048), (6, 3072)),
    ((8, 0), (8, 1024)),
    ((7, 0), (9, 0)),
)
HALF = 1024
KEPT = 512
WINDOWS = 4
STAGES = 3


def reduce_kernel(*refs):
    jobs = len(JOBS)
    total = len(ITEMS)
    lefts, rights = refs[:jobs], refs[jobs : 2 * jobs]
    last_ref, first_ref, point_ref, small_ref = refs[2 * jobs : 2 * jobs + 4]
    rest = refs[2 * jobs + 4 :]
    (sum_out, last_out, first_out, point_out, small_out, kin_left, kin_right) = rest[:7]
    (
        lwin,
        rwin,
        stage,
        merged,
        passing,
        lined,
        crossed,
        settled,
        point_in,
        point_sum,
        small_in,
        small_sum,
        kin_sems,
        win_sems,
        xy_sems,
        line_send,
        line_recv,
        cross_sems,
        out_sems,
        own_sems,
        lat_sems,
        far_sems,
        lat_own,
        point_sems,
        deal_sems,
        point_own,
        small_sems,
    ) = rest[7:]
    section_at = lax.axis_index("section")
    batch_at = lax.axis_index("batch")
    core = lax.rem(batch_at, 2)
    spot = batch_at // 2
    x_at = lax.rem(section_at, 2)
    y_at = section_at // 2
    beside = section_at + 1 - 2 * x_at
    above = lax.rem(section_at + 2, 4)
    across = lax.rem(beside + 2, 4)
    sibling = batch_at + 1 - 2 * core
    flat = (beside, above)

    peers = [(beside, batch_at), (above, batch_at), (across, batch_at), (section_at, sibling)]
    peers += [(section_at, lax.rem(spot + step, 4) * 2 + core) for step in (1, 2, 3)]
    barrier = pltpu.get_barrier_semaphore()
    for peer in peers:
        pl.semaphore_signal(barrier, inc=1, device_id=peer, device_id_type=MESH)
    pl.semaphore_wait(barrier, len(peers))

    def remote(source, target, sems, place, peer):
        return pltpu.make_async_remote_copy(
            source,
            target,
            sems.at[(0, *place)],
            sems.at[(1, *place)],
            device_id=peer,
            device_id_type=MESH,
        )

    starts = [sum(JOBS[:job]) for job in range(jobs)]

    def kin_copies(job):
        columns = pl.ds(starts[job], JOBS[job])
        return (
            remote(
                lefts[job].at[:, 1 - core],
                kin_left.at[job],
                kin_sems,
                (job, 0),
                (section_at, sibling),
            ),
            remote(
                rights[job],
                kin_right.at[:, columns],
                kin_sems,
                (job, 1),
                (section_at, sibling),
            ),
        )

    def small_copy(phase):
        if phase == 0:
            peer = (section_at, sibling)
        elif phase < 3:
            peer = (flat[phase - 1], batch_at)
        else:
            peer = (section_at, lax.rem(spot + phase - 2, 4) * 2 + core)
        return remote(
            small_sum.at[min(phase, 3)], small_in.at[phase], small_sems, (phase,), peer
        )

    quarter = point_ref.shape[0] // 4

    def point_copy(which):
        peer = (beside, above, across)[which]
        return remote(
            point_ref.at[pl.ds(pl.multiple_of(peer * quarter, quarter), quarter)],
            point_in.at[which],
            point_sems,
            (which,),
            (peer, batch_at),
        )

    def point_deal(which):
        peer = (beside, above, across)[which]
        return remote(
            point_sum,
            point_out.at[pl.ds(pl.multiple_of(section_at * quarter, quarter), quarter)],
            deal_sems,
            (which,),
            (peer, batch_at),
        )

    rows = last_ref.shape[0]
    pairs = ((last_ref, last_out), (first_ref, first_out))

    def lat_copy(which, way):
        source, target = pairs[which]
        return remote(
            source,
            target.at[pl.ds(pl.multiple_of(section_at * rows, rows), rows)],
            lat_sems,
            (which, way),
            (flat[way], batch_at),
        )

    def lat_far(which, way):
        target = pairs[which][1]
        first = flat[way] * rows + way * (rows // 2)
        part = target.at[pl.ds(pl.multiple_of(first, rows // 2), rows // 2)]
        return remote(part, part, far_sems, (which, way), (flat[1 - way], batch_at))

    def lat_local(which):
        source, target = pairs[which]
        return pltpu.make_async_copy(
            source,
            target.at[pl.ds(pl.multiple_of(section_at * rows, rows), rows)],
            lat_own.at[which],
        )

    def point_local():
        return pltpu.make_async_copy(
            point_sum,
            point_out.at[pl.ds(pl.multiple_of(section_at * quarter, quarter), quarter)],
            point_own.at[0],
        )

    def window_copies(item):
        slot = item % WINDOWS
        copies = []
        for side in range(2):
            job, start = ITEMS[item][side]
            here = pl.ds(side * HALF, HALF)
            copies += [
                pltpu.make_async_copy(
                    lefts[job].at[:, core],
                    lwin.at[slot, side, :, :, pl.ds(0, 256)],
                    win_sems.at[slot, side, 0],
                ),
                pltpu.make_async_copy(
                    kin_left.at[job],
                    lwin.at[slot, side, :, :, pl.ds(256, 256)],
                    win_sems.at[slot, side, 1],
                ),
                pltpu.make_async_copy(
                    rights[job].at[:, pl.ds(start, HALF)],
                    rwin.at[slot, pl.ds(0, 256), here],
                    win_sems.at[slot, side, 2],
                ),
                pltpu.make_async_copy(
                    kin_right.at[:, pl.ds(starts[job] + start, HALF)],
                    rwin.at[slot, pl.ds(256, 256), here],
                    win_sems.at[slot, side, 3],
                ),
            ]
        return copies

    seen = set()
    fresh = []
    for item in range(total):
        fresh.append([])
        for job, _ in ITEMS[item]:
            if job not in seen:
                seen.add(job)
                fresh[item].append(job)

    def load(item):
        for job in fresh[item]:
            for copy in kin_copies(job):
                copy.wait_recv()
        for copy in window_copies(item):
            copy.start()

    def loaded(slot):
        for side in range(2):
            job = 0
            for which, (source, target) in enumerate(
                (
                    (lefts[job].at[:, core], lwin.at[slot, side, :, :, pl.ds(0, 256)]),
                    (kin_left.at[job], lwin.at[slot, side, :, :, pl.ds(256, 256)]),
                    (
                        rights[job].at[:, pl.ds(0, HALF)],
                        rwin.at[slot, pl.ds(0, 256), pl.ds(side * HALF, HALF)],
                    ),
                    (
                        kin_right.at[:, pl.ds(0, HALF)],
                        rwin.at[slot, pl.ds(256, 256), pl.ds(side * HALF, HALF)],
                    ),
                )
            ):
                pltpu.make_async_copy(source, target, win_sems.at[slot, side, which]).wait()

    bits = (x_at, y_at)

    def product(slot, side, bit, upper):
        left = lwin[slot, side, pl.ds(upper * 2, 2)].reshape(256, 512)
        first = pl.multiple_of(side * HALF + bit * KEPT, KEPT)
        right = rwin[slot, :, pl.ds(first, KEPT)]
        return jnp.dot(left, right, preferred_element_type=F32).reshape(2, 128, KEPT)

    def xy_copy(item, side):
        here = pl.ds(side * KEPT, KEPT)
        return remote(
            stage.at[lax.rem(item, STAGES), :, :, here],
            merged.at[item, :, :, here],
            xy_sems,
            (item, side),
            (flat[side], batch_at),
        )

    def offer(item):
        slot = lax.rem(item, WINDOWS)
        loaded(slot)

        @pl.when(item >= STAGES)
        def _():
            for side in range(2):
                xy_copy(item - STAGES, side).wait_send()

        for side in range(2):

            def half(upper, carry):
                tile = product(slot, side, 1 - bits[side], upper)
                stage[
                    lax.rem(item, STAGES), pl.ds(upper * 2, 2), :, side * KEPT : side * KEPT + KEPT
                ] = tile.astype(BF)
                return carry

            lax.fori_loop(0, 2, half, 0)
            xy_copy(item, side).start()

    def line_copy(item, dest, place, rightward):
        step = 1 if rightward else -1
        slot = 4 if not rightward and place - 1 == dest else dest
        return pltpu.make_async_remote_copy(
            merged.at[item, dest],
            passing.at[item, slot],
            line_send.at[item, dest],
            line_recv.at[item, slot],
            device_id=(section_at, batch_at + 2 * step),
            device_id_type=MESH,
        )

    def line_wait(item, slot):
        pltpu.make_async_remote_copy(
            merged.at[item, 0],
            passing.at[item, slot],
            line_send.at[item, 0],
            line_recv.at[item, slot],
            device_id=(section_at, sibling),
            device_id_type=MESH,
        ).wait_recv()

    def keep(item):
        slot = lax.rem(item, WINDOWS)
        for side in range(2):
            xy_copy(item, side).wait_recv()

            def half(upper, carry):
                here = (item, pl.ds(upper * 2, 2), slice(None), slice(side * KEPT, side * KEPT + KEPT))
                tile = product(slot, side, bits[side], upper)
                merged[here] = (tile + merged[here].astype(F32)).astype(BF)
                return carry

            lax.fori_loop(0, 2, half, 0)

        @pl.when(spot == 0)
        def _():
            for dest in (3, 2, 1):
                line_copy(item, dest, 0, True).start()

        @pl.when(spot == 3)
        def _():
            for dest in (0, 1, 2):
                line_copy(item, dest, 3, False).start()

    def relay(item, dest, place, rightward):
        line_wait(item, dest)
        merged[item, dest] = (
            merged[item, dest].astype(F32) + passing[item, dest].astype(F32)
        ).astype(BF)
        line_copy(item, dest, place, rightward).start()

    def second(item):
        @pl.when(spot == 1)
        def _():
            for dest in (3, 2):
                relay(item, dest, 1, True)

        @pl.when(spot == 2)
        def _():
            for dest in (0, 1):
                relay(item, dest, 2, False)

    def third(item):
        @pl.when(spot == 1)
        def _():
            relay(item, 0, 1, False)

        @pl.when(spot == 2)
        def _():
            relay(item, 3, 2, True)

    def cross_copy(item, side):
        here = pl.ds(side * KEPT, KEPT)
        return remote(
            lined.at[item, :, here],
            crossed.at[item, :, here],
            cross_sems,
            (item, side),
            (flat[1 - side], batch_at),
        )

    def close(item):
        @pl.when(spot == 0)
        def _():
            line_wait(item, 4)
            lined[item] = (
                merged[item, 0].astype(F32) + passing[item, 4].astype(F32)
            ).astype(BF)

        @pl.when(spot == 3)
        def _():
            line_wait(item, 3)
            lined[item] = (
                merged[item, 3].astype(F32) + passing[item, 3].astype(F32)
            ).astype(BF)

        for middle in (1, 2):

            @pl.when(spot == middle)
            def _():
                line_wait(item, middle)
                line_wait(item, 4)
                lined[item] = (
                    merged[item, middle].astype(F32)
                    + passing[item, middle].astype(F32)
                    + passing[item, 4].astype(F32)
                ).astype(BF)

        for side in range(2):
            cross_copy(item, side).start()

    def out_place(item, side, bit):
        first = pl.multiple_of(item * (2 * HALF) + side * HALF + bit * KEPT, KEPT)
        return sum_out.at[:, pl.ds(first, KEPT)]

    def out_copy(item, side):
        return remote(
            settled.at[item, :, pl.ds(side * KEPT, KEPT)],
            out_place(item, side, bits[side]),
            out_sems,
            (item, side),
            (flat[side], batch_at),
        )

    def out_local(item, side):
        return pltpu.make_async_copy(
            settled.at[item, :, pl.ds(side * KEPT, KEPT)],
            out_place(item, side, bits[side]),
            own_sems.at[item, side],
        )

    def finish(item):
        for side in range(2):
            cross_copy(item, side).wait_recv()
        settled[item] = (lined[item].astype(F32) + crossed[item].astype(F32)).astype(BF)
        for side in range(2):
            out_copy(item, side).start()
            out_local(item, side).start()

    for job in range(2):
        for copy in kin_copies(job):
            copy.start()
    small_sum[0] = small_ref[...]
    small_copy(0).start()
    for which in range(2):
        lat_local(which).start()
        for way in range(2):
            lat_copy(which, way).start()
    for which in range(3):
        point_copy(which).start()
    for job in range(2, jobs):
        for copy in kin_copies(job):
            copy.start()
    load(0)

    def sidework(moment):
        @pl.when(moment == 2)
        def _():
            for which in range(2):
                for way in range(2):
                    lat_copy(which, way).wait_recv()
                    lat_far(which, way).start()
            for which in range(3):
                point_copy(which).wait_recv()
            gathered = point_ref[
                pl.ds(pl.multiple_of(section_at * quarter, quarter), quarter)
            ].astype(F32)
            for which in range(3):
                gathered += point_in[which].astype(F32)
            point_sum[...] = gathered.astype(BF)
            point_local().start()
            for which in range(3):
                point_deal(which).start()

        for phase in range(3):

            @pl.when(moment == 2 + 2 * phase)
            def _():
                small_copy(phase).wait_recv()
                small_sum[phase + 1] = small_sum[phase] + small_in[phase]
                if phase < 2:
                    small_copy(phase + 1).start()
                else:
                    for step in range(3):
                        small_copy(3 + step).start()

        @pl.when(moment == 8)
        def _():
            for step in range(3):
                small_copy(3 + step).wait_recv()
            small_out[...] = (small_sum[3] + small_in[4]) + (small_in[3] + small_in[5])

    def moment_body(moment, carry):
        for item in range(1, total):
            pl.when(moment == item - 1)(functools.partial(load, item))

        pl.when(moment < total)(lambda: offer(moment))
        for lag, action in ((2, keep), (3, second), (4, third), (5, close), (6, finish)):
            pl.when(jnp.logical_and(moment >= lag, moment < total + lag))(
                functools.partial(action, moment - lag)
            )
        sidework(moment)
        return carry

    lax.fori_loop(0, total + 6, moment_body, 0)

    for job in range(jobs):
        for copy in kin_copies(job):
            copy.wait_send()
    for phase in range(6):
        small_copy(phase).wait_send()
    for which in range(2):
        lat_local(which).wait()
        for way in range(2):
            lat_copy(which, way).wait_send()
            lat_far(which, way).wait()
    point_local().wait()
    for which in range(3):
        point_copy(which).wait_send()
        point_deal(which).wait()

    def drain(item, carry):
        @pl.when(item >= total - STAGES)
        def _():
            for side in range(2):
                xy_copy(item, side).wait_send()

        for step in (1, 2, 3):
            dest = lax.rem(spot + step, 4)
            pltpu.make_async_remote_copy(
                merged.at[item, dest],
                passing.at[item, 0],
                line_send.at[item, dest],
                line_recv.at[item, 0],
                device_id=(section_at, sibling),
                device_id_type=MESH,
            ).wait_send()
        for side in range(2):
            cross_copy(item, side).wait_send()
            out_copy(item, side).wait()
            out_local(item, side).wait()
        return carry

    lax.fori_loop(0, total, drain, 0)


def reduce_all(lefts, rights, last, first, point_part, small):
    jobs = len(JOBS)
    total = len(ITEMS)
    columns = sum(JOBS)
    width = last.shape[1]
    anywhere = pl.BlockSpec(memory_space=pl.ANY)
    vmem = pl.BlockSpec(memory_space=pltpu.VMEM)
    lefts = [left.T.reshape(4, 2, 128, 256) for left in lefts]
    dma = pltpu.SemaphoreType.DMA
    flops = 2 * columns * 512 * 512 * 2
    return pl.pallas_call(
        reduce_kernel,
        out_shape=[
            jax.ShapeDtypeStruct((128, columns), BF),
            jax.ShapeDtypeStruct((4 * last.shape[0], width), BF),
            jax.ShapeDtypeStruct((4 * first.shape[0], width), BF),
            jax.ShapeDtypeStruct(point_part.shape, BF),
            jax.ShapeDtypeStruct(small.shape, F32),
            jax.ShapeDtypeStruct((jobs, 4, 128, 256), BF),
            jax.ShapeDtypeStruct((256, columns), BF),
        ],
        in_specs=[anywhere] * (2 * jobs + 2) + [vmem, vmem],
        out_specs=[anywhere] * 4 + [vmem] + [anywhere] * 2,
        scratch_shapes=[
            pltpu.VMEM((WINDOWS, 2, 4, 128, 512), BF),
            pltpu.VMEM((WINDOWS, 512, 2 * HALF), BF),
            pltpu.VMEM((STAGES, 4, 128, 2 * KEPT), BF),
            pltpu.VMEM((total, 4, 128, 2 * KEPT), BF),
            pltpu.VMEM((total, 5, 128, 2 * KEPT), BF),
            pltpu.VMEM((total, 128, 2 * KEPT), BF),
            pltpu.VMEM((total, 128, 2 * KEPT), BF),
            pltpu.VMEM((total, 128, 2 * KEPT), BF),
            pltpu.VMEM((3, point_part.shape[0] // 4, width), BF),
            pltpu.VMEM((point_part.shape[0] // 4, width), BF),
            pltpu.VMEM((6, *small.shape), F32),
            pltpu.VMEM((4, *small.shape), F32),
            dma((2, jobs, 2)),
            dma((WINDOWS, 2, 4)),
            dma((2, total, 2)),
            dma((total, 4)),
            dma((total, 5)),
            dma((2, total, 2)),
            dma((2, total, 2)),
            dma((total, 2)),
            dma((2, 2, 2)),
            dma((2, 2, 2)),
            dma((2,)),
            dma((2, 3)),
            dma((2, 3)),
            dma((1,)),
            dma((2, 6)),
        ],
        compiler_params=pltpu.CompilerParams(
            collective_id=2, has_side_effects=True, vmem_limit_bytes=60 * 2**20
        ),
        cost_estimate=pl.CostEstimate(flops=flops, bytes_accessed=2**26, transcendentals=0),
    )(*lefts, *rights, last, first, point_part, small)[:5]


def per_device(
    latents,
    points,
    neighbours,
    lengths,
    cross_proj,
    cross_out,
    cross_gains,
    self_proj,
    self_out,
    self_gain,
    mlp_gain,
    mlp_in,
    mlp_in_bias,
    mlp_down,
    mlp_out_bias,
    cotangent,
):
    sections = lax.axis_size("section")
    section_at = lax.axis_index("section")
    width = latents.shape[1]
    hidden = mlp_in.shape[2]
    groups_dev = neighbours.shape[0]
    rows = latents.shape[0] // sections
    shard = cross_out.shape[0]
    piece = shard // sections
    groups_all = groups_dev * lax.axis_size("batch")

    def gathered(block):
        own = lax.dynamic_slice_in_dim(block, section_at * piece, piece, 0)
        return lax.all_gather(own, ALL, axis=0, tiled=True)

    vectors = jnp.concatenate(
        [
            cross_gains.reshape(-1),
            self_gain,
            mlp_gain.reshape(-1),
            mlp_out_bias.reshape(-1),
            mlp_in_bias.reshape(-1),
        ]
    ).reshape(-1, shard)
    spread = lax.all_gather(vectors, "batch", axis=0, tiled=False).astype(F32)

    def vector(first, count):
        return spread[:, first : first + count].reshape(-1)

    gains_cross = (vector(0, 1), vector(1, 1))
    gain_self = vector(2, 1)
    gains_mlp = (vector(3, 1), vector(4, 1))
    biases_out = (vector(5, 1), vector(6, 1))
    per_bias = hidden // width
    biases_in = (vector(7, per_bias), vector(7 + per_bias, per_bias))

    blocks = [
        cross_proj.reshape(shard, 3 * width),
        cross_out,
        mlp_in[0],
        mlp_down[0],
        self_proj.reshape(shard, 3 * width),
        self_out,
        mlp_in[1],
        mlp_down[1],
    ]
    small_slice = lax.axis_size("batch") == 8
    full = gather_all(blocks) if small_slice else [gathered(block) for block in blocks]
    proj_c, out_c, in_0, down_0, proj_s, out_s, in_1, down_1 = full

    mine = lax.dynamic_slice_in_dim(latents, section_at * rows, rows, 0).astype(F32)
    cot = lax.dynamic_slice_in_dim(cotangent, section_at * rows, rows, 0).astype(F32)
    listed = lax.dynamic_index_in_dim(neighbours, section_at, 0, keepdims=False)
    length = lax.dynamic_index_in_dim(lengths, section_at, 0, keepdims=False)
    valid = jnp.arange(listed.shape[0], dtype=jnp.int32) < length
    picks = listed[:, None] == jnp.arange(points.shape[0], dtype=jnp.int32)[None, :]
    picks = picks.astype(BF)
    source = mm(picks, points)

    u1, kept_c = attend(mine, source, valid, gains_cross[0], gains_cross[1], proj_c, out_c)
    u2, kept_0 = feed(u1.astype(F32), gains_mlp[0], in_0, biases_in[0], down_0, biases_out[0])
    u2 = u2.astype(F32)
    u3, kept_s = attend(u2, u2, None, gain_self, gain_self, proj_s, out_s)
    u4, kept_1 = feed(u3.astype(F32), gains_mlp[1], in_1, biases_in[1], down_1, biases_out[1])
    final = u4.astype(F32)
    group_norm = jnp.sqrt(jnp.mean(final * final) + EPSILON)
    norm_mean = lax.psum(group_norm, ALL) / groups_all

    g4 = (cot + (norm_mean / group_norm) * final).astype(BF)
    dx, gain_1_grad, bias_1_grad, ob_1_grad, pairs_1 = feed_back(
        g4, kept_1, gains_mlp[1], in_1, down_1
    )
    g3 = (g4.astype(F32) + dx).astype(BF)
    dx, ds, gq, gkv, pairs_s = attend_back(g3, kept_s, gain_self, gain_self, proj_s, out_s)
    gain_s_grad = gq + gkv
    g2 = (g3.astype(F32) + dx + ds).astype(BF)
    dx, gain_0_grad, bias_0_grad, ob_0_grad, pairs_0 = feed_back(
        g2, kept_0, gains_mlp[0], in_0, down_0
    )
    g1 = (g2.astype(F32) + dx).astype(BF)
    dx, ds, cq_grad, ckv_grad, pairs_c = attend_back(
        g1, kept_c, gains_cross[0], gains_cross[1], proj_c, out_c
    )
    g0 = (g1.astype(F32) + dx).astype(BF)
    high = ds.astype(BF)
    low = (ds - high.astype(F32)).astype(BF)
    point_part = (mm_rows(picks, high) + mm_rows(picks, low)).astype(BF)
    small = jnp.concatenate(
        [
            cq_grad,
            ckv_grad,
            gain_s_grad,
            gain_0_grad,
            gain_1_grad,
            ob_0_grad,
            ob_1_grad,
            bias_0_grad,
            bias_1_grad,
            jnp.zeros_like(cq_grad),
        ]
    ).reshape(-1, width)
    pairs = pairs_1 + pairs_s + pairs_0 + pairs_c
    lefts, rights = [pair[0] for pair in pairs], [pair[1] for pair in pairs]
    if small_slice:
        sums, latents_out, g0_all, points_sum, small = reduce_all(
            lefts, rights, u4, g0, point_part, small
        )

        def block(first, size):
            return sums[:, first : first + size].astype(F32)

        def layer(first):
            grads = [block(first, hidden), block(first + hidden, hidden)]
            query = block(first + 2 * hidden + 2 * width, width)
            both = block(first + 2 * hidden, 2 * width)
            grads.append(jnp.concatenate([query, both], axis=1))
            grads.append(block(first + 2 * hidden + 3 * width, width))
            return grads

        in_1_grad, down_1_grad, proj_s_grad, out_s_grad = layer(0)
        in_0_grad, down_0_grad, proj_c_grad, out_c_grad = layer(2 * hidden + 4 * width)
    else:

        def settled_grad(left, right):
            part = lax.psum_scatter(
                mm_rows(left, right).astype(BF), ALL, scatter_dimension=0, tiled=True
            )
            return lax.all_gather(part, "section", axis=0, tiled=True).astype(F32)

        done = [settled_grad(left, right) for left, right in pairs]
        in_1_grad, down_1_grad, q_s, kv_s, out_s_grad = done[:5]
        in_0_grad, down_0_grad, q_c, kv_c, out_c_grad = done[5:]
        proj_s_grad = jnp.concatenate([q_s, kv_s], axis=1)
        proj_c_grad = jnp.concatenate([q_c, kv_c], axis=1)
        points_sum = lax.psum(point_part, "section")
        latents_out = lax.all_gather(u4, "section", axis=0, tiled=True)
        g0_all = lax.all_gather(g0, "section", axis=0, tiled=True)
        small = lax.psum(small, ALL)
    points_grad = points_sum.astype(F32)
    latents_grad = g0_all.astype(F32)
    batch_at = lax.axis_index("batch")

    def own(first, count):
        flat = small[first : first + count].reshape(-1)
        size = flat.shape[0] // lax.axis_size("batch")
        return lax.dynamic_slice_in_dim(flat, batch_at * size, size, 0)

    return (
        latents_out,
        latents_grad,
        points_grad,
        proj_c_grad.reshape(shard, 3, width),
        out_c_grad,
        jnp.stack([own(0, 1), own(1, 1)]),
        proj_s_grad.reshape(shard, 3, width),
        out_s_grad,
        own(2, 1),
        jnp.stack([own(3, 1), own(4, 1)]),
        jnp.stack([in_0_grad, in_1_grad]),
        jnp.stack([own(7, per_bias), own(7 + per_bias, per_bias)]),
        jnp.stack([down_0_grad, down_1_grad]),
        jnp.stack([own(5, 1), own(6, 1)]),
        norm_mean,
    )


def solution(mesh):
    rows = P("batch", None)
    cols = P(None, "batch")
    block = P("batch", None, None)
    pair = P(None, "batch", None)
    return jax.shard_map(
        per_device,
        mesh=mesh,
        in_specs=(
            rows,
            rows,
            rows,
            P("batch"),
            block,
            rows,
            cols,
            block,
            rows,
            P("batch"),
            cols,
            pair,
            cols,
            pair,
            cols,
            rows,
        ),
        out_specs=(
            rows,
            rows,
            rows,
            block,
            rows,
            cols,
            block,
            rows,
            P("batch"),
            cols,
            pair,
            cols,
            pair,
            cols,
            P(),
        ),
        check_vma=False,
    )
```

```python
import functools
import math

import jax
import jax.numpy as jnp
from jax import lax
from jax.experimental import pallas as pl
from jax.experimental.pallas import tpu as pltpu
from jax.sharding import PartitionSpec as P

HD = 128
EPSILON = 1e-05
MASKED = -1e30
BF = jnp.bfloat16
F32 = jnp.float32
ALL = ("batch", "section")
MESH = pl.DeviceIdType.MESH
GATHER_WIDTH = 1024
AHEAD = 4


def mm(a, b):
    return jnp.dot(a, b, preferred_element_type=F32)


def mm_rows(a, b):
    return lax.dot_general(a, b, (((0,), (0,)), ((), ())), preferred_element_type=F32)


def mm_cols(a, b):
    return lax.dot_general(a, b, (((1,), (1,)), ((), ())), preferred_element_type=F32)


def unit_rows(values):
    centred = values - jnp.mean(values, axis=-1, keepdims=True)
    inverse = lax.rsqrt(jnp.mean(centred * centred, axis=-1, keepdims=True) + EPSILON)
    return centred * inverse, inverse


def norm_back(gradient, unit, inverse, gain):
    scaled = gradient * gain
    inner = (
        scaled
        - jnp.mean(scaled, axis=-1, keepdims=True)
        - unit * jnp.mean(scaled * unit, axis=-1, keepdims=True)
    )
    return inverse * inner, jnp.sum(gradient * unit, axis=0)


def heads_of(rows):
    return rows.reshape(rows.shape[0], -1, HD)


def attend(inputs, source, valid, gain_q, gain_kv, proj, out):
    unit_x, inv_x = unit_rows(inputs)
    queries_in = (unit_x * gain_q).astype(BF)
    unit_s, inv_s = unit_rows(source)
    keys_in = (unit_s * gain_kv).astype(BF)
    width = inputs.shape[1]
    q = mm(queries_in, proj[:, :width]).astype(BF)
    kv = mm(keys_in, proj[:, width:]).astype(BF)
    k, v = kv[:, :width], kv[:, width:]
    scores = jnp.einsum(
        "lhc,nhc->hln", heads_of(q), heads_of(k), preferred_element_type=F32
    ) * (1.0 / math.sqrt(HD))
    if valid is not None:
        scores = jnp.where(valid[None, None, :], scores, MASKED)
    grown = jnp.exp(scores - jnp.max(scores, axis=-1, keepdims=True))
    soft = grown / jnp.sum(grown, axis=-1, keepdims=True)
    mixture = jnp.einsum("hln,nhc->lhc", soft.astype(BF), heads_of(v), preferred_element_type=F32)
    mixture = mixture.reshape(inputs.shape).astype(BF)
    result = (inputs + mm(mixture, out)).astype(BF)
    return result, (unit_x, inv_x, queries_in, unit_s, inv_s, keys_in, q, k, v, soft, mixture)


def attend_back(gradient, kept, gain_q, gain_kv, proj, out):
    unit_x, inv_x, queries_in, unit_s, inv_s, keys_in, q, k, v, soft, mixture = kept
    width = gradient.shape[1]
    scale = 1.0 / math.sqrt(HD)
    grad_mix = mm_cols(gradient, out).astype(BF)
    grad_soft = jnp.einsum(
        "lhc,nhc->hln", heads_of(grad_mix), heads_of(v), preferred_element_type=F32
    )
    inner = jnp.sum(soft * grad_soft, axis=-1, keepdims=True)
    grad_scores = (soft * (grad_soft - inner)).astype(BF)
    dq = jnp.einsum("hln,nhc->lhc", grad_scores, heads_of(k), preferred_element_type=F32) * scale
    dk = jnp.einsum("hln,lhc->nhc", grad_scores, heads_of(q), preferred_element_type=F32) * scale
    dv = jnp.einsum(
        "hln,lhc->nhc", soft.astype(BF), heads_of(grad_mix), preferred_element_type=F32
    )
    dq = dq.reshape(gradient.shape).astype(BF)
    dk = dk.reshape(-1, width).astype(BF)
    dv = dv.reshape(-1, width).astype(BF)
    grad_x, gain_q_grad = norm_back(mm_cols(dq, proj[:, :width]), unit_x, inv_x, gain_q)
    back_s = mm_cols(dk, proj[:, width : 2 * width]) + mm_cols(dv, proj[:, 2 * width :])
    grad_s, gain_kv_grad = norm_back(back_s, unit_s, inv_s, gain_kv)
    pairs = ((queries_in, dq), (keys_in, dk), (keys_in, dv), (mixture, gradient))
    return grad_x, grad_s, gain_q_grad, gain_kv_grad, pairs


def feed(inputs, gain, w_in, b_in, w_down, b_out):
    unit, inverse = unit_rows(inputs)
    lowered = (unit * gain).astype(BF)
    pre_act = mm(lowered, w_in) + b_in
    active = jax.nn.gelu(pre_act).astype(BF)
    result = (inputs + mm_cols(active, w_down) + b_out).astype(BF)
    return result, (unit, inverse, lowered, pre_act, active)


def feed_back(gradient, kept, gain, w_in, w_down):
    unit, inverse, lowered, pre_act, active = kept
    grad_act = mm(gradient, w_down)
    grad_pre = jax.vjp(jax.nn.gelu, pre_act)[1](grad_act)[0].astype(BF)
    grad_x, gain_grad = norm_back(mm_cols(grad_pre, w_in), unit, inverse, gain)
    bias_grad = jnp.sum(grad_pre.astype(F32), axis=0)
    out_grad = jnp.sum(gradient.astype(F32), axis=0)
    return grad_x, gain_grad, bias_grad, out_grad, ((lowered, grad_pre), (gradient, active))


def gather_kernel(widths, *refs):
    cross_proj, cross_out, mlp_in, mlp_down, self_proj, self_out, vec_in = refs[:7]
    ins = (
        cross_proj,
        cross_out,
        mlp_in.at[0],
        mlp_down.at[0],
        self_proj,
        self_out,
        mlp_in.at[1],
        mlp_down.at[1],
    )
    count = len(widths)
    outs, vec_out = refs[7 : 7 + count], refs[7 + count]
    (own_sem, send, recv, kin_send, kin_recv, vec_sems) = refs[8 + count :]
    section_at = lax.axis_index("section")
    batch_at = lax.axis_index("batch")
    line = lax.axis_size("batch") // 2
    core = lax.rem(batch_at, 2)
    spot = batch_at // 2
    beside = section_at + 1 - 2 * lax.rem(section_at, 2)
    above = lax.rem(section_at + 2, 4)
    across = lax.rem(beside + 2, 4)
    sibling = batch_at + 1 - 2 * core
    shard = ins[0].shape[0]

    def down_line(step):
        return lax.rem(spot + step, line) * 2 + core

    def up_line(step):
        return lax.rem(spot + line - step, line) * 2 + core

    peers = [(beside, batch_at), (above, batch_at), (section_at, sibling)]
    peers += [(section_at, down_line(step)) for step in range(1, line)]
    peers += [(section_at, down_line(step) + 1 - 2 * core) for step in range(1, line)]
    barrier = pltpu.get_barrier_semaphore()
    for peer in peers:
        pl.semaphore_signal(barrier, inc=1, device_id=peer, device_id_type=MESH)
    pl.semaphore_wait(barrier, len(peers))

    items = [
        (index, start, min(GATHER_WIDTH, width - start))
        for index, width in enumerate(widths)
        for start in range(0, width, GATHER_WIDTH)
    ]

    def spread(ref, owner, first, size):
        return ref.at[pl.ds(pl.multiple_of(owner * shard, shard), shard), pl.ds(first, size)]

    def part(item, quarter):
        _, start, size = items[item]
        return pl.multiple_of(start + quarter * (size // 4), 128), size // 4

    def line_copy(item, step):
        index = items[item][0]
        first, size = part(item, section_at)
        return pltpu.make_async_remote_copy(
            ins[index].at[:, pl.ds(first, size)],
            spread(outs[index], batch_at, first, size),
            send.at[0, item, step],
            recv.at[0, item, step],
            device_id=(section_at, down_line(step)),
            device_id_type=MESH,
        )

    def plane_copy(item, step, way, quarter, low, size, peer):
        index = items[item][0]
        ref = spread(outs[index], up_line(step), low, size)
        return pltpu.make_async_remote_copy(
            ref,
            ref,
            send.at[way, item, step],
            recv.at[way, item, step],
            device_id=(peer, batch_at),
            device_id_type=MESH,
        )

    def near(item, step):
        first, size = part(item, section_at)
        return [
            plane_copy(item, step, 1, section_at, first, size, beside),
            plane_copy(item, step, 2, section_at, first, size, above),
        ]

    def far(item, step):
        size = items[item][2] // 8
        by_y, _ = part(item, beside)
        by_x, _ = part(item, above)
        by_x = pl.multiple_of(by_x + size, 128)
        return [
            plane_copy(item, step, 3, beside, by_y, size, above),
            plane_copy(item, step, 4, above, by_x, size, beside),
        ]

    def kin(item, step):
        index, start, size = items[item]
        if step == 0:
            source = ins[index].at[:, pl.ds(start, size)]
        else:
            source = spread(outs[index], up_line(step), start, size)
        return pltpu.make_async_remote_copy(
            source,
            spread(outs[index], up_line(step), start, size),
            kin_send.at[item, step],
            kin_recv.at[item, step],
            device_id=(section_at, sibling),
            device_id_type=MESH,
        )

    def own(item):
        index, start, size = items[item]
        return pltpu.make_async_copy(
            ins[index].at[:, pl.ds(start, size)],
            spread(outs[index], batch_at, start, size),
            own_sem.at[item],
        )

    def vec_copy(which):
        return pltpu.make_async_remote_copy(
            vec_in,
            vec_out.at[batch_at],
            vec_sems.at[0, which],
            vec_sems.at[1, which],
            device_id=peers[2 + which],
            device_id_type=MESH,
        )

    steps = range(1, line)
    total = len(items)
    started = []

    def launch(copies):
        for copy in copies:
            copy.start()
        started.extend(copies)

    for item in range(min(AHEAD, total)):
        launch([line_copy(item, step) for step in steps])
    vec_out[batch_at] = vec_in[...]
    for which in range(2 * line - 1):
        vec_copy(which).start()
    for moment in range(total + 2):
        if moment + AHEAD < total:
            launch([line_copy(moment + AHEAD, step) for step in steps])
        if moment < total:
            for step in steps:
                line_copy(moment, step).wait_recv()
                launch(near(moment, step))
            own(moment).start()
            launch([kin(moment, 0)])
        if 0 <= moment - 1 < total:
            for step in steps:
                for copy, onward in zip(near(moment - 1, step), far(moment - 1, step)):
                    copy.wait_recv()
                    launch([onward])
        if 0 <= moment - 2 < total:
            for step in steps:
                for copy in far(moment - 2, step):
                    copy.wait_recv()
                launch([kin(moment - 2, step)])
    for item in range(total):
        own(item).wait()
        for step in range(line):
            kin(item, step).wait_recv()
    for which in range(2 * line - 1):
        vec_copy(which).wait()
    for copy in started:
        copy.wait_send()


def gather_all(blocks, vectors):
    wide, feed_wide = blocks[0].shape[1], blocks[2].shape[2]
    thin = blocks[1].shape[1]
    widths = (wide, thin, feed_wide, feed_wide) * 2
    line = lax.axis_size("batch") // 2
    total = sum(-(-width // GATHER_WIDTH) for width in widths)
    full = blocks[0].shape[0] * line * 2
    anywhere = pl.BlockSpec(memory_space=pl.ANY)
    vmem = pl.BlockSpec(memory_space=pltpu.VMEM)
    return pl.pallas_call(
        functools.partial(gather_kernel, widths),
        out_shape=[jax.ShapeDtypeStruct((full, width), BF) for width in widths]
        + [jax.ShapeDtypeStruct((2 * line, *vectors.shape), BF)],
        in_specs=[anywhere] * len(blocks) + [vmem],
        out_specs=[anywhere] * len(widths) + [vmem],
        scratch_shapes=[
            pltpu.SemaphoreType.DMA((total,)),
            pltpu.SemaphoreType.DMA((5, total, line)),
            pltpu.SemaphoreType.DMA((5, total, line)),
            pltpu.SemaphoreType.DMA((total, line)),
            pltpu.SemaphoreType.DMA((total, line)),
            pltpu.SemaphoreType.DMA((2, 2 * line - 1)),
        ],
        compiler_params=pltpu.CompilerParams(collective_id=1, has_side_effects=True),
    )(*blocks, vectors)


def norm_kernel(value_ref, out_ref, plane, line_in, plane_sems, line_sems):
    section_at = lax.axis_index("section")
    batch_at = lax.axis_index("batch")
    core = lax.rem(batch_at, 2)
    spot = batch_at // 2
    place = section_at * 2 + core
    near = []
    for turn in range(1, 8):
        other = lax.rem(place + turn, 8)
        near.append((other // 2, spot * 2 + lax.rem(other, 2)))
    far = [(section_at, lax.rem(spot + step, 4) * 2 + core) for step in (1, 2, 3)]
    barrier = pltpu.get_barrier_semaphore()
    for peer in near + far:
        pl.semaphore_signal(barrier, inc=1, device_id=peer, device_id_type=MESH)
    pl.semaphore_wait(barrier, len(near) + len(far))

    def near_copy(turn):
        return pltpu.make_async_remote_copy(
            value_ref,
            plane.at[place],
            plane_sems.at[0, turn],
            plane_sems.at[1, turn],
            device_id=near[turn],
            device_id_type=MESH,
        )

    def far_copy(step):
        return pltpu.make_async_remote_copy(
            out_ref,
            line_in.at[spot],
            line_sems.at[0, step],
            line_sems.at[1, step],
            device_id=far[step],
            device_id_type=MESH,
        )

    for turn in range(7):
        near_copy(turn).start()
    plane[place] = value_ref[...]
    for turn in range(7):
        near_copy(turn).wait()
    out_ref[...] = jnp.sum(plane[...], axis=0)
    for step in range(3):
        far_copy(step).start()
    line_in[spot] = out_ref[...]
    for step in range(3):
        far_copy(step).wait()
    out_ref[...] = jnp.sum(line_in[...], axis=0)


def norm_sum(value):
    vmem = pl.BlockSpec(memory_space=pltpu.VMEM)
    tile = jnp.broadcast_to(value, (8, 128))
    return pl.pallas_call(
        norm_kernel,
        out_shape=jax.ShapeDtypeStruct((8, 128), F32),
        in_specs=[vmem],
        out_specs=vmem,
        scratch_shapes=[
            pltpu.VMEM((8, 8, 128), F32),
            pltpu.VMEM((4, 8, 128), F32),
            pltpu.SemaphoreType.DMA((2, 7)),
            pltpu.SemaphoreType.DMA((2, 3)),
        ],
        compiler_params=pltpu.CompilerParams(collective_id=3, has_side_effects=True),
    )(tile)[0, 0]


JOBS = (4096, 4096, 1024, 1024, 1024, 1024) * 2
HALF = 512
KEPT = 256
BLOCKS = [(job, start) for job, width in enumerate(JOBS) for start in range(0, width, HALF)]
ITEMS = tuple(zip(BLOCKS[::2], BLOCKS[1::2]))
WINDOWS = 4
STAGES = 4


def reduce_kernel(*refs):
    jobs = len(JOBS)
    total = len(ITEMS)
    lefts, rights = refs[:jobs], refs[jobs : 2 * jobs]
    last_ref, first_ref, point_ref, small_ref = refs[2 * jobs : 2 * jobs + 4]
    rest = refs[2 * jobs + 4 :]
    (sum_out, last_out, first_out, point_out, small_out, kin_left, kin_right) = rest[:7]
    (
        lwin,
        raw,
        rwin,
        stage,
        merged,
        passing,
        lined,
        crossed,
        settled,
        point_in,
        point_sum,
        small_in,
        small_sum,
        kin_sems,
        kin_block_sems,
        raw_sems,
        win_sems,
        xy_sems,
        line_send,
        line_recv,
        cross_sems,
        out_sems,
        own_sems,
        lat_sems,
        far_sems,
        lat_own,
        point_sems,
        deal_sems,
        point_own,
        small_sems,
    ) = rest[7:]
    section_at = lax.axis_index("section")
    batch_at = lax.axis_index("batch")
    core = lax.rem(batch_at, 2)
    spot = batch_at // 2
    x_at = lax.rem(section_at, 2)
    y_at = section_at // 2
    beside = section_at + 1 - 2 * x_at
    above = lax.rem(section_at + 2, 4)
    across = lax.rem(beside + 2, 4)
    sibling = batch_at + 1 - 2 * core
    flat = (beside, above)

    peers = [(beside, batch_at), (above, batch_at), (across, batch_at), (section_at, sibling)]
    peers += [(section_at, lax.rem(spot + step, 4) * 2 + core) for step in (1, 2, 3)]
    barrier = pltpu.get_barrier_semaphore()
    for peer in peers:
        pl.semaphore_signal(barrier, inc=1, device_id=peer, device_id_type=MESH)
    pl.semaphore_wait(barrier, len(peers))

    def remote(source, target, sems, place, peer):
        return pltpu.make_async_remote_copy(
            source,
            target,
            sems.at[(0, *place)],
            sems.at[(1, *place)],
            device_id=peer,
            device_id_type=MESH,
        )

    starts = [sum(JOBS[:job]) for job in range(jobs)]

    def columns(spot_of, parity):
        return pl.ds(pl.multiple_of((2 * spot_of + parity) * 128, 128), 128)

    def kin_lefts(job):
        return [
            remote(
                lefts[job].at[:, columns(part, 1 - core)],
                kin_left.at[job, part],
                kin_sems,
                (job, part),
                (section_at, sibling),
            )
            for part in range(4)
        ]

    def kin_block(item, side):
        job, start = ITEMS[item][side]
        return remote(
            rights[job].at[:, pl.ds(start, HALF)],
            kin_right.at[:, pl.ds(starts[job] + start, HALF)],
            kin_block_sems,
            (item, side),
            (section_at, sibling),
        )

    def small_copy(phase):
        if phase == 0:
            peer = (section_at, sibling)
        elif phase < 3:
            peer = (flat[phase - 1], batch_at)
        else:
            peer = (section_at, lax.rem(spot + phase - 2, 4) * 2 + core)
        return remote(
            small_sum.at[min(phase, 3)], small_in.at[phase], small_sems, (phase,), peer
        )

    quarter = point_ref.shape[0] // 4

    def point_copy(which):
        peer = (beside, above, across)[which]
        return remote(
            point_ref.at[pl.ds(pl.multiple_of(peer * quarter, quarter), quarter)],
            point_in.at[which],
            point_sems,
            (which,),
            (peer, batch_at),
        )

    def point_deal(which):
        peer = (beside, above, across)[which]
        return remote(
            point_sum,
            point_out.at[pl.ds(pl.multiple_of(section_at * quarter, quarter), quarter)],
            deal_sems,
            (which,),
            (peer, batch_at),
        )

    rows = last_ref.shape[0]
    pairs = ((last_ref, last_out), (first_ref, first_out))

    def lat_copy(which, way):
        source, target = pairs[which]
        return remote(
            source,
            target.at[pl.ds(pl.multiple_of(section_at * rows, rows), rows)],
            lat_sems,
            (which, way),
            (flat[way], batch_at),
        )

    def lat_far(which, way):
        target = pairs[which][1]
        first = flat[way] * rows + way * (rows // 2)
        part = target.at[pl.ds(pl.multiple_of(first, rows // 2), rows // 2)]
        return remote(part, part, far_sems, (which, way), (flat[1 - way], batch_at))

    def lat_local(which):
        source, target = pairs[which]
        return pltpu.make_async_copy(
            source,
            target.at[pl.ds(pl.multiple_of(section_at * rows, rows), rows)],
            lat_own.at[which],
        )

    def point_local():
        return pltpu.make_async_copy(
            point_sum,
            point_out.at[pl.ds(pl.multiple_of(section_at * quarter, quarter), quarter)],
            point_own.at[0],
        )

    def window_copies(item):
        slot = item % WINDOWS
        copies = []
        for side in range(2):
            job, start = ITEMS[item][side]
            here = pl.ds(side * HALF, HALF)
            copies += [
                pltpu.make_async_copy(
                    rights[job].at[:, pl.ds(start, HALF)],
                    rwin.at[slot, pl.ds(0, 256), here],
                    win_sems.at[slot, side, 0],
                ),
                pltpu.make_async_copy(
                    kin_right.at[:, pl.ds(starts[job] + start, HALF)],
                    rwin.at[slot, pl.ds(256, 256), here],
                    win_sems.at[slot, side, 1],
                ),
            ]
        return copies

    def raw_copies(job):
        copies = []
        for part in range(4):
            copies += [
                pltpu.make_async_copy(
                    lefts[job].at[:, columns(part, core)], raw.at[part, 0], raw_sems.at[part, 0]
                ),
                pltpu.make_async_copy(
                    kin_left.at[job, part], raw.at[part, 1], raw_sems.at[part, 1]
                ),
            ]
        return copies

    seen = set()
    fresh = []
    for item in range(total):
        fresh.append([])
        for job, _ in ITEMS[item]:
            if job not in seen:
                seen.add(job)
                fresh[item].append(job)

    def load(item):
        for side in range(2):
            kin_block(item, side).wait_recv()
        for copy in window_copies(item):
            copy.start()
        for job in fresh[item]:
            for copy in kin_lefts(job):
                copy.wait_recv()
            copies = raw_copies(job)
            for copy in copies:
                copy.start()
            for copy in copies:
                copy.wait()
            for part in range(4):
                for whose in range(2):
                    lwin[job, part, :, whose * 256 : whose * 256 + 256] = raw[part, whose].T

    def loaded(slot):
        for side in range(2):
            here = pl.ds(side * HALF, HALF)
            pltpu.make_async_copy(
                rights[0].at[:, pl.ds(0, HALF)],
                rwin.at[slot, pl.ds(0, 256), here],
                win_sems.at[slot, side, 0],
            ).wait()
            pltpu.make_async_copy(
                kin_right.at[:, pl.ds(0, HALF)],
                rwin.at[slot, pl.ds(256, 256), here],
                win_sems.at[slot, side, 1],
            ).wait()

    def job_of(item, side):
        job, base = 0, item * 0
        for index in range(1, jobs):
            base = base + (item * 2 + side >= starts[index] // HALF).astype(jnp.int32)
        return job + base

    bits = (x_at, y_at)

    def product(slot, job, side, bit, upper):
        left = lwin[job, pl.ds(upper * 2, 2)].reshape(256, 512)
        first = pl.multiple_of(side * HALF + bit * KEPT, KEPT)
        right = rwin[slot, :, pl.ds(first, KEPT)]
        return jnp.dot(left, right, preferred_element_type=F32).reshape(2, 128, KEPT)

    def xy_copy(item, side):
        here = pl.ds(side * KEPT, KEPT)
        return remote(
            stage.at[lax.rem(item, STAGES), :, :, here],
            merged.at[item, :, :, here],
            xy_sems,
            (item, side),
            (flat[side], batch_at),
        )

    def offer(item):
        slot = lax.rem(item, WINDOWS)
        loaded(slot)

        @pl.when(item >= STAGES)
        def _():
            for side in range(2):
                xy_copy(item - STAGES, side).wait_send()

        for side in range(2):
            job = job_of(item, side)

            def half(upper, carry):
                tile = product(slot, job, side, 1 - bits[side], upper)
                stage[
                    lax.rem(item, STAGES), pl.ds(upper * 2, 2), :, side * KEPT : side * KEPT + KEPT
                ] = tile.astype(BF)
                return carry

            lax.fori_loop(0, 2, half, 0)
            xy_copy(item, side).start()

    def line_copy(item, dest, place, rightward):
        step = 1 if rightward else -1
        slot = 4 if not rightward and place - 1 == dest else dest
        return pltpu.make_async_remote_copy(
            merged.at[item, dest],
            passing.at[item, slot],
            line_send.at[item, dest],
            line_recv.at[item, slot],
            device_id=(section_at, batch_at + 2 * step),
            device_id_type=MESH,
        )

    def line_wait(item, slot):
        pltpu.make_async_remote_copy(
            merged.at[item, 0],
            passing.at[item, slot],
            line_send.at[item, 0],
            line_recv.at[item, slot],
            device_id=(section_at, sibling),
            device_id_type=MESH,
        ).wait_recv()

    def keep(item):
        slot = lax.rem(item, WINDOWS)
        for side in range(2):
            xy_copy(item, side).wait_recv()
            job = job_of(item, side)

            def half(upper, carry):
                here = (item, pl.ds(upper * 2, 2), slice(None), slice(side * KEPT, side * KEPT + KEPT))
                tile = product(slot, job, side, bits[side], upper)
                merged[here] = (tile + merged[here].astype(F32)).astype(BF)
                return carry

            lax.fori_loop(0, 2, half, 0)

        @pl.when(spot == 0)
        def _():
            for dest in (3, 2, 1):
                line_copy(item, dest, 0, True).start()

        @pl.when(spot == 3)
        def _():
            for dest in (0, 1, 2):
                line_copy(item, dest, 3, False).start()

    def relay(item, dest, place, rightward):
        line_wait(item, dest)
        merged[item, dest] = (
            merged[item, dest].astype(F32) + passing[item, dest].astype(F32)
        ).astype(BF)
        line_copy(item, dest, place, rightward).start()

    def second(item):
        @pl.when(spot == 1)
        def _():
            for dest in (3, 2):
                relay(item, dest, 1, True)

        @pl.when(spot == 2)
        def _():
            for dest in (0, 1):
                relay(item, dest, 2, False)

    def third(item):
        @pl.when(spot == 1)
        def _():
            relay(item, 0, 1, False)

        @pl.when(spot == 2)
        def _():
            relay(item, 3, 2, True)

    def cross_copy(item, side):
        here = pl.ds(side * KEPT, KEPT)
        return remote(
            lined.at[item, :, here],
            crossed.at[item, :, here],
            cross_sems,
            (item, side),
            (flat[1 - side], batch_at),
        )

    def close(item):
        @pl.when(spot == 0)
        def _():
            line_wait(item, 4)
            lined[item] = (
                merged[item, 0].astype(F32) + passing[item, 4].astype(F32)
            ).astype(BF)

        @pl.when(spot == 3)
        def _():
            line_wait(item, 3)
            lined[item] = (
                merged[item, 3].astype(F32) + passing[item, 3].astype(F32)
            ).astype(BF)

        for middle in (1, 2):

            @pl.when(spot == middle)
            def _():
                line_wait(item, middle)
                line_wait(item, 4)
                lined[item] = (
                    merged[item, middle].astype(F32)
                    + passing[item, middle].astype(F32)
                    + passing[item, 4].astype(F32)
                ).astype(BF)

        for side in range(2):
            cross_copy(item, side).start()

    def out_place(item, side, bit):
        layer = 1 - item // (total // 2)
        inner = lax.rem(item, total // 2)
        first = pl.multiple_of(inner * (2 * HALF) + side * HALF + bit * KEPT, KEPT)
        return sum_out.at[layer, :, pl.ds(first, KEPT)]

    def out_copy(item, side):
        return remote(
            settled.at[item, :, pl.ds(side * KEPT, KEPT)],
            out_place(item, side, bits[side]),
            out_sems,
            (item, side),
            (flat[side], batch_at),
        )

    def out_local(item, side):
        return pltpu.make_async_copy(
            settled.at[item, :, pl.ds(side * KEPT, KEPT)],
            out_place(item, side, bits[side]),
            own_sems.at[item, side],
        )

    def finish(item):
        for side in range(2):
            cross_copy(item, side).wait_recv()
        settled[item] = (lined[item].astype(F32) + crossed[item].astype(F32)).astype(BF)
        for side in range(2):
            out_copy(item, side).start()
            out_local(item, side).start()

    def kin_start(item):
        for job in fresh[item]:
            for copy in kin_lefts(job):
                copy.start()
        for side in range(2):
            kin_block(item, side).start()

    for item in range(2):
        kin_start(item)
    small_sum[0] = small_ref[...]
    small_copy(0).start()
    for which in range(2):
        lat_local(which).start()
        for way in range(2):
            lat_copy(which, way).start()
    for which in range(3):
        point_copy(which).start()
    for item in range(2, total):
        kin_start(item)
    load(0)

    def sidework(moment):
        @pl.when(moment == 2)
        def _():
            for which in range(2):
                for way in range(2):
                    lat_copy(which, way).wait_recv()
                    lat_far(which, way).start()
            for which in range(3):
                point_copy(which).wait_recv()
            gathered = point_ref[
                pl.ds(pl.multiple_of(section_at * quarter, quarter), quarter)
            ].astype(F32)
            for which in range(3):
                gathered += point_in[which].astype(F32)
            point_sum[...] = gathered.astype(BF)
            point_local().start()
            for which in range(3):
                point_deal(which).start()

        for phase in range(3):

            @pl.when(moment == 2 + 2 * phase)
            def _():
                small_copy(phase).wait_recv()
                small_sum[phase + 1] = small_sum[phase] + small_in[phase]
                if phase < 2:
                    small_copy(phase + 1).start()
                else:
                    for step in range(3):
                        small_copy(3 + step).start()

        @pl.when(moment == 8)
        def _():
            for step in range(3):
                small_copy(3 + step).wait_recv()
            small_out[...] = (small_sum[3] + small_in[4]) + (small_in[3] + small_in[5])

    def moment_body(moment, carry):
        for item in range(1, total):
            pl.when(moment == item - 1)(functools.partial(load, item))

        pl.when(moment < total)(lambda: offer(moment))
        for lag, action in ((2, keep), (3, second), (4, third), (5, close), (6, finish)):
            pl.when(jnp.logical_and(moment >= lag, moment < total + lag))(
                functools.partial(action, moment - lag)
            )
        sidework(moment)
        return carry

    lax.fori_loop(0, total + 6, moment_body, 0)

    for job in range(jobs):
        for copy in kin_lefts(job):
            copy.wait_send()
    for item in range(total):
        for side in range(2):
            kin_block(item, side).wait_send()
    for phase in range(6):
        small_copy(phase).wait_send()
    for which in range(2):
        lat_local(which).wait()
        for way in range(2):
            lat_copy(which, way).wait_send()
            lat_far(which, way).wait()
    point_local().wait()
    for which in range(3):
        point_copy(which).wait_send()
        point_deal(which).wait()

    def drain(item, carry):
        @pl.when(item >= total - STAGES)
        def _():
            for side in range(2):
                xy_copy(item, side).wait_send()

        for step in (1, 2, 3):
            dest = lax.rem(spot + step, 4)
            pltpu.make_async_remote_copy(
                merged.at[item, dest],
                passing.at[item, 0],
                line_send.at[item, dest],
                line_recv.at[item, 0],
                device_id=(section_at, sibling),
                device_id_type=MESH,
            ).wait_send()
        for side in range(2):
            cross_copy(item, side).wait_send()
            out_copy(item, side).wait()
            out_local(item, side).wait()
        return carry

    lax.fori_loop(0, total, drain, 0)


def reduce_all(lefts, rights, last, first, point_part, small):
    jobs = len(JOBS)
    total = len(ITEMS)
    columns = sum(JOBS)
    width = last.shape[1]
    anywhere = pl.BlockSpec(memory_space=pl.ANY)
    vmem = pl.BlockSpec(memory_space=pltpu.VMEM)
    dma = pltpu.SemaphoreType.DMA
    flops = 2 * columns * 512 * 512 * 2
    return pl.pallas_call(
        reduce_kernel,
        out_shape=[
            jax.ShapeDtypeStruct((2, 128, columns // 2), BF),
            jax.ShapeDtypeStruct((4 * last.shape[0], width), BF),
            jax.ShapeDtypeStruct((4 * first.shape[0], width), BF),
            jax.ShapeDtypeStruct(point_part.shape, BF),
            jax.ShapeDtypeStruct(small.shape, F32),
            jax.ShapeDtypeStruct((jobs, 4, 256, 128), BF),
            jax.ShapeDtypeStruct((256, columns), BF),
        ],
        in_specs=[anywhere] * (2 * jobs + 2) + [vmem, vmem],
        out_specs=[anywhere] * 4 + [vmem] + [anywhere] * 2,
        scratch_shapes=[
            pltpu.VMEM((jobs, 4, 128, 512), BF),
            pltpu.VMEM((4, 2, 256, 128), BF),
            pltpu.VMEM((WINDOWS, 512, 2 * HALF), BF),
            pltpu.VMEM((STAGES, 4, 128, 2 * KEPT), BF),
            pltpu.VMEM((total, 4, 128, 2 * KEPT), BF),
            pltpu.VMEM((total, 5, 128, 2 * KEPT), BF),
            pltpu.VMEM((total, 128, 2 * KEPT), BF),
            pltpu.VMEM((total, 128, 2 * KEPT), BF),
            pltpu.VMEM((total, 128, 2 * KEPT), BF),
            pltpu.VMEM((3, point_part.shape[0] // 4, width), BF),
            pltpu.VMEM((point_part.shape[0] // 4, width), BF),
            pltpu.VMEM((6, *small.shape), F32),
            pltpu.VMEM((4, *small.shape), F32),
            dma((2, jobs, 4)),
            dma((2, total, 2)),
            dma((4, 2)),
            dma((WINDOWS, 2, 2)),
            dma((2, total, 2)),
            dma((total, 4)),
            dma((total, 5)),
            dma((2, total, 2)),
            dma((2, total, 2)),
            dma((total, 2)),
            dma((2, 2, 2)),
            dma((2, 2, 2)),
            dma((2,)),
            dma((2, 3)),
            dma((2, 3)),
            dma((1,)),
            dma((2, 6)),
        ],
        compiler_params=pltpu.CompilerParams(
            collective_id=2, has_side_effects=True, vmem_limit_bytes=60 * 2**20
        ),
        cost_estimate=pl.CostEstimate(flops=flops, bytes_accessed=2**26, transcendentals=0),
    )(*lefts, *rights, last, first, point_part, small)[:5]


def per_device(
    latents,
    points,
    neighbours,
    lengths,
    cross_proj,
    cross_out,
    cross_gains,
    self_proj,
    self_out,
    self_gain,
    mlp_gain,
    mlp_in,
    mlp_in_bias,
    mlp_down,
    mlp_out_bias,
    cotangent,
):
    sections = lax.axis_size("section")
    section_at = lax.axis_index("section")
    width = latents.shape[1]
    hidden = mlp_in.shape[2]
    groups_dev = neighbours.shape[0]
    rows = latents.shape[0] // sections
    shard = cross_out.shape[0]
    piece = shard // sections
    groups_all = groups_dev * lax.axis_size("batch")

    def gathered(block):
        own = lax.dynamic_slice_in_dim(block, section_at * piece, piece, 0)
        return lax.all_gather(own, ALL, axis=0, tiled=True)

    vectors = jnp.concatenate(
        [
            cross_gains.reshape(-1),
            self_gain,
            mlp_gain.reshape(-1),
            mlp_out_bias.reshape(-1),
            mlp_in_bias.reshape(-1),
            jnp.zeros_like(self_gain),
        ]
    ).reshape(-1, shard)
    projs = (cross_proj.reshape(shard, 3 * width), self_proj.reshape(shard, 3 * width))
    small_slice = lax.axis_size("batch") == 8
    if small_slice:
        *full, spread = gather_all(
            [projs[0], cross_out, mlp_in, mlp_down, projs[1], self_out], vectors
        )
    else:
        blocks = [projs[0], cross_out, mlp_in[0], mlp_down[0]]
        blocks += [projs[1], self_out, mlp_in[1], mlp_down[1]]
        full = [gathered(block) for block in blocks]
        spread = lax.all_gather(vectors, "batch", axis=0, tiled=False)
    proj_c, out_c, in_0, down_0, proj_s, out_s, in_1, down_1 = full
    spread = spread.astype(F32)

    def vector(first, count):
        return spread[:, first : first + count].reshape(-1)

    gains_cross = (vector(0, 1), vector(1, 1))
    gain_self = vector(2, 1)
    gains_mlp = (vector(3, 1), vector(4, 1))
    biases_out = (vector(5, 1), vector(6, 1))
    per_bias = hidden // width
    biases_in = (vector(7, per_bias), vector(7 + per_bias, per_bias))

    mine = lax.dynamic_slice_in_dim(latents, section_at * rows, rows, 0).astype(F32)
    cot = lax.dynamic_slice_in_dim(cotangent, section_at * rows, rows, 0).astype(F32)
    listed = lax.dynamic_index_in_dim(neighbours, section_at, 0, keepdims=False)
    length = lax.dynamic_index_in_dim(lengths, section_at, 0, keepdims=False)
    valid = jnp.arange(listed.shape[0], dtype=jnp.int32) < length
    picks = listed[:, None] == jnp.arange(points.shape[0], dtype=jnp.int32)[None, :]
    picks = picks.astype(BF)
    source = mm(picks, points)

    u1, kept_c = attend(mine, source, valid, gains_cross[0], gains_cross[1], proj_c, out_c)
    u2, kept_0 = feed(u1.astype(F32), gains_mlp[0], in_0, biases_in[0], down_0, biases_out[0])
    u2 = u2.astype(F32)
    u3, kept_s = attend(u2, u2, None, gain_self, gain_self, proj_s, out_s)
    u4, kept_1 = feed(u3.astype(F32), gains_mlp[1], in_1, biases_in[1], down_1, biases_out[1])
    final = u4.astype(F32)
    group_norm = jnp.sqrt(jnp.mean(final * final) + EPSILON)
    norm_total = norm_sum(group_norm) if small_slice else lax.psum(group_norm, ALL)
    norm_mean = norm_total / groups_all

    g4 = (cot + (norm_mean / group_norm) * final).astype(BF)
    dx, gain_1_grad, bias_1_grad, ob_1_grad, pairs_1 = feed_back(
        g4, kept_1, gains_mlp[1], in_1, down_1
    )
    g3 = (g4.astype(F32) + dx).astype(BF)
    dx, ds, gq, gkv, pairs_s = attend_back(g3, kept_s, gain_self, gain_self, proj_s, out_s)
    gain_s_grad = gq + gkv
    g2 = (g3.astype(F32) + dx + ds).astype(BF)
    dx, gain_0_grad, bias_0_grad, ob_0_grad, pairs_0 = feed_back(
        g2, kept_0, gains_mlp[0], in_0, down_0
    )
    g1 = (g2.astype(F32) + dx).astype(BF)
    dx, ds, cq_grad, ckv_grad, pairs_c = attend_back(
        g1, kept_c, gains_cross[0], gains_cross[1], proj_c, out_c
    )
    g0 = (g1.astype(F32) + dx).astype(BF)
    high = ds.astype(BF)
    low = (ds - high.astype(F32)).astype(BF)
    point_part = (mm_rows(picks, high) + mm_rows(picks, low)).astype(BF)
    small = jnp.concatenate(
        [
            cq_grad,
            ckv_grad,
            gain_s_grad,
            gain_0_grad,
            gain_1_grad,
            ob_0_grad,
            ob_1_grad,
            bias_0_grad,
            bias_1_grad,
            jnp.zeros_like(cq_grad),
        ]
    ).reshape(-1, width)
    pairs = pairs_1 + pairs_s + pairs_0 + pairs_c
    lefts, rights = [pair[0] for pair in pairs], [pair[1] for pair in pairs]
    if small_slice:
        sums, latents_out, g0_all, points_sum, small = reduce_all(
            lefts, rights, u4, g0, point_part, small
        )

        attn = 2 * hidden
        mlp_in_grad = sums[:, :, :hidden].astype(F32)
        mlp_down_grad = sums[:, :, hidden:attn].astype(F32)
        proj_c_grad, proj_s_grad = [
            sums[layer, :, attn : attn + 3 * width].astype(F32) for layer in range(2)
        ]
        out_c_grad, out_s_grad = [
            sums[layer, :, attn + 3 * width :].astype(F32) for layer in range(2)
        ]
    else:

        def settled_grad(left, right):
            part = lax.psum_scatter(
                mm_rows(left, right).astype(BF), ALL, scatter_dimension=0, tiled=True
            )
            return lax.all_gather(part, "section", axis=0, tiled=True).astype(F32)

        done = [settled_grad(left, right) for left, right in pairs]
        mlp_in_grad = jnp.stack([done[6], done[0]])
        mlp_down_grad = jnp.stack([done[7], done[1]])
        proj_s_grad = jnp.concatenate(done[2:5], axis=1)
        proj_c_grad = jnp.concatenate(done[8:11], axis=1)
        out_s_grad, out_c_grad = done[5], done[11]
        points_sum = lax.psum(point_part, "section")
        latents_out = lax.all_gather(u4, "section", axis=0, tiled=True)
        g0_all = lax.all_gather(g0, "section", axis=0, tiled=True)
        small = lax.psum(small, ALL)
    points_grad = points_sum.astype(F32)
    latents_grad = g0_all.astype(F32)
    batch_at = lax.axis_index("batch")

    def own(first, count):
        flat = small[first : first + count].reshape(-1)
        size = flat.shape[0] // lax.axis_size("batch")
        return lax.dynamic_slice_in_dim(flat, batch_at * size, size, 0)

    return (
        latents_out,
        latents_grad,
        points_grad,
        proj_c_grad.reshape(shard, 3, width),
        out_c_grad,
        jnp.stack([own(0, 1), own(1, 1)]),
        proj_s_grad.reshape(shard, 3, width),
        out_s_grad,
        own(2, 1),
        jnp.stack([own(3, 1), own(4, 1)]),
        mlp_in_grad,
        jnp.stack([own(7, per_bias), own(7 + per_bias, per_bias)]),
        mlp_down_grad,
        jnp.stack([own(5, 1), own(6, 1)]),
        norm_mean,
    )


def solution(mesh):
    rows = P("batch", None)
    cols = P(None, "batch")
    block = P("batch", None, None)
    pair = P(None, "batch", None)
    return jax.shard_map(
        per_device,
        mesh=mesh,
        in_specs=(
            rows,
            rows,
            rows,
            P("batch"),
            block,
            rows,
            cols,
            block,
            rows,
            P("batch"),
            cols,
            pair,
            cols,
            pair,
            cols,
            rows,
        ),
        out_specs=(
            rows,
            rows,
            rows,
            block,
            rows,
            cols,
            block,
            rows,
            P("batch"),
            cols,
            pair,
            cols,
            pair,
            cols,
            P(),
        ),
        check_vma=False,
    )
```

```python
import functools
import math

import jax
import jax.numpy as jnp
from jax import lax
from jax.experimental import pallas as pl
from jax.experimental.pallas import tpu as pltpu
from jax.sharding import PartitionSpec as P

HD = 128
EPSILON = 1e-05
MASKED = -1e30
BF = jnp.bfloat16
F32 = jnp.float32
ALL = ("batch", "section")
MESH = pl.DeviceIdType.MESH
GATHER_WIDTH = 1024
AHEAD = 4
SLOTS = 3
GATHERED = tuple(
    (4 * layer + index, start)
    for layer in range(2)
    for index, start in (
        [(0, 0), (0, 1024), (0, 2048), (1, 0)]
        + [(2 + which, chunk) for chunk in range(0, 4096, 1024) for which in range(2)]
    )
)


def mm(a, b):
    return jnp.dot(a, b, preferred_element_type=F32)


def mm_rows(a, b):
    return lax.dot_general(a, b, (((0,), (0,)), ((), ())), preferred_element_type=F32)


def mm_cols(a, b):
    return lax.dot_general(a, b, (((1,), (1,)), ((), ())), preferred_element_type=F32)


def unit_rows(values):
    centred = values - jnp.mean(values, axis=-1, keepdims=True)
    inverse = lax.rsqrt(jnp.mean(centred * centred, axis=-1, keepdims=True) + EPSILON)
    return centred * inverse, inverse


def norm_back(gradient, unit, inverse, gain):
    scaled = gradient * gain
    inner = (
        scaled
        - jnp.mean(scaled, axis=-1, keepdims=True)
        - unit * jnp.mean(scaled * unit, axis=-1, keepdims=True)
    )
    return inverse * inner, jnp.sum(gradient * unit, axis=0)


def heads_of(rows):
    return rows.reshape(rows.shape[0], -1, HD)


def softmax(q, k, valid):
    scores = jnp.einsum(
        "lhc,nhc->hln", heads_of(q), heads_of(k), preferred_element_type=F32
    ) * (1.0 / math.sqrt(HD))
    if valid is not None:
        scores = jnp.where(valid[None, None, :], scores, MASKED)
    grown = jnp.exp(scores - jnp.max(scores, axis=-1, keepdims=True))
    return grown / jnp.sum(grown, axis=-1, keepdims=True)


def attend(inputs, source, valid, gain_q, gain_kv, proj, out):
    unit_x, inv_x = unit_rows(inputs)
    queries_in = (unit_x * gain_q).astype(BF)
    unit_s, inv_s = unit_rows(source)
    keys_in = (unit_s * gain_kv).astype(BF)
    width = inputs.shape[1]
    q = mm(queries_in, proj[:, :width]).astype(BF)
    kv = mm(keys_in, proj[:, width:]).astype(BF)
    k, v = kv[:, :width], kv[:, width:]
    soft = softmax(q, k, valid)
    mixture = jnp.einsum("hln,nhc->lhc", soft.astype(BF), heads_of(v), preferred_element_type=F32)
    mixture = mixture.reshape(inputs.shape).astype(BF)
    result = (inputs + mm(mixture, out)).astype(BF)
    return result, (unit_x, inv_x, queries_in, unit_s, inv_s, keys_in, q, k, v, soft, mixture)


def attend_back(gradient, kept, gain_q, gain_kv, proj, out):
    unit_x, inv_x, queries_in, unit_s, inv_s, keys_in, q, k, v, soft, mixture = kept
    width = gradient.shape[1]
    scale = 1.0 / math.sqrt(HD)
    grad_mix = mm_cols(gradient, out).astype(BF)
    grad_soft = jnp.einsum(
        "lhc,nhc->hln", heads_of(grad_mix), heads_of(v), preferred_element_type=F32
    )
    inner = jnp.sum(soft * grad_soft, axis=-1, keepdims=True)
    grad_scores = (soft * (grad_soft - inner)).astype(BF)
    dq = jnp.einsum("hln,nhc->lhc", grad_scores, heads_of(k), preferred_element_type=F32) * scale
    dk = jnp.einsum("hln,lhc->nhc", grad_scores, heads_of(q), preferred_element_type=F32) * scale
    dv = jnp.einsum(
        "hln,lhc->nhc", soft.astype(BF), heads_of(grad_mix), preferred_element_type=F32
    )
    dq = dq.reshape(gradient.shape).astype(BF)
    dk = dk.reshape(-1, width).astype(BF)
    dv = dv.reshape(-1, width).astype(BF)
    grad_x, gain_q_grad = norm_back(mm_cols(dq, proj[:, :width]), unit_x, inv_x, gain_q)
    back_s = mm_cols(dk, proj[:, width : 2 * width]) + mm_cols(dv, proj[:, 2 * width :])
    grad_s, gain_kv_grad = norm_back(back_s, unit_s, inv_s, gain_kv)
    pairs = ((queries_in, dq), (keys_in, dk), (keys_in, dv), (mixture, gradient))
    return grad_x, grad_s, gain_q_grad, gain_kv_grad, pairs


def feed(inputs, gain, w_in, b_in, w_down, b_out):
    unit, inverse = unit_rows(inputs)
    lowered = (unit * gain).astype(BF)
    pre_act = mm(lowered, w_in) + b_in
    active = jax.nn.gelu(pre_act).astype(BF)
    result = (inputs + mm_cols(active, w_down) + b_out).astype(BF)
    return result, (unit, inverse, lowered, pre_act, active)


def feed_back(gradient, kept, gain, w_in, w_down):
    unit, inverse, lowered, pre_act, active = kept
    grad_act = mm(gradient, w_down)
    grad_pre = jax.vjp(jax.nn.gelu, pre_act)[1](grad_act)[0].astype(BF)
    grad_x, gain_grad = norm_back(mm_cols(grad_pre, w_in), unit, inverse, gain)
    bias_grad = jnp.sum(grad_pre.astype(F32), axis=0)
    out_grad = jnp.sum(gradient.astype(F32), axis=0)
    return grad_x, gain_grad, bias_grad, out_grad, ((lowered, grad_pre), (gradient, active))


def gelu(value):
    inner = math.sqrt(2.0 / math.pi) * (value + 0.044715 * (value * value * value))
    return value * (0.5 * (1.0 + jnp.tanh(inner)))


def tiles(count, body):
    def step(index, carry):
        body(pl.ds(pl.multiple_of(index * 256, 256), 256), index)
        return carry

    lax.fori_loop(0, count, step, 0)


def norm_into(source, gain, target):
    def step(index, carry):
        here = pl.ds(pl.multiple_of(index * 32, 32), 32)
        unit, _ = unit_rows(source[here, :].astype(F32))
        target[here, :] = (unit * gain).astype(BF)
        return carry

    lax.fori_loop(0, source.shape[0] // 32, step, 0)


def gather_kernel(*refs):
    cross_proj, cross_out, mlp_in, mlp_down, self_proj, self_out = refs[:6]
    vec_in, x_in, src_in, mask_in, cot_in = refs[6:11]
    ins = (
        cross_proj,
        cross_out,
        mlp_in.at[0],
        mlp_down.at[0],
        self_proj,
        self_out,
        mlp_in.at[1],
        mlp_down.at[1],
    )
    count = len(ins)
    outs = refs[11 : 11 + count]
    rest = refs[11 + count :]
    vec_out, norm_out = rest[:2]
    kept_outs = rest[2:21]
    (
        u1,
        u2,
        u3,
        u4,
        grad_top,
        xq_c,
        sn_c,
        q_c,
        k_c,
        v_c,
        o_c,
        xn_s,
        q_s,
        k_s,
        v_s,
        o_s,
        lowered,
        before,
        active,
        slots,
        total_rows,
        gains,
        biases,
        plane,
        line_in,
    ) = rest[21:46]
    (own_sem, send, recv, kin_send, kin_recv, vec_sems) = rest[46:52]
    (slot_sems, kept_sems, plane_sems, line_sems) = rest[52:]
    section_at = lax.axis_index("section")
    batch_at = lax.axis_index("batch")
    line = 4
    core = lax.rem(batch_at, 2)
    spot = batch_at // 2
    beside = section_at + 1 - 2 * lax.rem(section_at, 2)
    above = lax.rem(section_at + 2, 4)
    sibling = batch_at + 1 - 2 * core
    shard = ins[0].shape[0]
    place = section_at * 2 + core

    def down_line(step):
        return lax.rem(spot + step, line) * 2 + core

    def up_line(step):
        return lax.rem(spot + line - step, line) * 2 + core

    near_peers = []
    for turn in range(1, 8):
        other = lax.rem(place + turn, 8)
        near_peers.append((other // 2, spot * 2 + lax.rem(other, 2)))
    line_peers = [(section_at, down_line(step)) for step in range(1, line)]
    far_peers = [(section_at, down_line(step) + 1 - 2 * core) for step in range(1, line)]
    vec_peers = [(section_at, sibling)] + line_peers + far_peers
    peers = near_peers + line_peers + far_peers
    barrier = pltpu.get_barrier_semaphore()
    for peer in peers:
        pl.semaphore_signal(barrier, inc=1, device_id=peer, device_id_type=MESH)
    pl.semaphore_wait(barrier, len(peers))

    def spread(ref, owner, first, size):
        return ref.at[pl.ds(pl.multiple_of(owner * shard, shard), shard), pl.ds(first, size)]

    size = GATHER_WIDTH // 4

    def part(item, quarter):
        return pl.multiple_of(GATHERED[item][1] + quarter * size, 128)

    def line_copy(item, step):
        index = GATHERED[item][0]
        first = part(item, section_at)
        return pltpu.make_async_remote_copy(
            ins[index].at[:, pl.ds(first, size)],
            spread(outs[index], batch_at, first, size),
            send.at[0, item, step],
            recv.at[0, item, step],
            device_id=(section_at, down_line(step)),
            device_id_type=MESH,
        )

    def plane_copy(item, step, way, low, wide, peer):
        index = GATHERED[item][0]
        ref = spread(outs[index], up_line(step), low, wide)
        return pltpu.make_async_remote_copy(
            ref,
            ref,
            send.at[way, item, step],
            recv.at[way, item, step],
            device_id=(peer, batch_at),
            device_id_type=MESH,
        )

    def near(item, step):
        first = part(item, section_at)
        return [
            plane_copy(item, step, 1, first, size, beside),
            plane_copy(item, step, 2, first, size, above),
        ]

    def far(item, step):
        by_y = part(item, beside)
        by_x = pl.multiple_of(part(item, above) + size // 2, 128)
        return [
            plane_copy(item, step, 3, by_y, size // 2, above),
            plane_copy(item, step, 4, by_x, size // 2, beside),
        ]

    def kin(item, step):
        index, start = GATHERED[item]
        if step == 0:
            source = ins[index].at[:, pl.ds(start, GATHER_WIDTH)]
        else:
            source = spread(outs[index], up_line(step), start, GATHER_WIDTH)
        return pltpu.make_async_remote_copy(
            source,
            spread(outs[index], up_line(step), start, GATHER_WIDTH),
            kin_send.at[item, step],
            kin_recv.at[item, step],
            device_id=(section_at, sibling),
            device_id_type=MESH,
        )

    def own(item):
        index, start = GATHERED[item]
        return pltpu.make_async_copy(
            ins[index].at[:, pl.ds(start, GATHER_WIDTH)],
            spread(outs[index], batch_at, start, GATHER_WIDTH),
            own_sem.at[item],
        )

    def vec_copy(which):
        return pltpu.make_async_remote_copy(
            vec_in,
            vec_out.at[batch_at],
            vec_sems.at[0, which],
            vec_sems.at[1, which],
            device_id=vec_peers[which],
            device_id_type=MESH,
        )

    def slot_copy(item):
        index, start = GATHERED[item]
        return pltpu.make_async_copy(
            outs[index].at[:, pl.ds(start, GATHER_WIDTH)],
            slots.at[item % SLOTS],
            slot_sems.at[item % SLOTS],
        )

    def near_norm(turn):
        return pltpu.make_async_remote_copy(
            plane.at[8],
            plane.at[place],
            plane_sems.at[0, turn],
            plane_sems.at[1, turn],
            device_id=near_peers[turn],
            device_id_type=MESH,
        )

    def far_norm(step):
        return pltpu.make_async_remote_copy(
            line_in.at[4],
            line_in.at[spot],
            line_sems.at[0, step],
            line_sems.at[1, step],
            device_id=line_peers[step],
            device_id_type=MESH,
        )

    steps = range(1, line)
    total = len(GATHERED)
    started = []

    def launch(copies):
        for copy in copies:
            copy.start()
        started.extend(copies)

    kept = (
        (u1, u2, u3, u4, grad_top)
        + (xq_c, sn_c, q_c, k_c, v_c, o_c)
        + (xn_s, q_s, k_s, v_s, o_s)
        + (lowered, before, active)
    )
    names = {id(ref): place for place, ref in enumerate(kept)}

    def keep(*chosen):
        for ref in chosen:
            index = names[id(ref)]
            pltpu.make_async_copy(ref, kept_outs[index], kept_sems.at[index]).start()

    def row(index):
        return gains[index : index + 1, :]

    def project(source, target, slot):
        def tile(columns, _):
            target[:, columns] = mm(source[...], slots[slot, :, columns]).astype(BF)

        tiles(4, tile)

    def heads(q, k, v, o, masked):
        def head(index, carry):
            here = pl.ds(pl.multiple_of(index * HD, HD), HD)
            scores = mm_cols(q[:, here], k[:, here]) * (1.0 / math.sqrt(HD))
            if masked:
                scores = jnp.where(mask_in[...] > 0.0, scores, MASKED)
            grown = jnp.exp(scores - jnp.max(scores, axis=-1, keepdims=True))
            soft = grown / jnp.sum(grown, axis=-1, keepdims=True)
            o[:, here] = mm(soft.astype(BF), v[:, here]).astype(BF)
            return carry

        lax.fori_loop(0, q.shape[1] // HD, head, 0)

    def close_attention(inputs, o, target, slot):
        def tile(columns, _):
            target[:, columns] = (
                inputs[:, columns].astype(F32) + mm(o[...], slots[slot, :, columns])
            ).astype(BF)

        tiles(4, tile)

    def feed_up(layer, chunk, slot):
        def tile(columns, index):
            there = pl.ds(pl.multiple_of(chunk * GATHER_WIDTH + index * 256, 256), 256)
            value = mm(lowered[layer], slots[slot, :, columns]) + biases[layer : layer + 1, there]
            before[layer, :, there] = value
            active[layer, :, there] = gelu(value).astype(BF)

        tiles(4, tile)

    def feed_down(layer, chunk, slot, inputs, target):
        chosen = pl.ds(chunk * GATHER_WIDTH, GATHER_WIDTH)

        def tile(columns, _):
            value = mm_cols(active[layer, :, chosen], slots[slot, columns, :])
            if chunk == 0:
                total_rows[:, columns] = value
            elif chunk < 3:
                total_rows[:, columns] += value
            else:
                target[:, columns] = (
                    inputs[:, columns].astype(F32)
                    + (total_rows[:, columns] + value)
                    + gains[5 + layer : 6 + layer, columns]
                ).astype(BF)

        tiles(4, tile)

    def work(item):
        slot_copy(item).wait()
        slot = item % SLOTS
        layer, stage = item // 12, item % 12
        inputs = (x_in, u2)[layer]
        middle, result = (u1, u3)[layer], (u2, u4)[layer]
        q, k, v, o = ((q_c, k_c, v_c, o_c), (q_s, k_s, v_s, o_s))[layer]
        if stage == 0:
            if layer == 0:
                norm_into(x_in, row(0), xq_c)
                norm_into(src_in, row(1), sn_c)
                keep(xq_c, sn_c)
            else:
                norm_into(u2, row(2), xn_s)
                keep(xn_s)
            project((xq_c, xn_s)[layer], q, slot)
        elif stage == 1:
            project((sn_c, xn_s)[layer], k, slot)
        elif stage == 2:
            project((sn_c, xn_s)[layer], v, slot)
            heads(q, k, v, o, layer == 0)
            keep(q, k, v, o)
        elif stage == 3:
            close_attention(inputs, o, middle, slot)
            norm_into(middle, row(3 + layer), lowered.at[layer])
            keep(middle)
        elif stage % 2 == 0:
            feed_up(layer, (stage - 4) // 2, slot)
        else:
            feed_down(layer, (stage - 4) // 2, slot, middle, result)
            if stage == 11:
                keep(result)

    for item in range(AHEAD):
        launch([line_copy(item, step) for step in steps])
    vec_out[batch_at] = vec_in[...]
    for which in range(7):
        vec_copy(which).start()
    for moment in range(total + 4):
        if moment + AHEAD < total:
            launch([line_copy(moment + AHEAD, step) for step in steps])
        if moment < total:
            for step in steps:
                line_copy(moment, step).wait_recv()
                launch(near(moment, step))
            own(moment).start()
            launch([kin(moment, 0)])
        if 0 <= moment - 1 < total:
            for step in steps:
                for copy, onward in zip(near(moment - 1, step), far(moment - 1, step)):
                    copy.wait_recv()
                    launch([onward])
        if 0 <= moment - 2 < total:
            for step in steps:
                for copy in far(moment - 2, step):
                    copy.wait_recv()
                launch([kin(moment - 2, step)])
        if moment == 2:
            for which in range(7):
                vec_copy(which).wait()
            for owner in range(8):
                values = vec_out[owner].astype(F32)
                gains[:, owner * 128 : owner * 128 + 128] = values
                for layer in range(2):
                    for part_at in range(4):
                        first = owner * 512 + part_at * 128
                        index = 7 + 4 * layer + part_at
                        biases[layer : layer + 1, first : first + 128] = values[index : index + 1]
        if 0 <= moment - 4 < total:
            work(moment - 4)
        if 0 <= moment - 3 < total:
            own(moment - 3).wait()
            for step in range(line):
                kin(moment - 3, step).wait_recv()
            slot_copy(moment - 3).start()
    keep(lowered, before, active)

    def square(index, carry):
        here = pl.ds(pl.multiple_of(index * 32, 32), 32)
        values = u4[here, :].astype(F32)
        return carry + jnp.sum(values * values, axis=0, keepdims=True)

    squares = lax.fori_loop(0, u4.shape[0] // 32, square, jnp.zeros((1, u4.shape[1]), F32))
    mean = jnp.sum(squares, axis=1, keepdims=True) / (u4.shape[0] * u4.shape[1])
    group_norm = jnp.sqrt(mean + EPSILON)
    plane[8] = jnp.broadcast_to(group_norm, plane.shape[1:])
    for turn in range(7):
        near_norm(turn).start()
    plane[place] = plane[8]
    for turn in range(7):
        near_norm(turn).wait()
    line_in[4] = jnp.sum(plane[0:8], axis=0)
    for step in range(3):
        far_norm(step).start()
    line_in[spot] = line_in[4]
    for step in range(3):
        far_norm(step).wait()
    norm_mean = jnp.sum(line_in[0:4], axis=0) / 32.0
    norm_out[...] = norm_mean
    ratio = norm_mean[0:1, 0:1] / group_norm

    def top(index, carry):
        here = pl.ds(pl.multiple_of(index * 32, 32), 32)
        grad_top[here, :] = (
            cot_in[here, :].astype(F32) + ratio * u4[here, :].astype(F32)
        ).astype(BF)
        return carry

    lax.fori_loop(0, u4.shape[0] // 32, top, 0)
    keep(grad_top)
    for index, ref in enumerate(kept):
        pltpu.make_async_copy(ref, kept_outs[index], kept_sems.at[index]).wait()
    for copy in started:
        copy.wait_send()


def gather_forward(blocks, vectors, inputs, source, mask, cotangent):
    rows, width = inputs.shape
    hidden = blocks[2].shape[2]
    widths = (3 * width, width, hidden, hidden) * 2
    total = len(GATHERED)
    anywhere = pl.BlockSpec(memory_space=pl.ANY)
    vmem = pl.BlockSpec(memory_space=pltpu.VMEM)
    plain = ((rows, width), BF)
    kept = [plain] * 16 + [
        ((2, rows, width), BF),
        ((2, rows, hidden), F32),
        ((2, rows, hidden), BF),
    ]
    dma = pltpu.SemaphoreType.DMA
    return pl.pallas_call(
        gather_kernel,
        out_shape=[jax.ShapeDtypeStruct((width, size), BF) for size in widths]
        + [
            jax.ShapeDtypeStruct((8, *vectors.shape), BF),
            jax.ShapeDtypeStruct((8, 128), F32),
        ]
        + [jax.ShapeDtypeStruct(*one) for one in kept],
        in_specs=[anywhere] * len(blocks) + [vmem] * 5,
        out_specs=[anywhere] * len(widths) + [vmem] * 2 + [anywhere] * len(kept),
        scratch_shapes=[pltpu.VMEM(*one) for one in kept]
        + [
            pltpu.VMEM((SLOTS, width, GATHER_WIDTH), BF),
            pltpu.VMEM((rows, width), F32),
            pltpu.VMEM((vectors.shape[0], width), F32),
            pltpu.VMEM((2, hidden), F32),
            pltpu.VMEM((9, 8, 128), F32),
            pltpu.VMEM((5, 8, 128), F32),
            dma((total,)),
            dma((5, total, 4)),
            dma((5, total, 4)),
            dma((total, 4)),
            dma((total, 4)),
            dma((2, 7)),
            dma((SLOTS,)),
            dma((len(kept),)),
            dma((2, 7)),
            dma((2, 3)),
        ],
        compiler_params=pltpu.CompilerParams(
            collective_id=1, has_side_effects=True, vmem_limit_bytes=48 * 2**20
        ),
        cost_estimate=pl.CostEstimate(
            flops=2 * rows * width * sum(widths), bytes_accessed=2**27, transcendentals=2**21
        ),
    )(*blocks, vectors, inputs, source, mask, cotangent)


JOBS = (4096, 4096, 1024, 1024, 1024, 1024) * 2
HALF = 512
KEPT = 256
BLOCKS = [(job, start) for job, width in enumerate(JOBS) for start in range(0, width, HALF)]
ITEMS = tuple(zip(BLOCKS[::2], BLOCKS[1::2]))
WINDOWS = 4
STAGES = 4


def reduce_kernel(*refs):
    jobs = len(JOBS)
    total = len(ITEMS)
    lefts, rights = refs[:jobs], refs[jobs : 2 * jobs]
    last_ref, first_ref, point_ref, small_ref = refs[2 * jobs : 2 * jobs + 4]
    rest = refs[2 * jobs + 4 :]
    (sum_out, last_out, first_out, point_out, small_out, kin_left, kin_right) = rest[:7]
    (
        lwin,
        raw,
        rwin,
        stage,
        merged,
        passing,
        lined,
        crossed,
        settled,
        point_in,
        point_sum,
        small_in,
        small_sum,
        kin_sems,
        kin_block_sems,
        raw_sems,
        win_sems,
        xy_sems,
        line_send,
        line_recv,
        cross_sems,
        out_sems,
        own_sems,
        lat_sems,
        far_sems,
        lat_own,
        point_sems,
        deal_sems,
        point_own,
        small_sems,
    ) = rest[7:]
    section_at = lax.axis_index("section")
    batch_at = lax.axis_index("batch")
    core = lax.rem(batch_at, 2)
    spot = batch_at // 2
    x_at = lax.rem(section_at, 2)
    y_at = section_at // 2
    beside = section_at + 1 - 2 * x_at
    above = lax.rem(section_at + 2, 4)
    across = lax.rem(beside + 2, 4)
    sibling = batch_at + 1 - 2 * core
    flat = (beside, above)

    peers = [(beside, batch_at), (above, batch_at), (across, batch_at), (section_at, sibling)]
    peers += [(section_at, lax.rem(spot + step, 4) * 2 + core) for step in (1, 2, 3)]
    barrier = pltpu.get_barrier_semaphore()
    for peer in peers:
        pl.semaphore_signal(barrier, inc=1, device_id=peer, device_id_type=MESH)
    pl.semaphore_wait(barrier, len(peers))

    def remote(source, target, sems, place, peer):
        return pltpu.make_async_remote_copy(
            source,
            target,
            sems.at[(0, *place)],
            sems.at[(1, *place)],
            device_id=peer,
            device_id_type=MESH,
        )

    starts = [sum(JOBS[:job]) for job in range(jobs)]

    def columns(spot_of, parity):
        return pl.ds(pl.multiple_of((2 * spot_of + parity) * 128, 128), 128)

    def kin_lefts(job):
        return [
            remote(
                lefts[job].at[:, columns(part, 1 - core)],
                kin_left.at[job, part],
                kin_sems,
                (job, part),
                (section_at, sibling),
            )
            for part in range(4)
        ]

    def kin_block(item, side):
        job, start = ITEMS[item][side]
        return remote(
            rights[job].at[:, pl.ds(start, HALF)],
            kin_right.at[:, pl.ds(starts[job] + start, HALF)],
            kin_block_sems,
            (item, side),
            (section_at, sibling),
        )

    def small_copy(phase):
        if phase == 0:
            peer = (section_at, sibling)
        elif phase < 3:
            peer = (flat[phase - 1], batch_at)
        else:
            peer = (section_at, lax.rem(spot + phase - 2, 4) * 2 + core)
        return remote(
            small_sum.at[min(phase, 3)], small_in.at[phase], small_sems, (phase,), peer
        )

    quarter = point_ref.shape[0] // 4

    def point_copy(which):
        peer = (beside, above, across)[which]
        return remote(
            point_ref.at[pl.ds(pl.multiple_of(peer * quarter, quarter), quarter)],
            point_in.at[which],
            point_sems,
            (which,),
            (peer, batch_at),
        )

    def point_deal(which):
        peer = (beside, above, across)[which]
        return remote(
            point_sum,
            point_out.at[pl.ds(pl.multiple_of(section_at * quarter, quarter), quarter)],
            deal_sems,
            (which,),
            (peer, batch_at),
        )

    rows = last_ref.shape[0]
    pairs = ((last_ref, last_out), (first_ref, first_out))

    def lat_copy(which, way):
        source, target = pairs[which]
        return remote(
            source,
            target.at[pl.ds(pl.multiple_of(section_at * rows, rows), rows)],
            lat_sems,
            (which, way),
            (flat[way], batch_at),
        )

    def lat_far(which, way):
        target = pairs[which][1]
        first = flat[way] * rows + way * (rows // 2)
        part = target.at[pl.ds(pl.multiple_of(first, rows // 2), rows // 2)]
        return remote(part, part, far_sems, (which, way), (flat[1 - way], batch_at))

    def lat_local(which):
        source, target = pairs[which]
        return pltpu.make_async_copy(
            source,
            target.at[pl.ds(pl.multiple_of(section_at * rows, rows), rows)],
            lat_own.at[which],
        )

    def point_local():
        return pltpu.make_async_copy(
            point_sum,
            point_out.at[pl.ds(pl.multiple_of(section_at * quarter, quarter), quarter)],
            point_own.at[0],
        )

    def window_copies(item):
        slot = item % WINDOWS
        copies = []
        for side in range(2):
            job, start = ITEMS[item][side]
            here = pl.ds(side * HALF, HALF)
            copies += [
                pltpu.make_async_copy(
                    rights[job].at[:, pl.ds(start, HALF)],
                    rwin.at[slot, pl.ds(0, 256), here],
                    win_sems.at[slot, side, 0],
                ),
                pltpu.make_async_copy(
                    kin_right.at[:, pl.ds(starts[job] + start, HALF)],
                    rwin.at[slot, pl.ds(256, 256), here],
                    win_sems.at[slot, side, 1],
                ),
            ]
        return copies

    def raw_copies(job):
        copies = []
        for part in range(4):
            copies += [
                pltpu.make_async_copy(
                    lefts[job].at[:, columns(part, core)], raw.at[part, 0], raw_sems.at[part, 0]
                ),
                pltpu.make_async_copy(
                    kin_left.at[job, part], raw.at[part, 1], raw_sems.at[part, 1]
                ),
            ]
        return copies

    seen = set()
    fresh = []
    for item in range(total):
        fresh.append([])
        for job, _ in ITEMS[item]:
            if job not in seen:
                seen.add(job)
                fresh[item].append(job)

    def load(item):
        for side in range(2):
            kin_block(item, side).wait_recv()
        for copy in window_copies(item):
            copy.start()
        for job in fresh[item]:
            for copy in kin_lefts(job):
                copy.wait_recv()
            copies = raw_copies(job)
            for copy in copies:
                copy.start()
            for copy in copies:
                copy.wait()
            for part in range(4):
                for whose in range(2):
                    lwin[job, part, :, whose * 256 : whose * 256 + 256] = raw[part, whose].T

    def loaded(slot):
        for side in range(2):
            here = pl.ds(side * HALF, HALF)
            pltpu.make_async_copy(
                rights[0].at[:, pl.ds(0, HALF)],
                rwin.at[slot, pl.ds(0, 256), here],
                win_sems.at[slot, side, 0],
            ).wait()
            pltpu.make_async_copy(
                kin_right.at[:, pl.ds(0, HALF)],
                rwin.at[slot, pl.ds(256, 256), here],
                win_sems.at[slot, side, 1],
            ).wait()

    def job_of(item, side):
        job, base = 0, item * 0
        for index in range(1, jobs):
            base = base + (item * 2 + side >= starts[index] // HALF).astype(jnp.int32)
        return job + base

    bits = (x_at, y_at)

    def product(slot, job, side, bit, upper):
        left = lwin[job, pl.ds(upper * 2, 2)].reshape(256, 512)
        first = pl.multiple_of(side * HALF + bit * KEPT, KEPT)
        right = rwin[slot, :, pl.ds(first, KEPT)]
        return jnp.dot(left, right, preferred_element_type=F32).reshape(2, 128, KEPT)

    def xy_copy(item, side):
        here = pl.ds(side * KEPT, KEPT)
        return remote(
            stage.at[lax.rem(item, STAGES), :, :, here],
            merged.at[item, :, :, here],
            xy_sems,
            (item, side),
            (flat[side], batch_at),
        )

    def offer(item):
        slot = lax.rem(item, WINDOWS)
        loaded(slot)

        @pl.when(item >= STAGES)
        def _():
            for side in range(2):
                xy_copy(item - STAGES, side).wait_send()

        for side in range(2):
            job = job_of(item, side)

            def half(upper, carry):
                tile = product(slot, job, side, 1 - bits[side], upper)
                stage[
                    lax.rem(item, STAGES), pl.ds(upper * 2, 2), :, side * KEPT : side * KEPT + KEPT
                ] = tile.astype(BF)
                return carry

            lax.fori_loop(0, 2, half, 0)
            xy_copy(item, side).start()

    def line_copy(item, dest, place, rightward):
        step = 1 if rightward else -1
        slot = 4 if not rightward and place - 1 == dest else dest
        return pltpu.make_async_remote_copy(
            merged.at[item, dest],
            passing.at[item, slot],
            line_send.at[item, dest],
            line_recv.at[item, slot],
            device_id=(section_at, batch_at + 2 * step),
            device_id_type=MESH,
        )

    def line_wait(item, slot):
        pltpu.make_async_remote_copy(
            merged.at[item, 0],
            passing.at[item, slot],
            line_send.at[item, 0],
            line_recv.at[item, slot],
            device_id=(section_at, sibling),
            device_id_type=MESH,
        ).wait_recv()

    def keep(item):
        slot = lax.rem(item, WINDOWS)
        for side in range(2):
            xy_copy(item, side).wait_recv()
            job = job_of(item, side)

            def half(upper, carry):
                here = (item, pl.ds(upper * 2, 2), slice(None), slice(side * KEPT, side * KEPT + KEPT))
                tile = product(slot, job, side, bits[side], upper)
                merged[here] = (tile + merged[here].astype(F32)).astype(BF)
                return carry

            lax.fori_loop(0, 2, half, 0)

        @pl.when(spot == 0)
        def _():
            for dest in (3, 2, 1):
                line_copy(item, dest, 0, True).start()

        @pl.when(spot == 3)
        def _():
            for dest in (0, 1, 2):
                line_copy(item, dest, 3, False).start()

    def relay(item, dest, place, rightward):
        line_wait(item, dest)
        merged[item, dest] = (
            merged[item, dest].astype(F32) + passing[item, dest].astype(F32)
        ).astype(BF)
        line_copy(item, dest, place, rightward).start()

    def second(item):
        @pl.when(spot == 1)
        def _():
            for dest in (3, 2):
                relay(item, dest, 1, True)

        @pl.when(spot == 2)
        def _():
            for dest in (0, 1):
                relay(item, dest, 2, False)

    def third(item):
        @pl.when(spot == 1)
        def _():
            relay(item, 0, 1, False)

        @pl.when(spot == 2)
        def _():
            relay(item, 3, 2, True)

    def cross_copy(item, side):
        here = pl.ds(side * KEPT, KEPT)
        return remote(
            lined.at[item, :, here],
            crossed.at[item, :, here],
            cross_sems,
            (item, side),
            (flat[1 - side], batch_at),
        )

    def close(item):
        @pl.when(spot == 0)
        def _():
            line_wait(item, 4)
            lined[item] = (
                merged[item, 0].astype(F32) + passing[item, 4].astype(F32)
            ).astype(BF)

        @pl.when(spot == 3)
        def _():
            line_wait(item, 3)
            lined[item] = (
                merged[item, 3].astype(F32) + passing[item, 3].astype(F32)
            ).astype(BF)

        for middle in (1, 2):

            @pl.when(spot == middle)
            def _():
                line_wait(item, middle)
                line_wait(item, 4)
                lined[item] = (
                    merged[item, middle].astype(F32)
                    + passing[item, middle].astype(F32)
                    + passing[item, 4].astype(F32)
                ).astype(BF)

        for side in range(2):
            cross_copy(item, side).start()

    def out_place(item, side, bit):
        layer = 1 - item // (total // 2)
        inner = lax.rem(item, total // 2)
        first = pl.multiple_of(inner * (2 * HALF) + side * HALF + bit * KEPT, KEPT)
        return sum_out.at[layer, :, pl.ds(first, KEPT)]

    def out_copy(item, side):
        return remote(
            settled.at[item, :, pl.ds(side * KEPT, KEPT)],
            out_place(item, side, bits[side]),
            out_sems,
            (item, side),
            (flat[side], batch_at),
        )

    def out_local(item, side):
        return pltpu.make_async_copy(
            settled.at[item, :, pl.ds(side * KEPT, KEPT)],
            out_place(item, side, bits[side]),
            own_sems.at[item, side],
        )

    def finish(item):
        for side in range(2):
            cross_copy(item, side).wait_recv()
        settled[item] = (lined[item].astype(F32) + crossed[item].astype(F32)).astype(BF)
        for side in range(2):
            out_copy(item, side).start()
            out_local(item, side).start()

    def kin_start(item):
        for job in fresh[item]:
            for copy in kin_lefts(job):
                copy.start()
        for side in range(2):
            kin_block(item, side).start()

    for item in range(2):
        kin_start(item)
    small_sum[0] = small_ref[...]
    small_copy(0).start()
    for which in range(2):
        lat_local(which).start()
        for way in range(2):
            lat_copy(which, way).start()
    for which in range(3):
        point_copy(which).start()
    for item in range(2, total):
        kin_start(item)
    load(0)

    def sidework(moment):
        @pl.when(moment == 2)
        def _():
            for which in range(2):
                for way in range(2):
                    lat_copy(which, way).wait_recv()
                    lat_far(which, way).start()
            for which in range(3):
                point_copy(which).wait_recv()
            gathered = point_ref[
                pl.ds(pl.multiple_of(section_at * quarter, quarter), quarter)
            ].astype(F32)
            for which in range(3):
                gathered += point_in[which].astype(F32)
            point_sum[...] = gathered.astype(BF)
            point_local().start()
            for which in range(3):
                point_deal(which).start()

        for phase in range(3):

            @pl.when(moment == 2 + 2 * phase)
            def _():
                small_copy(phase).wait_recv()
                small_sum[phase + 1] = small_sum[phase] + small_in[phase]
                if phase < 2:
                    small_copy(phase + 1).start()
                else:
                    for step in range(3):
                        small_copy(3 + step).start()

        @pl.when(moment == 8)
        def _():
            for step in range(3):
                small_copy(3 + step).wait_recv()
            small_out[...] = (small_sum[3] + small_in[4]) + (small_in[3] + small_in[5])

    def moment_body(moment, carry):
        for item in range(1, total):
            pl.when(moment == item - 1)(functools.partial(load, item))

        pl.when(moment < total)(lambda: offer(moment))
        for lag, action in ((2, keep), (3, second), (4, third), (5, close), (6, finish)):
            pl.when(jnp.logical_and(moment >= lag, moment < total + lag))(
                functools.partial(action, moment - lag)
            )
        sidework(moment)
        return carry

    lax.fori_loop(0, total + 6, moment_body, 0)

    for job in range(jobs):
        for copy in kin_lefts(job):
            copy.wait_send()
    for item in range(total):
        for side in range(2):
            kin_block(item, side).wait_send()
    for phase in range(6):
        small_copy(phase).wait_send()
    for which in range(2):
        lat_local(which).wait()
        for way in range(2):
            lat_copy(which, way).wait_send()
            lat_far(which, way).wait()
    point_local().wait()
    for which in range(3):
        point_copy(which).wait_send()
        point_deal(which).wait()

    def drain(item, carry):
        @pl.when(item >= total - STAGES)
        def _():
            for side in range(2):
                xy_copy(item, side).wait_send()

        for step in (1, 2, 3):
            dest = lax.rem(spot + step, 4)
            pltpu.make_async_remote_copy(
                merged.at[item, dest],
                passing.at[item, 0],
                line_send.at[item, dest],
                line_recv.at[item, 0],
                device_id=(section_at, sibling),
                device_id_type=MESH,
            ).wait_send()
        for side in range(2):
            cross_copy(item, side).wait_send()
            out_copy(item, side).wait()
            out_local(item, side).wait()
        return carry

    lax.fori_loop(0, total, drain, 0)


def reduce_all(lefts, rights, last, first, point_part, small):
    jobs = len(JOBS)
    total = len(ITEMS)
    columns = sum(JOBS)
    width = last.shape[1]
    anywhere = pl.BlockSpec(memory_space=pl.ANY)
    vmem = pl.BlockSpec(memory_space=pltpu.VMEM)
    dma = pltpu.SemaphoreType.DMA
    flops = 2 * columns * 512 * 512 * 2
    return pl.pallas_call(
        reduce_kernel,
        out_shape=[
            jax.ShapeDtypeStruct((2, 128, columns // 2), BF),
            jax.ShapeDtypeStruct((4 * last.shape[0], width), BF),
            jax.ShapeDtypeStruct((4 * first.shape[0], width), BF),
            jax.ShapeDtypeStruct(point_part.shape, BF),
            jax.ShapeDtypeStruct(small.shape, F32),
            jax.ShapeDtypeStruct((jobs, 4, 256, 128), BF),
            jax.ShapeDtypeStruct((256, columns), BF),
        ],
        in_specs=[anywhere] * (2 * jobs + 2) + [vmem, vmem],
        out_specs=[anywhere] * 4 + [vmem] + [anywhere] * 2,
        scratch_shapes=[
            pltpu.VMEM((jobs, 4, 128, 512), BF),
            pltpu.VMEM((4, 2, 256, 128), BF),
            pltpu.VMEM((WINDOWS, 512, 2 * HALF), BF),
            pltpu.VMEM((STAGES, 4, 128, 2 * KEPT), BF),
            pltpu.VMEM((total, 4, 128, 2 * KEPT), BF),
            pltpu.VMEM((total, 5, 128, 2 * KEPT), BF),
            pltpu.VMEM((total, 128, 2 * KEPT), BF),
            pltpu.VMEM((total, 128, 2 * KEPT), BF),
            pltpu.VMEM((total, 128, 2 * KEPT), BF),
            pltpu.VMEM((3, point_part.shape[0] // 4, width), BF),
            pltpu.VMEM((point_part.shape[0] // 4, width), BF),
            pltpu.VMEM((6, *small.shape), F32),
            pltpu.VMEM((4, *small.shape), F32),
            dma((2, jobs, 4)),
            dma((2, total, 2)),
            dma((4, 2)),
            dma((WINDOWS, 2, 2)),
            dma((2, total, 2)),
            dma((total, 4)),
            dma((total, 5)),
            dma((2, total, 2)),
            dma((2, total, 2)),
            dma((total, 2)),
            dma((2, 2, 2)),
            dma((2, 2, 2)),
            dma((2,)),
            dma((2, 3)),
            dma((2, 3)),
            dma((1,)),
            dma((2, 6)),
        ],
        compiler_params=pltpu.CompilerParams(
            collective_id=2, has_side_effects=True, vmem_limit_bytes=60 * 2**20
        ),
        cost_estimate=pl.CostEstimate(flops=flops, bytes_accessed=2**26, transcendentals=0),
    )(*lefts, *rights, last, first, point_part, small)[:5]


def per_device(
    latents,
    points,
    neighbours,
    lengths,
    cross_proj,
    cross_out,
    cross_gains,
    self_proj,
    self_out,
    self_gain,
    mlp_gain,
    mlp_in,
    mlp_in_bias,
    mlp_down,
    mlp_out_bias,
    cotangent,
):
    sections = lax.axis_size("section")
    section_at = lax.axis_index("section")
    width = latents.shape[1]
    hidden = mlp_in.shape[2]
    groups_dev = neighbours.shape[0]
    rows = latents.shape[0] // sections
    shard = cross_out.shape[0]
    piece = shard // sections
    groups_all = groups_dev * lax.axis_size("batch")

    def gathered(block):
        own = lax.dynamic_slice_in_dim(block, section_at * piece, piece, 0)
        return lax.all_gather(own, ALL, axis=0, tiled=True)

    vectors = jnp.concatenate(
        [
            cross_gains.reshape(-1),
            self_gain,
            mlp_gain.reshape(-1),
            mlp_out_bias.reshape(-1),
            mlp_in_bias.reshape(-1),
            jnp.zeros_like(self_gain),
        ]
    ).reshape(-1, shard)
    projs = (cross_proj.reshape(shard, 3 * width), self_proj.reshape(shard, 3 * width))
    small_slice = lax.axis_size("batch") == 8
    latents_own = lax.dynamic_slice_in_dim(latents, section_at * rows, rows, 0)
    cot_own = lax.dynamic_slice_in_dim(cotangent, section_at * rows, rows, 0)
    mine = latents_own.astype(F32)
    listed = lax.dynamic_index_in_dim(neighbours, section_at, 0, keepdims=False)
    length = lax.dynamic_index_in_dim(lengths, section_at, 0, keepdims=False)
    valid = jnp.arange(listed.shape[0], dtype=jnp.int32) < length
    picks = listed[:, None] == jnp.arange(points.shape[0], dtype=jnp.int32)[None, :]
    picks = picks.astype(BF)
    source = mm(picks, points)
    if small_slice:
        made = gather_forward(
            [projs[0], cross_out, mlp_in, mlp_down, projs[1], self_out],
            vectors,
            latents_own,
            source.astype(BF),
            valid.astype(F32)[None, :],
            cot_own,
        )
        full, spread, norm_tile, made = made[:8], made[8], made[9], made[10:]
    else:
        blocks = [projs[0], cross_out, mlp_in[0], mlp_down[0]]
        blocks += [projs[1], self_out, mlp_in[1], mlp_down[1]]
        full = [gathered(block) for block in blocks]
        spread = lax.all_gather(vectors, "batch", axis=0, tiled=False)
    proj_c, out_c, in_0, down_0, proj_s, out_s, in_1, down_1 = full
    spread = spread.astype(F32)

    def vector(first, count):
        return spread[:, first : first + count].reshape(-1)

    gains_cross = (vector(0, 1), vector(1, 1))
    gain_self = vector(2, 1)
    gains_mlp = (vector(3, 1), vector(4, 1))
    biases_out = (vector(5, 1), vector(6, 1))
    per_bias = hidden // width
    biases_in = (vector(7, per_bias), vector(7 + per_bias, per_bias))

    if small_slice:
        u1, u2, u3, u4, g4, xq_c, sn_c, q_c, k_c, v_c, o_c, xn_s, q_s, k_s, v_s, o_s = made[:16]
        lowered, before, active = made[16:]
        norm_mean = norm_tile[0, 0]
        unit_x, unit_s = unit_rows(mine), unit_rows(source)
        kept_c = (*unit_x, xq_c, *unit_s, sn_c, q_c, k_c, v_c, softmax(q_c, k_c, valid), o_c)
        unit_u = unit_rows(u2.astype(F32))
        kept_s = (*unit_u, xn_s, *unit_u, xn_s, q_s, k_s, v_s, softmax(q_s, k_s, None), o_s)
        kept_0 = (*unit_rows(u1.astype(F32)), lowered[0], before[0], active[0])
        kept_1 = (*unit_rows(u3.astype(F32)), lowered[1], before[1], active[1])
    else:
        cot = cot_own.astype(F32)
        u1, kept_c = attend(mine, source, valid, gains_cross[0], gains_cross[1], proj_c, out_c)
        u2, kept_0 = feed(u1.astype(F32), gains_mlp[0], in_0, biases_in[0], down_0, biases_out[0])
        u2 = u2.astype(F32)
        u3, kept_s = attend(u2, u2, None, gain_self, gain_self, proj_s, out_s)
        u4, kept_1 = feed(u3.astype(F32), gains_mlp[1], in_1, biases_in[1], down_1, biases_out[1])
        final = u4.astype(F32)
        group_norm = jnp.sqrt(jnp.mean(final * final) + EPSILON)
        norm_mean = lax.psum(group_norm, ALL) / groups_all
        g4 = (cot + (norm_mean / group_norm) * final).astype(BF)

    dx, gain_1_grad, bias_1_grad, ob_1_grad, pairs_1 = feed_back(
        g4, kept_1, gains_mlp[1], in_1, down_1
    )
    g3 = (g4.astype(F32) + dx).astype(BF)
    dx, ds, gq, gkv, pairs_s = attend_back(g3, kept_s, gain_self, gain_self, proj_s, out_s)
    gain_s_grad = gq + gkv
    g2 = (g3.astype(F32) + dx + ds).astype(BF)
    dx, gain_0_grad, bias_0_grad, ob_0_grad, pairs_0 = feed_back(
        g2, kept_0, gains_mlp[0], in_0, down_0
    )
    g1 = (g2.astype(F32) + dx).astype(BF)
    dx, ds, cq_grad, ckv_grad, pairs_c = attend_back(
        g1, kept_c, gains_cross[0], gains_cross[1], proj_c, out_c
    )
    g0 = (g1.astype(F32) + dx).astype(BF)
    high = ds.astype(BF)
    low = (ds - high.astype(F32)).astype(BF)
    point_part = (mm_rows(picks, high) + mm_rows(picks, low)).astype(BF)
    small = jnp.concatenate(
        [
            cq_grad,
            ckv_grad,
            gain_s_grad,
            gain_0_grad,
            gain_1_grad,
            ob_0_grad,
            ob_1_grad,
            bias_0_grad,
            bias_1_grad,
            jnp.zeros_like(cq_grad),
        ]
    ).reshape(-1, width)
    pairs = pairs_1 + pairs_s + pairs_0 + pairs_c
    lefts, rights = [pair[0] for pair in pairs], [pair[1] for pair in pairs]
    if small_slice:
        sums, latents_out, g0_all, points_sum, small = reduce_all(
            lefts, rights, u4, g0, point_part, small
        )

        attn = 2 * hidden
        mlp_in_grad = sums[:, :, :hidden].astype(F32)
        mlp_down_grad = sums[:, :, hidden:attn].astype(F32)
        proj_c_grad, proj_s_grad = [
            sums[layer, :, attn : attn + 3 * width].astype(F32) for layer in range(2)
        ]
        out_c_grad, out_s_grad = [
            sums[layer, :, attn + 3 * width :].astype(F32) for layer in range(2)
        ]
    else:

        def settled_grad(left, right):
            part = lax.psum_scatter(
                mm_rows(left, right).astype(BF), ALL, scatter_dimension=0, tiled=True
            )
            return lax.all_gather(part, "section", axis=0, tiled=True).astype(F32)

        done = [settled_grad(left, right) for left, right in pairs]
        mlp_in_grad = jnp.stack([done[6], done[0]])
        mlp_down_grad = jnp.stack([done[7], done[1]])
        proj_s_grad = jnp.concatenate(done[2:5], axis=1)
        proj_c_grad = jnp.concatenate(done[8:11], axis=1)
        out_s_grad, out_c_grad = done[5], done[11]
        points_sum = lax.psum(point_part, "section")
        latents_out = lax.all_gather(u4, "section", axis=0, tiled=True)
        g0_all = lax.all_gather(g0, "section", axis=0, tiled=True)
        small = lax.psum(small, ALL)
    points_grad = points_sum.astype(F32)
    latents_grad = g0_all.astype(F32)
    batch_at = lax.axis_index("batch")

    def own(first, count):
        flat = small[first : first + count].reshape(-1)
        size = flat.shape[0] // lax.axis_size("batch")
        return lax.dynamic_slice_in_dim(flat, batch_at * size, size, 0)

    return (
        latents_out,
        latents_grad,
        points_grad,
        proj_c_grad.reshape(shard, 3, width),
        out_c_grad,
        jnp.stack([own(0, 1), own(1, 1)]),
        proj_s_grad.reshape(shard, 3, width),
        out_s_grad,
        own(2, 1),
        jnp.stack([own(3, 1), own(4, 1)]),
        mlp_in_grad,
        jnp.stack([own(7, per_bias), own(7 + per_bias, per_bias)]),
        mlp_down_grad,
        jnp.stack([own(5, 1), own(6, 1)]),
        norm_mean,
    )


def solution(mesh):
    rows = P("batch", None)
    cols = P(None, "batch")
    block = P("batch", None, None)
    pair = P(None, "batch", None)
    return jax.shard_map(
        per_device,
        mesh=mesh,
        in_specs=(
            rows,
            rows,
            rows,
            P("batch"),
            block,
            rows,
            cols,
            block,
            rows,
            P("batch"),
            cols,
            pair,
            cols,
            pair,
            cols,
            rows,
        ),
        out_specs=(
            rows,
            rows,
            rows,
            block,
            rows,
            cols,
            block,
            rows,
            P("batch"),
            cols,
            pair,
            cols,
            pair,
            cols,
            P(),
        ),
        check_vma=False,
    )
```

```python
import functools
import math

import jax
import jax.numpy as jnp
from jax import lax
from jax.experimental import pallas as pl
from jax.experimental.pallas import tpu as pltpu
from jax.sharding import PartitionSpec as P

HD = 128
EPSILON = 1e-05
MASKED = -1e30
BF = jnp.bfloat16
F32 = jnp.float32
ALL = ("batch", "section")
MESH = pl.DeviceIdType.MESH
GATHER_WIDTH = 1024
AHEAD = 4
SLOTS = 3
GATHERED = tuple(
    (4 * layer + index, start)
    for layer in range(2)
    for index, start in (
        [(0, 0), (0, 1024), (0, 2048), (1, 0)]
        + [(2 + which, chunk) for chunk in range(0, 2048, 1024) for which in range(2)]
    )
)


def mm(a, b):
    return jnp.dot(a, b, preferred_element_type=F32)


def mm_rows(a, b):
    return lax.dot_general(a, b, (((0,), (0,)), ((), ())), preferred_element_type=F32)


def mm_cols(a, b):
    return lax.dot_general(a, b, (((1,), (1,)), ((), ())), preferred_element_type=F32)


def unit_rows(values):
    centred = values - jnp.mean(values, axis=-1, keepdims=True)
    inverse = lax.rsqrt(jnp.mean(centred * centred, axis=-1, keepdims=True) + EPSILON)
    return centred * inverse, inverse


def norm_back(gradient, unit, inverse, gain):
    scaled = gradient * gain
    inner = (
        scaled
        - jnp.mean(scaled, axis=-1, keepdims=True)
        - unit * jnp.mean(scaled * unit, axis=-1, keepdims=True)
    )
    return inverse * inner, jnp.sum(gradient * unit, axis=0)


def heads_of(rows):
    return rows.reshape(rows.shape[0], -1, HD)


def softmax(q, k, valid):
    scores = jnp.einsum(
        "lhc,nhc->hln", heads_of(q), heads_of(k), preferred_element_type=F32
    ) * (1.0 / math.sqrt(HD))
    if valid is not None:
        scores = jnp.where(valid[None, None, :], scores, MASKED)
    grown = jnp.exp(scores - jnp.max(scores, axis=-1, keepdims=True))
    return grown / jnp.sum(grown, axis=-1, keepdims=True)


def attend(inputs, source, valid, gain_q, gain_kv, proj, out):
    unit_x, inv_x = unit_rows(inputs)
    queries_in = (unit_x * gain_q).astype(BF)
    unit_s, inv_s = unit_rows(source)
    keys_in = (unit_s * gain_kv).astype(BF)
    width = inputs.shape[1]
    q = mm(queries_in, proj[:, :width]).astype(BF)
    kv = mm(keys_in, proj[:, width:]).astype(BF)
    k, v = kv[:, :width], kv[:, width:]
    soft = softmax(q, k, valid)
    mixture = jnp.einsum("hln,nhc->lhc", soft.astype(BF), heads_of(v), preferred_element_type=F32)
    mixture = mixture.reshape(inputs.shape).astype(BF)
    result = (inputs + mm(mixture, out)).astype(BF)
    return result, (unit_x, inv_x, queries_in, unit_s, inv_s, keys_in, q, k, v, soft, mixture)


def attend_back(gradient, kept, gain_q, gain_kv, proj, out):
    unit_x, inv_x, queries_in, unit_s, inv_s, keys_in, q, k, v, soft, mixture = kept
    width = gradient.shape[1]
    scale = 1.0 / math.sqrt(HD)
    grad_mix = mm_cols(gradient, out).astype(BF)
    grad_soft = jnp.einsum(
        "lhc,nhc->hln", heads_of(grad_mix), heads_of(v), preferred_element_type=F32
    )
    inner = jnp.sum(soft * grad_soft, axis=-1, keepdims=True)
    grad_scores = (soft * (grad_soft - inner)).astype(BF)
    dq = jnp.einsum("hln,nhc->lhc", grad_scores, heads_of(k), preferred_element_type=F32) * scale
    dk = jnp.einsum("hln,lhc->nhc", grad_scores, heads_of(q), preferred_element_type=F32) * scale
    dv = jnp.einsum(
        "hln,lhc->nhc", soft.astype(BF), heads_of(grad_mix), preferred_element_type=F32
    )
    dq = dq.reshape(gradient.shape).astype(BF)
    dk = dk.reshape(-1, width).astype(BF)
    dv = dv.reshape(-1, width).astype(BF)
    grad_x, gain_q_grad = norm_back(mm_cols(dq, proj[:, :width]), unit_x, inv_x, gain_q)
    back_s = mm_cols(dk, proj[:, width : 2 * width]) + mm_cols(dv, proj[:, 2 * width :])
    grad_s, gain_kv_grad = norm_back(back_s, unit_s, inv_s, gain_kv)
    pairs = ((queries_in, dq), (keys_in, dk), (keys_in, dv), (mixture, gradient))
    return grad_x, grad_s, gain_q_grad, gain_kv_grad, pairs


def feed(inputs, gain, w_in, b_in, w_down, b_out):
    unit, inverse = unit_rows(inputs)
    lowered = (unit * gain).astype(BF)
    pre_act = mm(lowered, w_in) + b_in
    active = jax.nn.gelu(pre_act).astype(BF)
    result = (inputs + mm_cols(active, w_down) + b_out).astype(BF)
    return result, (unit, inverse, lowered, pre_act, active)


def feed_back(gradient, kept, gain, w_in, w_down):
    unit, inverse, lowered, pre_act, active = kept
    grad_act = mm(gradient, w_down)
    grad_pre = jax.vjp(jax.nn.gelu, pre_act)[1](grad_act)[0].astype(BF)
    grad_x, gain_grad = norm_back(mm_cols(grad_pre, w_in), unit, inverse, gain)
    bias_grad = jnp.sum(grad_pre.astype(F32), axis=0)
    out_grad = jnp.sum(gradient.astype(F32), axis=0)
    return grad_x, gain_grad, bias_grad, out_grad, ((lowered, grad_pre), (gradient, active))


def gelu(value):
    inner = math.sqrt(2.0 / math.pi) * (value + 0.044715 * (value * value * value))
    return value * (0.5 * (1.0 + jnp.tanh(inner)))


def tiles(count, body):
    def step(index, carry):
        body(pl.ds(pl.multiple_of(index * 256, 256), 256), index)
        return carry

    lax.fori_loop(0, count, step, 0)


def norm_into(source, gain, target):
    def step(index, carry):
        here = pl.ds(pl.multiple_of(index * 32, 32), 32)
        unit, _ = unit_rows(source[here, :].astype(F32))
        target[here, :] = (unit * gain).astype(BF)
        return carry

    lax.fori_loop(0, source.shape[0] // 32, step, 0)


def gather_kernel(*refs):
    cross_proj, cross_out, mlp_in, mlp_down, self_proj, self_out = refs[:6]
    vec_in, x_in, src_in, mask_in, cot_in = refs[6:11]
    section_at = lax.axis_index("section")
    batch_at = lax.axis_index("batch")
    x_at = lax.rem(section_at, 2)
    y_at = section_at // 2
    ins = (
        cross_proj,
        cross_out,
        mlp_in.at[0],
        mlp_down.at[0],
        self_proj,
        self_out,
        mlp_in.at[1],
        mlp_down.at[1],
    )
    count = len(ins)
    outs = refs[11 : 11 + count]
    rest = refs[11 + count :]
    gains, norm_out = rest[:2]
    kept_outs = rest[2:21]
    (
        u1,
        u2,
        u3,
        u4,
        grad_top,
        xq_c,
        sn_c,
        q_c,
        k_c,
        v_c,
        o_c,
        xn_s,
        q_s,
        k_s,
        v_s,
        o_s,
        lowered,
        before,
        active,
        slots,
        total_rows,
        part_out,
        part_in,
        vec_out,
        biases,
        plane,
        line_in,
    ) = rest[21:48]
    (own_sem, send, recv, kin_send, kin_recv, vec_sems) = rest[48:54]
    (slot_sems, kept_sems, plane_sems, line_sems, pair_sems) = rest[54:]
    line = 4
    core = lax.rem(batch_at, 2)
    spot = batch_at // 2
    beside = section_at + 1 - 2 * x_at
    above = lax.rem(section_at + 2, 4)
    sibling = batch_at + 1 - 2 * core
    shard = ins[0].shape[0]
    place = section_at * 2 + core
    rows = x_in.shape[0]

    def down_line(step):
        return lax.rem(spot + step, line) * 2 + core

    def up_line(step):
        return lax.rem(spot + line - step, line) * 2 + core

    near_peers = []
    for turn in range(1, 8):
        other = lax.rem(place + turn, 8)
        near_peers.append((other // 2, spot * 2 + lax.rem(other, 2)))
    line_peers = [(section_at, down_line(step)) for step in range(1, line)]
    far_peers = [(section_at, down_line(step) + 1 - 2 * core) for step in range(1, line)]
    vec_peers = [(section_at, sibling)] + line_peers + far_peers
    peers = near_peers + line_peers + far_peers
    barrier = pltpu.get_barrier_semaphore()
    for peer in peers:
        pl.semaphore_signal(barrier, inc=1, device_id=peer, device_id_type=MESH)
    pl.semaphore_wait(barrier, len(peers))

    def spread(ref, owner, first, size):
        return ref.at[pl.ds(pl.multiple_of(owner * shard, shard), shard), pl.ds(first, size)]

    def is_feed(item):
        return item % 8 >= 4

    def source_of(item, first, size):
        index, start = GATHERED[item]
        if is_feed(item):
            first = pl.multiple_of(first + y_at * outs[index].shape[1], 128)
        return ins[index].at[:, pl.ds(first, size)]

    def piece(item):
        start = GATHERED[item][1]
        if is_feed(item):
            return pl.multiple_of(start + x_at * 512, 128), 512
        return pl.multiple_of(start + section_at * 256, 128), 256

    def line_copy(item, step):
        first, size = piece(item)
        return pltpu.make_async_remote_copy(
            source_of(item, first, size),
            spread(outs[GATHERED[item][0]], batch_at, first, size),
            send.at[0, item, step],
            recv.at[0, item, step],
            device_id=(section_at, down_line(step)),
            device_id_type=MESH,
        )

    def plane_copy(item, step, way, low, wide, peer):
        ref = spread(outs[GATHERED[item][0]], up_line(step), low, wide)
        return pltpu.make_async_remote_copy(
            ref,
            ref,
            send.at[way, item, step],
            recv.at[way, item, step],
            device_id=(peer, batch_at),
            device_id_type=MESH,
        )

    def near(item, step):
        first, size = piece(item)
        copies = [plane_copy(item, step, 1, first, size, beside)]
        if not is_feed(item):
            copies.append(plane_copy(item, step, 2, first, size, above))
        return copies

    def far(item, step):
        start = GATHERED[item][1]
        by_y = pl.multiple_of(start + beside * 256, 128)
        by_x = pl.multiple_of(start + above * 256 + 128, 128)
        return [
            plane_copy(item, step, 3, by_y, 128, above),
            plane_copy(item, step, 4, by_x, 128, beside),
        ]

    def kin(item, step):
        index, start = GATHERED[item]
        if step == 0:
            source = source_of(item, start, GATHER_WIDTH)
        else:
            source = spread(outs[index], up_line(step), start, GATHER_WIDTH)
        return pltpu.make_async_remote_copy(
            source,
            spread(outs[index], up_line(step), start, GATHER_WIDTH),
            kin_send.at[item, step],
            kin_recv.at[item, step],
            device_id=(section_at, sibling),
            device_id_type=MESH,
        )

    def own(item):
        index, start = GATHERED[item]
        return pltpu.make_async_copy(
            source_of(item, start, GATHER_WIDTH),
            spread(outs[index], batch_at, start, GATHER_WIDTH),
            own_sem.at[item],
        )

    def vec_copy(which):
        return pltpu.make_async_remote_copy(
            vec_in,
            vec_out.at[batch_at],
            vec_sems.at[0, which],
            vec_sems.at[1, which],
            device_id=vec_peers[which],
            device_id_type=MESH,
        )

    def slot_copy(item):
        index, start = GATHERED[item]
        return pltpu.make_async_copy(
            outs[index].at[:, pl.ds(start, GATHER_WIDTH)],
            slots.at[item % SLOTS],
            slot_sems.at[item % SLOTS],
        )

    def near_norm(turn):
        return pltpu.make_async_remote_copy(
            plane.at[8],
            plane.at[place],
            plane_sems.at[0, turn],
            plane_sems.at[1, turn],
            device_id=near_peers[turn],
            device_id_type=MESH,
        )

    def far_norm(step):
        return pltpu.make_async_remote_copy(
            line_in.at[4],
            line_in.at[spot],
            line_sems.at[0, step],
            line_sems.at[1, step],
            device_id=line_peers[step],
            device_id_type=MESH,
        )

    def rows_over(layer):
        return pltpu.make_async_remote_copy(
            lowered.at[layer, pl.ds(0, rows)],
            lowered.at[layer, pl.ds(rows, rows)],
            pair_sems.at[0, layer, 0],
            pair_sems.at[1, layer, 0],
            device_id=(above, batch_at),
            device_id_type=MESH,
        )

    def part_over(layer):
        return pltpu.make_async_remote_copy(
            part_out.at[layer],
            part_in.at[layer],
            pair_sems.at[0, layer, 1],
            pair_sems.at[1, layer, 1],
            device_id=(above, batch_at),
            device_id_type=MESH,
        )

    steps = range(1, line)
    total = len(GATHERED)
    started = []

    def launch(copies):
        for copy in copies:
            copy.start()
        started.extend(copies)

    kept = (
        (u1, u2, u3, u4, grad_top)
        + (xq_c, sn_c, q_c, k_c, v_c, o_c)
        + (xn_s, q_s, k_s, v_s, o_s)
        + (lowered, before, active)
    )
    names = {id(ref): place for place, ref in enumerate(kept)}

    def keep(*chosen):
        for ref in chosen:
            index = names[id(ref)]
            pltpu.make_async_copy(ref, kept_outs[index], kept_sems.at[index]).start()

    def row(index):
        return gains[index : index + 1, :]

    def project(source, target, slot):
        def tile(columns, _):
            target[:, columns] = mm(source[...], slots[slot, :, columns]).astype(BF)

        tiles(4, tile)

    def heads(q, k, v, o, masked):
        def head(index, carry):
            here = pl.ds(pl.multiple_of(index * HD, HD), HD)
            scores = mm_cols(q[:, here], k[:, here]) * (1.0 / math.sqrt(HD))
            if masked:
                scores = jnp.where(mask_in[...] > 0.0, scores, MASKED)
            grown = jnp.exp(scores - jnp.max(scores, axis=-1, keepdims=True))
            soft = grown / jnp.sum(grown, axis=-1, keepdims=True)
            o[:, here] = mm(soft.astype(BF), v[:, here]).astype(BF)
            return carry

        lax.fori_loop(0, q.shape[1] // HD, head, 0)

    def close_attention(inputs, o, target, slot):
        def tile(columns, _):
            target[:, columns] = (
                inputs[:, columns].astype(F32) + mm(o[...], slots[slot, :, columns])
            ).astype(BF)

        tiles(4, tile)

    def feed_up(layer, chunk, slot):
        def tile(columns, index):
            first = chunk * GATHER_WIDTH + index * 256
            there = pl.ds(pl.multiple_of(first, 256), 256)
            lanes = pl.ds(pl.multiple_of(y_at * 2048 + first, 256), 256)
            value = mm(lowered[layer], slots[slot, :, columns]) + biases[layer : layer + 1, lanes]
            before[layer, :, there] = value
            active[layer, :, there] = gelu(value).astype(BF)

        tiles(4, tile)

    def feed_down(layer, chunk, slot):
        chosen = pl.ds(chunk * GATHER_WIDTH, GATHER_WIDTH)

        def tile(columns, _):
            value = mm_cols(active[layer, :, chosen], slots[slot, columns, :])
            if chunk == 0:
                total_rows[:, columns] = value
            else:
                value = total_rows[:, columns] + value
                total_rows[:, columns] = value
                part_out[layer, :, columns] = value[rows:].astype(BF)

        tiles(4, tile)

    def feed_close(layer):
        inputs, target = (u1, u3)[layer], (u2, u4)[layer]
        part_over(layer).wait_recv()

        def tile(columns, _):
            target[:, columns] = (
                inputs[:, columns].astype(F32)
                + (total_rows[0:rows, columns] + part_in[layer, :, columns].astype(F32))
                + gains[5 + layer : 6 + layer, columns]
            ).astype(BF)

        tiles(4, tile)
        keep(target)

    def work(item):
        slot_copy(item).wait()
        slot = item % SLOTS
        layer, stage = item // 8, item % 8
        inputs = (x_in, u2)[layer]
        middle = (u1, u3)[layer]
        q, k, v, o = ((q_c, k_c, v_c, o_c), (q_s, k_s, v_s, o_s))[layer]
        if stage == 0:
            if layer == 0:
                norm_into(x_in, row(0), xq_c)
                norm_into(src_in, row(1), sn_c)
                keep(xq_c, sn_c)
            else:
                feed_close(0)
                norm_into(u2, row(2), xn_s)
                keep(xn_s)
            project((xq_c, xn_s)[layer], q, slot)
        elif stage == 1:
            project((sn_c, xn_s)[layer], k, slot)
        elif stage == 2:
            project((sn_c, xn_s)[layer], v, slot)
            heads(q, k, v, o, layer == 0)
            keep(q, k, v, o)
        elif stage == 3:
            close_attention(inputs, o, middle, slot)
            norm_into(middle, row(3 + layer), lowered.at[layer, pl.ds(0, rows)])
            launch([rows_over(layer)])
            keep(middle)
        elif stage % 2 == 0:
            if stage == 4:
                rows_over(layer).wait_recv()
            feed_up(layer, (stage - 4) // 2, slot)
        else:
            feed_down(layer, (stage - 4) // 2, slot)
            if stage == 7:
                launch([part_over(layer)])

    for item in range(AHEAD):
        launch([line_copy(item, step) for step in steps])
    vec_out[batch_at] = vec_in[...]
    for which in range(7):
        vec_copy(which).start()
    for moment in range(total + 4):
        if moment + AHEAD < total:
            launch([line_copy(moment + AHEAD, step) for step in steps])
        if moment < total:
            for step in steps:
                line_copy(moment, step).wait_recv()
                launch(near(moment, step))
            own(moment).start()
            launch([kin(moment, 0)])
        if 0 <= moment - 1 < total:
            for step in steps:
                if is_feed(moment - 1):
                    near(moment - 1, step)[0].wait_recv()
                    launch([kin(moment - 1, step)])
                else:
                    for copy, onward in zip(near(moment - 1, step), far(moment - 1, step)):
                        copy.wait_recv()
                        launch([onward])
        if 0 <= moment - 2 < total and not is_feed(moment - 2):
            for step in steps:
                for copy in far(moment - 2, step):
                    copy.wait_recv()
                launch([kin(moment - 2, step)])
        if moment == 2:
            for which in range(7):
                vec_copy(which).wait()
            for owner in range(8):
                values = vec_out[owner].astype(F32)
                gains[:, owner * 128 : owner * 128 + 128] = values
                for layer in range(2):
                    for part_at in range(4):
                        first = owner * 512 + part_at * 128
                        index = 7 + 4 * layer + part_at
                        biases[layer : layer + 1, first : first + 128] = values[index : index + 1]
        if 0 <= moment - 4 < total:
            work(moment - 4)
        if 0 <= moment - 3 < total:
            own(moment - 3).wait()
            for step in range(line):
                kin(moment - 3, step).wait_recv()
            slot_copy(moment - 3).start()
    keep(lowered, before, active)
    feed_close(1)

    def square(index, carry):
        here = pl.ds(pl.multiple_of(index * 32, 32), 32)
        values = u4[here, :].astype(F32)
        return carry + jnp.sum(values * values, axis=0, keepdims=True)

    squares = lax.fori_loop(0, u4.shape[0] // 32, square, jnp.zeros((1, u4.shape[1]), F32))
    mean = jnp.sum(squares, axis=1, keepdims=True) / (u4.shape[0] * u4.shape[1])
    group_norm = jnp.sqrt(mean + EPSILON)
    plane[8] = jnp.broadcast_to(group_norm, plane.shape[1:])
    for turn in range(7):
        near_norm(turn).start()
    plane[place] = plane[8]
    for turn in range(7):
        near_norm(turn).wait()
    line_in[4] = jnp.sum(plane[0:8], axis=0)
    for step in range(3):
        far_norm(step).start()
    line_in[spot] = line_in[4]
    for step in range(3):
        far_norm(step).wait()
    norm_mean = jnp.sum(line_in[0:4], axis=0) / 32.0
    norm_out[...] = norm_mean
    ratio = norm_mean[0:1, 0:1] / group_norm

    def top(index, carry):
        here = pl.ds(pl.multiple_of(index * 32, 32), 32)
        grad_top[here, :] = (
            cot_in[here, :].astype(F32) + ratio * u4[here, :].astype(F32)
        ).astype(BF)
        return carry

    lax.fori_loop(0, u4.shape[0] // 32, top, 0)
    keep(grad_top)
    for index, ref in enumerate(kept):
        pltpu.make_async_copy(ref, kept_outs[index], kept_sems.at[index]).wait()
    for copy in started:
        copy.wait_send()


def gather_forward(blocks, vectors, inputs, source, mask, cotangent):
    rows, width = inputs.shape
    half = blocks[2].shape[2] // 2
    widths = (3 * width, width, half, half) * 2
    total = len(GATHERED)
    anywhere = pl.BlockSpec(memory_space=pl.ANY)
    vmem = pl.BlockSpec(memory_space=pltpu.VMEM)
    plain = ((rows, width), BF)
    kept = [plain] * 16 + [
        ((2, 2 * rows, width), BF),
        ((2, 2 * rows, half), F32),
        ((2, 2 * rows, half), BF),
    ]
    dma = pltpu.SemaphoreType.DMA
    return pl.pallas_call(
        gather_kernel,
        out_shape=[jax.ShapeDtypeStruct((width, size), BF) for size in widths]
        + [
            jax.ShapeDtypeStruct((vectors.shape[0], width), F32),
            jax.ShapeDtypeStruct((8, 128), F32),
        ]
        + [jax.ShapeDtypeStruct(*one) for one in kept],
        in_specs=[anywhere] * len(blocks) + [vmem] * 5,
        out_specs=[anywhere] * len(widths) + [vmem] * 2 + [anywhere] * len(kept),
        scratch_shapes=[pltpu.VMEM(*one) for one in kept]
        + [
            pltpu.VMEM((SLOTS, width, GATHER_WIDTH), BF),
            pltpu.VMEM((2 * rows, width), F32),
            pltpu.VMEM((2, rows, width), BF),
            pltpu.VMEM((2, rows, width), BF),
            pltpu.VMEM((8, *vectors.shape), BF),
            pltpu.VMEM((2, 2 * half), F32),
            pltpu.VMEM((9, 8, 128), F32),
            pltpu.VMEM((5, 8, 128), F32),
            dma((total,)),
            dma((5, total, 4)),
            dma((5, total, 4)),
            dma((total, 4)),
            dma((total, 4)),
            dma((2, 7)),
            dma((SLOTS,)),
            dma((len(kept),)),
            dma((2, 7)),
            dma((2, 3)),
            dma((2, 2, 2)),
        ],
        compiler_params=pltpu.CompilerParams(
            collective_id=1, has_side_effects=True, vmem_limit_bytes=52 * 2**20
        ),
        cost_estimate=pl.CostEstimate(
            flops=2 * rows * width * sum(widths), bytes_accessed=2**27, transcendentals=2**21
        ),
    )(*blocks, vectors, inputs, source, mask, cotangent)


ITEM_COUNT = 16
WINDOWS = 4
STAGES = 3


def gelu_slope(value):
    factor = math.sqrt(2.0 / math.pi)
    square = value * value
    bent = jnp.tanh(factor * value * (1.0 + 0.044715 * square))
    inner = factor * (1.0 + 3.0 * 0.044715 * square)
    return 0.5 * (1.0 + bent) + 0.5 * value * (1.0 - bent * bent) * inner


def reduce_kernel(*refs):
    total = ITEM_COUNT
    (
        proj_c,
        out_c,
        in_0,
        down_0,
        proj_s,
        out_s,
        in_1,
        down_1,
        u1_in,
        u2_in,
        u3_in,
        last_ref,
        top_in,
        xq_c,
        sn_c,
        q_c,
        k_c,
        v_c,
        o_c,
        xn_s,
        q_s,
        k_s,
        v_s,
        o_s,
        lowered,
        before,
        active,
        x_in,
        src_in,
        gains,
        mask_in,
        picks_in,
    ) = refs[:32]
    (sum_out, last_out, first_out, point_out, small_out) = refs[32:37]
    (pair_h, slope_h, dqkv_h, grads_h, kin_lf, kin_la, kin_rf, kin_ra) = refs[37:45]
    (
        lwin_f,
        lwin_a,
        raw,
        rwin,
        stage,
        merged,
        passing,
        lined,
        crossed,
        pair,
        slope,
        rows_sum,
        hbuf,
        slots,
        qb,
        kb,
        vb,
        dob,
        dqkv,
        part_out,
        part_in,
        grad,
        ub,
        point_in,
        point_sum,
        small_in,
        small_sum,
    ) = refs[45:72]
    (
        kin_l_sems,
        kin_r_sems,
        raw_sems,
        win_sems,
        xy_sems,
        line_send,
        line_recv,
        cross_sems,
        out_sems,
        own_sems,
        lat_sems,
        far_sems,
        lat_own,
        point_sems,
        deal_sems,
        point_own,
        small_sems,
        pair_sems,
        slot_sems,
        h_sem,
        save_sems,
        act_sems,
    ) = refs[72:]
    section_at = lax.axis_index("section")
    batch_at = lax.axis_index("batch")
    core = lax.rem(batch_at, 2)
    spot = batch_at // 2
    x_at = lax.rem(section_at, 2)
    y_at = section_at // 2
    beside = section_at + 1 - 2 * x_at
    above = lax.rem(section_at + 2, 4)
    across = lax.rem(beside + 2, 4)
    sibling = batch_at + 1 - 2 * core
    flat = (beside, above)
    bits = (x_at, y_at)
    rows, width = 256, 1024

    peers = [(beside, batch_at), (above, batch_at), (across, batch_at), (section_at, sibling)]
    peers += [(section_at, lax.rem(spot + step, 4) * 2 + core) for step in (1, 2, 3)]
    barrier = pltpu.get_barrier_semaphore()
    for peer in peers:
        pl.semaphore_signal(barrier, inc=1, device_id=peer, device_id_type=MESH)
    pl.semaphore_wait(barrier, len(peers))

    def remote(source, target, sems, where, peer):
        return pltpu.make_async_remote_copy(
            source,
            target,
            sems.at[(0, *where)],
            sems.at[(1, *where)],
            device_id=peer,
            device_id_type=MESH,
        )

    feed_left = (pair_h.at[0], lowered.at[1], pair_h.at[1], lowered.at[0])
    feed_right = (active.at[1], slope_h.at[0], active.at[0], slope_h.at[1])
    att_left = (o_s, xn_s, xn_s, xn_s, o_c, xq_c, sn_c, sn_c)
    att_right = tuple(
        ref
        for turn in range(2)
        for ref in (grads_h.at[turn], dqkv_h.at[turn, 0], dqkv_h.at[turn, 1], dqkv_h.at[turn, 2])
    )

    def columns(spot_of, parity):
        return pl.ds(pl.multiple_of((2 * spot_of + parity) * 128, 128), 128)

    def kin_lefts(feed, job):
        source, target = (feed_left, kin_lf) if feed else (att_left, kin_la)
        return [
            remote(
                source[job].at[:, columns(part, 1 - core)],
                target.at[job, part],
                kin_l_sems,
                (job if feed else 4 + job, part),
                (section_at, sibling),
            )
            for part in range(4)
        ]

    def kin_right(feed, job, chunk):
        if feed:
            here = pl.ds(chunk * 1024, 1024)
            source, target = feed_right[job].at[:, here], kin_rf.at[job, :, here]
        else:
            source, target = att_right[job], kin_ra.at[job]
        where = (2 * job + chunk if feed else 8 + job,)
        return remote(source, target, kin_r_sems, where, (section_at, sibling))

    def item_of(index):
        turn, inner = index // 8, index % 8
        if inner < 4:
            return True, 2 * turn + inner // 2, inner % 2
        return False, 4 * turn + inner - 4, 0

    def window_copies(index):
        feed, job, chunk = item_of(index)
        slot = index % WINDOWS
        size = 512 if feed else 256
        if feed:
            here = pl.ds(chunk * 1024, 1024)
            sources = (feed_right[job].at[:, here], kin_rf.at[job, :, here])
        else:
            sources = (att_right[job], kin_ra.at[job])
        return [
            pltpu.make_async_copy(
                sources[whose],
                rwin.at[slot, pl.ds(whose * size, size)],
                win_sems.at[slot, whose],
            )
            for whose in range(2)
        ]

    def load(index):
        feed, job, chunk = item_of(index)
        kin_right(feed, job, chunk).wait_recv()
        for copy in window_copies(index):
            copy.start()
        if chunk == 0:
            for copy in kin_lefts(feed, job):
                copy.wait_recv()
            size = 512 if feed else 256
            own_left = (feed_left if feed else att_left)[job]
            kin_left = (kin_lf if feed else kin_la).at[job]
            target = (lwin_f if feed else lwin_a).at[job]
            for part in range(4):
                copies = [
                    pltpu.make_async_copy(
                        own_left.at[:, columns(part, core)],
                        raw.at[part, 0, pl.ds(0, size)],
                        raw_sems.at[part, 0],
                    ),
                    pltpu.make_async_copy(
                        kin_left.at[part], raw.at[part, 1, pl.ds(0, size)], raw_sems.at[part, 1]
                    ),
                ]
                for copy in copies:
                    copy.start()
            for part in range(4):
                for whose, source in enumerate(
                    (own_left.at[:, columns(part, core)], kin_left.at[part])
                ):
                    place = raw.at[part, whose, pl.ds(0, size)]
                    pltpu.make_async_copy(source, place, raw_sems.at[part, whose]).wait()
                    target[part, :, whose * size : whose * size + size] = place[...].T

    def is_feed(item):
        return lax.rem(item, 8) < 4

    def feed_job(item):
        return 2 * (item // 8) + lax.rem(item, 8) // 2

    def att_job(item):
        return 4 * (item // 8) + lax.rem(item, 8) - 4

    def loaded(slot, feed):
        size = 512 if feed else 256
        for whose in range(2):
            source = kin_rf.at[0, :, pl.ds(0, 1024)] if feed else kin_ra.at[0]
            pltpu.make_async_copy(
                source, rwin.at[slot, pl.ds(whose * size, size)], win_sems.at[slot, whose]
            ).wait()

    def products(item, feed, choice, store):
        slot = lax.rem(item, WINDOWS)

        def quarter(index, carry):
            upper, part = index // 2, lax.rem(index, 2)
            here = pl.ds(pl.multiple_of(part * 256, 256), 256)
            if feed:
                first = pl.multiple_of(choice[0] * 512 + part * 256, 256)
                left = lwin_f[feed_job(item), pl.ds(upper * 2, 2)].reshape(256, 1024)
                right = rwin[slot, :, pl.ds(first, 256)]
            else:
                bit = choice[0] + part * (choice[1] - choice[0])
                first = pl.multiple_of(part * 512 + bit * 256, 256)
                left = lwin_a[att_job(item), pl.ds(upper * 2, 2)].reshape(256, 512)
                right = rwin[slot, 0:512, pl.ds(first, 256)]
            tile = jnp.dot(left, right, preferred_element_type=F32).reshape(2, 128, 256)
            store(pl.ds(upper * 2, 2), here, tile)
            return carry

        lax.fori_loop(0, 4, quarter, 0)

    def by_kind(item, action):
        pl.when(is_feed(item))(functools.partial(action, item, True))
        pl.when(jnp.logical_not(is_feed(item)))(functools.partial(action, item, False))

    def xy_copies(item, feed):
        spans = ((0, 512),) if feed else ((0, 256), (256, 256))
        return [
            remote(
                stage.at[lax.rem(item, STAGES), :, :, pl.ds(*span)],
                merged.at[item, :, :, pl.ds(*span)],
                xy_sems,
                (item, side),
                (flat[side], batch_at),
            )
            for side, span in enumerate(spans)
        ]

    def xy_sent(item, feed):
        for copy in xy_copies(item, feed):
            copy.wait_send()

    def offer(item, feed):
        loaded(lax.rem(item, WINDOWS), feed)

        def store(blocks, here, tile):
            stage[lax.rem(item, STAGES), blocks, :, here] = tile.astype(BF)

        products(item, feed, (1 - x_at, 1 - y_at), store)
        for copy in xy_copies(item, feed):
            copy.start()

    def line_copy(item, dest, place, rightward):
        step = 1 if rightward else -1
        slot = 4 if not rightward and place - 1 == dest else dest
        return pltpu.make_async_remote_copy(
            merged.at[item, dest],
            passing.at[item, slot],
            line_send.at[item, dest],
            line_recv.at[item, slot],
            device_id=(section_at, batch_at + 2 * step),
            device_id_type=MESH,
        )

    def line_wait(item, slot):
        pltpu.make_async_remote_copy(
            merged.at[item, 0],
            passing.at[item, slot],
            line_send.at[item, 0],
            line_recv.at[item, slot],
            device_id=(section_at, sibling),
            device_id_type=MESH,
        ).wait_recv()

    def take(item, feed):
        for copy in xy_copies(item, feed):
            copy.wait_recv()

        def store(blocks, here, tile):
            where = (item, blocks, slice(None), here)
            merged[where] = (tile + merged[where].astype(F32)).astype(BF)

        products(item, feed, bits, store)

    def first(item):
        by_kind(item, take)

        @pl.when(spot == 0)
        def _():
            for dest in (3, 2, 1):
                line_copy(item, dest, 0, True).start()

        @pl.when(spot == 3)
        def _():
            for dest in (0, 1, 2):
                line_copy(item, dest, 3, False).start()

    def relay(item, dest, place, rightward):
        line_wait(item, dest)
        merged[item, dest] = (
            merged[item, dest].astype(F32) + passing[item, dest].astype(F32)
        ).astype(BF)
        line_copy(item, dest, place, rightward).start()

    def second(item):
        @pl.when(spot == 1)
        def _():
            for dest in (3, 2):
                relay(item, dest, 1, True)

        @pl.when(spot == 2)
        def _():
            for dest in (0, 1):
                relay(item, dest, 2, False)

    def third(item):
        @pl.when(spot == 1)
        def _():
            relay(item, 0, 1, False)

        @pl.when(spot == 2)
        def _():
            relay(item, 3, 2, True)

    def cross_copy(item, side):
        here = pl.ds(side * 256, 256)
        return remote(
            lined.at[item, :, here],
            crossed.at[att_job(item), :, here],
            cross_sems,
            (item, side),
            (flat[1 - side], batch_at),
        )

    def layer_of(item):
        return 1 - item // 8

    def feed_place(item):
        inner = lax.rem(item, 8)
        base = (1 - inner // 2) * 4096 + y_at * 2048 + lax.rem(inner, 2) * 1024 + x_at * 512
        return sum_out.at[layer_of(item), :, pl.ds(pl.multiple_of(base, 512), 512)]

    def feed_out(item, which):
        peer = (beside, above, across)[which]
        return remote(
            lined.at[item], feed_place(item), out_sems, (item, which), (peer, batch_at)
        )

    def feed_own(item):
        return pltpu.make_async_copy(lined.at[item], feed_place(item), own_sems.at[item, 0])

    def att_place(item, side):
        inner = lax.rem(lax.rem(item, 8) + 3, 4)
        base = 8192 + inner * 1024 + side * 512 + bits[side] * 256
        return sum_out.at[layer_of(item), :, pl.ds(pl.multiple_of(base, 256), 256)]

    def att_out(item, side):
        return remote(
            lined.at[item, :, pl.ds(side * 256, 256)],
            att_place(item, side),
            out_sems,
            (item, side),
            (flat[side], batch_at),
        )

    def att_own(item, side):
        return pltpu.make_async_copy(
            lined.at[item, :, pl.ds(side * 256, 256)],
            att_place(item, side),
            own_sems.at[item, side],
        )

    def deliver(item, feed):
        if feed:
            for which in range(3):
                feed_out(item, which).start()
            feed_own(item).start()
        else:
            for side in range(2):
                cross_copy(item, side).start()

    def close(item):
        @pl.when(spot == 0)
        def _():
            line_wait(item, 4)
            lined[item] = (
                merged[item, 0].astype(F32) + passing[item, 4].astype(F32)
            ).astype(BF)

        @pl.when(spot == 3)
        def _():
            line_wait(item, 3)
            lined[item] = (
                merged[item, 3].astype(F32) + passing[item, 3].astype(F32)
            ).astype(BF)

        for middle in (1, 2):

            @pl.when(spot == middle)
            def _():
                line_wait(item, middle)
                line_wait(item, 4)
                lined[item] = (
                    merged[item, middle].astype(F32)
                    + passing[item, middle].astype(F32)
                    + passing[item, 4].astype(F32)
                ).astype(BF)

        by_kind(item, deliver)

    def finish(item):
        @pl.when(jnp.logical_not(is_feed(item)))
        def _():
            for side in range(2):
                cross_copy(item, side).wait()
            lined[item] = (lined[item].astype(F32) + crossed[att_job(item)].astype(F32)).astype(BF)
            for side in range(2):
                att_out(item, side).start()
                att_own(item, side).start()

    def small_copy(phase):
        if phase == 0:
            peer = (section_at, sibling)
        elif phase < 3:
            peer = (flat[phase - 1], batch_at)
        else:
            peer = (section_at, lax.rem(spot + phase - 2, 4) * 2 + core)
        return remote(
            small_sum.at[min(phase, 3)], small_in.at[phase], small_sems, (phase,), peer
        )

    quarter_rows = pair.shape[0] // 4

    def point_copy(which):
        peer = (beside, above, across)[which]
        return remote(
            pair.at[pl.ds(pl.multiple_of(peer * quarter_rows, 128), quarter_rows)],
            point_in.at[which],
            point_sems,
            (which,),
            (peer, batch_at),
        )

    def point_place():
        return point_out.at[pl.ds(pl.multiple_of(section_at * quarter_rows, 128), quarter_rows)]

    def point_deal(which):
        peer = (beside, above, across)[which]
        return remote(point_sum, point_place(), deal_sems, (which,), (peer, batch_at))

    def point_local():
        return pltpu.make_async_copy(point_sum, point_place(), point_own.at[0])

    pairs = ((last_ref, last_out), (grad, first_out))

    def lat_copy(which, way):
        source, target = pairs[which]
        return remote(
            source,
            target.at[pl.ds(pl.multiple_of(section_at * rows, rows), rows)],
            lat_sems,
            (which, way),
            (flat[way], batch_at),
        )

    def lat_far(which, way):
        target = pairs[which][1]
        low = flat[way] * rows + way * (rows // 2)
        part = target.at[pl.ds(pl.multiple_of(low, rows // 2), rows // 2)]
        return remote(part, part, far_sems, (which, way), (flat[1 - way], batch_at))

    def lat_local(which):
        source, target = pairs[which]
        return pltpu.make_async_copy(
            source,
            target.at[pl.ds(pl.multiple_of(section_at * rows, rows), rows)],
            lat_own.at[which],
        )

    def lat_start(which):
        lat_local(which).start()
        for way in range(2):
            lat_copy(which, way).start()

    def lat_onward(which):
        for way in range(2):
            lat_copy(which, way).wait_recv()
            lat_far(which, way).start()

    loads = []
    for turn, (proj, out, up, down) in enumerate(
        ((proj_s, out_s, in_1, down_1), (proj_c, out_c, in_0, down_0))
    ):
        for chunk in range(2):
            loads += [down.at[:, pl.ds(chunk * 1024, 1024)], up.at[:, pl.ds(chunk * 1024, 1024)]]
        loads.append(out)
        loads += [proj.at[:, pl.ds(which * 1024, 1024)] for which in range(3)]

    def slot_copy(index):
        return pltpu.make_async_copy(loads[index], slots.at[index % 2], slot_sems.at[index % 2])

    def opened(index):
        slot_copy(index).wait()
        return index % 2

    def closed(index):
        if index + 2 < len(loads):
            slot_copy(index + 2).start()

    def h_copy(index):
        layer, chunk = 1 - index // 2, index % 2
        return pltpu.make_async_copy(
            before.at[layer, :, pl.ds(chunk * 1024, 1024)], hbuf, h_sem.at[0]
        )

    def pair_over(turn):
        return remote(
            pair.at[pl.ds(0, rows)],
            pair.at[pl.ds(rows, rows)],
            pair_sems,
            (turn, 0),
            (above, batch_at),
        )

    def part_over(turn):
        return remote(
            part_out.at[turn], part_in.at[turn], pair_sems, (turn, 1), (above, batch_at)
        )

    def saved(source, target, index):
        copy = pltpu.make_async_copy(source, target, save_sems.at[index])
        copy.start()
        copy.wait()

    def act_copies(turn):
        chosen = ((q_s, k_s, v_s), (q_c, k_c, v_c))[turn]
        return [
            pltpu.make_async_copy(source, target, act_sems.at[index])
            for index, (source, target) in enumerate(zip(chosen, (qb, kb, vb)))
        ]

    def row_copy(index):
        source = (u3_in, u2_in, u1_in, x_in)[index]
        return pltpu.make_async_copy(source, ub, act_sems.at[3])

    def small_row(index, value):
        small_sum[0, index : index + 1, :] = value

    def open_pair(turn):
        pair[0:rows, :] = grad[...]
        pair_over(turn).start()

    def feed_chunk(turn, chunk):
        layer = 1 - turn
        base = 8 * turn + 2 * chunk
        if chunk == 0:
            pair_over(turn).wait()
            saved(pair, pair_h.at[turn], 0)
            for copy in kin_lefts(True, 2 * turn):
                copy.start()
            for part in range(2):
                kin_right(True, 2 * turn, part).start()
            for copy in kin_lefts(True, 2 * turn + 1):
                copy.start()
        h_copy(2 * turn + chunk).wait()
        slot = opened(base)

        def up_tile(here, index):
            there = pl.ds(pl.multiple_of(chunk * 1024 + index * 256, 256), 256)
            value = mm(pair[...], slots[slot, :, here]) * gelu_slope(hbuf[:, here])
            short = value.astype(BF)
            slope[:, there] = short
            column = jnp.sum(short.astype(F32), axis=0, keepdims=True)
            for half in range(2):
                index_at = 7 + 4 * layer + 2 * half + chunk
                small_sum[0, index_at : index_at + 1, here] = jnp.where(
                    y_at == half, column, jnp.zeros_like(column)
                )

        tiles(4, up_tile)
        closed(base)
        if 2 * turn + chunk + 1 < 4:
            h_copy(2 * turn + chunk + 1).start()
        here = pl.ds(chunk * 1024, 1024)
        saved(slope.at[:, here], slope_h.at[turn, :, here], 0)
        kin_right(True, 2 * turn + 1, chunk).start()
        slot = opened(base + 1)

        def down_tile(there, _):
            value = mm_cols(slope[:, chunk * 1024 : chunk * 1024 + 1024], slots[slot, there, :])
            if chunk == 0:
                rows_sum[:, there] = value
            else:
                value = rows_sum[:, there] + value
                rows_sum[:, there] = value
                part_out[turn, :, there] = value[rows:].astype(BF)

        tiles(4, down_tile)
        closed(base + 1)
        if chunk == 1:
            part_over(turn).start()

    def row_steps(body, count):
        zero = jnp.zeros((1, width), F32)

        def step(index, carry):
            here = pl.ds(pl.multiple_of(index * 32, 32), 32)
            return tuple(a + b for a, b in zip(carry, body(here)))

        return lax.fori_loop(0, rows // 32, step, (zero,) * count)

    def lean(back, unit, inverse, gain):
        scaled = back * gain
        inner = (
            scaled
            - jnp.mean(scaled, axis=-1, keepdims=True)
            - unit * jnp.mean(scaled * unit, axis=-1, keepdims=True)
        )
        return inverse * inner, jnp.sum(back * unit, axis=0, keepdims=True)

    def feed_end(turn):
        layer = 1 - turn
        gain = gains[3 + layer : 4 + layer, :]
        part_over(turn).wait_recv()
        row_copy(2 * turn).wait()

        def body(here):
            unit, inverse = unit_rows(ub[here, :].astype(F32))
            back = rows_sum[here, :] + part_in[turn, here, :].astype(F32)
            dx, gain_part = lean(back, unit, inverse, gain)
            old = grad[here, :].astype(F32)
            grad[here, :] = (old + dx).astype(BF)
            return gain_part, jnp.sum(old, axis=0, keepdims=True)

        gain_grad, out_grad = row_steps(body, 2)
        row_copy(2 * turn + 1).start()
        small_row(3 + layer, gain_grad)
        small_row(5 + layer, out_grad)
        saved(grad, grads_h.at[turn], 0)
        for copy in kin_lefts(False, 4 * turn):
            copy.start()
        kin_right(False, 4 * turn, 0).start()
        slot = opened(8 * turn + 4)

        def tile(there, _):
            dob[:, there] = mm_cols(grad[...], slots[slot, there, :]).astype(BF)

        tiles(4, tile)
        closed(8 * turn + 4)

    def attend_heads(turn):
        scale = 1.0 / math.sqrt(HD)
        for copy in act_copies(turn):
            copy.wait()

        def head(index, carry):
            here = pl.ds(pl.multiple_of(index * HD, HD), HD)
            q, k, v, do = qb[:, here], kb[:, here], vb[:, here], dob[:, here]
            scores = mm_cols(q, k) * scale
            if turn == 1:
                scores = jnp.where(mask_in[...] > 0.0, scores, MASKED)
            grown = jnp.exp(scores - jnp.max(scores, axis=-1, keepdims=True))
            soft = grown / jnp.sum(grown, axis=-1, keepdims=True)
            back = mm_cols(do, v)
            short = soft * (back - jnp.sum(soft * back, axis=-1, keepdims=True))
            dqkv[0, :, here] = (mm(short.astype(BF), k) * scale).astype(BF)
            dqkv[1, :, here] = (mm(short.T.astype(BF), q) * scale).astype(BF)
            dqkv[2, :, here] = mm(soft.T.astype(BF), do).astype(BF)
            return carry

        lax.fori_loop(0, width // HD, head, 0)
        if turn == 0:
            for copy in act_copies(1):
                copy.start()
        saved(dqkv, dqkv_h.at[turn], 0)
        for which in range(3):
            for copy in kin_lefts(False, 4 * turn + 1 + which):
                copy.start()
            kin_right(False, 4 * turn + 1 + which, 0).start()

    def attend_end(turn):
        base = 8 * turn + 5
        for which in range(3):
            slot = opened(base + which)

            def tile(there, _):
                value = mm_cols(dqkv[which], slots[slot, there, :])
                if which == 0:
                    rows_sum[0:rows, there] = value
                elif which == 1:
                    rows_sum[rows : 2 * rows, there] = value
                else:
                    rows_sum[rows : 2 * rows, there] += value

            tiles(4, tile)
            closed(base + which)
        row_copy(2 * turn + 1).wait()
        gain_q = gains[2:3, :] if turn == 0 else gains[0:1, :]
        gain_kv = gains[2:3, :] if turn == 0 else gains[1:2, :]

        def body(here):
            unit, inverse = unit_rows(ub[here, :].astype(F32))
            dx, gain_part = lean(rows_sum[here, :], unit, inverse, gain_q)
            if turn == 1:
                unit, inverse = unit_rows(src_in[here, :].astype(F32))
            there = pl.ds(pl.multiple_of(rows + here.start, 32), 32)
            ds, kv_part = lean(rows_sum[there, :], unit, inverse, gain_kv)
            fresh = grad[here, :].astype(F32) + dx
            if turn == 0:
                fresh += ds
            else:
                high = ds.astype(BF)
                part_out[0, here, :] = high
                part_out[1, here, :] = (ds - high.astype(F32)).astype(BF)
            grad[here, :] = fresh.astype(BF)
            return gain_part, kv_part

        if turn == 1:
            for which in range(2):
                part_over(which).wait_send()
        gain_grad, kv_grad = row_steps(body, 2)
        if turn == 0:
            row_copy(2).start()
            small_row(2, gain_grad + kv_grad)
            open_pair(1)
        else:
            small_row(0, gain_grad)
            small_row(1, kv_grad)
            small_row(15, jnp.zeros_like(gain_grad))

            def tile(there, _):
                pair[:, there] = (
                    mm(picks_in[...], part_out[0, :, there])
                    + mm(picks_in[...], part_out[1, :, there])
                ).astype(BF)

            tiles(4, tile)
            small_copy(0).start()
            for which in range(3):
                point_copy(which).start()
            lat_start(1)

    def point_total():
        for which in range(3):
            point_copy(which).wait_recv()
        gathered = pair[
            pl.ds(pl.multiple_of(section_at * quarter_rows, 128), quarter_rows)
        ].astype(F32)
        for which in range(3):
            gathered += point_in[which].astype(F32)
        point_sum[...] = gathered.astype(BF)
        point_local().start()
        for which in range(3):
            point_deal(which).start()

    def small_step(phase):
        small_copy(phase).wait_recv()
        small_sum[phase + 1] = small_sum[phase] + small_in[phase]
        if phase < 2:
            small_copy(phase + 1).start()
        else:
            for step in range(3):
                small_copy(3 + step).start()

    def small_end():
        for step in range(3):
            small_copy(3 + step).wait_recv()
        small_out[...] = (small_sum[3] + small_in[4]) + (small_in[3] + small_in[5])

    def rows_end():
        lat_onward(1)
        point_total()

    begin = pltpu.make_async_copy(top_in, grad, act_sems.at[4])
    begin.start()
    for index in range(2):
        slot_copy(index).start()
    h_copy(0).start()
    row_copy(0).start()
    for copy in act_copies(0):
        copy.start()
    lat_start(0)
    begin.wait()
    open_pair(0)
    feed_chunk(0, 0)
    load(0)
    chain = {
        0: [functools.partial(feed_chunk, 0, 1)],
        1: [functools.partial(feed_end, 0)],
        2: [functools.partial(attend_heads, 0), functools.partial(lat_onward, 0)],
        3: [functools.partial(attend_end, 0)],
        4: [functools.partial(feed_chunk, 1, 0)],
        5: [functools.partial(feed_chunk, 1, 1)],
        6: [functools.partial(feed_end, 1)],
        7: [functools.partial(attend_heads, 1)],
        8: [functools.partial(attend_end, 1)],
        10: [functools.partial(small_step, 0), rows_end],
        12: [functools.partial(small_step, 1)],
        14: [functools.partial(small_step, 2)],
        16: [small_end],
    }

    def moment_body(moment, carry):
        @pl.when(moment < total)
        def _():
            @pl.when(moment >= STAGES)
            def _():
                by_kind(moment - STAGES, xy_sent)

            by_kind(moment, offer)

        for lag, action in ((2, first), (3, second), (4, third), (5, close), (6, finish)):
            pl.when(jnp.logical_and(moment >= lag, moment < total + lag))(
                functools.partial(action, moment - lag)
            )
        for when, actions in chain.items():

            @pl.when(moment == when)
            def _():
                for action in actions:
                    action()

        for item in range(1, total):
            pl.when(moment == item - 1)(functools.partial(load, item))
        return carry

    lax.fori_loop(0, total + 6, moment_body, 0)

    for index in range(4):
        for copy in kin_lefts(True, index):
            copy.wait_send()
        for chunk in range(2):
            kin_right(True, index, chunk).wait_send()
    for index in range(8):
        for copy in kin_lefts(False, index):
            copy.wait_send()
        kin_right(False, index, 0).wait_send()
    for phase in range(6):
        small_copy(phase).wait_send()
    for which in range(2):
        lat_local(which).wait()
        for way in range(2):
            lat_copy(which, way).wait_send()
            lat_far(which, way).wait()
    point_local().wait()
    for which in range(3):
        point_copy(which).wait_send()
        point_deal(which).wait()

    def drained(item, feed):
        if feed:
            for which in range(3):
                feed_out(item, which).wait()
            feed_own(item).wait()
        else:
            for side in range(2):
                att_out(item, side).wait()
                att_own(item, side).wait()

    def drain(item, carry):
        pl.when(item >= total - STAGES)(functools.partial(by_kind, item, xy_sent))
        for step in (1, 2, 3):
            dest = lax.rem(spot + step, 4)
            pltpu.make_async_remote_copy(
                merged.at[item, dest],
                passing.at[item, 0],
                line_send.at[item, dest],
                line_recv.at[item, 0],
                device_id=(section_at, sibling),
                device_id_type=MESH,
            ).wait_send()
        by_kind(item, drained)
        return carry

    lax.fori_loop(0, total, drain, 0)


def reduce_all(full, kept, inputs, source, gains, mask, picks):
    total = ITEM_COUNT
    rows, width = inputs.shape
    points = picks.shape[0]
    anywhere = pl.BlockSpec(memory_space=pl.ANY)
    vmem = pl.BlockSpec(memory_space=pltpu.VMEM)
    u1, u2, u3, u4, top = kept[:5]
    operands = [*full, u1, u2, u3, u4, top, *kept[5:], inputs, source, gains, mask, picks]
    spaces = [anywhere] * (len(operands) - 4) + [vmem] * 4
    dma = pltpu.SemaphoreType.DMA
    flops = 2 * width * width * 24 * rows * 2
    return pl.pallas_call(
        reduce_kernel,
        out_shape=[
            jax.ShapeDtypeStruct((2, 128, 12 * width), BF),
            jax.ShapeDtypeStruct((4 * rows, width), BF),
            jax.ShapeDtypeStruct((4 * rows, width), BF),
            jax.ShapeDtypeStruct((points, width), BF),
            jax.ShapeDtypeStruct((16, width), F32),
            jax.ShapeDtypeStruct((2, 2 * rows, width), BF),
            jax.ShapeDtypeStruct((2, 2 * rows, 2 * width), BF),
            jax.ShapeDtypeStruct((2, 3, rows, width), BF),
            jax.ShapeDtypeStruct((2, rows, width), BF),
            jax.ShapeDtypeStruct((4, 4, 2 * rows, 128), BF),
            jax.ShapeDtypeStruct((8, 4, rows, 128), BF),
            jax.ShapeDtypeStruct((4, 2 * rows, 2 * width), BF),
            jax.ShapeDtypeStruct((8, rows, width), BF),
        ],
        in_specs=spaces,
        out_specs=[anywhere] * 4 + [vmem] + [anywhere] * 8,
        scratch_shapes=[
            pltpu.VMEM((4, 4, 128, 1024), BF),
            pltpu.VMEM((8, 4, 128, 512), BF),
            pltpu.VMEM((4, 2, 512, 128), BF),
            pltpu.VMEM((WINDOWS, 1024, 1024), BF),
            pltpu.VMEM((STAGES, 4, 128, 512), BF),
            pltpu.VMEM((total, 4, 128, 512), BF),
            pltpu.VMEM((total, 5, 128, 512), BF),
            pltpu.VMEM((total, 128, 512), BF),
            pltpu.VMEM((8, 128, 512), BF),
            pltpu.VMEM((512, 1024), BF),
            pltpu.VMEM((512, 2048), BF),
            pltpu.VMEM((512, 1024), F32),
            pltpu.VMEM((512, 1024), F32),
            pltpu.VMEM((2, 1024, 1024), BF),
            pltpu.VMEM((256, 1024), BF),
            pltpu.VMEM((256, 1024), BF),
            pltpu.VMEM((256, 1024), BF),
            pltpu.VMEM((256, 1024), BF),
            pltpu.VMEM((3, 256, 1024), BF),
            pltpu.VMEM((2, 256, 1024), BF),
            pltpu.VMEM((2, 256, 1024), BF),
            pltpu.VMEM((256, 1024), BF),
            pltpu.VMEM((256, 1024), BF),
            pltpu.VMEM((3, points // 4, width), BF),
            pltpu.VMEM((points // 4, width), BF),
            pltpu.VMEM((6, 16, width), F32),
            pltpu.VMEM((4, 16, width), F32),
            dma((2, 12, 4)),
            dma((2, 16)),
            dma((4, 2)),
            dma((WINDOWS, 2)),
            dma((2, total, 2)),
            dma((total, 4)),
            dma((total, 5)),
            dma((2, total, 2)),
            dma((2, total, 3)),
            dma((total, 2)),
            dma((2, 2, 2)),
            dma((2, 2, 2)),
            dma((2,)),
            dma((2, 3)),
            dma((2, 3)),
            dma((1,)),
            dma((2, 6)),
            dma((2, 2, 2)),
            dma((2,)),
            dma((1,)),
            dma((1,)),
            dma((5,)),
        ],
        compiler_params=pltpu.CompilerParams(
            collective_id=2, has_side_effects=True, vmem_limit_bytes=62 * 2**20
        ),
        cost_estimate=pl.CostEstimate(
            flops=flops, bytes_accessed=2**27, transcendentals=2**21
        ),
    )(*operands)[:5]


def plain_layers(full, spread, mine, source, valid, cot_own, picks, groups_all):
    proj_c, out_c, in_0, down_0, proj_s, out_s, in_1, down_1 = full
    width, hidden = in_0.shape

    def vector(first, count):
        return spread[:, first : first + count].reshape(-1)

    gains_cross = (vector(0, 1), vector(1, 1))
    gain_self = vector(2, 1)
    gains_mlp = (vector(3, 1), vector(4, 1))
    biases_out = (vector(5, 1), vector(6, 1))
    per_bias = hidden // width
    biases_in = (vector(7, per_bias), vector(7 + per_bias, per_bias))
    cot = cot_own.astype(F32)
    u1, kept_c = attend(mine, source, valid, gains_cross[0], gains_cross[1], proj_c, out_c)
    u2, kept_0 = feed(u1.astype(F32), gains_mlp[0], in_0, biases_in[0], down_0, biases_out[0])
    u2 = u2.astype(F32)
    u3, kept_s = attend(u2, u2, None, gain_self, gain_self, proj_s, out_s)
    u4, kept_1 = feed(u3.astype(F32), gains_mlp[1], in_1, biases_in[1], down_1, biases_out[1])
    final = u4.astype(F32)
    group_norm = jnp.sqrt(jnp.mean(final * final) + EPSILON)
    norm_mean = lax.psum(group_norm, ALL) / groups_all
    g4 = (cot + (norm_mean / group_norm) * final).astype(BF)

    dx, gain_1_grad, bias_1_grad, ob_1_grad, pairs_1 = feed_back(
        g4, kept_1, gains_mlp[1], in_1, down_1
    )
    g3 = (g4.astype(F32) + dx).astype(BF)
    dx, ds, gq, gkv, pairs_s = attend_back(g3, kept_s, gain_self, gain_self, proj_s, out_s)
    gain_s_grad = gq + gkv
    g2 = (g3.astype(F32) + dx + ds).astype(BF)
    dx, gain_0_grad, bias_0_grad, ob_0_grad, pairs_0 = feed_back(
        g2, kept_0, gains_mlp[0], in_0, down_0
    )
    g1 = (g2.astype(F32) + dx).astype(BF)
    dx, ds, cq_grad, ckv_grad, pairs_c = attend_back(
        g1, kept_c, gains_cross[0], gains_cross[1], proj_c, out_c
    )
    g0 = (g1.astype(F32) + dx).astype(BF)
    high = ds.astype(BF)
    low = (ds - high.astype(F32)).astype(BF)
    point_part = (mm_rows(picks, high) + mm_rows(picks, low)).astype(BF)
    small = jnp.concatenate(
        [
            cq_grad,
            ckv_grad,
            gain_s_grad,
            gain_0_grad,
            gain_1_grad,
            ob_0_grad,
            ob_1_grad,
            bias_0_grad,
            bias_1_grad,
            jnp.zeros_like(cq_grad),
        ]
    ).reshape(-1, width)
    pairs = pairs_1 + pairs_s + pairs_0 + pairs_c
    lefts, rights = [pair[0] for pair in pairs], [pair[1] for pair in pairs]
    def settled_grad(left, right):
        part = lax.psum_scatter(
            mm_rows(left, right).astype(BF), ALL, scatter_dimension=0, tiled=True
        )
        return lax.all_gather(part, "section", axis=0, tiled=True).astype(F32)

    done = [settled_grad(left, right) for left, right in pairs]
    mlp_in_grad = jnp.stack([done[6], done[0]])
    mlp_down_grad = jnp.stack([done[7], done[1]])
    proj_s_grad = jnp.concatenate(done[2:5], axis=1)
    proj_c_grad = jnp.concatenate(done[8:11], axis=1)
    out_s_grad, out_c_grad = done[5], done[11]
    points_sum = lax.psum(point_part, "section")
    latents_out = lax.all_gather(u4, "section", axis=0, tiled=True)
    g0_all = lax.all_gather(g0, "section", axis=0, tiled=True)
    small = lax.psum(small, ALL)
    return (
        norm_mean,
        latents_out,
        g0_all,
        points_sum,
        small,
        mlp_in_grad,
        mlp_down_grad,
        proj_c_grad,
        proj_s_grad,
        out_c_grad,
        out_s_grad,
    )


def per_device(
    latents,
    points,
    neighbours,
    lengths,
    cross_proj,
    cross_out,
    cross_gains,
    self_proj,
    self_out,
    self_gain,
    mlp_gain,
    mlp_in,
    mlp_in_bias,
    mlp_down,
    mlp_out_bias,
    cotangent,
):
    sections = lax.axis_size("section")
    section_at = lax.axis_index("section")
    width = latents.shape[1]
    hidden = mlp_in.shape[2]
    groups_dev = neighbours.shape[0]
    rows = latents.shape[0] // sections
    shard = cross_out.shape[0]
    piece = shard // sections
    groups_all = groups_dev * lax.axis_size("batch")

    def gathered(block):
        own = lax.dynamic_slice_in_dim(block, section_at * piece, piece, 0)
        return lax.all_gather(own, ALL, axis=0, tiled=True)

    vectors = jnp.concatenate(
        [
            cross_gains.reshape(-1),
            self_gain,
            mlp_gain.reshape(-1),
            mlp_out_bias.reshape(-1),
            mlp_in_bias.reshape(-1),
            jnp.zeros_like(self_gain),
        ]
    ).reshape(-1, shard)
    projs = (cross_proj.reshape(shard, 3 * width), self_proj.reshape(shard, 3 * width))
    small_slice = lax.axis_size("batch") == 8
    latents_own = lax.dynamic_slice_in_dim(latents, section_at * rows, rows, 0)
    cot_own = lax.dynamic_slice_in_dim(cotangent, section_at * rows, rows, 0)
    mine = latents_own.astype(F32)
    listed = lax.dynamic_index_in_dim(neighbours, section_at, 0, keepdims=False)
    length = lax.dynamic_index_in_dim(lengths, section_at, 0, keepdims=False)
    valid = jnp.arange(listed.shape[0], dtype=jnp.int32) < length
    picks = listed[:, None] == jnp.arange(points.shape[0], dtype=jnp.int32)[None, :]
    picks = picks.astype(BF)
    source = mm(picks, points)
    if small_slice:
        made = gather_forward(
            [projs[0], cross_out, mlp_in, mlp_down, projs[1], self_out],
            vectors,
            latents_own,
            source.astype(BF),
            valid.astype(F32)[None, :],
            cot_own,
        )
        full, gain_rows, norm_tile, made = made[:8], made[8], made[9], made[10:]
        norm_mean = norm_tile[0, 0]
        sums, latents_out, g0_all, points_sum, small = reduce_all(
            full,
            made,
            latents_own,
            source.astype(BF),
            gain_rows,
            valid.astype(F32)[None, :],
            picks.T,
        )
        attn = 2 * hidden
        mlp_in_grad = sums[:, :, :hidden].astype(F32)
        mlp_down_grad = sums[:, :, hidden:attn].astype(F32)
        proj_c_grad, proj_s_grad = [
            sums[layer, :, attn : attn + 3 * width].astype(F32) for layer in range(2)
        ]
        out_c_grad, out_s_grad = [
            sums[layer, :, attn + 3 * width :].astype(F32) for layer in range(2)
        ]
    else:
        blocks = [projs[0], cross_out, mlp_in[0], mlp_down[0]]
        blocks += [projs[1], self_out, mlp_in[1], mlp_down[1]]
        full = [gathered(block) for block in blocks]
        spread = lax.all_gather(vectors, "batch", axis=0, tiled=False)
        (
            norm_mean,
            latents_out,
            g0_all,
            points_sum,
            small,
            mlp_in_grad,
            mlp_down_grad,
            proj_c_grad,
            proj_s_grad,
            out_c_grad,
            out_s_grad,
        ) = plain_layers(full, spread.astype(F32), mine, source, valid, cot_own, picks, groups_all)
    points_grad = points_sum.astype(F32)
    latents_grad = g0_all.astype(F32)
    per_bias = hidden // width
    batch_at = lax.axis_index("batch")

    def own(first, count):
        flat = small[first : first + count].reshape(-1)
        size = flat.shape[0] // lax.axis_size("batch")
        return lax.dynamic_slice_in_dim(flat, batch_at * size, size, 0)

    return (
        latents_out,
        latents_grad,
        points_grad,
        proj_c_grad.reshape(shard, 3, width),
        out_c_grad,
        jnp.stack([own(0, 1), own(1, 1)]),
        proj_s_grad.reshape(shard, 3, width),
        out_s_grad,
        own(2, 1),
        jnp.stack([own(3, 1), own(4, 1)]),
        mlp_in_grad,
        jnp.stack([own(7, per_bias), own(7 + per_bias, per_bias)]),
        mlp_down_grad,
        jnp.stack([own(5, 1), own(6, 1)]),
        norm_mean,
    )


def solution(mesh):
    rows = P("batch", None)
    cols = P(None, "batch")
    block = P("batch", None, None)
    pair = P(None, "batch", None)
    return jax.shard_map(
        per_device,
        mesh=mesh,
        in_specs=(
            rows,
            rows,
            rows,
            P("batch"),
            block,
            rows,
            cols,
            block,
            rows,
            P("batch"),
            cols,
            pair,
            cols,
            pair,
            cols,
            rows,
        ),
        out_specs=(
            rows,
            rows,
            rows,
            block,
            rows,
            cols,
            block,
            rows,
            P("batch"),
            cols,
            pair,
            cols,
            pair,
            cols,
            P(),
        ),
        check_vma=False,
    )
```

```python
import functools
import math

import jax
import jax.numpy as jnp
from jax import lax
from jax.experimental import pallas as pl
from jax.experimental.pallas import tpu as pltpu
from jax.sharding import PartitionSpec as P

HD = 128
EPSILON = 1e-05
MASKED = -1e30
BF = jnp.bfloat16
F32 = jnp.float32
ALL = ("batch", "section")
MESH = pl.DeviceIdType.MESH
GATHER_WIDTH = 1024
AHEAD = 4
SLOTS = 3
GATHERED = tuple(
    (4 * layer + index, start)
    for layer in range(2)
    for index, start in (
        [(0, 0), (0, 1024), (0, 2048), (1, 0)]
        + [(2 + which, chunk) for chunk in range(0, 2048, 1024) for which in range(2)]
    )
)


def mm(a, b):
    return jnp.dot(a, b, preferred_element_type=F32)


def mm_rows(a, b):
    return lax.dot_general(a, b, (((0,), (0,)), ((), ())), preferred_element_type=F32)


def mm_cols(a, b):
    return lax.dot_general(a, b, (((1,), (1,)), ((), ())), preferred_element_type=F32)


def unit_rows(values):
    centred = values - jnp.mean(values, axis=-1, keepdims=True)
    inverse = lax.rsqrt(jnp.mean(centred * centred, axis=-1, keepdims=True) + EPSILON)
    return centred * inverse, inverse


def norm_back(gradient, unit, inverse, gain):
    scaled = gradient * gain
    inner = (
        scaled
        - jnp.mean(scaled, axis=-1, keepdims=True)
        - unit * jnp.mean(scaled * unit, axis=-1, keepdims=True)
    )
    return inverse * inner, jnp.sum(gradient * unit, axis=0)


def heads_of(rows):
    return rows.reshape(rows.shape[0], -1, HD)


def softmax(q, k, valid):
    scores = jnp.einsum(
        "lhc,nhc->hln", heads_of(q), heads_of(k), preferred_element_type=F32
    ) * (1.0 / math.sqrt(HD))
    if valid is not None:
        scores = jnp.where(valid[None, None, :], scores, MASKED)
    grown = jnp.exp(scores - jnp.max(scores, axis=-1, keepdims=True))
    return grown / jnp.sum(grown, axis=-1, keepdims=True)


def attend(inputs, source, valid, gain_q, gain_kv, proj, out):
    unit_x, inv_x = unit_rows(inputs)
    queries_in = (unit_x * gain_q).astype(BF)
    unit_s, inv_s = unit_rows(source)
    keys_in = (unit_s * gain_kv).astype(BF)
    width = inputs.shape[1]
    q = mm(queries_in, proj[:, :width]).astype(BF)
    kv = mm(keys_in, proj[:, width:]).astype(BF)
    k, v = kv[:, :width], kv[:, width:]
    soft = softmax(q, k, valid)
    mixture = jnp.einsum("hln,nhc->lhc", soft.astype(BF), heads_of(v), preferred_element_type=F32)
    mixture = mixture.reshape(inputs.shape).astype(BF)
    result = (inputs + mm(mixture, out)).astype(BF)
    return result, (unit_x, inv_x, queries_in, unit_s, inv_s, keys_in, q, k, v, soft, mixture)


def attend_back(gradient, kept, gain_q, gain_kv, proj, out):
    unit_x, inv_x, queries_in, unit_s, inv_s, keys_in, q, k, v, soft, mixture = kept
    width = gradient.shape[1]
    scale = 1.0 / math.sqrt(HD)
    grad_mix = mm_cols(gradient, out).astype(BF)
    grad_soft = jnp.einsum(
        "lhc,nhc->hln", heads_of(grad_mix), heads_of(v), preferred_element_type=F32
    )
    inner = jnp.sum(soft * grad_soft, axis=-1, keepdims=True)
    grad_scores = (soft * (grad_soft - inner)).astype(BF)
    dq = jnp.einsum("hln,nhc->lhc", grad_scores, heads_of(k), preferred_element_type=F32) * scale
    dk = jnp.einsum("hln,lhc->nhc", grad_scores, heads_of(q), preferred_element_type=F32) * scale
    dv = jnp.einsum(
        "hln,lhc->nhc", soft.astype(BF), heads_of(grad_mix), preferred_element_type=F32
    )
    dq = dq.reshape(gradient.shape).astype(BF)
    dk = dk.reshape(-1, width).astype(BF)
    dv = dv.reshape(-1, width).astype(BF)
    grad_x, gain_q_grad = norm_back(mm_cols(dq, proj[:, :width]), unit_x, inv_x, gain_q)
    back_s = mm_cols(dk, proj[:, width : 2 * width]) + mm_cols(dv, proj[:, 2 * width :])
    grad_s, gain_kv_grad = norm_back(back_s, unit_s, inv_s, gain_kv)
    pairs = ((queries_in, dq), (keys_in, dk), (keys_in, dv), (mixture, gradient))
    return grad_x, grad_s, gain_q_grad, gain_kv_grad, pairs


def feed(inputs, gain, w_in, b_in, w_down, b_out):
    unit, inverse = unit_rows(inputs)
    lowered = (unit * gain).astype(BF)
    pre_act = mm(lowered, w_in) + b_in
    active = jax.nn.gelu(pre_act).astype(BF)
    result = (inputs + mm_cols(active, w_down) + b_out).astype(BF)
    return result, (unit, inverse, lowered, pre_act, active)


def feed_back(gradient, kept, gain, w_in, w_down):
    unit, inverse, lowered, pre_act, active = kept
    grad_act = mm(gradient, w_down)
    grad_pre = jax.vjp(jax.nn.gelu, pre_act)[1](grad_act)[0].astype(BF)
    grad_x, gain_grad = norm_back(mm_cols(grad_pre, w_in), unit, inverse, gain)
    bias_grad = jnp.sum(grad_pre.astype(F32), axis=0)
    out_grad = jnp.sum(gradient.astype(F32), axis=0)
    return grad_x, gain_grad, bias_grad, out_grad, ((lowered, grad_pre), (gradient, active))


def gelu(value):
    inner = math.sqrt(2.0 / math.pi) * (value + 0.044715 * (value * value * value))
    return value * (0.5 * (1.0 + jnp.tanh(inner)))


def tiles(count, body):
    def step(index, carry):
        body(pl.ds(pl.multiple_of(index * 256, 256), 256), index)
        return carry

    lax.fori_loop(0, count, step, 0)


def norm_into(source, gain, target):
    def step(index, carry):
        here = pl.ds(pl.multiple_of(index * 32, 32), 32)
        unit, _ = unit_rows(source[here, :].astype(F32))
        target[here, :] = (unit * gain).astype(BF)
        return carry

    lax.fori_loop(0, source.shape[0] // 32, step, 0)


def gather_kernel(*refs):
    cross_proj, cross_out, mlp_in, mlp_down, self_proj, self_out = refs[:6]
    vec_in, x_in, src_in, mask_in, cot_in = refs[6:11]
    section_at = lax.axis_index("section")
    batch_at = lax.axis_index("batch")
    x_at = lax.rem(section_at, 2)
    y_at = section_at // 2
    ins = (
        cross_proj,
        cross_out,
        mlp_in.at[0],
        mlp_down.at[0],
        self_proj,
        self_out,
        mlp_in.at[1],
        mlp_down.at[1],
    )
    count = len(ins)
    outs = refs[11 : 11 + count]
    rest = refs[11 + count :]
    gains, norm_out = rest[:2]
    kept_outs = rest[2:21]
    (
        u1,
        u2,
        u3,
        u4,
        grad_top,
        xq_c,
        sn_c,
        q_c,
        k_c,
        v_c,
        o_c,
        xn_s,
        q_s,
        k_s,
        v_s,
        o_s,
        lowered,
        before,
        active,
        slots,
        total_rows,
        part_out,
        part_in,
        vec_out,
        biases,
        plane,
        line_in,
    ) = rest[21:48]
    (own_sem, send, recv, kin_send, kin_recv, vec_sems) = rest[48:54]
    (slot_sems, kept_sems, plane_sems, line_sems, pair_sems) = rest[54:]
    line = 4
    core = lax.rem(batch_at, 2)
    spot = batch_at // 2
    beside = section_at + 1 - 2 * x_at
    above = lax.rem(section_at + 2, 4)
    sibling = batch_at + 1 - 2 * core
    shard = ins[0].shape[0]
    place = section_at * 2 + core
    rows = x_in.shape[0]

    def down_line(step):
        return lax.rem(spot + step, line) * 2 + core

    def up_line(step):
        return lax.rem(spot + line - step, line) * 2 + core

    near_peers = []
    for turn in range(1, 8):
        other = lax.rem(place + turn, 8)
        near_peers.append((other // 2, spot * 2 + lax.rem(other, 2)))
    line_peers = [(section_at, down_line(step)) for step in range(1, line)]
    far_peers = [(section_at, down_line(step) + 1 - 2 * core) for step in range(1, line)]
    vec_peers = [(section_at, sibling)] + line_peers + far_peers
    peers = near_peers + line_peers + far_peers
    barrier = pltpu.get_barrier_semaphore()
    for peer in peers:
        pl.semaphore_signal(barrier, inc=1, device_id=peer, device_id_type=MESH)
    pl.semaphore_wait(barrier, len(peers))

    def spread(ref, owner, first, size):
        return ref.at[pl.ds(pl.multiple_of(owner * shard, shard), shard), pl.ds(first, size)]

    def is_feed(item):
        return item % 8 >= 4

    def source_of(item, first, size):
        index, start = GATHERED[item]
        if is_feed(item):
            first = pl.multiple_of(first + y_at * outs[index].shape[1], 128)
        return ins[index].at[:, pl.ds(first, size)]

    def piece(item):
        start = GATHERED[item][1]
        if is_feed(item):
            return pl.multiple_of(start + x_at * 512, 128), 512
        return pl.multiple_of(start + section_at * 256, 128), 256

    def own_line(item, way):
        first, size = piece(item)
        return pltpu.make_async_remote_copy(
            source_of(item, first, size),
            spread(outs[GATHERED[item][0]], batch_at, first, size),
            send.at[5 * way, item, 0],
            recv.at[0, item, 3 if way else 1],
            device_id=(section_at, batch_at + (-2 if way else 2)),
            device_id_type=MESH,
        )

    def onward_line(item, step, way):
        first, size = piece(item)
        ref = spread(outs[GATHERED[item][0]], up_line(step), first, size)
        return pltpu.make_async_remote_copy(
            ref,
            ref,
            send.at[0, item, step],
            recv.at[0, item, step - 1 if way else step + 1],
            device_id=(section_at, batch_at + (-2 if way else 2)),
            device_id_type=MESH,
        )

    def came_line(item, step):
        first, size = piece(item)
        ref = spread(outs[GATHERED[item][0]], up_line(step), first, size)
        return pltpu.make_async_remote_copy(
            ref,
            ref,
            send.at[0, item, step],
            recv.at[0, item, step],
            device_id=(section_at, sibling),
            device_id_type=MESH,
        )

    def start_line(item):
        @pl.when(spot < 3)
        def _():
            own_line(item, 0).start()

        @pl.when(spot > 0)
        def _():
            own_line(item, 1).start()

    def arrive_line(item):
        for apart in (1, 2, 3):

            @pl.when(spot >= apart)
            def _():
                came_line(item, apart).wait_recv()

                @pl.when(spot < 3)
                def _():
                    onward_line(item, apart, 0).start()

                for copy in near(item, apart):
                    copy.start()

            @pl.when(spot + apart <= 3)
            def _():
                came_line(item, 4 - apart).wait_recv()

                @pl.when(spot > 0)
                def _():
                    onward_line(item, 4 - apart, 1).start()

                for copy in near(item, 4 - apart):
                    copy.start()

    def sent_line(item):
        @pl.when(spot < 3)
        def _():
            own_line(item, 0).wait_send()

        @pl.when(spot > 0)
        def _():
            own_line(item, 1).wait_send()

        for apart in (1, 2, 3):

            @pl.when(jnp.logical_and(spot >= apart, spot < 3))
            def _():
                onward_line(item, apart, 0).wait_send()

            @pl.when(jnp.logical_and(spot + apart <= 3, spot > 0))
            def _():
                onward_line(item, 4 - apart, 1).wait_send()

        for step in (1, 2, 3):
            for copy in near(item, step):
                copy.wait_send()

    def plane_copy(item, step, way, low, wide, peer):
        ref = spread(outs[GATHERED[item][0]], up_line(step), low, wide)
        return pltpu.make_async_remote_copy(
            ref,
            ref,
            send.at[way, item, step],
            recv.at[way, item, step],
            device_id=(peer, batch_at),
            device_id_type=MESH,
        )

    def near(item, step):
        first, size = piece(item)
        copies = [plane_copy(item, step, 1, first, size, beside)]
        if not is_feed(item):
            copies.append(plane_copy(item, step, 2, first, size, above))
        return copies

    def far(item, step):
        start = GATHERED[item][1]
        by_y = pl.multiple_of(start + beside * 256, 128)
        by_x = pl.multiple_of(start + above * 256 + 128, 128)
        return [
            plane_copy(item, step, 3, by_y, 128, above),
            plane_copy(item, step, 4, by_x, 128, beside),
        ]

    def kin(item, step):
        index, start = GATHERED[item]
        if step == 0:
            source = source_of(item, start, GATHER_WIDTH)
        else:
            source = spread(outs[index], up_line(step), start, GATHER_WIDTH)
        return pltpu.make_async_remote_copy(
            source,
            spread(outs[index], up_line(step), start, GATHER_WIDTH),
            kin_send.at[item, step],
            kin_recv.at[item, step],
            device_id=(section_at, sibling),
            device_id_type=MESH,
        )

    def own(item):
        index, start = GATHERED[item]
        return pltpu.make_async_copy(
            source_of(item, start, GATHER_WIDTH),
            spread(outs[index], batch_at, start, GATHER_WIDTH),
            own_sem.at[item],
        )

    def vec_copy(which):
        return pltpu.make_async_remote_copy(
            vec_in,
            vec_out.at[batch_at],
            vec_sems.at[0, which],
            vec_sems.at[1, which],
            device_id=vec_peers[which],
            device_id_type=MESH,
        )

    def slot_copy(item):
        index, start = GATHERED[item]
        return pltpu.make_async_copy(
            outs[index].at[:, pl.ds(start, GATHER_WIDTH)],
            slots.at[item % SLOTS],
            slot_sems.at[item % SLOTS],
        )

    def near_norm(turn):
        return pltpu.make_async_remote_copy(
            plane.at[8],
            plane.at[place],
            plane_sems.at[0, turn],
            plane_sems.at[1, turn],
            device_id=near_peers[turn],
            device_id_type=MESH,
        )

    def far_norm(step):
        return pltpu.make_async_remote_copy(
            line_in.at[4],
            line_in.at[spot],
            line_sems.at[0, step],
            line_sems.at[1, step],
            device_id=line_peers[step],
            device_id_type=MESH,
        )

    def rows_over(layer):
        return pltpu.make_async_remote_copy(
            lowered.at[layer, pl.ds(0, rows)],
            lowered.at[layer, pl.ds(rows, rows)],
            pair_sems.at[0, layer, 0],
            pair_sems.at[1, layer, 0],
            device_id=(above, batch_at),
            device_id_type=MESH,
        )

    def part_over(layer):
        return pltpu.make_async_remote_copy(
            part_out.at[layer],
            part_in.at[layer],
            pair_sems.at[0, layer, 1],
            pair_sems.at[1, layer, 1],
            device_id=(above, batch_at),
            device_id_type=MESH,
        )

    steps = range(1, line)
    total = len(GATHERED)
    started = []

    def launch(copies):
        for copy in copies:
            copy.start()
        started.extend(copies)

    kept = (
        (u1, u2, u3, u4, grad_top)
        + (xq_c, sn_c, q_c, k_c, v_c, o_c)
        + (xn_s, q_s, k_s, v_s, o_s)
        + (lowered, before, active)
    )
    names = {id(ref): place for place, ref in enumerate(kept)}

    def keep(*chosen):
        for ref in chosen:
            index = names[id(ref)]
            pltpu.make_async_copy(ref, kept_outs[index], kept_sems.at[index]).start()

    def row(index):
        return gains[index : index + 1, :]

    def project(source, target, slot):
        def tile(columns, _):
            target[:, columns] = mm(source[...], slots[slot, :, columns]).astype(BF)

        tiles(4, tile)

    def heads(q, k, v, o, masked):
        def head(index, carry):
            here = pl.ds(pl.multiple_of(index * HD, HD), HD)
            scores = mm_cols(q[:, here], k[:, here]) * (1.0 / math.sqrt(HD))
            if masked:
                scores = jnp.where(mask_in[...] > 0.0, scores, MASKED)
            grown = jnp.exp(scores - jnp.max(scores, axis=-1, keepdims=True))
            soft = grown / jnp.sum(grown, axis=-1, keepdims=True)
            o[:, here] = mm(soft.astype(BF), v[:, here]).astype(BF)
            return carry

        lax.fori_loop(0, q.shape[1] // HD, head, 0)

    def close_attention(inputs, o, target, slot):
        def tile(columns, _):
            target[:, columns] = (
                inputs[:, columns].astype(F32) + mm(o[...], slots[slot, :, columns])
            ).astype(BF)

        tiles(4, tile)

    def feed_up(layer, chunk, slot):
        def tile(columns, index):
            first = chunk * GATHER_WIDTH + index * 256
            there = pl.ds(pl.multiple_of(first, 256), 256)
            lanes = pl.ds(pl.multiple_of(y_at * 2048 + first, 256), 256)
            value = mm(lowered[layer], slots[slot, :, columns]) + biases[layer : layer + 1, lanes]
            before[layer, :, there] = value
            active[layer, :, there] = gelu(value).astype(BF)

        tiles(4, tile)

    def feed_down(layer, chunk, slot):
        chosen = pl.ds(chunk * GATHER_WIDTH, GATHER_WIDTH)

        def tile(columns, _):
            value = mm_cols(active[layer, :, chosen], slots[slot, columns, :])
            if chunk == 0:
                total_rows[:, columns] = value
            else:
                value = total_rows[:, columns] + value
                total_rows[:, columns] = value
                part_out[layer, :, columns] = value[rows:].astype(BF)

        tiles(4, tile)

    def feed_close(layer):
        inputs, target = (u1, u3)[layer], (u2, u4)[layer]
        part_over(layer).wait_recv()

        def tile(columns, _):
            target[:, columns] = (
                inputs[:, columns].astype(F32)
                + (total_rows[0:rows, columns] + part_in[layer, :, columns].astype(F32))
                + gains[5 + layer : 6 + layer, columns]
            ).astype(BF)

        tiles(4, tile)
        keep(target)

    def work(item):
        slot_copy(item).wait()
        slot = item % SLOTS
        layer, stage = item // 8, item % 8
        inputs = (x_in, u2)[layer]
        middle = (u1, u3)[layer]
        q, k, v, o = ((q_c, k_c, v_c, o_c), (q_s, k_s, v_s, o_s))[layer]
        if stage == 0:
            if layer == 0:
                norm_into(x_in, row(0), xq_c)
                norm_into(src_in, row(1), sn_c)
                keep(xq_c, sn_c)
            else:
                feed_close(0)
                norm_into(u2, row(2), xn_s)
                keep(xn_s)
            project((xq_c, xn_s)[layer], q, slot)
        elif stage == 1:
            project((sn_c, xn_s)[layer], k, slot)
        elif stage == 2:
            project((sn_c, xn_s)[layer], v, slot)
            heads(q, k, v, o, layer == 0)
            keep(q, k, v, o)
        elif stage == 3:
            close_attention(inputs, o, middle, slot)
            norm_into(middle, row(3 + layer), lowered.at[layer, pl.ds(0, rows)])
            launch([rows_over(layer)])
            keep(middle)
        elif stage % 2 == 0:
            if stage == 4:
                rows_over(layer).wait_recv()
            feed_up(layer, (stage - 4) // 2, slot)
        else:
            feed_down(layer, (stage - 4) // 2, slot)
            if stage == 7:
                launch([part_over(layer)])

    for item in range(AHEAD):
        start_line(item)
    vec_out[batch_at] = vec_in[...]
    for which in range(7):
        vec_copy(which).start()
    for moment in range(total + 4):
        if moment + AHEAD < total:
            start_line(moment + AHEAD)
        if moment < total:
            arrive_line(moment)
            own(moment).start()
            launch([kin(moment, 0)])
        if 0 <= moment - 1 < total:
            for step in steps:
                if is_feed(moment - 1):
                    near(moment - 1, step)[0].wait_recv()
                    launch([kin(moment - 1, step)])
                else:
                    for copy, onward in zip(near(moment - 1, step), far(moment - 1, step)):
                        copy.wait_recv()
                        launch([onward])
        if 0 <= moment - 2 < total and not is_feed(moment - 2):
            for step in steps:
                for copy in far(moment - 2, step):
                    copy.wait_recv()
                launch([kin(moment - 2, step)])
        if moment == 2:
            for which in range(7):
                vec_copy(which).wait()
            for owner in range(8):
                values = vec_out[owner].astype(F32)
                gains[:, owner * 128 : owner * 128 + 128] = values
                for layer in range(2):
                    for part_at in range(4):
                        first = owner * 512 + part_at * 128
                        index = 7 + 4 * layer + part_at
                        biases[layer : layer + 1, first : first + 128] = values[index : index + 1]
        if 0 <= moment - 4 < total:
            work(moment - 4)
        if 0 <= moment - 3 < total:
            own(moment - 3).wait()
            for step in range(line):
                kin(moment - 3, step).wait_recv()
            slot_copy(moment - 3).start()
    keep(lowered, before, active)
    feed_close(1)

    def square(index, carry):
        here = pl.ds(pl.multiple_of(index * 32, 32), 32)
        values = u4[here, :].astype(F32)
        return carry + jnp.sum(values * values, axis=0, keepdims=True)

    squares = lax.fori_loop(0, u4.shape[0] // 32, square, jnp.zeros((1, u4.shape[1]), F32))
    mean = jnp.sum(squares, axis=1, keepdims=True) / (u4.shape[0] * u4.shape[1])
    group_norm = jnp.sqrt(mean + EPSILON)
    plane[8] = jnp.broadcast_to(group_norm, plane.shape[1:])
    for turn in range(7):
        near_norm(turn).start()
    plane[place] = plane[8]
    for turn in range(7):
        near_norm(turn).wait()
    line_in[4] = jnp.sum(plane[0:8], axis=0)
    for step in range(3):
        far_norm(step).start()
    line_in[spot] = line_in[4]
    for step in range(3):
        far_norm(step).wait()
    norm_mean = jnp.sum(line_in[0:4], axis=0) / 32.0
    norm_out[...] = norm_mean
    ratio = norm_mean[0:1, 0:1] / group_norm

    def top(index, carry):
        here = pl.ds(pl.multiple_of(index * 32, 32), 32)
        grad_top[here, :] = (
            cot_in[here, :].astype(F32) + ratio * u4[here, :].astype(F32)
        ).astype(BF)
        return carry

    lax.fori_loop(0, u4.shape[0] // 32, top, 0)
    keep(grad_top)
    for index, ref in enumerate(kept):
        pltpu.make_async_copy(ref, kept_outs[index], kept_sems.at[index]).wait()
    for item in range(total):
        sent_line(item)
    for copy in started:
        copy.wait_send()


def gather_forward(blocks, vectors, inputs, source, mask, cotangent):
    rows, width = inputs.shape
    half = blocks[2].shape[2] // 2
    widths = (3 * width, width, half, half) * 2
    total = len(GATHERED)
    anywhere = pl.BlockSpec(memory_space=pl.ANY)
    vmem = pl.BlockSpec(memory_space=pltpu.VMEM)
    plain = ((rows, width), BF)
    kept = [plain] * 16 + [
        ((2, 2 * rows, width), BF),
        ((2, 2 * rows, half), F32),
        ((2, 2 * rows, half), BF),
    ]
    dma = pltpu.SemaphoreType.DMA
    return pl.pallas_call(
        gather_kernel,
        out_shape=[jax.ShapeDtypeStruct((width, size), BF) for size in widths]
        + [
            jax.ShapeDtypeStruct((vectors.shape[0], width), F32),
            jax.ShapeDtypeStruct((8, 128), F32),
        ]
        + [jax.ShapeDtypeStruct(*one) for one in kept],
        in_specs=[anywhere] * len(blocks) + [vmem] * 5,
        out_specs=[anywhere] * len(widths) + [vmem] * 2 + [anywhere] * len(kept),
        scratch_shapes=[pltpu.VMEM(*one) for one in kept]
        + [
            pltpu.VMEM((SLOTS, width, GATHER_WIDTH), BF),
            pltpu.VMEM((2 * rows, width), F32),
            pltpu.VMEM((2, rows, width), BF),
            pltpu.VMEM((2, rows, width), BF),
            pltpu.VMEM((8, *vectors.shape), BF),
            pltpu.VMEM((2, 2 * half), F32),
            pltpu.VMEM((9, 8, 128), F32),
            pltpu.VMEM((5, 8, 128), F32),
            dma((total,)),
            dma((6, total, 4)),
            dma((5, total, 4)),
            dma((total, 4)),
            dma((total, 4)),
            dma((2, 7)),
            dma((SLOTS,)),
            dma((len(kept),)),
            dma((2, 7)),
            dma((2, 3)),
            dma((2, 2, 2)),
        ],
        compiler_params=pltpu.CompilerParams(
            collective_id=1, has_side_effects=True, vmem_limit_bytes=52 * 2**20
        ),
        cost_estimate=pl.CostEstimate(
            flops=2 * rows * width * sum(widths), bytes_accessed=2**27, transcendentals=2**21
        ),
    )(*blocks, vectors, inputs, source, mask, cotangent)


ITEM_COUNT = 16
WINDOWS = 4
STAGES = 3


def gelu_slope(value):
    factor = math.sqrt(2.0 / math.pi)
    square = value * value
    bent = jnp.tanh(factor * value * (1.0 + 0.044715 * square))
    inner = factor * (1.0 + 3.0 * 0.044715 * square)
    return 0.5 * (1.0 + bent) + 0.5 * value * (1.0 - bent * bent) * inner


def reduce_kernel(*refs):
    total = ITEM_COUNT
    (
        proj_c,
        out_c,
        in_0,
        down_0,
        proj_s,
        out_s,
        in_1,
        down_1,
        u1_in,
        u2_in,
        u3_in,
        last_ref,
        top_in,
        xq_c,
        sn_c,
        q_c,
        k_c,
        v_c,
        o_c,
        xn_s,
        q_s,
        k_s,
        v_s,
        o_s,
        lowered,
        before,
        active,
        x_in,
        src_in,
        gains,
        mask_in,
        picks_in,
    ) = refs[:32]
    (sum_out, last_out, first_out, point_out, small_out) = refs[32:37]
    (pair_h, slope_h, dqkv_h, grads_h, kin_lf, kin_la, kin_rf, kin_ra) = refs[37:45]
    (
        lwin_f,
        lwin_a,
        raw,
        rwin,
        stage,
        merged_f,
        merged_a,
        passing,
        lined_f,
        lined_a,
        crossed_f,
        crossed_a,
        pair,
        slope,
        rows_sum,
        hbuf,
        slots,
        qb,
        kb,
        vb,
        dob,
        dqkv,
        part_out,
        part_in,
        grad,
        ub,
        point_in,
        point_sum,
        small_in,
        small_sum,
    ) = refs[45:75]
    (
        kin_l_sems,
        kin_r_sems,
        raw_sems,
        win_sems,
        xy_sems,
        line_send,
        line_recv,
        cross_sems,
        out_sems,
        own_sems,
        lat_sems,
        far_sems,
        lat_own,
        point_sems,
        deal_sems,
        point_own,
        small_sems,
        pair_sems,
        slot_sems,
        h_sem,
        save_sems,
        act_sems,
    ) = refs[75:]
    section_at = lax.axis_index("section")
    batch_at = lax.axis_index("batch")
    core = lax.rem(batch_at, 2)
    spot = batch_at // 2
    x_at = lax.rem(section_at, 2)
    y_at = section_at // 2
    beside = section_at + 1 - 2 * x_at
    above = lax.rem(section_at + 2, 4)
    across = lax.rem(beside + 2, 4)
    sibling = batch_at + 1 - 2 * core
    flat = (beside, above)
    bits = (x_at, y_at)
    rows, width = 256, 1024

    peers = [(beside, batch_at), (above, batch_at), (across, batch_at), (section_at, sibling)]
    peers += [(section_at, lax.rem(spot + step, 4) * 2 + core) for step in (1, 2, 3)]
    barrier = pltpu.get_barrier_semaphore()
    for peer in peers:
        pl.semaphore_signal(barrier, inc=1, device_id=peer, device_id_type=MESH)
    pl.semaphore_wait(barrier, len(peers))

    def remote(source, target, sems, where, peer):
        return pltpu.make_async_remote_copy(
            source,
            target,
            sems.at[(0, *where)],
            sems.at[(1, *where)],
            device_id=peer,
            device_id_type=MESH,
        )

    feed_left = (pair_h.at[0], lowered.at[1], pair_h.at[1], lowered.at[0])
    feed_right = (active.at[1], slope_h.at[0], active.at[0], slope_h.at[1])
    att_left = (o_s, xn_s, xn_s, xn_s, o_c, xq_c, sn_c, sn_c)
    att_right = tuple(
        ref
        for turn in range(2)
        for ref in (grads_h.at[turn], dqkv_h.at[turn, 0], dqkv_h.at[turn, 1], dqkv_h.at[turn, 2])
    )

    def columns(spot_of, parity):
        return pl.ds(pl.multiple_of((2 * spot_of + parity) * 128, 128), 128)

    def kin_lefts(feed, job):
        source, target = (feed_left, kin_lf) if feed else (att_left, kin_la)
        return [
            remote(
                source[job].at[:, columns(part, 1 - core)],
                target.at[job, part],
                kin_l_sems,
                (job if feed else 4 + job, part),
                (section_at, sibling),
            )
            for part in range(4)
        ]

    def kin_right(feed, job, chunk):
        if feed:
            here = pl.ds(chunk * 1024, 1024)
            source, target = feed_right[job].at[:, here], kin_rf.at[job, :, here]
        else:
            source, target = att_right[job], kin_ra.at[job]
        where = (2 * job + chunk if feed else 8 + job,)
        return remote(source, target, kin_r_sems, where, (section_at, sibling))

    def item_of(index):
        turn, inner = index // 8, index % 8
        if inner < 4:
            return True, 2 * turn + inner // 2, inner % 2
        return False, 4 * turn + inner - 4, 0

    def window_copies(index):
        feed, job, chunk = item_of(index)
        slot = index % WINDOWS
        size = 512 if feed else 256
        if feed:
            here = pl.ds(chunk * 1024, 1024)
            sources = (feed_right[job].at[:, here], kin_rf.at[job, :, here])
        else:
            sources = (att_right[job], kin_ra.at[job])
        return [
            pltpu.make_async_copy(
                sources[whose],
                rwin.at[slot, pl.ds(whose * size, size)],
                win_sems.at[slot, whose],
            )
            for whose in range(2)
        ]

    def load(index):
        feed, job, chunk = item_of(index)
        kin_right(feed, job, chunk).wait_recv()
        for copy in window_copies(index):
            copy.start()
        if chunk == 0:
            for copy in kin_lefts(feed, job):
                copy.wait_recv()
            size = 512 if feed else 256
            own_left = (feed_left if feed else att_left)[job]
            kin_left = (kin_lf if feed else kin_la).at[job]
            target = (lwin_f if feed else lwin_a).at[job]
            for part in range(4):
                copies = [
                    pltpu.make_async_copy(
                        own_left.at[:, columns(part, core)],
                        raw.at[part, 0, pl.ds(0, size)],
                        raw_sems.at[part, 0],
                    ),
                    pltpu.make_async_copy(
                        kin_left.at[part], raw.at[part, 1, pl.ds(0, size)], raw_sems.at[part, 1]
                    ),
                ]
                for copy in copies:
                    copy.start()
            for part in range(4):
                for whose, source in enumerate(
                    (own_left.at[:, columns(part, core)], kin_left.at[part])
                ):
                    place = raw.at[part, whose, pl.ds(0, size)]
                    pltpu.make_async_copy(source, place, raw_sems.at[part, whose]).wait()
                    target[part, :, whose * size : whose * size + size] = place[...].T

    def is_feed(item):
        return lax.rem(item, 8) < 4

    def feed_job(item):
        return 2 * (item // 8) + lax.rem(item, 8) // 2

    def att_job(item):
        return 4 * (item // 8) + lax.rem(item, 8) - 4

    def loaded(slot, feed):
        size = 512 if feed else 256
        for whose in range(2):
            source = kin_rf.at[0, :, pl.ds(0, 1024)] if feed else kin_ra.at[0]
            pltpu.make_async_copy(
                source, rwin.at[slot, pl.ds(whose * size, size)], win_sems.at[slot, whose]
            ).wait()

    def by_kind(item, action):
        pl.when(is_feed(item))(functools.partial(action, item, True))
        pl.when(jnp.logical_not(is_feed(item)))(functools.partial(action, item, False))

    def merged_of(item, feed):
        return merged_f.at[lax.rem(item, 4)] if feed else merged_a.at[att_job(item)]

    def passing_of(item, feed, slot):
        ref = passing.at[lax.rem(item, 8), slot]
        return ref if feed else ref.at[:, pl.ds(0, 512)]

    def lined_of(item, feed):
        return lined_f.at[lax.rem(item, 4)] if feed else lined_a.at[att_job(item)]

    def crossed_of(item, feed):
        return crossed_f.at[lax.rem(item, 4)] if feed else crossed_a.at[att_job(item)]

    def products(item, choice, store):
        slot = lax.rem(item, WINDOWS)

        def quarter(index, carry):
            upper, part = index // 2, lax.rem(index, 2)
            here = pl.ds(pl.multiple_of(part * 256, 256), 256)
            bit = choice[0] + part * (choice[1] - choice[0])
            first = pl.multiple_of(part * 512 + bit * 256, 256)
            left = lwin_a[att_job(item), pl.ds(upper * 2, 2)].reshape(256, 512)
            right = rwin[slot, 0:512, pl.ds(first, 256)]
            tile = jnp.dot(left, right, preferred_element_type=F32).reshape(2, 128, 256)
            store(pl.ds(upper * 2, 2), here, tile)
            return carry

        lax.fori_loop(0, 4, quarter, 0)

    def xy_copies(item):
        return [
            remote(
                stage.at[lax.rem(att_job(item), STAGES), :, :, pl.ds(side * 256, 256)],
                merged_a.at[att_job(item), :, :, pl.ds(side * 256, 256)],
                xy_sems,
                (att_job(item), side),
                (flat[side], batch_at),
            )
            for side in range(2)
        ]

    def xy_sent(item):
        for copy in xy_copies(item):
            copy.wait_send()

    def line_copy(item, feed, dest, place, rightward):
        step = 1 if rightward else -1
        slot = 4 if not rightward and place - 1 == dest else dest
        return pltpu.make_async_remote_copy(
            merged_of(item, feed).at[dest],
            passing_of(item, feed, slot),
            line_send.at[item, dest],
            line_recv.at[item, slot],
            device_id=(section_at, batch_at + 2 * step),
            device_id_type=MESH,
        )

    def line_wait(item, feed, slot):
        pltpu.make_async_remote_copy(
            merged_of(item, feed).at[0],
            passing_of(item, feed, slot),
            line_send.at[item, 0],
            line_recv.at[item, slot],
            device_id=(section_at, sibling),
            device_id_type=MESH,
        ).wait_recv()

    def line_sent(item, feed):
        for step in (1, 2, 3):
            dest = lax.rem(spot + step, 4)
            pltpu.make_async_remote_copy(
                merged_of(item, feed).at[dest],
                passing_of(item, feed, 0),
                line_send.at[item, dest],
                line_recv.at[item, 0],
                device_id=(section_at, sibling),
                device_id_type=MESH,
            ).wait_send()

    def outset(item, feed):
        @pl.when(spot == 0)
        def _():
            for dest in (3, 2, 1):
                line_copy(item, feed, dest, 0, True).start()

        @pl.when(spot == 3)
        def _():
            for dest in (0, 1, 2):
                line_copy(item, feed, dest, 3, False).start()

    def drained(item, feed):
        line_sent(item, feed)
        if feed:
            feed_out(item).wait()
            feed_own(item).wait()
        else:
            for side in range(2):
                att_out(item, side).wait()
                att_own(item, side).wait()

    def offer(item, feed):
        slot = lax.rem(item, WINDOWS)
        loaded(slot, feed)
        if feed:

            @pl.when(item >= 8)
            def _():
                drained(item - 8, True)

            target = merged_of(item, True)

            def tile(index, carry):
                upper, part = index // 4, lax.rem(index, 4)
                here = pl.ds(pl.multiple_of(part * 256, 256), 256)
                left = lwin_f[feed_job(item), pl.ds(upper * 2, 2)].reshape(256, 1024)
                right = rwin[slot, :, here]
                value = jnp.dot(left, right, preferred_element_type=F32)
                target[pl.ds(upper * 2, 2), :, here] = value.reshape(2, 128, 256).astype(BF)
                return carry

            lax.fori_loop(0, 8, tile, 0)
            outset(item, True)
        else:

            @pl.when(lax.rem(item, 8) >= 4 + STAGES)
            def _():
                xy_sent(item - STAGES)

            @pl.when(jnp.logical_and(item >= 12, lax.rem(item, 8) < 4 + STAGES))
            def _():
                xy_sent(item - STAGES - 4)

            def store(blocks, here, tile):
                stage[lax.rem(att_job(item), STAGES), blocks, :, here] = tile.astype(BF)

            products(item, (1 - x_at, 1 - y_at), store)
            for copy in xy_copies(item):
                copy.start()

    def take(item):
        for copy in xy_copies(item):
            copy.wait_recv()
        target = merged_a.at[att_job(item)]

        def store(blocks, here, tile):
            target[blocks, :, here] = (tile + target[blocks, :, here].astype(F32)).astype(BF)

        products(item, bits, store)
        outset(item, False)

    def first(item):
        pl.when(jnp.logical_not(is_feed(item)))(functools.partial(take, item))

    def relay(item, feed, dest, place, rightward):
        line_wait(item, feed, dest)
        target = merged_of(item, feed)
        arrived = passing_of(item, feed, dest)
        target[dest] = (target[dest].astype(F32) + arrived[...].astype(F32)).astype(BF)
        line_copy(item, feed, dest, place, rightward).start()

    def second_of(item, feed):
        @pl.when(spot == 1)
        def _():
            for dest in (3, 2):
                relay(item, feed, dest, 1, True)

        @pl.when(spot == 2)
        def _():
            for dest in (0, 1):
                relay(item, feed, dest, 2, False)

    def third_of(item, feed):
        @pl.when(spot == 1)
        def _():
            relay(item, feed, 0, 1, False)

        @pl.when(spot == 2)
        def _():
            relay(item, feed, 3, 2, True)

    def second(item):
        by_kind(item, second_of)

    def third(item):
        by_kind(item, third_of)

    def feed_cross(item):
        return remote(
            lined_of(item, True),
            crossed_of(item, True),
            cross_sems,
            (item, 0),
            (beside, batch_at),
        )

    def cross_copy(item, side):
        here = pl.ds(side * 256, 256)
        return remote(
            lined_of(item, False).at[:, here],
            crossed_of(item, False).at[:, here],
            cross_sems,
            (item, side),
            (flat[1 - side], batch_at),
        )

    def layer_of(item):
        return 1 - item // 8

    def feed_place(item):
        inner = lax.rem(item, 8)
        base = (1 - inner // 2) * 4096 + y_at * 2048 + lax.rem(inner, 2) * 1024
        return sum_out.at[layer_of(item), :, pl.ds(pl.multiple_of(base, 1024), 1024)]

    def feed_out(item):
        return remote(
            lined_of(item, True), feed_place(item), out_sems, (item, 0), (above, batch_at)
        )

    def feed_own(item):
        return pltpu.make_async_copy(
            lined_of(item, True), feed_place(item), own_sems.at[item, 0]
        )

    def att_place(item, side):
        inner = lax.rem(lax.rem(item, 8) + 3, 4)
        base = 8192 + inner * 1024 + side * 512 + bits[side] * 256
        return sum_out.at[layer_of(item), :, pl.ds(pl.multiple_of(base, 256), 256)]

    def att_out(item, side):
        return remote(
            lined_of(item, False).at[:, pl.ds(side * 256, 256)],
            att_place(item, side),
            out_sems,
            (item, side),
            (flat[side], batch_at),
        )

    def att_own(item, side):
        return pltpu.make_async_copy(
            lined_of(item, False).at[:, pl.ds(side * 256, 256)],
            att_place(item, side),
            own_sems.at[item, side],
        )

    def close_of(item, feed):
        for place in range(4):

            @pl.when(spot == place)
            def _():
                value = merged_of(item, feed)[place].astype(F32)
                if place > 0:
                    line_wait(item, feed, place)
                    value += passing_of(item, feed, place)[...].astype(F32)
                if place < 3:
                    line_wait(item, feed, 4)
                    value += passing_of(item, feed, 4)[...].astype(F32)
                lined_of(item, feed)[...] = value.astype(BF)

        if feed:
            feed_cross(item).start()
        else:
            for side in range(2):
                cross_copy(item, side).start()

    def close(item):
        by_kind(item, close_of)

    def finish_of(item, feed):
        if feed:
            feed_cross(item).wait()
        else:
            for side in range(2):
                cross_copy(item, side).wait()
        target = lined_of(item, feed)
        target[...] = (
            target[...].astype(F32) + crossed_of(item, feed)[...].astype(F32)
        ).astype(BF)
        if feed:
            feed_out(item).start()
            feed_own(item).start()
        else:
            for side in range(2):
                att_out(item, side).start()
                att_own(item, side).start()

    def finish(item):
        by_kind(item, finish_of)

    def small_copy(phase):
        if phase == 0:
            peer = (section_at, sibling)
        elif phase < 3:
            peer = (flat[phase - 1], batch_at)
        else:
            peer = (section_at, lax.rem(spot + phase - 2, 4) * 2 + core)
        return remote(
            small_sum.at[min(phase, 3)], small_in.at[phase], small_sems, (phase,), peer
        )

    quarter_rows = pair.shape[0] // 4

    def point_copy(which):
        peer = (beside, above, across)[which]
        return remote(
            pair.at[pl.ds(pl.multiple_of(peer * quarter_rows, 128), quarter_rows)],
            point_in.at[which],
            point_sems,
            (which,),
            (peer, batch_at),
        )

    def point_place():
        return point_out.at[pl.ds(pl.multiple_of(section_at * quarter_rows, 128), quarter_rows)]

    def point_deal(which):
        peer = (beside, above, across)[which]
        return remote(point_sum, point_place(), deal_sems, (which,), (peer, batch_at))

    def point_local():
        return pltpu.make_async_copy(point_sum, point_place(), point_own.at[0])

    pairs = ((last_ref, last_out), (grad, first_out))

    def lat_copy(which, way):
        source, target = pairs[which]
        return remote(
            source,
            target.at[pl.ds(pl.multiple_of(section_at * rows, rows), rows)],
            lat_sems,
            (which, way),
            (flat[way], batch_at),
        )

    def lat_far(which, way):
        target = pairs[which][1]
        low = flat[way] * rows + way * (rows // 2)
        part = target.at[pl.ds(pl.multiple_of(low, rows // 2), rows // 2)]
        return remote(part, part, far_sems, (which, way), (flat[1 - way], batch_at))

    def lat_local(which):
        source, target = pairs[which]
        return pltpu.make_async_copy(
            source,
            target.at[pl.ds(pl.multiple_of(section_at * rows, rows), rows)],
            lat_own.at[which],
        )

    def lat_start(which):
        lat_local(which).start()
        for way in range(2):
            lat_copy(which, way).start()

    def lat_onward(which):
        for way in range(2):
            lat_copy(which, way).wait_recv()
            lat_far(which, way).start()

    loads = []
    for turn, (proj, out, up, down) in enumerate(
        ((proj_s, out_s, in_1, down_1), (proj_c, out_c, in_0, down_0))
    ):
        for chunk in range(2):
            loads += [down.at[:, pl.ds(chunk * 1024, 1024)], up.at[:, pl.ds(chunk * 1024, 1024)]]
        loads.append(out)
        loads += [proj.at[:, pl.ds(which * 1024, 1024)] for which in range(3)]

    def slot_copy(index):
        return pltpu.make_async_copy(loads[index], slots.at[index % 2], slot_sems.at[index % 2])

    def opened(index):
        slot_copy(index).wait()
        return index % 2

    def closed(index):
        if index + 2 < len(loads):
            slot_copy(index + 2).start()

    def h_copy(index):
        layer, chunk = 1 - index // 2, index % 2
        return pltpu.make_async_copy(
            before.at[layer, :, pl.ds(chunk * 1024, 1024)], hbuf, h_sem.at[0]
        )

    def pair_over(turn):
        return remote(
            pair.at[pl.ds(0, rows)],
            pair.at[pl.ds(rows, rows)],
            pair_sems,
            (turn, 0),
            (above, batch_at),
        )

    def part_over(turn):
        return remote(
            part_out.at[turn], part_in.at[turn], pair_sems, (turn, 1), (above, batch_at)
        )

    def saved(source, target, index):
        copy = pltpu.make_async_copy(source, target, save_sems.at[index])
        copy.start()
        copy.wait()

    def act_copies(turn):
        chosen = ((q_s, k_s, v_s), (q_c, k_c, v_c))[turn]
        return [
            pltpu.make_async_copy(source, target, act_sems.at[index])
            for index, (source, target) in enumerate(zip(chosen, (qb, kb, vb)))
        ]

    def row_copy(index):
        source = (u3_in, u2_in, u1_in, x_in)[index]
        return pltpu.make_async_copy(source, ub, act_sems.at[3])

    def small_row(index, value):
        small_sum[0, index : index + 1, :] = value

    def open_pair(turn):
        pair[0:rows, :] = grad[...]
        pair_over(turn).start()

    def pair_ready(turn):
        pair_over(turn).wait()
        saved(pair, pair_h.at[turn], 0)
        for copy in kin_lefts(True, 2 * turn):
            copy.start()

    def feed_chunk(turn, chunk):
        layer = 1 - turn
        base = 8 * turn + 2 * chunk
        h_copy(2 * turn + chunk).wait()
        slot = opened(base)

        def up_tile(here, index):
            there = pl.ds(pl.multiple_of(chunk * 1024 + index * 256, 256), 256)
            value = mm(pair[...], slots[slot, :, here]) * gelu_slope(hbuf[:, here])
            short = value.astype(BF)
            slope[:, there] = short
            column = jnp.sum(short.astype(F32), axis=0, keepdims=True)
            for half in range(2):
                index_at = 7 + 4 * layer + 2 * half + chunk
                small_sum[0, index_at : index_at + 1, here] = jnp.where(
                    y_at == half, column, jnp.zeros_like(column)
                )

        tiles(4, up_tile)
        closed(base)
        if 2 * turn + chunk + 1 < 4:
            h_copy(2 * turn + chunk + 1).start()
        here = pl.ds(chunk * 1024, 1024)
        saved(slope.at[:, here], slope_h.at[turn, :, here], 0)
        kin_right(True, 2 * turn + 1, chunk).start()
        slot = opened(base + 1)

        def down_tile(there, _):
            value = mm_cols(slope[:, chunk * 1024 : chunk * 1024 + 1024], slots[slot, there, :])
            if chunk == 0:
                rows_sum[:, there] = value
            else:
                value = rows_sum[:, there] + value
                rows_sum[:, there] = value
                part_out[turn, :, there] = value[rows:].astype(BF)

        tiles(4, down_tile)
        closed(base + 1)
        if chunk == 1:
            part_over(turn).start()

    def row_steps(body, count):
        zero = jnp.zeros((1, width), F32)

        def step(index, carry):
            here = pl.ds(pl.multiple_of(index * 32, 32), 32)
            return tuple(a + b for a, b in zip(carry, body(here)))

        return lax.fori_loop(0, rows // 32, step, (zero,) * count)

    def lean(back, unit, inverse, gain):
        scaled = back * gain
        inner = (
            scaled
            - jnp.mean(scaled, axis=-1, keepdims=True)
            - unit * jnp.mean(scaled * unit, axis=-1, keepdims=True)
        )
        return inverse * inner, jnp.sum(back * unit, axis=0, keepdims=True)

    def feed_end(turn):
        layer = 1 - turn
        gain = gains[3 + layer : 4 + layer, :]
        part_over(turn).wait_recv()
        row_copy(2 * turn).wait()

        def body(here):
            unit, inverse = unit_rows(ub[here, :].astype(F32))
            back = rows_sum[here, :] + part_in[turn, here, :].astype(F32)
            dx, gain_part = lean(back, unit, inverse, gain)
            old = grad[here, :].astype(F32)
            grad[here, :] = (old + dx).astype(BF)
            return gain_part, jnp.sum(old, axis=0, keepdims=True)

        gain_grad, out_grad = row_steps(body, 2)
        row_copy(2 * turn + 1).start()
        small_row(3 + layer, gain_grad)
        small_row(5 + layer, out_grad)
        saved(grad, grads_h.at[turn], 0)
        for copy in kin_lefts(False, 4 * turn):
            copy.start()
        kin_right(False, 4 * turn, 0).start()
        slot = opened(8 * turn + 4)

        def tile(there, _):
            dob[:, there] = mm_cols(grad[...], slots[slot, there, :]).astype(BF)

        tiles(4, tile)
        closed(8 * turn + 4)

    def attend_heads(turn):
        scale = 1.0 / math.sqrt(HD)
        for copy in act_copies(turn):
            copy.wait()

        def head(index, carry):
            here = pl.ds(pl.multiple_of(index * HD, HD), HD)
            q, k, v, do = qb[:, here], kb[:, here], vb[:, here], dob[:, here]
            scores = mm_cols(q, k) * scale
            if turn == 1:
                scores = jnp.where(mask_in[...] > 0.0, scores, MASKED)
            grown = jnp.exp(scores - jnp.max(scores, axis=-1, keepdims=True))
            soft = grown / jnp.sum(grown, axis=-1, keepdims=True)
            back = mm_cols(do, v)
            short = soft * (back - jnp.sum(soft * back, axis=-1, keepdims=True))
            dqkv[0, :, here] = (mm(short.astype(BF), k) * scale).astype(BF)
            dqkv[1, :, here] = (mm(short.T.astype(BF), q) * scale).astype(BF)
            dqkv[2, :, here] = mm(soft.T.astype(BF), do).astype(BF)
            return carry

        lax.fori_loop(0, width // HD, head, 0)
        if turn == 0:
            for copy in act_copies(1):
                copy.start()
        saved(dqkv, dqkv_h.at[turn], 0)
        for which in range(3):
            for copy in kin_lefts(False, 4 * turn + 1 + which):
                copy.start()
            kin_right(False, 4 * turn + 1 + which, 0).start()

    def attend_end(turn):
        base = 8 * turn + 5
        for which in range(3):
            slot = opened(base + which)

            def tile(there, _):
                value = mm_cols(dqkv[which], slots[slot, there, :])
                if which == 0:
                    rows_sum[0:rows, there] = value
                elif which == 1:
                    rows_sum[rows : 2 * rows, there] = value
                else:
                    rows_sum[rows : 2 * rows, there] += value

            tiles(4, tile)
            closed(base + which)
        row_copy(2 * turn + 1).wait()
        gain_q = gains[2:3, :] if turn == 0 else gains[0:1, :]
        gain_kv = gains[2:3, :] if turn == 0 else gains[1:2, :]

        def body(here):
            unit, inverse = unit_rows(ub[here, :].astype(F32))
            dx, gain_part = lean(rows_sum[here, :], unit, inverse, gain_q)
            if turn == 1:
                unit, inverse = unit_rows(src_in[here, :].astype(F32))
            there = pl.ds(pl.multiple_of(rows + here.start, 32), 32)
            ds, kv_part = lean(rows_sum[there, :], unit, inverse, gain_kv)
            fresh = grad[here, :].astype(F32) + dx
            if turn == 0:
                fresh += ds
            else:
                high = ds.astype(BF)
                part_out[0, here, :] = high
                part_out[1, here, :] = (ds - high.astype(F32)).astype(BF)
            grad[here, :] = fresh.astype(BF)
            return gain_part, kv_part

        if turn == 1:
            for which in range(2):
                part_over(which).wait_send()
        gain_grad, kv_grad = row_steps(body, 2)
        if turn == 0:
            row_copy(2).start()
            small_row(2, gain_grad + kv_grad)
            open_pair(1)
        else:
            small_row(0, gain_grad)
            small_row(1, kv_grad)
            small_row(15, jnp.zeros_like(gain_grad))

            def tile(there, _):
                pair[:, there] = (
                    mm(picks_in[...], part_out[0, :, there])
                    + mm(picks_in[...], part_out[1, :, there])
                ).astype(BF)

            tiles(4, tile)
            small_copy(0).start()
            for which in range(3):
                point_copy(which).start()
            lat_start(1)

    def point_total():
        for which in range(3):
            point_copy(which).wait_recv()
        gathered = pair[
            pl.ds(pl.multiple_of(section_at * quarter_rows, 128), quarter_rows)
        ].astype(F32)
        for which in range(3):
            gathered += point_in[which].astype(F32)
        point_sum[...] = gathered.astype(BF)
        point_local().start()
        for which in range(3):
            point_deal(which).start()

    def small_step(phase):
        small_copy(phase).wait_recv()
        small_sum[phase + 1] = small_sum[phase] + small_in[phase]
        if phase < 2:
            small_copy(phase + 1).start()
        else:
            for step in range(3):
                small_copy(3 + step).start()

    def small_end():
        for step in range(3):
            small_copy(3 + step).wait_recv()
        small_out[...] = (small_sum[3] + small_in[4]) + (small_in[3] + small_in[5])

    def rows_end():
        lat_onward(1)
        point_total()

    begin = pltpu.make_async_copy(top_in, grad, act_sems.at[4])
    begin.start()
    for index in range(2):
        slot_copy(index).start()
    h_copy(0).start()
    row_copy(0).start()
    for copy in act_copies(0):
        copy.start()
    begin.wait()
    open_pair(0)
    for turn in range(2):
        for part in range(2):
            kin_right(True, 2 * turn, part).start()
        for copy in kin_lefts(True, 2 * turn + 1):
            copy.start()
    pair_ready(0)
    load(0)
    chain = {
        0: [functools.partial(feed_chunk, 0, 0), functools.partial(lat_start, 0)],
        1: [functools.partial(feed_chunk, 0, 1)],
        2: [functools.partial(feed_end, 0), functools.partial(lat_onward, 0)],
        3: [functools.partial(attend_heads, 0)],
        4: [functools.partial(attend_end, 0)],
        5: [functools.partial(pair_ready, 1), functools.partial(feed_chunk, 1, 0)],
        6: [functools.partial(feed_chunk, 1, 1)],
        7: [functools.partial(feed_end, 1)],
        8: [functools.partial(attend_heads, 1)],
        9: [functools.partial(attend_end, 1)],
        11: [functools.partial(small_step, 0), rows_end],
        13: [functools.partial(small_step, 1)],
        15: [functools.partial(small_step, 2)],
        17: [small_end],
    }

    def moment_body(moment, carry):
        @pl.when(moment < total)
        def _():
            by_kind(moment, offer)

        for lag, action in ((2, first), (3, second), (4, third), (5, close), (6, finish)):
            pl.when(jnp.logical_and(moment >= lag, moment < total + lag))(
                functools.partial(action, moment - lag)
            )
        for when, actions in chain.items():

            @pl.when(moment == when)
            def _():
                for action in actions:
                    action()

        for item in range(1, total):
            pl.when(moment == item - 1)(functools.partial(load, item))
        return carry

    lax.fori_loop(0, total + 6, moment_body, 0)

    for index in range(4):
        for copy in kin_lefts(True, index):
            copy.wait_send()
        for chunk in range(2):
            kin_right(True, index, chunk).wait_send()
    for index in range(8):
        for copy in kin_lefts(False, index):
            copy.wait_send()
        kin_right(False, index, 0).wait_send()
    for phase in range(6):
        small_copy(phase).wait_send()
    for which in range(2):
        lat_local(which).wait()
        for way in range(2):
            lat_copy(which, way).wait_send()
            lat_far(which, way).wait()
    point_local().wait()
    for which in range(3):
        point_copy(which).wait_send()
        point_deal(which).wait()

    def drain(item, carry):
        @pl.when(item >= 4)
        def _():
            by_kind(item, drained)

        return carry

    for item in range(total - STAGES, total):
        xy_sent(item)
    lax.fori_loop(0, total, drain, 0)


def reduce_all(full, kept, inputs, source, gains, mask, picks):
    total = ITEM_COUNT
    rows, width = inputs.shape
    points = picks.shape[0]
    anywhere = pl.BlockSpec(memory_space=pl.ANY)
    vmem = pl.BlockSpec(memory_space=pltpu.VMEM)
    u1, u2, u3, u4, top = kept[:5]
    operands = [*full, u1, u2, u3, u4, top, *kept[5:], inputs, source, gains, mask, picks]
    spaces = [anywhere] * (len(operands) - 4) + [vmem] * 4
    dma = pltpu.SemaphoreType.DMA
    flops = 2 * width * width * 24 * rows * 2
    return pl.pallas_call(
        reduce_kernel,
        out_shape=[
            jax.ShapeDtypeStruct((2, 128, 12 * width), BF),
            jax.ShapeDtypeStruct((4 * rows, width), BF),
            jax.ShapeDtypeStruct((4 * rows, width), BF),
            jax.ShapeDtypeStruct((points, width), BF),
            jax.ShapeDtypeStruct((16, width), F32),
            jax.ShapeDtypeStruct((2, 2 * rows, width), BF),
            jax.ShapeDtypeStruct((2, 2 * rows, 2 * width), BF),
            jax.ShapeDtypeStruct((2, 3, rows, width), BF),
            jax.ShapeDtypeStruct((2, rows, width), BF),
            jax.ShapeDtypeStruct((4, 4, 2 * rows, 128), BF),
            jax.ShapeDtypeStruct((8, 4, rows, 128), BF),
            jax.ShapeDtypeStruct((4, 2 * rows, 2 * width), BF),
            jax.ShapeDtypeStruct((8, rows, width), BF),
        ],
        in_specs=spaces,
        out_specs=[anywhere] * 4 + [vmem] + [anywhere] * 8,
        scratch_shapes=[
            pltpu.VMEM((4, 4, 128, 1024), BF),
            pltpu.VMEM((8, 4, 128, 512), BF),
            pltpu.VMEM((4, 2, 512, 128), BF),
            pltpu.VMEM((WINDOWS, 1024, 1024), BF),
            pltpu.VMEM((STAGES, 4, 128, 512), BF),
            pltpu.VMEM((4, 4, 128, 1024), BF),
            pltpu.VMEM((8, 4, 128, 512), BF),
            pltpu.VMEM((8, 5, 128, 1024), BF),
            pltpu.VMEM((4, 128, 1024), BF),
            pltpu.VMEM((8, 128, 512), BF),
            pltpu.VMEM((4, 128, 1024), BF),
            pltpu.VMEM((8, 128, 512), BF),
            pltpu.VMEM((512, 1024), BF),
            pltpu.VMEM((512, 2048), BF),
            pltpu.VMEM((512, 1024), F32),
            pltpu.VMEM((512, 1024), F32),
            pltpu.VMEM((2, 1024, 1024), BF),
            pltpu.VMEM((256, 1024), BF),
            pltpu.VMEM((256, 1024), BF),
            pltpu.VMEM((256, 1024), BF),
            pltpu.VMEM((256, 1024), BF),
            pltpu.VMEM((3, 256, 1024), BF),
            pltpu.VMEM((2, 256, 1024), BF),
            pltpu.VMEM((2, 256, 1024), BF),
            pltpu.VMEM((256, 1024), BF),
            pltpu.VMEM((256, 1024), BF),
            pltpu.VMEM((3, points // 4, width), BF),
            pltpu.VMEM((points // 4, width), BF),
            pltpu.VMEM((6, 16, width), F32),
            pltpu.VMEM((4, 16, width), F32),
            dma((2, 12, 4)),
            dma((2, 16)),
            dma((4, 2)),
            dma((WINDOWS, 2)),
            dma((2, 8, 2)),
            dma((total, 4)),
            dma((total, 5)),
            dma((2, total, 2)),
            dma((2, total, 2)),
            dma((total, 2)),
            dma((2, 2, 2)),
            dma((2, 2, 2)),
            dma((2,)),
            dma((2, 3)),
            dma((2, 3)),
            dma((1,)),
            dma((2, 6)),
            dma((2, 2, 2)),
            dma((2,)),
            dma((1,)),
            dma((1,)),
            dma((5,)),
        ],
        compiler_params=pltpu.CompilerParams(
            collective_id=2, has_side_effects=True, vmem_limit_bytes=62 * 2**20
        ),
        cost_estimate=pl.CostEstimate(
            flops=flops, bytes_accessed=2**27, transcendentals=2**21
        ),
    )(*operands)[:5]


def plain_layers(full, spread, mine, source, valid, cot_own, picks, groups_all):
    proj_c, out_c, in_0, down_0, proj_s, out_s, in_1, down_1 = full
    width, hidden = in_0.shape

    def vector(first, count):
        return spread[:, first : first + count].reshape(-1)

    gains_cross = (vector(0, 1), vector(1, 1))
    gain_self = vector(2, 1)
    gains_mlp = (vector(3, 1), vector(4, 1))
    biases_out = (vector(5, 1), vector(6, 1))
    per_bias = hidden // width
    biases_in = (vector(7, per_bias), vector(7 + per_bias, per_bias))
    cot = cot_own.astype(F32)
    u1, kept_c = attend(mine, source, valid, gains_cross[0], gains_cross[1], proj_c, out_c)
    u2, kept_0 = feed(u1.astype(F32), gains_mlp[0], in_0, biases_in[0], down_0, biases_out[0])
    u2 = u2.astype(F32)
    u3, kept_s = attend(u2, u2, None, gain_self, gain_self, proj_s, out_s)
    u4, kept_1 = feed(u3.astype(F32), gains_mlp[1], in_1, biases_in[1], down_1, biases_out[1])
    final = u4.astype(F32)
    group_norm = jnp.sqrt(jnp.mean(final * final) + EPSILON)
    norm_mean = lax.psum(group_norm, ALL) / groups_all
    g4 = (cot + (norm_mean / group_norm) * final).astype(BF)

    dx, gain_1_grad, bias_1_grad, ob_1_grad, pairs_1 = feed_back(
        g4, kept_1, gains_mlp[1], in_1, down_1
    )
    g3 = (g4.astype(F32) + dx).astype(BF)
    dx, ds, gq, gkv, pairs_s = attend_back(g3, kept_s, gain_self, gain_self, proj_s, out_s)
    gain_s_grad = gq + gkv
    g2 = (g3.astype(F32) + dx + ds).astype(BF)
    dx, gain_0_grad, bias_0_grad, ob_0_grad, pairs_0 = feed_back(
        g2, kept_0, gains_mlp[0], in_0, down_0
    )
    g1 = (g2.astype(F32) + dx).astype(BF)
    dx, ds, cq_grad, ckv_grad, pairs_c = attend_back(
        g1, kept_c, gains_cross[0], gains_cross[1], proj_c, out_c
    )
    g0 = (g1.astype(F32) + dx).astype(BF)
    high = ds.astype(BF)
    low = (ds - high.astype(F32)).astype(BF)
    point_part = (mm_rows(picks, high) + mm_rows(picks, low)).astype(BF)
    small = jnp.concatenate(
        [
            cq_grad,
            ckv_grad,
            gain_s_grad,
            gain_0_grad,
            gain_1_grad,
            ob_0_grad,
            ob_1_grad,
            bias_0_grad,
            bias_1_grad,
            jnp.zeros_like(cq_grad),
        ]
    ).reshape(-1, width)
    pairs = pairs_1 + pairs_s + pairs_0 + pairs_c
    lefts, rights = [pair[0] for pair in pairs], [pair[1] for pair in pairs]
    def settled_grad(left, right):
        part = lax.psum_scatter(
            mm_rows(left, right).astype(BF), ALL, scatter_dimension=0, tiled=True
        )
        return lax.all_gather(part, "section", axis=0, tiled=True).astype(F32)

    done = [settled_grad(left, right) for left, right in pairs]
    mlp_in_grad = jnp.stack([done[6], done[0]])
    mlp_down_grad = jnp.stack([done[7], done[1]])
    proj_s_grad = jnp.concatenate(done[2:5], axis=1)
    proj_c_grad = jnp.concatenate(done[8:11], axis=1)
    out_s_grad, out_c_grad = done[5], done[11]
    points_sum = lax.psum(point_part, "section")
    latents_out = lax.all_gather(u4, "section", axis=0, tiled=True)
    g0_all = lax.all_gather(g0, "section", axis=0, tiled=True)
    small = lax.psum(small, ALL)
    return (
        norm_mean,
        latents_out,
        g0_all,
        points_sum,
        small,
        mlp_in_grad,
        mlp_down_grad,
        proj_c_grad,
        proj_s_grad,
        out_c_grad,
        out_s_grad,
    )


def per_device(
    latents,
    points,
    neighbours,
    lengths,
    cross_proj,
    cross_out,
    cross_gains,
    self_proj,
    self_out,
    self_gain,
    mlp_gain,
    mlp_in,
    mlp_in_bias,
    mlp_down,
    mlp_out_bias,
    cotangent,
):
    sections = lax.axis_size("section")
    section_at = lax.axis_index("section")
    width = latents.shape[1]
    hidden = mlp_in.shape[2]
    groups_dev = neighbours.shape[0]
    rows = latents.shape[0] // sections
    shard = cross_out.shape[0]
    piece = shard // sections
    groups_all = groups_dev * lax.axis_size("batch")

    def gathered(block):
        own = lax.dynamic_slice_in_dim(block, section_at * piece, piece, 0)
        return lax.all_gather(own, ALL, axis=0, tiled=True)

    vectors = jnp.concatenate(
        [
            cross_gains.reshape(-1),
            self_gain,
            mlp_gain.reshape(-1),
            mlp_out_bias.reshape(-1),
            mlp_in_bias.reshape(-1),
            jnp.zeros_like(self_gain),
        ]
    ).reshape(-1, shard)
    projs = (cross_proj.reshape(shard, 3 * width), self_proj.reshape(shard, 3 * width))
    small_slice = lax.axis_size("batch") == 8
    latents_own = lax.dynamic_slice_in_dim(latents, section_at * rows, rows, 0)
    cot_own = lax.dynamic_slice_in_dim(cotangent, section_at * rows, rows, 0)
    mine = latents_own.astype(F32)
    listed = lax.dynamic_index_in_dim(neighbours, section_at, 0, keepdims=False)
    length = lax.dynamic_index_in_dim(lengths, section_at, 0, keepdims=False)
    valid = jnp.arange(listed.shape[0], dtype=jnp.int32) < length
    picks = listed[:, None] == jnp.arange(points.shape[0], dtype=jnp.int32)[None, :]
    picks = picks.astype(BF)
    source = mm(picks, points)
    if small_slice:
        made = gather_forward(
            [projs[0], cross_out, mlp_in, mlp_down, projs[1], self_out],
            vectors,
            latents_own,
            source.astype(BF),
            valid.astype(F32)[None, :],
            cot_own,
        )
        full, gain_rows, norm_tile, made = made[:8], made[8], made[9], made[10:]
        norm_mean = norm_tile[0, 0]
        sums, latents_out, g0_all, points_sum, small = reduce_all(
            full,
            made,
            latents_own,
            source.astype(BF),
            gain_rows,
            valid.astype(F32)[None, :],
            picks.T,
        )
        attn = 2 * hidden
        mlp_in_grad = sums[:, :, :hidden].astype(F32)
        mlp_down_grad = sums[:, :, hidden:attn].astype(F32)
        proj_c_grad, proj_s_grad = [
            sums[layer, :, attn : attn + 3 * width].astype(F32) for layer in range(2)
        ]
        out_c_grad, out_s_grad = [
            sums[layer, :, attn + 3 * width :].astype(F32) for layer in range(2)
        ]
    else:
        blocks = [projs[0], cross_out, mlp_in[0], mlp_down[0]]
        blocks += [projs[1], self_out, mlp_in[1], mlp_down[1]]
        full = [gathered(block) for block in blocks]
        spread = lax.all_gather(vectors, "batch", axis=0, tiled=False)
        (
            norm_mean,
            latents_out,
            g0_all,
            points_sum,
            small,
            mlp_in_grad,
            mlp_down_grad,
            proj_c_grad,
            proj_s_grad,
            out_c_grad,
            out_s_grad,
        ) = plain_layers(full, spread.astype(F32), mine, source, valid, cot_own, picks, groups_all)
    points_grad = points_sum.astype(F32)
    latents_grad = g0_all.astype(F32)
    per_bias = hidden // width
    batch_at = lax.axis_index("batch")

    def own(first, count):
        flat = small[first : first + count].reshape(-1)
        size = flat.shape[0] // lax.axis_size("batch")
        return lax.dynamic_slice_in_dim(flat, batch_at * size, size, 0)

    return (
        latents_out,
        latents_grad,
        points_grad,
        proj_c_grad.reshape(shard, 3, width),
        out_c_grad,
        jnp.stack([own(0, 1), own(1, 1)]),
        proj_s_grad.reshape(shard, 3, width),
        out_s_grad,
        own(2, 1),
        jnp.stack([own(3, 1), own(4, 1)]),
        mlp_in_grad,
        jnp.stack([own(7, per_bias), own(7 + per_bias, per_bias)]),
        mlp_down_grad,
        jnp.stack([own(5, 1), own(6, 1)]),
        norm_mean,
    )


def solution(mesh):
    rows = P("batch", None)
    cols = P(None, "batch")
    block = P("batch", None, None)
    pair = P(None, "batch", None)
    return jax.shard_map(
        per_device,
        mesh=mesh,
        in_specs=(
            rows,
            rows,
            rows,
            P("batch"),
            block,
            rows,
            cols,
            block,
            rows,
            P("batch"),
            cols,
            pair,
            cols,
            pair,
            cols,
            rows,
        ),
        out_specs=(
            rows,
            rows,
            rows,
            block,
            rows,
            cols,
            block,
            rows,
            P("batch"),
            cols,
            pair,
            cols,
            pair,
            cols,
            P(),
        ),
        check_vma=False,
    )
```

```python
import functools
import math

import jax
import jax.numpy as jnp
from jax import lax
from jax.experimental import pallas as pl
from jax.experimental.pallas import tpu as pltpu
from jax.sharding import PartitionSpec as P

HD = 128
EPSILON = 1e-05
MASKED = -1e30
BF = jnp.bfloat16
F32 = jnp.float32
ALL = ("batch", "section")
MESH = pl.DeviceIdType.MESH
GATHER_WIDTH = 1024
AHEAD = 4
SLOTS = 3
GATHERED = tuple(
    (4 * layer + index, start)
    for layer in range(2)
    for index, start in (
        [(0, 0), (0, 1024), (0, 2048), (1, 0)]
        + [(2 + which, chunk) for chunk in range(0, 2048, 1024) for which in range(2)]
    )
)


def mm(a, b):
    return jnp.dot(a, b, preferred_element_type=F32)


def mm_rows(a, b):
    return lax.dot_general(a, b, (((0,), (0,)), ((), ())), preferred_element_type=F32)


def mm_cols(a, b):
    return lax.dot_general(a, b, (((1,), (1,)), ((), ())), preferred_element_type=F32)


def unit_rows(values):
    centred = values - jnp.mean(values, axis=-1, keepdims=True)
    inverse = lax.rsqrt(jnp.mean(centred * centred, axis=-1, keepdims=True) + EPSILON)
    return centred * inverse, inverse


def norm_back(gradient, unit, inverse, gain):
    scaled = gradient * gain
    inner = (
        scaled
        - jnp.mean(scaled, axis=-1, keepdims=True)
        - unit * jnp.mean(scaled * unit, axis=-1, keepdims=True)
    )
    return inverse * inner, jnp.sum(gradient * unit, axis=0)


def heads_of(rows):
    return rows.reshape(rows.shape[0], -1, HD)


def softmax(q, k, valid):
    scores = jnp.einsum(
        "lhc,nhc->hln", heads_of(q), heads_of(k), preferred_element_type=F32
    ) * (1.0 / math.sqrt(HD))
    if valid is not None:
        scores = jnp.where(valid[None, None, :], scores, MASKED)
    grown = jnp.exp(scores - jnp.max(scores, axis=-1, keepdims=True))
    return grown / jnp.sum(grown, axis=-1, keepdims=True)


def attend(inputs, source, valid, gain_q, gain_kv, proj, out):
    unit_x, inv_x = unit_rows(inputs)
    queries_in = (unit_x * gain_q).astype(BF)
    unit_s, inv_s = unit_rows(source)
    keys_in = (unit_s * gain_kv).astype(BF)
    width = inputs.shape[1]
    q = mm(queries_in, proj[:, :width]).astype(BF)
    kv = mm(keys_in, proj[:, width:]).astype(BF)
    k, v = kv[:, :width], kv[:, width:]
    soft = softmax(q, k, valid)
    mixture = jnp.einsum("hln,nhc->lhc", soft.astype(BF), heads_of(v), preferred_element_type=F32)
    mixture = mixture.reshape(inputs.shape).astype(BF)
    result = (inputs + mm(mixture, out)).astype(BF)
    return result, (unit_x, inv_x, queries_in, unit_s, inv_s, keys_in, q, k, v, soft, mixture)


def attend_back(gradient, kept, gain_q, gain_kv, proj, out):
    unit_x, inv_x, queries_in, unit_s, inv_s, keys_in, q, k, v, soft, mixture = kept
    width = gradient.shape[1]
    scale = 1.0 / math.sqrt(HD)
    grad_mix = mm_cols(gradient, out).astype(BF)
    grad_soft = jnp.einsum(
        "lhc,nhc->hln", heads_of(grad_mix), heads_of(v), preferred_element_type=F32
    )
    inner = jnp.sum(soft * grad_soft, axis=-1, keepdims=True)
    grad_scores = (soft * (grad_soft - inner)).astype(BF)
    dq = jnp.einsum("hln,nhc->lhc", grad_scores, heads_of(k), preferred_element_type=F32) * scale
    dk = jnp.einsum("hln,lhc->nhc", grad_scores, heads_of(q), preferred_element_type=F32) * scale
    dv = jnp.einsum(
        "hln,lhc->nhc", soft.astype(BF), heads_of(grad_mix), preferred_element_type=F32
    )
    dq = dq.reshape(gradient.shape).astype(BF)
    dk = dk.reshape(-1, width).astype(BF)
    dv = dv.reshape(-1, width).astype(BF)
    grad_x, gain_q_grad = norm_back(mm_cols(dq, proj[:, :width]), unit_x, inv_x, gain_q)
    back_s = mm_cols(dk, proj[:, width : 2 * width]) + mm_cols(dv, proj[:, 2 * width :])
    grad_s, gain_kv_grad = norm_back(back_s, unit_s, inv_s, gain_kv)
    pairs = ((queries_in, dq), (keys_in, dk), (keys_in, dv), (mixture, gradient))
    return grad_x, grad_s, gain_q_grad, gain_kv_grad, pairs


def feed(inputs, gain, w_in, b_in, w_down, b_out):
    unit, inverse = unit_rows(inputs)
    lowered = (unit * gain).astype(BF)
    pre_act = mm(lowered, w_in) + b_in
    active = jax.nn.gelu(pre_act).astype(BF)
    result = (inputs + mm_cols(active, w_down) + b_out).astype(BF)
    return result, (unit, inverse, lowered, pre_act, active)


def feed_back(gradient, kept, gain, w_in, w_down):
    unit, inverse, lowered, pre_act, active = kept
    grad_act = mm(gradient, w_down)
    grad_pre = jax.vjp(jax.nn.gelu, pre_act)[1](grad_act)[0].astype(BF)
    grad_x, gain_grad = norm_back(mm_cols(grad_pre, w_in), unit, inverse, gain)
    bias_grad = jnp.sum(grad_pre.astype(F32), axis=0)
    out_grad = jnp.sum(gradient.astype(F32), axis=0)
    return grad_x, gain_grad, bias_grad, out_grad, ((lowered, grad_pre), (gradient, active))


def gelu_both(value):
    factor = math.sqrt(2.0 / math.pi)
    square = value * value
    bent = jnp.tanh(factor * value * (1.0 + 0.044715 * square))
    inner = factor * (1.0 + 3.0 * 0.044715 * square)
    half = 0.5 * (1.0 + bent)
    return value * half, half + 0.5 * value * (1.0 - bent * bent) * inner


def tiles(count, body):
    def step(index, carry):
        body(pl.ds(pl.multiple_of(index * 256, 256), 256), index)
        return carry

    lax.fori_loop(0, count, step, 0)


def norm_into(source, gain, target):
    def step(index, carry):
        here = pl.ds(pl.multiple_of(index * 32, 32), 32)
        unit, _ = unit_rows(source[here, :].astype(F32))
        target[here, :] = (unit * gain).astype(BF)
        return carry

    lax.fori_loop(0, source.shape[0] // 32, step, 0)


def gather_kernel(*refs):
    cross_proj, cross_out, mlp_in, mlp_down, self_proj, self_out = refs[:6]
    latents_in, cot_all, points_in, near_in, length_in = refs[6:11]
    vec_parts = refs[11:16]
    section_at = lax.axis_index("section")
    batch_at = lax.axis_index("batch")
    x_at = lax.rem(section_at, 2)
    y_at = section_at // 2
    ins = (
        cross_proj,
        cross_out,
        mlp_in.at[0],
        mlp_down.at[0],
        self_proj,
        self_out,
        mlp_in.at[1],
        mlp_down.at[1],
    )
    count = len(ins)
    outs = refs[16 : 16 + count]
    rest = refs[16 + count :]
    gains, norm_out, mask_in, picks_out = rest[:4]
    kept_outs = rest[4:24]
    (
        u1,
        u2,
        u3,
        u4,
        grad_top,
        xq_c,
        sn_c,
        q_c,
        k_c,
        v_c,
        o_c,
        xn_s,
        q_s,
        k_s,
        v_s,
        o_s,
        src_in,
        lowered,
        before,
        active,
        x_in,
        cot_in,
        vec_in,
        vec_rows,
        slots,
        total_rows,
        part_out,
        part_in,
        vec_out,
        biases,
        plane,
        line_in,
    ) = rest[24:56]
    (own_sem, send, recv, kin_send, kin_recv, vec_sems) = rest[56:62]
    (slot_sems, kept_sems, plane_sems, line_sems, pair_sems, row_sems) = rest[62:]
    line = 4
    core = lax.rem(batch_at, 2)
    spot = batch_at // 2
    beside = section_at + 1 - 2 * x_at
    above = lax.rem(section_at + 2, 4)
    sibling = batch_at + 1 - 2 * core
    shard = ins[0].shape[0]
    place = section_at * 2 + core
    rows = x_in.shape[0]

    def down_line(step):
        return lax.rem(spot + step, line) * 2 + core

    def up_line(step):
        return lax.rem(spot + line - step, line) * 2 + core

    near_peers = []
    for turn in range(1, 8):
        other = lax.rem(place + turn, 8)
        near_peers.append((other // 2, spot * 2 + lax.rem(other, 2)))
    line_peers = [(section_at, down_line(step)) for step in range(1, line)]
    far_peers = [(section_at, down_line(step) + 1 - 2 * core) for step in range(1, line)]
    vec_peers = [(section_at, sibling)] + line_peers + far_peers
    peers = near_peers + line_peers + far_peers
    barrier = pltpu.get_barrier_semaphore()
    for peer in peers:
        pl.semaphore_signal(barrier, inc=1, device_id=peer, device_id_type=MESH)
    pl.semaphore_wait(barrier, len(peers))

    def spread(ref, owner, first, size):
        return ref.at[pl.ds(pl.multiple_of(owner * shard, shard), shard), pl.ds(first, size)]

    def is_feed(item):
        return item % 8 >= 4

    def source_of(item, first, size):
        index, start = GATHERED[item]
        if is_feed(item):
            first = pl.multiple_of(first + y_at * outs[index].shape[1], 128)
        return ins[index].at[:, pl.ds(first, size)]

    def piece(item):
        start = GATHERED[item][1]
        if is_feed(item):
            return pl.multiple_of(start + x_at * 512, 128), 512
        return pl.multiple_of(start + section_at * 256, 128), 256

    def own_line(item, way):
        first, size = piece(item)
        return pltpu.make_async_remote_copy(
            source_of(item, first, size),
            spread(outs[GATHERED[item][0]], batch_at, first, size),
            send.at[5 * way, item, 0],
            recv.at[0, item, 3 if way else 1],
            device_id=(section_at, batch_at + (-2 if way else 2)),
            device_id_type=MESH,
        )

    def onward_line(item, step, way):
        first, size = piece(item)
        ref = spread(outs[GATHERED[item][0]], up_line(step), first, size)
        return pltpu.make_async_remote_copy(
            ref,
            ref,
            send.at[0, item, step],
            recv.at[0, item, step - 1 if way else step + 1],
            device_id=(section_at, batch_at + (-2 if way else 2)),
            device_id_type=MESH,
        )

    def came_line(item, step):
        first, size = piece(item)
        ref = spread(outs[GATHERED[item][0]], up_line(step), first, size)
        return pltpu.make_async_remote_copy(
            ref,
            ref,
            send.at[0, item, step],
            recv.at[0, item, step],
            device_id=(section_at, sibling),
            device_id_type=MESH,
        )

    def start_line(item):
        @pl.when(spot < 3)
        def _():
            own_line(item, 0).start()

        @pl.when(spot > 0)
        def _():
            own_line(item, 1).start()

    def arrive_line(item, apart):
        @pl.when(spot >= apart)
        def _():
            came_line(item, apart).wait_recv()

            @pl.when(spot < 3)
            def _():
                onward_line(item, apart, 0).start()

            for copy in near(item, apart):
                copy.start()

        @pl.when(spot + apart <= 3)
        def _():
            came_line(item, 4 - apart).wait_recv()

            @pl.when(spot > 0)
            def _():
                onward_line(item, 4 - apart, 1).start()

            for copy in near(item, 4 - apart):
                copy.start()

    def sent_line(item):
        @pl.when(spot < 3)
        def _():
            own_line(item, 0).wait_send()

        @pl.when(spot > 0)
        def _():
            own_line(item, 1).wait_send()

        for apart in (1, 2, 3):

            @pl.when(jnp.logical_and(spot >= apart, spot < 3))
            def _():
                onward_line(item, apart, 0).wait_send()

            @pl.when(jnp.logical_and(spot + apart <= 3, spot > 0))
            def _():
                onward_line(item, 4 - apart, 1).wait_send()

        for step in (1, 2, 3):
            for copy in near(item, step):
                copy.wait_send()

    def plane_copy(item, step, way, low, wide, peer):
        ref = spread(outs[GATHERED[item][0]], up_line(step), low, wide)
        return pltpu.make_async_remote_copy(
            ref,
            ref,
            send.at[way, item, step],
            recv.at[way, item, step],
            device_id=(peer, batch_at),
            device_id_type=MESH,
        )

    def near(item, step):
        first, size = piece(item)
        copies = [plane_copy(item, step, 1, first, size, beside)]
        if not is_feed(item):
            copies.append(plane_copy(item, step, 2, first, size, above))
        return copies

    def far(item, step):
        start = GATHERED[item][1]
        by_y = pl.multiple_of(start + beside * 256, 128)
        by_x = pl.multiple_of(start + above * 256 + 128, 128)
        return [
            plane_copy(item, step, 3, by_y, 128, above),
            plane_copy(item, step, 4, by_x, 128, beside),
        ]

    def kin(item, step):
        index, start = GATHERED[item]
        if step == 0:
            source = source_of(item, start, GATHER_WIDTH)
        else:
            source = spread(outs[index], up_line(step), start, GATHER_WIDTH)
        return pltpu.make_async_remote_copy(
            source,
            spread(outs[index], up_line(step), start, GATHER_WIDTH),
            kin_send.at[item, step],
            kin_recv.at[item, step],
            device_id=(section_at, sibling),
            device_id_type=MESH,
        )

    def own(item):
        index, start = GATHERED[item]
        return pltpu.make_async_copy(
            source_of(item, start, GATHER_WIDTH),
            spread(outs[index], batch_at, start, GATHER_WIDTH),
            own_sem.at[item],
        )

    def vec_copy(which):
        return pltpu.make_async_remote_copy(
            vec_in,
            vec_out.at[batch_at],
            vec_sems.at[0, which],
            vec_sems.at[1, which],
            device_id=vec_peers[which],
            device_id_type=MESH,
        )

    def slot_copy(item):
        index, start = GATHERED[item]
        return pltpu.make_async_copy(
            outs[index].at[:, pl.ds(start, GATHER_WIDTH)],
            slots.at[item % SLOTS],
            slot_sems.at[item % SLOTS],
        )

    def near_norm(turn):
        return pltpu.make_async_remote_copy(
            plane.at[8],
            plane.at[place],
            plane_sems.at[0, turn],
            plane_sems.at[1, turn],
            device_id=near_peers[turn],
            device_id_type=MESH,
        )

    def far_norm(step):
        return pltpu.make_async_remote_copy(
            line_in.at[4],
            line_in.at[spot],
            line_sems.at[0, step],
            line_sems.at[1, step],
            device_id=line_peers[step],
            device_id_type=MESH,
        )

    def rows_over(layer):
        return pltpu.make_async_remote_copy(
            lowered.at[layer, pl.ds(0, rows)],
            lowered.at[layer, pl.ds(rows, rows)],
            pair_sems.at[0, layer, 0],
            pair_sems.at[1, layer, 0],
            device_id=(above, batch_at),
            device_id_type=MESH,
        )

    def part_over(layer):
        return pltpu.make_async_remote_copy(
            part_out.at[layer],
            part_in.at[layer],
            pair_sems.at[0, layer, 1],
            pair_sems.at[1, layer, 1],
            device_id=(above, batch_at),
            device_id_type=MESH,
        )

    steps = range(1, line)
    total = len(GATHERED)
    started = []

    def launch(copies):
        for copy in copies:
            copy.start()
        started.extend(copies)

    kept = (
        (u1, u2, u3, u4, grad_top)
        + (xq_c, sn_c, q_c, k_c, v_c, o_c)
        + (xn_s, q_s, k_s, v_s, o_s)
        + (src_in, lowered, before, active)
    )
    names = {id(ref): place for place, ref in enumerate(kept)}

    def keep(*chosen):
        for ref in chosen:
            index = names[id(ref)]
            pltpu.make_async_copy(ref, kept_outs[index], kept_sems.at[index]).start()

    def row(index):
        return gains[index : index + 1, :]

    def project(source, target, slot):
        def tile(columns, _):
            target[:, columns] = mm(source[...], slots[slot, :, columns]).astype(BF)

        tiles(4, tile)

    def heads(q, k, v, o, masked):
        def head(index, carry):
            here = pl.ds(pl.multiple_of(index * HD, HD), HD)
            scores = mm_cols(q[:, here], k[:, here]) * (1.0 / math.sqrt(HD))
            if masked:
                scores = jnp.where(mask_in[...] > 0.0, scores, MASKED)
            grown = jnp.exp(scores - jnp.max(scores, axis=-1, keepdims=True))
            soft = grown / jnp.sum(grown, axis=-1, keepdims=True)
            o[:, here] = mm(soft.astype(BF), v[:, here]).astype(BF)
            return carry

        lax.fori_loop(0, q.shape[1] // HD, head, 0)

    def close_attention(inputs, o, target, slot):
        def tile(columns, _):
            target[:, columns] = (
                inputs[:, columns].astype(F32) + mm(o[...], slots[slot, :, columns])
            ).astype(BF)

        tiles(4, tile)

    def feed_up(layer, chunk, slot):
        def tile(columns, index):
            first = chunk * GATHER_WIDTH + index * 256
            there = pl.ds(pl.multiple_of(first, 256), 256)
            lanes = pl.ds(pl.multiple_of(y_at * 2048 + first, 256), 256)
            value = mm(lowered[layer], slots[slot, :, columns]) + biases[layer : layer + 1, lanes]
            active_part, slope = gelu_both(value)
            before[layer, :, there] = slope
            active[layer, :, there] = active_part.astype(BF)

        tiles(4, tile)

    def feed_down(layer, chunk, slot):
        chosen = pl.ds(chunk * GATHER_WIDTH, GATHER_WIDTH)

        def tile(columns, _):
            value = mm_cols(active[layer, :, chosen], slots[slot, columns, :])
            if chunk == 0:
                total_rows[:, columns] = value
            else:
                value = total_rows[:, columns] + value
                total_rows[:, columns] = value
                part_out[layer, :, columns] = value[rows:].astype(BF)

        tiles(4, tile)

    def feed_close(layer):
        inputs, target = (u1, u3)[layer], (u2, u4)[layer]
        part_over(layer).wait_recv()

        def tile(columns, _):
            target[:, columns] = (
                inputs[:, columns].astype(F32)
                + (total_rows[0:rows, columns] + part_in[layer, :, columns].astype(F32))
                + gains[5 + layer : 6 + layer, columns]
            ).astype(BF)

        tiles(4, tile)
        keep(target)

    def work(item):
        slot_copy(item).wait()
        slot = item % SLOTS
        layer, stage = item // 8, item % 8
        inputs = (x_in, u2)[layer]
        middle = (u1, u3)[layer]
        q, k, v, o = ((q_c, k_c, v_c, o_c), (q_s, k_s, v_s, o_s))[layer]
        if stage == 0:
            if layer == 0:
                norm_into(x_in, row(0), xq_c)
                norm_into(src_in, row(1), sn_c)
                keep(xq_c, sn_c)
            else:
                feed_close(0)
                norm_into(u2, row(2), xn_s)
                keep(xn_s)
            project((xq_c, xn_s)[layer], q, slot)
        elif stage == 1:
            project((sn_c, xn_s)[layer], k, slot)
        elif stage == 2:
            project((sn_c, xn_s)[layer], v, slot)
            heads(q, k, v, o, layer == 0)
            keep(q, k, v, o)
        elif stage == 3:
            close_attention(inputs, o, middle, slot)
            norm_into(middle, row(3 + layer), lowered.at[layer, pl.ds(0, rows)])
            launch([rows_over(layer)])
            keep(middle)
        elif stage % 2 == 0:
            if stage == 4:
                rows_over(layer).wait_recv()
            feed_up(layer, (stage - 4) // 2, slot)
        else:
            feed_down(layer, (stage - 4) // 2, slot)
            if stage == 7:
                launch([part_over(layer)])

    for item in range(AHEAD):
        start_line(item)
    here = pl.ds(pl.multiple_of(section_at * rows, rows), rows)
    row_copies = [
        pltpu.make_async_copy(latents_in.at[here], x_in, row_sems.at[0]),
        pltpu.make_async_copy(cot_all.at[here], cot_in, row_sems.at[1]),
    ]
    for copy in row_copies:
        copy.start()
    cross_gain, self_gain, feed_gain, out_bias, in_bias = vec_parts
    vec_rows[...] = jnp.zeros_like(vec_rows)
    vec_rows[0:2, :] = cross_gain[...].astype(F32)
    vec_rows[2:3, :] = self_gain[...].astype(F32)
    vec_rows[3:5, :] = feed_gain[...].astype(F32)
    vec_rows[5:7, :] = out_bias[...].astype(F32)
    bias_rows = in_bias[...].astype(F32)
    for layer in range(2):
        for part_at in range(4):
            index = 7 + 4 * layer + part_at
            vec_rows[index : index + 1, :] = bias_rows[
                layer : layer + 1, part_at * 128 : part_at * 128 + 128
            ]
    vec_in[...] = vec_rows[...].astype(BF)
    vec_out[batch_at] = vec_in[...]
    for which in range(7):
        vec_copy(which).start()
    lanes = lax.broadcasted_iota(jnp.int32, (1, rows), 1)
    length = length_in[pl.ds(section_at, 1), :]
    mask_in[...] = jnp.where(lanes < length, 1.0, 0.0)
    point_at = lax.broadcasted_iota(jnp.int32, (points_in.shape[0], rows), 0)
    wanted = near_in[pl.ds(section_at, 1), :]
    picks = jnp.where(point_at == wanted, 1.0, 0.0)
    picks_out[...] = picks.astype(BF)
    turned = picks.T.astype(BF)

    def source_tile(columns, _):
        src_in[:, columns] = mm(turned, points_in[:, columns]).astype(BF)

    tiles(4, source_tile)
    keep(src_in)
    for copy in row_copies:
        copy.wait()
    for moment in range(-2, total + 4):
        if moment + 2 + AHEAD < total:
            start_line(moment + 2 + AHEAD)
        for apart in (1, 2, 3):
            if 0 <= moment + 3 - apart < total:
                arrive_line(moment + 3 - apart, apart)
        if 0 <= moment < total:
            own(moment).start()
            launch([kin(moment, 0)])
        if 0 <= moment - 1 < total:
            for step in steps:
                if is_feed(moment - 1):
                    near(moment - 1, step)[0].wait_recv()
                    launch([kin(moment - 1, step)])
                else:
                    for copy, onward in zip(near(moment - 1, step), far(moment - 1, step)):
                        copy.wait_recv()
                        launch([onward])
        if 0 <= moment - 2 < total and not is_feed(moment - 2):
            for step in steps:
                for copy in far(moment - 2, step):
                    copy.wait_recv()
                launch([kin(moment - 2, step)])
        if moment == 2:
            for which in range(7):
                vec_copy(which).wait()
            for owner in range(8):
                values = vec_out[owner].astype(F32)
                gains[:, owner * 128 : owner * 128 + 128] = values
                for layer in range(2):
                    for part_at in range(4):
                        first = owner * 512 + part_at * 128
                        index = 7 + 4 * layer + part_at
                        biases[layer : layer + 1, first : first + 128] = values[index : index + 1]
        if 0 <= moment - 4 < total:
            work(moment - 4)
        if 0 <= moment - 3 < total:
            own(moment - 3).wait()
            for step in range(line):
                kin(moment - 3, step).wait_recv()
            slot_copy(moment - 3).start()
    keep(lowered, before, active)
    feed_close(1)

    def square(index, carry):
        here = pl.ds(pl.multiple_of(index * 32, 32), 32)
        values = u4[here, :].astype(F32)
        return carry + jnp.sum(values * values, axis=0, keepdims=True)

    squares = lax.fori_loop(0, u4.shape[0] // 32, square, jnp.zeros((1, u4.shape[1]), F32))
    mean = jnp.sum(squares, axis=1, keepdims=True) / (u4.shape[0] * u4.shape[1])
    group_norm = jnp.sqrt(mean + EPSILON)
    plane[8] = jnp.broadcast_to(group_norm, plane.shape[1:])
    for turn in range(7):
        near_norm(turn).start()
    plane[place] = plane[8]
    for turn in range(7):
        near_norm(turn).wait()
    line_in[4] = jnp.sum(plane[0:8], axis=0)
    for step in range(3):
        far_norm(step).start()
    line_in[spot] = line_in[4]
    for step in range(3):
        far_norm(step).wait()
    norm_mean = jnp.sum(line_in[0:4], axis=0) / 32.0
    norm_out[...] = norm_mean
    ratio = norm_mean[0:1, 0:1] / group_norm

    def top(index, carry):
        here = pl.ds(pl.multiple_of(index * 32, 32), 32)
        grad_top[here, :] = (
            cot_in[here, :].astype(F32) + ratio * u4[here, :].astype(F32)
        ).astype(BF)
        return carry

    lax.fori_loop(0, u4.shape[0] // 32, top, 0)
    keep(grad_top)
    for index, ref in enumerate(kept):
        pltpu.make_async_copy(ref, kept_outs[index], kept_sems.at[index]).wait()
    for item in range(total):
        sent_line(item)
    for copy in started:
        copy.wait_send()


def gather_forward(blocks, latents, cotangent, points, near, lengths, vectors):
    width = latents.shape[1]
    rows = near.shape[1]
    half = blocks[2].shape[2] // 2
    widths = (3 * width, width, half, half) * 2
    total = len(GATHERED)
    anywhere = pl.BlockSpec(memory_space=pl.ANY)
    vmem = pl.BlockSpec(memory_space=pltpu.VMEM)
    plain = ((rows, width), BF)
    kept = [plain] * 17 + [
        ((2, 2 * rows, width), BF),
        ((2, 2 * rows, half), F32),
        ((2, 2 * rows, half), BF),
    ]
    dma = pltpu.SemaphoreType.DMA
    return pl.pallas_call(
        gather_kernel,
        out_shape=[jax.ShapeDtypeStruct((width, size), BF) for size in widths]
        + [
            jax.ShapeDtypeStruct((16, width), F32),
            jax.ShapeDtypeStruct((8, 128), F32),
            jax.ShapeDtypeStruct((1, rows), F32),
            jax.ShapeDtypeStruct((points.shape[0], rows), BF),
        ]
        + [jax.ShapeDtypeStruct(*one) for one in kept],
        in_specs=[anywhere] * (len(blocks) + 2) + [vmem] * 8,
        out_specs=[anywhere] * len(widths) + [vmem] * 4 + [anywhere] * len(kept),
        scratch_shapes=[pltpu.VMEM(*one) for one in kept]
        + [
            pltpu.VMEM((rows, width), BF),
            pltpu.VMEM((rows, width), BF),
            pltpu.VMEM((16, 128), BF),
            pltpu.VMEM((16, 128), F32),
            pltpu.VMEM((SLOTS, width, GATHER_WIDTH), BF),
            pltpu.VMEM((2 * rows, width), F32),
            pltpu.VMEM((2, rows, width), BF),
            pltpu.VMEM((2, rows, width), BF),
            pltpu.VMEM((8, 16, 128), BF),
            pltpu.VMEM((2, 2 * half), F32),
            pltpu.VMEM((9, 8, 128), F32),
            pltpu.VMEM((5, 8, 128), F32),
            dma((total,)),
            dma((6, total, 4)),
            dma((5, total, 4)),
            dma((total, 4)),
            dma((total, 4)),
            dma((2, 7)),
            dma((SLOTS,)),
            dma((len(kept),)),
            dma((2, 7)),
            dma((2, 3)),
            dma((2, 2, 2)),
            dma((2,)),
        ],
        compiler_params=pltpu.CompilerParams(
            collective_id=1, has_side_effects=True, vmem_limit_bytes=56 * 2**20
        ),
        cost_estimate=pl.CostEstimate(
            flops=2 * rows * width * sum(widths), bytes_accessed=2**27, transcendentals=2**21
        ),
    )(*blocks, latents, cotangent, points, near, lengths, *vectors)


ITEM_COUNT = 16
WINDOWS = 4
STAGES = 3


def reduce_kernel(*refs):
    total = ITEM_COUNT
    (
        proj_c,
        out_c,
        in_0,
        down_0,
        proj_s,
        out_s,
        in_1,
        down_1,
        u1_in,
        u2_in,
        u3_in,
        last_ref,
        top_in,
        xq_c,
        sn_c,
        q_c,
        k_c,
        v_c,
        o_c,
        xn_s,
        q_s,
        k_s,
        v_s,
        o_s,
        lowered,
        before,
        active,
        latents_in,
        src_in,
        gains,
        mask_in,
        picks_in,
    ) = refs[:32]
    (up_out, down_out, proj_out_c, proj_out_s, end_out_c, end_out_s) = refs[32:38]
    (last_out, first_out, point_out, small_out) = refs[38:42]
    (grads_h, kin_lf, kin_la, kin_rf, kin_ra) = refs[42:47]
    (
        lwin_f,
        lwin_a,
        raw,
        rwin,
        stage,
        merged_f,
        merged_a,
        passing,
        lined_f,
        lined_a,
        crossed_f,
        crossed_a,
        pair,
        slope,
        rows_sum,
        hbuf,
        slots,
        qb,
        kb,
        vb,
        dob,
        dqkv,
        part_out,
        part_in,
        grad,
        ub,
        point_in,
        point_sum,
        small_in,
        small_sum,
    ) = refs[47:77]
    (
        kin_l_sems,
        kin_r_sems,
        raw_sems,
        win_sems,
        xy_sems,
        line_send,
        line_recv,
        cross_sems,
        out_sems,
        own_sems,
        lat_sems,
        far_sems,
        lat_own,
        point_sems,
        deal_sems,
        point_own,
        small_sems,
        pair_sems,
        slot_sems,
        h_sem,
        save_sems,
        act_sems,
    ) = refs[77:]
    section_at = lax.axis_index("section")
    batch_at = lax.axis_index("batch")
    core = lax.rem(batch_at, 2)
    spot = batch_at // 2
    x_at = lax.rem(section_at, 2)
    y_at = section_at // 2
    beside = section_at + 1 - 2 * x_at
    above = lax.rem(section_at + 2, 4)
    across = lax.rem(beside + 2, 4)
    sibling = batch_at + 1 - 2 * core
    flat = (beside, above)
    bits = (x_at, y_at)
    rows, width = 256, 1024

    peers = [(beside, batch_at), (above, batch_at), (across, batch_at), (section_at, sibling)]
    peers += [(section_at, lax.rem(spot + step, 4) * 2 + core) for step in (1, 2, 3)]
    barrier = pltpu.get_barrier_semaphore()
    for peer in peers:
        pl.semaphore_signal(barrier, inc=1, device_id=peer, device_id_type=MESH)
    pl.semaphore_wait(barrier, len(peers))

    def remote(source, target, sems, where, peer):
        return pltpu.make_async_remote_copy(
            source,
            target,
            sems.at[(0, *where)],
            sems.at[(1, *where)],
            device_id=peer,
            device_id_type=MESH,
        )

    feed_left = (pair, lowered.at[1], pair, lowered.at[0])
    feed_right = (active.at[1], slope, active.at[0], slope)
    att_left = (o_s, xn_s, xn_s, xn_s, o_c, xq_c, sn_c, sn_c)
    att_right = tuple(
        ref
        for turn in range(2)
        for ref in (grads_h.at[turn], dqkv.at[0], dqkv.at[1], dqkv.at[2])
    )

    def columns(spot_of, parity):
        return pl.ds(pl.multiple_of((2 * spot_of + parity) * 128, 128), 128)

    def kin_lefts(feed, job):
        source, target = (feed_left, kin_lf) if feed else (att_left, kin_la)
        return [
            remote(
                source[job].at[:, columns(part, 1 - core)],
                target.at[job, part],
                kin_l_sems,
                (job if feed else 4 + job, part),
                (section_at, sibling),
            )
            for part in range(4)
        ]

    def kin_right(feed, job, chunk):
        if feed:
            here = pl.ds(chunk * 1024, 1024)
            source, target = feed_right[job].at[:, here], kin_rf.at[job, :, here]
        else:
            source, target = att_right[job], kin_ra.at[job]
        where = (2 * job + chunk if feed else 8 + job,)
        return remote(source, target, kin_r_sems, where, (section_at, sibling))

    def item_of(index):
        turn, inner = index // 8, index % 8
        if inner < 4:
            return True, 2 * turn + inner // 2, inner % 2
        return False, 4 * turn + inner - 4, 0

    def window_copies(index):
        feed, job, chunk = item_of(index)
        slot = index % WINDOWS
        size = 512 if feed else 256
        if feed:
            here = pl.ds(chunk * 1024, 1024)
            sources = (feed_right[job].at[:, here], kin_rf.at[job, :, here])
        else:
            sources = (att_right[job], kin_ra.at[job])
        return [
            pltpu.make_async_copy(
                sources[whose],
                rwin.at[slot, pl.ds(whose * size, size)],
                win_sems.at[slot, whose],
            )
            for whose in range(2)
        ]

    def load(index):
        feed, job, chunk = item_of(index)
        kin_right(feed, job, chunk).wait_recv()
        for copy in window_copies(index):
            copy.start()
        if chunk == 0:
            for copy in kin_lefts(feed, job):
                copy.wait_recv()
            size = 512 if feed else 256
            own_left = (feed_left if feed else att_left)[job]
            kin_left = (kin_lf if feed else kin_la).at[job]
            target = (lwin_f if feed else lwin_a).at[job]
            for part in range(4):
                copies = [
                    pltpu.make_async_copy(
                        own_left.at[:, columns(part, core)],
                        raw.at[part, 0, pl.ds(0, size)],
                        raw_sems.at[part, 0],
                    ),
                    pltpu.make_async_copy(
                        kin_left.at[part], raw.at[part, 1, pl.ds(0, size)], raw_sems.at[part, 1]
                    ),
                ]
                for copy in copies:
                    copy.start()
            for part in range(4):
                for whose, source in enumerate(
                    (own_left.at[:, columns(part, core)], kin_left.at[part])
                ):
                    place = raw.at[part, whose, pl.ds(0, size)]
                    pltpu.make_async_copy(source, place, raw_sems.at[part, whose]).wait()
                    target[part, :, whose * size : whose * size + size] = place[...].T

    def is_feed(item):
        return lax.rem(item, 8) < 4

    def feed_job(item):
        return 2 * (item // 8) + lax.rem(item, 8) // 2

    def att_job(item):
        return 4 * (item // 8) + lax.rem(item, 8) - 4

    def loaded(slot, feed):
        size = 512 if feed else 256
        for whose in range(2):
            source = kin_rf.at[0, :, pl.ds(0, 1024)] if feed else kin_ra.at[0]
            pltpu.make_async_copy(
                source, rwin.at[slot, pl.ds(whose * size, size)], win_sems.at[slot, whose]
            ).wait()

    def by_kind(item, action):
        pl.when(is_feed(item))(functools.partial(action, item, True))
        pl.when(jnp.logical_not(is_feed(item)))(functools.partial(action, item, False))

    def merged_of(item, feed):
        return merged_f.at[lax.rem(item, 4)] if feed else merged_a.at[att_job(item)]

    def passing_of(item, feed, slot):
        ref = passing.at[lax.rem(item, 8), slot]
        return ref if feed else ref.at[:, pl.ds(0, 512)]

    def lined_of(item, feed):
        return lined_f.at[lax.rem(item, 4)] if feed else lined_a.at[att_job(item)]

    def crossed_of(item, feed):
        return crossed_f.at[lax.rem(item, 4)] if feed else crossed_a.at[att_job(item)]

    def products(item, choice, store):
        slot = lax.rem(item, WINDOWS)

        def quarter(index, carry):
            upper, part = index // 2, lax.rem(index, 2)
            here = pl.ds(pl.multiple_of(part * 256, 256), 256)
            bit = choice[0] + part * (choice[1] - choice[0])
            first = pl.multiple_of(part * 512 + bit * 256, 256)
            left = lwin_a[att_job(item), pl.ds(upper * 2, 2)].reshape(256, 512)
            right = rwin[slot, 0:512, pl.ds(first, 256)]
            tile = jnp.dot(left, right, preferred_element_type=F32).reshape(2, 128, 256)
            store(pl.ds(upper * 2, 2), here, tile)
            return carry

        lax.fori_loop(0, 4, quarter, 0)

    def xy_copies(item):
        return [
            remote(
                stage.at[lax.rem(att_job(item), STAGES), :, :, pl.ds(side * 256, 256)],
                merged_a.at[att_job(item), :, :, pl.ds(side * 256, 256)],
                xy_sems,
                (att_job(item), side),
                (flat[side], batch_at),
            )
            for side in range(2)
        ]

    def xy_sent(item):
        for copy in xy_copies(item):
            copy.wait_send()

    def line_copy(item, feed, dest, place, rightward):
        step = 1 if rightward else -1
        slot = 4 if not rightward and place - 1 == dest else dest
        return pltpu.make_async_remote_copy(
            merged_of(item, feed).at[dest],
            passing_of(item, feed, slot),
            line_send.at[item, dest],
            line_recv.at[item, slot],
            device_id=(section_at, batch_at + 2 * step),
            device_id_type=MESH,
        )

    def line_wait(item, feed, slot):
        pltpu.make_async_remote_copy(
            merged_of(item, feed).at[0],
            passing_of(item, feed, slot),
            line_send.at[item, 0],
            line_recv.at[item, slot],
            device_id=(section_at, sibling),
            device_id_type=MESH,
        ).wait_recv()

    def line_sent(item, feed):
        for step in (1, 2, 3):
            dest = lax.rem(spot + step, 4)
            pltpu.make_async_remote_copy(
                merged_of(item, feed).at[dest],
                passing_of(item, feed, 0),
                line_send.at[item, dest],
                line_recv.at[item, 0],
                device_id=(section_at, sibling),
                device_id_type=MESH,
            ).wait_send()

    def outset(item, feed):
        @pl.when(spot == 0)
        def _():
            for dest in (3, 2, 1):
                line_copy(item, feed, dest, 0, True).start()

        @pl.when(spot == 3)
        def _():
            for dest in (0, 1, 2):
                line_copy(item, feed, dest, 3, False).start()

    def drained(item, feed):
        line_sent(item, feed)
        if feed:
            feed_out(item, up_out).wait()
            feed_own(item, up_out).wait()
        else:
            for side in range(2):
                att_out(item, side, end_out_s, 0).wait()
                att_own(item, side, end_out_s, 0).wait()

    def offer(item, feed):
        slot = lax.rem(item, WINDOWS)
        loaded(slot, feed)
        if feed:

            @pl.when(item >= 8)
            def _():
                drained(item - 8, True)

            target = merged_of(item, True)

            def tile(index, carry):
                upper, part = index // 4, lax.rem(index, 4)
                here = pl.ds(pl.multiple_of(part * 256, 256), 256)
                left = lwin_f[feed_job(item), pl.ds(upper * 2, 2)].reshape(256, 1024)
                right = rwin[slot, :, here]
                value = jnp.dot(left, right, preferred_element_type=F32)
                target[pl.ds(upper * 2, 2), :, here] = value.reshape(2, 128, 256).astype(BF)
                return carry

            lax.fori_loop(0, 8, tile, 0)
            outset(item, True)
        else:

            @pl.when(lax.rem(item, 8) >= 4 + STAGES)
            def _():
                xy_sent(item - STAGES)

            @pl.when(jnp.logical_and(item >= 12, lax.rem(item, 8) < 4 + STAGES))
            def _():
                xy_sent(item - STAGES - 4)

            def store(blocks, here, tile):
                stage[lax.rem(att_job(item), STAGES), blocks, :, here] = tile.astype(BF)

            products(item, (1 - x_at, 1 - y_at), store)
            for copy in xy_copies(item):
                copy.start()

    def take(item):
        for copy in xy_copies(item):
            copy.wait_recv()
        target = merged_a.at[att_job(item)]

        def store(blocks, here, tile):
            target[blocks, :, here] = (tile + target[blocks, :, here].astype(F32)).astype(BF)

        products(item, bits, store)
        outset(item, False)

    def first(item):
        pl.when(jnp.logical_not(is_feed(item)))(functools.partial(take, item))

    def relay(item, feed, dest, place, rightward):
        line_wait(item, feed, dest)
        target = merged_of(item, feed)
        arrived = passing_of(item, feed, dest)
        target[dest] = (target[dest].astype(F32) + arrived[...].astype(F32)).astype(BF)
        line_copy(item, feed, dest, place, rightward).start()

    def second_of(item, feed):
        @pl.when(spot == 1)
        def _():
            for dest in (3, 2):
                relay(item, feed, dest, 1, True)

        @pl.when(spot == 2)
        def _():
            for dest in (0, 1):
                relay(item, feed, dest, 2, False)

    def third_of(item, feed):
        @pl.when(spot == 1)
        def _():
            relay(item, feed, 0, 1, False)

        @pl.when(spot == 2)
        def _():
            relay(item, feed, 3, 2, True)

    def second(item):
        by_kind(item, second_of)

    def third(item):
        by_kind(item, third_of)

    def feed_cross(item):
        return remote(
            lined_of(item, True),
            crossed_of(item, True),
            cross_sems,
            (item, 0),
            (beside, batch_at),
        )

    def cross_copy(item, side):
        here = pl.ds(side * 256, 256)
        return remote(
            lined_of(item, False).at[:, here],
            crossed_of(item, False).at[:, here],
            cross_sems,
            (item, side),
            (flat[1 - side], batch_at),
        )

    def layer_of(item):
        return 1 - item // 8

    def feed_place(item, target):
        base = y_at * 2048 + lax.rem(item, 2) * 1024
        return target.at[layer_of(item), :, pl.ds(pl.multiple_of(base, 1024), 1024)]

    def feed_out(item, target):
        return remote(
            lined_of(item, True),
            feed_place(item, target),
            out_sems,
            (item, 0),
            (above, batch_at),
        )

    def feed_own(item, target):
        return pltpu.make_async_copy(
            lined_of(item, True), feed_place(item, target), own_sems.at[item, 0]
        )

    def feed_write(item):
        @pl.when(lax.rem(item, 8) < 2)
        def _():
            feed_out(item, down_out).start()
            feed_own(item, down_out).start()

        @pl.when(lax.rem(item, 8) >= 2)
        def _():
            feed_out(item, up_out).start()
            feed_own(item, up_out).start()

    def att_place(item, side, target, inner):
        base = inner * 1024 + side * 512 + bits[side] * 256
        return target.at[:, pl.ds(pl.multiple_of(base, 256), 256)]

    def att_out(item, side, target, inner):
        return remote(
            lined_of(item, False).at[:, pl.ds(side * 256, 256)],
            att_place(item, side, target, inner),
            out_sems,
            (item, side),
            (flat[side], batch_at),
        )

    def att_own(item, side, target, inner):
        return pltpu.make_async_copy(
            lined_of(item, False).at[:, pl.ds(side * 256, 256)],
            att_place(item, side, target, inner),
            own_sems.at[item, side],
        )

    def att_write(item):
        inner = lax.rem(item, 8) - 5
        for turn, proj, end in ((0, proj_out_s, end_out_s), (1, proj_out_c, end_out_c)):

            @pl.when(jnp.logical_and(item // 8 == turn, inner >= 0))
            def _():
                for side in range(2):
                    att_out(item, side, proj, inner).start()
                    att_own(item, side, proj, inner).start()

            @pl.when(jnp.logical_and(item // 8 == turn, inner < 0))
            def _():
                for side in range(2):
                    att_out(item, side, end, 0).start()
                    att_own(item, side, end, 0).start()

    def close_of(item, feed):
        for place in range(4):

            @pl.when(spot == place)
            def _():
                value = merged_of(item, feed)[place].astype(F32)
                if place > 0:
                    line_wait(item, feed, place)
                    value += passing_of(item, feed, place)[...].astype(F32)
                if place < 3:
                    line_wait(item, feed, 4)
                    value += passing_of(item, feed, 4)[...].astype(F32)
                lined_of(item, feed)[...] = value.astype(BF)

        if feed:
            feed_cross(item).start()
        else:
            for side in range(2):
                cross_copy(item, side).start()

    def close(item):
        by_kind(item, close_of)

    def finish_of(item, feed):
        if feed:
            feed_cross(item).wait()
        else:
            for side in range(2):
                cross_copy(item, side).wait()
        target = lined_of(item, feed)
        target[...] = (
            target[...].astype(F32) + crossed_of(item, feed)[...].astype(F32)
        ).astype(BF)
        if feed:
            feed_write(item)
        else:
            att_write(item)

    def finish(item):
        by_kind(item, finish_of)

    def small_copy(phase):
        if phase == 0:
            peer = (section_at, sibling)
        elif phase < 3:
            peer = (flat[phase - 1], batch_at)
        else:
            peer = (section_at, lax.rem(spot + phase - 2, 4) * 2 + core)
        return remote(
            small_sum.at[min(phase, 3)], small_in.at[phase], small_sems, (phase,), peer
        )

    quarter_rows = pair.shape[0] // 4

    def point_copy(which):
        peer = (beside, above, across)[which]
        return remote(
            pair.at[pl.ds(pl.multiple_of(peer * quarter_rows, 128), quarter_rows)],
            point_in.at[which],
            point_sems,
            (which,),
            (peer, batch_at),
        )

    def point_place():
        return point_out.at[pl.ds(pl.multiple_of(section_at * quarter_rows, 128), quarter_rows)]

    def point_deal(which):
        peer = (beside, above, across)[which]
        return remote(point_sum, point_place(), deal_sems, (which,), (peer, batch_at))

    def point_local():
        return pltpu.make_async_copy(point_sum, point_place(), point_own.at[0])

    pairs = ((last_ref, last_out), (grad, first_out))

    def lat_copy(which, way):
        source, target = pairs[which]
        return remote(
            source,
            target.at[pl.ds(pl.multiple_of(section_at * rows, rows), rows)],
            lat_sems,
            (which, way),
            (flat[way], batch_at),
        )

    def lat_far(which, way):
        target = pairs[which][1]
        low = flat[way] * rows + way * (rows // 2)
        part = target.at[pl.ds(pl.multiple_of(low, rows // 2), rows // 2)]
        return remote(part, part, far_sems, (which, way), (flat[1 - way], batch_at))

    def lat_local(which):
        source, target = pairs[which]
        return pltpu.make_async_copy(
            source,
            target.at[pl.ds(pl.multiple_of(section_at * rows, rows), rows)],
            lat_own.at[which],
        )

    def lat_start(which):
        lat_local(which).start()
        for way in range(2):
            lat_copy(which, way).start()

    def lat_onward(which):
        for way in range(2):
            lat_copy(which, way).wait_recv()
            lat_far(which, way).start()

    loads = []
    for turn, (proj, out, up, down) in enumerate(
        ((proj_s, out_s, in_1, down_1), (proj_c, out_c, in_0, down_0))
    ):
        for chunk in range(2):
            loads += [down.at[:, pl.ds(chunk * 1024, 1024)], up.at[:, pl.ds(chunk * 1024, 1024)]]
        loads.append(out)
        loads += [proj.at[:, pl.ds(which * 1024, 1024)] for which in range(3)]

    def slot_copy(index):
        return pltpu.make_async_copy(loads[index], slots.at[index % 2], slot_sems.at[index % 2])

    def opened(index):
        slot_copy(index).wait()
        return index % 2

    def closed(index):
        if index + 2 < len(loads):
            slot_copy(index + 2).start()

    def h_copy(index):
        layer, chunk = 1 - index // 2, index % 2
        return pltpu.make_async_copy(
            before.at[layer, :, pl.ds(chunk * 1024, 1024)], hbuf, h_sem.at[0]
        )

    def pair_over(turn):
        return remote(
            pair.at[pl.ds(0, rows)],
            pair.at[pl.ds(rows, rows)],
            pair_sems,
            (turn, 0),
            (above, batch_at),
        )

    def part_over(turn):
        return remote(
            part_out.at[turn], part_in.at[turn], pair_sems, (turn, 1), (above, batch_at)
        )

    def grad_saved(turn):
        return pltpu.make_async_copy(grad, grads_h.at[turn], save_sems.at[0])

    def act_copies(turn):
        chosen = ((q_s, k_s, v_s), (q_c, k_c, v_c))[turn]
        return [
            pltpu.make_async_copy(source, target, act_sems.at[index])
            for index, (source, target) in enumerate(zip(chosen, (qb, kb, vb)))
        ]

    def row_copy(index):
        if index == 3:
            source = latents_in.at[pl.ds(pl.multiple_of(section_at * rows, rows), rows)]
        else:
            source = (u3_in, u2_in, u1_in)[index]
        return pltpu.make_async_copy(source, ub, act_sems.at[3])

    def small_row(index, value):
        small_sum[0, index : index + 1, :] = value

    def open_pair(turn):
        pair[0:rows, :] = grad[...]
        pair_over(turn).start()

    def pair_ready(turn):
        pair_over(turn).wait()
        for copy in kin_lefts(True, 2 * turn):
            copy.start()

    def feed_chunk(turn, chunk):
        layer = 1 - turn
        base = 8 * turn + 2 * chunk
        h_copy(2 * turn + chunk).wait()
        if turn == 1:
            kin_right(True, 1, chunk).wait_send()
        slot = opened(base)

        def up_tile(here, index):
            there = pl.ds(pl.multiple_of(chunk * 1024 + index * 256, 256), 256)
            value = mm(pair[...], slots[slot, :, here]) * hbuf[:, here]
            short = value.astype(BF)
            slope[:, there] = short
            column = jnp.sum(short.astype(F32), axis=0, keepdims=True)
            for half in range(2):
                index_at = 7 + 4 * layer + 2 * half + chunk
                small_sum[0, index_at : index_at + 1, here] = jnp.where(
                    y_at == half, column, jnp.zeros_like(column)
                )

        tiles(4, up_tile)
        closed(base)
        if 2 * turn + chunk + 1 < 4:
            h_copy(2 * turn + chunk + 1).start()
        kin_right(True, 2 * turn + 1, chunk).start()
        slot = opened(base + 1)

        def down_tile(there, _):
            value = mm_cols(slope[:, chunk * 1024 : chunk * 1024 + 1024], slots[slot, there, :])
            if chunk == 0:
                rows_sum[:, there] = value
            else:
                value = rows_sum[:, there] + value
                rows_sum[:, there] = value
                part_out[turn, :, there] = value[rows:].astype(BF)

        tiles(4, down_tile)
        closed(base + 1)
        if chunk == 1:
            if turn == 0:
                for copy in kin_lefts(True, 0):
                    copy.wait_send()
            part_over(turn).start()

    def row_steps(body, count):
        zero = jnp.zeros((1, width), F32)

        def step(index, carry):
            here = pl.ds(pl.multiple_of(index * 32, 32), 32)
            return tuple(a + b for a, b in zip(carry, body(here)))

        return lax.fori_loop(0, rows // 32, step, (zero,) * count)

    def lean(back, unit, inverse, gain):
        scaled = back * gain
        inner = (
            scaled
            - jnp.mean(scaled, axis=-1, keepdims=True)
            - unit * jnp.mean(scaled * unit, axis=-1, keepdims=True)
        )
        return inverse * inner, jnp.sum(back * unit, axis=0, keepdims=True)

    def feed_end(turn):
        layer = 1 - turn
        gain = gains[3 + layer : 4 + layer, :]
        part_over(turn).wait_recv()
        row_copy(2 * turn).wait()

        def body(here):
            unit, inverse = unit_rows(ub[here, :].astype(F32))
            back = rows_sum[here, :] + part_in[turn, here, :].astype(F32)
            dx, gain_part = lean(back, unit, inverse, gain)
            old = grad[here, :].astype(F32)
            grad[here, :] = (old + dx).astype(BF)
            return gain_part, jnp.sum(old, axis=0, keepdims=True)

        gain_grad, out_grad = row_steps(body, 2)
        row_copy(2 * turn + 1).start()
        small_row(3 + layer, gain_grad)
        small_row(5 + layer, out_grad)
        grad_saved(turn).start()
        for copy in kin_lefts(False, 4 * turn):
            copy.start()
        slot = opened(8 * turn + 4)

        def tile(there, _):
            dob[:, there] = mm_cols(grad[...], slots[slot, there, :]).astype(BF)

        tiles(4, tile)
        closed(8 * turn + 4)
        grad_saved(turn).wait()
        kin_right(False, 4 * turn, 0).start()

    def attend_heads(turn):
        scale = 1.0 / math.sqrt(HD)
        for copy in act_copies(turn):
            copy.wait()
        if turn == 1:
            for which in range(3):
                kin_right(False, 1 + which, 0).wait_send()

        def head(index, carry):
            here = pl.ds(pl.multiple_of(index * HD, HD), HD)
            q, k, v, do = qb[:, here], kb[:, here], vb[:, here], dob[:, here]
            scores = mm_cols(q, k) * scale
            if turn == 1:
                scores = jnp.where(mask_in[...] > 0.0, scores, MASKED)
            grown = jnp.exp(scores - jnp.max(scores, axis=-1, keepdims=True))
            soft = grown / jnp.sum(grown, axis=-1, keepdims=True)
            back = mm_cols(do, v)
            short = soft * (back - jnp.sum(soft * back, axis=-1, keepdims=True))
            dqkv[0, :, here] = (mm(short.astype(BF), k) * scale).astype(BF)
            dqkv[1, :, here] = (mm(short.T.astype(BF), q) * scale).astype(BF)
            dqkv[2, :, here] = mm(soft.T.astype(BF), do).astype(BF)
            return carry

        lax.fori_loop(0, width // HD, head, 0)
        if turn == 0:
            for copy in act_copies(1):
                copy.start()
        for which in range(3):
            for copy in kin_lefts(False, 4 * turn + 1 + which):
                copy.start()
            kin_right(False, 4 * turn + 1 + which, 0).start()

    def attend_end(turn):
        base = 8 * turn + 5
        for which in range(3):
            slot = opened(base + which)

            def tile(there, _):
                value = mm_cols(dqkv[which], slots[slot, there, :])
                if which == 0:
                    rows_sum[0:rows, there] = value
                elif which == 1:
                    rows_sum[rows : 2 * rows, there] = value
                else:
                    rows_sum[rows : 2 * rows, there] += value

            tiles(4, tile)
            closed(base + which)
        row_copy(2 * turn + 1).wait()
        gain_q = gains[2:3, :] if turn == 0 else gains[0:1, :]
        gain_kv = gains[2:3, :] if turn == 0 else gains[1:2, :]

        def body(here):
            unit, inverse = unit_rows(ub[here, :].astype(F32))
            dx, gain_part = lean(rows_sum[here, :], unit, inverse, gain_q)
            if turn == 1:
                unit, inverse = unit_rows(src_in[here, :].astype(F32))
            there = pl.ds(pl.multiple_of(rows + here.start, 32), 32)
            ds, kv_part = lean(rows_sum[there, :], unit, inverse, gain_kv)
            fresh = grad[here, :].astype(F32) + dx
            if turn == 0:
                fresh += ds
            else:
                high = ds.astype(BF)
                part_out[0, here, :] = high
                part_out[1, here, :] = (ds - high.astype(F32)).astype(BF)
            grad[here, :] = fresh.astype(BF)
            return gain_part, kv_part

        if turn == 1:
            for which in range(2):
                part_over(which).wait_send()
            for copy in kin_lefts(True, 2):
                copy.wait_send()
        gain_grad, kv_grad = row_steps(body, 2)
        if turn == 0:
            row_copy(2).start()
            small_row(2, gain_grad + kv_grad)
            open_pair(1)
        else:
            small_row(0, gain_grad)
            small_row(1, kv_grad)
            small_row(15, jnp.zeros_like(gain_grad))

            def tile(there, _):
                pair[:, there] = (
                    mm(picks_in[...], part_out[0, :, there])
                    + mm(picks_in[...], part_out[1, :, there])
                ).astype(BF)

            tiles(4, tile)
            small_copy(0).start()
            for which in range(3):
                point_copy(which).start()
            lat_start(1)

    def point_total():
        for which in range(3):
            point_copy(which).wait_recv()
        gathered = pair[
            pl.ds(pl.multiple_of(section_at * quarter_rows, 128), quarter_rows)
        ].astype(F32)
        for which in range(3):
            gathered += point_in[which].astype(F32)
        point_sum[...] = gathered.astype(BF)
        point_local().start()
        for which in range(3):
            point_deal(which).start()

    def small_step(phase):
        small_copy(phase).wait_recv()
        small_sum[phase + 1] = small_sum[phase] + small_in[phase]
        if phase < 2:
            small_copy(phase + 1).start()
        else:
            for step in range(3):
                small_copy(3 + step).start()

    def small_end():
        for step in range(3):
            small_copy(3 + step).wait_recv()
        small_out[...] = (small_sum[3] + small_in[4]) + (small_in[3] + small_in[5])

    def rows_end():
        lat_onward(1)
        point_total()

    begin = pltpu.make_async_copy(top_in, grad, act_sems.at[4])
    begin.start()
    for index in range(2):
        slot_copy(index).start()
    h_copy(0).start()
    row_copy(0).start()
    for copy in act_copies(0):
        copy.start()
    begin.wait()
    open_pair(0)
    for turn in range(2):
        for part in range(2):
            kin_right(True, 2 * turn, part).start()
        for copy in kin_lefts(True, 2 * turn + 1):
            copy.start()
    pair_ready(0)
    load(0)
    chain = {
        0: [functools.partial(feed_chunk, 0, 0), functools.partial(lat_start, 0)],
        1: [functools.partial(feed_chunk, 0, 1)],
        2: [functools.partial(feed_end, 0), functools.partial(lat_onward, 0)],
        3: [functools.partial(attend_heads, 0)],
        4: [functools.partial(attend_end, 0)],
        5: [functools.partial(pair_ready, 1), functools.partial(feed_chunk, 1, 0)],
        6: [functools.partial(feed_chunk, 1, 1)],
        7: [functools.partial(feed_end, 1)],
        8: [functools.partial(attend_heads, 1)],
        9: [functools.partial(attend_end, 1)],
        11: [functools.partial(small_step, 0), rows_end],
        13: [functools.partial(small_step, 1)],
        15: [functools.partial(small_step, 2)],
        17: [small_end],
    }

    def moment_body(moment, carry):
        @pl.when(moment < total)
        def _():
            by_kind(moment, offer)

        for lag, action in ((2, first), (3, second), (4, third), (5, close), (6, finish)):
            pl.when(jnp.logical_and(moment >= lag, moment < total + lag))(
                functools.partial(action, moment - lag)
            )
        for when, actions in chain.items():

            @pl.when(moment == when)
            def _():
                for action in actions:
                    action()

        for item in range(1, total):
            pl.when(moment == item - 1)(functools.partial(load, item))
        return carry

    lax.fori_loop(0, total + 6, moment_body, 0)

    for index in range(4):
        if index % 2 == 1:
            for copy in kin_lefts(True, index):
                copy.wait_send()
        if index != 1:
            for chunk in range(2):
                kin_right(True, index, chunk).wait_send()
    for index in range(8):
        for copy in kin_lefts(False, index):
            copy.wait_send()
        if index not in (1, 2, 3):
            kin_right(False, index, 0).wait_send()
    for phase in range(6):
        small_copy(phase).wait_send()
    for which in range(2):
        lat_local(which).wait()
        for way in range(2):
            lat_copy(which, way).wait_send()
            lat_far(which, way).wait()
    point_local().wait()
    for which in range(3):
        point_copy(which).wait_send()
        point_deal(which).wait()

    def drain(item, carry):
        @pl.when(item >= 4)
        def _():
            by_kind(item, drained)

        return carry

    for item in range(total - STAGES, total):
        xy_sent(item)
    lax.fori_loop(0, total, drain, 0)


def reduce_all(full, kept, latents, gains, mask, picks):
    total = ITEM_COUNT
    rows, width = kept[0].shape
    points = picks.shape[0]
    anywhere = pl.BlockSpec(memory_space=pl.ANY)
    vmem = pl.BlockSpec(memory_space=pltpu.VMEM)
    u1, u2, u3, u4, top = kept[:5]
    operands = [*full, u1, u2, u3, u4, top, *kept[5:16], *kept[17:], latents, kept[16]]
    operands += [gains, mask, picks]
    spaces = [anywhere] * (len(operands) - 4) + [vmem] * 4
    dma = pltpu.SemaphoreType.DMA
    flops = 2 * width * width * 24 * rows * 2
    return pl.pallas_call(
        reduce_kernel,
        out_shape=[
            jax.ShapeDtypeStruct((2, 128, 4 * width), BF),
            jax.ShapeDtypeStruct((2, 128, 4 * width), BF),
            jax.ShapeDtypeStruct((128, 3 * width), BF),
            jax.ShapeDtypeStruct((128, 3 * width), BF),
            jax.ShapeDtypeStruct((128, width), BF),
            jax.ShapeDtypeStruct((128, width), BF),
            jax.ShapeDtypeStruct((4 * rows, width), BF),
            jax.ShapeDtypeStruct((4 * rows, width), BF),
            jax.ShapeDtypeStruct((points, width), BF),
            jax.ShapeDtypeStruct((16, width), F32),
            jax.ShapeDtypeStruct((2, rows, width), BF),
            jax.ShapeDtypeStruct((4, 4, 2 * rows, 128), BF),
            jax.ShapeDtypeStruct((8, 4, rows, 128), BF),
            jax.ShapeDtypeStruct((4, 2 * rows, 2 * width), BF),
            jax.ShapeDtypeStruct((8, rows, width), BF),
        ],
        in_specs=spaces,
        out_specs=[anywhere] * 9 + [vmem] + [anywhere] * 5,
        scratch_shapes=[
            pltpu.VMEM((4, 4, 128, 1024), BF),
            pltpu.VMEM((8, 4, 128, 512), BF),
            pltpu.VMEM((4, 2, 512, 128), BF),
            pltpu.VMEM((WINDOWS, 1024, 1024), BF),
            pltpu.VMEM((STAGES, 4, 128, 512), BF),
            pltpu.VMEM((4, 4, 128, 1024), BF),
            pltpu.VMEM((8, 4, 128, 512), BF),
            pltpu.VMEM((8, 5, 128, 1024), BF),
            pltpu.VMEM((4, 128, 1024), BF),
            pltpu.VMEM((8, 128, 512), BF),
            pltpu.VMEM((4, 128, 1024), BF),
            pltpu.VMEM((8, 128, 512), BF),
            pltpu.VMEM((512, 1024), BF),
            pltpu.VMEM((512, 2048), BF),
            pltpu.VMEM((512, 1024), F32),
            pltpu.VMEM((512, 1024), F32),
            pltpu.VMEM((2, 1024, 1024), BF),
            pltpu.VMEM((256, 1024), BF),
            pltpu.VMEM((256, 1024), BF),
            pltpu.VMEM((256, 1024), BF),
            pltpu.VMEM((256, 1024), BF),
            pltpu.VMEM((3, 256, 1024), BF),
            pltpu.VMEM((2, 256, 1024), BF),
            pltpu.VMEM((2, 256, 1024), BF),
            pltpu.VMEM((256, 1024), BF),
            pltpu.VMEM((256, 1024), BF),
            pltpu.VMEM((3, points // 4, width), BF),
            pltpu.VMEM((points // 4, width), BF),
            pltpu.VMEM((6, 16, width), F32),
            pltpu.VMEM((4, 16, width), F32),
            dma((2, 12, 4)),
            dma((2, 16)),
            dma((4, 2)),
            dma((WINDOWS, 2)),
            dma((2, 8, 2)),
            dma((total, 4)),
            dma((total, 5)),
            dma((2, total, 2)),
            dma((2, total, 2)),
            dma((total, 2)),
            dma((2, 2, 2)),
            dma((2, 2, 2)),
            dma((2,)),
            dma((2, 3)),
            dma((2, 3)),
            dma((1,)),
            dma((2, 6)),
            dma((2, 2, 2)),
            dma((2,)),
            dma((1,)),
            dma((1,)),
            dma((5,)),
        ],
        compiler_params=pltpu.CompilerParams(
            collective_id=2, has_side_effects=True, vmem_limit_bytes=62 * 2**20
        ),
        cost_estimate=pl.CostEstimate(
            flops=flops, bytes_accessed=2**27, transcendentals=2**21
        ),
    )(*operands)[:10]


def plain_layers(full, spread, mine, source, valid, cot_own, picks, groups_all):
    proj_c, out_c, in_0, down_0, proj_s, out_s, in_1, down_1 = full
    width, hidden = in_0.shape

    def vector(first, count):
        return spread[:, first : first + count].reshape(-1)

    gains_cross = (vector(0, 1), vector(1, 1))
    gain_self = vector(2, 1)
    gains_mlp = (vector(3, 1), vector(4, 1))
    biases_out = (vector(5, 1), vector(6, 1))
    per_bias = hidden // width
    biases_in = (vector(7, per_bias), vector(7 + per_bias, per_bias))
    cot = cot_own.astype(F32)
    u1, kept_c = attend(mine, source, valid, gains_cross[0], gains_cross[1], proj_c, out_c)
    u2, kept_0 = feed(u1.astype(F32), gains_mlp[0], in_0, biases_in[0], down_0, biases_out[0])
    u2 = u2.astype(F32)
    u3, kept_s = attend(u2, u2, None, gain_self, gain_self, proj_s, out_s)
    u4, kept_1 = feed(u3.astype(F32), gains_mlp[1], in_1, biases_in[1], down_1, biases_out[1])
    final = u4.astype(F32)
    group_norm = jnp.sqrt(jnp.mean(final * final) + EPSILON)
    norm_mean = lax.psum(group_norm, ALL) / groups_all
    g4 = (cot + (norm_mean / group_norm) * final).astype(BF)

    dx, gain_1_grad, bias_1_grad, ob_1_grad, pairs_1 = feed_back(
        g4, kept_1, gains_mlp[1], in_1, down_1
    )
    g3 = (g4.astype(F32) + dx).astype(BF)
    dx, ds, gq, gkv, pairs_s = attend_back(g3, kept_s, gain_self, gain_self, proj_s, out_s)
    gain_s_grad = gq + gkv
    g2 = (g3.astype(F32) + dx + ds).astype(BF)
    dx, gain_0_grad, bias_0_grad, ob_0_grad, pairs_0 = feed_back(
        g2, kept_0, gains_mlp[0], in_0, down_0
    )
    g1 = (g2.astype(F32) + dx).astype(BF)
    dx, ds, cq_grad, ckv_grad, pairs_c = attend_back(
        g1, kept_c, gains_cross[0], gains_cross[1], proj_c, out_c
    )
    g0 = (g1.astype(F32) + dx).astype(BF)
    high = ds.astype(BF)
    low = (ds - high.astype(F32)).astype(BF)
    point_part = (mm_rows(picks, high) + mm_rows(picks, low)).astype(BF)
    small = jnp.concatenate(
        [
            cq_grad,
            ckv_grad,
            gain_s_grad,
            gain_0_grad,
            gain_1_grad,
            ob_0_grad,
            ob_1_grad,
            bias_0_grad,
            bias_1_grad,
            jnp.zeros_like(cq_grad),
        ]
    ).reshape(-1, width)
    pairs = pairs_1 + pairs_s + pairs_0 + pairs_c
    lefts, rights = [pair[0] for pair in pairs], [pair[1] for pair in pairs]
    def settled_grad(left, right):
        part = lax.psum_scatter(
            mm_rows(left, right).astype(BF), ALL, scatter_dimension=0, tiled=True
        )
        return lax.all_gather(part, "section", axis=0, tiled=True).astype(F32)

    done = [settled_grad(left, right) for left, right in pairs]
    mlp_in_grad = jnp.stack([done[6], done[0]])
    mlp_down_grad = jnp.stack([done[7], done[1]])
    proj_s_grad = jnp.concatenate(done[2:5], axis=1)
    proj_c_grad = jnp.concatenate(done[8:11], axis=1)
    out_s_grad, out_c_grad = done[5], done[11]
    points_sum = lax.psum(point_part, "section")
    latents_out = lax.all_gather(u4, "section", axis=0, tiled=True)
    g0_all = lax.all_gather(g0, "section", axis=0, tiled=True)
    small = lax.psum(small, ALL)
    return (
        norm_mean,
        latents_out,
        g0_all,
        points_sum,
        small,
        mlp_in_grad,
        mlp_down_grad,
        proj_c_grad,
        proj_s_grad,
        out_c_grad,
        out_s_grad,
    )


def per_device(
    latents,
    points,
    neighbours,
    lengths,
    cross_proj,
    cross_out,
    cross_gains,
    self_proj,
    self_out,
    self_gain,
    mlp_gain,
    mlp_in,
    mlp_in_bias,
    mlp_down,
    mlp_out_bias,
    cotangent,
):
    sections = lax.axis_size("section")
    section_at = lax.axis_index("section")
    width = latents.shape[1]
    hidden = mlp_in.shape[2]
    groups_dev = neighbours.shape[0]
    rows = latents.shape[0] // sections
    shard = cross_out.shape[0]
    piece = shard // sections
    groups_all = groups_dev * lax.axis_size("batch")

    def gathered(block):
        own = lax.dynamic_slice_in_dim(block, section_at * piece, piece, 0)
        return lax.all_gather(own, ALL, axis=0, tiled=True)

    projs = (cross_proj.reshape(shard, 3 * width), self_proj.reshape(shard, 3 * width))
    if lax.axis_size("batch") == 8:
        made = gather_forward(
            [projs[0], cross_out, mlp_in, mlp_down, projs[1], self_out],
            latents,
            cotangent,
            points,
            neighbours,
            lengths[:, None],
            [cross_gains, self_gain[None, :], mlp_gain, mlp_out_bias, mlp_in_bias],
        )
        full, gain_rows, norm_tile, mask, picks = made[:8], *made[8:12]
        norm_mean = norm_tile[0, 0]
        (
            mlp_in_grad,
            mlp_down_grad,
            proj_c_grad,
            proj_s_grad,
            out_c_grad,
            out_s_grad,
            latents_out,
            g0_all,
            points_sum,
            small,
        ) = reduce_all(full, made[12:], latents, gain_rows, mask, picks)
        mlp_in_grad = mlp_in_grad.astype(F32)
        mlp_down_grad = mlp_down_grad.astype(F32)
        proj_c_grad, proj_s_grad = proj_c_grad.astype(F32), proj_s_grad.astype(F32)
        out_c_grad, out_s_grad = out_c_grad.astype(F32), out_s_grad.astype(F32)
    else:
        vectors = jnp.concatenate(
            [
                cross_gains.reshape(-1),
                self_gain,
                mlp_gain.reshape(-1),
                mlp_out_bias.reshape(-1),
                mlp_in_bias.reshape(-1),
                jnp.zeros_like(self_gain),
            ]
        ).reshape(-1, shard)
        cot_own = lax.dynamic_slice_in_dim(cotangent, section_at * rows, rows, 0)
        mine = lax.dynamic_slice_in_dim(latents, section_at * rows, rows, 0).astype(F32)
        listed = lax.dynamic_index_in_dim(neighbours, section_at, 0, keepdims=False)
        length = lax.dynamic_index_in_dim(lengths, section_at, 0, keepdims=False)
        valid = jnp.arange(listed.shape[0], dtype=jnp.int32) < length
        picks = listed[:, None] == jnp.arange(points.shape[0], dtype=jnp.int32)[None, :]
        picks = picks.astype(BF)
        source = mm(picks, points)
        blocks = [projs[0], cross_out, mlp_in[0], mlp_down[0]]
        blocks += [projs[1], self_out, mlp_in[1], mlp_down[1]]
        full = [gathered(block) for block in blocks]
        spread = lax.all_gather(vectors, "batch", axis=0, tiled=False)
        (
            norm_mean,
            latents_out,
            g0_all,
            points_sum,
            small,
            mlp_in_grad,
            mlp_down_grad,
            proj_c_grad,
            proj_s_grad,
            out_c_grad,
            out_s_grad,
        ) = plain_layers(full, spread.astype(F32), mine, source, valid, cot_own, picks, groups_all)
    points_grad = points_sum.astype(F32)
    latents_grad = g0_all.astype(F32)
    per_bias = hidden // width
    batch_at = lax.axis_index("batch")

    def own(first, count):
        flat = small[first : first + count].reshape(-1)
        size = flat.shape[0] // lax.axis_size("batch")
        return lax.dynamic_slice_in_dim(flat, batch_at * size, size, 0)

    return (
        latents_out,
        latents_grad,
        points_grad,
        proj_c_grad.reshape(shard, 3, width),
        out_c_grad,
        jnp.stack([own(0, 1), own(1, 1)]),
        proj_s_grad.reshape(shard, 3, width),
        out_s_grad,
        own(2, 1),
        jnp.stack([own(3, 1), own(4, 1)]),
        mlp_in_grad,
        jnp.stack([own(7, per_bias), own(7 + per_bias, per_bias)]),
        mlp_down_grad,
        jnp.stack([own(5, 1), own(6, 1)]),
        norm_mean,
    )


def solution(mesh):
    rows = P("batch", None)
    cols = P(None, "batch")
    block = P("batch", None, None)
    pair = P(None, "batch", None)
    return jax.shard_map(
        per_device,
        mesh=mesh,
        in_specs=(
            rows,
            rows,
            rows,
            P("batch"),
            block,
            rows,
            cols,
            block,
            rows,
            P("batch"),
            cols,
            pair,
            cols,
            pair,
            cols,
            rows,
        ),
        out_specs=(
            rows,
            rows,
            rows,
            block,
            rows,
            cols,
            block,
            rows,
            P("batch"),
            cols,
            pair,
            cols,
            pair,
            cols,
            P(),
        ),
        check_vma=False,
    )
```

```python
import functools
import math

import jax
import jax.numpy as jnp
from jax import lax
from jax.experimental import pallas as pl
from jax.experimental.pallas import tpu as pltpu
from jax.sharding import PartitionSpec as P

HD = 128
EPSILON = 1e-05
MASKED = -1e30
BF = jnp.bfloat16
F32 = jnp.float32
ALL = ("batch", "section")
MESH = pl.DeviceIdType.MESH
GATHER_WIDTH = 1024
AHEAD = 4
LOCAL = 1
SLOTS = 3
GATHERED = tuple(
    (4 * layer + index, start)
    for layer in range(2)
    for index, start in (
        [(0, 0), (0, 1024), (0, 2048), (1, 0)]
        + [(2 + which, chunk) for chunk in range(0, 2048, 1024) for which in range(2)]
    )
)


def mm(a, b):
    return jnp.dot(a, b, preferred_element_type=F32)


def mm_rows(a, b):
    return lax.dot_general(a, b, (((0,), (0,)), ((), ())), preferred_element_type=F32)


def mm_cols(a, b):
    return lax.dot_general(a, b, (((1,), (1,)), ((), ())), preferred_element_type=F32)


def unit_rows(values):
    centred = values - jnp.mean(values, axis=-1, keepdims=True)
    inverse = lax.rsqrt(jnp.mean(centred * centred, axis=-1, keepdims=True) + EPSILON)
    return centred * inverse, inverse


def norm_back(gradient, unit, inverse, gain):
    scaled = gradient * gain
    inner = (
        scaled
        - jnp.mean(scaled, axis=-1, keepdims=True)
        - unit * jnp.mean(scaled * unit, axis=-1, keepdims=True)
    )
    return inverse * inner, jnp.sum(gradient * unit, axis=0)


def heads_of(rows):
    return rows.reshape(rows.shape[0], -1, HD)


def softmax(q, k, valid):
    scores = jnp.einsum(
        "lhc,nhc->hln", heads_of(q), heads_of(k), preferred_element_type=F32
    ) * (1.0 / math.sqrt(HD))
    if valid is not None:
        scores = jnp.where(valid[None, None, :], scores, MASKED)
    grown = jnp.exp(scores - jnp.max(scores, axis=-1, keepdims=True))
    return grown / jnp.sum(grown, axis=-1, keepdims=True)


def attend(inputs, source, valid, gain_q, gain_kv, proj, out):
    unit_x, inv_x = unit_rows(inputs)
    queries_in = (unit_x * gain_q).astype(BF)
    unit_s, inv_s = unit_rows(source)
    keys_in = (unit_s * gain_kv).astype(BF)
    width = inputs.shape[1]
    q = mm(queries_in, proj[:, :width]).astype(BF)
    kv = mm(keys_in, proj[:, width:]).astype(BF)
    k, v = kv[:, :width], kv[:, width:]
    soft = softmax(q, k, valid)
    mixture = jnp.einsum("hln,nhc->lhc", soft.astype(BF), heads_of(v), preferred_element_type=F32)
    mixture = mixture.reshape(inputs.shape).astype(BF)
    result = (inputs + mm(mixture, out)).astype(BF)
    return result, (unit_x, inv_x, queries_in, unit_s, inv_s, keys_in, q, k, v, soft, mixture)


def attend_back(gradient, kept, gain_q, gain_kv, proj, out):
    unit_x, inv_x, queries_in, unit_s, inv_s, keys_in, q, k, v, soft, mixture = kept
    width = gradient.shape[1]
    scale = 1.0 / math.sqrt(HD)
    grad_mix = mm_cols(gradient, out).astype(BF)
    grad_soft = jnp.einsum(
        "lhc,nhc->hln", heads_of(grad_mix), heads_of(v), preferred_element_type=F32
    )
    inner = jnp.sum(soft * grad_soft, axis=-1, keepdims=True)
    grad_scores = (soft * (grad_soft - inner)).astype(BF)
    dq = jnp.einsum("hln,nhc->lhc", grad_scores, heads_of(k), preferred_element_type=F32) * scale
    dk = jnp.einsum("hln,lhc->nhc", grad_scores, heads_of(q), preferred_element_type=F32) * scale
    dv = jnp.einsum(
        "hln,lhc->nhc", soft.astype(BF), heads_of(grad_mix), preferred_element_type=F32
    )
    dq = dq.reshape(gradient.shape).astype(BF)
    dk = dk.reshape(-1, width).astype(BF)
    dv = dv.reshape(-1, width).astype(BF)
    grad_x, gain_q_grad = norm_back(mm_cols(dq, proj[:, :width]), unit_x, inv_x, gain_q)
    back_s = mm_cols(dk, proj[:, width : 2 * width]) + mm_cols(dv, proj[:, 2 * width :])
    grad_s, gain_kv_grad = norm_back(back_s, unit_s, inv_s, gain_kv)
    pairs = ((queries_in, dq), (keys_in, dk), (keys_in, dv), (mixture, gradient))
    return grad_x, grad_s, gain_q_grad, gain_kv_grad, pairs


def feed(inputs, gain, w_in, b_in, w_down, b_out):
    unit, inverse = unit_rows(inputs)
    lowered = (unit * gain).astype(BF)
    pre_act = mm(lowered, w_in) + b_in
    active = jax.nn.gelu(pre_act).astype(BF)
    result = (inputs + mm_cols(active, w_down) + b_out).astype(BF)
    return result, (unit, inverse, lowered, pre_act, active)


def feed_back(gradient, kept, gain, w_in, w_down):
    unit, inverse, lowered, pre_act, active = kept
    grad_act = mm(gradient, w_down)
    grad_pre = jax.vjp(jax.nn.gelu, pre_act)[1](grad_act)[0].astype(BF)
    grad_x, gain_grad = norm_back(mm_cols(grad_pre, w_in), unit, inverse, gain)
    bias_grad = jnp.sum(grad_pre.astype(F32), axis=0)
    out_grad = jnp.sum(gradient.astype(F32), axis=0)
    return grad_x, gain_grad, bias_grad, out_grad, ((lowered, grad_pre), (gradient, active))


def gelu_both(value):
    factor = math.sqrt(2.0 / math.pi)
    square = value * value
    bent = jnp.tanh(factor * value * (1.0 + 0.044715 * square))
    inner = factor * (1.0 + 3.0 * 0.044715 * square)
    half = 0.5 * (1.0 + bent)
    return value * half, half + 0.5 * value * (1.0 - bent * bent) * inner


def tiles(count, body):
    def step(index, carry):
        body(pl.ds(pl.multiple_of(index * 256, 256), 256), index)
        return carry

    lax.fori_loop(0, count, step, 0)


def norm_into(source, gain, target):
    def step(index, carry):
        here = pl.ds(pl.multiple_of(index * 32, 32), 32)
        unit, _ = unit_rows(source[here, :].astype(F32))
        target[here, :] = (unit * gain).astype(BF)
        return carry

    lax.fori_loop(0, source.shape[0] // 32, step, 0)


def gather_kernel(*refs):
    cross_proj, cross_out, mlp_in, mlp_down, self_proj, self_out = refs[:6]
    latents_in, cot_all, points_in, near_in, length_in = refs[6:11]
    vec_parts = refs[11:16]
    section_at = lax.axis_index("section")
    batch_at = lax.axis_index("batch")
    x_at = lax.rem(section_at, 2)
    y_at = section_at // 2
    ins = (
        cross_proj,
        cross_out,
        mlp_in.at[0],
        mlp_down.at[0],
        self_proj,
        self_out,
        mlp_in.at[1],
        mlp_down.at[1],
    )
    count = len(ins)
    outs = refs[16 : 16 + count]
    rest = refs[16 + count :]
    gains, norm_out, mask_in, picks_out = rest[:4]
    kept_outs = rest[4:24]
    (
        u1,
        u2,
        u3,
        u4,
        grad_top,
        xq_c,
        sn_c,
        q_c,
        k_c,
        v_c,
        o_c,
        xn_s,
        q_s,
        k_s,
        v_s,
        o_s,
        src_in,
        lowered,
        before,
        active,
        x_in,
        cot_in,
        vec_in,
        vec_rows,
        slots,
        total_rows,
        part_out,
        part_in,
        vec_out,
        biases,
        plane,
        line_in,
    ) = rest[24:56]
    (own_sem, send, recv, kin_send, kin_recv, vec_sems) = rest[56:62]
    (slot_sems, kept_sems, plane_sems, line_sems, pair_sems, row_sems) = rest[62:]
    line = 4
    core = lax.rem(batch_at, 2)
    spot = batch_at // 2
    beside = section_at + 1 - 2 * x_at
    above = lax.rem(section_at + 2, 4)
    sibling = batch_at + 1 - 2 * core
    shard = ins[0].shape[0]
    place = section_at * 2 + core
    rows = x_in.shape[0]

    def down_line(step):
        return lax.rem(spot + step, line) * 2 + core

    def up_line(step):
        return lax.rem(spot + line - step, line) * 2 + core

    near_peers = []
    for turn in range(1, 8):
        other = lax.rem(place + turn, 8)
        near_peers.append((other // 2, spot * 2 + lax.rem(other, 2)))
    line_peers = [(section_at, down_line(step)) for step in range(1, line)]
    far_peers = [(section_at, down_line(step) + 1 - 2 * core) for step in range(1, line)]
    vec_peers = [(section_at, sibling)] + line_peers + far_peers
    peers = near_peers + line_peers + far_peers
    barrier = pltpu.get_barrier_semaphore()
    for peer in peers:
        pl.semaphore_signal(barrier, inc=1, device_id=peer, device_id_type=MESH)
    pl.semaphore_wait(barrier, len(peers))

    def spread(ref, owner, first, size):
        return ref.at[pl.ds(pl.multiple_of(owner * shard, shard), shard), pl.ds(first, size)]

    def is_feed(item):
        return item % 8 >= 4

    def source_of(item, first, size):
        index, start = GATHERED[item]
        if is_feed(item):
            first = pl.multiple_of(first + y_at * outs[index].shape[1], 128)
        return ins[index].at[:, pl.ds(first, size)]

    def piece(item):
        start = GATHERED[item][1]
        if is_feed(item):
            return pl.multiple_of(start + x_at * 512, 128), 512
        return pl.multiple_of(start + section_at * 256, 128), 256

    def own_line(item, way):
        first, size = piece(item)
        return pltpu.make_async_remote_copy(
            source_of(item, first, size),
            spread(outs[GATHERED[item][0]], batch_at, first, size),
            send.at[5 * way, item, 0],
            recv.at[0, item, 3 if way else 1],
            device_id=(section_at, batch_at + (-2 if way else 2)),
            device_id_type=MESH,
        )

    def onward_line(item, step, way):
        first, size = piece(item)
        ref = spread(outs[GATHERED[item][0]], up_line(step), first, size)
        return pltpu.make_async_remote_copy(
            ref,
            ref,
            send.at[0, item, step],
            recv.at[0, item, step - 1 if way else step + 1],
            device_id=(section_at, batch_at + (-2 if way else 2)),
            device_id_type=MESH,
        )

    def came_line(item, step):
        first, size = piece(item)
        ref = spread(outs[GATHERED[item][0]], up_line(step), first, size)
        return pltpu.make_async_remote_copy(
            ref,
            ref,
            send.at[0, item, step],
            recv.at[0, item, step],
            device_id=(section_at, sibling),
            device_id_type=MESH,
        )

    def start_line(item):
        @pl.when(spot < 3)
        def _():
            own_line(item, 0).start()

        @pl.when(spot > 0)
        def _():
            own_line(item, 1).start()

    def arrive_line(item, apart):
        @pl.when(spot >= apart)
        def _():
            came_line(item, apart).wait_recv()

            @pl.when(spot < 3)
            def _():
                onward_line(item, apart, 0).start()

            for copy in near(item, apart):
                copy.start()

        @pl.when(spot + apart <= 3)
        def _():
            came_line(item, 4 - apart).wait_recv()

            @pl.when(spot > 0)
            def _():
                onward_line(item, 4 - apart, 1).start()

            for copy in near(item, 4 - apart):
                copy.start()

    def sent_line(item):
        @pl.when(spot < 3)
        def _():
            own_line(item, 0).wait_send()

        @pl.when(spot > 0)
        def _():
            own_line(item, 1).wait_send()

        for apart in (1, 2, 3):

            @pl.when(jnp.logical_and(spot >= apart, spot < 3))
            def _():
                onward_line(item, apart, 0).wait_send()

            @pl.when(jnp.logical_and(spot + apart <= 3, spot > 0))
            def _():
                onward_line(item, 4 - apart, 1).wait_send()

        for step in (1, 2, 3):
            for copy in near(item, step):
                copy.wait_send()

    def plane_copy(item, step, way, low, wide, peer):
        ref = spread(outs[GATHERED[item][0]], up_line(step), low, wide)
        return pltpu.make_async_remote_copy(
            ref,
            ref,
            send.at[way, item, step],
            recv.at[way, item, step],
            device_id=(peer, batch_at),
            device_id_type=MESH,
        )

    def near(item, step):
        first, size = piece(item)
        copies = [plane_copy(item, step, 1, first, size, beside)]
        if not is_feed(item):
            copies.append(plane_copy(item, step, 2, first, size, above))
        return copies

    def far(item, step):
        start = GATHERED[item][1]
        by_y = pl.multiple_of(start + beside * 256, 128)
        by_x = pl.multiple_of(start + above * 256 + 128, 128)
        return [
            plane_copy(item, step, 3, by_y, 128, above),
            plane_copy(item, step, 4, by_x, 128, beside),
        ]

    def kin(item, step):
        index, start = GATHERED[item]
        if step == 0:
            source = source_of(item, start, GATHER_WIDTH)
        else:
            source = spread(outs[index], up_line(step), start, GATHER_WIDTH)
        return pltpu.make_async_remote_copy(
            source,
            spread(outs[index], up_line(step), start, GATHER_WIDTH),
            kin_send.at[item, step],
            kin_recv.at[item, step],
            device_id=(section_at, sibling),
            device_id_type=MESH,
        )

    def own(item):
        index, start = GATHERED[item]
        return pltpu.make_async_copy(
            source_of(item, start, GATHER_WIDTH),
            spread(outs[index], batch_at, start, GATHER_WIDTH),
            own_sem.at[item],
        )

    def vec_copy(which):
        return pltpu.make_async_remote_copy(
            vec_in,
            vec_out.at[batch_at],
            vec_sems.at[0, which],
            vec_sems.at[1, which],
            device_id=vec_peers[which],
            device_id_type=MESH,
        )

    def slot_copy(item):
        index, start = GATHERED[item]
        return pltpu.make_async_copy(
            outs[index].at[:, pl.ds(start, GATHER_WIDTH)],
            slots.at[item % SLOTS],
            slot_sems.at[item % SLOTS],
        )

    def near_norm(turn):
        return pltpu.make_async_remote_copy(
            plane.at[8],
            plane.at[place],
            plane_sems.at[0, turn],
            plane_sems.at[1, turn],
            device_id=near_peers[turn],
            device_id_type=MESH,
        )

    def far_norm(step):
        return pltpu.make_async_remote_copy(
            line_in.at[4],
            line_in.at[spot],
            line_sems.at[0, step],
            line_sems.at[1, step],
            device_id=line_peers[step],
            device_id_type=MESH,
        )

    def rows_over(layer):
        return pltpu.make_async_remote_copy(
            lowered.at[layer, pl.ds(0, rows)],
            lowered.at[layer, pl.ds(rows, rows)],
            pair_sems.at[0, layer, 0],
            pair_sems.at[1, layer, 0],
            device_id=(above, batch_at),
            device_id_type=MESH,
        )

    def part_over(layer):
        return pltpu.make_async_remote_copy(
            part_out.at[layer],
            part_in.at[layer],
            pair_sems.at[0, layer, 1],
            pair_sems.at[1, layer, 1],
            device_id=(above, batch_at),
            device_id_type=MESH,
        )

    steps = range(1, line)
    total = len(GATHERED)
    started = []

    def launch(copies):
        for copy in copies:
            copy.start()
        started.extend(copies)

    kept = (
        (u1, u2, u3, u4, grad_top)
        + (xq_c, sn_c, q_c, k_c, v_c, o_c)
        + (xn_s, q_s, k_s, v_s, o_s)
        + (src_in, lowered, before, active)
    )
    names = {id(ref): place for place, ref in enumerate(kept)}

    def keep(*chosen):
        for ref in chosen:
            index = names[id(ref)]
            pltpu.make_async_copy(ref, kept_outs[index], kept_sems.at[index]).start(priority=LOCAL)

    def row(index):
        return gains[index : index + 1, :]

    def project(source, target, slot):
        def tile(columns, _):
            target[:, columns] = mm(source[...], slots[slot, :, columns]).astype(BF)

        tiles(4, tile)

    def heads(q, k, v, o, masked):
        def head(index, carry):
            here = pl.ds(pl.multiple_of(index * HD, HD), HD)
            scores = mm_cols(q[:, here], k[:, here]) * (1.0 / math.sqrt(HD))
            if masked:
                scores = jnp.where(mask_in[...] > 0.0, scores, MASKED)
            grown = jnp.exp(scores - jnp.max(scores, axis=-1, keepdims=True))
            soft = grown / jnp.sum(grown, axis=-1, keepdims=True)
            o[:, here] = mm(soft.astype(BF), v[:, here]).astype(BF)
            return carry

        lax.fori_loop(0, q.shape[1] // HD, head, 0)

    def close_attention(inputs, o, target, slot):
        def tile(columns, _):
            target[:, columns] = (
                inputs[:, columns].astype(F32) + mm(o[...], slots[slot, :, columns])
            ).astype(BF)

        tiles(4, tile)

    def feed_up(layer, chunk, slot):
        def tile(columns, index):
            first = chunk * GATHER_WIDTH + index * 256
            there = pl.ds(pl.multiple_of(first, 256), 256)
            lanes = pl.ds(pl.multiple_of(y_at * 2048 + first, 256), 256)
            value = mm(lowered[layer], slots[slot, :, columns]) + biases[layer : layer + 1, lanes]
            active_part, slope = gelu_both(value)
            before[layer, :, there] = slope
            active[layer, :, there] = active_part.astype(BF)

        tiles(4, tile)

    def feed_down(layer, chunk, slot):
        chosen = pl.ds(chunk * GATHER_WIDTH, GATHER_WIDTH)

        def tile(columns, _):
            value = mm_cols(active[layer, :, chosen], slots[slot, columns, :])
            if chunk == 0:
                total_rows[:, columns] = value
            else:
                value = total_rows[:, columns] + value
                total_rows[:, columns] = value
                part_out[layer, :, columns] = value[rows:].astype(BF)

        tiles(4, tile)

    def feed_close(layer):
        inputs, target = (u1, u3)[layer], (u2, u4)[layer]
        part_over(layer).wait_recv()

        def tile(columns, _):
            target[:, columns] = (
                inputs[:, columns].astype(F32)
                + (total_rows[0:rows, columns] + part_in[layer, :, columns].astype(F32))
                + gains[5 + layer : 6 + layer, columns]
            ).astype(BF)

        tiles(4, tile)
        keep(target)

    def work(item):
        slot_copy(item).wait()
        slot = item % SLOTS
        layer, stage = item // 8, item % 8
        inputs = (x_in, u2)[layer]
        middle = (u1, u3)[layer]
        q, k, v, o = ((q_c, k_c, v_c, o_c), (q_s, k_s, v_s, o_s))[layer]
        if stage == 0:
            if layer == 0:
                norm_into(x_in, row(0), xq_c)
                norm_into(src_in, row(1), sn_c)
                keep(xq_c, sn_c)
            else:
                feed_close(0)
                norm_into(u2, row(2), xn_s)
                keep(xn_s)
            project((xq_c, xn_s)[layer], q, slot)
        elif stage == 1:
            project((sn_c, xn_s)[layer], k, slot)
        elif stage == 2:
            project((sn_c, xn_s)[layer], v, slot)
            heads(q, k, v, o, layer == 0)
            keep(q, k, v, o)
        elif stage == 3:
            close_attention(inputs, o, middle, slot)
            norm_into(middle, row(3 + layer), lowered.at[layer, pl.ds(0, rows)])
            launch([rows_over(layer)])
            keep(middle)
        elif stage % 2 == 0:
            if stage == 4:
                rows_over(layer).wait_recv()
            feed_up(layer, (stage - 4) // 2, slot)
        else:
            feed_down(layer, (stage - 4) // 2, slot)
            if stage == 7:
                launch([part_over(layer)])

    for item in range(AHEAD):
        start_line(item)
    here = pl.ds(pl.multiple_of(section_at * rows, rows), rows)
    row_copies = [
        pltpu.make_async_copy(latents_in.at[here], x_in, row_sems.at[0]),
        pltpu.make_async_copy(cot_all.at[here], cot_in, row_sems.at[1]),
    ]
    for copy in row_copies:
        copy.start()
    cross_gain, self_gain, feed_gain, out_bias, in_bias = vec_parts
    vec_rows[...] = jnp.zeros_like(vec_rows)
    vec_rows[0:2, :] = cross_gain[...].astype(F32)
    vec_rows[2:3, :] = self_gain[...].astype(F32)
    vec_rows[3:5, :] = feed_gain[...].astype(F32)
    vec_rows[5:7, :] = out_bias[...].astype(F32)
    bias_rows = in_bias[...].astype(F32)
    for layer in range(2):
        for part_at in range(4):
            index = 7 + 4 * layer + part_at
            vec_rows[index : index + 1, :] = bias_rows[
                layer : layer + 1, part_at * 128 : part_at * 128 + 128
            ]
    vec_in[...] = vec_rows[...].astype(BF)
    vec_out[batch_at] = vec_in[...]
    for which in range(7):
        vec_copy(which).start()
    lanes = lax.broadcasted_iota(jnp.int32, (1, rows), 1)
    length = length_in[pl.ds(section_at, 1), :]
    mask_in[...] = jnp.where(lanes < length, 1.0, 0.0)
    point_at = lax.broadcasted_iota(jnp.int32, (points_in.shape[0], rows), 0)
    wanted = near_in[pl.ds(section_at, 1), :]
    picks = jnp.where(point_at == wanted, 1.0, 0.0)
    picks_out[...] = picks.astype(BF)
    turned = picks.T.astype(BF)

    def source_tile(columns, _):
        src_in[:, columns] = mm(turned, points_in[:, columns]).astype(BF)

    tiles(4, source_tile)
    keep(src_in)
    for copy in row_copies:
        copy.wait()
    for moment in range(-2, total + 4):
        if moment + 2 + AHEAD < total:
            start_line(moment + 2 + AHEAD)
        for apart in (1, 2, 3):
            if 0 <= moment + 3 - apart < total:
                arrive_line(moment + 3 - apart, apart)
        if 0 <= moment < total:
            own(moment).start(priority=LOCAL)
            launch([kin(moment, 0)])
        if 0 <= moment - 1 < total:
            for step in steps:
                if is_feed(moment - 1):
                    near(moment - 1, step)[0].wait_recv()
                    launch([kin(moment - 1, step)])
                else:
                    for copy, onward in zip(near(moment - 1, step), far(moment - 1, step)):
                        copy.wait_recv()
                        launch([onward])
        if 0 <= moment - 2 < total and not is_feed(moment - 2):
            for step in steps:
                for copy in far(moment - 2, step):
                    copy.wait_recv()
                launch([kin(moment - 2, step)])
        if moment == 2:
            for which in range(7):
                vec_copy(which).wait()
            for owner in range(8):
                values = vec_out[owner].astype(F32)
                gains[:, owner * 128 : owner * 128 + 128] = values
                for layer in range(2):
                    for part_at in range(4):
                        first = owner * 512 + part_at * 128
                        index = 7 + 4 * layer + part_at
                        biases[layer : layer + 1, first : first + 128] = values[index : index + 1]
        if 0 <= moment - 4 < total:
            work(moment - 4)
        if 0 <= moment - 3 < total:
            own(moment - 3).wait()
            for step in range(line):
                kin(moment - 3, step).wait_recv()
            slot_copy(moment - 3).start(priority=LOCAL)
    keep(lowered, before, active)
    feed_close(1)

    def square(index, carry):
        here = pl.ds(pl.multiple_of(index * 32, 32), 32)
        values = u4[here, :].astype(F32)
        return carry + jnp.sum(values * values, axis=0, keepdims=True)

    squares = lax.fori_loop(0, u4.shape[0] // 32, square, jnp.zeros((1, u4.shape[1]), F32))
    mean = jnp.sum(squares, axis=1, keepdims=True) / (u4.shape[0] * u4.shape[1])
    group_norm = jnp.sqrt(mean + EPSILON)
    plane[8] = jnp.broadcast_to(group_norm, plane.shape[1:])
    for turn in range(7):
        near_norm(turn).start()
    plane[place] = plane[8]
    for turn in range(7):
        near_norm(turn).wait()
    line_in[4] = jnp.sum(plane[0:8], axis=0)
    for step in range(3):
        far_norm(step).start()
    line_in[spot] = line_in[4]
    for step in range(3):
        far_norm(step).wait()
    norm_mean = jnp.sum(line_in[0:4], axis=0) / 32.0
    norm_out[...] = norm_mean
    ratio = norm_mean[0:1, 0:1] / group_norm

    def top(index, carry):
        here = pl.ds(pl.multiple_of(index * 32, 32), 32)
        grad_top[here, :] = (
            cot_in[here, :].astype(F32) + ratio * u4[here, :].astype(F32)
        ).astype(BF)
        return carry

    lax.fori_loop(0, u4.shape[0] // 32, top, 0)
    keep(grad_top)
    for index, ref in enumerate(kept):
        pltpu.make_async_copy(ref, kept_outs[index], kept_sems.at[index]).wait()
    for item in range(total):
        sent_line(item)
    for copy in started:
        copy.wait_send()


def gather_forward(blocks, latents, cotangent, points, near, lengths, vectors):
    width = latents.shape[1]
    rows = near.shape[1]
    half = blocks[2].shape[2] // 2
    widths = (3 * width, width, half, half) * 2
    total = len(GATHERED)
    anywhere = pl.BlockSpec(memory_space=pl.ANY)
    vmem = pl.BlockSpec(memory_space=pltpu.VMEM)
    plain = ((rows, width), BF)
    kept = [plain] * 17 + [
        ((2, 2 * rows, width), BF),
        ((2, 2 * rows, half), F32),
        ((2, 2 * rows, half), BF),
    ]
    dma = pltpu.SemaphoreType.DMA
    return pl.pallas_call(
        gather_kernel,
        out_shape=[jax.ShapeDtypeStruct((width, size), BF) for size in widths]
        + [
            jax.ShapeDtypeStruct((16, width), F32),
            jax.ShapeDtypeStruct((8, 128), F32),
            jax.ShapeDtypeStruct((1, rows), F32),
            jax.ShapeDtypeStruct((points.shape[0], rows), BF),
        ]
        + [jax.ShapeDtypeStruct(*one) for one in kept],
        in_specs=[anywhere] * (len(blocks) + 2) + [vmem] * 8,
        out_specs=[anywhere] * len(widths) + [vmem] * 4 + [anywhere] * len(kept),
        scratch_shapes=[pltpu.VMEM(*one) for one in kept]
        + [
            pltpu.VMEM((rows, width), BF),
            pltpu.VMEM((rows, width), BF),
            pltpu.VMEM((16, 128), BF),
            pltpu.VMEM((16, 128), F32),
            pltpu.VMEM((SLOTS, width, GATHER_WIDTH), BF),
            pltpu.VMEM((2 * rows, width), F32),
            pltpu.VMEM((2, rows, width), BF),
            pltpu.VMEM((2, rows, width), BF),
            pltpu.VMEM((8, 16, 128), BF),
            pltpu.VMEM((2, 2 * half), F32),
            pltpu.VMEM((9, 8, 128), F32),
            pltpu.VMEM((5, 8, 128), F32),
            dma((total,)),
            dma((6, total, 4)),
            dma((5, total, 4)),
            dma((total, 4)),
            dma((total, 4)),
            dma((2, 7)),
            dma((SLOTS,)),
            dma((len(kept),)),
            dma((2, 7)),
            dma((2, 3)),
            dma((2, 2, 2)),
            dma((2,)),
        ],
        compiler_params=pltpu.CompilerParams(
            collective_id=1, has_side_effects=True, vmem_limit_bytes=56 * 2**20
        ),
        cost_estimate=pl.CostEstimate(
            flops=2 * rows * width * sum(widths), bytes_accessed=2**27, transcendentals=2**21
        ),
    )(*blocks, latents, cotangent, points, near, lengths, *vectors)


ITEM_COUNT = 16
WINDOWS = 4
STAGES = 3


def reduce_kernel(*refs):
    total = ITEM_COUNT
    (
        proj_c,
        out_c,
        in_0,
        down_0,
        proj_s,
        out_s,
        in_1,
        down_1,
        u1_in,
        u2_in,
        u3_in,
        last_ref,
        top_in,
        xq_c,
        sn_c,
        q_c,
        k_c,
        v_c,
        o_c,
        xn_s,
        q_s,
        k_s,
        v_s,
        o_s,
        lowered,
        before,
        active,
        latents_in,
        src_in,
        gains,
        mask_in,
        picks_in,
    ) = refs[:32]
    (up_out, down_out, proj_out_c, proj_out_s, end_out_c, end_out_s) = refs[32:38]
    (last_out, first_out, point_out, small_out) = refs[38:42]
    (grads_h, kin_lf, kin_la, kin_rf, kin_ra) = refs[42:47]
    (
        lwin_f,
        lwin_a,
        raw,
        rwin,
        stage,
        merged_f,
        merged_a,
        passing,
        lined_f,
        lined_a,
        crossed_f,
        crossed_a,
        pair,
        slope,
        rows_sum,
        hbuf,
        slots,
        qb,
        kb,
        vb,
        dob,
        dqkv,
        part_out,
        part_in,
        grad,
        ub,
        point_in,
        point_sum,
        small_in,
        small_sum,
    ) = refs[47:77]
    (
        kin_l_sems,
        kin_r_sems,
        raw_sems,
        win_sems,
        xy_sems,
        line_send,
        line_recv,
        cross_sems,
        out_sems,
        own_sems,
        lat_sems,
        far_sems,
        lat_own,
        point_sems,
        deal_sems,
        point_own,
        small_sems,
        pair_sems,
        slot_sems,
        h_sem,
        save_sems,
        act_sems,
    ) = refs[77:]
    section_at = lax.axis_index("section")
    batch_at = lax.axis_index("batch")
    core = lax.rem(batch_at, 2)
    spot = batch_at // 2
    x_at = lax.rem(section_at, 2)
    y_at = section_at // 2
    beside = section_at + 1 - 2 * x_at
    above = lax.rem(section_at + 2, 4)
    across = lax.rem(beside + 2, 4)
    sibling = batch_at + 1 - 2 * core
    flat = (beside, above)
    bits = (x_at, y_at)
    rows, width = 256, 1024

    peers = [(beside, batch_at), (above, batch_at), (across, batch_at), (section_at, sibling)]
    peers += [(section_at, lax.rem(spot + step, 4) * 2 + core) for step in (1, 2, 3)]
    barrier = pltpu.get_barrier_semaphore()
    for peer in peers:
        pl.semaphore_signal(barrier, inc=1, device_id=peer, device_id_type=MESH)
    pl.semaphore_wait(barrier, len(peers))

    def remote(source, target, sems, where, peer):
        return pltpu.make_async_remote_copy(
            source,
            target,
            sems.at[(0, *where)],
            sems.at[(1, *where)],
            device_id=peer,
            device_id_type=MESH,
        )

    feed_left = (pair, lowered.at[1], pair, lowered.at[0])
    feed_right = (active.at[1], slope, active.at[0], slope)
    att_left = (o_s, xn_s, xn_s, xn_s, o_c, xq_c, sn_c, sn_c)
    att_right = tuple(
        ref
        for turn in range(2)
        for ref in (grads_h.at[turn], dqkv.at[0], dqkv.at[1], dqkv.at[2])
    )

    def columns(spot_of, parity):
        return pl.ds(pl.multiple_of((2 * spot_of + parity) * 128, 128), 128)

    def kin_lefts(feed, job):
        source, target = (feed_left, kin_lf) if feed else (att_left, kin_la)
        return [
            remote(
                source[job].at[:, columns(part, 1 - core)],
                target.at[job, part],
                kin_l_sems,
                (job if feed else 4 + job, part),
                (section_at, sibling),
            )
            for part in range(4)
        ]

    def kin_right(feed, job, chunk):
        if feed:
            here = pl.ds(chunk * 1024, 1024)
            source, target = feed_right[job].at[:, here], kin_rf.at[job, :, here]
        else:
            source, target = att_right[job], kin_ra.at[job]
        where = (2 * job + chunk if feed else 8 + job,)
        return remote(source, target, kin_r_sems, where, (section_at, sibling))

    def item_of(index):
        turn, inner = index // 8, index % 8
        if inner < 4:
            return True, 2 * turn + inner // 2, inner % 2
        return False, 4 * turn + inner - 4, 0

    def window_copies(index):
        feed, job, chunk = item_of(index)
        slot = index % WINDOWS
        size = 512 if feed else 256
        if feed:
            here = pl.ds(chunk * 1024, 1024)
            sources = (feed_right[job].at[:, here], kin_rf.at[job, :, here])
        else:
            sources = (att_right[job], kin_ra.at[job])
        return [
            pltpu.make_async_copy(
                sources[whose],
                rwin.at[slot, pl.ds(whose * size, size)],
                win_sems.at[slot, whose],
            )
            for whose in range(2)
        ]

    def load(index):
        feed, job, chunk = item_of(index)
        kin_right(feed, job, chunk).wait_recv()
        for copy in window_copies(index):
            copy.start(priority=LOCAL)
        if chunk == 0:
            for copy in kin_lefts(feed, job):
                copy.wait_recv()
            size = 512 if feed else 256
            own_left = (feed_left if feed else att_left)[job]
            kin_left = (kin_lf if feed else kin_la).at[job]
            target = (lwin_f if feed else lwin_a).at[job]
            for part in range(4):
                copies = [
                    pltpu.make_async_copy(
                        own_left.at[:, columns(part, core)],
                        raw.at[part, 0, pl.ds(0, size)],
                        raw_sems.at[part, 0],
                    ),
                    pltpu.make_async_copy(
                        kin_left.at[part], raw.at[part, 1, pl.ds(0, size)], raw_sems.at[part, 1]
                    ),
                ]
                for copy in copies:
                    copy.start(priority=LOCAL)
            for part in range(4):
                for whose, source in enumerate(
                    (own_left.at[:, columns(part, core)], kin_left.at[part])
                ):
                    place = raw.at[part, whose, pl.ds(0, size)]
                    pltpu.make_async_copy(source, place, raw_sems.at[part, whose]).wait()
                    target[part, :, whose * size : whose * size + size] = place[...].T

    def is_feed(item):
        return lax.rem(item, 8) < 4

    def feed_job(item):
        return 2 * (item // 8) + lax.rem(item, 8) // 2

    def att_job(item):
        return 4 * (item // 8) + lax.rem(item, 8) - 4

    def loaded(slot, feed):
        size = 512 if feed else 256
        for whose in range(2):
            source = kin_rf.at[0, :, pl.ds(0, 1024)] if feed else kin_ra.at[0]
            pltpu.make_async_copy(
                source, rwin.at[slot, pl.ds(whose * size, size)], win_sems.at[slot, whose]
            ).wait()

    def by_kind(item, action):
        pl.when(is_feed(item))(functools.partial(action, item, True))
        pl.when(jnp.logical_not(is_feed(item)))(functools.partial(action, item, False))

    def merged_of(item, feed):
        return merged_f.at[lax.rem(item, 4)] if feed else merged_a.at[att_job(item)]

    def passing_of(item, feed, slot):
        ref = passing.at[lax.rem(item, 8), slot]
        return ref if feed else ref.at[:, pl.ds(0, 512)]

    def lined_of(item, feed):
        return lined_f.at[lax.rem(item, 4)] if feed else lined_a.at[att_job(item)]

    def crossed_of(item, feed):
        return crossed_f.at[lax.rem(item, 4)] if feed else crossed_a.at[att_job(item)]

    def products(item, choice, store):
        slot = lax.rem(item, WINDOWS)

        def quarter(index, carry):
            upper, part = index // 2, lax.rem(index, 2)
            here = pl.ds(pl.multiple_of(part * 256, 256), 256)
            bit = choice[0] + part * (choice[1] - choice[0])
            first = pl.multiple_of(part * 512 + bit * 256, 256)
            left = lwin_a[att_job(item), pl.ds(upper * 2, 2)].reshape(256, 512)
            right = rwin[slot, 0:512, pl.ds(first, 256)]
            tile = jnp.dot(left, right, preferred_element_type=F32).reshape(2, 128, 256)
            store(pl.ds(upper * 2, 2), here, tile)
            return carry

        lax.fori_loop(0, 4, quarter, 0)

    def xy_copies(item):
        return [
            remote(
                stage.at[lax.rem(att_job(item), STAGES), :, :, pl.ds(side * 256, 256)],
                merged_a.at[att_job(item), :, :, pl.ds(side * 256, 256)],
                xy_sems,
                (att_job(item), side),
                (flat[side], batch_at),
            )
            for side in range(2)
        ]

    def xy_sent(item):
        for copy in xy_copies(item):
            copy.wait_send()

    def line_copy(item, feed, dest, place, rightward):
        step = 1 if rightward else -1
        slot = 4 if not rightward and place - 1 == dest else dest
        return pltpu.make_async_remote_copy(
            merged_of(item, feed).at[dest],
            passing_of(item, feed, slot),
            line_send.at[item, dest],
            line_recv.at[item, slot],
            device_id=(section_at, batch_at + 2 * step),
            device_id_type=MESH,
        )

    def line_wait(item, feed, slot):
        pltpu.make_async_remote_copy(
            merged_of(item, feed).at[0],
            passing_of(item, feed, slot),
            line_send.at[item, 0],
            line_recv.at[item, slot],
            device_id=(section_at, sibling),
            device_id_type=MESH,
        ).wait_recv()

    def line_sent(item, feed):
        for step in (1, 2, 3):
            dest = lax.rem(spot + step, 4)
            pltpu.make_async_remote_copy(
                merged_of(item, feed).at[dest],
                passing_of(item, feed, 0),
                line_send.at[item, dest],
                line_recv.at[item, 0],
                device_id=(section_at, sibling),
                device_id_type=MESH,
            ).wait_send()

    def outset(item, feed):
        @pl.when(spot == 0)
        def _():
            for dest in (3, 2, 1):
                line_copy(item, feed, dest, 0, True).start()

        @pl.when(spot == 3)
        def _():
            for dest in (0, 1, 2):
                line_copy(item, feed, dest, 3, False).start()

    def drained(item, feed):
        line_sent(item, feed)
        if feed:
            feed_out(item, up_out).wait()
            feed_own(item, up_out).wait()
        else:
            for side in range(2):
                att_out(item, side, end_out_s, 0).wait()
                att_own(item, side, end_out_s, 0).wait()

    def offer(item, feed):
        slot = lax.rem(item, WINDOWS)
        loaded(slot, feed)
        if feed:

            @pl.when(item >= 8)
            def _():
                drained(item - 8, True)

            target = merged_of(item, True)

            def tile(index, carry):
                upper, part = index // 4, lax.rem(index, 4)
                here = pl.ds(pl.multiple_of(part * 256, 256), 256)
                left = lwin_f[feed_job(item), pl.ds(upper * 2, 2)].reshape(256, 1024)
                right = rwin[slot, :, here]
                value = jnp.dot(left, right, preferred_element_type=F32)
                target[pl.ds(upper * 2, 2), :, here] = value.reshape(2, 128, 256).astype(BF)
                return carry

            lax.fori_loop(0, 8, tile, 0)
            outset(item, True)
        else:

            @pl.when(lax.rem(item, 8) >= 4 + STAGES)
            def _():
                xy_sent(item - STAGES)

            @pl.when(jnp.logical_and(item >= 12, lax.rem(item, 8) < 4 + STAGES))
            def _():
                xy_sent(item - STAGES - 4)

            def store(blocks, here, tile):
                stage[lax.rem(att_job(item), STAGES), blocks, :, here] = tile.astype(BF)

            products(item, (1 - x_at, 1 - y_at), store)
            for copy in xy_copies(item):
                copy.start()

    def take(item):
        for copy in xy_copies(item):
            copy.wait_recv()
        target = merged_a.at[att_job(item)]

        def store(blocks, here, tile):
            target[blocks, :, here] = (tile + target[blocks, :, here].astype(F32)).astype(BF)

        products(item, bits, store)
        outset(item, False)

    def first(item):
        pl.when(jnp.logical_not(is_feed(item)))(functools.partial(take, item))

    def relay(item, feed, dest, place, rightward):
        line_wait(item, feed, dest)
        target = merged_of(item, feed)
        arrived = passing_of(item, feed, dest)
        target[dest] = (target[dest].astype(F32) + arrived[...].astype(F32)).astype(BF)
        line_copy(item, feed, dest, place, rightward).start()

    def second_of(item, feed):
        @pl.when(spot == 1)
        def _():
            for dest in (3, 2):
                relay(item, feed, dest, 1, True)

        @pl.when(spot == 2)
        def _():
            for dest in (0, 1):
                relay(item, feed, dest, 2, False)

    def third_of(item, feed):
        @pl.when(spot == 1)
        def _():
            relay(item, feed, 0, 1, False)

        @pl.when(spot == 2)
        def _():
            relay(item, feed, 3, 2, True)

    def second(item):
        by_kind(item, second_of)

    def third(item):
        by_kind(item, third_of)

    def feed_cross(item):
        return remote(
            lined_of(item, True),
            crossed_of(item, True),
            cross_sems,
            (item, 0),
            (beside, batch_at),
        )

    def cross_copy(item, side):
        here = pl.ds(side * 256, 256)
        return remote(
            lined_of(item, False).at[:, here],
            crossed_of(item, False).at[:, here],
            cross_sems,
            (item, side),
            (flat[1 - side], batch_at),
        )

    def layer_of(item):
        return 1 - item // 8

    def feed_place(item, target):
        base = y_at * 2048 + lax.rem(item, 2) * 1024
        return target.at[layer_of(item), :, pl.ds(pl.multiple_of(base, 1024), 1024)]

    def feed_out(item, target):
        return remote(
            lined_of(item, True),
            feed_place(item, target),
            out_sems,
            (item, 0),
            (above, batch_at),
        )

    def feed_own(item, target):
        return pltpu.make_async_copy(
            lined_of(item, True), feed_place(item, target), own_sems.at[item, 0]
        )

    def feed_write(item):
        @pl.when(lax.rem(item, 8) < 2)
        def _():
            feed_out(item, down_out).start()
            feed_own(item, down_out).start(priority=LOCAL)

        @pl.when(lax.rem(item, 8) >= 2)
        def _():
            feed_out(item, up_out).start()
            feed_own(item, up_out).start(priority=LOCAL)

    def att_place(item, side, target, inner):
        base = inner * 1024 + side * 512 + bits[side] * 256
        return target.at[:, pl.ds(pl.multiple_of(base, 256), 256)]

    def att_out(item, side, target, inner):
        return remote(
            lined_of(item, False).at[:, pl.ds(side * 256, 256)],
            att_place(item, side, target, inner),
            out_sems,
            (item, side),
            (flat[side], batch_at),
        )

    def att_own(item, side, target, inner):
        return pltpu.make_async_copy(
            lined_of(item, False).at[:, pl.ds(side * 256, 256)],
            att_place(item, side, target, inner),
            own_sems.at[item, side],
        )

    def att_write(item):
        inner = lax.rem(item, 8) - 5
        for turn, proj, end in ((0, proj_out_s, end_out_s), (1, proj_out_c, end_out_c)):

            @pl.when(jnp.logical_and(item // 8 == turn, inner >= 0))
            def _():
                for side in range(2):
                    att_out(item, side, proj, inner).start()
                    att_own(item, side, proj, inner).start(priority=LOCAL)

            @pl.when(jnp.logical_and(item // 8 == turn, inner < 0))
            def _():
                for side in range(2):
                    att_out(item, side, end, 0).start()
                    att_own(item, side, end, 0).start(priority=LOCAL)

    def close_of(item, feed):
        for place in range(4):

            @pl.when(spot == place)
            def _():
                value = merged_of(item, feed)[place].astype(F32)
                if place > 0:
                    line_wait(item, feed, place)
                    value += passing_of(item, feed, place)[...].astype(F32)
                if place < 3:
                    line_wait(item, feed, 4)
                    value += passing_of(item, feed, 4)[...].astype(F32)
                lined_of(item, feed)[...] = value.astype(BF)

        if feed:
            feed_cross(item).start()
        else:
            for side in range(2):
                cross_copy(item, side).start()

    def close(item):
        by_kind(item, close_of)

    def finish_of(item, feed):
        if feed:
            feed_cross(item).wait()
        else:
            for side in range(2):
                cross_copy(item, side).wait()
        target = lined_of(item, feed)
        target[...] = (
            target[...].astype(F32) + crossed_of(item, feed)[...].astype(F32)
        ).astype(BF)
        if feed:
            feed_write(item)
        else:
            att_write(item)

    def finish(item):
        by_kind(item, finish_of)

    def small_copy(phase):
        if phase == 0:
            peer = (section_at, sibling)
        elif phase < 3:
            peer = (flat[phase - 1], batch_at)
        else:
            peer = (section_at, lax.rem(spot + phase - 2, 4) * 2 + core)
        return remote(
            small_sum.at[min(phase, 3)], small_in.at[phase], small_sems, (phase,), peer
        )

    quarter_rows = pair.shape[0] // 4

    def point_copy(which):
        peer = (beside, above, across)[which]
        return remote(
            pair.at[pl.ds(pl.multiple_of(peer * quarter_rows, 128), quarter_rows)],
            point_in.at[which],
            point_sems,
            (which,),
            (peer, batch_at),
        )

    def point_place():
        return point_out.at[pl.ds(pl.multiple_of(section_at * quarter_rows, 128), quarter_rows)]

    def point_deal(which):
        peer = (beside, above, across)[which]
        return remote(point_sum, point_place(), deal_sems, (which,), (peer, batch_at))

    def point_local():
        return pltpu.make_async_copy(point_sum, point_place(), point_own.at[0])

    pairs = ((last_ref, last_out), (grad, first_out))

    def lat_copy(which, way):
        source, target = pairs[which]
        return remote(
            source,
            target.at[pl.ds(pl.multiple_of(section_at * rows, rows), rows)],
            lat_sems,
            (which, way),
            (flat[way], batch_at),
        )

    def lat_far(which, way):
        target = pairs[which][1]
        low = flat[way] * rows + way * (rows // 2)
        part = target.at[pl.ds(pl.multiple_of(low, rows // 2), rows // 2)]
        return remote(part, part, far_sems, (which, way), (flat[1 - way], batch_at))

    def lat_local(which):
        source, target = pairs[which]
        return pltpu.make_async_copy(
            source,
            target.at[pl.ds(pl.multiple_of(section_at * rows, rows), rows)],
            lat_own.at[which],
        )

    def lat_start(which):
        lat_local(which).start(priority=LOCAL)
        for way in range(2):
            lat_copy(which, way).start()

    def lat_onward(which):
        for way in range(2):
            lat_copy(which, way).wait_recv()
            lat_far(which, way).start()

    loads = []
    for turn, (proj, out, up, down) in enumerate(
        ((proj_s, out_s, in_1, down_1), (proj_c, out_c, in_0, down_0))
    ):
        for chunk in range(2):
            loads += [down.at[:, pl.ds(chunk * 1024, 1024)], up.at[:, pl.ds(chunk * 1024, 1024)]]
        loads.append(out)
        loads += [proj.at[:, pl.ds(which * 1024, 1024)] for which in range(3)]

    def slot_copy(index):
        return pltpu.make_async_copy(loads[index], slots.at[index % 2], slot_sems.at[index % 2])

    def opened(index):
        slot_copy(index).wait()
        return index % 2

    def closed(index):
        if index + 2 < len(loads):
            slot_copy(index + 2).start(priority=LOCAL)

    def h_copy(index):
        layer, chunk = 1 - index // 2, index % 2
        return pltpu.make_async_copy(
            before.at[layer, :, pl.ds(chunk * 1024, 1024)], hbuf, h_sem.at[0]
        )

    def pair_over(turn):
        return remote(
            pair.at[pl.ds(0, rows)],
            pair.at[pl.ds(rows, rows)],
            pair_sems,
            (turn, 0),
            (above, batch_at),
        )

    def part_over(turn):
        return remote(
            part_out.at[turn], part_in.at[turn], pair_sems, (turn, 1), (above, batch_at)
        )

    def grad_saved(turn):
        return pltpu.make_async_copy(grad, grads_h.at[turn], save_sems.at[0])

    def act_copies(turn):
        chosen = ((q_s, k_s, v_s), (q_c, k_c, v_c))[turn]
        return [
            pltpu.make_async_copy(source, target, act_sems.at[index])
            for index, (source, target) in enumerate(zip(chosen, (qb, kb, vb)))
        ]

    def row_copy(index):
        if index == 3:
            source = latents_in.at[pl.ds(pl.multiple_of(section_at * rows, rows), rows)]
        else:
            source = (u3_in, u2_in, u1_in)[index]
        return pltpu.make_async_copy(source, ub, act_sems.at[3])

    def small_row(index, value):
        small_sum[0, index : index + 1, :] = value

    def open_pair(turn):
        pair[0:rows, :] = grad[...]
        pair_over(turn).start()

    def pair_ready(turn):
        pair_over(turn).wait()
        for copy in kin_lefts(True, 2 * turn):
            copy.start()

    def feed_chunk(turn, chunk):
        layer = 1 - turn
        base = 8 * turn + 2 * chunk
        h_copy(2 * turn + chunk).wait()
        if turn == 1:
            kin_right(True, 1, chunk).wait_send()
        slot = opened(base)

        def up_tile(here, index):
            there = pl.ds(pl.multiple_of(chunk * 1024 + index * 256, 256), 256)
            value = mm(pair[...], slots[slot, :, here]) * hbuf[:, here]
            short = value.astype(BF)
            slope[:, there] = short
            column = jnp.sum(short.astype(F32), axis=0, keepdims=True)
            for half in range(2):
                index_at = 7 + 4 * layer + 2 * half + chunk
                small_sum[0, index_at : index_at + 1, here] = jnp.where(
                    y_at == half, column, jnp.zeros_like(column)
                )

        tiles(4, up_tile)
        closed(base)
        if 2 * turn + chunk + 1 < 4:
            h_copy(2 * turn + chunk + 1).start(priority=LOCAL)
        kin_right(True, 2 * turn + 1, chunk).start()
        slot = opened(base + 1)

        def down_tile(there, _):
            value = mm_cols(slope[:, chunk * 1024 : chunk * 1024 + 1024], slots[slot, there, :])
            if chunk == 0:
                rows_sum[:, there] = value
            else:
                value = rows_sum[:, there] + value
                rows_sum[:, there] = value
                part_out[turn, :, there] = value[rows:].astype(BF)

        tiles(4, down_tile)
        closed(base + 1)
        if chunk == 1:
            if turn == 0:
                for copy in kin_lefts(True, 0):
                    copy.wait_send()
            part_over(turn).start()

    def row_steps(body, count):
        zero = jnp.zeros((1, width), F32)

        def step(index, carry):
            here = pl.ds(pl.multiple_of(index * 32, 32), 32)
            return tuple(a + b for a, b in zip(carry, body(here)))

        return lax.fori_loop(0, rows // 32, step, (zero,) * count)

    def lean(back, unit, inverse, gain):
        scaled = back * gain
        inner = (
            scaled
            - jnp.mean(scaled, axis=-1, keepdims=True)
            - unit * jnp.mean(scaled * unit, axis=-1, keepdims=True)
        )
        return inverse * inner, jnp.sum(back * unit, axis=0, keepdims=True)

    def feed_end(turn):
        layer = 1 - turn
        gain = gains[3 + layer : 4 + layer, :]
        part_over(turn).wait_recv()
        row_copy(2 * turn).wait()

        def body(here):
            unit, inverse = unit_rows(ub[here, :].astype(F32))
            back = rows_sum[here, :] + part_in[turn, here, :].astype(F32)
            dx, gain_part = lean(back, unit, inverse, gain)
            old = grad[here, :].astype(F32)
            grad[here, :] = (old + dx).astype(BF)
            return gain_part, jnp.sum(old, axis=0, keepdims=True)

        gain_grad, out_grad = row_steps(body, 2)
        row_copy(2 * turn + 1).start(priority=LOCAL)
        small_row(3 + layer, gain_grad)
        small_row(5 + layer, out_grad)
        grad_saved(turn).start(priority=LOCAL)
        for copy in kin_lefts(False, 4 * turn):
            copy.start()
        slot = opened(8 * turn + 4)

        def tile(there, _):
            dob[:, there] = mm_cols(grad[...], slots[slot, there, :]).astype(BF)

        tiles(4, tile)
        closed(8 * turn + 4)
        grad_saved(turn).wait()
        kin_right(False, 4 * turn, 0).start()

    def attend_heads(turn):
        scale = 1.0 / math.sqrt(HD)
        for copy in act_copies(turn):
            copy.wait()
        if turn == 1:
            for which in range(3):
                kin_right(False, 1 + which, 0).wait_send()

        def head(index, carry):
            here = pl.ds(pl.multiple_of(index * HD, HD), HD)
            q, k, v, do = qb[:, here], kb[:, here], vb[:, here], dob[:, here]
            scores = mm_cols(q, k) * scale
            if turn == 1:
                scores = jnp.where(mask_in[...] > 0.0, scores, MASKED)
            grown = jnp.exp(scores - jnp.max(scores, axis=-1, keepdims=True))
            soft = grown / jnp.sum(grown, axis=-1, keepdims=True)
            back = mm_cols(do, v)
            short = soft * (back - jnp.sum(soft * back, axis=-1, keepdims=True))
            dqkv[0, :, here] = (mm(short.astype(BF), k) * scale).astype(BF)
            dqkv[1, :, here] = (mm(short.T.astype(BF), q) * scale).astype(BF)
            dqkv[2, :, here] = mm(soft.T.astype(BF), do).astype(BF)
            return carry

        lax.fori_loop(0, width // HD, head, 0)
        if turn == 0:
            for copy in act_copies(1):
                copy.start(priority=LOCAL)
        for which in range(3):
            for copy in kin_lefts(False, 4 * turn + 1 + which):
                copy.start()
            kin_right(False, 4 * turn + 1 + which, 0).start()

    def attend_end(turn):
        base = 8 * turn + 5
        for which in range(3):
            slot = opened(base + which)

            def tile(there, _):
                value = mm_cols(dqkv[which], slots[slot, there, :])
                if which == 0:
                    rows_sum[0:rows, there] = value
                elif which == 1:
                    rows_sum[rows : 2 * rows, there] = value
                else:
                    rows_sum[rows : 2 * rows, there] += value

            tiles(4, tile)
            closed(base + which)
        row_copy(2 * turn + 1).wait()
        gain_q = gains[2:3, :] if turn == 0 else gains[0:1, :]
        gain_kv = gains[2:3, :] if turn == 0 else gains[1:2, :]

        def body(here):
            unit, inverse = unit_rows(ub[here, :].astype(F32))
            dx, gain_part = lean(rows_sum[here, :], unit, inverse, gain_q)
            if turn == 1:
                unit, inverse = unit_rows(src_in[here, :].astype(F32))
            there = pl.ds(pl.multiple_of(rows + here.start, 32), 32)
            ds, kv_part = lean(rows_sum[there, :], unit, inverse, gain_kv)
            fresh = grad[here, :].astype(F32) + dx
            if turn == 0:
                fresh += ds
            else:
                high = ds.astype(BF)
                part_out[0, here, :] = high
                part_out[1, here, :] = (ds - high.astype(F32)).astype(BF)
            grad[here, :] = fresh.astype(BF)
            return gain_part, kv_part

        if turn == 1:
            for which in range(2):
                part_over(which).wait_send()
            for copy in kin_lefts(True, 2):
                copy.wait_send()
        gain_grad, kv_grad = row_steps(body, 2)
        if turn == 0:
            row_copy(2).start(priority=LOCAL)
            small_row(2, gain_grad + kv_grad)
            open_pair(1)
        else:
            small_row(0, gain_grad)
            small_row(1, kv_grad)
            small_row(15, jnp.zeros_like(gain_grad))

            def tile(there, _):
                pair[:, there] = (
                    mm(picks_in[...], part_out[0, :, there])
                    + mm(picks_in[...], part_out[1, :, there])
                ).astype(BF)

            tiles(4, tile)
            small_copy(0).start()
            for which in range(3):
                point_copy(which).start()
            lat_start(1)

    def point_total():
        for which in range(3):
            point_copy(which).wait_recv()
        gathered = pair[
            pl.ds(pl.multiple_of(section_at * quarter_rows, 128), quarter_rows)
        ].astype(F32)
        for which in range(3):
            gathered += point_in[which].astype(F32)
        point_sum[...] = gathered.astype(BF)
        point_local().start(priority=LOCAL)
        for which in range(3):
            point_deal(which).start()

    def small_step(phase):
        small_copy(phase).wait_recv()
        small_sum[phase + 1] = small_sum[phase] + small_in[phase]
        if phase < 2:
            small_copy(phase + 1).start()
        else:
            for step in range(3):
                small_copy(3 + step).start()

    def small_end():
        for step in range(3):
            small_copy(3 + step).wait_recv()
        small_out[...] = (small_sum[3] + small_in[4]) + (small_in[3] + small_in[5])

    def rows_end():
        lat_onward(1)
        point_total()

    begin = pltpu.make_async_copy(top_in, grad, act_sems.at[4])
    begin.start()
    for index in range(2):
        slot_copy(index).start(priority=LOCAL)
    h_copy(0).start(priority=LOCAL)
    row_copy(0).start(priority=LOCAL)
    for copy in act_copies(0):
        copy.start(priority=LOCAL)
    begin.wait()
    open_pair(0)
    for turn in range(2):
        for part in range(2):
            kin_right(True, 2 * turn, part).start()
        for copy in kin_lefts(True, 2 * turn + 1):
            copy.start()
    pair_ready(0)
    load(0)
    chain = {
        0: [functools.partial(feed_chunk, 0, 0), functools.partial(lat_start, 0)],
        1: [functools.partial(feed_chunk, 0, 1)],
        2: [functools.partial(feed_end, 0), functools.partial(lat_onward, 0)],
        3: [functools.partial(attend_heads, 0)],
        4: [functools.partial(attend_end, 0)],
        5: [functools.partial(pair_ready, 1), functools.partial(feed_chunk, 1, 0)],
        6: [functools.partial(feed_chunk, 1, 1)],
        7: [functools.partial(feed_end, 1)],
        8: [functools.partial(attend_heads, 1)],
        9: [functools.partial(attend_end, 1)],
        11: [functools.partial(small_step, 0), rows_end],
        13: [functools.partial(small_step, 1)],
        15: [functools.partial(small_step, 2)],
        17: [small_end],
    }

    def moment_body(moment, carry):
        @pl.when(moment < total)
        def _():
            by_kind(moment, offer)

        for lag, action in ((2, first), (3, second), (4, third), (5, close), (6, finish)):
            pl.when(jnp.logical_and(moment >= lag, moment < total + lag))(
                functools.partial(action, moment - lag)
            )
        for when, actions in chain.items():

            @pl.when(moment == when)
            def _():
                for action in actions:
                    action()

        for item in range(1, total):
            pl.when(moment == item - 1)(functools.partial(load, item))
        return carry

    lax.fori_loop(0, total + 6, moment_body, 0)

    for index in range(4):
        if index % 2 == 1:
            for copy in kin_lefts(True, index):
                copy.wait_send()
        if index != 1:
            for chunk in range(2):
                kin_right(True, index, chunk).wait_send()
    for index in range(8):
        for copy in kin_lefts(False, index):
            copy.wait_send()
        if index not in (1, 2, 3):
            kin_right(False, index, 0).wait_send()
    for phase in range(6):
        small_copy(phase).wait_send()
    for which in range(2):
        lat_local(which).wait()
        for way in range(2):
            lat_copy(which, way).wait_send()
            lat_far(which, way).wait()
    point_local().wait()
    for which in range(3):
        point_copy(which).wait_send()
        point_deal(which).wait()

    def drain(item, carry):
        @pl.when(item >= 4)
        def _():
            by_kind(item, drained)

        return carry

    for item in range(total - STAGES, total):
        xy_sent(item)
    lax.fori_loop(0, total, drain, 0)


def reduce_all(full, kept, latents, gains, mask, picks):
    total = ITEM_COUNT
    rows, width = kept[0].shape
    points = picks.shape[0]
    anywhere = pl.BlockSpec(memory_space=pl.ANY)
    vmem = pl.BlockSpec(memory_space=pltpu.VMEM)
    u1, u2, u3, u4, top = kept[:5]
    operands = [*full, u1, u2, u3, u4, top, *kept[5:16], *kept[17:], latents, kept[16]]
    operands += [gains, mask, picks]
    spaces = [anywhere] * (len(operands) - 4) + [vmem] * 4
    dma = pltpu.SemaphoreType.DMA
    flops = 2 * width * width * 24 * rows * 2
    return pl.pallas_call(
        reduce_kernel,
        out_shape=[
            jax.ShapeDtypeStruct((2, 128, 4 * width), BF),
            jax.ShapeDtypeStruct((2, 128, 4 * width), BF),
            jax.ShapeDtypeStruct((128, 3 * width), BF),
            jax.ShapeDtypeStruct((128, 3 * width), BF),
            jax.ShapeDtypeStruct((128, width), BF),
            jax.ShapeDtypeStruct((128, width), BF),
            jax.ShapeDtypeStruct((4 * rows, width), BF),
            jax.ShapeDtypeStruct((4 * rows, width), BF),
            jax.ShapeDtypeStruct((points, width), BF),
            jax.ShapeDtypeStruct((16, width), F32),
            jax.ShapeDtypeStruct((2, rows, width), BF),
            jax.ShapeDtypeStruct((4, 4, 2 * rows, 128), BF),
            jax.ShapeDtypeStruct((8, 4, rows, 128), BF),
            jax.ShapeDtypeStruct((4, 2 * rows, 2 * width), BF),
            jax.ShapeDtypeStruct((8, rows, width), BF),
        ],
        in_specs=spaces,
        out_specs=[anywhere] * 9 + [vmem] + [anywhere] * 5,
        scratch_shapes=[
            pltpu.VMEM((4, 4, 128, 1024), BF),
            pltpu.VMEM((8, 4, 128, 512), BF),
            pltpu.VMEM((4, 2, 512, 128), BF),
            pltpu.VMEM((WINDOWS, 1024, 1024), BF),
            pltpu.VMEM((STAGES, 4, 128, 512), BF),
            pltpu.VMEM((4, 4, 128, 1024), BF),
            pltpu.VMEM((8, 4, 128, 512), BF),
            pltpu.VMEM((8, 5, 128, 1024), BF),
            pltpu.VMEM((4, 128, 1024), BF),
            pltpu.VMEM((8, 128, 512), BF),
            pltpu.VMEM((4, 128, 1024), BF),
            pltpu.VMEM((8, 128, 512), BF),
            pltpu.VMEM((512, 1024), BF),
            pltpu.VMEM((512, 2048), BF),
            pltpu.VMEM((512, 1024), F32),
            pltpu.VMEM((512, 1024), F32),
            pltpu.VMEM((2, 1024, 1024), BF),
            pltpu.VMEM((256, 1024), BF),
            pltpu.VMEM((256, 1024), BF),
            pltpu.VMEM((256, 1024), BF),
            pltpu.VMEM((256, 1024), BF),
            pltpu.VMEM((3, 256, 1024), BF),
            pltpu.VMEM((2, 256, 1024), BF),
            pltpu.VMEM((2, 256, 1024), BF),
            pltpu.VMEM((256, 1024), BF),
            pltpu.VMEM((256, 1024), BF),
            pltpu.VMEM((3, points // 4, width), BF),
            pltpu.VMEM((points // 4, width), BF),
            pltpu.VMEM((6, 16, width), F32),
            pltpu.VMEM((4, 16, width), F32),
            dma((2, 12, 4)),
            dma((2, 16)),
            dma((4, 2)),
            dma((WINDOWS, 2)),
            dma((2, 8, 2)),
            dma((total, 4)),
            dma((total, 5)),
            dma((2, total, 2)),
            dma((2, total, 2)),
            dma((total, 2)),
            dma((2, 2, 2)),
            dma((2, 2, 2)),
            dma((2,)),
            dma((2, 3)),
            dma((2, 3)),
            dma((1,)),
            dma((2, 6)),
            dma((2, 2, 2)),
            dma((2,)),
            dma((1,)),
            dma((1,)),
            dma((5,)),
        ],
        compiler_params=pltpu.CompilerParams(
            collective_id=2, has_side_effects=True, vmem_limit_bytes=62 * 2**20
        ),
        cost_estimate=pl.CostEstimate(
            flops=flops, bytes_accessed=2**27, transcendentals=2**21
        ),
    )(*operands)[:10]


def plain_layers(full, spread, mine, source, valid, cot_own, picks, groups_all):
    proj_c, out_c, in_0, down_0, proj_s, out_s, in_1, down_1 = full
    width, hidden = in_0.shape

    def vector(first, count):
        return spread[:, first : first + count].reshape(-1)

    gains_cross = (vector(0, 1), vector(1, 1))
    gain_self = vector(2, 1)
    gains_mlp = (vector(3, 1), vector(4, 1))
    biases_out = (vector(5, 1), vector(6, 1))
    per_bias = hidden // width
    biases_in = (vector(7, per_bias), vector(7 + per_bias, per_bias))
    cot = cot_own.astype(F32)
    u1, kept_c = attend(mine, source, valid, gains_cross[0], gains_cross[1], proj_c, out_c)
    u2, kept_0 = feed(u1.astype(F32), gains_mlp[0], in_0, biases_in[0], down_0, biases_out[0])
    u2 = u2.astype(F32)
    u3, kept_s = attend(u2, u2, None, gain_self, gain_self, proj_s, out_s)
    u4, kept_1 = feed(u3.astype(F32), gains_mlp[1], in_1, biases_in[1], down_1, biases_out[1])
    final = u4.astype(F32)
    group_norm = jnp.sqrt(jnp.mean(final * final) + EPSILON)
    norm_mean = lax.psum(group_norm, ALL) / groups_all
    g4 = (cot + (norm_mean / group_norm) * final).astype(BF)

    dx, gain_1_grad, bias_1_grad, ob_1_grad, pairs_1 = feed_back(
        g4, kept_1, gains_mlp[1], in_1, down_1
    )
    g3 = (g4.astype(F32) + dx).astype(BF)
    dx, ds, gq, gkv, pairs_s = attend_back(g3, kept_s, gain_self, gain_self, proj_s, out_s)
    gain_s_grad = gq + gkv
    g2 = (g3.astype(F32) + dx + ds).astype(BF)
    dx, gain_0_grad, bias_0_grad, ob_0_grad, pairs_0 = feed_back(
        g2, kept_0, gains_mlp[0], in_0, down_0
    )
    g1 = (g2.astype(F32) + dx).astype(BF)
    dx, ds, cq_grad, ckv_grad, pairs_c = attend_back(
        g1, kept_c, gains_cross[0], gains_cross[1], proj_c, out_c
    )
    g0 = (g1.astype(F32) + dx).astype(BF)
    high = ds.astype(BF)
    low = (ds - high.astype(F32)).astype(BF)
    point_part = (mm_rows(picks, high) + mm_rows(picks, low)).astype(BF)
    small = jnp.concatenate(
        [
            cq_grad,
            ckv_grad,
            gain_s_grad,
            gain_0_grad,
            gain_1_grad,
            ob_0_grad,
            ob_1_grad,
            bias_0_grad,
            bias_1_grad,
            jnp.zeros_like(cq_grad),
        ]
    ).reshape(-1, width)
    pairs = pairs_1 + pairs_s + pairs_0 + pairs_c
    lefts, rights = [pair[0] for pair in pairs], [pair[1] for pair in pairs]
    def settled_grad(left, right):
        part = lax.psum_scatter(
            mm_rows(left, right).astype(BF), ALL, scatter_dimension=0, tiled=True
        )
        return lax.all_gather(part, "section", axis=0, tiled=True).astype(F32)

    done = [settled_grad(left, right) for left, right in pairs]
    mlp_in_grad = jnp.stack([done[6], done[0]])
    mlp_down_grad = jnp.stack([done[7], done[1]])
    proj_s_grad = jnp.concatenate(done[2:5], axis=1)
    proj_c_grad = jnp.concatenate(done[8:11], axis=1)
    out_s_grad, out_c_grad = done[5], done[11]
    points_sum = lax.psum(point_part, "section")
    latents_out = lax.all_gather(u4, "section", axis=0, tiled=True)
    g0_all = lax.all_gather(g0, "section", axis=0, tiled=True)
    small = lax.psum(small, ALL)
    return (
        norm_mean,
        latents_out,
        g0_all,
        points_sum,
        small,
        mlp_in_grad,
        mlp_down_grad,
        proj_c_grad,
        proj_s_grad,
        out_c_grad,
        out_s_grad,
    )


def per_device(
    latents,
    points,
    neighbours,
    lengths,
    cross_proj,
    cross_out,
    cross_gains,
    self_proj,
    self_out,
    self_gain,
    mlp_gain,
    mlp_in,
    mlp_in_bias,
    mlp_down,
    mlp_out_bias,
    cotangent,
):
    sections = lax.axis_size("section")
    section_at = lax.axis_index("section")
    width = latents.shape[1]
    hidden = mlp_in.shape[2]
    groups_dev = neighbours.shape[0]
    rows = latents.shape[0] // sections
    shard = cross_out.shape[0]
    piece = shard // sections
    groups_all = groups_dev * lax.axis_size("batch")

    def gathered(block):
        own = lax.dynamic_slice_in_dim(block, section_at * piece, piece, 0)
        return lax.all_gather(own, ALL, axis=0, tiled=True)

    projs = (cross_proj.reshape(shard, 3 * width), self_proj.reshape(shard, 3 * width))
    if lax.axis_size("batch") == 8:
        made = gather_forward(
            [projs[0], cross_out, mlp_in, mlp_down, projs[1], self_out],
            latents,
            cotangent,
            points,
            neighbours,
            lengths[:, None],
            [cross_gains, self_gain[None, :], mlp_gain, mlp_out_bias, mlp_in_bias],
        )
        full, gain_rows, norm_tile, mask, picks = made[:8], *made[8:12]
        norm_mean = norm_tile[0, 0]
        (
            mlp_in_grad,
            mlp_down_grad,
            proj_c_grad,
            proj_s_grad,
            out_c_grad,
            out_s_grad,
            latents_out,
            g0_all,
            points_sum,
            small,
        ) = reduce_all(full, made[12:], latents, gain_rows, mask, picks)
        mlp_in_grad = mlp_in_grad.astype(F32)
        mlp_down_grad = mlp_down_grad.astype(F32)
        proj_c_grad, proj_s_grad = proj_c_grad.astype(F32), proj_s_grad.astype(F32)
        out_c_grad, out_s_grad = out_c_grad.astype(F32), out_s_grad.astype(F32)
    else:
        vectors = jnp.concatenate(
            [
                cross_gains.reshape(-1),
                self_gain,
                mlp_gain.reshape(-1),
                mlp_out_bias.reshape(-1),
                mlp_in_bias.reshape(-1),
                jnp.zeros_like(self_gain),
            ]
        ).reshape(-1, shard)
        cot_own = lax.dynamic_slice_in_dim(cotangent, section_at * rows, rows, 0)
        mine = lax.dynamic_slice_in_dim(latents, section_at * rows, rows, 0).astype(F32)
        listed = lax.dynamic_index_in_dim(neighbours, section_at, 0, keepdims=False)
        length = lax.dynamic_index_in_dim(lengths, section_at, 0, keepdims=False)
        valid = jnp.arange(listed.shape[0], dtype=jnp.int32) < length
        picks = listed[:, None] == jnp.arange(points.shape[0], dtype=jnp.int32)[None, :]
        picks = picks.astype(BF)
        source = mm(picks, points)
        blocks = [projs[0], cross_out, mlp_in[0], mlp_down[0]]
        blocks += [projs[1], self_out, mlp_in[1], mlp_down[1]]
        full = [gathered(block) for block in blocks]
        spread = lax.all_gather(vectors, "batch", axis=0, tiled=False)
        (
            norm_mean,
            latents_out,
            g0_all,
            points_sum,
            small,
            mlp_in_grad,
            mlp_down_grad,
            proj_c_grad,
            proj_s_grad,
            out_c_grad,
            out_s_grad,
        ) = plain_layers(full, spread.astype(F32), mine, source, valid, cot_own, picks, groups_all)
    points_grad = points_sum.astype(F32)
    latents_grad = g0_all.astype(F32)
    per_bias = hidden // width
    batch_at = lax.axis_index("batch")

    def own(first, count):
        flat = small[first : first + count].reshape(-1)
        size = flat.shape[0] // lax.axis_size("batch")
        return lax.dynamic_slice_in_dim(flat, batch_at * size, size, 0)

    return (
        latents_out,
        latents_grad,
        points_grad,
        proj_c_grad.reshape(shard, 3, width),
        out_c_grad,
        jnp.stack([own(0, 1), own(1, 1)]),
        proj_s_grad.reshape(shard, 3, width),
        out_s_grad,
        own(2, 1),
        jnp.stack([own(3, 1), own(4, 1)]),
        mlp_in_grad,
        jnp.stack([own(7, per_bias), own(7 + per_bias, per_bias)]),
        mlp_down_grad,
        jnp.stack([own(5, 1), own(6, 1)]),
        norm_mean,
    )


def solution(mesh):
    rows = P("batch", None)
    cols = P(None, "batch")
    block = P("batch", None, None)
    pair = P(None, "batch", None)
    return jax.shard_map(
        per_device,
        mesh=mesh,
        in_specs=(
            rows,
            rows,
            rows,
            P("batch"),
            block,
            rows,
            cols,
            block,
            rows,
            P("batch"),
            cols,
            pair,
            cols,
            pair,
            cols,
            rows,
        ),
        out_specs=(
            rows,
            rows,
            rows,
            block,
            rows,
            cols,
            block,
            rows,
            P("batch"),
            cols,
            pair,
            cols,
            pair,
            cols,
            P(),
        ),
        check_vma=False,
    )
```

```python
import functools
import math

import jax
import jax.numpy as jnp
from jax import lax
from jax.experimental import pallas as pl
from jax.experimental.pallas import tpu as pltpu
from jax.sharding import PartitionSpec as P

HD = 128
EPSILON = 1e-05
MASKED = -1e30
BF = jnp.bfloat16
F32 = jnp.float32
ALL = ("batch", "section")
MESH = pl.DeviceIdType.MESH
GATHER_WIDTH = 1024
AHEAD = 4
LOCAL = 1
SLOTS = 3
GATHERED = tuple(
    (4 * layer + index, start)
    for layer in range(2)
    for index, start in (
        [(0, 0), (0, 1024), (0, 2048), (1, 0)]
        + [(2 + which, chunk) for chunk in range(0, 2048, 1024) for which in range(2)]
    )
)


def mm(a, b):
    return jnp.dot(a, b, preferred_element_type=F32)


def mm_rows(a, b):
    return lax.dot_general(a, b, (((0,), (0,)), ((), ())), preferred_element_type=F32)


def mm_cols(a, b):
    return lax.dot_general(a, b, (((1,), (1,)), ((), ())), preferred_element_type=F32)


def unit_rows(values):
    centred = values - jnp.mean(values, axis=-1, keepdims=True)
    inverse = lax.rsqrt(jnp.mean(centred * centred, axis=-1, keepdims=True) + EPSILON)
    return centred * inverse, inverse


def norm_back(gradient, unit, inverse, gain):
    scaled = gradient * gain
    inner = (
        scaled
        - jnp.mean(scaled, axis=-1, keepdims=True)
        - unit * jnp.mean(scaled * unit, axis=-1, keepdims=True)
    )
    return inverse * inner, jnp.sum(gradient * unit, axis=0)


def heads_of(rows):
    return rows.reshape(rows.shape[0], -1, HD)


def softmax(q, k, valid):
    scores = jnp.einsum(
        "lhc,nhc->hln", heads_of(q), heads_of(k), preferred_element_type=F32
    ) * (1.0 / math.sqrt(HD))
    if valid is not None:
        scores = jnp.where(valid[None, None, :], scores, MASKED)
    grown = jnp.exp(scores - jnp.max(scores, axis=-1, keepdims=True))
    return grown / jnp.sum(grown, axis=-1, keepdims=True)


def attend(inputs, source, valid, gain_q, gain_kv, proj, out):
    unit_x, inv_x = unit_rows(inputs)
    queries_in = (unit_x * gain_q).astype(BF)
    unit_s, inv_s = unit_rows(source)
    keys_in = (unit_s * gain_kv).astype(BF)
    width = inputs.shape[1]
    q = mm(queries_in, proj[:, :width]).astype(BF)
    kv = mm(keys_in, proj[:, width:]).astype(BF)
    k, v = kv[:, :width], kv[:, width:]
    soft = softmax(q, k, valid)
    mixture = jnp.einsum("hln,nhc->lhc", soft.astype(BF), heads_of(v), preferred_element_type=F32)
    mixture = mixture.reshape(inputs.shape).astype(BF)
    result = (inputs + mm(mixture, out)).astype(BF)
    return result, (unit_x, inv_x, queries_in, unit_s, inv_s, keys_in, q, k, v, soft, mixture)


def attend_back(gradient, kept, gain_q, gain_kv, proj, out):
    unit_x, inv_x, queries_in, unit_s, inv_s, keys_in, q, k, v, soft, mixture = kept
    width = gradient.shape[1]
    scale = 1.0 / math.sqrt(HD)
    grad_mix = mm_cols(gradient, out).astype(BF)
    grad_soft = jnp.einsum(
        "lhc,nhc->hln", heads_of(grad_mix), heads_of(v), preferred_element_type=F32
    )
    inner = jnp.sum(soft * grad_soft, axis=-1, keepdims=True)
    grad_scores = (soft * (grad_soft - inner)).astype(BF)
    dq = jnp.einsum("hln,nhc->lhc", grad_scores, heads_of(k), preferred_element_type=F32) * scale
    dk = jnp.einsum("hln,lhc->nhc", grad_scores, heads_of(q), preferred_element_type=F32) * scale
    dv = jnp.einsum(
        "hln,lhc->nhc", soft.astype(BF), heads_of(grad_mix), preferred_element_type=F32
    )
    dq = dq.reshape(gradient.shape).astype(BF)
    dk = dk.reshape(-1, width).astype(BF)
    dv = dv.reshape(-1, width).astype(BF)
    grad_x, gain_q_grad = norm_back(mm_cols(dq, proj[:, :width]), unit_x, inv_x, gain_q)
    back_s = mm_cols(dk, proj[:, width : 2 * width]) + mm_cols(dv, proj[:, 2 * width :])
    grad_s, gain_kv_grad = norm_back(back_s, unit_s, inv_s, gain_kv)
    pairs = ((queries_in, dq), (keys_in, dk), (keys_in, dv), (mixture, gradient))
    return grad_x, grad_s, gain_q_grad, gain_kv_grad, pairs


def feed(inputs, gain, w_in, b_in, w_down, b_out):
    unit, inverse = unit_rows(inputs)
    lowered = (unit * gain).astype(BF)
    pre_act = mm(lowered, w_in) + b_in
    active = jax.nn.gelu(pre_act).astype(BF)
    result = (inputs + mm_cols(active, w_down) + b_out).astype(BF)
    return result, (unit, inverse, lowered, pre_act, active)


def feed_back(gradient, kept, gain, w_in, w_down):
    unit, inverse, lowered, pre_act, active = kept
    grad_act = mm(gradient, w_down)
    grad_pre = jax.vjp(jax.nn.gelu, pre_act)[1](grad_act)[0].astype(BF)
    grad_x, gain_grad = norm_back(mm_cols(grad_pre, w_in), unit, inverse, gain)
    bias_grad = jnp.sum(grad_pre.astype(F32), axis=0)
    out_grad = jnp.sum(gradient.astype(F32), axis=0)
    return grad_x, gain_grad, bias_grad, out_grad, ((lowered, grad_pre), (gradient, active))


def gelu_both(value):
    factor = math.sqrt(2.0 / math.pi)
    square = value * value
    bent = jnp.tanh(factor * value * (1.0 + 0.044715 * square))
    inner = factor * (1.0 + 3.0 * 0.044715 * square)
    half = 0.5 * (1.0 + bent)
    return value * half, half + 0.5 * value * (1.0 - bent * bent) * inner


def tiles(count, body):
    def step(index, carry):
        body(pl.ds(pl.multiple_of(index * 256, 256), 256), index)
        return carry

    lax.fori_loop(0, count, step, 0)


def norm_into(source, gain, target):
    def step(index, carry):
        here = pl.ds(pl.multiple_of(index * 32, 32), 32)
        unit, _ = unit_rows(source[here, :].astype(F32))
        target[here, :] = (unit * gain).astype(BF)
        return carry

    lax.fori_loop(0, source.shape[0] // 32, step, 0)


def gather_kernel(*refs):
    cross_proj, cross_out, mlp_in, mlp_down, self_proj, self_out = refs[:6]
    latents_in, cot_all, points_in, near_in, length_in = refs[6:11]
    vec_parts = refs[11:16]
    section_at = lax.axis_index("section")
    batch_at = lax.axis_index("batch")
    x_at = lax.rem(section_at, 2)
    y_at = section_at // 2
    ins = (
        cross_proj,
        cross_out,
        mlp_in.at[0],
        mlp_down.at[0],
        self_proj,
        self_out,
        mlp_in.at[1],
        mlp_down.at[1],
    )
    count = len(ins)
    outs = refs[16 : 16 + count]
    rest = refs[16 + count :]
    gains, norm_out, mask_in, picks_out = rest[:4]
    kept_outs = rest[4:24]
    (
        u1,
        u2,
        u3,
        u4,
        grad_top,
        xq_c,
        sn_c,
        q_c,
        k_c,
        v_c,
        o_c,
        xn_s,
        q_s,
        k_s,
        v_s,
        o_s,
        src_in,
        lowered,
        before,
        active,
        x_in,
        cot_in,
        vec_in,
        vec_rows,
        slots,
        total_rows,
        part_out,
        part_in,
        vec_out,
        biases,
        plane,
        line_in,
    ) = rest[24:56]
    (own_sem, send, recv, kin_send, kin_recv, vec_sems) = rest[56:62]
    (slot_sems, kept_sems, plane_sems, line_sems, pair_sems, row_sems) = rest[62:]
    line = 4
    core = lax.rem(batch_at, 2)
    spot = batch_at // 2
    beside = section_at + 1 - 2 * x_at
    above = lax.rem(section_at + 2, 4)
    sibling = batch_at + 1 - 2 * core
    shard = ins[0].shape[0]
    place = section_at * 2 + core
    rows = x_in.shape[0]

    def down_line(step):
        return lax.rem(spot + step, line) * 2 + core

    def up_line(step):
        return lax.rem(spot + line - step, line) * 2 + core

    near_peers = []
    for turn in range(1, 8):
        other = lax.rem(place + turn, 8)
        near_peers.append((other // 2, spot * 2 + lax.rem(other, 2)))
    line_peers = [(section_at, down_line(step)) for step in range(1, line)]
    far_peers = [(section_at, down_line(step) + 1 - 2 * core) for step in range(1, line)]
    vec_peers = [(section_at, sibling)] + line_peers + far_peers
    peers = near_peers + line_peers + far_peers
    barrier = pltpu.get_barrier_semaphore()
    for peer in peers:
        pl.semaphore_signal(barrier, inc=1, device_id=peer, device_id_type=MESH)
    pl.semaphore_wait(barrier, len(peers))

    def spread(ref, owner, first, size):
        return ref.at[pl.ds(pl.multiple_of(owner * shard, shard), shard), pl.ds(first, size)]

    def is_feed(item):
        return item % 8 >= 4

    def source_of(item, first, size):
        index, start = GATHERED[item]
        if is_feed(item):
            first = pl.multiple_of(first + y_at * outs[index].shape[1], 128)
        return ins[index].at[:, pl.ds(first, size)]

    def piece(item):
        start = GATHERED[item][1]
        if is_feed(item):
            return pl.multiple_of(start + x_at * 512, 128), 512
        return pl.multiple_of(start + section_at * 256, 128), 256

    def own_line(item, way):
        first, size = piece(item)
        return pltpu.make_async_remote_copy(
            source_of(item, first, size),
            spread(outs[GATHERED[item][0]], batch_at, first, size),
            send.at[5 * way, item, 0],
            recv.at[0, item, 3 if way else 1],
            device_id=(section_at, batch_at + (-2 if way else 2)),
            device_id_type=MESH,
        )

    def onward_line(item, step, way):
        first, size = piece(item)
        ref = spread(outs[GATHERED[item][0]], up_line(step), first, size)
        return pltpu.make_async_remote_copy(
            ref,
            ref,
            send.at[0, item, step],
            recv.at[0, item, step - 1 if way else step + 1],
            device_id=(section_at, batch_at + (-2 if way else 2)),
            device_id_type=MESH,
        )

    def came_line(item, step):
        first, size = piece(item)
        ref = spread(outs[GATHERED[item][0]], up_line(step), first, size)
        return pltpu.make_async_remote_copy(
            ref,
            ref,
            send.at[0, item, step],
            recv.at[0, item, step],
            device_id=(section_at, sibling),
            device_id_type=MESH,
        )

    def start_line(item):
        @pl.when(spot < 3)
        def _():
            own_line(item, 0).start()

        @pl.when(spot > 0)
        def _():
            own_line(item, 1).start()

    def arrive_line(item, apart):
        @pl.when(spot >= apart)
        def _():
            came_line(item, apart).wait_recv()

            @pl.when(spot < 3)
            def _():
                onward_line(item, apart, 0).start()

            for copy in near(item, apart):
                copy.start()

        @pl.when(spot + apart <= 3)
        def _():
            came_line(item, 4 - apart).wait_recv()

            @pl.when(spot > 0)
            def _():
                onward_line(item, 4 - apart, 1).start()

            for copy in near(item, 4 - apart):
                copy.start()

    def sent_line(item):
        @pl.when(spot < 3)
        def _():
            own_line(item, 0).wait_send()

        @pl.when(spot > 0)
        def _():
            own_line(item, 1).wait_send()

        for apart in (1, 2, 3):

            @pl.when(jnp.logical_and(spot >= apart, spot < 3))
            def _():
                onward_line(item, apart, 0).wait_send()

            @pl.when(jnp.logical_and(spot + apart <= 3, spot > 0))
            def _():
                onward_line(item, 4 - apart, 1).wait_send()

        for step in (1, 2, 3):
            for copy in near(item, step):
                copy.wait_send()

    def plane_copy(item, step, way, low, wide, peer):
        ref = spread(outs[GATHERED[item][0]], up_line(step), low, wide)
        return pltpu.make_async_remote_copy(
            ref,
            ref,
            send.at[way, item, step],
            recv.at[way, item, step],
            device_id=(peer, batch_at),
            device_id_type=MESH,
        )

    def near(item, step):
        first, size = piece(item)
        copies = [plane_copy(item, step, 1, first, size, beside)]
        if not is_feed(item):
            copies.append(plane_copy(item, step, 2, first, size, above))
        return copies

    def far(item, step):
        start = GATHERED[item][1]
        by_y = pl.multiple_of(start + beside * 256, 128)
        by_x = pl.multiple_of(start + above * 256 + 128, 128)
        if item >= 8:
            return [plane_copy(item, step, 3, by_y, 256, above)]
        return [
            plane_copy(item, step, 3, by_y, 128, above),
            plane_copy(item, step, 4, by_x, 128, beside),
        ]

    def kin(item, step):
        index, start = GATHERED[item]
        if step == 0:
            source = source_of(item, start, GATHER_WIDTH)
        else:
            source = spread(outs[index], up_line(step), start, GATHER_WIDTH)
        return pltpu.make_async_remote_copy(
            source,
            spread(outs[index], up_line(step), start, GATHER_WIDTH),
            kin_send.at[item, step],
            kin_recv.at[item, step],
            device_id=(section_at, sibling),
            device_id_type=MESH,
        )

    def own(item):
        index, start = GATHERED[item]
        return pltpu.make_async_copy(
            source_of(item, start, GATHER_WIDTH),
            spread(outs[index], batch_at, start, GATHER_WIDTH),
            own_sem.at[item],
        )

    def vec_copy(which):
        return pltpu.make_async_remote_copy(
            vec_in,
            vec_out.at[batch_at],
            vec_sems.at[0, which],
            vec_sems.at[1, which],
            device_id=vec_peers[which],
            device_id_type=MESH,
        )

    def slot_copy(item):
        index, start = GATHERED[item]
        return pltpu.make_async_copy(
            outs[index].at[:, pl.ds(start, GATHER_WIDTH)],
            slots.at[item % SLOTS],
            slot_sems.at[item % SLOTS],
        )

    def near_norm(turn):
        return pltpu.make_async_remote_copy(
            plane.at[8],
            plane.at[place],
            plane_sems.at[0, turn],
            plane_sems.at[1, turn],
            device_id=near_peers[turn],
            device_id_type=MESH,
        )

    def far_norm(step):
        return pltpu.make_async_remote_copy(
            line_in.at[4],
            line_in.at[spot],
            line_sems.at[0, step],
            line_sems.at[1, step],
            device_id=line_peers[step],
            device_id_type=MESH,
        )

    def rows_over(layer):
        return pltpu.make_async_remote_copy(
            lowered.at[layer, pl.ds(0, rows)],
            lowered.at[layer, pl.ds(rows, rows)],
            pair_sems.at[0, layer, 0],
            pair_sems.at[1, layer, 0],
            device_id=(above, batch_at),
            device_id_type=MESH,
        )

    def part_over(layer):
        return pltpu.make_async_remote_copy(
            part_out.at[layer],
            part_in.at[layer],
            pair_sems.at[0, layer, 1],
            pair_sems.at[1, layer, 1],
            device_id=(above, batch_at),
            device_id_type=MESH,
        )

    steps = range(1, line)
    total = len(GATHERED)
    started = []

    def launch(copies):
        for copy in copies:
            copy.start()
        started.extend(copies)

    kept = (
        (u1, u2, u3, u4, grad_top)
        + (xq_c, sn_c, q_c, k_c, v_c, o_c)
        + (xn_s, q_s, k_s, v_s, o_s)
        + (src_in, lowered, before, active)
    )
    names = {id(ref): place for place, ref in enumerate(kept)}

    def keep(*chosen):
        for ref in chosen:
            index = names[id(ref)]
            pltpu.make_async_copy(ref, kept_outs[index], kept_sems.at[index]).start(priority=LOCAL)

    def row(index):
        return gains[index : index + 1, :]

    def project(source, target, slot):
        def tile(columns, _):
            target[:, columns] = mm(source[...], slots[slot, :, columns]).astype(BF)

        tiles(4, tile)

    def heads(q, k, v, o, masked):
        def head(index, carry):
            here = pl.ds(pl.multiple_of(index * HD, HD), HD)
            scores = mm_cols(q[:, here], k[:, here]) * (1.0 / math.sqrt(HD))
            if masked:
                scores = jnp.where(mask_in[...] > 0.0, scores, MASKED)
            grown = jnp.exp(scores - jnp.max(scores, axis=-1, keepdims=True))
            soft = grown / jnp.sum(grown, axis=-1, keepdims=True)
            o[:, here] = mm(soft.astype(BF), v[:, here]).astype(BF)
            return carry

        lax.fori_loop(0, q.shape[1] // HD, head, 0)

    def close_attention(inputs, o, target, slot):
        def tile(columns, _):
            target[:, columns] = (
                inputs[:, columns].astype(F32) + mm(o[...], slots[slot, :, columns])
            ).astype(BF)

        tiles(4, tile)

    def feed_up(layer, chunk, slot):
        def tile(columns, index):
            first = chunk * GATHER_WIDTH + index * 256
            there = pl.ds(pl.multiple_of(first, 256), 256)
            lanes = pl.ds(pl.multiple_of(y_at * 2048 + first, 256), 256)
            value = mm(lowered[layer], slots[slot, :, columns]) + biases[layer : layer + 1, lanes]
            active_part, slope = gelu_both(value)
            before[layer, :, there] = slope
            active[layer, :, there] = active_part.astype(BF)

        tiles(4, tile)

    def feed_down(layer, chunk, slot):
        chosen = pl.ds(chunk * GATHER_WIDTH, GATHER_WIDTH)

        def tile(columns, _):
            value = mm_cols(active[layer, :, chosen], slots[slot, columns, :])
            if chunk == 0:
                total_rows[:, columns] = value
            else:
                value = total_rows[:, columns] + value
                total_rows[:, columns] = value
                part_out[layer, :, columns] = value[rows:].astype(BF)

        tiles(4, tile)

    def feed_close(layer):
        inputs, target = (u1, u3)[layer], (u2, u4)[layer]
        part_over(layer).wait_recv()

        def tile(columns, _):
            target[:, columns] = (
                inputs[:, columns].astype(F32)
                + (total_rows[0:rows, columns] + part_in[layer, :, columns].astype(F32))
                + gains[5 + layer : 6 + layer, columns]
            ).astype(BF)

        tiles(4, tile)
        keep(target)

    def work(item):
        slot_copy(item).wait()
        slot = item % SLOTS
        layer, stage = item // 8, item % 8
        inputs = (x_in, u2)[layer]
        middle = (u1, u3)[layer]
        q, k, v, o = ((q_c, k_c, v_c, o_c), (q_s, k_s, v_s, o_s))[layer]
        if stage == 0:
            if layer == 0:
                norm_into(x_in, row(0), xq_c)
                norm_into(src_in, row(1), sn_c)
                keep(xq_c, sn_c)
            else:
                feed_close(0)
                norm_into(u2, row(2), xn_s)
                keep(xn_s)
            project((xq_c, xn_s)[layer], q, slot)
        elif stage == 1:
            project((sn_c, xn_s)[layer], k, slot)
        elif stage == 2:
            project((sn_c, xn_s)[layer], v, slot)
            heads(q, k, v, o, layer == 0)
            keep(q, k, v, o)
        elif stage == 3:
            close_attention(inputs, o, middle, slot)
            norm_into(middle, row(3 + layer), lowered.at[layer, pl.ds(0, rows)])
            launch([rows_over(layer)])
            keep(middle)
        elif stage % 2 == 0:
            if stage == 4:
                rows_over(layer).wait_recv()
            feed_up(layer, (stage - 4) // 2, slot)
        else:
            feed_down(layer, (stage - 4) // 2, slot)
            if stage == 7:
                launch([part_over(layer)])

    for item in range(AHEAD):
        start_line(item)
    here = pl.ds(pl.multiple_of(section_at * rows, rows), rows)
    row_copies = [
        pltpu.make_async_copy(latents_in.at[here], x_in, row_sems.at[0]),
        pltpu.make_async_copy(cot_all.at[here], cot_in, row_sems.at[1]),
    ]
    for copy in row_copies:
        copy.start()
    cross_gain, self_gain, feed_gain, out_bias, in_bias = vec_parts
    vec_rows[...] = jnp.zeros_like(vec_rows)
    vec_rows[0:2, :] = cross_gain[...].astype(F32)
    vec_rows[2:3, :] = self_gain[...].astype(F32)
    vec_rows[3:5, :] = feed_gain[...].astype(F32)
    vec_rows[5:7, :] = out_bias[...].astype(F32)
    bias_rows = in_bias[...].astype(F32)
    for layer in range(2):
        for part_at in range(4):
            index = 7 + 4 * layer + part_at
            vec_rows[index : index + 1, :] = bias_rows[
                layer : layer + 1, part_at * 128 : part_at * 128 + 128
            ]
    vec_in[...] = vec_rows[...].astype(BF)
    vec_out[batch_at] = vec_in[...]
    for which in range(7):
        vec_copy(which).start()
    lanes = lax.broadcasted_iota(jnp.int32, (1, rows), 1)
    length = length_in[pl.ds(section_at, 1), :]
    mask_in[...] = jnp.where(lanes < length, 1.0, 0.0)
    point_at = lax.broadcasted_iota(jnp.int32, (points_in.shape[0], rows), 0)
    wanted = near_in[pl.ds(section_at, 1), :]
    picks = jnp.where(point_at == wanted, 1.0, 0.0)
    picks_out[...] = picks.astype(BF)
    turned = picks.T.astype(BF)

    def source_tile(columns, _):
        src_in[:, columns] = mm(turned, points_in[:, columns]).astype(BF)

    tiles(4, source_tile)
    keep(src_in)
    for copy in row_copies:
        copy.wait()
    for moment in range(-2, total + 4):
        if moment + 2 + AHEAD < total:
            start_line(moment + 2 + AHEAD)
        for apart in (1, 2, 3):
            if 0 <= moment + 3 - apart < total:
                arrive_line(moment + 3 - apart, apart)
        if 0 <= moment < total:
            own(moment).start(priority=LOCAL)
            launch([kin(moment, 0)])
        if 0 <= moment - 1 < total:
            for step in steps:
                if is_feed(moment - 1):
                    near(moment - 1, step)[0].wait_recv()
                    launch([kin(moment - 1, step)])
                else:
                    onward = far(moment - 1, step)
                    for index, copy in enumerate(near(moment - 1, step)):
                        copy.wait_recv()
                        launch(onward[index : index + 1])
        if 0 <= moment - 2 < total and not is_feed(moment - 2):
            for step in steps:
                for copy in far(moment - 2, step):
                    copy.wait_recv()
                launch([kin(moment - 2, step)])
        if moment == 2:
            for which in range(7):
                vec_copy(which).wait()
            for owner in range(8):
                values = vec_out[owner].astype(F32)
                gains[:, owner * 128 : owner * 128 + 128] = values
                for layer in range(2):
                    for part_at in range(4):
                        first = owner * 512 + part_at * 128
                        index = 7 + 4 * layer + part_at
                        biases[layer : layer + 1, first : first + 128] = values[index : index + 1]
        if 0 <= moment - 4 < total:
            work(moment - 4)
        if 0 <= moment - 3 < total:
            own(moment - 3).wait()
            for step in range(line):
                kin(moment - 3, step).wait_recv()
            slot_copy(moment - 3).start(priority=LOCAL)
    keep(lowered, before, active)
    feed_close(1)

    def square(index, carry):
        here = pl.ds(pl.multiple_of(index * 32, 32), 32)
        values = u4[here, :].astype(F32)
        return carry + jnp.sum(values * values, axis=0, keepdims=True)

    squares = lax.fori_loop(0, u4.shape[0] // 32, square, jnp.zeros((1, u4.shape[1]), F32))
    mean = jnp.sum(squares, axis=1, keepdims=True) / (u4.shape[0] * u4.shape[1])
    group_norm = jnp.sqrt(mean + EPSILON)
    plane[8] = jnp.broadcast_to(group_norm, plane.shape[1:])
    for turn in range(7):
        near_norm(turn).start()
    plane[place] = plane[8]
    for turn in range(7):
        near_norm(turn).wait()
    line_in[4] = jnp.sum(plane[0:8], axis=0)
    for step in range(3):
        far_norm(step).start()
    line_in[spot] = line_in[4]
    for step in range(3):
        far_norm(step).wait()
    norm_mean = jnp.sum(line_in[0:4], axis=0) / 32.0
    norm_out[...] = norm_mean
    ratio = norm_mean[0:1, 0:1] / group_norm

    def top(index, carry):
        here = pl.ds(pl.multiple_of(index * 32, 32), 32)
        grad_top[here, :] = (
            cot_in[here, :].astype(F32) + ratio * u4[here, :].astype(F32)
        ).astype(BF)
        return carry

    lax.fori_loop(0, u4.shape[0] // 32, top, 0)
    keep(grad_top)
    for index, ref in enumerate(kept):
        pltpu.make_async_copy(ref, kept_outs[index], kept_sems.at[index]).wait()
    for item in range(total):
        sent_line(item)
    for copy in started:
        copy.wait_send()


def gather_forward(blocks, latents, cotangent, points, near, lengths, vectors):
    width = latents.shape[1]
    rows = near.shape[1]
    half = blocks[2].shape[2] // 2
    widths = (3 * width, width, half, half) * 2
    total = len(GATHERED)
    anywhere = pl.BlockSpec(memory_space=pl.ANY)
    vmem = pl.BlockSpec(memory_space=pltpu.VMEM)
    plain = ((rows, width), BF)
    kept = [plain] * 17 + [
        ((2, 2 * rows, width), BF),
        ((2, 2 * rows, half), F32),
        ((2, 2 * rows, half), BF),
    ]
    dma = pltpu.SemaphoreType.DMA
    return pl.pallas_call(
        gather_kernel,
        out_shape=[jax.ShapeDtypeStruct((width, size), BF) for size in widths]
        + [
            jax.ShapeDtypeStruct((16, width), F32),
            jax.ShapeDtypeStruct((8, 128), F32),
            jax.ShapeDtypeStruct((1, rows), F32),
            jax.ShapeDtypeStruct((points.shape[0], rows), BF),
        ]
        + [jax.ShapeDtypeStruct(*one) for one in kept],
        in_specs=[anywhere] * (len(blocks) + 2) + [vmem] * 8,
        out_specs=[anywhere] * len(widths) + [vmem] * 4 + [anywhere] * len(kept),
        scratch_shapes=[pltpu.VMEM(*one) for one in kept]
        + [
            pltpu.VMEM((rows, width), BF),
            pltpu.VMEM((rows, width), BF),
            pltpu.VMEM((16, 128), BF),
            pltpu.VMEM((16, 128), F32),
            pltpu.VMEM((SLOTS, width, GATHER_WIDTH), BF),
            pltpu.VMEM((2 * rows, width), F32),
            pltpu.VMEM((2, rows, width), BF),
            pltpu.VMEM((2, rows, width), BF),
            pltpu.VMEM((8, 16, 128), BF),
            pltpu.VMEM((2, 2 * half), F32),
            pltpu.VMEM((9, 8, 128), F32),
            pltpu.VMEM((5, 8, 128), F32),
            dma((total,)),
            dma((6, total, 4)),
            dma((5, total, 4)),
            dma((total, 4)),
            dma((total, 4)),
            dma((2, 7)),
            dma((SLOTS,)),
            dma((len(kept),)),
            dma((2, 7)),
            dma((2, 3)),
            dma((2, 2, 2)),
            dma((2,)),
        ],
        compiler_params=pltpu.CompilerParams(
            collective_id=1, has_side_effects=True, vmem_limit_bytes=56 * 2**20
        ),
        cost_estimate=pl.CostEstimate(
            flops=2 * rows * width * sum(widths), bytes_accessed=2**27, transcendentals=2**21
        ),
    )(*blocks, latents, cotangent, points, near, lengths, *vectors)


ITEM_COUNT = 16
WINDOWS = 3
STAGES = 3


def reduce_kernel(*refs):
    total = ITEM_COUNT
    (
        proj_c,
        out_c,
        in_0,
        down_0,
        proj_s,
        out_s,
        in_1,
        down_1,
        u1_in,
        u2_in,
        u3_in,
        last_ref,
        top_in,
        xq_c,
        sn_c,
        q_c,
        k_c,
        v_c,
        o_c,
        xn_s,
        q_s,
        k_s,
        v_s,
        o_s,
        lowered,
        before,
        active,
        latents_in,
        src_in,
        gains,
        mask_in,
        picks_in,
    ) = refs[:32]
    (up_out, down_out, proj_out_c, proj_out_s, end_out_c, end_out_s) = refs[32:38]
    (last_out, first_out, point_out, small_out) = refs[38:42]
    (grads_h, kin_lf, kin_la, kin_rf, kin_ra) = refs[42:47]
    (
        lwin_f,
        lwin_a,
        raw,
        rwin,
        stage,
        merged_f,
        merged_a,
        passing,
        lined_f,
        lined_a,
        crossed_f,
        crossed_a,
        pair,
        slope,
        rows_sum,
        hbuf,
        slots,
        qb,
        kb,
        vb,
        dob,
        dqkv,
        part_out,
        part_in,
        grad,
        ub,
        point_in,
        point_sum,
        small_in,
        small_sum,
    ) = refs[47:77]
    (
        kin_l_sems,
        kin_r_sems,
        raw_sems,
        win_sems,
        xy_sems,
        line_send,
        line_recv,
        cross_sems,
        out_sems,
        own_sems,
        lat_sems,
        far_sems,
        lat_own,
        point_sems,
        deal_sems,
        point_own,
        small_sems,
        pair_sems,
        slot_sems,
        h_sem,
        save_sems,
        act_sems,
    ) = refs[77:]
    section_at = lax.axis_index("section")
    batch_at = lax.axis_index("batch")
    core = lax.rem(batch_at, 2)
    spot = batch_at // 2
    x_at = lax.rem(section_at, 2)
    y_at = section_at // 2
    beside = section_at + 1 - 2 * x_at
    above = lax.rem(section_at + 2, 4)
    across = lax.rem(beside + 2, 4)
    sibling = batch_at + 1 - 2 * core
    flat = (beside, above)
    bits = (x_at, y_at)
    rows, width = 256, 1024

    peers = [(beside, batch_at), (above, batch_at), (across, batch_at), (section_at, sibling)]
    peers += [(section_at, lax.rem(spot + step, 4) * 2 + core) for step in (1, 2, 3)]
    barrier = pltpu.get_barrier_semaphore()
    for peer in peers:
        pl.semaphore_signal(barrier, inc=1, device_id=peer, device_id_type=MESH)
    pl.semaphore_wait(barrier, len(peers))

    def remote(source, target, sems, where, peer):
        return pltpu.make_async_remote_copy(
            source,
            target,
            sems.at[(0, *where)],
            sems.at[(1, *where)],
            device_id=peer,
            device_id_type=MESH,
        )

    feed_left = (pair, lowered.at[1], pair, lowered.at[0])
    feed_right = (active.at[1], slope, active.at[0], slope)
    att_left = (o_s, xn_s, xn_s, xn_s, o_c, xq_c, sn_c, sn_c)
    att_right = tuple(
        ref
        for turn in range(2)
        for ref in (grads_h.at[turn], dqkv.at[0], dqkv.at[1], dqkv.at[2])
    )

    def columns(spot_of, parity):
        return pl.ds(pl.multiple_of((2 * spot_of + parity) * 128, 128), 128)

    def kin_lefts(feed, job):
        source, target = (feed_left, kin_lf) if feed else (att_left, kin_la)
        return [
            remote(
                source[job].at[:, columns(part, 1 - core)],
                target.at[job, part],
                kin_l_sems,
                (job if feed else 4 + job, part),
                (section_at, sibling),
            )
            for part in range(4)
        ]

    def kin_right(feed, job, chunk):
        if feed:
            here = pl.ds(chunk * 1024, 1024)
            source, target = feed_right[job].at[:, here], kin_rf.at[job, :, here]
        else:
            source, target = att_right[job], kin_ra.at[job]
        where = (2 * job + chunk if feed else 8 + job,)
        return remote(source, target, kin_r_sems, where, (section_at, sibling))

    def item_of(index):
        turn, inner = index // 8, index % 8
        if inner < 2:
            return True, 2 * turn, inner
        if inner >= 6 and turn == 1 or inner < 4 and turn == 0:
            return True, 2 * turn + 1, inner % 2
        return False, 4 * turn + inner - (4 - 2 * turn), 0

    def window_copies(index):
        feed, job, chunk = item_of(index)
        slot = index % WINDOWS
        size = 512 if feed else 256
        if feed:
            here = pl.ds(chunk * 1024, 1024)
            sources = (feed_right[job].at[:, here], kin_rf.at[job, :, here])
        else:
            sources = (att_right[job], kin_ra.at[job])
        return [
            pltpu.make_async_copy(
                sources[whose],
                rwin.at[slot, pl.ds(whose * size, size)],
                win_sems.at[slot, whose],
            )
            for whose in range(2)
        ]

    def load(index):
        feed, job, chunk = item_of(index)
        kin_right(feed, job, chunk).wait_recv()
        for copy in window_copies(index):
            copy.start(priority=LOCAL)
        if chunk == 0:
            for copy in kin_lefts(feed, job):
                copy.wait_recv()
            size = 512 if feed else 256
            own_left = (feed_left if feed else att_left)[job]
            kin_left = (kin_lf if feed else kin_la).at[job]
            target = (lwin_f if feed else lwin_a).at[job]
            for part in range(4):
                copies = [
                    pltpu.make_async_copy(
                        own_left.at[:, columns(part, core)],
                        raw.at[part, 0, pl.ds(0, size)],
                        raw_sems.at[part, 0],
                    ),
                    pltpu.make_async_copy(
                        kin_left.at[part], raw.at[part, 1, pl.ds(0, size)], raw_sems.at[part, 1]
                    ),
                ]
                for copy in copies:
                    copy.start(priority=LOCAL)
            for part in range(4):
                for whose, source in enumerate(
                    (own_left.at[:, columns(part, core)], kin_left.at[part])
                ):
                    place = raw.at[part, whose, pl.ds(0, size)]
                    pltpu.make_async_copy(source, place, raw_sems.at[part, whose]).wait()
                    target[part, :, whose * size : whose * size + size] = place[...].T

    def is_feed(item):
        late = jnp.logical_or(item < 10, item >= 14)
        return jnp.logical_or(item < 4, jnp.logical_and(item >= 8, late))

    def feed_job(item):
        return 2 * (item // 8) + lax.rem(item, 8) // (2 + 4 * (item // 8))

    def att_job(item):
        return item - 4 - 2 * (item // 8)

    def loaded(slot, feed):
        size = 512 if feed else 256
        for whose in range(2):
            source = kin_rf.at[0, :, pl.ds(0, 1024)] if feed else kin_ra.at[0]
            pltpu.make_async_copy(
                source, rwin.at[slot, pl.ds(whose * size, size)], win_sems.at[slot, whose]
            ).wait()

    def by_kind(item, action):
        pl.when(is_feed(item))(functools.partial(action, item, True))
        pl.when(jnp.logical_not(is_feed(item)))(functools.partial(action, item, False))

    def merged_of(item, feed):
        return merged_f.at[lax.rem(item, 4)] if feed else merged_a.at[att_job(item)]

    def passing_of(item, feed, slot):
        ref = passing.at[lax.rem(item, 8), slot]
        return ref if feed else ref.at[:, pl.ds(0, 512)]

    def lined_of(item, feed):
        return lined_f.at[lax.rem(item, 4)] if feed else lined_a.at[att_job(item)]

    def crossed_of(item, feed):
        return crossed_f.at[lax.rem(item, 4)] if feed else crossed_a.at[att_job(item)]

    def products(item, choice, store):
        slot = lax.rem(item, WINDOWS)

        def quarter(index, carry):
            upper, part = index // 2, lax.rem(index, 2)
            here = pl.ds(pl.multiple_of(part * 256, 256), 256)
            bit = choice[0] + part * (choice[1] - choice[0])
            first = pl.multiple_of(part * 512 + bit * 256, 256)
            left = lwin_a[att_job(item), pl.ds(upper * 2, 2)].reshape(256, 512)
            right = rwin[slot, 0:512, pl.ds(first, 256)]
            tile = jnp.dot(left, right, preferred_element_type=F32).reshape(2, 128, 256)
            store(pl.ds(upper * 2, 2), here, tile)
            return carry

        lax.fori_loop(0, 4, quarter, 0)

    def xy_copies(item):
        return [
            remote(
                stage.at[lax.rem(att_job(item), STAGES), :, :, pl.ds(side * 256, 256)],
                merged_a.at[att_job(item), :, :, pl.ds(side * 256, 256)],
                xy_sems,
                (att_job(item), side),
                (flat[side], batch_at),
            )
            for side in range(2)
        ]

    def xy_sent(item):
        for copy in xy_copies(item):
            copy.wait_send()

    def line_copy(item, feed, dest, place, rightward):
        step = 1 if rightward else -1
        slot = 4 if not rightward and place - 1 == dest else dest
        return pltpu.make_async_remote_copy(
            merged_of(item, feed).at[dest],
            passing_of(item, feed, slot),
            line_send.at[item, dest],
            line_recv.at[item, slot],
            device_id=(section_at, batch_at + 2 * step),
            device_id_type=MESH,
        )

    def line_wait(item, feed, slot):
        pltpu.make_async_remote_copy(
            merged_of(item, feed).at[0],
            passing_of(item, feed, slot),
            line_send.at[item, 0],
            line_recv.at[item, slot],
            device_id=(section_at, sibling),
            device_id_type=MESH,
        ).wait_recv()

    def line_sent(item, feed):
        for step in (1, 2, 3):
            dest = lax.rem(spot + step, 4)
            pltpu.make_async_remote_copy(
                merged_of(item, feed).at[dest],
                passing_of(item, feed, 0),
                line_send.at[item, dest],
                line_recv.at[item, 0],
                device_id=(section_at, sibling),
                device_id_type=MESH,
            ).wait_send()

    def outset(item, feed):
        @pl.when(spot == 0)
        def _():
            for dest in (3, 2, 1):
                line_copy(item, feed, dest, 0, True).start()

        @pl.when(spot == 3)
        def _():
            for dest in (0, 1, 2):
                line_copy(item, feed, dest, 3, False).start()

    def drained(item, feed):
        line_sent(item, feed)
        if feed:
            feed_out(item, up_out).wait()
            feed_own(item, up_out).wait()
        else:
            for side in range(2):
                att_out(item, side, end_out_s, 0).wait()
                att_own(item, side, end_out_s, 0).wait()

    def offer(item, feed):
        slot = lax.rem(item, WINDOWS)
        loaded(slot, feed)
        if feed:

            @pl.when(item >= 8)
            def _():
                drained(lax.rem(item, 4), True)

            target = merged_of(item, True)

            def tile(index, carry):
                upper, part = index // 4, lax.rem(index, 4)
                here = pl.ds(pl.multiple_of(part * 256, 256), 256)
                left = lwin_f[feed_job(item), pl.ds(upper * 2, 2)].reshape(256, 1024)
                right = rwin[slot, :, here]
                value = jnp.dot(left, right, preferred_element_type=F32)
                target[pl.ds(upper * 2, 2), :, here] = value.reshape(2, 128, 256).astype(BF)
                return carry

            lax.fori_loop(0, 8, tile, 0)
            outset(item, True)
        else:

            @pl.when(jnp.logical_or(item == 7, item == 13))
            def _():
                xy_sent(item - STAGES)

            @pl.when(jnp.logical_and(item >= 10, item <= 12))
            def _():
                xy_sent(item - STAGES - 2)

            def store(blocks, here, tile):
                stage[lax.rem(att_job(item), STAGES), blocks, :, here] = tile.astype(BF)

            products(item, (1 - x_at, 1 - y_at), store)
            for copy in xy_copies(item):
                copy.start()

    def take(item):
        for copy in xy_copies(item):
            copy.wait_recv()
        target = merged_a.at[att_job(item)]

        def store(blocks, here, tile):
            target[blocks, :, here] = (tile + target[blocks, :, here].astype(F32)).astype(BF)

        products(item, bits, store)
        outset(item, False)

    def relay(item, feed, dest, place, rightward):
        line_wait(item, feed, dest)
        target = merged_of(item, feed)
        arrived = passing_of(item, feed, dest)
        target[dest] = (target[dest].astype(F32) + arrived[...].astype(F32)).astype(BF)
        line_copy(item, feed, dest, place, rightward).start()

    def second_of(item, feed):
        @pl.when(spot == 1)
        def _():
            for dest in (3, 2):
                relay(item, feed, dest, 1, True)

        @pl.when(spot == 2)
        def _():
            for dest in (0, 1):
                relay(item, feed, dest, 2, False)

    def third_of(item, feed):
        @pl.when(spot == 1)
        def _():
            relay(item, feed, 0, 1, False)

        @pl.when(spot == 2)
        def _():
            relay(item, feed, 3, 2, True)

    def feed_cross(item):
        return remote(
            lined_of(item, True),
            crossed_of(item, True),
            cross_sems,
            (item, 0),
            (beside, batch_at),
        )

    def cross_copy(item, side):
        here = pl.ds(side * 256, 256)
        return remote(
            lined_of(item, False).at[:, here],
            crossed_of(item, False).at[:, here],
            cross_sems,
            (item, side),
            (flat[1 - side], batch_at),
        )

    def layer_of(item):
        return 1 - item // 8

    def feed_place(item, target):
        base = y_at * 2048 + lax.rem(item, 2) * 1024
        return target.at[layer_of(item), :, pl.ds(pl.multiple_of(base, 1024), 1024)]

    def feed_out(item, target):
        return remote(
            lined_of(item, True),
            feed_place(item, target),
            out_sems,
            (item, 0),
            (above, batch_at),
        )

    def feed_own(item, target):
        return pltpu.make_async_copy(
            lined_of(item, True), feed_place(item, target), own_sems.at[item, 0]
        )

    def feed_write(item):
        @pl.when(lax.rem(item, 8) < 2)
        def _():
            feed_out(item, down_out).start()
            feed_own(item, down_out).start(priority=LOCAL)

        @pl.when(lax.rem(item, 8) >= 2)
        def _():
            feed_out(item, up_out).start()
            feed_own(item, up_out).start(priority=LOCAL)

    def att_place(item, side, target, inner):
        base = inner * 1024 + side * 512 + bits[side] * 256
        return target.at[:, pl.ds(pl.multiple_of(base, 256), 256)]

    def att_out(item, side, target, inner):
        return remote(
            lined_of(item, False).at[:, pl.ds(side * 256, 256)],
            att_place(item, side, target, inner),
            out_sems,
            (item, side),
            (flat[side], batch_at),
        )

    def att_own(item, side, target, inner):
        return pltpu.make_async_copy(
            lined_of(item, False).at[:, pl.ds(side * 256, 256)],
            att_place(item, side, target, inner),
            own_sems.at[item, side],
        )

    def att_write(item):
        inner = lax.rem(att_job(item), 4) - 1
        for turn, proj, end in ((0, proj_out_s, end_out_s), (1, proj_out_c, end_out_c)):

            @pl.when(jnp.logical_and(item // 8 == turn, inner >= 0))
            def _():
                for side in range(2):
                    att_out(item, side, proj, inner).start()
                    att_own(item, side, proj, inner).start(priority=LOCAL)

            @pl.when(jnp.logical_and(item // 8 == turn, inner < 0))
            def _():
                for side in range(2):
                    att_out(item, side, end, 0).start()
                    att_own(item, side, end, 0).start(priority=LOCAL)

    def close_of(item, feed):
        for place in range(4):

            @pl.when(spot == place)
            def _():
                value = merged_of(item, feed)[place].astype(F32)
                if place > 0:
                    line_wait(item, feed, place)
                    value += passing_of(item, feed, place)[...].astype(F32)
                if place < 3:
                    line_wait(item, feed, 4)
                    value += passing_of(item, feed, 4)[...].astype(F32)
                lined_of(item, feed)[...] = value.astype(BF)

        if feed:
            feed_cross(item).start()
        else:
            for side in range(2):
                cross_copy(item, side).start()

    def finish_of(item, feed):
        if feed:
            feed_cross(item).wait()
        else:
            for side in range(2):
                cross_copy(item, side).wait()
        target = lined_of(item, feed)
        target[...] = (
            target[...].astype(F32) + crossed_of(item, feed)[...].astype(F32)
        ).astype(BF)
        if feed:
            feed_write(item)
        else:
            att_write(item)

    def small_copy(phase):
        if phase == 0:
            peer = (section_at, sibling)
        elif phase < 3:
            peer = (flat[phase - 1], batch_at)
        else:
            peer = (section_at, lax.rem(spot + phase - 2, 4) * 2 + core)
        return remote(
            small_sum.at[min(phase, 3)], small_in.at[phase], small_sems, (phase,), peer
        )

    quarter_rows = pair.shape[0] // 4

    def point_copy(which):
        peer = (beside, above, across)[which]
        return remote(
            pair.at[pl.ds(pl.multiple_of(peer * quarter_rows, 128), quarter_rows)],
            point_in.at[which],
            point_sems,
            (which,),
            (peer, batch_at),
        )

    def point_place():
        return point_out.at[pl.ds(pl.multiple_of(section_at * quarter_rows, 128), quarter_rows)]

    def point_deal(which):
        peer = (beside, above, across)[which]
        return remote(point_sum, point_place(), deal_sems, (which,), (peer, batch_at))

    def point_local():
        return pltpu.make_async_copy(point_sum, point_place(), point_own.at[0])

    pairs = ((last_ref, last_out), (grad, first_out))

    def lat_copy(which, way):
        source, target = pairs[which]
        return remote(
            source,
            target.at[pl.ds(pl.multiple_of(section_at * rows, rows), rows)],
            lat_sems,
            (which, way),
            (flat[way], batch_at),
        )

    def lat_far(which):
        target = pairs[which][1]
        part = target.at[pl.ds(pl.multiple_of(above * rows, rows), rows)]
        return remote(part, part, far_sems, (which, 0), (beside, batch_at))

    def lat_local(which):
        source, target = pairs[which]
        return pltpu.make_async_copy(
            source,
            target.at[pl.ds(pl.multiple_of(section_at * rows, rows), rows)],
            lat_own.at[which],
        )

    def lat_start(which):
        lat_local(which).start(priority=LOCAL)
        for way in range(2):
            lat_copy(which, way).start()

    def lat_onward(which):
        lat_copy(which, 1).wait_recv()
        lat_far(which).start()
        lat_copy(which, 0).wait_recv()

    loads = []
    for turn, (proj, out, up, down) in enumerate(
        ((proj_s, out_s, in_1, down_1), (proj_c, out_c, in_0, down_0))
    ):
        for chunk in range(2):
            loads += [down.at[:, pl.ds(chunk * 1024, 1024)], up.at[:, pl.ds(chunk * 1024, 1024)]]
        loads.append(out)
        loads += [proj.at[:, pl.ds(which * 1024, 1024)] for which in range(3)]

    def slot_copy(index):
        return pltpu.make_async_copy(loads[index], slots.at[index % 2], slot_sems.at[index % 2])

    def opened(index):
        slot_copy(index).wait()
        return index % 2

    def closed(index):
        if index + 2 < len(loads):
            slot_copy(index + 2).start(priority=LOCAL)

    def h_copy(index):
        layer, chunk = 1 - index // 2, index % 2
        return pltpu.make_async_copy(
            before.at[layer, :, pl.ds(chunk * 1024, 1024)], hbuf, h_sem.at[0]
        )

    def pair_over(turn):
        return remote(
            pair.at[pl.ds(0, rows)],
            pair.at[pl.ds(rows, rows)],
            pair_sems,
            (turn, 0),
            (above, batch_at),
        )

    def part_over(turn):
        return remote(
            part_out.at[turn], part_in.at[turn], pair_sems, (turn, 1), (above, batch_at)
        )

    def grad_saved(turn):
        return pltpu.make_async_copy(grad, grads_h.at[turn], save_sems.at[0])

    def act_copies(turn):
        chosen = ((q_s, k_s, v_s), (q_c, k_c, v_c))[turn]
        return [
            pltpu.make_async_copy(source, target, act_sems.at[index])
            for index, (source, target) in enumerate(zip(chosen, (qb, kb, vb)))
        ]

    def row_copy(index):
        if index == 3:
            source = latents_in.at[pl.ds(pl.multiple_of(section_at * rows, rows), rows)]
        else:
            source = (u3_in, u2_in, u1_in)[index]
        return pltpu.make_async_copy(source, ub, act_sems.at[3])

    def small_row(index, value):
        small_sum[0, index : index + 1, :] = value

    def open_pair(turn):
        pair[0:rows, :] = grad[...]
        pair_over(turn).start()

    def pair_ready(turn):
        pair_over(turn).wait()
        for copy in kin_lefts(True, 2 * turn):
            copy.start()

    def feed_chunk(turn, chunk):
        layer = 1 - turn
        base = 8 * turn + 2 * chunk
        h_copy(2 * turn + chunk).wait()
        if turn == 1:
            kin_right(True, 1, chunk).wait_send()
        slot = opened(base)

        def up_tile(here, index):
            there = pl.ds(pl.multiple_of(chunk * 1024 + index * 256, 256), 256)
            value = mm(pair[...], slots[slot, :, here]) * hbuf[:, here]
            short = value.astype(BF)
            slope[:, there] = short
            column = jnp.sum(short.astype(F32), axis=0, keepdims=True)
            for half in range(2):
                index_at = 7 + 4 * layer + 2 * half + chunk
                small_sum[0, index_at : index_at + 1, here] = jnp.where(
                    y_at == half, column, jnp.zeros_like(column)
                )

        tiles(4, up_tile)
        closed(base)
        if 2 * turn + chunk + 1 < 4:
            h_copy(2 * turn + chunk + 1).start(priority=LOCAL)
        kin_right(True, 2 * turn + 1, chunk).start()
        slot = opened(base + 1)

        def down_tile(there, _):
            value = mm_cols(slope[:, chunk * 1024 : chunk * 1024 + 1024], slots[slot, there, :])
            if chunk == 0:
                rows_sum[:, there] = value
            else:
                value = rows_sum[:, there] + value
                rows_sum[:, there] = value
                part_out[turn, :, there] = value[rows:].astype(BF)

        tiles(4, down_tile)
        closed(base + 1)
        if chunk == 1:
            if turn == 0:
                for copy in kin_lefts(True, 0):
                    copy.wait_send()
            part_over(turn).start()

    def row_steps(body, count):
        zero = jnp.zeros((1, width), F32)

        def step(index, carry):
            here = pl.ds(pl.multiple_of(index * 32, 32), 32)
            return tuple(a + b for a, b in zip(carry, body(here)))

        return lax.fori_loop(0, rows // 32, step, (zero,) * count)

    def lean(back, unit, inverse, gain):
        scaled = back * gain
        inner = (
            scaled
            - jnp.mean(scaled, axis=-1, keepdims=True)
            - unit * jnp.mean(scaled * unit, axis=-1, keepdims=True)
        )
        return inverse * inner, jnp.sum(back * unit, axis=0, keepdims=True)

    def feed_end(turn):
        layer = 1 - turn
        gain = gains[3 + layer : 4 + layer, :]
        part_over(turn).wait_recv()
        row_copy(2 * turn).wait()

        def body(here):
            unit, inverse = unit_rows(ub[here, :].astype(F32))
            back = rows_sum[here, :] + part_in[turn, here, :].astype(F32)
            dx, gain_part = lean(back, unit, inverse, gain)
            old = grad[here, :].astype(F32)
            grad[here, :] = (old + dx).astype(BF)
            return gain_part, jnp.sum(old, axis=0, keepdims=True)

        gain_grad, out_grad = row_steps(body, 2)
        row_copy(2 * turn + 1).start(priority=LOCAL)
        small_row(3 + layer, gain_grad)
        small_row(5 + layer, out_grad)
        grad_saved(turn).start(priority=LOCAL)
        for copy in kin_lefts(False, 4 * turn):
            copy.start()
        slot = opened(8 * turn + 4)

        def tile(there, _):
            dob[:, there] = mm_cols(grad[...], slots[slot, there, :]).astype(BF)

        tiles(4, tile)
        closed(8 * turn + 4)
        grad_saved(turn).wait()
        kin_right(False, 4 * turn, 0).start()

    def attend_heads(turn):
        scale = 1.0 / math.sqrt(HD)
        for copy in act_copies(turn):
            copy.wait()
        if turn == 1:
            for which in range(3):
                kin_right(False, 1 + which, 0).wait_send()

        def head(index, carry):
            here = pl.ds(pl.multiple_of(index * HD, HD), HD)
            q, k, v, do = qb[:, here], kb[:, here], vb[:, here], dob[:, here]
            scores = mm_cols(q, k) * scale
            if turn == 1:
                scores = jnp.where(mask_in[...] > 0.0, scores, MASKED)
            grown = jnp.exp(scores - jnp.max(scores, axis=-1, keepdims=True))
            soft = grown / jnp.sum(grown, axis=-1, keepdims=True)
            back = mm_cols(do, v)
            short = soft * (back - jnp.sum(soft * back, axis=-1, keepdims=True))
            dqkv[0, :, here] = (mm(short.astype(BF), k) * scale).astype(BF)
            dqkv[1, :, here] = (mm(short.T.astype(BF), q) * scale).astype(BF)
            dqkv[2, :, here] = mm(soft.T.astype(BF), do).astype(BF)
            return carry

        lax.fori_loop(0, width // HD, head, 0)
        if turn == 0:
            for copy in act_copies(1):
                copy.start(priority=LOCAL)
        for which in range(3):
            for copy in kin_lefts(False, 4 * turn + 1 + which):
                copy.start()
            kin_right(False, 4 * turn + 1 + which, 0).start()

    def attend_end(turn):
        base = 8 * turn + 5
        for which in range(3):
            slot = opened(base + which)

            def tile(there, _):
                value = mm_cols(dqkv[which], slots[slot, there, :])
                if which == 0:
                    rows_sum[0:rows, there] = value
                elif which == 1:
                    rows_sum[rows : 2 * rows, there] = value
                else:
                    rows_sum[rows : 2 * rows, there] += value

            tiles(4, tile)
            closed(base + which)
        row_copy(2 * turn + 1).wait()
        gain_q = gains[2:3, :] if turn == 0 else gains[0:1, :]
        gain_kv = gains[2:3, :] if turn == 0 else gains[1:2, :]

        def body(here):
            unit, inverse = unit_rows(ub[here, :].astype(F32))
            dx, gain_part = lean(rows_sum[here, :], unit, inverse, gain_q)
            if turn == 1:
                unit, inverse = unit_rows(src_in[here, :].astype(F32))
            there = pl.ds(pl.multiple_of(rows + here.start, 32), 32)
            ds, kv_part = lean(rows_sum[there, :], unit, inverse, gain_kv)
            fresh = grad[here, :].astype(F32) + dx
            if turn == 0:
                fresh += ds
            else:
                high = ds.astype(BF)
                part_out[0, here, :] = high
                part_out[1, here, :] = (ds - high.astype(F32)).astype(BF)
            grad[here, :] = fresh.astype(BF)
            return gain_part, kv_part

        if turn == 1:
            for which in range(2):
                part_over(which).wait_send()
            for copy in kin_lefts(True, 2):
                copy.wait_send()
        gain_grad, kv_grad = row_steps(body, 2)
        if turn == 0:
            row_copy(2).start(priority=LOCAL)
            small_row(2, gain_grad + kv_grad)
            open_pair(1)
        else:
            small_row(0, gain_grad)
            small_row(1, kv_grad)
            small_row(15, jnp.zeros_like(gain_grad))

            def tile(there, _):
                pair[:, there] = (
                    mm(picks_in[...], part_out[0, :, there])
                    + mm(picks_in[...], part_out[1, :, there])
                ).astype(BF)

            tiles(4, tile)
            small_copy(0).start()
            for which in range(3):
                point_copy(which).start()
            lat_start(1)

    def point_total():
        for which in range(3):
            point_copy(which).wait_recv()
        gathered = pair[
            pl.ds(pl.multiple_of(section_at * quarter_rows, 128), quarter_rows)
        ].astype(F32)
        for which in range(3):
            gathered += point_in[which].astype(F32)
        point_sum[...] = gathered.astype(BF)
        point_local().start(priority=LOCAL)
        for which in range(3):
            point_deal(which).start()

    def small_step(phase):
        small_copy(phase).wait_recv()
        small_sum[phase + 1] = small_sum[phase] + small_in[phase]
        if phase < 2:
            small_copy(phase + 1).start()
        else:
            for step in range(3):
                small_copy(3 + step).start()

    def small_end():
        for step in range(3):
            small_copy(3 + step).wait_recv()
        small_out[...] = (small_sum[3] + small_in[4]) + (small_in[3] + small_in[5])

    def rows_end():
        lat_onward(1)
        point_total()

    begin = pltpu.make_async_copy(top_in, grad, act_sems.at[4])
    begin.start()
    for index in range(2):
        slot_copy(index).start(priority=LOCAL)
    h_copy(0).start(priority=LOCAL)
    row_copy(0).start(priority=LOCAL)
    for copy in act_copies(0):
        copy.start(priority=LOCAL)
    begin.wait()
    open_pair(0)
    for turn in range(2):
        for part in range(2):
            kin_right(True, 2 * turn, part).start()
        for copy in kin_lefts(True, 2 * turn + 1):
            copy.start()
    lat_start(0)
    pair_ready(0)
    load(0)
    chain = {
        0: [functools.partial(feed_chunk, 0, 0)],
        1: [functools.partial(lat_onward, 0), functools.partial(feed_chunk, 0, 1)],
        2: [functools.partial(feed_end, 0)],
        3: [functools.partial(attend_heads, 0)],
        4: [functools.partial(attend_end, 0)],
        5: [functools.partial(pair_ready, 1), functools.partial(feed_chunk, 1, 0)],
        6: [functools.partial(feed_chunk, 1, 1)],
        7: [functools.partial(feed_end, 1)],
        8: [functools.partial(attend_heads, 1)],
        9: [functools.partial(attend_end, 1)],
        11: [functools.partial(small_step, 0), rows_end],
        13: [functools.partial(small_step, 1)],
        15: [functools.partial(small_step, 2)],
        17: [small_end],
    }

    def moment_body(moment, carry):
        @pl.when(moment < total)
        def _():
            by_kind(moment, offer)

        for lag, action in enumerate((None, second_of, third_of, close_of, finish_of)):
            for later, feed in ((0, True), (1, False)):
                if action is None and feed:
                    continue
                item = moment - lag - later
                right_kind = is_feed(item) if feed else jnp.logical_not(is_feed(item))
                there = jnp.logical_and(item >= 0, item < total)

                @pl.when(jnp.logical_and(there, right_kind))
                def _():
                    if action is None:
                        take(item)
                    else:
                        action(item, feed)

        for when, actions in chain.items():

            @pl.when(moment == when)
            def _():
                for action in actions:
                    action()

        for item in range(1, total):
            pl.when(moment == item - 1)(functools.partial(load, item))
        return carry

    lax.fori_loop(0, total + 4, moment_body, 0)

    for index in range(4):
        if index % 2 == 1:
            for copy in kin_lefts(True, index):
                copy.wait_send()
        if index != 1:
            for chunk in range(2):
                kin_right(True, index, chunk).wait_send()
    for index in range(8):
        for copy in kin_lefts(False, index):
            copy.wait_send()
        if index not in (1, 2, 3):
            kin_right(False, index, 0).wait_send()
    for phase in range(6):
        small_copy(phase).wait_send()
    for which in range(2):
        lat_local(which).wait()
        for way in range(2):
            lat_copy(which, way).wait_send()
        lat_far(which).wait()
    point_local().wait()
    for which in range(3):
        point_copy(which).wait_send()
        point_deal(which).wait()

    def drain(item, carry):
        @pl.when(item >= 4)
        def _():
            by_kind(item, drained)

        return carry

    for item in (11, 12, 13):
        xy_sent(item)
    lax.fori_loop(0, total, drain, 0)


def reduce_all(full, kept, latents, gains, mask, picks):
    total = ITEM_COUNT
    rows, width = kept[0].shape
    points = picks.shape[0]
    anywhere = pl.BlockSpec(memory_space=pl.ANY)
    vmem = pl.BlockSpec(memory_space=pltpu.VMEM)
    u1, u2, u3, u4, top = kept[:5]
    operands = [*full, u1, u2, u3, u4, top, *kept[5:16], *kept[17:], latents, kept[16]]
    operands += [gains, mask, picks]
    spaces = [anywhere] * (len(operands) - 4) + [vmem] * 4
    dma = pltpu.SemaphoreType.DMA
    flops = 2 * width * width * 24 * rows * 2
    return pl.pallas_call(
        reduce_kernel,
        out_shape=[
            jax.ShapeDtypeStruct((2, 128, 4 * width), BF),
            jax.ShapeDtypeStruct((2, 128, 4 * width), BF),
            jax.ShapeDtypeStruct((128, 3 * width), BF),
            jax.ShapeDtypeStruct((128, 3 * width), BF),
            jax.ShapeDtypeStruct((128, width), BF),
            jax.ShapeDtypeStruct((128, width), BF),
            jax.ShapeDtypeStruct((4 * rows, width), BF),
            jax.ShapeDtypeStruct((4 * rows, width), BF),
            jax.ShapeDtypeStruct((points, width), BF),
            jax.ShapeDtypeStruct((16, width), F32),
            jax.ShapeDtypeStruct((2, rows, width), BF),
            jax.ShapeDtypeStruct((4, 4, 2 * rows, 128), BF),
            jax.ShapeDtypeStruct((8, 4, rows, 128), BF),
            jax.ShapeDtypeStruct((4, 2 * rows, 2 * width), BF),
            jax.ShapeDtypeStruct((8, rows, width), BF),
        ],
        in_specs=spaces,
        out_specs=[anywhere] * 9 + [vmem] + [anywhere] * 5,
        scratch_shapes=[
            pltpu.VMEM((4, 4, 128, 1024), BF),
            pltpu.VMEM((8, 4, 128, 512), BF),
            pltpu.VMEM((4, 2, 512, 128), BF),
            pltpu.VMEM((WINDOWS, 1024, 1024), BF),
            pltpu.VMEM((STAGES, 4, 128, 512), BF),
            pltpu.VMEM((4, 4, 128, 1024), BF),
            pltpu.VMEM((8, 4, 128, 512), BF),
            pltpu.VMEM((8, 5, 128, 1024), BF),
            pltpu.VMEM((4, 128, 1024), BF),
            pltpu.VMEM((8, 128, 512), BF),
            pltpu.VMEM((4, 128, 1024), BF),
            pltpu.VMEM((8, 128, 512), BF),
            pltpu.VMEM((512, 1024), BF),
            pltpu.VMEM((512, 2048), BF),
            pltpu.VMEM((512, 1024), F32),
            pltpu.VMEM((512, 1024), F32),
            pltpu.VMEM((2, 1024, 1024), BF),
            pltpu.VMEM((256, 1024), BF),
            pltpu.VMEM((256, 1024), BF),
            pltpu.VMEM((256, 1024), BF),
            pltpu.VMEM((256, 1024), BF),
            pltpu.VMEM((3, 256, 1024), BF),
            pltpu.VMEM((2, 256, 1024), BF),
            pltpu.VMEM((2, 256, 1024), BF),
            pltpu.VMEM((256, 1024), BF),
            pltpu.VMEM((256, 1024), BF),
            pltpu.VMEM((3, points // 4, width), BF),
            pltpu.VMEM((points // 4, width), BF),
            pltpu.VMEM((6, 16, width), F32),
            pltpu.VMEM((4, 16, width), F32),
            dma((2, 12, 4)),
            dma((2, 16)),
            dma((4, 2)),
            dma((WINDOWS, 2)),
            dma((2, 8, 2)),
            dma((total, 4)),
            dma((total, 5)),
            dma((2, total, 2)),
            dma((2, total, 2)),
            dma((total, 2)),
            dma((2, 2, 2)),
            dma((2, 2, 2)),
            dma((2,)),
            dma((2, 3)),
            dma((2, 3)),
            dma((1,)),
            dma((2, 6)),
            dma((2, 2, 2)),
            dma((2,)),
            dma((1,)),
            dma((1,)),
            dma((5,)),
        ],
        compiler_params=pltpu.CompilerParams(
            collective_id=2, has_side_effects=True, vmem_limit_bytes=62 * 2**20
        ),
        cost_estimate=pl.CostEstimate(
            flops=flops, bytes_accessed=2**27, transcendentals=2**21
        ),
    )(*operands)[:10]


def plain_layers(full, spread, mine, source, valid, cot_own, picks, groups_all):
    proj_c, out_c, in_0, down_0, proj_s, out_s, in_1, down_1 = full
    width, hidden = in_0.shape

    def vector(first, count):
        return spread[:, first : first + count].reshape(-1)

    gains_cross = (vector(0, 1), vector(1, 1))
    gain_self = vector(2, 1)
    gains_mlp = (vector(3, 1), vector(4, 1))
    biases_out = (vector(5, 1), vector(6, 1))
    per_bias = hidden // width
    biases_in = (vector(7, per_bias), vector(7 + per_bias, per_bias))
    cot = cot_own.astype(F32)
    u1, kept_c = attend(mine, source, valid, gains_cross[0], gains_cross[1], proj_c, out_c)
    u2, kept_0 = feed(u1.astype(F32), gains_mlp[0], in_0, biases_in[0], down_0, biases_out[0])
    u2 = u2.astype(F32)
    u3, kept_s = attend(u2, u2, None, gain_self, gain_self, proj_s, out_s)
    u4, kept_1 = feed(u3.astype(F32), gains_mlp[1], in_1, biases_in[1], down_1, biases_out[1])
    final = u4.astype(F32)
    group_norm = jnp.sqrt(jnp.mean(final * final) + EPSILON)
    norm_mean = lax.psum(group_norm, ALL) / groups_all
    g4 = (cot + (norm_mean / group_norm) * final).astype(BF)

    dx, gain_1_grad, bias_1_grad, ob_1_grad, pairs_1 = feed_back(
        g4, kept_1, gains_mlp[1], in_1, down_1
    )
    g3 = (g4.astype(F32) + dx).astype(BF)
    dx, ds, gq, gkv, pairs_s = attend_back(g3, kept_s, gain_self, gain_self, proj_s, out_s)
    gain_s_grad = gq + gkv
    g2 = (g3.astype(F32) + dx + ds).astype(BF)
    dx, gain_0_grad, bias_0_grad, ob_0_grad, pairs_0 = feed_back(
        g2, kept_0, gains_mlp[0], in_0, down_0
    )
    g1 = (g2.astype(F32) + dx).astype(BF)
    dx, ds, cq_grad, ckv_grad, pairs_c = attend_back(
        g1, kept_c, gains_cross[0], gains_cross[1], proj_c, out_c
    )
    g0 = (g1.astype(F32) + dx).astype(BF)
    high = ds.astype(BF)
    low = (ds - high.astype(F32)).astype(BF)
    point_part = (mm_rows(picks, high) + mm_rows(picks, low)).astype(BF)
    small = jnp.concatenate(
        [
            cq_grad,
            ckv_grad,
            gain_s_grad,
            gain_0_grad,
            gain_1_grad,
            ob_0_grad,
            ob_1_grad,
            bias_0_grad,
            bias_1_grad,
            jnp.zeros_like(cq_grad),
        ]
    ).reshape(-1, width)
    pairs = pairs_1 + pairs_s + pairs_0 + pairs_c
    lefts, rights = [pair[0] for pair in pairs], [pair[1] for pair in pairs]
    def settled_grad(left, right):
        part = lax.psum_scatter(
            mm_rows(left, right).astype(BF), ALL, scatter_dimension=0, tiled=True
        )
        return lax.all_gather(part, "section", axis=0, tiled=True).astype(F32)

    done = [settled_grad(left, right) for left, right in pairs]
    mlp_in_grad = jnp.stack([done[6], done[0]])
    mlp_down_grad = jnp.stack([done[7], done[1]])
    proj_s_grad = jnp.concatenate(done[2:5], axis=1)
    proj_c_grad = jnp.concatenate(done[8:11], axis=1)
    out_s_grad, out_c_grad = done[5], done[11]
    points_sum = lax.psum(point_part, "section")
    latents_out = lax.all_gather(u4, "section", axis=0, tiled=True)
    g0_all = lax.all_gather(g0, "section", axis=0, tiled=True)
    small = lax.psum(small, ALL)
    return (
        norm_mean,
        latents_out,
        g0_all,
        points_sum,
        small,
        mlp_in_grad,
        mlp_down_grad,
        proj_c_grad,
        proj_s_grad,
        out_c_grad,
        out_s_grad,
    )


def per_device(
    latents,
    points,
    neighbours,
    lengths,
    cross_proj,
    cross_out,
    cross_gains,
    self_proj,
    self_out,
    self_gain,
    mlp_gain,
    mlp_in,
    mlp_in_bias,
    mlp_down,
    mlp_out_bias,
    cotangent,
):
    sections = lax.axis_size("section")
    section_at = lax.axis_index("section")
    width = latents.shape[1]
    hidden = mlp_in.shape[2]
    groups_dev = neighbours.shape[0]
    rows = latents.shape[0] // sections
    shard = cross_out.shape[0]
    piece = shard // sections
    groups_all = groups_dev * lax.axis_size("batch")

    def gathered(block):
        own = lax.dynamic_slice_in_dim(block, section_at * piece, piece, 0)
        return lax.all_gather(own, ALL, axis=0, tiled=True)

    projs = (cross_proj.reshape(shard, 3 * width), self_proj.reshape(shard, 3 * width))
    if lax.axis_size("batch") == 8:
        made = gather_forward(
            [projs[0], cross_out, mlp_in, mlp_down, projs[1], self_out],
            latents,
            cotangent,
            points,
            neighbours,
            lengths[:, None],
            [cross_gains, self_gain[None, :], mlp_gain, mlp_out_bias, mlp_in_bias],
        )
        full, gain_rows, norm_tile, mask, picks = made[:8], *made[8:12]
        norm_mean = norm_tile[0, 0]
        (
            mlp_in_grad,
            mlp_down_grad,
            proj_c_grad,
            proj_s_grad,
            out_c_grad,
            out_s_grad,
            latents_out,
            g0_all,
            points_sum,
            small,
        ) = reduce_all(full, made[12:], latents, gain_rows, mask, picks)
        mlp_in_grad = mlp_in_grad.astype(F32)
        mlp_down_grad = mlp_down_grad.astype(F32)
        proj_c_grad, proj_s_grad = proj_c_grad.astype(F32), proj_s_grad.astype(F32)
        out_c_grad, out_s_grad = out_c_grad.astype(F32), out_s_grad.astype(F32)
    else:
        vectors = jnp.concatenate(
            [
                cross_gains.reshape(-1),
                self_gain,
                mlp_gain.reshape(-1),
                mlp_out_bias.reshape(-1),
                mlp_in_bias.reshape(-1),
                jnp.zeros_like(self_gain),
            ]
        ).reshape(-1, shard)
        cot_own = lax.dynamic_slice_in_dim(cotangent, section_at * rows, rows, 0)
        mine = lax.dynamic_slice_in_dim(latents, section_at * rows, rows, 0).astype(F32)
        listed = lax.dynamic_index_in_dim(neighbours, section_at, 0, keepdims=False)
        length = lax.dynamic_index_in_dim(lengths, section_at, 0, keepdims=False)
        valid = jnp.arange(listed.shape[0], dtype=jnp.int32) < length
        picks = listed[:, None] == jnp.arange(points.shape[0], dtype=jnp.int32)[None, :]
        picks = picks.astype(BF)
        source = mm(picks, points)
        blocks = [projs[0], cross_out, mlp_in[0], mlp_down[0]]
        blocks += [projs[1], self_out, mlp_in[1], mlp_down[1]]
        full = [gathered(block) for block in blocks]
        spread = lax.all_gather(vectors, "batch", axis=0, tiled=False)
        (
            norm_mean,
            latents_out,
            g0_all,
            points_sum,
            small,
            mlp_in_grad,
            mlp_down_grad,
            proj_c_grad,
            proj_s_grad,
            out_c_grad,
            out_s_grad,
        ) = plain_layers(full, spread.astype(F32), mine, source, valid, cot_own, picks, groups_all)
    points_grad = points_sum.astype(F32)
    latents_grad = g0_all.astype(F32)
    per_bias = hidden // width
    batch_at = lax.axis_index("batch")

    def own(first, count):
        flat = small[first : first + count].reshape(-1)
        size = flat.shape[0] // lax.axis_size("batch")
        return lax.dynamic_slice_in_dim(flat, batch_at * size, size, 0)

    return (
        latents_out,
        latents_grad,
        points_grad,
        proj_c_grad.reshape(shard, 3, width),
        out_c_grad,
        jnp.stack([own(0, 1), own(1, 1)]),
        proj_s_grad.reshape(shard, 3, width),
        out_s_grad,
        own(2, 1),
        jnp.stack([own(3, 1), own(4, 1)]),
        mlp_in_grad,
        jnp.stack([own(7, per_bias), own(7 + per_bias, per_bias)]),
        mlp_down_grad,
        jnp.stack([own(5, 1), own(6, 1)]),
        norm_mean,
    )


def solution(mesh):
    rows = P("batch", None)
    cols = P(None, "batch")
    block = P("batch", None, None)
    pair = P(None, "batch", None)
    return jax.shard_map(
        per_device,
        mesh=mesh,
        in_specs=(
            rows,
            rows,
            rows,
            P("batch"),
            block,
            rows,
            cols,
            block,
            rows,
            P("batch"),
            cols,
            pair,
            cols,
            pair,
            cols,
            rows,
        ),
        out_specs=(
            rows,
            rows,
            rows,
            block,
            rows,
            cols,
            block,
            rows,
            P("batch"),
            cols,
            pair,
            cols,
            pair,
            cols,
            P(),
        ),
        check_vma=False,
    )
```

```python
import functools
import math

import jax
import jax.numpy as jnp
from jax import lax
from jax.experimental import pallas as pl
from jax.experimental.pallas import tpu as pltpu
from jax.sharding import PartitionSpec as P

HD = 128
EPSILON = 1e-05
MASKED = -1e30
BF = jnp.bfloat16
F32 = jnp.float32
ALL = ("batch", "section")
MESH = pl.DeviceIdType.MESH
GATHER_WIDTH = 1024
AHEAD = 4
LOCAL = 1
SLOTS = 3
GATHERED = tuple(
    (4 * layer + index, start)
    for layer in range(2)
    for index, start in (
        [(0, 0), (0, 1024), (0, 2048), (1, 0)]
        + [(2 + which, chunk) for chunk in range(0, 2048, 1024) for which in range(2)]
    )
)


def mm(a, b):
    return jnp.dot(a, b, preferred_element_type=F32)


def mm_rows(a, b):
    return lax.dot_general(a, b, (((0,), (0,)), ((), ())), preferred_element_type=F32)


def mm_cols(a, b):
    return lax.dot_general(a, b, (((1,), (1,)), ((), ())), preferred_element_type=F32)


def unit_rows(values):
    centred = values - jnp.mean(values, axis=-1, keepdims=True)
    inverse = lax.rsqrt(jnp.mean(centred * centred, axis=-1, keepdims=True) + EPSILON)
    return centred * inverse, inverse


def norm_back(gradient, unit, inverse, gain):
    scaled = gradient * gain
    inner = (
        scaled
        - jnp.mean(scaled, axis=-1, keepdims=True)
        - unit * jnp.mean(scaled * unit, axis=-1, keepdims=True)
    )
    return inverse * inner, jnp.sum(gradient * unit, axis=0)


def heads_of(rows):
    return rows.reshape(rows.shape[0], -1, HD)


def softmax(q, k, valid):
    scores = jnp.einsum(
        "lhc,nhc->hln", heads_of(q), heads_of(k), preferred_element_type=F32
    ) * (1.0 / math.sqrt(HD))
    if valid is not None:
        scores = jnp.where(valid[None, None, :], scores, MASKED)
    grown = jnp.exp(scores - jnp.max(scores, axis=-1, keepdims=True))
    return grown / jnp.sum(grown, axis=-1, keepdims=True)


def attend(inputs, source, valid, gain_q, gain_kv, proj, out):
    unit_x, inv_x = unit_rows(inputs)
    queries_in = (unit_x * gain_q).astype(BF)
    unit_s, inv_s = unit_rows(source)
    keys_in = (unit_s * gain_kv).astype(BF)
    width = inputs.shape[1]
    q = mm(queries_in, proj[:, :width]).astype(BF)
    kv = mm(keys_in, proj[:, width:]).astype(BF)
    k, v = kv[:, :width], kv[:, width:]
    soft = softmax(q, k, valid)
    mixture = jnp.einsum("hln,nhc->lhc", soft.astype(BF), heads_of(v), preferred_element_type=F32)
    mixture = mixture.reshape(inputs.shape).astype(BF)
    result = (inputs + mm(mixture, out)).astype(BF)
    return result, (unit_x, inv_x, queries_in, unit_s, inv_s, keys_in, q, k, v, soft, mixture)


def attend_back(gradient, kept, gain_q, gain_kv, proj, out):
    unit_x, inv_x, queries_in, unit_s, inv_s, keys_in, q, k, v, soft, mixture = kept
    width = gradient.shape[1]
    scale = 1.0 / math.sqrt(HD)
    grad_mix = mm_cols(gradient, out).astype(BF)
    grad_soft = jnp.einsum(
        "lhc,nhc->hln", heads_of(grad_mix), heads_of(v), preferred_element_type=F32
    )
    inner = jnp.sum(soft * grad_soft, axis=-1, keepdims=True)
    grad_scores = (soft * (grad_soft - inner)).astype(BF)
    dq = jnp.einsum("hln,nhc->lhc", grad_scores, heads_of(k), preferred_element_type=F32) * scale
    dk = jnp.einsum("hln,lhc->nhc", grad_scores, heads_of(q), preferred_element_type=F32) * scale
    dv = jnp.einsum(
        "hln,lhc->nhc", soft.astype(BF), heads_of(grad_mix), preferred_element_type=F32
    )
    dq = dq.reshape(gradient.shape).astype(BF)
    dk = dk.reshape(-1, width).astype(BF)
    dv = dv.reshape(-1, width).astype(BF)
    grad_x, gain_q_grad = norm_back(mm_cols(dq, proj[:, :width]), unit_x, inv_x, gain_q)
    back_s = mm_cols(dk, proj[:, width : 2 * width]) + mm_cols(dv, proj[:, 2 * width :])
    grad_s, gain_kv_grad = norm_back(back_s, unit_s, inv_s, gain_kv)
    pairs = ((queries_in, dq), (keys_in, dk), (keys_in, dv), (mixture, gradient))
    return grad_x, grad_s, gain_q_grad, gain_kv_grad, pairs


def feed(inputs, gain, w_in, b_in, w_down, b_out):
    unit, inverse = unit_rows(inputs)
    lowered = (unit * gain).astype(BF)
    pre_act = mm(lowered, w_in) + b_in
    active = jax.nn.gelu(pre_act).astype(BF)
    result = (inputs + mm_cols(active, w_down) + b_out).astype(BF)
    return result, (unit, inverse, lowered, pre_act, active)


def feed_back(gradient, kept, gain, w_in, w_down):
    unit, inverse, lowered, pre_act, active = kept
    grad_act = mm(gradient, w_down)
    grad_pre = jax.vjp(jax.nn.gelu, pre_act)[1](grad_act)[0].astype(BF)
    grad_x, gain_grad = norm_back(mm_cols(grad_pre, w_in), unit, inverse, gain)
    bias_grad = jnp.sum(grad_pre.astype(F32), axis=0)
    out_grad = jnp.sum(gradient.astype(F32), axis=0)
    return grad_x, gain_grad, bias_grad, out_grad, ((lowered, grad_pre), (gradient, active))


def gelu_both(value):
    factor = math.sqrt(2.0 / math.pi)
    square = value * value
    bent = jnp.tanh(factor * value * (1.0 + 0.044715 * square))
    inner = factor * (1.0 + 3.0 * 0.044715 * square)
    half = 0.5 * (1.0 + bent)
    return value * half, half + 0.5 * value * (1.0 - bent * bent) * inner


def tiles(count, body, size=256):
    def step(index, carry):
        body(pl.ds(pl.multiple_of(index * size, size), size), index)
        return carry

    lax.fori_loop(0, count, step, 0)


def norm_into(source, gain, target):
    def step(index, carry):
        here = pl.ds(pl.multiple_of(index * 32, 32), 32)
        unit, _ = unit_rows(source[here, :].astype(F32))
        target[here, :] = (unit * gain).astype(BF)
        return carry

    lax.fori_loop(0, source.shape[0] // 32, step, 0)


def gather_kernel(*refs):
    cross_proj, cross_out, mlp_in, mlp_down, self_proj, self_out = refs[:6]
    latents_in, cot_all, points_in, near_in, length_in = refs[6:11]
    vec_parts = refs[11:16]
    section_at = lax.axis_index("section")
    batch_at = lax.axis_index("batch")
    x_at = lax.rem(section_at, 2)
    y_at = section_at // 2
    ins = (
        cross_proj,
        cross_out,
        mlp_in.at[0],
        mlp_down.at[0],
        self_proj,
        self_out,
        mlp_in.at[1],
        mlp_down.at[1],
    )
    count = len(ins)
    outs = refs[16 : 16 + count]
    rest = refs[16 + count :]
    gains, norm_out, mask_in, picks_out = rest[:4]
    kept_outs = rest[4:24]
    (
        u1,
        u2,
        u3,
        u4,
        grad_top,
        xq_c,
        sn_c,
        q_c,
        k_c,
        v_c,
        o_c,
        xn_s,
        q_s,
        k_s,
        v_s,
        o_s,
        src_in,
        lowered,
        before,
        active,
        x_in,
        cot_in,
        vec_in,
        vec_rows,
        slots,
        total_rows,
        part_out,
        part_in,
        vec_out,
        biases,
        plane,
        line_in,
    ) = rest[24:56]
    (own_sem, send, recv, kin_send, kin_recv, vec_sems) = rest[56:62]
    (slot_sems, kept_sems, plane_sems, line_sems, pair_sems, row_sems) = rest[62:]
    line = 4
    core = lax.rem(batch_at, 2)
    spot = batch_at // 2
    beside = section_at + 1 - 2 * x_at
    above = lax.rem(section_at + 2, 4)
    sibling = batch_at + 1 - 2 * core
    shard = ins[0].shape[0]
    place = section_at * 2 + core
    rows = x_in.shape[0]

    def down_line(step):
        return lax.rem(spot + step, line) * 2 + core

    def up_line(step):
        return lax.rem(spot + line - step, line) * 2 + core

    near_peers = []
    for turn in range(1, 8):
        other = lax.rem(place + turn, 8)
        near_peers.append((other // 2, spot * 2 + lax.rem(other, 2)))
    line_peers = [(section_at, down_line(step)) for step in range(1, line)]
    far_peers = [(section_at, down_line(step) + 1 - 2 * core) for step in range(1, line)]
    vec_peers = [(section_at, sibling)] + line_peers + far_peers
    peers = near_peers + line_peers + far_peers
    barrier = pltpu.get_barrier_semaphore()
    for peer in peers:
        pl.semaphore_signal(barrier, inc=1, device_id=peer, device_id_type=MESH)
    pl.semaphore_wait(barrier, len(peers))

    def spread(ref, owner, first, size):
        return ref.at[pl.ds(pl.multiple_of(owner * shard, shard), shard), pl.ds(first, size)]

    def is_feed(item):
        return item % 8 >= 4

    def source_of(item, first, size):
        index, start = GATHERED[item]
        if is_feed(item):
            first = pl.multiple_of(first + y_at * outs[index].shape[1], 128)
        return ins[index].at[:, pl.ds(first, size)]

    def piece(item):
        start = GATHERED[item][1]
        if is_feed(item):
            return pl.multiple_of(start + x_at * 512, 128), 512
        return pl.multiple_of(start + section_at * 256, 128), 256

    def own_line(item, way):
        first, size = piece(item)
        return pltpu.make_async_remote_copy(
            source_of(item, first, size),
            spread(outs[GATHERED[item][0]], batch_at, first, size),
            send.at[5 * way, item, 0],
            recv.at[0, item, 3 if way else 1],
            device_id=(section_at, batch_at + (-2 if way else 2)),
            device_id_type=MESH,
        )

    def onward_line(item, step, way):
        first, size = piece(item)
        ref = spread(outs[GATHERED[item][0]], up_line(step), first, size)
        return pltpu.make_async_remote_copy(
            ref,
            ref,
            send.at[0, item, step],
            recv.at[0, item, step - 1 if way else step + 1],
            device_id=(section_at, batch_at + (-2 if way else 2)),
            device_id_type=MESH,
        )

    def came_line(item, step):
        first, size = piece(item)
        ref = spread(outs[GATHERED[item][0]], up_line(step), first, size)
        return pltpu.make_async_remote_copy(
            ref,
            ref,
            send.at[0, item, step],
            recv.at[0, item, step],
            device_id=(section_at, sibling),
            device_id_type=MESH,
        )

    def start_line(item):
        @pl.when(spot < 3)
        def _():
            own_line(item, 0).start()

        @pl.when(spot > 0)
        def _():
            own_line(item, 1).start()

    def arrive_line(item, apart):
        @pl.when(spot >= apart)
        def _():
            came_line(item, apart).wait_recv()

            @pl.when(spot < 3)
            def _():
                onward_line(item, apart, 0).start()

            for copy in near(item, apart):
                copy.start()

        @pl.when(spot + apart <= 3)
        def _():
            came_line(item, 4 - apart).wait_recv()

            @pl.when(spot > 0)
            def _():
                onward_line(item, 4 - apart, 1).start()

            for copy in near(item, 4 - apart):
                copy.start()

    def sent_line(item):
        @pl.when(spot < 3)
        def _():
            own_line(item, 0).wait_send()

        @pl.when(spot > 0)
        def _():
            own_line(item, 1).wait_send()

        for apart in (1, 2, 3):

            @pl.when(jnp.logical_and(spot >= apart, spot < 3))
            def _():
                onward_line(item, apart, 0).wait_send()

            @pl.when(jnp.logical_and(spot + apart <= 3, spot > 0))
            def _():
                onward_line(item, 4 - apart, 1).wait_send()

        for step in (1, 2, 3):
            for copy in near(item, step):
                copy.wait_send()

    def plane_copy(item, step, way, low, wide, peer):
        ref = spread(outs[GATHERED[item][0]], up_line(step), low, wide)
        return pltpu.make_async_remote_copy(
            ref,
            ref,
            send.at[way, item, step],
            recv.at[way, item, step],
            device_id=(peer, batch_at),
            device_id_type=MESH,
        )

    def near(item, step):
        first, size = piece(item)
        copies = [plane_copy(item, step, 1, first, size, beside)]
        if not is_feed(item):
            copies.append(plane_copy(item, step, 2, first, size, above))
        return copies

    def far(item, step):
        start = GATHERED[item][1]
        by_y = pl.multiple_of(start + beside * 256, 128)
        by_x = pl.multiple_of(start + above * 256 + 128, 128)
        return [
            plane_copy(item, step, 3, by_y, 128, above),
            plane_copy(item, step, 4, by_x, 128, beside),
        ]

    def kin(item, step):
        index, start = GATHERED[item]
        if step == 0:
            source = source_of(item, start, GATHER_WIDTH)
        else:
            source = spread(outs[index], up_line(step), start, GATHER_WIDTH)
        return pltpu.make_async_remote_copy(
            source,
            spread(outs[index], up_line(step), start, GATHER_WIDTH),
            kin_send.at[item, step],
            kin_recv.at[item, step],
            device_id=(section_at, sibling),
            device_id_type=MESH,
        )

    def own(item):
        index, start = GATHERED[item]
        return pltpu.make_async_copy(
            source_of(item, start, GATHER_WIDTH),
            spread(outs[index], batch_at, start, GATHER_WIDTH),
            own_sem.at[item],
        )

    def vec_copy(which):
        return pltpu.make_async_remote_copy(
            vec_in,
            vec_out.at[batch_at],
            vec_sems.at[0, which],
            vec_sems.at[1, which],
            device_id=vec_peers[which],
            device_id_type=MESH,
        )

    def slot_copy(item):
        index, start = GATHERED[item]
        return pltpu.make_async_copy(
            outs[index].at[:, pl.ds(start, GATHER_WIDTH)],
            slots.at[item % SLOTS],
            slot_sems.at[item % SLOTS],
        )

    def near_norm(turn):
        return pltpu.make_async_remote_copy(
            plane.at[8],
            plane.at[place],
            plane_sems.at[0, turn],
            plane_sems.at[1, turn],
            device_id=near_peers[turn],
            device_id_type=MESH,
        )

    def far_norm(step):
        return pltpu.make_async_remote_copy(
            line_in.at[4],
            line_in.at[spot],
            line_sems.at[0, step],
            line_sems.at[1, step],
            device_id=line_peers[step],
            device_id_type=MESH,
        )

    def rows_over(layer):
        return pltpu.make_async_remote_copy(
            lowered.at[layer, pl.ds(0, rows)],
            lowered.at[layer, pl.ds(rows, rows)],
            pair_sems.at[0, layer, 0],
            pair_sems.at[1, layer, 0],
            device_id=(above, batch_at),
            device_id_type=MESH,
        )

    def part_over(layer):
        return pltpu.make_async_remote_copy(
            part_out.at[layer],
            part_in.at[layer],
            pair_sems.at[0, layer, 1],
            pair_sems.at[1, layer, 1],
            device_id=(above, batch_at),
            device_id_type=MESH,
        )

    steps = range(1, line)
    total = len(GATHERED)
    started = []

    def launch(copies):
        for copy in copies:
            copy.start()
        started.extend(copies)

    kept = (
        (u1, u2, u3, u4, grad_top)
        + (xq_c, sn_c, q_c, k_c, v_c, o_c)
        + (xn_s, q_s, k_s, v_s, o_s)
        + (src_in, lowered, before, active)
    )
    names = {id(ref): place for place, ref in enumerate(kept)}

    def keep(*chosen):
        for ref in chosen:
            index = names[id(ref)]
            pltpu.make_async_copy(ref, kept_outs[index], kept_sems.at[index]).start(priority=LOCAL)

    def row(index):
        return gains[index : index + 1, :]

    def project(source, target, slot):
        def tile(columns, _):
            target[:, columns] = mm(source[...], slots[slot, :, columns]).astype(BF)

        tiles(2, tile, 512)

    def heads(q, k, v, o, masked):
        def head(index, carry):
            here = pl.ds(pl.multiple_of(index * HD, HD), HD)
            scores = mm_cols(q[:, here], k[:, here]) * (1.0 / math.sqrt(HD))
            if masked:
                scores = jnp.where(mask_in[...] > 0.0, scores, MASKED)
            grown = jnp.exp(scores - jnp.max(scores, axis=-1, keepdims=True))
            soft = grown / jnp.sum(grown, axis=-1, keepdims=True)
            o[:, here] = mm(soft.astype(BF), v[:, here]).astype(BF)
            return carry

        lax.fori_loop(0, q.shape[1] // HD, head, 0)

    def close_attention(inputs, o, target, slot):
        def tile(columns, _):
            target[:, columns] = (
                inputs[:, columns].astype(F32) + mm(o[...], slots[slot, :, columns])
            ).astype(BF)

        tiles(2, tile, 512)

    def feed_up(layer, chunk, slot):
        def tile(columns, index):
            first = chunk * GATHER_WIDTH + index * 512
            there = pl.ds(pl.multiple_of(first, 512), 512)
            lanes = pl.ds(pl.multiple_of(y_at * 2048 + first, 512), 512)
            value = mm(lowered[layer], slots[slot, :, columns]) + biases[layer : layer + 1, lanes]
            active_part, slope = gelu_both(value)
            before[layer, :, there] = slope
            active[layer, :, there] = active_part.astype(BF)

        tiles(2, tile, 512)

    def feed_down(layer, chunk, slot):
        chosen = pl.ds(chunk * GATHER_WIDTH, GATHER_WIDTH)

        def tile(columns, _):
            value = mm_cols(active[layer, :, chosen], slots[slot, columns, :])
            if chunk == 0:
                total_rows[:, columns] = value
            else:
                value = total_rows[:, columns] + value
                total_rows[:, columns] = value
                part_out[layer, :, columns] = value[rows:].astype(BF)

        tiles(2, tile, 512)

    def feed_close(layer):
        inputs, target = (u1, u3)[layer], (u2, u4)[layer]
        part_over(layer).wait_recv()

        def tile(columns, _):
            target[:, columns] = (
                inputs[:, columns].astype(F32)
                + (total_rows[0:rows, columns] + part_in[layer, :, columns].astype(F32))
                + gains[5 + layer : 6 + layer, columns]
            ).astype(BF)

        tiles(2, tile, 512)
        keep(target)

    def work(item):
        slot_copy(item).wait()
        slot = item % SLOTS
        layer, stage = item // 8, item % 8
        inputs = (x_in, u2)[layer]
        middle = (u1, u3)[layer]
        q, k, v, o = ((q_c, k_c, v_c, o_c), (q_s, k_s, v_s, o_s))[layer]
        if stage == 0:
            if layer == 0:
                norm_into(x_in, row(0), xq_c)
                norm_into(src_in, row(1), sn_c)
                keep(xq_c, sn_c)
            else:
                feed_close(0)
                norm_into(u2, row(2), xn_s)
                keep(xn_s)
            project((xq_c, xn_s)[layer], q, slot)
        elif stage == 1:
            project((sn_c, xn_s)[layer], k, slot)
        elif stage == 2:
            project((sn_c, xn_s)[layer], v, slot)
            heads(q, k, v, o, layer == 0)
            keep(q, k, v, o)
        elif stage == 3:
            close_attention(inputs, o, middle, slot)
            norm_into(middle, row(3 + layer), lowered.at[layer, pl.ds(0, rows)])
            launch([rows_over(layer)])
            keep(middle)
        elif stage % 2 == 0:
            if stage == 4:
                rows_over(layer).wait_recv()
            feed_up(layer, (stage - 4) // 2, slot)
        else:
            feed_down(layer, (stage - 4) // 2, slot)
            if stage == 7:
                launch([part_over(layer)])

    for item in range(AHEAD):
        start_line(item)
    here = pl.ds(pl.multiple_of(section_at * rows, rows), rows)
    row_copies = [
        pltpu.make_async_copy(latents_in.at[here], x_in, row_sems.at[0]),
        pltpu.make_async_copy(cot_all.at[here], cot_in, row_sems.at[1]),
    ]
    for copy in row_copies:
        copy.start()
    cross_gain, self_gain, feed_gain, out_bias, in_bias = vec_parts
    vec_rows[...] = jnp.zeros_like(vec_rows)
    vec_rows[0:2, :] = cross_gain[...].astype(F32)
    vec_rows[2:3, :] = self_gain[...].astype(F32)
    vec_rows[3:5, :] = feed_gain[...].astype(F32)
    vec_rows[5:7, :] = out_bias[...].astype(F32)
    bias_rows = in_bias[...].astype(F32)
    for layer in range(2):
        for part_at in range(4):
            index = 7 + 4 * layer + part_at
            vec_rows[index : index + 1, :] = bias_rows[
                layer : layer + 1, part_at * 128 : part_at * 128 + 128
            ]
    vec_in[...] = vec_rows[...].astype(BF)
    vec_out[batch_at] = vec_in[...]
    for which in range(7):
        vec_copy(which).start()
    lanes = lax.broadcasted_iota(jnp.int32, (1, rows), 1)
    length = length_in[pl.ds(section_at, 1), :]
    mask_in[...] = jnp.where(lanes < length, 1.0, 0.0)
    point_at = lax.broadcasted_iota(jnp.int32, (points_in.shape[0], rows), 0)
    wanted = near_in[pl.ds(section_at, 1), :]
    picks = jnp.where(point_at == wanted, 1.0, 0.0)
    picks_out[...] = picks.astype(BF)
    turned = picks.T.astype(BF)

    def source_tile(columns, _):
        src_in[:, columns] = mm(turned, points_in[:, columns]).astype(BF)

    tiles(2, source_tile, 512)
    keep(src_in)
    for copy in row_copies:
        copy.wait()
    for moment in range(-2, total + 4):
        if moment + 2 + AHEAD < total:
            start_line(moment + 2 + AHEAD)
        for apart in (1, 2, 3):
            if 0 <= moment + 3 - apart < total:
                arrive_line(moment + 3 - apart, apart)
        if 0 <= moment < total:
            own(moment).start(priority=LOCAL)
            launch([kin(moment, 0)])
        if 0 <= moment - 1 < total:
            for step in steps:
                if is_feed(moment - 1):
                    near(moment - 1, step)[0].wait_recv()
                    launch([kin(moment - 1, step)])
                else:
                    for copy, onward in zip(near(moment - 1, step), far(moment - 1, step)):
                        copy.wait_recv()
                        launch([onward])
        if 0 <= moment - 2 < total and not is_feed(moment - 2):
            for step in steps:
                for copy in far(moment - 2, step):
                    copy.wait_recv()
                launch([kin(moment - 2, step)])
        if moment == 2:
            for which in range(7):
                vec_copy(which).wait()
            for owner in range(8):
                values = vec_out[owner].astype(F32)
                gains[:, owner * 128 : owner * 128 + 128] = values
                for layer in range(2):
                    for part_at in range(4):
                        first = owner * 512 + part_at * 128
                        index = 7 + 4 * layer + part_at
                        biases[layer : layer + 1, first : first + 128] = values[index : index + 1]
        if 0 <= moment - 4 < total:
            work(moment - 4)
        if 0 <= moment - 3 < total:
            own(moment - 3).wait()
            for step in range(line):
                kin(moment - 3, step).wait_recv()
            slot_copy(moment - 3).start(priority=LOCAL)
    keep(lowered, before, active)
    feed_close(1)

    def square(index, carry):
        here = pl.ds(pl.multiple_of(index * 32, 32), 32)
        values = u4[here, :].astype(F32)
        return carry + jnp.sum(values * values, axis=0, keepdims=True)

    squares = lax.fori_loop(0, u4.shape[0] // 32, square, jnp.zeros((1, u4.shape[1]), F32))
    mean = jnp.sum(squares, axis=1, keepdims=True) / (u4.shape[0] * u4.shape[1])
    group_norm = jnp.sqrt(mean + EPSILON)
    plane[8] = jnp.broadcast_to(group_norm, plane.shape[1:])
    for turn in range(7):
        near_norm(turn).start()
    plane[place] = plane[8]
    for turn in range(7):
        near_norm(turn).wait()
    line_in[4] = jnp.sum(plane[0:8], axis=0)
    for step in range(3):
        far_norm(step).start()
    line_in[spot] = line_in[4]
    for step in range(3):
        far_norm(step).wait()
    norm_mean = jnp.sum(line_in[0:4], axis=0) / 32.0
    norm_out[...] = norm_mean
    ratio = norm_mean[0:1, 0:1] / group_norm

    def top(index, carry):
        here = pl.ds(pl.multiple_of(index * 32, 32), 32)
        grad_top[here, :] = (
            cot_in[here, :].astype(F32) + ratio * u4[here, :].astype(F32)
        ).astype(BF)
        return carry

    lax.fori_loop(0, u4.shape[0] // 32, top, 0)
    keep(grad_top)
    for index, ref in enumerate(kept):
        pltpu.make_async_copy(ref, kept_outs[index], kept_sems.at[index]).wait()
    for item in range(total):
        sent_line(item)
    for copy in started:
        copy.wait_send()


def gather_forward(blocks, latents, cotangent, points, near, lengths, vectors):
    width = latents.shape[1]
    rows = near.shape[1]
    half = blocks[2].shape[2] // 2
    widths = (3 * width, width, half, half) * 2
    total = len(GATHERED)
    anywhere = pl.BlockSpec(memory_space=pl.ANY)
    vmem = pl.BlockSpec(memory_space=pltpu.VMEM)
    plain = ((rows, width), BF)
    kept = [plain] * 17 + [
        ((2, 2 * rows, width), BF),
        ((2, 2 * rows, half), F32),
        ((2, 2 * rows, half), BF),
    ]
    dma = pltpu.SemaphoreType.DMA
    return pl.pallas_call(
        gather_kernel,
        out_shape=[jax.ShapeDtypeStruct((width, size), BF) for size in widths]
        + [
            jax.ShapeDtypeStruct((16, width), F32),
            jax.ShapeDtypeStruct((8, 128), F32),
            jax.ShapeDtypeStruct((1, rows), F32),
            jax.ShapeDtypeStruct((points.shape[0], rows), BF),
        ]
        + [jax.ShapeDtypeStruct(*one) for one in kept],
        in_specs=[anywhere] * (len(blocks) + 2) + [vmem] * 8,
        out_specs=[anywhere] * len(widths) + [vmem] * 4 + [anywhere] * len(kept),
        scratch_shapes=[pltpu.VMEM(*one) for one in kept]
        + [
            pltpu.VMEM((rows, width), BF),
            pltpu.VMEM((rows, width), BF),
            pltpu.VMEM((16, 128), BF),
            pltpu.VMEM((16, 128), F32),
            pltpu.VMEM((SLOTS, width, GATHER_WIDTH), BF),
            pltpu.VMEM((2 * rows, width), F32),
            pltpu.VMEM((2, rows, width), BF),
            pltpu.VMEM((2, rows, width), BF),
            pltpu.VMEM((8, 16, 128), BF),
            pltpu.VMEM((2, 2 * half), F32),
            pltpu.VMEM((9, 8, 128), F32),
            pltpu.VMEM((5, 8, 128), F32),
            dma((total,)),
            dma((6, total, 4)),
            dma((5, total, 4)),
            dma((total, 4)),
            dma((total, 4)),
            dma((2, 7)),
            dma((SLOTS,)),
            dma((len(kept),)),
            dma((2, 7)),
            dma((2, 3)),
            dma((2, 2, 2)),
            dma((2,)),
        ],
        compiler_params=pltpu.CompilerParams(
            collective_id=1, has_side_effects=True, vmem_limit_bytes=56 * 2**20
        ),
        cost_estimate=pl.CostEstimate(
            flops=2 * rows * width * sum(widths), bytes_accessed=2**27, transcendentals=2**21
        ),
    )(*blocks, latents, cotangent, points, near, lengths, *vectors)


ITEM_COUNT = 16
WINDOWS = 4
STAGES = 3


def reduce_kernel(*refs):
    total = ITEM_COUNT
    (
        proj_c,
        out_c,
        in_0,
        down_0,
        proj_s,
        out_s,
        in_1,
        down_1,
        u1_in,
        u2_in,
        u3_in,
        last_ref,
        top_in,
        xq_c,
        sn_c,
        q_c,
        k_c,
        v_c,
        o_c,
        xn_s,
        q_s,
        k_s,
        v_s,
        o_s,
        lowered,
        before,
        active,
        latents_in,
        src_in,
        gains,
        mask_in,
        picks_in,
    ) = refs[:32]
    (up_out, down_out, proj_out_c, proj_out_s, end_out_c, end_out_s) = refs[32:38]
    (last_out, first_out, point_out, small_out) = refs[38:42]
    (grads_h, kin_lf, kin_la, kin_rf, kin_ra) = refs[42:47]
    (
        lwin_f,
        lwin_a,
        raw,
        rwin,
        stage,
        merged_f,
        merged_a,
        passing,
        lined_f,
        lined_a,
        crossed_f,
        crossed_a,
        pair,
        slope,
        rows_sum,
        hbuf,
        slots,
        qb,
        kb,
        vb,
        dob,
        dqkv,
        part_out,
        part_in,
        grad,
        ub,
        point_in,
        point_sum,
        small_in,
        small_sum,
    ) = refs[47:77]
    (
        kin_l_sems,
        kin_r_sems,
        raw_sems,
        win_sems,
        xy_sems,
        line_send,
        line_recv,
        cross_sems,
        out_sems,
        own_sems,
        lat_sems,
        far_sems,
        lat_own,
        point_sems,
        deal_sems,
        point_own,
        small_sems,
        pair_sems,
        slot_sems,
        h_sem,
        save_sems,
        act_sems,
    ) = refs[77:]
    section_at = lax.axis_index("section")
    batch_at = lax.axis_index("batch")
    core = lax.rem(batch_at, 2)
    spot = batch_at // 2
    x_at = lax.rem(section_at, 2)
    y_at = section_at // 2
    beside = section_at + 1 - 2 * x_at
    above = lax.rem(section_at + 2, 4)
    across = lax.rem(beside + 2, 4)
    sibling = batch_at + 1 - 2 * core
    flat = (beside, above)
    bits = (x_at, y_at)
    rows, width = 256, 1024

    peers = [(beside, batch_at), (above, batch_at), (across, batch_at), (section_at, sibling)]
    peers += [(section_at, lax.rem(spot + step, 4) * 2 + core) for step in (1, 2, 3)]
    barrier = pltpu.get_barrier_semaphore()
    for peer in peers:
        pl.semaphore_signal(barrier, inc=1, device_id=peer, device_id_type=MESH)
    pl.semaphore_wait(barrier, len(peers))

    def remote(source, target, sems, where, peer):
        return pltpu.make_async_remote_copy(
            source,
            target,
            sems.at[(0, *where)],
            sems.at[(1, *where)],
            device_id=peer,
            device_id_type=MESH,
        )

    feed_left = (pair, lowered.at[1], pair, lowered.at[0])
    feed_right = (active.at[1], slope, active.at[0], slope)
    att_left = (o_s, xn_s, xn_s, xn_s, o_c, xq_c, sn_c, sn_c)
    att_right = tuple(
        ref
        for turn in range(2)
        for ref in (grads_h.at[turn], dqkv.at[0], dqkv.at[1], dqkv.at[2])
    )

    def columns(spot_of, parity):
        return pl.ds(pl.multiple_of((2 * spot_of + parity) * 128, 128), 128)

    def kin_lefts(feed, job):
        source, target = (feed_left, kin_lf) if feed else (att_left, kin_la)
        return [
            remote(
                source[job].at[:, columns(part, 1 - core)],
                target.at[job, part],
                kin_l_sems,
                (job if feed else 4 + job, part),
                (section_at, sibling),
            )
            for part in range(4)
        ]

    def kin_right(feed, job, chunk):
        if feed:
            here = pl.ds(chunk * 1024, 1024)
            source, target = feed_right[job].at[:, here], kin_rf.at[job, :, here]
        else:
            source, target = att_right[job], kin_ra.at[job]
        where = (2 * job + chunk if feed else 8 + job,)
        return remote(source, target, kin_r_sems, where, (section_at, sibling))

    def item_of(index):
        turn, inner = index // 8, index % 8
        if inner < 4:
            return True, 2 * turn + inner // 2, inner % 2
        return False, 4 * turn + inner - 4, 0

    def window_copies(index):
        feed, job, chunk = item_of(index)
        slot = index % WINDOWS
        size = 512 if feed else 256
        if feed:
            here = pl.ds(chunk * 1024, 1024)
            sources = (feed_right[job].at[:, here], kin_rf.at[job, :, here])
        else:
            sources = (att_right[job], kin_ra.at[job])
        return [
            pltpu.make_async_copy(
                sources[whose],
                rwin.at[slot, pl.ds(whose * size, size)],
                win_sems.at[slot, whose],
            )
            for whose in range(2)
        ]

    def load(index):
        feed, job, chunk = item_of(index)
        kin_right(feed, job, chunk).wait_recv()
        for copy in window_copies(index):
            copy.start(priority=LOCAL)
        if chunk == 0:
            for copy in kin_lefts(feed, job):
                copy.wait_recv()
            size = 512 if feed else 256
            own_left = (feed_left if feed else att_left)[job]
            kin_left = (kin_lf if feed else kin_la).at[job]
            target = (lwin_f if feed else lwin_a).at[job]
            for part in range(4):
                copies = [
                    pltpu.make_async_copy(
                        own_left.at[:, columns(part, core)],
                        raw.at[part, 0, pl.ds(0, size)],
                        raw_sems.at[part, 0],
                    ),
                    pltpu.make_async_copy(
                        kin_left.at[part], raw.at[part, 1, pl.ds(0, size)], raw_sems.at[part, 1]
                    ),
                ]
                for copy in copies:
                    copy.start(priority=LOCAL)
            for part in range(4):
                for whose, source in enumerate(
                    (own_left.at[:, columns(part, core)], kin_left.at[part])
                ):
                    place = raw.at[part, whose, pl.ds(0, size)]
                    pltpu.make_async_copy(source, place, raw_sems.at[part, whose]).wait()
                    target[part, :, whose * size : whose * size + size] = place[...].T

    def is_feed(item):
        return lax.rem(item, 8) < 4

    def feed_job(item):
        return 2 * (item // 8) + lax.rem(item, 8) // 2

    def att_job(item):
        return 4 * (item // 8) + lax.rem(item, 8) - 4

    def loaded(slot, feed):
        size = 512 if feed else 256
        for whose in range(2):
            source = kin_rf.at[0, :, pl.ds(0, 1024)] if feed else kin_ra.at[0]
            pltpu.make_async_copy(
                source, rwin.at[slot, pl.ds(whose * size, size)], win_sems.at[slot, whose]
            ).wait()

    def by_kind(item, action):
        pl.when(is_feed(item))(functools.partial(action, item, True))
        pl.when(jnp.logical_not(is_feed(item)))(functools.partial(action, item, False))

    def merged_of(item, feed):
        return merged_f.at[lax.rem(item, 4)] if feed else merged_a.at[att_job(item)]

    def passing_of(item, feed, slot):
        ref = passing.at[lax.rem(item, 8), slot]
        return ref if feed else ref.at[:, pl.ds(0, 512)]

    def lined_of(item, feed):
        return lined_f.at[lax.rem(item, 4)] if feed else lined_a.at[att_job(item)]

    def crossed_of(item, feed):
        return crossed_f.at[lax.rem(item, 4)] if feed else crossed_a.at[att_job(item)]

    def products(item, choice, store):
        slot = lax.rem(item, WINDOWS)

        def quarter(index, carry):
            upper, part = index // 2, lax.rem(index, 2)
            here = pl.ds(pl.multiple_of(part * 256, 256), 256)
            bit = choice[0] + part * (choice[1] - choice[0])
            first = pl.multiple_of(part * 512 + bit * 256, 256)
            left = lwin_a[att_job(item), pl.ds(upper * 2, 2)].reshape(256, 512)
            right = rwin[slot, 0:512, pl.ds(first, 256)]
            tile = jnp.dot(left, right, preferred_element_type=F32).reshape(2, 128, 256)
            store(pl.ds(upper * 2, 2), here, tile)
            return carry

        lax.fori_loop(0, 4, quarter, 0)

    def xy_copies(item):
        return [
            remote(
                stage.at[lax.rem(att_job(item), STAGES), :, :, pl.ds(side * 256, 256)],
                merged_a.at[att_job(item), :, :, pl.ds(side * 256, 256)],
                xy_sems,
                (att_job(item), side),
                (flat[side], batch_at),
            )
            for side in range(2)
        ]

    def xy_sent(item):
        for copy in xy_copies(item):
            copy.wait_send()

    def line_copy(item, feed, dest, place, rightward):
        step = 1 if rightward else -1
        slot = 4 if not rightward and place - 1 == dest else dest
        return pltpu.make_async_remote_copy(
            merged_of(item, feed).at[dest],
            passing_of(item, feed, slot),
            line_send.at[item, dest],
            line_recv.at[item, slot],
            device_id=(section_at, batch_at + 2 * step),
            device_id_type=MESH,
        )

    def line_wait(item, feed, slot):
        pltpu.make_async_remote_copy(
            merged_of(item, feed).at[0],
            passing_of(item, feed, slot),
            line_send.at[item, 0],
            line_recv.at[item, slot],
            device_id=(section_at, sibling),
            device_id_type=MESH,
        ).wait_recv()

    def line_sent(item, feed):
        for step in (1, 2, 3):
            dest = lax.rem(spot + step, 4)
            pltpu.make_async_remote_copy(
                merged_of(item, feed).at[dest],
                passing_of(item, feed, 0),
                line_send.at[item, dest],
                line_recv.at[item, 0],
                device_id=(section_at, sibling),
                device_id_type=MESH,
            ).wait_send()

    def outset(item, feed):
        @pl.when(spot == 0)
        def _():
            for dest in (3, 2, 1):
                line_copy(item, feed, dest, 0, True).start()

        @pl.when(spot == 3)
        def _():
            for dest in (0, 1, 2):
                line_copy(item, feed, dest, 3, False).start()

    def drained(item, feed):
        line_sent(item, feed)
        if feed:
            feed_out(item, up_out).wait()
            feed_own(item, up_out).wait()
        else:
            for side in range(2):
                att_out(item, side, end_out_s, 0).wait()
                att_own(item, side, end_out_s, 0).wait()

    def offer(item, feed):
        slot = lax.rem(item, WINDOWS)
        loaded(slot, feed)
        if feed:

            @pl.when(item >= 8)
            def _():
                drained(item - 8, True)

            target = merged_of(item, True)

            def tile(index, carry):
                upper, part = index // 4, lax.rem(index, 4)
                here = pl.ds(pl.multiple_of(part * 256, 256), 256)
                left = lwin_f[feed_job(item), pl.ds(upper * 2, 2)].reshape(256, 1024)
                right = rwin[slot, :, here]
                value = jnp.dot(left, right, preferred_element_type=F32)
                target[pl.ds(upper * 2, 2), :, here] = value.reshape(2, 128, 256).astype(BF)
                return carry

            lax.fori_loop(0, 8, tile, 0)
            outset(item, True)
        else:

            @pl.when(lax.rem(item, 8) >= 4 + STAGES)
            def _():
                xy_sent(item - STAGES)

            @pl.when(jnp.logical_and(item >= 12, lax.rem(item, 8) < 4 + STAGES))
            def _():
                xy_sent(item - STAGES - 4)

            def store(blocks, here, tile):
                stage[lax.rem(att_job(item), STAGES), blocks, :, here] = tile.astype(BF)

            products(item, (1 - x_at, 1 - y_at), store)
            for copy in xy_copies(item):
                copy.start()

    def take(item):
        for copy in xy_copies(item):
            copy.wait_recv()
        target = merged_a.at[att_job(item)]

        def store(blocks, here, tile):
            target[blocks, :, here] = (tile + target[blocks, :, here].astype(F32)).astype(BF)

        products(item, bits, store)
        outset(item, False)

    def first(item):
        pl.when(jnp.logical_not(is_feed(item)))(functools.partial(take, item))

    def relay(item, feed, dest, place, rightward):
        line_wait(item, feed, dest)
        target = merged_of(item, feed)
        arrived = passing_of(item, feed, dest)
        target[dest] = (target[dest].astype(F32) + arrived[...].astype(F32)).astype(BF)
        line_copy(item, feed, dest, place, rightward).start()

    def second_of(item, feed):
        @pl.when(spot == 1)
        def _():
            for dest in (3, 2):
                relay(item, feed, dest, 1, True)

        @pl.when(spot == 2)
        def _():
            for dest in (0, 1):
                relay(item, feed, dest, 2, False)

    def third_of(item, feed):
        @pl.when(spot == 1)
        def _():
            relay(item, feed, 0, 1, False)

        @pl.when(spot == 2)
        def _():
            relay(item, feed, 3, 2, True)

    def second(item):
        by_kind(item, second_of)

    def third(item):
        by_kind(item, third_of)

    def feed_cross(item):
        return remote(
            lined_of(item, True),
            crossed_of(item, True),
            cross_sems,
            (item, 0),
            (beside, batch_at),
        )

    def cross_copy(item, side):
        here = pl.ds(side * 256, 256)
        return remote(
            lined_of(item, False).at[:, here],
            crossed_of(item, False).at[:, here],
            cross_sems,
            (item, side),
            (flat[1 - side], batch_at),
        )

    def layer_of(item):
        return 1 - item // 8

    def feed_place(item, target):
        base = y_at * 2048 + lax.rem(item, 2) * 1024
        return target.at[layer_of(item), :, pl.ds(pl.multiple_of(base, 1024), 1024)]

    def feed_out(item, target):
        return remote(
            lined_of(item, True),
            feed_place(item, target),
            out_sems,
            (item, 0),
            (above, batch_at),
        )

    def feed_own(item, target):
        return pltpu.make_async_copy(
            lined_of(item, True), feed_place(item, target), own_sems.at[item, 0]
        )

    def feed_write(item):
        @pl.when(lax.rem(item, 8) < 2)
        def _():
            feed_out(item, down_out).start()
            feed_own(item, down_out).start(priority=LOCAL)

        @pl.when(lax.rem(item, 8) >= 2)
        def _():
            feed_out(item, up_out).start()
            feed_own(item, up_out).start(priority=LOCAL)

    def att_place(item, side, target, inner):
        base = inner * 1024 + side * 512 + bits[side] * 256
        return target.at[:, pl.ds(pl.multiple_of(base, 256), 256)]

    def att_out(item, side, target, inner):
        return remote(
            lined_of(item, False).at[:, pl.ds(side * 256, 256)],
            att_place(item, side, target, inner),
            out_sems,
            (item, side),
            (flat[side], batch_at),
        )

    def att_own(item, side, target, inner):
        return pltpu.make_async_copy(
            lined_of(item, False).at[:, pl.ds(side * 256, 256)],
            att_place(item, side, target, inner),
            own_sems.at[item, side],
        )

    def att_write(item):
        inner = lax.rem(item, 8) - 5
        for turn, proj, end in ((0, proj_out_s, end_out_s), (1, proj_out_c, end_out_c)):

            @pl.when(jnp.logical_and(item // 8 == turn, inner >= 0))
            def _():
                for side in range(2):
                    att_out(item, side, proj, inner).start()
                    att_own(item, side, proj, inner).start(priority=LOCAL)

            @pl.when(jnp.logical_and(item // 8 == turn, inner < 0))
            def _():
                for side in range(2):
                    att_out(item, side, end, 0).start()
                    att_own(item, side, end, 0).start(priority=LOCAL)

    def close_of(item, feed):
        for place in range(4):

            @pl.when(spot == place)
            def _():
                value = merged_of(item, feed)[place].astype(F32)
                if place > 0:
                    line_wait(item, feed, place)
                    value += passing_of(item, feed, place)[...].astype(F32)
                if place < 3:
                    line_wait(item, feed, 4)
                    value += passing_of(item, feed, 4)[...].astype(F32)
                lined_of(item, feed)[...] = value.astype(BF)

        if feed:
            feed_cross(item).start()
        else:
            for side in range(2):
                cross_copy(item, side).start()

    def close(item):
        by_kind(item, close_of)

    def finish_of(item, feed):
        if feed:
            feed_cross(item).wait()
        else:
            for side in range(2):
                cross_copy(item, side).wait()
        target = lined_of(item, feed)
        target[...] = (
            target[...].astype(F32) + crossed_of(item, feed)[...].astype(F32)
        ).astype(BF)
        if feed:
            feed_write(item)
        else:
            att_write(item)

    def finish(item):
        by_kind(item, finish_of)

    def small_copy(phase):
        if phase == 0:
            peer = (section_at, sibling)
        elif phase < 3:
            peer = (flat[phase - 1], batch_at)
        else:
            peer = (section_at, lax.rem(spot + phase - 2, 4) * 2 + core)
        return remote(
            small_sum.at[min(phase, 3)], small_in.at[phase], small_sems, (phase,), peer
        )

    quarter_rows = pair.shape[0] // 4

    def point_copy(which):
        peer = (beside, above, across)[which]
        return remote(
            pair.at[pl.ds(pl.multiple_of(peer * quarter_rows, 128), quarter_rows)],
            point_in.at[which],
            point_sems,
            (which,),
            (peer, batch_at),
        )

    def point_place():
        return point_out.at[pl.ds(pl.multiple_of(section_at * quarter_rows, 128), quarter_rows)]

    def point_deal(which):
        peer = (beside, above, across)[which]
        return remote(point_sum, point_place(), deal_sems, (which,), (peer, batch_at))

    def point_local():
        return pltpu.make_async_copy(point_sum, point_place(), point_own.at[0])

    pairs = ((last_ref, last_out), (grad, first_out))

    def lat_copy(which, way):
        source, target = pairs[which]
        return remote(
            source,
            target.at[pl.ds(pl.multiple_of(section_at * rows, rows), rows)],
            lat_sems,
            (which, way),
            (flat[way], batch_at),
        )

    def lat_far(which):
        target = pairs[which][1]
        part = target.at[pl.ds(pl.multiple_of(above * rows, rows), rows)]
        return remote(part, part, far_sems, (which, 0), (beside, batch_at))

    def lat_local(which):
        source, target = pairs[which]
        return pltpu.make_async_copy(
            source,
            target.at[pl.ds(pl.multiple_of(section_at * rows, rows), rows)],
            lat_own.at[which],
        )

    def lat_start(which):
        lat_local(which).start(priority=LOCAL)
        for way in range(2):
            lat_copy(which, way).start()

    def lat_onward(which):
        lat_copy(which, 1).wait_recv()
        lat_far(which).start()
        lat_copy(which, 0).wait_recv()

    loads = []
    for turn, (proj, out, up, down) in enumerate(
        ((proj_s, out_s, in_1, down_1), (proj_c, out_c, in_0, down_0))
    ):
        for chunk in range(2):
            loads += [down.at[:, pl.ds(chunk * 1024, 1024)], up.at[:, pl.ds(chunk * 1024, 1024)]]
        loads.append(out)
        loads += [proj.at[:, pl.ds(which * 1024, 1024)] for which in range(3)]

    def slot_copy(index):
        return pltpu.make_async_copy(loads[index], slots.at[index % 2], slot_sems.at[index % 2])

    def opened(index):
        slot_copy(index).wait()
        return index % 2

    def closed(index):
        if index + 2 < len(loads):
            slot_copy(index + 2).start(priority=LOCAL)

    def h_copy(index):
        layer, chunk = 1 - index // 2, index % 2
        return pltpu.make_async_copy(
            before.at[layer, :, pl.ds(chunk * 1024, 1024)], hbuf, h_sem.at[0]
        )

    def pair_over(turn):
        return remote(
            pair.at[pl.ds(0, rows)],
            pair.at[pl.ds(rows, rows)],
            pair_sems,
            (turn, 0),
            (above, batch_at),
        )

    def part_over(turn):
        return remote(
            part_out.at[turn], part_in.at[turn], pair_sems, (turn, 1), (above, batch_at)
        )

    def grad_saved(turn):
        return pltpu.make_async_copy(grad, grads_h.at[turn], save_sems.at[0])

    def act_copies(turn):
        chosen = ((q_s, k_s, v_s), (q_c, k_c, v_c))[turn]
        return [
            pltpu.make_async_copy(source, target, act_sems.at[index])
            for index, (source, target) in enumerate(zip(chosen, (qb, kb, vb)))
        ]

    def row_copy(index):
        if index == 3:
            source = latents_in.at[pl.ds(pl.multiple_of(section_at * rows, rows), rows)]
        else:
            source = (u3_in, u2_in, u1_in)[index]
        return pltpu.make_async_copy(source, ub, act_sems.at[3])

    def small_row(index, value):
        small_sum[0, index : index + 1, :] = value

    def open_pair(turn):
        pair[0:rows, :] = grad[...]
        pair_over(turn).start()

    def pair_ready(turn):
        pair_over(turn).wait()
        for copy in kin_lefts(True, 2 * turn):
            copy.start()

    def feed_chunk(turn, chunk):
        layer = 1 - turn
        base = 8 * turn + 2 * chunk
        h_copy(2 * turn + chunk).wait()
        if turn == 1:
            kin_right(True, 1, chunk).wait_send()
        slot = opened(base)

        def up_tile(here, index):
            there = pl.ds(pl.multiple_of(chunk * 1024 + index * 256, 256), 256)
            value = mm(pair[...], slots[slot, :, here]) * hbuf[:, here]
            short = value.astype(BF)
            slope[:, there] = short
            column = jnp.sum(short.astype(F32), axis=0, keepdims=True)
            for half in range(2):
                index_at = 7 + 4 * layer + 2 * half + chunk
                small_sum[0, index_at : index_at + 1, here] = jnp.where(
                    y_at == half, column, jnp.zeros_like(column)
                )

        tiles(4, up_tile)
        closed(base)
        if 2 * turn + chunk + 1 < 4:
            h_copy(2 * turn + chunk + 1).start(priority=LOCAL)
        kin_right(True, 2 * turn + 1, chunk).start()
        slot = opened(base + 1)

        def down_tile(there, _):
            value = mm_cols(slope[:, chunk * 1024 : chunk * 1024 + 1024], slots[slot, there, :])
            if chunk == 0:
                rows_sum[:, there] = value
            else:
                value = rows_sum[:, there] + value
                rows_sum[:, there] = value
                part_out[turn, :, there] = value[rows:].astype(BF)

        tiles(4, down_tile)
        closed(base + 1)
        if chunk == 1:
            if turn == 0:
                for copy in kin_lefts(True, 0):
                    copy.wait_send()
            part_over(turn).start()

    def row_steps(body, count):
        zero = jnp.zeros((1, width), F32)

        def step(index, carry):
            here = pl.ds(pl.multiple_of(index * 32, 32), 32)
            return tuple(a + b for a, b in zip(carry, body(here)))

        return lax.fori_loop(0, rows // 32, step, (zero,) * count)

    def lean(back, unit, inverse, gain):
        scaled = back * gain
        inner = (
            scaled
            - jnp.mean(scaled, axis=-1, keepdims=True)
            - unit * jnp.mean(scaled * unit, axis=-1, keepdims=True)
        )
        return inverse * inner, jnp.sum(back * unit, axis=0, keepdims=True)

    def feed_end(turn):
        layer = 1 - turn
        gain = gains[3 + layer : 4 + layer, :]
        part_over(turn).wait_recv()
        row_copy(2 * turn).wait()

        def body(here):
            unit, inverse = unit_rows(ub[here, :].astype(F32))
            back = rows_sum[here, :] + part_in[turn, here, :].astype(F32)
            dx, gain_part = lean(back, unit, inverse, gain)
            old = grad[here, :].astype(F32)
            grad[here, :] = (old + dx).astype(BF)
            return gain_part, jnp.sum(old, axis=0, keepdims=True)

        gain_grad, out_grad = row_steps(body, 2)
        row_copy(2 * turn + 1).start(priority=LOCAL)
        small_row(3 + layer, gain_grad)
        small_row(5 + layer, out_grad)
        grad_saved(turn).start(priority=LOCAL)
        for copy in kin_lefts(False, 4 * turn):
            copy.start()
        slot = opened(8 * turn + 4)

        def tile(there, _):
            dob[:, there] = mm_cols(grad[...], slots[slot, there, :]).astype(BF)

        tiles(4, tile)
        closed(8 * turn + 4)
        grad_saved(turn).wait()
        kin_right(False, 4 * turn, 0).start()

    def attend_heads(turn):
        scale = 1.0 / math.sqrt(HD)
        for copy in act_copies(turn):
            copy.wait()
        if turn == 1:
            for which in range(3):
                kin_right(False, 1 + which, 0).wait_send()

        def head(index, carry):
            here = pl.ds(pl.multiple_of(index * HD, HD), HD)
            q, k, v, do = qb[:, here], kb[:, here], vb[:, here], dob[:, here]
            scores = mm_cols(q, k) * scale
            if turn == 1:
                scores = jnp.where(mask_in[...] > 0.0, scores, MASKED)
            grown = jnp.exp(scores - jnp.max(scores, axis=-1, keepdims=True))
            soft = grown / jnp.sum(grown, axis=-1, keepdims=True)
            back = mm_cols(do, v)
            short = soft * (back - jnp.sum(soft * back, axis=-1, keepdims=True))
            dqkv[0, :, here] = (mm(short.astype(BF), k) * scale).astype(BF)
            dqkv[1, :, here] = (mm(short.T.astype(BF), q) * scale).astype(BF)
            dqkv[2, :, here] = mm(soft.T.astype(BF), do).astype(BF)
            return carry

        lax.fori_loop(0, width // HD, head, 0)
        if turn == 0:
            for copy in act_copies(1):
                copy.start(priority=LOCAL)
        for which in range(3):
            for copy in kin_lefts(False, 4 * turn + 1 + which):
                copy.start()
            kin_right(False, 4 * turn + 1 + which, 0).start()

    def attend_end(turn):
        base = 8 * turn + 5
        for which in range(3):
            slot = opened(base + which)

            def tile(there, _):
                value = mm_cols(dqkv[which], slots[slot, there, :])
                if which == 0:
                    rows_sum[0:rows, there] = value
                elif which == 1:
                    rows_sum[rows : 2 * rows, there] = value
                else:
                    rows_sum[rows : 2 * rows, there] += value

            tiles(4, tile)
            closed(base + which)
        row_copy(2 * turn + 1).wait()
        gain_q = gains[2:3, :] if turn == 0 else gains[0:1, :]
        gain_kv = gains[2:3, :] if turn == 0 else gains[1:2, :]

        def body(here):
            unit, inverse = unit_rows(ub[here, :].astype(F32))
            dx, gain_part = lean(rows_sum[here, :], unit, inverse, gain_q)
            if turn == 1:
                unit, inverse = unit_rows(src_in[here, :].astype(F32))
            there = pl.ds(pl.multiple_of(rows + here.start, 32), 32)
            ds, kv_part = lean(rows_sum[there, :], unit, inverse, gain_kv)
            fresh = grad[here, :].astype(F32) + dx
            if turn == 0:
                fresh += ds
            else:
                high = ds.astype(BF)
                part_out[0, here, :] = high
                part_out[1, here, :] = (ds - high.astype(F32)).astype(BF)
            grad[here, :] = fresh.astype(BF)
            return gain_part, kv_part

        if turn == 1:
            for which in range(2):
                part_over(which).wait_send()
            for copy in kin_lefts(True, 2):
                copy.wait_send()
        gain_grad, kv_grad = row_steps(body, 2)
        if turn == 0:
            row_copy(2).start(priority=LOCAL)
            small_row(2, gain_grad + kv_grad)
            open_pair(1)
        else:
            small_row(0, gain_grad)
            small_row(1, kv_grad)
            small_row(15, jnp.zeros_like(gain_grad))

            def tile(there, _):
                pair[:, there] = (
                    mm(picks_in[...], part_out[0, :, there])
                    + mm(picks_in[...], part_out[1, :, there])
                ).astype(BF)

            tiles(4, tile)
            small_copy(0).start()
            for which in range(3):
                point_copy(which).start()
            lat_start(1)

    def point_total():
        for which in range(3):
            point_copy(which).wait_recv()
        gathered = pair[
            pl.ds(pl.multiple_of(section_at * quarter_rows, 128), quarter_rows)
        ].astype(F32)
        for which in range(3):
            gathered += point_in[which].astype(F32)
        point_sum[...] = gathered.astype(BF)
        point_local().start(priority=LOCAL)
        for which in range(3):
            point_deal(which).start()

    def small_step(phase):
        small_copy(phase).wait_recv()
        small_sum[phase + 1] = small_sum[phase] + small_in[phase]
        if phase < 2:
            small_copy(phase + 1).start()
        else:
            for step in range(3):
                small_copy(3 + step).start()

    def small_end():
        for step in range(3):
            small_copy(3 + step).wait_recv()
        small_out[...] = (small_sum[3] + small_in[4]) + (small_in[3] + small_in[5])

    def rows_end():
        lat_onward(1)
        point_total()

    begin = pltpu.make_async_copy(top_in, grad, act_sems.at[4])
    begin.start()
    for index in range(2):
        slot_copy(index).start(priority=LOCAL)
    h_copy(0).start(priority=LOCAL)
    row_copy(0).start(priority=LOCAL)
    for copy in act_copies(0):
        copy.start(priority=LOCAL)
    begin.wait()
    open_pair(0)
    for turn in range(2):
        for part in range(2):
            kin_right(True, 2 * turn, part).start()
        for copy in kin_lefts(True, 2 * turn + 1):
            copy.start()
    lat_start(0)
    pair_ready(0)
    load(0)
    chain = {
        0: [functools.partial(feed_chunk, 0, 0)],
        1: [functools.partial(feed_chunk, 0, 1)],
        2: [functools.partial(feed_end, 0), functools.partial(lat_onward, 0)],
        3: [functools.partial(attend_heads, 0)],
        4: [functools.partial(attend_end, 0)],
        5: [functools.partial(pair_ready, 1), functools.partial(feed_chunk, 1, 0)],
        6: [functools.partial(feed_chunk, 1, 1)],
        7: [functools.partial(feed_end, 1)],
        8: [functools.partial(attend_heads, 1)],
        9: [functools.partial(attend_end, 1)],
        11: [functools.partial(small_step, 0), rows_end],
        13: [functools.partial(small_step, 1)],
        15: [functools.partial(small_step, 2)],
        17: [small_end],
    }

    def moment_body(moment, carry):
        @pl.when(moment < total)
        def _():
            by_kind(moment, offer)

        for lag, action in ((2, first), (3, second), (4, third), (5, close), (6, finish)):
            pl.when(jnp.logical_and(moment >= lag, moment < total + lag))(
                functools.partial(action, moment - lag)
            )
        for when, actions in chain.items():

            @pl.when(moment == when)
            def _():
                for action in actions:
                    action()

        for item in range(1, total):
            pl.when(moment == item - 1)(functools.partial(load, item))
        return carry

    lax.fori_loop(0, total + 6, moment_body, 0)

    for index in range(4):
        if index % 2 == 1:
            for copy in kin_lefts(True, index):
                copy.wait_send()
        if index != 1:
            for chunk in range(2):
                kin_right(True, index, chunk).wait_send()
    for index in range(8):
        for copy in kin_lefts(False, index):
            copy.wait_send()
        if index not in (1, 2, 3):
            kin_right(False, index, 0).wait_send()
    for phase in range(6):
        small_copy(phase).wait_send()
    for which in range(2):
        lat_local(which).wait()
        for way in range(2):
            lat_copy(which, way).wait_send()
        lat_far(which).wait()
    point_local().wait()
    for which in range(3):
        point_copy(which).wait_send()
        point_deal(which).wait()

    def drain(item, carry):
        @pl.when(item >= 4)
        def _():
            by_kind(item, drained)

        return carry

    for item in range(total - STAGES, total):
        xy_sent(item)
    lax.fori_loop(0, total, drain, 0)


def reduce_all(full, kept, latents, gains, mask, picks):
    total = ITEM_COUNT
    rows, width = kept[0].shape
    points = picks.shape[0]
    anywhere = pl.BlockSpec(memory_space=pl.ANY)
    vmem = pl.BlockSpec(memory_space=pltpu.VMEM)
    u1, u2, u3, u4, top = kept[:5]
    operands = [*full, u1, u2, u3, u4, top, *kept[5:16], *kept[17:], latents, kept[16]]
    operands += [gains, mask, picks]
    spaces = [anywhere] * (len(operands) - 4) + [vmem] * 4
    dma = pltpu.SemaphoreType.DMA
    flops = 2 * width * width * 24 * rows * 2
    return pl.pallas_call(
        reduce_kernel,
        out_shape=[
            jax.ShapeDtypeStruct((2, 128, 4 * width), BF),
            jax.ShapeDtypeStruct((2, 128, 4 * width), BF),
            jax.ShapeDtypeStruct((128, 3 * width), BF),
            jax.ShapeDtypeStruct((128, 3 * width), BF),
            jax.ShapeDtypeStruct((128, width), BF),
            jax.ShapeDtypeStruct((128, width), BF),
            jax.ShapeDtypeStruct((4 * rows, width), BF),
            jax.ShapeDtypeStruct((4 * rows, width), BF),
            jax.ShapeDtypeStruct((points, width), BF),
            jax.ShapeDtypeStruct((16, width), F32),
            jax.ShapeDtypeStruct((2, rows, width), BF),
            jax.ShapeDtypeStruct((4, 4, 2 * rows, 128), BF),
            jax.ShapeDtypeStruct((8, 4, rows, 128), BF),
            jax.ShapeDtypeStruct((4, 2 * rows, 2 * width), BF),
            jax.ShapeDtypeStruct((8, rows, width), BF),
        ],
        in_specs=spaces,
        out_specs=[anywhere] * 9 + [vmem] + [anywhere] * 5,
        scratch_shapes=[
            pltpu.VMEM((4, 4, 128, 1024), BF),
            pltpu.VMEM((8, 4, 128, 512), BF),
            pltpu.VMEM((4, 2, 512, 128), BF),
            pltpu.VMEM((WINDOWS, 1024, 1024), BF),
            pltpu.VMEM((STAGES, 4, 128, 512), BF),
            pltpu.VMEM((4, 4, 128, 1024), BF),
            pltpu.VMEM((8, 4, 128, 512), BF),
            pltpu.VMEM((8, 5, 128, 1024), BF),
            pltpu.VMEM((4, 128, 1024), BF),
            pltpu.VMEM((8, 128, 512), BF),
            pltpu.VMEM((4, 128, 1024), BF),
            pltpu.VMEM((8, 128, 512), BF),
            pltpu.VMEM((512, 1024), BF),
            pltpu.VMEM((512, 2048), BF),
            pltpu.VMEM((512, 1024), F32),
            pltpu.VMEM((512, 1024), F32),
            pltpu.VMEM((2, 1024, 1024), BF),
            pltpu.VMEM((256, 1024), BF),
            pltpu.VMEM((256, 1024), BF),
            pltpu.VMEM((256, 1024), BF),
            pltpu.VMEM((256, 1024), BF),
            pltpu.VMEM((3, 256, 1024), BF),
            pltpu.VMEM((2, 256, 1024), BF),
            pltpu.VMEM((2, 256, 1024), BF),
            pltpu.VMEM((256, 1024), BF),
            pltpu.VMEM((256, 1024), BF),
            pltpu.VMEM((3, points // 4, width), BF),
            pltpu.VMEM((points // 4, width), BF),
            pltpu.VMEM((6, 16, width), F32),
            pltpu.VMEM((4, 16, width), F32),
            dma((2, 12, 4)),
            dma((2, 16)),
            dma((4, 2)),
            dma((WINDOWS, 2)),
            dma((2, 8, 2)),
            dma((total, 4)),
            dma((total, 5)),
            dma((2, total, 2)),
            dma((2, total, 2)),
            dma((total, 2)),
            dma((2, 2, 2)),
            dma((2, 2, 2)),
            dma((2,)),
            dma((2, 3)),
            dma((2, 3)),
            dma((1,)),
            dma((2, 6)),
            dma((2, 2, 2)),
            dma((2,)),
            dma((1,)),
            dma((1,)),
            dma((5,)),
        ],
        compiler_params=pltpu.CompilerParams(
            collective_id=2, has_side_effects=True, vmem_limit_bytes=62 * 2**20
        ),
        cost_estimate=pl.CostEstimate(
            flops=flops, bytes_accessed=2**27, transcendentals=2**21
        ),
    )(*operands)[:10]


def plain_layers(full, spread, mine, source, valid, cot_own, picks, groups_all):
    proj_c, out_c, in_0, down_0, proj_s, out_s, in_1, down_1 = full
    width, hidden = in_0.shape

    def vector(first, count):
        return spread[:, first : first + count].reshape(-1)

    gains_cross = (vector(0, 1), vector(1, 1))
    gain_self = vector(2, 1)
    gains_mlp = (vector(3, 1), vector(4, 1))
    biases_out = (vector(5, 1), vector(6, 1))
    per_bias = hidden // width
    biases_in = (vector(7, per_bias), vector(7 + per_bias, per_bias))
    cot = cot_own.astype(F32)
    u1, kept_c = attend(mine, source, valid, gains_cross[0], gains_cross[1], proj_c, out_c)
    u2, kept_0 = feed(u1.astype(F32), gains_mlp[0], in_0, biases_in[0], down_0, biases_out[0])
    u2 = u2.astype(F32)
    u3, kept_s = attend(u2, u2, None, gain_self, gain_self, proj_s, out_s)
    u4, kept_1 = feed(u3.astype(F32), gains_mlp[1], in_1, biases_in[1], down_1, biases_out[1])
    final = u4.astype(F32)
    group_norm = jnp.sqrt(jnp.mean(final * final) + EPSILON)
    norm_mean = lax.psum(group_norm, ALL) / groups_all
    g4 = (cot + (norm_mean / group_norm) * final).astype(BF)

    dx, gain_1_grad, bias_1_grad, ob_1_grad, pairs_1 = feed_back(
        g4, kept_1, gains_mlp[1], in_1, down_1
    )
    g3 = (g4.astype(F32) + dx).astype(BF)
    dx, ds, gq, gkv, pairs_s = attend_back(g3, kept_s, gain_self, gain_self, proj_s, out_s)
    gain_s_grad = gq + gkv
    g2 = (g3.astype(F32) + dx + ds).astype(BF)
    dx, gain_0_grad, bias_0_grad, ob_0_grad, pairs_0 = feed_back(
        g2, kept_0, gains_mlp[0], in_0, down_0
    )
    g1 = (g2.astype(F32) + dx).astype(BF)
    dx, ds, cq_grad, ckv_grad, pairs_c = attend_back(
        g1, kept_c, gains_cross[0], gains_cross[1], proj_c, out_c
    )
    g0 = (g1.astype(F32) + dx).astype(BF)
    high = ds.astype(BF)
    low = (ds - high.astype(F32)).astype(BF)
    point_part = (mm_rows(picks, high) + mm_rows(picks, low)).astype(BF)
    small = jnp.concatenate(
        [
            cq_grad,
            ckv_grad,
            gain_s_grad,
            gain_0_grad,
            gain_1_grad,
            ob_0_grad,
            ob_1_grad,
            bias_0_grad,
            bias_1_grad,
            jnp.zeros_like(cq_grad),
        ]
    ).reshape(-1, width)
    pairs = pairs_1 + pairs_s + pairs_0 + pairs_c
    lefts, rights = [pair[0] for pair in pairs], [pair[1] for pair in pairs]
    def settled_grad(left, right):
        part = lax.psum_scatter(
            mm_rows(left, right).astype(BF), ALL, scatter_dimension=0, tiled=True
        )
        return lax.all_gather(part, "section", axis=0, tiled=True).astype(F32)

    done = [settled_grad(left, right) for left, right in pairs]
    mlp_in_grad = jnp.stack([done[6], done[0]])
    mlp_down_grad = jnp.stack([done[7], done[1]])
    proj_s_grad = jnp.concatenate(done[2:5], axis=1)
    proj_c_grad = jnp.concatenate(done[8:11], axis=1)
    out_s_grad, out_c_grad = done[5], done[11]
    points_sum = lax.psum(point_part, "section")
    latents_out = lax.all_gather(u4, "section", axis=0, tiled=True)
    g0_all = lax.all_gather(g0, "section", axis=0, tiled=True)
    small = lax.psum(small, ALL)
    return (
        norm_mean,
        latents_out,
        g0_all,
        points_sum,
        small,
        mlp_in_grad,
        mlp_down_grad,
        proj_c_grad,
        proj_s_grad,
        out_c_grad,
        out_s_grad,
    )


def per_device(
    latents,
    points,
    neighbours,
    lengths,
    cross_proj,
    cross_out,
    cross_gains,
    self_proj,
    self_out,
    self_gain,
    mlp_gain,
    mlp_in,
    mlp_in_bias,
    mlp_down,
    mlp_out_bias,
    cotangent,
):
    sections = lax.axis_size("section")
    section_at = lax.axis_index("section")
    width = latents.shape[1]
    hidden = mlp_in.shape[2]
    groups_dev = neighbours.shape[0]
    rows = latents.shape[0] // sections
    shard = cross_out.shape[0]
    piece = shard // sections
    groups_all = groups_dev * lax.axis_size("batch")

    def gathered(block):
        own = lax.dynamic_slice_in_dim(block, section_at * piece, piece, 0)
        return lax.all_gather(own, ALL, axis=0, tiled=True)

    projs = (cross_proj.reshape(shard, 3 * width), self_proj.reshape(shard, 3 * width))
    if lax.axis_size("batch") == 8:
        made = gather_forward(
            [projs[0], cross_out, mlp_in, mlp_down, projs[1], self_out],
            latents,
            cotangent,
            points,
            neighbours,
            lengths[:, None],
            [cross_gains, self_gain[None, :], mlp_gain, mlp_out_bias, mlp_in_bias],
        )
        full, gain_rows, norm_tile, mask, picks = made[:8], *made[8:12]
        norm_mean = norm_tile[0, 0]
        (
            mlp_in_grad,
            mlp_down_grad,
            proj_c_grad,
            proj_s_grad,
            out_c_grad,
            out_s_grad,
            latents_out,
            g0_all,
            points_sum,
            small,
        ) = reduce_all(full, made[12:], latents, gain_rows, mask, picks)
        mlp_in_grad = mlp_in_grad.astype(F32)
        mlp_down_grad = mlp_down_grad.astype(F32)
        proj_c_grad, proj_s_grad = proj_c_grad.astype(F32), proj_s_grad.astype(F32)
        out_c_grad, out_s_grad = out_c_grad.astype(F32), out_s_grad.astype(F32)
    else:
        vectors = jnp.concatenate(
            [
                cross_gains.reshape(-1),
                self_gain,
                mlp_gain.reshape(-1),
                mlp_out_bias.reshape(-1),
                mlp_in_bias.reshape(-1),
                jnp.zeros_like(self_gain),
            ]
        ).reshape(-1, shard)
        cot_own = lax.dynamic_slice_in_dim(cotangent, section_at * rows, rows, 0)
        mine = lax.dynamic_slice_in_dim(latents, section_at * rows, rows, 0).astype(F32)
        listed = lax.dynamic_index_in_dim(neighbours, section_at, 0, keepdims=False)
        length = lax.dynamic_index_in_dim(lengths, section_at, 0, keepdims=False)
        valid = jnp.arange(listed.shape[0], dtype=jnp.int32) < length
        picks = listed[:, None] == jnp.arange(points.shape[0], dtype=jnp.int32)[None, :]
        picks = picks.astype(BF)
        source = mm(picks, points)
        blocks = [projs[0], cross_out, mlp_in[0], mlp_down[0]]
        blocks += [projs[1], self_out, mlp_in[1], mlp_down[1]]
        full = [gathered(block) for block in blocks]
        spread = lax.all_gather(vectors, "batch", axis=0, tiled=False)
        (
            norm_mean,
            latents_out,
            g0_all,
            points_sum,
            small,
            mlp_in_grad,
            mlp_down_grad,
            proj_c_grad,
            proj_s_grad,
            out_c_grad,
            out_s_grad,
        ) = plain_layers(full, spread.astype(F32), mine, source, valid, cot_own, picks, groups_all)
    points_grad = points_sum.astype(F32)
    latents_grad = g0_all.astype(F32)
    per_bias = hidden // width
    batch_at = lax.axis_index("batch")

    def own(first, count):
        flat = small[first : first + count].reshape(-1)
        size = flat.shape[0] // lax.axis_size("batch")
        return lax.dynamic_slice_in_dim(flat, batch_at * size, size, 0)

    return (
        latents_out,
        latents_grad,
        points_grad,
        proj_c_grad.reshape(shard, 3, width),
        out_c_grad,
        jnp.stack([own(0, 1), own(1, 1)]),
        proj_s_grad.reshape(shard, 3, width),
        out_s_grad,
        own(2, 1),
        jnp.stack([own(3, 1), own(4, 1)]),
        mlp_in_grad,
        jnp.stack([own(7, per_bias), own(7 + per_bias, per_bias)]),
        mlp_down_grad,
        jnp.stack([own(5, 1), own(6, 1)]),
        norm_mean,
    )


def solution(mesh):
    rows = P("batch", None)
    cols = P(None, "batch")
    block = P("batch", None, None)
    pair = P(None, "batch", None)
    return jax.shard_map(
        per_device,
        mesh=mesh,
        in_specs=(
            rows,
            rows,
            rows,
            P("batch"),
            block,
            rows,
            cols,
            block,
            rows,
            P("batch"),
            cols,
            pair,
            cols,
            pair,
            cols,
            rows,
        ),
        out_specs=(
            rows,
            rows,
            rows,
            block,
            rows,
            cols,
            block,
            rows,
            P("batch"),
            cols,
            pair,
            cols,
            pair,
            cols,
            P(),
        ),
        check_vma=False,
    )
```

```python
import functools
import math

import jax
import jax.numpy as jnp
from jax import lax
from jax.experimental import pallas as pl
from jax.experimental.pallas import tpu as pltpu
from jax.sharding import PartitionSpec as P

HD = 128
EPSILON = 1e-05
MASKED = -1e30
BF = jnp.bfloat16
F32 = jnp.float32
ALL = ("batch", "section")
MESH = pl.DeviceIdType.MESH
GATHER_WIDTH = 1024
AHEAD = 4
LOCAL = 1
SLOTS = 3
GATHERED = tuple(
    (4 * layer + index, start)
    for layer in range(2)
    for index, start in (
        [(0, 0), (0, 1024), (0, 2048), (1, 0)]
        + [(2 + which, chunk) for chunk in range(0, 2048, 1024) for which in range(2)]
    )
)


def mm(a, b):
    return jnp.dot(a, b, preferred_element_type=F32)


def mm_rows(a, b):
    return lax.dot_general(a, b, (((0,), (0,)), ((), ())), preferred_element_type=F32)


def mm_cols(a, b):
    return lax.dot_general(a, b, (((1,), (1,)), ((), ())), preferred_element_type=F32)


def unit_rows(values):
    centred = values - jnp.mean(values, axis=-1, keepdims=True)
    inverse = lax.rsqrt(jnp.mean(centred * centred, axis=-1, keepdims=True) + EPSILON)
    return centred * inverse, inverse


def norm_back(gradient, unit, inverse, gain):
    scaled = gradient * gain
    inner = (
        scaled
        - jnp.mean(scaled, axis=-1, keepdims=True)
        - unit * jnp.mean(scaled * unit, axis=-1, keepdims=True)
    )
    return inverse * inner, jnp.sum(gradient * unit, axis=0)


def heads_of(rows):
    return rows.reshape(rows.shape[0], -1, HD)


def softmax(q, k, valid):
    scores = jnp.einsum(
        "lhc,nhc->hln", heads_of(q), heads_of(k), preferred_element_type=F32
    ) * (1.0 / math.sqrt(HD))
    if valid is not None:
        scores = jnp.where(valid[None, None, :], scores, MASKED)
    grown = jnp.exp(scores - jnp.max(scores, axis=-1, keepdims=True))
    return grown / jnp.sum(grown, axis=-1, keepdims=True)


def attend(inputs, source, valid, gain_q, gain_kv, proj, out):
    unit_x, inv_x = unit_rows(inputs)
    queries_in = (unit_x * gain_q).astype(BF)
    unit_s, inv_s = unit_rows(source)
    keys_in = (unit_s * gain_kv).astype(BF)
    width = inputs.shape[1]
    q = mm(queries_in, proj[:, :width]).astype(BF)
    kv = mm(keys_in, proj[:, width:]).astype(BF)
    k, v = kv[:, :width], kv[:, width:]
    soft = softmax(q, k, valid)
    mixture = jnp.einsum("hln,nhc->lhc", soft.astype(BF), heads_of(v), preferred_element_type=F32)
    mixture = mixture.reshape(inputs.shape).astype(BF)
    result = (inputs + mm(mixture, out)).astype(BF)
    return result, (unit_x, inv_x, queries_in, unit_s, inv_s, keys_in, q, k, v, soft, mixture)


def attend_back(gradient, kept, gain_q, gain_kv, proj, out):
    unit_x, inv_x, queries_in, unit_s, inv_s, keys_in, q, k, v, soft, mixture = kept
    width = gradient.shape[1]
    scale = 1.0 / math.sqrt(HD)
    grad_mix = mm_cols(gradient, out).astype(BF)
    grad_soft = jnp.einsum(
        "lhc,nhc->hln", heads_of(grad_mix), heads_of(v), preferred_element_type=F32
    )
    inner = jnp.sum(soft * grad_soft, axis=-1, keepdims=True)
    grad_scores = (soft * (grad_soft - inner)).astype(BF)
    dq = jnp.einsum("hln,nhc->lhc", grad_scores, heads_of(k), preferred_element_type=F32) * scale
    dk = jnp.einsum("hln,lhc->nhc", grad_scores, heads_of(q), preferred_element_type=F32) * scale
    dv = jnp.einsum(
        "hln,lhc->nhc", soft.astype(BF), heads_of(grad_mix), preferred_element_type=F32
    )
    dq = dq.reshape(gradient.shape).astype(BF)
    dk = dk.reshape(-1, width).astype(BF)
    dv = dv.reshape(-1, width).astype(BF)
    grad_x, gain_q_grad = norm_back(mm_cols(dq, proj[:, :width]), unit_x, inv_x, gain_q)
    back_s = mm_cols(dk, proj[:, width : 2 * width]) + mm_cols(dv, proj[:, 2 * width :])
    grad_s, gain_kv_grad = norm_back(back_s, unit_s, inv_s, gain_kv)
    pairs = ((queries_in, dq), (keys_in, dk), (keys_in, dv), (mixture, gradient))
    return grad_x, grad_s, gain_q_grad, gain_kv_grad, pairs


def feed(inputs, gain, w_in, b_in, w_down, b_out):
    unit, inverse = unit_rows(inputs)
    lowered = (unit * gain).astype(BF)
    pre_act = mm(lowered, w_in) + b_in
    active = jax.nn.gelu(pre_act).astype(BF)
    result = (inputs + mm_cols(active, w_down) + b_out).astype(BF)
    return result, (unit, inverse, lowered, pre_act, active)


def feed_back(gradient, kept, gain, w_in, w_down):
    unit, inverse, lowered, pre_act, active = kept
    grad_act = mm(gradient, w_down)
    grad_pre = jax.vjp(jax.nn.gelu, pre_act)[1](grad_act)[0].astype(BF)
    grad_x, gain_grad = norm_back(mm_cols(grad_pre, w_in), unit, inverse, gain)
    bias_grad = jnp.sum(grad_pre.astype(F32), axis=0)
    out_grad = jnp.sum(gradient.astype(F32), axis=0)
    return grad_x, gain_grad, bias_grad, out_grad, ((lowered, grad_pre), (gradient, active))


def gelu_both(value):
    factor = math.sqrt(2.0 / math.pi)
    square = value * value
    bent = jnp.tanh(factor * value * (1.0 + 0.044715 * square))
    inner = factor * (1.0 + 3.0 * 0.044715 * square)
    half = 0.5 * (1.0 + bent)
    return value * half, half + 0.5 * value * (1.0 - bent * bent) * inner


def tiles(count, body, size=256):
    def step(index, carry):
        body(pl.ds(pl.multiple_of(index * size, size), size), index)
        return carry

    lax.fori_loop(0, count, step, 0)


def norm_into(source, gain, target):
    def step(index, carry):
        here = pl.ds(pl.multiple_of(index * 32, 32), 32)
        unit, _ = unit_rows(source[here, :].astype(F32))
        target[here, :] = (unit * gain).astype(BF)
        return carry

    lax.fori_loop(0, source.shape[0] // 32, step, 0)


def gather_kernel(*refs):
    cross_proj, cross_out, mlp_in, mlp_down, self_proj, self_out = refs[:6]
    latents_in, cot_all, points_in, near_in, length_in = refs[6:11]
    vec_parts = refs[11:16]
    section_at = lax.axis_index("section")
    batch_at = lax.axis_index("batch")
    x_at = lax.rem(section_at, 2)
    y_at = section_at // 2
    ins = (
        cross_proj,
        cross_out,
        mlp_in.at[0],
        mlp_down.at[0],
        self_proj,
        self_out,
        mlp_in.at[1],
        mlp_down.at[1],
    )
    count = len(ins)
    outs = refs[16 : 16 + count]
    rest = refs[16 + count :]
    gains, norm_out, mask_in, picks_out = rest[:4]
    kept_outs = rest[4:24]
    (
        u1,
        u2,
        u3,
        u4,
        grad_top,
        xq_c,
        sn_c,
        q_c,
        k_c,
        v_c,
        o_c,
        xn_s,
        q_s,
        k_s,
        v_s,
        o_s,
        src_in,
        lowered,
        before,
        active,
        x_in,
        cot_in,
        vec_in,
        vec_rows,
        slots,
        total_rows,
        part_out,
        part_in,
        vec_out,
        biases,
        plane,
        line_in,
    ) = rest[24:56]
    (own_sem, send, recv, kin_send, kin_recv, vec_sems) = rest[56:62]
    (slot_sems, kept_sems, plane_sems, line_sems, pair_sems, row_sems) = rest[62:]
    line = 4
    core = lax.rem(batch_at, 2)
    spot = batch_at // 2
    beside = section_at + 1 - 2 * x_at
    above = lax.rem(section_at + 2, 4)
    sibling = batch_at + 1 - 2 * core
    shard = ins[0].shape[0]
    place = section_at * 2 + core
    rows = x_in.shape[0]

    def down_line(step):
        return lax.rem(spot + step, line) * 2 + core

    def up_line(step):
        return lax.rem(spot + line - step, line) * 2 + core

    near_peers = []
    for turn in range(1, 8):
        other = lax.rem(place + turn, 8)
        near_peers.append((other // 2, spot * 2 + lax.rem(other, 2)))
    line_peers = [(section_at, down_line(step)) for step in range(1, line)]
    far_peers = [(section_at, down_line(step) + 1 - 2 * core) for step in range(1, line)]
    vec_peers = [(section_at, sibling)] + line_peers + far_peers
    peers = near_peers + line_peers + far_peers
    barrier = pltpu.get_barrier_semaphore()
    for peer in peers:
        pl.semaphore_signal(barrier, inc=1, device_id=peer, device_id_type=MESH)
    pl.semaphore_wait(barrier, len(peers))

    def spread(ref, owner, first, size):
        return ref.at[pl.ds(pl.multiple_of(owner * shard, shard), shard), pl.ds(first, size)]

    def is_feed(item):
        return item % 8 >= 4

    def source_of(item, first, size):
        index, start = GATHERED[item]
        if is_feed(item):
            first = pl.multiple_of(first + y_at * outs[index].shape[1], 128)
        return ins[index].at[:, pl.ds(first, size)]

    def piece(item):
        start = GATHERED[item][1]
        if is_feed(item):
            return pl.multiple_of(start + x_at * 512, 128), 512
        return pl.multiple_of(start + section_at * 256, 128), 256

    def own_line(item, way):
        first, size = piece(item)
        return pltpu.make_async_remote_copy(
            source_of(item, first, size),
            spread(outs[GATHERED[item][0]], batch_at, first, size),
            send.at[5 * way, item, 0],
            recv.at[0, item, 3 if way else 1],
            device_id=(section_at, batch_at + (-2 if way else 2)),
            device_id_type=MESH,
        )

    def onward_line(item, step, way):
        first, size = piece(item)
        ref = spread(outs[GATHERED[item][0]], up_line(step), first, size)
        return pltpu.make_async_remote_copy(
            ref,
            ref,
            send.at[0, item, step],
            recv.at[0, item, step - 1 if way else step + 1],
            device_id=(section_at, batch_at + (-2 if way else 2)),
            device_id_type=MESH,
        )

    def came_line(item, step):
        first, size = piece(item)
        ref = spread(outs[GATHERED[item][0]], up_line(step), first, size)
        return pltpu.make_async_remote_copy(
            ref,
            ref,
            send.at[0, item, step],
            recv.at[0, item, step],
            device_id=(section_at, sibling),
            device_id_type=MESH,
        )

    def start_line(item):
        @pl.when(spot < 3)
        def _():
            own_line(item, 0).start()

        @pl.when(spot > 0)
        def _():
            own_line(item, 1).start()

    def arrive_line(item, apart):
        @pl.when(spot >= apart)
        def _():
            came_line(item, apart).wait_recv()

            @pl.when(spot < 3)
            def _():
                onward_line(item, apart, 0).start()

            for copy in near(item, apart):
                copy.start()

        @pl.when(spot + apart <= 3)
        def _():
            came_line(item, 4 - apart).wait_recv()

            @pl.when(spot > 0)
            def _():
                onward_line(item, 4 - apart, 1).start()

            for copy in near(item, 4 - apart):
                copy.start()

    def sent_line(item):
        @pl.when(spot < 3)
        def _():
            own_line(item, 0).wait_send()

        @pl.when(spot > 0)
        def _():
            own_line(item, 1).wait_send()

        for apart in (1, 2, 3):

            @pl.when(jnp.logical_and(spot >= apart, spot < 3))
            def _():
                onward_line(item, apart, 0).wait_send()

            @pl.when(jnp.logical_and(spot + apart <= 3, spot > 0))
            def _():
                onward_line(item, 4 - apart, 1).wait_send()

        for step in (1, 2, 3):
            for copy in near(item, step):
                copy.wait_send()

    def plane_copy(item, step, way, low, wide, peer):
        ref = spread(outs[GATHERED[item][0]], up_line(step), low, wide)
        return pltpu.make_async_remote_copy(
            ref,
            ref,
            send.at[way, item, step],
            recv.at[way, item, step],
            device_id=(peer, batch_at),
            device_id_type=MESH,
        )

    def near(item, step):
        first, size = piece(item)
        copies = [plane_copy(item, step, 1, first, size, beside)]
        if not is_feed(item):
            copies.append(plane_copy(item, step, 2, first, size, above))
        return copies

    def far(item, step):
        start = GATHERED[item][1]
        by_y = pl.multiple_of(start + beside * 256, 128)
        by_x = pl.multiple_of(start + above * 256 + 128, 128)
        return [
            plane_copy(item, step, 3, by_y, 128, above),
            plane_copy(item, step, 4, by_x, 128, beside),
        ]

    def kin(item, step):
        index, start = GATHERED[item]
        if step == 0:
            source = source_of(item, start, GATHER_WIDTH)
        else:
            source = spread(outs[index], up_line(step), start, GATHER_WIDTH)
        return pltpu.make_async_remote_copy(
            source,
            spread(outs[index], up_line(step), start, GATHER_WIDTH),
            kin_send.at[item, step],
            kin_recv.at[item, step],
            device_id=(section_at, sibling),
            device_id_type=MESH,
        )

    def own(item):
        index, start = GATHERED[item]
        return pltpu.make_async_copy(
            source_of(item, start, GATHER_WIDTH),
            spread(outs[index], batch_at, start, GATHER_WIDTH),
            own_sem.at[item],
        )

    def vec_copy(which):
        return pltpu.make_async_remote_copy(
            vec_in,
            vec_out.at[batch_at],
            vec_sems.at[0, which],
            vec_sems.at[1, which],
            device_id=vec_peers[which],
            device_id_type=MESH,
        )

    def slot_copy(item):
        index, start = GATHERED[item]
        return pltpu.make_async_copy(
            outs[index].at[:, pl.ds(start, GATHER_WIDTH)],
            slots.at[item % SLOTS],
            slot_sems.at[item % SLOTS],
        )

    def near_norm(turn):
        return pltpu.make_async_remote_copy(
            plane.at[8],
            plane.at[place],
            plane_sems.at[0, turn],
            plane_sems.at[1, turn],
            device_id=near_peers[turn],
            device_id_type=MESH,
        )

    def far_norm(step):
        return pltpu.make_async_remote_copy(
            line_in.at[4],
            line_in.at[spot],
            line_sems.at[0, step],
            line_sems.at[1, step],
            device_id=line_peers[step],
            device_id_type=MESH,
        )

    def rows_over(layer):
        return pltpu.make_async_remote_copy(
            lowered.at[layer, pl.ds(0, rows)],
            lowered.at[layer, pl.ds(rows, rows)],
            pair_sems.at[0, layer, 0],
            pair_sems.at[1, layer, 0],
            device_id=(above, batch_at),
            device_id_type=MESH,
        )

    def part_over(layer):
        return pltpu.make_async_remote_copy(
            part_out.at[layer],
            part_in.at[layer],
            pair_sems.at[0, layer, 1],
            pair_sems.at[1, layer, 1],
            device_id=(above, batch_at),
            device_id_type=MESH,
        )

    steps = range(1, line)
    total = len(GATHERED)
    started = []

    def launch(copies):
        for copy in copies:
            copy.start()
        started.extend(copies)

    kept = (
        (u1, u2, u3, u4, grad_top)
        + (xq_c, sn_c, q_c, k_c, v_c, o_c)
        + (xn_s, q_s, k_s, v_s, o_s)
        + (src_in, lowered, before, active)
    )
    names = {id(ref): place for place, ref in enumerate(kept)}

    def keep(*chosen):
        for ref in chosen:
            index = names[id(ref)]
            pltpu.make_async_copy(ref, kept_outs[index], kept_sems.at[index]).start(priority=LOCAL)

    def row(index):
        return gains[index : index + 1, :]

    def project(source, target, slot):
        def tile(columns, _):
            target[:, columns] = mm(source[...], slots[slot, :, columns]).astype(BF)

        tiles(2, tile, 512)

    def heads(q, k, v, o, masked):
        def head(index, carry):
            here = pl.ds(pl.multiple_of(index * HD, HD), HD)
            scores = mm_cols(q[:, here], k[:, here]) * (1.0 / math.sqrt(HD))
            if masked:
                scores = jnp.where(mask_in[...] > 0.0, scores, MASKED)
            grown = jnp.exp(scores - jnp.max(scores, axis=-1, keepdims=True))
            soft = grown / jnp.sum(grown, axis=-1, keepdims=True)
            o[:, here] = mm(soft.astype(BF), v[:, here]).astype(BF)
            return carry

        lax.fori_loop(0, q.shape[1] // HD, head, 0)

    def close_attention(inputs, o, target, slot):
        def tile(columns, _):
            target[:, columns] = (
                inputs[:, columns].astype(F32) + mm(o[...], slots[slot, :, columns])
            ).astype(BF)

        tiles(2, tile, 512)

    def feed_up(layer, chunk, slot):
        def tile(columns, index):
            first = chunk * GATHER_WIDTH + index * 512
            there = pl.ds(pl.multiple_of(first, 512), 512)
            lanes = pl.ds(pl.multiple_of(y_at * 2048 + first, 512), 512)
            value = mm(lowered[layer], slots[slot, :, columns]) + biases[layer : layer + 1, lanes]
            active_part, slope = gelu_both(value)
            before[layer, :, there] = slope
            active[layer, :, there] = active_part.astype(BF)

        tiles(2, tile, 512)

    def feed_down(layer, chunk, slot):
        chosen = pl.ds(chunk * GATHER_WIDTH, GATHER_WIDTH)

        def tile(columns, _):
            value = mm_cols(active[layer, :, chosen], slots[slot, columns, :])
            if chunk == 0:
                total_rows[:, columns] = value
            else:
                value = total_rows[:, columns] + value
                total_rows[:, columns] = value
                part_out[layer, :, columns] = value[rows:].astype(BF)

        tiles(2, tile, 512)

    def feed_close(layer):
        inputs, target = (u1, u3)[layer], (u2, u4)[layer]
        part_over(layer).wait_recv()

        def tile(columns, _):
            target[:, columns] = (
                inputs[:, columns].astype(F32)
                + (total_rows[0:rows, columns] + part_in[layer, :, columns].astype(F32))
                + gains[5 + layer : 6 + layer, columns]
            ).astype(BF)

        tiles(2, tile, 512)
        keep(target)

    def work(item):
        slot_copy(item).wait()
        slot = item % SLOTS
        layer, stage = item // 8, item % 8
        inputs = (x_in, u2)[layer]
        middle = (u1, u3)[layer]
        q, k, v, o = ((q_c, k_c, v_c, o_c), (q_s, k_s, v_s, o_s))[layer]
        if stage == 0:
            if layer == 0:
                norm_into(x_in, row(0), xq_c)
                norm_into(src_in, row(1), sn_c)
                keep(xq_c, sn_c)
            else:
                feed_close(0)
                norm_into(u2, row(2), xn_s)
                keep(xn_s)
            project((xq_c, xn_s)[layer], q, slot)
        elif stage == 1:
            project((sn_c, xn_s)[layer], k, slot)
        elif stage == 2:
            project((sn_c, xn_s)[layer], v, slot)
            heads(q, k, v, o, layer == 0)
            keep(q, k, v, o)
        elif stage == 3:
            close_attention(inputs, o, middle, slot)
            norm_into(middle, row(3 + layer), lowered.at[layer, pl.ds(0, rows)])
            launch([rows_over(layer)])
            keep(middle)
        elif stage % 2 == 0:
            if stage == 4:
                rows_over(layer).wait_recv()
            feed_up(layer, (stage - 4) // 2, slot)
        else:
            feed_down(layer, (stage - 4) // 2, slot)
            if stage == 7:
                launch([part_over(layer)])

    for item in range(AHEAD):
        start_line(item)
    here = pl.ds(pl.multiple_of(section_at * rows, rows), rows)
    row_copies = [
        pltpu.make_async_copy(latents_in.at[here], x_in, row_sems.at[0]),
        pltpu.make_async_copy(cot_all.at[here], cot_in, row_sems.at[1]),
    ]
    for copy in row_copies:
        copy.start()
    cross_gain, self_gain, feed_gain, out_bias, in_bias = vec_parts
    vec_rows[...] = jnp.zeros_like(vec_rows)
    vec_rows[0:2, :] = cross_gain[...].astype(F32)
    vec_rows[2:3, :] = self_gain[...].astype(F32)
    vec_rows[3:5, :] = feed_gain[...].astype(F32)
    vec_rows[5:7, :] = out_bias[...].astype(F32)
    bias_rows = in_bias[...].astype(F32)
    for layer in range(2):
        for part_at in range(4):
            index = 7 + 4 * layer + part_at
            vec_rows[index : index + 1, :] = bias_rows[
                layer : layer + 1, part_at * 128 : part_at * 128 + 128
            ]
    vec_in[...] = vec_rows[...].astype(BF)
    vec_out[batch_at] = vec_in[...]
    for which in range(7):
        vec_copy(which).start()
    lanes = lax.broadcasted_iota(jnp.int32, (1, rows), 1)
    length = length_in[pl.ds(section_at, 1), :]
    mask_in[...] = jnp.where(lanes < length, 1.0, 0.0)
    point_at = lax.broadcasted_iota(jnp.int32, (points_in.shape[0], rows), 0)
    wanted = near_in[pl.ds(section_at, 1), :]
    picks = jnp.where(point_at == wanted, 1.0, 0.0)
    picks_out[...] = picks.astype(BF)
    turned = picks.T.astype(BF)

    def source_tile(columns, _):
        src_in[:, columns] = mm(turned, points_in[:, columns]).astype(BF)

    tiles(2, source_tile, 512)
    keep(src_in)
    for copy in row_copies:
        copy.wait()
    for moment in range(-2, total + 4):
        if moment + 2 + AHEAD < total:
            start_line(moment + 2 + AHEAD)
        for apart in (1, 2, 3):
            if 0 <= moment + 3 - apart < total:
                arrive_line(moment + 3 - apart, apart)
        if 0 <= moment < total:
            own(moment).start(priority=LOCAL)
            launch([kin(moment, 0)])
        if 0 <= moment - 1 < total:
            for step in steps:
                if is_feed(moment - 1):
                    near(moment - 1, step)[0].wait_recv()
                    launch([kin(moment - 1, step)])
                else:
                    for copy, onward in zip(near(moment - 1, step), far(moment - 1, step)):
                        copy.wait_recv()
                        launch([onward])
        if 0 <= moment - 2 < total and not is_feed(moment - 2):
            for step in steps:
                for copy in far(moment - 2, step):
                    copy.wait_recv()
                launch([kin(moment - 2, step)])
        if moment == 2:
            for which in range(7):
                vec_copy(which).wait()
            for owner in range(8):
                values = vec_out[owner].astype(F32)
                gains[:, owner * 128 : owner * 128 + 128] = values
                for layer in range(2):
                    for part_at in range(4):
                        first = owner * 512 + part_at * 128
                        index = 7 + 4 * layer + part_at
                        biases[layer : layer + 1, first : first + 128] = values[index : index + 1]
        if 0 <= moment - 4 < total:
            work(moment - 4)
        if 0 <= moment - 3 < total:
            own(moment - 3).wait()
            for step in range(line):
                kin(moment - 3, step).wait_recv()
            slot_copy(moment - 3).start(priority=LOCAL)
    keep(lowered, before, active)
    feed_close(1)

    def square(index, carry):
        here = pl.ds(pl.multiple_of(index * 32, 32), 32)
        values = u4[here, :].astype(F32)
        return carry + jnp.sum(values * values, axis=0, keepdims=True)

    squares = lax.fori_loop(0, u4.shape[0] // 32, square, jnp.zeros((1, u4.shape[1]), F32))
    mean = jnp.sum(squares, axis=1, keepdims=True) / (u4.shape[0] * u4.shape[1])
    group_norm = jnp.sqrt(mean + EPSILON)
    plane[8] = jnp.broadcast_to(group_norm, plane.shape[1:])
    for turn in range(7):
        near_norm(turn).start()
    plane[place] = plane[8]
    for turn in range(7):
        near_norm(turn).wait()
    line_in[4] = jnp.sum(plane[0:8], axis=0)
    for step in range(3):
        far_norm(step).start()
    line_in[spot] = line_in[4]
    for step in range(3):
        far_norm(step).wait()
    norm_mean = jnp.sum(line_in[0:4], axis=0) / 32.0
    norm_out[...] = norm_mean
    ratio = norm_mean[0:1, 0:1] / group_norm

    def top(index, carry):
        here = pl.ds(pl.multiple_of(index * 32, 32), 32)
        grad_top[here, :] = (
            cot_in[here, :].astype(F32) + ratio * u4[here, :].astype(F32)
        ).astype(BF)
        return carry

    lax.fori_loop(0, u4.shape[0] // 32, top, 0)
    keep(grad_top)
    for index, ref in enumerate(kept):
        pltpu.make_async_copy(ref, kept_outs[index], kept_sems.at[index]).wait()
    for item in range(total):
        sent_line(item)
    for copy in started:
        copy.wait_send()


def gather_forward(blocks, latents, cotangent, points, near, lengths, vectors):
    width = latents.shape[1]
    rows = near.shape[1]
    half = blocks[2].shape[2] // 2
    widths = (3 * width, width, half, half) * 2
    total = len(GATHERED)
    anywhere = pl.BlockSpec(memory_space=pl.ANY)
    vmem = pl.BlockSpec(memory_space=pltpu.VMEM)
    plain = ((rows, width), BF)
    kept = [plain] * 17 + [
        ((2, 2 * rows, width), BF),
        ((2, 2 * rows, half), F32),
        ((2, 2 * rows, half), BF),
    ]
    dma = pltpu.SemaphoreType.DMA
    return pl.pallas_call(
        gather_kernel,
        out_shape=[jax.ShapeDtypeStruct((width, size), BF) for size in widths]
        + [
            jax.ShapeDtypeStruct((16, width), F32),
            jax.ShapeDtypeStruct((8, 128), F32),
            jax.ShapeDtypeStruct((1, rows), F32),
            jax.ShapeDtypeStruct((points.shape[0], rows), BF),
        ]
        + [jax.ShapeDtypeStruct(*one) for one in kept],
        in_specs=[anywhere] * (len(blocks) + 2) + [vmem] * 8,
        out_specs=[anywhere] * len(widths) + [vmem] * 4 + [anywhere] * len(kept),
        scratch_shapes=[pltpu.VMEM(*one) for one in kept]
        + [
            pltpu.VMEM((rows, width), BF),
            pltpu.VMEM((rows, width), BF),
            pltpu.VMEM((16, 128), BF),
            pltpu.VMEM((16, 128), F32),
            pltpu.VMEM((SLOTS, width, GATHER_WIDTH), BF),
            pltpu.VMEM((2 * rows, width), F32),
            pltpu.VMEM((2, rows, width), BF),
            pltpu.VMEM((2, rows, width), BF),
            pltpu.VMEM((8, 16, 128), BF),
            pltpu.VMEM((2, 2 * half), F32),
            pltpu.VMEM((9, 8, 128), F32),
            pltpu.VMEM((5, 8, 128), F32),
            dma((total,)),
            dma((6, total, 4)),
            dma((5, total, 4)),
            dma((total, 4)),
            dma((total, 4)),
            dma((2, 7)),
            dma((SLOTS,)),
            dma((len(kept),)),
            dma((2, 7)),
            dma((2, 3)),
            dma((2, 2, 2)),
            dma((2,)),
        ],
        compiler_params=pltpu.CompilerParams(
            collective_id=1, has_side_effects=True, vmem_limit_bytes=56 * 2**20
        ),
        cost_estimate=pl.CostEstimate(
            flops=2 * rows * width * sum(widths), bytes_accessed=2**27, transcendentals=2**21
        ),
    )(*blocks, latents, cotangent, points, near, lengths, *vectors)


ITEM_COUNT = 16
WINDOWS = 4
STAGES = 3


def reduce_kernel(*refs):
    total = ITEM_COUNT
    (
        proj_c,
        out_c,
        in_0,
        down_0,
        proj_s,
        out_s,
        in_1,
        down_1,
        u1_in,
        u2_in,
        u3_in,
        last_ref,
        top_in,
        xq_c,
        sn_c,
        q_c,
        k_c,
        v_c,
        o_c,
        xn_s,
        q_s,
        k_s,
        v_s,
        o_s,
        lowered,
        before,
        active,
        latents_in,
        src_in,
        gains,
        mask_in,
        picks_in,
    ) = refs[:32]
    (up_out, down_out, proj_out_c, proj_out_s, end_out_c, end_out_s) = refs[32:38]
    (last_out, first_out, point_out, small_out) = refs[38:42]
    (grads_h, kin_lf, kin_la, kin_rf, kin_ra) = refs[42:47]
    (
        lwin_f,
        lwin_a,
        raw,
        rwin,
        stage,
        merged_f,
        merged_a,
        passing,
        lined_f,
        lined_a,
        crossed_f,
        crossed_a,
        pair,
        slope,
        rows_sum,
        hbuf,
        slots,
        qb,
        kb,
        vb,
        dob,
        dqkv,
        part_out,
        part_in,
        grad,
        ub,
        point_in,
        point_sum,
        small_in,
        small_sum,
    ) = refs[47:77]
    (
        kin_l_sems,
        kin_r_sems,
        raw_sems,
        win_sems,
        xy_sems,
        line_send,
        line_recv,
        cross_sems,
        out_sems,
        own_sems,
        lat_sems,
        far_sems,
        lat_own,
        point_sems,
        deal_sems,
        point_own,
        small_sems,
        pair_sems,
        slot_sems,
        h_sem,
        save_sems,
        act_sems,
    ) = refs[77:]
    section_at = lax.axis_index("section")
    batch_at = lax.axis_index("batch")
    core = lax.rem(batch_at, 2)
    spot = batch_at // 2
    x_at = lax.rem(section_at, 2)
    y_at = section_at // 2
    beside = section_at + 1 - 2 * x_at
    above = lax.rem(section_at + 2, 4)
    across = lax.rem(beside + 2, 4)
    sibling = batch_at + 1 - 2 * core
    flat = (beside, above)
    bits = (x_at, y_at)
    rows, width = 256, 1024

    peers = [(beside, batch_at), (above, batch_at), (across, batch_at), (section_at, sibling)]
    peers += [(section_at, lax.rem(spot + step, 4) * 2 + core) for step in (1, 2, 3)]
    barrier = pltpu.get_barrier_semaphore()
    for peer in peers:
        pl.semaphore_signal(barrier, inc=1, device_id=peer, device_id_type=MESH)
    pl.semaphore_wait(barrier, len(peers))

    def remote(source, target, sems, where, peer):
        return pltpu.make_async_remote_copy(
            source,
            target,
            sems.at[(0, *where)],
            sems.at[(1, *where)],
            device_id=peer,
            device_id_type=MESH,
        )

    feed_left = (pair, lowered.at[1], pair, lowered.at[0])
    feed_right = (active.at[1], slope, active.at[0], slope)
    att_left = (o_s, xn_s, xn_s, xn_s, o_c, xq_c, sn_c, sn_c)
    att_right = tuple(
        ref
        for turn in range(2)
        for ref in (grads_h.at[turn], dqkv.at[0], dqkv.at[1], dqkv.at[2])
    )

    def columns(spot_of, parity):
        return pl.ds(pl.multiple_of((2 * spot_of + parity) * 128, 128), 128)

    def kin_lefts(feed, job):
        source, target = (feed_left, kin_lf) if feed else (att_left, kin_la)
        return [
            remote(
                source[job].at[:, columns(part, 1 - core)],
                target.at[job, part],
                kin_l_sems,
                (job if feed else 4 + job, part),
                (section_at, sibling),
            )
            for part in range(4)
        ]

    def kin_right(feed, job, chunk):
        if feed:
            here = pl.ds(chunk * 1024, 1024)
            source, target = feed_right[job].at[:, here], kin_rf.at[job, :, here]
        else:
            source, target = att_right[job], kin_ra.at[job]
        where = (2 * job + chunk if feed else 8 + job,)
        return remote(source, target, kin_r_sems, where, (section_at, sibling))

    def item_of(index):
        turn, inner = index // 8, index % 8
        if inner < 4:
            return True, 2 * turn + inner // 2, inner % 2
        return False, 4 * turn + inner - 4, 0

    def window_copies(index):
        feed, job, chunk = item_of(index)
        slot = index % WINDOWS
        size = 512 if feed else 256
        if feed:
            here = pl.ds(chunk * 1024, 1024)
            sources = (feed_right[job].at[:, here], kin_rf.at[job, :, here])
        else:
            sources = (att_right[job], kin_ra.at[job])
        return [
            pltpu.make_async_copy(
                sources[whose],
                rwin.at[slot, pl.ds(whose * size, size)],
                win_sems.at[slot, whose],
            )
            for whose in range(2)
        ]

    def raw_copies(index, part):
        feed, job, _ = item_of(index)
        size = 512 if feed else 256
        own_left = (feed_left if feed else att_left)[job]
        kin_left = (kin_lf if feed else kin_la).at[job]
        sources = (own_left.at[:, columns(part, core)], kin_left.at[part])
        return [
            pltpu.make_async_copy(
                source, raw.at[part, whose, pl.ds(0, size)], raw_sems.at[part, whose]
            )
            for whose, source in enumerate(sources)
        ]

    def raw_start(index):
        feed, job, chunk = item_of(index)
        if chunk == 0:
            for copy in kin_lefts(feed, job):
                copy.wait_recv()
            for part in range(4):
                for copy in raw_copies(index, part):
                    copy.start(priority=LOCAL)

    def load(index):
        feed, job, chunk = item_of(index)
        kin_right(feed, job, chunk).wait_recv()
        for copy in window_copies(index):
            copy.start(priority=LOCAL)
        if chunk == 0:
            size = 512 if feed else 256
            target = (lwin_f if feed else lwin_a).at[job]
            for part in range(4):
                for whose, copy in enumerate(raw_copies(index, part)):
                    copy.wait()
                    place = raw.at[part, whose, pl.ds(0, size)]
                    target[part, :, whose * size : whose * size + size] = place[...].T
        if index + 1 < total:
            raw_start(index + 1)

    def is_feed(item):
        return lax.rem(item, 8) < 4

    def feed_job(item):
        return 2 * (item // 8) + lax.rem(item, 8) // 2

    def att_job(item):
        return 4 * (item // 8) + lax.rem(item, 8) - 4

    def loaded(slot, feed):
        size = 512 if feed else 256
        for whose in range(2):
            source = kin_rf.at[0, :, pl.ds(0, 1024)] if feed else kin_ra.at[0]
            pltpu.make_async_copy(
                source, rwin.at[slot, pl.ds(whose * size, size)], win_sems.at[slot, whose]
            ).wait()

    def by_kind(item, action):
        pl.when(is_feed(item))(functools.partial(action, item, True))
        pl.when(jnp.logical_not(is_feed(item)))(functools.partial(action, item, False))

    def merged_of(item, feed):
        return merged_f.at[lax.rem(item, 4)] if feed else merged_a.at[att_job(item)]

    def passing_of(item, feed, slot):
        ref = passing.at[lax.rem(item, 8), slot]
        return ref if feed else ref.at[:, pl.ds(0, 512)]

    def lined_of(item, feed):
        return lined_f.at[lax.rem(item, 4)] if feed else lined_a.at[att_job(item)]

    def crossed_of(item, feed):
        return crossed_f.at[lax.rem(item, 4)] if feed else crossed_a.at[att_job(item)]

    def products(item, choice, store):
        slot = lax.rem(item, WINDOWS)

        def quarter(index, carry):
            here = pl.ds(pl.multiple_of(index * 256, 256), 256)
            bit = choice[0] + index * (choice[1] - choice[0])
            first = pl.multiple_of(index * 512 + bit * 256, 256)
            left = lwin_a[att_job(item)].reshape(512, 512)
            right = rwin[slot, 0:512, pl.ds(first, 256)]
            tile = jnp.dot(left, right, preferred_element_type=F32).reshape(4, 128, 256)
            store(pl.ds(0, 4), here, tile)
            return carry

        lax.fori_loop(0, 2, quarter, 0)

    def xy_copies(item):
        return [
            remote(
                stage.at[lax.rem(att_job(item), STAGES), :, :, pl.ds(side * 256, 256)],
                merged_a.at[att_job(item), :, :, pl.ds(side * 256, 256)],
                xy_sems,
                (att_job(item), side),
                (flat[side], batch_at),
            )
            for side in range(2)
        ]

    def xy_sent(item):
        for copy in xy_copies(item):
            copy.wait_send()

    def line_copy(item, feed, dest, place, rightward):
        step = 1 if rightward else -1
        slot = 4 if not rightward and place - 1 == dest else dest
        return pltpu.make_async_remote_copy(
            merged_of(item, feed).at[dest],
            passing_of(item, feed, slot),
            line_send.at[item, dest],
            line_recv.at[item, slot],
            device_id=(section_at, batch_at + 2 * step),
            device_id_type=MESH,
        )

    def line_wait(item, feed, slot):
        pltpu.make_async_remote_copy(
            merged_of(item, feed).at[0],
            passing_of(item, feed, slot),
            line_send.at[item, 0],
            line_recv.at[item, slot],
            device_id=(section_at, sibling),
            device_id_type=MESH,
        ).wait_recv()

    def line_sent(item, feed):
        for step in (1, 2, 3):
            dest = lax.rem(spot + step, 4)
            pltpu.make_async_remote_copy(
                merged_of(item, feed).at[dest],
                passing_of(item, feed, 0),
                line_send.at[item, dest],
                line_recv.at[item, 0],
                device_id=(section_at, sibling),
                device_id_type=MESH,
            ).wait_send()

    def outset(item, feed):
        @pl.when(spot == 0)
        def _():
            for dest in (3, 2, 1):
                line_copy(item, feed, dest, 0, True).start()

        @pl.when(spot == 3)
        def _():
            for dest in (0, 1, 2):
                line_copy(item, feed, dest, 3, False).start()

    def drained(item, feed):
        line_sent(item, feed)
        if feed:
            feed_out(item, up_out).wait()
            feed_own(item, up_out).wait()
        else:
            for side in range(2):
                att_out(item, side, end_out_s, 0).wait()
                att_own(item, side, end_out_s, 0).wait()

    def offer(item, feed):
        slot = lax.rem(item, WINDOWS)
        loaded(slot, feed)
        if feed:

            @pl.when(item >= 8)
            def _():
                drained(item - 8, True)

            target = merged_of(item, True)

            def tile(index, carry):
                here = pl.ds(pl.multiple_of(index * 256, 256), 256)
                left = lwin_f[feed_job(item)].reshape(512, 1024)
                right = rwin[slot, :, here]
                value = jnp.dot(left, right, preferred_element_type=F32)
                target[:, :, here] = value.reshape(4, 128, 256).astype(BF)
                return carry

            lax.fori_loop(0, 4, tile, 0)
            outset(item, True)
        else:

            @pl.when(lax.rem(item, 8) >= 4 + STAGES)
            def _():
                xy_sent(item - STAGES)

            @pl.when(jnp.logical_and(item >= 12, lax.rem(item, 8) < 4 + STAGES))
            def _():
                xy_sent(item - STAGES - 4)

            def store(blocks, here, tile):
                stage[lax.rem(att_job(item), STAGES), blocks, :, here] = tile.astype(BF)

            products(item, (1 - x_at, 1 - y_at), store)
            for copy in xy_copies(item):
                copy.start()

    def take(item):
        for copy in xy_copies(item):
            copy.wait_recv()
        target = merged_a.at[att_job(item)]

        def store(blocks, here, tile):
            target[blocks, :, here] = (tile + target[blocks, :, here].astype(F32)).astype(BF)

        products(item, bits, store)
        outset(item, False)

    def first(item):
        pl.when(jnp.logical_not(is_feed(item)))(functools.partial(take, item))

    def relay(item, feed, dest, place, rightward):
        line_wait(item, feed, dest)
        target = merged_of(item, feed)
        arrived = passing_of(item, feed, dest)
        target[dest] = (target[dest].astype(F32) + arrived[...].astype(F32)).astype(BF)
        line_copy(item, feed, dest, place, rightward).start()

    def second_of(item, feed):
        @pl.when(spot == 1)
        def _():
            for dest in (3, 2):
                relay(item, feed, dest, 1, True)

        @pl.when(spot == 2)
        def _():
            for dest in (0, 1):
                relay(item, feed, dest, 2, False)

    def third_of(item, feed):
        @pl.when(spot == 1)
        def _():
            relay(item, feed, 0, 1, False)

        @pl.when(spot == 2)
        def _():
            relay(item, feed, 3, 2, True)

    def second(item):
        by_kind(item, second_of)

    def third(item):
        by_kind(item, third_of)

    def feed_cross(item):
        return remote(
            lined_of(item, True),
            crossed_of(item, True),
            cross_sems,
            (item, 0),
            (beside, batch_at),
        )

    def cross_copy(item, side):
        here = pl.ds(side * 256, 256)
        return remote(
            lined_of(item, False).at[:, here],
            crossed_of(item, False).at[:, here],
            cross_sems,
            (item, side),
            (flat[1 - side], batch_at),
        )

    def layer_of(item):
        return 1 - item // 8

    def feed_place(item, target):
        base = y_at * 2048 + lax.rem(item, 2) * 1024
        return target.at[layer_of(item), :, pl.ds(pl.multiple_of(base, 1024), 1024)]

    def feed_out(item, target):
        return remote(
            lined_of(item, True),
            feed_place(item, target),
            out_sems,
            (item, 0),
            (above, batch_at),
        )

    def feed_own(item, target):
        return pltpu.make_async_copy(
            lined_of(item, True), feed_place(item, target), own_sems.at[item, 0]
        )

    def feed_write(item):
        @pl.when(lax.rem(item, 8) < 2)
        def _():
            feed_out(item, down_out).start()
            feed_own(item, down_out).start(priority=LOCAL)

        @pl.when(lax.rem(item, 8) >= 2)
        def _():
            feed_out(item, up_out).start()
            feed_own(item, up_out).start(priority=LOCAL)

    def att_place(item, side, target, inner):
        base = inner * 1024 + side * 512 + bits[side] * 256
        return target.at[:, pl.ds(pl.multiple_of(base, 256), 256)]

    def att_out(item, side, target, inner):
        return remote(
            lined_of(item, False).at[:, pl.ds(side * 256, 256)],
            att_place(item, side, target, inner),
            out_sems,
            (item, side),
            (flat[side], batch_at),
        )

    def att_own(item, side, target, inner):
        return pltpu.make_async_copy(
            lined_of(item, False).at[:, pl.ds(side * 256, 256)],
            att_place(item, side, target, inner),
            own_sems.at[item, side],
        )

    def att_write(item):
        inner = lax.rem(item, 8) - 5
        for turn, proj, end in ((0, proj_out_s, end_out_s), (1, proj_out_c, end_out_c)):

            @pl.when(jnp.logical_and(item // 8 == turn, inner >= 0))
            def _():
                for side in range(2):
                    att_out(item, side, proj, inner).start()
                    att_own(item, side, proj, inner).start(priority=LOCAL)

            @pl.when(jnp.logical_and(item // 8 == turn, inner < 0))
            def _():
                for side in range(2):
                    att_out(item, side, end, 0).start()
                    att_own(item, side, end, 0).start(priority=LOCAL)

    def close_of(item, feed):
        for place in range(4):

            @pl.when(spot == place)
            def _():
                value = merged_of(item, feed)[place].astype(F32)
                if place > 0:
                    line_wait(item, feed, place)
                    value += passing_of(item, feed, place)[...].astype(F32)
                if place < 3:
                    line_wait(item, feed, 4)
                    value += passing_of(item, feed, 4)[...].astype(F32)
                lined_of(item, feed)[...] = value.astype(BF)

        if feed:
            feed_cross(item).start()
        else:
            for side in range(2):
                cross_copy(item, side).start()

    def close(item):
        by_kind(item, close_of)

    def finish_of(item, feed):
        if feed:
            feed_cross(item).wait()
        else:
            for side in range(2):
                cross_copy(item, side).wait()
        target = lined_of(item, feed)
        target[...] = (
            target[...].astype(F32) + crossed_of(item, feed)[...].astype(F32)
        ).astype(BF)
        if feed:
            feed_write(item)
        else:
            att_write(item)

    def finish(item):
        by_kind(item, finish_of)

    def small_copy(phase):
        if phase == 0:
            peer = (section_at, sibling)
        elif phase < 3:
            peer = (flat[phase - 1], batch_at)
        else:
            peer = (section_at, lax.rem(spot + phase - 2, 4) * 2 + core)
        return remote(
            small_sum.at[min(phase, 3)], small_in.at[phase], small_sems, (phase,), peer
        )

    quarter_rows = pair.shape[0] // 4

    def point_copy(which):
        peer = (beside, above, across)[which]
        return remote(
            pair.at[pl.ds(pl.multiple_of(peer * quarter_rows, 128), quarter_rows)],
            point_in.at[which],
            point_sems,
            (which,),
            (peer, batch_at),
        )

    def point_place():
        return point_out.at[pl.ds(pl.multiple_of(section_at * quarter_rows, 128), quarter_rows)]

    def point_deal(which):
        peer = (beside, above, across)[which]
        return remote(point_sum, point_place(), deal_sems, (which,), (peer, batch_at))

    def point_local():
        return pltpu.make_async_copy(point_sum, point_place(), point_own.at[0])

    pairs = ((last_ref, last_out), (grad, first_out))

    def lat_copy(which, way):
        source, target = pairs[which]
        return remote(
            source,
            target.at[pl.ds(pl.multiple_of(section_at * rows, rows), rows)],
            lat_sems,
            (which, way),
            (flat[way], batch_at),
        )

    def lat_far(which, way):
        target = pairs[which][1]
        low = flat[way] * rows + way * (rows // 2)
        part = target.at[pl.ds(pl.multiple_of(low, rows // 2), rows // 2)]
        return remote(part, part, far_sems, (which, way), (flat[1 - way], batch_at))

    def lat_local(which):
        source, target = pairs[which]
        return pltpu.make_async_copy(
            source,
            target.at[pl.ds(pl.multiple_of(section_at * rows, rows), rows)],
            lat_own.at[which],
        )

    def lat_start(which):
        lat_local(which).start(priority=LOCAL)
        for way in range(2):
            lat_copy(which, way).start()

    def lat_onward(which):
        for way in range(2):
            lat_copy(which, way).wait_recv()
            lat_far(which, way).start()

    loads = []
    for turn, (proj, out, up, down) in enumerate(
        ((proj_s, out_s, in_1, down_1), (proj_c, out_c, in_0, down_0))
    ):
        for chunk in range(2):
            loads += [down.at[:, pl.ds(chunk * 1024, 1024)], up.at[:, pl.ds(chunk * 1024, 1024)]]
        loads.append(out)
        loads += [proj.at[:, pl.ds(which * 1024, 1024)] for which in range(3)]

    def slot_copy(index):
        return pltpu.make_async_copy(loads[index], slots.at[index % 2], slot_sems.at[index % 2])

    def opened(index):
        slot_copy(index).wait()
        return index % 2

    def closed(index):
        if index + 2 < len(loads):
            slot_copy(index + 2).start(priority=LOCAL)

    def h_copy(index):
        layer, chunk = 1 - index // 2, index % 2
        return pltpu.make_async_copy(
            before.at[layer, :, pl.ds(chunk * 1024, 1024)], hbuf, h_sem.at[0]
        )

    def pair_over(turn):
        return remote(
            pair.at[pl.ds(0, rows)],
            pair.at[pl.ds(rows, rows)],
            pair_sems,
            (turn, 0),
            (above, batch_at),
        )

    def part_over(turn):
        return remote(
            part_out.at[turn], part_in.at[turn], pair_sems, (turn, 1), (above, batch_at)
        )

    def grad_saved(turn):
        return pltpu.make_async_copy(grad, grads_h.at[turn], save_sems.at[0])

    def act_copies(turn):
        chosen = ((q_s, k_s, v_s), (q_c, k_c, v_c))[turn]
        return [
            pltpu.make_async_copy(source, target, act_sems.at[index])
            for index, (source, target) in enumerate(zip(chosen, (qb, kb, vb)))
        ]

    def row_copy(index):
        if index == 3:
            source = latents_in.at[pl.ds(pl.multiple_of(section_at * rows, rows), rows)]
        else:
            source = (u3_in, u2_in, u1_in)[index]
        return pltpu.make_async_copy(source, ub, act_sems.at[3])

    def small_row(index, value):
        small_sum[0, index : index + 1, :] = value

    def open_pair(turn):
        pair[0:rows, :] = grad[...]
        pair_over(turn).start()

    def pair_ready(turn):
        pair_over(turn).wait()
        for copy in kin_lefts(True, 2 * turn):
            copy.start()

    def feed_chunk(turn, chunk):
        layer = 1 - turn
        base = 8 * turn + 2 * chunk
        h_copy(2 * turn + chunk).wait()
        if turn == 1:
            kin_right(True, 1, chunk).wait_send()
        slot = opened(base)

        def up_tile(here, index):
            there = pl.ds(pl.multiple_of(chunk * 1024 + index * 256, 256), 256)
            value = mm(pair[...], slots[slot, :, here]) * hbuf[:, here]
            short = value.astype(BF)
            slope[:, there] = short
            column = jnp.sum(short.astype(F32), axis=0, keepdims=True)
            for half in range(2):
                index_at = 7 + 4 * layer + 2 * half + chunk
                small_sum[0, index_at : index_at + 1, here] = jnp.where(
                    y_at == half, column, jnp.zeros_like(column)
                )

        tiles(4, up_tile)
        closed(base)
        if 2 * turn + chunk + 1 < 4:
            h_copy(2 * turn + chunk + 1).start(priority=LOCAL)
        kin_right(True, 2 * turn + 1, chunk).start()
        slot = opened(base + 1)

        def down_tile(there, _):
            value = mm_cols(slope[:, chunk * 1024 : chunk * 1024 + 1024], slots[slot, there, :])
            if chunk == 0:
                rows_sum[:, there] = value
            else:
                value = rows_sum[:, there] + value
                rows_sum[:, there] = value
                part_out[turn, :, there] = value[rows:].astype(BF)

        tiles(4, down_tile)
        closed(base + 1)
        if chunk == 1:
            if turn == 0:
                for copy in kin_lefts(True, 0):
                    copy.wait_send()
            part_over(turn).start()

    def row_steps(body, count):
        zero = jnp.zeros((1, width), F32)

        def step(index, carry):
            here = pl.ds(pl.multiple_of(index * 32, 32), 32)
            return tuple(a + b for a, b in zip(carry, body(here)))

        return lax.fori_loop(0, rows // 32, step, (zero,) * count)

    def lean(back, unit, inverse, gain):
        scaled = back * gain
        inner = (
            scaled
            - jnp.mean(scaled, axis=-1, keepdims=True)
            - unit * jnp.mean(scaled * unit, axis=-1, keepdims=True)
        )
        return inverse * inner, jnp.sum(back * unit, axis=0, keepdims=True)

    def feed_end(turn):
        layer = 1 - turn
        gain = gains[3 + layer : 4 + layer, :]
        part_over(turn).wait_recv()
        row_copy(2 * turn).wait()

        def body(here):
            unit, inverse = unit_rows(ub[here, :].astype(F32))
            back = rows_sum[here, :] + part_in[turn, here, :].astype(F32)
            dx, gain_part = lean(back, unit, inverse, gain)
            old = grad[here, :].astype(F32)
            grad[here, :] = (old + dx).astype(BF)
            return gain_part, jnp.sum(old, axis=0, keepdims=True)

        gain_grad, out_grad = row_steps(body, 2)
        row_copy(2 * turn + 1).start(priority=LOCAL)
        small_row(3 + layer, gain_grad)
        small_row(5 + layer, out_grad)
        grad_saved(turn).start(priority=LOCAL)
        slot = opened(8 * turn + 4)

        def tile(there, _):
            dob[:, there] = mm_cols(grad[...], slots[slot, there, :]).astype(BF)

        tiles(2, tile, 512)
        closed(8 * turn + 4)
        grad_saved(turn).wait()
        kin_right(False, 4 * turn, 0).start()

    def attend_heads(turn):
        scale = 1.0 / math.sqrt(HD)
        for copy in act_copies(turn):
            copy.wait()
        if turn == 1:
            for which in range(3):
                kin_right(False, 1 + which, 0).wait_send()

        def head(index, carry):
            here = pl.ds(pl.multiple_of(index * HD, HD), HD)
            q, k, v, do = qb[:, here], kb[:, here], vb[:, here], dob[:, here]
            scores = mm_cols(q, k) * scale
            if turn == 1:
                scores = jnp.where(mask_in[...] > 0.0, scores, MASKED)
            grown = jnp.exp(scores - jnp.max(scores, axis=-1, keepdims=True))
            soft = grown / jnp.sum(grown, axis=-1, keepdims=True)
            back = mm_cols(do, v)
            short = soft * (back - jnp.sum(soft * back, axis=-1, keepdims=True))
            dqkv[0, :, here] = (mm(short.astype(BF), k) * scale).astype(BF)
            dqkv[1, :, here] = (mm(short.T.astype(BF), q) * scale).astype(BF)
            dqkv[2, :, here] = mm(soft.T.astype(BF), do).astype(BF)
            return carry

        lax.fori_loop(0, width // HD, head, 0)
        if turn == 0:
            for copy in act_copies(1):
                copy.start(priority=LOCAL)
        for which in range(3):
            kin_right(False, 4 * turn + 1 + which, 0).start()

    def attend_end(turn):
        base = 8 * turn + 5
        for which in range(3):
            slot = opened(base + which)

            def tile(there, _):
                value = mm_cols(dqkv[which], slots[slot, there, :])
                if which == 0:
                    rows_sum[0:rows, there] = value
                elif which == 1:
                    rows_sum[rows : 2 * rows, there] = value
                else:
                    rows_sum[rows : 2 * rows, there] += value

            tiles(2, tile, 512)
            closed(base + which)
        row_copy(2 * turn + 1).wait()
        gain_q = gains[2:3, :] if turn == 0 else gains[0:1, :]
        gain_kv = gains[2:3, :] if turn == 0 else gains[1:2, :]

        def body(here):
            unit, inverse = unit_rows(ub[here, :].astype(F32))
            dx, gain_part = lean(rows_sum[here, :], unit, inverse, gain_q)
            if turn == 1:
                unit, inverse = unit_rows(src_in[here, :].astype(F32))
            there = pl.ds(pl.multiple_of(rows + here.start, 32), 32)
            ds, kv_part = lean(rows_sum[there, :], unit, inverse, gain_kv)
            fresh = grad[here, :].astype(F32) + dx
            if turn == 0:
                fresh += ds
            else:
                high = ds.astype(BF)
                part_out[0, here, :] = high
                part_out[1, here, :] = (ds - high.astype(F32)).astype(BF)
            grad[here, :] = fresh.astype(BF)
            return gain_part, kv_part

        if turn == 1:
            for which in range(2):
                part_over(which).wait_send()
            for copy in kin_lefts(True, 2):
                copy.wait_send()
        gain_grad, kv_grad = row_steps(body, 2)
        if turn == 0:
            row_copy(2).start(priority=LOCAL)
            small_row(2, gain_grad + kv_grad)
            open_pair(1)
        else:
            small_row(0, gain_grad)
            small_row(1, kv_grad)
            small_row(15, jnp.zeros_like(gain_grad))

            def tile(there, _):
                pair[:, there] = (
                    mm(picks_in[...], part_out[0, :, there])
                    + mm(picks_in[...], part_out[1, :, there])
                ).astype(BF)

            tiles(4, tile)
            small_copy(0).start()
            for which in range(3):
                point_copy(which).start()
            lat_start(1)

    def point_total():
        for which in range(3):
            point_copy(which).wait_recv()
        gathered = pair[
            pl.ds(pl.multiple_of(section_at * quarter_rows, 128), quarter_rows)
        ].astype(F32)
        for which in range(3):
            gathered += point_in[which].astype(F32)
        point_sum[...] = gathered.astype(BF)
        point_local().start(priority=LOCAL)
        for which in range(3):
            point_deal(which).start()

    def small_step(phase):
        small_copy(phase).wait_recv()
        small_sum[phase + 1] = small_sum[phase] + small_in[phase]
        if phase < 2:
            small_copy(phase + 1).start()
        else:
            for step in range(3):
                small_copy(3 + step).start()

    def small_end():
        for step in range(3):
            small_copy(3 + step).wait_recv()
        small_out[...] = (small_sum[3] + small_in[4]) + (small_in[3] + small_in[5])

    def rows_end():
        lat_onward(1)
        point_total()

    begin = pltpu.make_async_copy(top_in, grad, act_sems.at[4])
    begin.start()
    for index in range(2):
        slot_copy(index).start(priority=LOCAL)
    h_copy(0).start(priority=LOCAL)
    row_copy(0).start(priority=LOCAL)
    for copy in act_copies(0):
        copy.start(priority=LOCAL)
    begin.wait()
    open_pair(0)
    for part in range(2):
        kin_right(True, 0, part).start()
    pair_ready(0)
    for copy in kin_lefts(True, 1):
        copy.start()
    for job in range(4):
        for copy in kin_lefts(False, job):
            copy.start()
    for part in range(2):
        kin_right(True, 2, part).start()
    for copy in kin_lefts(True, 3):
        copy.start()
    for job in range(4, 8):
        for copy in kin_lefts(False, job):
            copy.start()
    raw_start(0)
    load(0)
    chain = {
        0: [functools.partial(feed_chunk, 0, 0), functools.partial(lat_start, 0)],
        1: [functools.partial(feed_chunk, 0, 1)],
        2: [functools.partial(feed_end, 0), functools.partial(lat_onward, 0)],
        3: [functools.partial(attend_heads, 0)],
        4: [functools.partial(attend_end, 0)],
        5: [functools.partial(pair_ready, 1), functools.partial(feed_chunk, 1, 0)],
        6: [functools.partial(feed_chunk, 1, 1)],
        7: [functools.partial(feed_end, 1)],
        8: [functools.partial(attend_heads, 1)],
        9: [functools.partial(attend_end, 1)],
        11: [functools.partial(small_step, 0), rows_end],
        13: [functools.partial(small_step, 1)],
        15: [functools.partial(small_step, 2)],
        17: [small_end],
    }

    def moment_body(moment, carry):
        @pl.when(moment < total)
        def _():
            by_kind(moment, offer)

        for lag, action in ((2, first), (3, second), (4, third), (5, close), (6, finish)):
            pl.when(jnp.logical_and(moment >= lag, moment < total + lag))(
                functools.partial(action, moment - lag)
            )
        for when, actions in chain.items():

            @pl.when(moment == when)
            def _():
                for action in actions:
                    action()

        for item in range(1, total):
            pl.when(moment == item - 1)(functools.partial(load, item))
        return carry

    lax.fori_loop(0, total + 6, moment_body, 0)

    for index in range(4):
        if index % 2 == 1:
            for copy in kin_lefts(True, index):
                copy.wait_send()
        if index != 1:
            for chunk in range(2):
                kin_right(True, index, chunk).wait_send()
    for index in range(8):
        for copy in kin_lefts(False, index):
            copy.wait_send()
        if index not in (1, 2, 3):
            kin_right(False, index, 0).wait_send()
    for phase in range(6):
        small_copy(phase).wait_send()
    for which in range(2):
        lat_local(which).wait()
        for way in range(2):
            lat_copy(which, way).wait_send()
            lat_far(which, way).wait()
    point_local().wait()
    for which in range(3):
        point_copy(which).wait_send()
        point_deal(which).wait()

    def drain(item, carry):
        @pl.when(item >= 4)
        def _():
            by_kind(item, drained)

        return carry

    for item in range(total - STAGES, total):
        xy_sent(item)
    lax.fori_loop(0, total, drain, 0)


def reduce_all(full, kept, latents, gains, mask, picks):
    total = ITEM_COUNT
    rows, width = kept[0].shape
    points = picks.shape[0]
    anywhere = pl.BlockSpec(memory_space=pl.ANY)
    vmem = pl.BlockSpec(memory_space=pltpu.VMEM)
    u1, u2, u3, u4, top = kept[:5]
    operands = [*full, u1, u2, u3, u4, top, *kept[5:16], *kept[17:], latents, kept[16]]
    operands += [gains, mask, picks]
    spaces = [anywhere] * (len(operands) - 4) + [vmem] * 4
    dma = pltpu.SemaphoreType.DMA
    flops = 2 * width * width * 24 * rows * 2
    return pl.pallas_call(
        reduce_kernel,
        out_shape=[
            jax.ShapeDtypeStruct((2, 128, 4 * width), BF),
            jax.ShapeDtypeStruct((2, 128, 4 * width), BF),
            jax.ShapeDtypeStruct((128, 3 * width), BF),
            jax.ShapeDtypeStruct((128, 3 * width), BF),
            jax.ShapeDtypeStruct((128, width), BF),
            jax.ShapeDtypeStruct((128, width), BF),
            jax.ShapeDtypeStruct((4 * rows, width), BF),
            jax.ShapeDtypeStruct((4 * rows, width), BF),
            jax.ShapeDtypeStruct((points, width), BF),
            jax.ShapeDtypeStruct((16, width), F32),
            jax.ShapeDtypeStruct((2, rows, width), BF),
            jax.ShapeDtypeStruct((4, 4, 2 * rows, 128), BF),
            jax.ShapeDtypeStruct((8, 4, rows, 128), BF),
            jax.ShapeDtypeStruct((4, 2 * rows, 2 * width), BF),
            jax.ShapeDtypeStruct((8, rows, width), BF),
        ],
        in_specs=spaces,
        out_specs=[anywhere] * 9 + [vmem] + [anywhere] * 5,
        scratch_shapes=[
            pltpu.VMEM((4, 4, 128, 1024), BF),
            pltpu.VMEM((8, 4, 128, 512), BF),
            pltpu.VMEM((4, 2, 512, 128), BF),
            pltpu.VMEM((WINDOWS, 1024, 1024), BF),
            pltpu.VMEM((STAGES, 4, 128, 512), BF),
            pltpu.VMEM((4, 4, 128, 1024), BF),
            pltpu.VMEM((8, 4, 128, 512), BF),
            pltpu.VMEM((8, 5, 128, 1024), BF),
            pltpu.VMEM((4, 128, 1024), BF),
            pltpu.VMEM((8, 128, 512), BF),
            pltpu.VMEM((4, 128, 1024), BF),
            pltpu.VMEM((8, 128, 512), BF),
            pltpu.VMEM((512, 1024), BF),
            pltpu.VMEM((512, 2048), BF),
            pltpu.VMEM((512, 1024), F32),
            pltpu.VMEM((512, 1024), F32),
            pltpu.VMEM((2, 1024, 1024), BF),
            pltpu.VMEM((256, 1024), BF),
            pltpu.VMEM((256, 1024), BF),
            pltpu.VMEM((256, 1024), BF),
            pltpu.VMEM((256, 1024), BF),
            pltpu.VMEM((3, 256, 1024), BF),
            pltpu.VMEM((2, 256, 1024), BF),
            pltpu.VMEM((2, 256, 1024), BF),
            pltpu.VMEM((256, 1024), BF),
            pltpu.VMEM((256, 1024), BF),
            pltpu.VMEM((3, points // 4, width), BF),
            pltpu.VMEM((points // 4, width), BF),
            pltpu.VMEM((6, 16, width), F32),
            pltpu.VMEM((4, 16, width), F32),
            dma((2, 12, 4)),
            dma((2, 16)),
            dma((4, 2)),
            dma((WINDOWS, 2)),
            dma((2, 8, 2)),
            dma((total, 4)),
            dma((total, 5)),
            dma((2, total, 2)),
            dma((2, total, 2)),
            dma((total, 2)),
            dma((2, 2, 2)),
            dma((2, 2, 2)),
            dma((2,)),
            dma((2, 3)),
            dma((2, 3)),
            dma((1,)),
            dma((2, 6)),
            dma((2, 2, 2)),
            dma((2,)),
            dma((1,)),
            dma((1,)),
            dma((5,)),
        ],
        compiler_params=pltpu.CompilerParams(
            collective_id=2, has_side_effects=True, vmem_limit_bytes=62 * 2**20
        ),
        cost_estimate=pl.CostEstimate(
            flops=flops, bytes_accessed=2**27, transcendentals=2**21
        ),
    )(*operands)[:10]


def plain_layers(full, spread, mine, source, valid, cot_own, picks, groups_all):
    proj_c, out_c, in_0, down_0, proj_s, out_s, in_1, down_1 = full
    width, hidden = in_0.shape

    def vector(first, count):
        return spread[:, first : first + count].reshape(-1)

    gains_cross = (vector(0, 1), vector(1, 1))
    gain_self = vector(2, 1)
    gains_mlp = (vector(3, 1), vector(4, 1))
    biases_out = (vector(5, 1), vector(6, 1))
    per_bias = hidden // width
    biases_in = (vector(7, per_bias), vector(7 + per_bias, per_bias))
    cot = cot_own.astype(F32)
    u1, kept_c = attend(mine, source, valid, gains_cross[0], gains_cross[1], proj_c, out_c)
    u2, kept_0 = feed(u1.astype(F32), gains_mlp[0], in_0, biases_in[0], down_0, biases_out[0])
    u2 = u2.astype(F32)
    u3, kept_s = attend(u2, u2, None, gain_self, gain_self, proj_s, out_s)
    u4, kept_1 = feed(u3.astype(F32), gains_mlp[1], in_1, biases_in[1], down_1, biases_out[1])
    final = u4.astype(F32)
    group_norm = jnp.sqrt(jnp.mean(final * final) + EPSILON)
    norm_mean = lax.psum(group_norm, ALL) / groups_all
    g4 = (cot + (norm_mean / group_norm) * final).astype(BF)

    dx, gain_1_grad, bias_1_grad, ob_1_grad, pairs_1 = feed_back(
        g4, kept_1, gains_mlp[1], in_1, down_1
    )
    g3 = (g4.astype(F32) + dx).astype(BF)
    dx, ds, gq, gkv, pairs_s = attend_back(g3, kept_s, gain_self, gain_self, proj_s, out_s)
    gain_s_grad = gq + gkv
    g2 = (g3.astype(F32) + dx + ds).astype(BF)
    dx, gain_0_grad, bias_0_grad, ob_0_grad, pairs_0 = feed_back(
        g2, kept_0, gains_mlp[0], in_0, down_0
    )
    g1 = (g2.astype(F32) + dx).astype(BF)
    dx, ds, cq_grad, ckv_grad, pairs_c = attend_back(
        g1, kept_c, gains_cross[0], gains_cross[1], proj_c, out_c
    )
    g0 = (g1.astype(F32) + dx).astype(BF)
    high = ds.astype(BF)
    low = (ds - high.astype(F32)).astype(BF)
    point_part = (mm_rows(picks, high) + mm_rows(picks, low)).astype(BF)
    small = jnp.concatenate(
        [
            cq_grad,
            ckv_grad,
            gain_s_grad,
            gain_0_grad,
            gain_1_grad,
            ob_0_grad,
            ob_1_grad,
            bias_0_grad,
            bias_1_grad,
            jnp.zeros_like(cq_grad),
        ]
    ).reshape(-1, width)
    pairs = pairs_1 + pairs_s + pairs_0 + pairs_c
    lefts, rights = [pair[0] for pair in pairs], [pair[1] for pair in pairs]
    def settled_grad(left, right):
        part = lax.psum_scatter(
            mm_rows(left, right).astype(BF), ALL, scatter_dimension=0, tiled=True
        )
        return lax.all_gather(part, "section", axis=0, tiled=True).astype(F32)

    done = [settled_grad(left, right) for left, right in pairs]
    mlp_in_grad = jnp.stack([done[6], done[0]])
    mlp_down_grad = jnp.stack([done[7], done[1]])
    proj_s_grad = jnp.concatenate(done[2:5], axis=1)
    proj_c_grad = jnp.concatenate(done[8:11], axis=1)
    out_s_grad, out_c_grad = done[5], done[11]
    points_sum = lax.psum(point_part, "section")
    latents_out = lax.all_gather(u4, "section", axis=0, tiled=True)
    g0_all = lax.all_gather(g0, "section", axis=0, tiled=True)
    small = lax.psum(small, ALL)
    return (
        norm_mean,
        latents_out,
        g0_all,
        points_sum,
        small,
        mlp_in_grad,
        mlp_down_grad,
        proj_c_grad,
        proj_s_grad,
        out_c_grad,
        out_s_grad,
    )


def per_device(
    latents,
    points,
    neighbours,
    lengths,
    cross_proj,
    cross_out,
    cross_gains,
    self_proj,
    self_out,
    self_gain,
    mlp_gain,
    mlp_in,
    mlp_in_bias,
    mlp_down,
    mlp_out_bias,
    cotangent,
):
    sections = lax.axis_size("section")
    section_at = lax.axis_index("section")
    width = latents.shape[1]
    hidden = mlp_in.shape[2]
    groups_dev = neighbours.shape[0]
    rows = latents.shape[0] // sections
    shard = cross_out.shape[0]
    piece = shard // sections
    groups_all = groups_dev * lax.axis_size("batch")

    def gathered(block):
        own = lax.dynamic_slice_in_dim(block, section_at * piece, piece, 0)
        return lax.all_gather(own, ALL, axis=0, tiled=True)

    projs = (cross_proj.reshape(shard, 3 * width), self_proj.reshape(shard, 3 * width))
    if lax.axis_size("batch") == 8:
        made = gather_forward(
            [projs[0], cross_out, mlp_in, mlp_down, projs[1], self_out],
            latents,
            cotangent,
            points,
            neighbours,
            lengths[:, None],
            [cross_gains, self_gain[None, :], mlp_gain, mlp_out_bias, mlp_in_bias],
        )
        full, gain_rows, norm_tile, mask, picks = made[:8], *made[8:12]
        norm_mean = norm_tile[0, 0]
        (
            mlp_in_grad,
            mlp_down_grad,
            proj_c_grad,
            proj_s_grad,
            out_c_grad,
            out_s_grad,
            latents_out,
            g0_all,
            points_sum,
            small,
        ) = reduce_all(full, made[12:], latents, gain_rows, mask, picks)
        mlp_in_grad = mlp_in_grad.astype(F32)
        mlp_down_grad = mlp_down_grad.astype(F32)
        proj_c_grad, proj_s_grad = proj_c_grad.astype(F32), proj_s_grad.astype(F32)
        out_c_grad, out_s_grad = out_c_grad.astype(F32), out_s_grad.astype(F32)
    else:
        vectors = jnp.concatenate(
            [
                cross_gains.reshape(-1),
                self_gain,
                mlp_gain.reshape(-1),
                mlp_out_bias.reshape(-1),
                mlp_in_bias.reshape(-1),
                jnp.zeros_like(self_gain),
            ]
        ).reshape(-1, shard)
        cot_own = lax.dynamic_slice_in_dim(cotangent, section_at * rows, rows, 0)
        mine = lax.dynamic_slice_in_dim(latents, section_at * rows, rows, 0).astype(F32)
        listed = lax.dynamic_index_in_dim(neighbours, section_at, 0, keepdims=False)
        length = lax.dynamic_index_in_dim(lengths, section_at, 0, keepdims=False)
        valid = jnp.arange(listed.shape[0], dtype=jnp.int32) < length
        picks = listed[:, None] == jnp.arange(points.shape[0], dtype=jnp.int32)[None, :]
        picks = picks.astype(BF)
        source = mm(picks, points)
        blocks = [projs[0], cross_out, mlp_in[0], mlp_down[0]]
        blocks += [projs[1], self_out, mlp_in[1], mlp_down[1]]
        full = [gathered(block) for block in blocks]
        spread = lax.all_gather(vectors, "batch", axis=0, tiled=False)
        (
            norm_mean,
            latents_out,
            g0_all,
            points_sum,
            small,
            mlp_in_grad,
            mlp_down_grad,
            proj_c_grad,
            proj_s_grad,
            out_c_grad,
            out_s_grad,
        ) = plain_layers(full, spread.astype(F32), mine, source, valid, cot_own, picks, groups_all)
    points_grad = points_sum.astype(F32)
    latents_grad = g0_all.astype(F32)
    per_bias = hidden // width
    batch_at = lax.axis_index("batch")

    def own(first, count):
        flat = small[first : first + count].reshape(-1)
        size = flat.shape[0] // lax.axis_size("batch")
        return lax.dynamic_slice_in_dim(flat, batch_at * size, size, 0)

    return (
        latents_out,
        latents_grad,
        points_grad,
        proj_c_grad.reshape(shard, 3, width),
        out_c_grad,
        jnp.stack([own(0, 1), own(1, 1)]),
        proj_s_grad.reshape(shard, 3, width),
        out_s_grad,
        own(2, 1),
        jnp.stack([own(3, 1), own(4, 1)]),
        mlp_in_grad,
        jnp.stack([own(7, per_bias), own(7 + per_bias, per_bias)]),
        mlp_down_grad,
        jnp.stack([own(5, 1), own(6, 1)]),
        norm_mean,
    )


def solution(mesh):
    rows = P("batch", None)
    cols = P(None, "batch")
    block = P("batch", None, None)
    pair = P(None, "batch", None)
    return jax.shard_map(
        per_device,
        mesh=mesh,
        in_specs=(
            rows,
            rows,
            rows,
            P("batch"),
            block,
            rows,
            cols,
            block,
            rows,
            P("batch"),
            cols,
            pair,
            cols,
            pair,
            cols,
            rows,
        ),
        out_specs=(
            rows,
            rows,
            rows,
            block,
            rows,
            cols,
            block,
            rows,
            P("batch"),
            cols,
            pair,
            cols,
            pair,
            cols,
            P(),
        ),
        check_vma=False,
    )
```

```python
import functools
import math

import jax
import jax.numpy as jnp
from jax import lax
from jax.experimental import pallas as pl
from jax.experimental.pallas import tpu as pltpu
from jax.sharding import PartitionSpec as P

HD = 128
EPSILON = 1e-05
MASKED = -1e30
BF = jnp.bfloat16
F32 = jnp.float32
ALL = ("batch", "section")
MESH = pl.DeviceIdType.MESH
GATHER_WIDTH = 1024
AHEAD = 4
LOCAL = 1
SLOTS = 3
GATHERED = tuple(
    (4 * layer + index, start)
    for layer in range(2)
    for index, start in (
        [(0, 0), (0, 1024), (0, 2048), (1, 0)]
        + [(2 + which, chunk) for chunk in range(0, 2048, 1024) for which in range(2)]
    )
)


def mm(a, b):
    return jnp.dot(a, b, preferred_element_type=F32)


def mm_rows(a, b):
    return lax.dot_general(a, b, (((0,), (0,)), ((), ())), preferred_element_type=F32)


def mm_cols(a, b):
    return lax.dot_general(a, b, (((1,), (1,)), ((), ())), preferred_element_type=F32)


def unit_rows(values):
    centred = values - jnp.mean(values, axis=-1, keepdims=True)
    inverse = lax.rsqrt(jnp.mean(centred * centred, axis=-1, keepdims=True) + EPSILON)
    return centred * inverse, inverse


def norm_back(gradient, unit, inverse, gain):
    scaled = gradient * gain
    inner = (
        scaled
        - jnp.mean(scaled, axis=-1, keepdims=True)
        - unit * jnp.mean(scaled * unit, axis=-1, keepdims=True)
    )
    return inverse * inner, jnp.sum(gradient * unit, axis=0)


def heads_of(rows):
    return rows.reshape(rows.shape[0], -1, HD)


def softmax(q, k, valid):
    scores = jnp.einsum(
        "lhc,nhc->hln", heads_of(q), heads_of(k), preferred_element_type=F32
    ) * (1.0 / math.sqrt(HD))
    if valid is not None:
        scores = jnp.where(valid[None, None, :], scores, MASKED)
    grown = jnp.exp(scores - jnp.max(scores, axis=-1, keepdims=True))
    return grown / jnp.sum(grown, axis=-1, keepdims=True)


def attend(inputs, source, valid, gain_q, gain_kv, proj, out):
    unit_x, inv_x = unit_rows(inputs)
    queries_in = (unit_x * gain_q).astype(BF)
    unit_s, inv_s = unit_rows(source)
    keys_in = (unit_s * gain_kv).astype(BF)
    width = inputs.shape[1]
    q = mm(queries_in, proj[:, :width]).astype(BF)
    kv = mm(keys_in, proj[:, width:]).astype(BF)
    k, v = kv[:, :width], kv[:, width:]
    soft = softmax(q, k, valid)
    mixture = jnp.einsum("hln,nhc->lhc", soft.astype(BF), heads_of(v), preferred_element_type=F32)
    mixture = mixture.reshape(inputs.shape).astype(BF)
    result = (inputs + mm(mixture, out)).astype(BF)
    return result, (unit_x, inv_x, queries_in, unit_s, inv_s, keys_in, q, k, v, soft, mixture)


def attend_back(gradient, kept, gain_q, gain_kv, proj, out):
    unit_x, inv_x, queries_in, unit_s, inv_s, keys_in, q, k, v, soft, mixture = kept
    width = gradient.shape[1]
    scale = 1.0 / math.sqrt(HD)
    grad_mix = mm_cols(gradient, out).astype(BF)
    grad_soft = jnp.einsum(
        "lhc,nhc->hln", heads_of(grad_mix), heads_of(v), preferred_element_type=F32
    )
    inner = jnp.sum(soft * grad_soft, axis=-1, keepdims=True)
    grad_scores = (soft * (grad_soft - inner)).astype(BF)
    dq = jnp.einsum("hln,nhc->lhc", grad_scores, heads_of(k), preferred_element_type=F32) * scale
    dk = jnp.einsum("hln,lhc->nhc", grad_scores, heads_of(q), preferred_element_type=F32) * scale
    dv = jnp.einsum(
        "hln,lhc->nhc", soft.astype(BF), heads_of(grad_mix), preferred_element_type=F32
    )
    dq = dq.reshape(gradient.shape).astype(BF)
    dk = dk.reshape(-1, width).astype(BF)
    dv = dv.reshape(-1, width).astype(BF)
    grad_x, gain_q_grad = norm_back(mm_cols(dq, proj[:, :width]), unit_x, inv_x, gain_q)
    back_s = mm_cols(dk, proj[:, width : 2 * width]) + mm_cols(dv, proj[:, 2 * width :])
    grad_s, gain_kv_grad = norm_back(back_s, unit_s, inv_s, gain_kv)
    pairs = ((queries_in, dq), (keys_in, dk), (keys_in, dv), (mixture, gradient))
    return grad_x, grad_s, gain_q_grad, gain_kv_grad, pairs


def feed(inputs, gain, w_in, b_in, w_down, b_out):
    unit, inverse = unit_rows(inputs)
    lowered = (unit * gain).astype(BF)
    pre_act = mm(lowered, w_in) + b_in
    active = jax.nn.gelu(pre_act).astype(BF)
    result = (inputs + mm_cols(active, w_down) + b_out).astype(BF)
    return result, (unit, inverse, lowered, pre_act, active)


def feed_back(gradient, kept, gain, w_in, w_down):
    unit, inverse, lowered, pre_act, active = kept
    grad_act = mm(gradient, w_down)
    grad_pre = jax.vjp(jax.nn.gelu, pre_act)[1](grad_act)[0].astype(BF)
    grad_x, gain_grad = norm_back(mm_cols(grad_pre, w_in), unit, inverse, gain)
    bias_grad = jnp.sum(grad_pre.astype(F32), axis=0)
    out_grad = jnp.sum(gradient.astype(F32), axis=0)
    return grad_x, gain_grad, bias_grad, out_grad, ((lowered, grad_pre), (gradient, active))


def gelu_both(value):
    factor = math.sqrt(2.0 / math.pi)
    square = value * value
    bent = jnp.tanh(factor * value * (1.0 + 0.044715 * square))
    inner = factor * (1.0 + 3.0 * 0.044715 * square)
    half = 0.5 * (1.0 + bent)
    return value * half, half + 0.5 * value * (1.0 - bent * bent) * inner


def tiles(count, body, size=256):
    def step(index, carry):
        body(pl.ds(pl.multiple_of(index * size, size), size), index)
        return carry

    lax.fori_loop(0, count, step, 0)


def norm_into(source, gain, target):
    def step(index, carry):
        here = pl.ds(pl.multiple_of(index * 32, 32), 32)
        unit, _ = unit_rows(source[here, :].astype(F32))
        target[here, :] = (unit * gain).astype(BF)
        return carry

    lax.fori_loop(0, source.shape[0] // 32, step, 0)


def gather_kernel(*refs):
    cross_proj, cross_out, mlp_in, mlp_down, self_proj, self_out = refs[:6]
    latents_in, cot_all, points_in, near_in, length_in = refs[6:11]
    vec_parts = refs[11:16]
    section_at = lax.axis_index("section")
    batch_at = lax.axis_index("batch")
    x_at = lax.rem(section_at, 2)
    y_at = section_at // 2
    ins = (
        cross_proj,
        cross_out,
        mlp_in.at[0],
        mlp_down.at[0],
        self_proj,
        self_out,
        mlp_in.at[1],
        mlp_down.at[1],
    )
    count = len(ins)
    outs = refs[16 : 16 + count]
    rest = refs[16 + count :]
    gains, norm_out, mask_in, picks_out = rest[:4]
    kept_outs = rest[4:24]
    (
        u1,
        u2,
        u3,
        u4,
        grad_top,
        xq_c,
        sn_c,
        q_c,
        k_c,
        v_c,
        o_c,
        xn_s,
        q_s,
        k_s,
        v_s,
        o_s,
        src_in,
        lowered,
        before,
        active,
        x_in,
        cot_in,
        vec_in,
        vec_rows,
        slots,
        total_rows,
        part_out,
        part_in,
        vec_out,
        biases,
        plane,
        line_in,
    ) = rest[24:56]
    (own_sem, send, recv, kin_send, kin_recv, vec_sems) = rest[56:62]
    (slot_sems, kept_sems, plane_sems, line_sems, pair_sems, row_sems) = rest[62:]
    line = 4
    core = lax.rem(batch_at, 2)
    spot = batch_at // 2
    beside = section_at + 1 - 2 * x_at
    above = lax.rem(section_at + 2, 4)
    sibling = batch_at + 1 - 2 * core
    shard = ins[0].shape[0]
    place = section_at * 2 + core
    rows = x_in.shape[0]

    def down_line(step):
        return lax.rem(spot + step, line) * 2 + core

    def up_line(step):
        return lax.rem(spot + line - step, line) * 2 + core

    near_peers = []
    for turn in range(1, 8):
        other = lax.rem(place + turn, 8)
        near_peers.append((other // 2, spot * 2 + lax.rem(other, 2)))
    line_peers = [(section_at, down_line(step)) for step in range(1, line)]
    far_peers = [(section_at, down_line(step) + 1 - 2 * core) for step in range(1, line)]
    vec_peers = [(section_at, sibling)] + line_peers + far_peers
    peers = near_peers + line_peers + far_peers
    barrier = pltpu.get_barrier_semaphore()
    for peer in peers:
        pl.semaphore_signal(barrier, inc=1, device_id=peer, device_id_type=MESH)
    pl.semaphore_wait(barrier, len(peers))

    def spread(ref, owner, first, size):
        return ref.at[pl.ds(pl.multiple_of(owner * shard, shard), shard), pl.ds(first, size)]

    def is_feed(item):
        return item % 8 >= 4

    def source_of(item, first, size):
        index, start = GATHERED[item]
        if is_feed(item):
            first = pl.multiple_of(first + y_at * outs[index].shape[1], 128)
        return ins[index].at[:, pl.ds(first, size)]

    def piece(item):
        start = GATHERED[item][1]
        if is_feed(item):
            return pl.multiple_of(start + x_at * 512, 128), 512
        return pl.multiple_of(start + section_at * 256, 128), 256

    def own_line(item, way):
        first, size = piece(item)
        return pltpu.make_async_remote_copy(
            source_of(item, first, size),
            spread(outs[GATHERED[item][0]], batch_at, first, size),
            send.at[5 * way, item, 0],
            recv.at[0, item, 3 if way else 1],
            device_id=(section_at, batch_at + (-2 if way else 2)),
            device_id_type=MESH,
        )

    def onward_line(item, step, way):
        first, size = piece(item)
        ref = spread(outs[GATHERED[item][0]], up_line(step), first, size)
        return pltpu.make_async_remote_copy(
            ref,
            ref,
            send.at[0, item, step],
            recv.at[0, item, step - 1 if way else step + 1],
            device_id=(section_at, batch_at + (-2 if way else 2)),
            device_id_type=MESH,
        )

    def came_line(item, step):
        first, size = piece(item)
        ref = spread(outs[GATHERED[item][0]], up_line(step), first, size)
        return pltpu.make_async_remote_copy(
            ref,
            ref,
            send.at[0, item, step],
            recv.at[0, item, step],
            device_id=(section_at, sibling),
            device_id_type=MESH,
        )

    def start_line(item):
        @pl.when(spot < 3)
        def _():
            own_line(item, 0).start()

        @pl.when(spot > 0)
        def _():
            own_line(item, 1).start()

    def arrive_line(item, apart):
        @pl.when(spot >= apart)
        def _():
            came_line(item, apart).wait_recv()

            @pl.when(spot < 3)
            def _():
                onward_line(item, apart, 0).start()

            for copy in near(item, apart):
                copy.start()

        @pl.when(spot + apart <= 3)
        def _():
            came_line(item, 4 - apart).wait_recv()

            @pl.when(spot > 0)
            def _():
                onward_line(item, 4 - apart, 1).start()

            for copy in near(item, 4 - apart):
                copy.start()

    def sent_line(item):
        @pl.when(spot < 3)
        def _():
            own_line(item, 0).wait_send()

        @pl.when(spot > 0)
        def _():
            own_line(item, 1).wait_send()

        for apart in (1, 2, 3):

            @pl.when(jnp.logical_and(spot >= apart, spot < 3))
            def _():
                onward_line(item, apart, 0).wait_send()

            @pl.when(jnp.logical_and(spot + apart <= 3, spot > 0))
            def _():
                onward_line(item, 4 - apart, 1).wait_send()

        for step in (1, 2, 3):
            for copy in near(item, step):
                copy.wait_send()

    def plane_copy(item, step, way, low, wide, peer):
        ref = spread(outs[GATHERED[item][0]], up_line(step), low, wide)
        return pltpu.make_async_remote_copy(
            ref,
            ref,
            send.at[way, item, step],
            recv.at[way, item, step],
            device_id=(peer, batch_at),
            device_id_type=MESH,
        )

    def near(item, step):
        first, size = piece(item)
        copies = [plane_copy(item, step, 1, first, size, beside)]
        if not is_feed(item):
            copies.append(plane_copy(item, step, 2, first, size, above))
        return copies

    def far(item, step):
        start = GATHERED[item][1]
        by_y = pl.multiple_of(start + beside * 256, 128)
        by_x = pl.multiple_of(start + above * 256 + 128, 128)
        return [
            plane_copy(item, step, 3, by_y, 128, above),
            plane_copy(item, step, 4, by_x, 128, beside),
        ]

    def kin(item, step):
        index, start = GATHERED[item]
        if step == 0:
            source = source_of(item, start, GATHER_WIDTH)
        else:
            source = spread(outs[index], up_line(step), start, GATHER_WIDTH)
        return pltpu.make_async_remote_copy(
            source,
            spread(outs[index], up_line(step), start, GATHER_WIDTH),
            kin_send.at[item, step],
            kin_recv.at[item, step],
            device_id=(section_at, sibling),
            device_id_type=MESH,
        )

    def own(item):
        index, start = GATHERED[item]
        return pltpu.make_async_copy(
            source_of(item, start, GATHER_WIDTH),
            spread(outs[index], batch_at, start, GATHER_WIDTH),
            own_sem.at[item],
        )

    def vec_copy(which):
        return pltpu.make_async_remote_copy(
            vec_in,
            vec_out.at[batch_at],
            vec_sems.at[0, which],
            vec_sems.at[1, which],
            device_id=vec_peers[which],
            device_id_type=MESH,
        )

    def slot_copy(item):
        index, start = GATHERED[item]
        return pltpu.make_async_copy(
            outs[index].at[:, pl.ds(start, GATHER_WIDTH)],
            slots.at[item % SLOTS],
            slot_sems.at[item % SLOTS],
        )

    def near_norm(turn):
        return pltpu.make_async_remote_copy(
            plane.at[8],
            plane.at[place],
            plane_sems.at[0, turn],
            plane_sems.at[1, turn],
            device_id=near_peers[turn],
            device_id_type=MESH,
        )

    def far_norm(step):
        return pltpu.make_async_remote_copy(
            line_in.at[4],
            line_in.at[spot],
            line_sems.at[0, step],
            line_sems.at[1, step],
            device_id=line_peers[step],
            device_id_type=MESH,
        )

    def rows_over(layer):
        return pltpu.make_async_remote_copy(
            lowered.at[layer, pl.ds(0, rows)],
            lowered.at[layer, pl.ds(rows, rows)],
            pair_sems.at[0, layer, 0],
            pair_sems.at[1, layer, 0],
            device_id=(above, batch_at),
            device_id_type=MESH,
        )

    def part_over(layer):
        return pltpu.make_async_remote_copy(
            part_out.at[layer],
            part_in.at[layer],
            pair_sems.at[0, layer, 1],
            pair_sems.at[1, layer, 1],
            device_id=(above, batch_at),
            device_id_type=MESH,
        )

    steps = range(1, line)
    total = len(GATHERED)
    started = []

    def launch(copies):
        for copy in copies:
            copy.start()
        started.extend(copies)

    kept = (
        (u1, u2, u3, u4, grad_top)
        + (xq_c, sn_c, q_c, k_c, v_c, o_c)
        + (xn_s, q_s, k_s, v_s, o_s)
        + (src_in, lowered, before, active)
    )
    names = {id(ref): place for place, ref in enumerate(kept)}

    def keep(*chosen):
        for ref in chosen:
            index = names[id(ref)]
            pltpu.make_async_copy(ref, kept_outs[index], kept_sems.at[index]).start(priority=LOCAL)

    def row(index):
        return gains[index : index + 1, :]

    def project(source, target, slot):
        def tile(columns, _):
            target[:, columns] = mm(source[...], slots[slot, :, columns]).astype(BF)

        tiles(2, tile, 512)

    def heads(q, k, v, o, masked):
        def head(index, carry):
            here = pl.ds(pl.multiple_of(index * HD, HD), HD)
            scores = mm_cols(q[:, here], k[:, here]) * (1.0 / math.sqrt(HD))
            if masked:
                scores = jnp.where(mask_in[...] > 0.0, scores, MASKED)
            grown = jnp.exp(scores - jnp.max(scores, axis=-1, keepdims=True))
            soft = grown / jnp.sum(grown, axis=-1, keepdims=True)
            o[:, here] = mm(soft.astype(BF), v[:, here]).astype(BF)
            return carry

        lax.fori_loop(0, q.shape[1] // HD, head, 0)

    def close_attention(inputs, o, target, slot):
        def tile(columns, _):
            target[:, columns] = (
                inputs[:, columns].astype(F32) + mm(o[...], slots[slot, :, columns])
            ).astype(BF)

        tiles(2, tile, 512)

    def feed_up(layer, chunk, slot):
        def tile(columns, index):
            first = chunk * GATHER_WIDTH + index * 512
            there = pl.ds(pl.multiple_of(first, 512), 512)
            lanes = pl.ds(pl.multiple_of(y_at * 2048 + first, 512), 512)
            value = mm(lowered[layer], slots[slot, :, columns]) + biases[layer : layer + 1, lanes]
            active_part, slope = gelu_both(value)
            before[layer, :, there] = slope
            active[layer, :, there] = active_part.astype(BF)

        tiles(2, tile, 512)

    def feed_down(layer, chunk, slot):
        chosen = pl.ds(chunk * GATHER_WIDTH, GATHER_WIDTH)

        def tile(columns, _):
            value = mm_cols(active[layer, :, chosen], slots[slot, columns, :])
            if chunk == 0:
                total_rows[:, columns] = value
            else:
                value = total_rows[:, columns] + value
                total_rows[:, columns] = value
                part_out[layer, :, columns] = value[rows:].astype(BF)

        tiles(2, tile, 512)

    def feed_close(layer):
        inputs, target = (u1, u3)[layer], (u2, u4)[layer]
        part_over(layer).wait_recv()

        def tile(columns, _):
            target[:, columns] = (
                inputs[:, columns].astype(F32)
                + (total_rows[0:rows, columns] + part_in[layer, :, columns].astype(F32))
                + gains[5 + layer : 6 + layer, columns]
            ).astype(BF)

        tiles(2, tile, 512)
        keep(target)

    def work(item):
        slot_copy(item).wait()
        slot = item % SLOTS
        layer, stage = item // 8, item % 8
        inputs = (x_in, u2)[layer]
        middle = (u1, u3)[layer]
        q, k, v, o = ((q_c, k_c, v_c, o_c), (q_s, k_s, v_s, o_s))[layer]
        if stage == 0:
            if layer == 0:
                norm_into(x_in, row(0), xq_c)
                norm_into(src_in, row(1), sn_c)
                keep(xq_c, sn_c)
            else:
                feed_close(0)
                norm_into(u2, row(2), xn_s)
                keep(xn_s)
            project((xq_c, xn_s)[layer], q, slot)
        elif stage == 1:
            project((sn_c, xn_s)[layer], k, slot)
        elif stage == 2:
            project((sn_c, xn_s)[layer], v, slot)
            heads(q, k, v, o, layer == 0)
            keep(q, k, v, o)
        elif stage == 3:
            close_attention(inputs, o, middle, slot)
            norm_into(middle, row(3 + layer), lowered.at[layer, pl.ds(0, rows)])
            launch([rows_over(layer)])
            keep(middle)
        elif stage % 2 == 0:
            if stage == 4:
                rows_over(layer).wait_recv()
            feed_up(layer, (stage - 4) // 2, slot)
        else:
            feed_down(layer, (stage - 4) // 2, slot)
            if stage == 7:
                launch([part_over(layer)])

    for item in range(AHEAD):
        start_line(item)
    here = pl.ds(pl.multiple_of(section_at * rows, rows), rows)
    row_copies = [
        pltpu.make_async_copy(latents_in.at[here], x_in, row_sems.at[0]),
        pltpu.make_async_copy(cot_all.at[here], cot_in, row_sems.at[1]),
    ]
    for copy in row_copies:
        copy.start()
    cross_gain, self_gain, feed_gain, out_bias, in_bias = vec_parts
    vec_rows[...] = jnp.zeros_like(vec_rows)
    vec_rows[0:2, :] = cross_gain[...].astype(F32)
    vec_rows[2:3, :] = self_gain[...].astype(F32)
    vec_rows[3:5, :] = feed_gain[...].astype(F32)
    vec_rows[5:7, :] = out_bias[...].astype(F32)
    bias_rows = in_bias[...].astype(F32)
    for layer in range(2):
        for part_at in range(4):
            index = 7 + 4 * layer + part_at
            vec_rows[index : index + 1, :] = bias_rows[
                layer : layer + 1, part_at * 128 : part_at * 128 + 128
            ]
    vec_in[...] = vec_rows[...].astype(BF)
    vec_out[batch_at] = vec_in[...]
    for which in range(7):
        vec_copy(which).start()
    lanes = lax.broadcasted_iota(jnp.int32, (1, rows), 1)
    length = length_in[pl.ds(section_at, 1), :]
    mask_in[...] = jnp.where(lanes < length, 1.0, 0.0)
    point_at = lax.broadcasted_iota(jnp.int32, (points_in.shape[0], rows), 0)
    wanted = near_in[pl.ds(section_at, 1), :]
    picks = jnp.where(point_at == wanted, 1.0, 0.0)
    picks_out[...] = picks.astype(BF)
    turned = picks.T.astype(BF)

    def source_tile(columns, _):
        src_in[:, columns] = mm(turned, points_in[:, columns]).astype(BF)

    tiles(2, source_tile, 512)
    keep(src_in)
    for copy in row_copies:
        copy.wait()
    for moment in range(-2, total + 4):
        if moment + 2 + AHEAD < total:
            start_line(moment + 2 + AHEAD)
        for apart in (1, 2, 3):
            if 0 <= moment + 3 - apart < total:
                arrive_line(moment + 3 - apart, apart)
        if 0 <= moment < total:
            own(moment).start(priority=LOCAL)
            launch([kin(moment, 0)])
        if 0 <= moment - 1 < total:
            for step in steps:
                if is_feed(moment - 1):
                    near(moment - 1, step)[0].wait_recv()
                    launch([kin(moment - 1, step)])
                else:
                    for copy, onward in zip(near(moment - 1, step), far(moment - 1, step)):
                        copy.wait_recv()
                        launch([onward])
        if 0 <= moment - 2 < total and not is_feed(moment - 2):
            for step in steps:
                for copy in far(moment - 2, step):
                    copy.wait_recv()
                launch([kin(moment - 2, step)])
        if moment == 2:
            for which in range(7):
                vec_copy(which).wait()
            for owner in range(8):
                values = vec_out[owner].astype(F32)
                gains[:, owner * 128 : owner * 128 + 128] = values
                for layer in range(2):
                    for part_at in range(4):
                        first = owner * 512 + part_at * 128
                        index = 7 + 4 * layer + part_at
                        biases[layer : layer + 1, first : first + 128] = values[index : index + 1]
        if 0 <= moment - 4 < total:
            work(moment - 4)
        if 0 <= moment - 3 < total:
            own(moment - 3).wait()
            for step in range(line):
                kin(moment - 3, step).wait_recv()
            slot_copy(moment - 3).start(priority=LOCAL)
    keep(lowered, before, active)
    feed_close(1)

    def square(index, carry):
        here = pl.ds(pl.multiple_of(index * 32, 32), 32)
        values = u4[here, :].astype(F32)
        return carry + jnp.sum(values * values, axis=0, keepdims=True)

    squares = lax.fori_loop(0, u4.shape[0] // 32, square, jnp.zeros((1, u4.shape[1]), F32))
    mean = jnp.sum(squares, axis=1, keepdims=True) / (u4.shape[0] * u4.shape[1])
    group_norm = jnp.sqrt(mean + EPSILON)
    plane[8] = jnp.broadcast_to(group_norm, plane.shape[1:])
    for turn in range(7):
        near_norm(turn).start()
    plane[place] = plane[8]
    for turn in range(7):
        near_norm(turn).wait()
    line_in[4] = jnp.sum(plane[0:8], axis=0)
    for step in range(3):
        far_norm(step).start()
    line_in[spot] = line_in[4]
    for step in range(3):
        far_norm(step).wait()
    norm_mean = jnp.sum(line_in[0:4], axis=0) / 32.0
    norm_out[...] = norm_mean
    ratio = norm_mean[0:1, 0:1] / group_norm

    def top(index, carry):
        here = pl.ds(pl.multiple_of(index * 32, 32), 32)
        grad_top[here, :] = (
            cot_in[here, :].astype(F32) + ratio * u4[here, :].astype(F32)
        ).astype(BF)
        return carry

    lax.fori_loop(0, u4.shape[0] // 32, top, 0)
    keep(grad_top)
    for index, ref in enumerate(kept):
        pltpu.make_async_copy(ref, kept_outs[index], kept_sems.at[index]).wait()
    for item in range(total):
        sent_line(item)
    for copy in started:
        copy.wait_send()


def gather_forward(blocks, latents, cotangent, points, near, lengths, vectors):
    width = latents.shape[1]
    rows = near.shape[1]
    half = blocks[2].shape[2] // 2
    widths = (3 * width, width, half, half) * 2
    total = len(GATHERED)
    anywhere = pl.BlockSpec(memory_space=pl.ANY)
    vmem = pl.BlockSpec(memory_space=pltpu.VMEM)
    plain = ((rows, width), BF)
    kept = [plain] * 17 + [
        ((2, 2 * rows, width), BF),
        ((2, 2 * rows, half), F32),
        ((2, 2 * rows, half), BF),
    ]
    dma = pltpu.SemaphoreType.DMA
    return pl.pallas_call(
        gather_kernel,
        out_shape=[jax.ShapeDtypeStruct((width, size), BF) for size in widths]
        + [
            jax.ShapeDtypeStruct((16, width), F32),
            jax.ShapeDtypeStruct((8, 128), F32),
            jax.ShapeDtypeStruct((1, rows), F32),
            jax.ShapeDtypeStruct((points.shape[0], rows), BF),
        ]
        + [jax.ShapeDtypeStruct(*one) for one in kept],
        in_specs=[anywhere] * (len(blocks) + 2) + [vmem] * 8,
        out_specs=[anywhere] * len(widths) + [vmem] * 4 + [anywhere] * len(kept),
        scratch_shapes=[pltpu.VMEM(*one) for one in kept]
        + [
            pltpu.VMEM((rows, width), BF),
            pltpu.VMEM((rows, width), BF),
            pltpu.VMEM((16, 128), BF),
            pltpu.VMEM((16, 128), F32),
            pltpu.VMEM((SLOTS, width, GATHER_WIDTH), BF),
            pltpu.VMEM((2 * rows, width), F32),
            pltpu.VMEM((2, rows, width), BF),
            pltpu.VMEM((2, rows, width), BF),
            pltpu.VMEM((8, 16, 128), BF),
            pltpu.VMEM((2, 2 * half), F32),
            pltpu.VMEM((9, 8, 128), F32),
            pltpu.VMEM((5, 8, 128), F32),
            dma((total,)),
            dma((6, total, 4)),
            dma((5, total, 4)),
            dma((total, 4)),
            dma((total, 4)),
            dma((2, 7)),
            dma((SLOTS,)),
            dma((len(kept),)),
            dma((2, 7)),
            dma((2, 3)),
            dma((2, 2, 2)),
            dma((2,)),
        ],
        compiler_params=pltpu.CompilerParams(
            collective_id=1, has_side_effects=True, vmem_limit_bytes=56 * 2**20
        ),
        cost_estimate=pl.CostEstimate(
            flops=2 * rows * width * sum(widths), bytes_accessed=2**27, transcendentals=2**21
        ),
    )(*blocks, latents, cotangent, points, near, lengths, *vectors)


ITEM_COUNT = 16
WINDOWS = 4
STAGES = 3


def reduce_kernel(*refs):
    total = ITEM_COUNT
    (
        proj_c,
        out_c,
        in_0,
        down_0,
        proj_s,
        out_s,
        in_1,
        down_1,
        u1_in,
        u2_in,
        u3_in,
        last_ref,
        top_in,
        xq_c,
        sn_c,
        q_c,
        k_c,
        v_c,
        o_c,
        xn_s,
        q_s,
        k_s,
        v_s,
        o_s,
        lowered,
        before,
        active,
        latents_in,
        src_in,
        gains,
        mask_in,
        picks_in,
    ) = refs[:32]
    (up_out, down_out, proj_out_c, proj_out_s, end_out_c, end_out_s) = refs[32:38]
    (last_out, first_out, point_out, small_out) = refs[38:42]
    (grads_h, kin_lf, kin_la, kin_rf, kin_ra) = refs[42:47]
    (
        lwin_f,
        lwin_a,
        raw,
        rwin,
        stage,
        merged_f,
        merged_a,
        passing,
        lined_f,
        lined_a,
        crossed_f,
        crossed_a,
        pair,
        slope,
        rows_sum,
        hbuf,
        slots,
        qb,
        kb,
        vb,
        dob,
        dqkv,
        part_out,
        part_in,
        grad,
        ub,
        point_in,
        point_sum,
        small_in,
        small_sum,
    ) = refs[47:77]
    (
        kin_l_sems,
        kin_r_sems,
        raw_sems,
        win_sems,
        xy_sems,
        line_send,
        line_recv,
        cross_sems,
        out_sems,
        own_sems,
        lat_sems,
        far_sems,
        lat_own,
        point_sems,
        deal_sems,
        point_own,
        small_sems,
        pair_sems,
        slot_sems,
        h_sem,
        save_sems,
        act_sems,
    ) = refs[77:]
    section_at = lax.axis_index("section")
    batch_at = lax.axis_index("batch")
    core = lax.rem(batch_at, 2)
    spot = batch_at // 2
    x_at = lax.rem(section_at, 2)
    y_at = section_at // 2
    beside = section_at + 1 - 2 * x_at
    above = lax.rem(section_at + 2, 4)
    across = lax.rem(beside + 2, 4)
    sibling = batch_at + 1 - 2 * core
    flat = (beside, above)
    bits = (x_at, y_at)
    rows, width = 256, 1024

    peers = [(beside, batch_at), (above, batch_at), (across, batch_at), (section_at, sibling)]
    peers += [(section_at, lax.rem(spot + step, 4) * 2 + core) for step in (1, 2, 3)]
    barrier = pltpu.get_barrier_semaphore()
    for peer in peers:
        pl.semaphore_signal(barrier, inc=1, device_id=peer, device_id_type=MESH)
    pl.semaphore_wait(barrier, len(peers))

    def remote(source, target, sems, where, peer):
        return pltpu.make_async_remote_copy(
            source,
            target,
            sems.at[(0, *where)],
            sems.at[(1, *where)],
            device_id=peer,
            device_id_type=MESH,
        )

    feed_left = (pair, lowered.at[1], pair, lowered.at[0])
    feed_right = (active.at[1], slope, active.at[0], slope)
    att_left = (o_s, xn_s, xn_s, xn_s, o_c, xq_c, sn_c, sn_c)
    att_right = tuple(
        ref
        for turn in range(2)
        for ref in (grads_h.at[turn], dqkv.at[0], dqkv.at[1], dqkv.at[2])
    )

    def columns(spot_of, parity):
        return pl.ds(pl.multiple_of((2 * spot_of + parity) * 128, 128), 128)

    def kin_lefts(feed, job):
        source, target = (feed_left, kin_lf) if feed else (att_left, kin_la)
        return [
            remote(
                source[job].at[:, columns(part, 1 - core)],
                target.at[job, part],
                kin_l_sems,
                (job if feed else 4 + job, part),
                (section_at, sibling),
            )
            for part in range(4)
        ]

    def kin_right(feed, job, chunk):
        if feed:
            here = pl.ds(chunk * 1024, 1024)
            source, target = feed_right[job].at[:, here], kin_rf.at[job, :, here]
        else:
            source, target = att_right[job], kin_ra.at[job]
        where = (2 * job + chunk if feed else 8 + job,)
        return remote(source, target, kin_r_sems, where, (section_at, sibling))

    def item_of(index):
        turn, inner = index // 8, index % 8
        if inner < 4:
            return True, 2 * turn + inner // 2, inner % 2
        return False, 4 * turn + inner - 4, 0

    def window_copies(index):
        feed, job, chunk = item_of(index)
        slot = index % WINDOWS
        size = 512 if feed else 256
        if feed:
            here = pl.ds(chunk * 1024, 1024)
            sources = (feed_right[job].at[:, here], kin_rf.at[job, :, here])
        else:
            sources = (att_right[job], kin_ra.at[job])
        return [
            pltpu.make_async_copy(
                sources[whose],
                rwin.at[slot, pl.ds(whose * size, size)],
                win_sems.at[slot, whose],
            )
            for whose in range(2)
        ]

    def raw_copies(index, part):
        feed, job, _ = item_of(index)
        size = 512 if feed else 256
        own_left = (feed_left if feed else att_left)[job]
        kin_left = (kin_lf if feed else kin_la).at[job]
        sources = (own_left.at[:, columns(part, core)], kin_left.at[part])
        return [
            pltpu.make_async_copy(
                source, raw.at[part, whose, pl.ds(0, size)], raw_sems.at[part, whose]
            )
            for whose, source in enumerate(sources)
        ]

    def raw_start(index):
        feed, job, chunk = item_of(index)
        if chunk == 0:
            for copy in kin_lefts(feed, job):
                copy.wait_recv()
            for part in range(4):
                for copy in raw_copies(index, part):
                    copy.start(priority=LOCAL)

    def load(index):
        feed, job, chunk = item_of(index)
        kin_right(feed, job, chunk).wait_recv()
        for copy in window_copies(index):
            copy.start(priority=LOCAL)
        if chunk == 0:
            size = 512 if feed else 256
            target = (lwin_f if feed else lwin_a).at[job]
            for part in range(4):
                for whose, copy in enumerate(raw_copies(index, part)):
                    copy.wait()
                    place = raw.at[part, whose, pl.ds(0, size)]
                    target[part, :, whose * size : whose * size + size] = place[...].T
        if index + 1 < total:
            raw_start(index + 1)

    def is_feed(item):
        return lax.rem(item, 8) < 4

    def feed_job(item):
        return 2 * (item // 8) + lax.rem(item, 8) // 2

    def att_job(item):
        return 4 * (item // 8) + lax.rem(item, 8) - 4

    def loaded(slot, feed):
        size = 512 if feed else 256
        for whose in range(2):
            source = kin_rf.at[0, :, pl.ds(0, 1024)] if feed else kin_ra.at[0]
            pltpu.make_async_copy(
                source, rwin.at[slot, pl.ds(whose * size, size)], win_sems.at[slot, whose]
            ).wait()

    def by_kind(item, action):
        pl.when(is_feed(item))(functools.partial(action, item, True))
        pl.when(jnp.logical_not(is_feed(item)))(functools.partial(action, item, False))

    def merged_of(item, feed):
        return merged_f.at[lax.rem(item, 4)] if feed else merged_a.at[att_job(item)]

    def passing_of(item, feed, slot):
        ref = passing.at[lax.rem(item, 8), slot]
        return ref if feed else ref.at[:, pl.ds(0, 512)]

    def lined_of(item, feed):
        return lined_f.at[lax.rem(item, 4)] if feed else lined_a.at[att_job(item)]

    def crossed_of(item, feed):
        return crossed_f.at[lax.rem(item, 4)] if feed else crossed_a.at[att_job(item)]

    def products(item, choice, store):
        slot = lax.rem(item, WINDOWS)

        def quarter(index, carry):
            here = pl.ds(pl.multiple_of(index * 256, 256), 256)
            bit = choice[0] + index * (choice[1] - choice[0])
            first = pl.multiple_of(index * 512 + bit * 256, 256)
            left = lwin_a[att_job(item)].reshape(512, 512)
            right = rwin[slot, 0:512, pl.ds(first, 256)]
            tile = jnp.dot(left, right, preferred_element_type=F32).reshape(4, 128, 256)
            store(pl.ds(0, 4), here, tile)
            return carry

        lax.fori_loop(0, 2, quarter, 0)

    def xy_copies(item):
        return [
            remote(
                stage.at[lax.rem(att_job(item), STAGES), :, :, pl.ds(side * 256, 256)],
                merged_a.at[att_job(item), :, :, pl.ds(side * 256, 256)],
                xy_sems,
                (att_job(item), side),
                (flat[side], batch_at),
            )
            for side in range(2)
        ]

    def xy_sent(item):
        for copy in xy_copies(item):
            copy.wait_send()

    def line_copy(item, feed, dest, place, rightward):
        step = 1 if rightward else -1
        slot = 4 if not rightward and place - 1 == dest else dest
        return pltpu.make_async_remote_copy(
            merged_of(item, feed).at[dest],
            passing_of(item, feed, slot),
            line_send.at[item, dest],
            line_recv.at[item, slot],
            device_id=(section_at, batch_at + 2 * step),
            device_id_type=MESH,
        )

    def line_wait(item, feed, slot):
        pltpu.make_async_remote_copy(
            merged_of(item, feed).at[0],
            passing_of(item, feed, slot),
            line_send.at[item, 0],
            line_recv.at[item, slot],
            device_id=(section_at, sibling),
            device_id_type=MESH,
        ).wait_recv()

    def line_sent(item, feed):
        for step in (1, 2, 3):
            dest = lax.rem(spot + step, 4)
            pltpu.make_async_remote_copy(
                merged_of(item, feed).at[dest],
                passing_of(item, feed, 0),
                line_send.at[item, dest],
                line_recv.at[item, 0],
                device_id=(section_at, sibling),
                device_id_type=MESH,
            ).wait_send()

    def outset(item, feed):
        @pl.when(spot == 0)
        def _():
            for dest in (3, 2, 1):
                line_copy(item, feed, dest, 0, True).start()

        @pl.when(spot == 3)
        def _():
            for dest in (0, 1, 2):
                line_copy(item, feed, dest, 3, False).start()

    def drained(item, feed):
        line_sent(item, feed)
        if feed:
            feed_out(item, up_out).wait()
            feed_own(item, up_out).wait()
        else:
            for side in range(2):
                att_out(item, side, end_out_s, 0).wait()
                att_own(item, side, end_out_s, 0).wait()

    def offer(item, feed):
        slot = lax.rem(item, WINDOWS)
        loaded(slot, feed)
        if feed:

            @pl.when(item >= 8)
            def _():
                drained(item - 8, True)

            target = merged_of(item, True)

            def tile(index, carry):
                here = pl.ds(pl.multiple_of(index * 256, 256), 256)
                left = lwin_f[feed_job(item)].reshape(512, 1024)
                right = rwin[slot, :, here]
                value = jnp.dot(left, right, preferred_element_type=F32)
                target[:, :, here] = value.reshape(4, 128, 256).astype(BF)
                return carry

            lax.fori_loop(0, 4, tile, 0)
            outset(item, True)
        else:

            @pl.when(lax.rem(item, 8) >= 4 + STAGES)
            def _():
                xy_sent(item - STAGES)

            @pl.when(jnp.logical_and(item >= 12, lax.rem(item, 8) < 4 + STAGES))
            def _():
                xy_sent(item - STAGES - 4)

            def store(blocks, here, tile):
                stage[lax.rem(att_job(item), STAGES), blocks, :, here] = tile.astype(BF)

            products(item, (1 - x_at, 1 - y_at), store)
            for copy in xy_copies(item):
                copy.start()

    def take(item):
        for copy in xy_copies(item):
            copy.wait_recv()
        target = merged_a.at[att_job(item)]

        def store(blocks, here, tile):
            target[blocks, :, here] = (tile + target[blocks, :, here].astype(F32)).astype(BF)

        products(item, bits, store)
        outset(item, False)

    def first(item):
        pl.when(jnp.logical_not(is_feed(item)))(functools.partial(take, item))

    def relay(item, feed, dest, place, rightward):
        line_wait(item, feed, dest)
        target = merged_of(item, feed)
        arrived = passing_of(item, feed, dest)
        target[dest] = (target[dest].astype(F32) + arrived[...].astype(F32)).astype(BF)
        line_copy(item, feed, dest, place, rightward).start()

    def second_of(item, feed):
        @pl.when(spot == 1)
        def _():
            for dest in (3, 2):
                relay(item, feed, dest, 1, True)

        @pl.when(spot == 2)
        def _():
            for dest in (0, 1):
                relay(item, feed, dest, 2, False)

    def third_of(item, feed):
        @pl.when(spot == 1)
        def _():
            relay(item, feed, 0, 1, False)

        @pl.when(spot == 2)
        def _():
            relay(item, feed, 3, 2, True)

    def second(item):
        by_kind(item, second_of)

    def third(item):
        by_kind(item, third_of)

    def feed_cross(item):
        return remote(
            lined_of(item, True),
            crossed_of(item, True),
            cross_sems,
            (item, 0),
            (beside, batch_at),
        )

    def cross_copy(item, side):
        here = pl.ds(side * 256, 256)
        return remote(
            lined_of(item, False).at[:, here],
            crossed_of(item, False).at[:, here],
            cross_sems,
            (item, side),
            (flat[1 - side], batch_at),
        )

    def layer_of(item):
        return 1 - item // 8

    def feed_place(item, target):
        base = y_at * 2048 + lax.rem(item, 2) * 1024
        return target.at[layer_of(item), :, pl.ds(pl.multiple_of(base, 1024), 1024)]

    def feed_out(item, target):
        return remote(
            lined_of(item, True),
            feed_place(item, target),
            out_sems,
            (item, 0),
            (above, batch_at),
        )

    def feed_own(item, target):
        return pltpu.make_async_copy(
            lined_of(item, True), feed_place(item, target), own_sems.at[item, 0]
        )

    def feed_write(item):
        @pl.when(lax.rem(item, 8) < 2)
        def _():
            feed_out(item, down_out).start()
            feed_own(item, down_out).start(priority=LOCAL)

        @pl.when(lax.rem(item, 8) >= 2)
        def _():
            feed_out(item, up_out).start()
            feed_own(item, up_out).start(priority=LOCAL)

    def att_place(item, side, target, inner):
        base = side * 512 + bits[side] * 256
        return target.at[inner, :, pl.ds(pl.multiple_of(base, 256), 256)]

    def att_out(item, side, target, inner):
        return remote(
            lined_of(item, False).at[:, pl.ds(side * 256, 256)],
            att_place(item, side, target, inner),
            out_sems,
            (item, side),
            (flat[side], batch_at),
        )

    def att_own(item, side, target, inner):
        return pltpu.make_async_copy(
            lined_of(item, False).at[:, pl.ds(side * 256, 256)],
            att_place(item, side, target, inner),
            own_sems.at[item, side],
        )

    def att_write(item):
        inner = lax.rem(item, 8) - 5
        for turn, proj, end in ((0, proj_out_s, end_out_s), (1, proj_out_c, end_out_c)):

            @pl.when(jnp.logical_and(item // 8 == turn, inner >= 0))
            def _():
                for side in range(2):
                    att_out(item, side, proj, inner).start()
                    att_own(item, side, proj, inner).start(priority=LOCAL)

            @pl.when(jnp.logical_and(item // 8 == turn, inner < 0))
            def _():
                for side in range(2):
                    att_out(item, side, end, 0).start()
                    att_own(item, side, end, 0).start(priority=LOCAL)

    def close_of(item, feed):
        for place in range(4):

            @pl.when(spot == place)
            def _():
                value = merged_of(item, feed)[place].astype(F32)
                if place > 0:
                    line_wait(item, feed, place)
                    value += passing_of(item, feed, place)[...].astype(F32)
                if place < 3:
                    line_wait(item, feed, 4)
                    value += passing_of(item, feed, 4)[...].astype(F32)
                lined_of(item, feed)[...] = value.astype(BF)

        if feed:
            feed_cross(item).start()
        else:
            for side in range(2):
                cross_copy(item, side).start()

    def close(item):
        by_kind(item, close_of)

    def finish_of(item, feed):
        if feed:
            feed_cross(item).wait()
        else:
            for side in range(2):
                cross_copy(item, side).wait()
        target = lined_of(item, feed)
        target[...] = (
            target[...].astype(F32) + crossed_of(item, feed)[...].astype(F32)
        ).astype(BF)
        if feed:
            feed_write(item)
        else:
            att_write(item)

    def finish(item):
        by_kind(item, finish_of)

    def small_copy(phase):
        if phase == 0:
            peer = (section_at, sibling)
        elif phase < 3:
            peer = (flat[phase - 1], batch_at)
        else:
            peer = (section_at, lax.rem(spot + phase - 2, 4) * 2 + core)
        return remote(
            small_sum.at[min(phase, 3)], small_in.at[phase], small_sems, (phase,), peer
        )

    quarter_rows = pair.shape[0] // 4

    def point_copy(which):
        peer = (beside, above, across)[which]
        return remote(
            pair.at[pl.ds(pl.multiple_of(peer * quarter_rows, 128), quarter_rows)],
            point_in.at[which],
            point_sems,
            (which,),
            (peer, batch_at),
        )

    def point_place():
        return point_out.at[pl.ds(pl.multiple_of(section_at * quarter_rows, 128), quarter_rows)]

    def point_deal(which):
        peer = (beside, above, across)[which]
        return remote(point_sum, point_place(), deal_sems, (which,), (peer, batch_at))

    def point_local():
        return pltpu.make_async_copy(point_sum, point_place(), point_own.at[0])

    pairs = ((last_ref, last_out), (grad, first_out))

    def lat_copy(which, way):
        source, target = pairs[which]
        return remote(
            source,
            target.at[pl.ds(pl.multiple_of(section_at * rows, rows), rows)],
            lat_sems,
            (which, way),
            (flat[way], batch_at),
        )

    def lat_far(which, way):
        target = pairs[which][1]
        low = flat[way] * rows + way * (rows // 2)
        part = target.at[pl.ds(pl.multiple_of(low, rows // 2), rows // 2)]
        return remote(part, part, far_sems, (which, way), (flat[1 - way], batch_at))

    def lat_local(which):
        source, target = pairs[which]
        return pltpu.make_async_copy(
            source,
            target.at[pl.ds(pl.multiple_of(section_at * rows, rows), rows)],
            lat_own.at[which],
        )

    def lat_start(which):
        lat_local(which).start(priority=LOCAL)
        for way in range(2):
            lat_copy(which, way).start()

    def lat_onward(which):
        for way in range(2):
            lat_copy(which, way).wait_recv()
            lat_far(which, way).start()

    loads = []
    for turn, (proj, out, up, down) in enumerate(
        ((proj_s, out_s, in_1, down_1), (proj_c, out_c, in_0, down_0))
    ):
        for chunk in range(2):
            loads += [down.at[:, pl.ds(chunk * 1024, 1024)], up.at[:, pl.ds(chunk * 1024, 1024)]]
        loads.append(out)
        loads += [proj.at[:, pl.ds(which * 1024, 1024)] for which in range(3)]

    def slot_copy(index):
        return pltpu.make_async_copy(loads[index], slots.at[index % 2], slot_sems.at[index % 2])

    def opened(index):
        slot_copy(index).wait()
        return index % 2

    def closed(index):
        if index + 2 < len(loads):
            slot_copy(index + 2).start(priority=LOCAL)

    def h_copy(index):
        layer, chunk = 1 - index // 2, index % 2
        return pltpu.make_async_copy(
            before.at[layer, :, pl.ds(chunk * 1024, 1024)], hbuf, h_sem.at[0]
        )

    def pair_over(turn):
        return remote(
            pair.at[pl.ds(0, rows)],
            pair.at[pl.ds(rows, rows)],
            pair_sems,
            (turn, 0),
            (above, batch_at),
        )

    def part_over(turn):
        return remote(
            part_out.at[turn], part_in.at[turn], pair_sems, (turn, 1), (above, batch_at)
        )

    def grad_saved(turn):
        return pltpu.make_async_copy(grad, grads_h.at[turn], save_sems.at[0])

    def act_copies(turn):
        chosen = ((q_s, k_s, v_s), (q_c, k_c, v_c))[turn]
        return [
            pltpu.make_async_copy(source, target, act_sems.at[index])
            for index, (source, target) in enumerate(zip(chosen, (qb, kb, vb)))
        ]

    def row_copy(index):
        if index == 3:
            source = latents_in.at[pl.ds(pl.multiple_of(section_at * rows, rows), rows)]
        else:
            source = (u3_in, u2_in, u1_in)[index]
        return pltpu.make_async_copy(source, ub, act_sems.at[3])

    def small_row(index, value):
        small_sum[0, index : index + 1, :] = value

    def open_pair(turn):
        pair[0:rows, :] = grad[...]
        pair_over(turn).start()

    def pair_ready(turn):
        pair_over(turn).wait()
        for copy in kin_lefts(True, 2 * turn):
            copy.start()

    def feed_chunk(turn, chunk):
        layer = 1 - turn
        base = 8 * turn + 2 * chunk
        h_copy(2 * turn + chunk).wait()
        if turn == 1:
            kin_right(True, 1, chunk).wait_send()
        slot = opened(base)

        def up_tile(here, index):
            there = pl.ds(pl.multiple_of(chunk * 1024 + index * 256, 256), 256)
            value = mm(pair[...], slots[slot, :, here]) * hbuf[:, here]
            short = value.astype(BF)
            slope[:, there] = short
            column = jnp.sum(short.astype(F32), axis=0, keepdims=True)
            for half in range(2):
                index_at = 7 + 4 * layer + 2 * half + chunk
                small_sum[0, index_at : index_at + 1, here] = jnp.where(
                    y_at == half, column, jnp.zeros_like(column)
                )

        tiles(4, up_tile)
        closed(base)
        if 2 * turn + chunk + 1 < 4:
            h_copy(2 * turn + chunk + 1).start(priority=LOCAL)
        kin_right(True, 2 * turn + 1, chunk).start()
        slot = opened(base + 1)

        def down_tile(there, _):
            value = mm_cols(slope[:, chunk * 1024 : chunk * 1024 + 1024], slots[slot, there, :])
            if chunk == 0:
                rows_sum[:, there] = value
            else:
                value = rows_sum[:, there] + value
                rows_sum[:, there] = value
                part_out[turn, :, there] = value[rows:].astype(BF)

        tiles(4, down_tile)
        closed(base + 1)
        if chunk == 1:
            if turn == 0:
                for copy in kin_lefts(True, 0):
                    copy.wait_send()
            part_over(turn).start()

    def row_steps(body, count):
        zero = jnp.zeros((1, width), F32)

        def step(index, carry):
            here = pl.ds(pl.multiple_of(index * 32, 32), 32)
            return tuple(a + b for a, b in zip(carry, body(here)))

        return lax.fori_loop(0, rows // 32, step, (zero,) * count)

    def lean(back, unit, inverse, gain):
        scaled = back * gain
        inner = (
            scaled
            - jnp.mean(scaled, axis=-1, keepdims=True)
            - unit * jnp.mean(scaled * unit, axis=-1, keepdims=True)
        )
        return inverse * inner, jnp.sum(back * unit, axis=0, keepdims=True)

    def feed_end(turn):
        layer = 1 - turn
        gain = gains[3 + layer : 4 + layer, :]
        part_over(turn).wait_recv()
        row_copy(2 * turn).wait()

        def body(here):
            unit, inverse = unit_rows(ub[here, :].astype(F32))
            back = rows_sum[here, :] + part_in[turn, here, :].astype(F32)
            dx, gain_part = lean(back, unit, inverse, gain)
            old = grad[here, :].astype(F32)
            grad[here, :] = (old + dx).astype(BF)
            return gain_part, jnp.sum(old, axis=0, keepdims=True)

        gain_grad, out_grad = row_steps(body, 2)
        row_copy(2 * turn + 1).start(priority=LOCAL)
        small_row(3 + layer, gain_grad)
        small_row(5 + layer, out_grad)
        grad_saved(turn).start(priority=LOCAL)
        slot = opened(8 * turn + 4)

        def tile(there, _):
            dob[:, there] = mm_cols(grad[...], slots[slot, there, :]).astype(BF)

        tiles(2, tile, 512)
        closed(8 * turn + 4)
        grad_saved(turn).wait()
        kin_right(False, 4 * turn, 0).start()

    def attend_heads(turn):
        scale = 1.0 / math.sqrt(HD)
        for copy in act_copies(turn):
            copy.wait()
        if turn == 1:
            for which in range(3):
                kin_right(False, 1 + which, 0).wait_send()

        def head(index, carry):
            here = pl.ds(pl.multiple_of(index * HD, HD), HD)
            q, k, v, do = qb[:, here], kb[:, here], vb[:, here], dob[:, here]
            scores = mm_cols(q, k) * scale
            if turn == 1:
                scores = jnp.where(mask_in[...] > 0.0, scores, MASKED)
            grown = jnp.exp(scores - jnp.max(scores, axis=-1, keepdims=True))
            soft = grown / jnp.sum(grown, axis=-1, keepdims=True)
            back = mm_cols(do, v)
            short = soft * (back - jnp.sum(soft * back, axis=-1, keepdims=True))
            dqkv[0, :, here] = (mm(short.astype(BF), k) * scale).astype(BF)
            dqkv[1, :, here] = (mm(short.T.astype(BF), q) * scale).astype(BF)
            dqkv[2, :, here] = mm(soft.T.astype(BF), do).astype(BF)
            return carry

        lax.fori_loop(0, width // HD, head, 0)
        if turn == 0:
            for copy in act_copies(1):
                copy.start(priority=LOCAL)
        for which in range(3):
            kin_right(False, 4 * turn + 1 + which, 0).start()

    def attend_end(turn):
        base = 8 * turn + 5
        for which in range(3):
            slot = opened(base + which)

            def tile(there, _):
                value = mm_cols(dqkv[which], slots[slot, there, :])
                if which == 0:
                    rows_sum[0:rows, there] = value
                elif which == 1:
                    rows_sum[rows : 2 * rows, there] = value
                else:
                    rows_sum[rows : 2 * rows, there] += value

            tiles(2, tile, 512)
            closed(base + which)
        row_copy(2 * turn + 1).wait()
        gain_q = gains[2:3, :] if turn == 0 else gains[0:1, :]
        gain_kv = gains[2:3, :] if turn == 0 else gains[1:2, :]

        def body(here):
            unit, inverse = unit_rows(ub[here, :].astype(F32))
            dx, gain_part = lean(rows_sum[here, :], unit, inverse, gain_q)
            if turn == 1:
                unit, inverse = unit_rows(src_in[here, :].astype(F32))
            there = pl.ds(pl.multiple_of(rows + here.start, 32), 32)
            ds, kv_part = lean(rows_sum[there, :], unit, inverse, gain_kv)
            fresh = grad[here, :].astype(F32) + dx
            if turn == 0:
                fresh += ds
            else:
                high = ds.astype(BF)
                part_out[0, here, :] = high
                part_out[1, here, :] = (ds - high.astype(F32)).astype(BF)
            grad[here, :] = fresh.astype(BF)
            return gain_part, kv_part

        if turn == 1:
            for which in range(2):
                part_over(which).wait_send()
            for copy in kin_lefts(True, 2):
                copy.wait_send()
        gain_grad, kv_grad = row_steps(body, 2)
        if turn == 0:
            row_copy(2).start(priority=LOCAL)
            small_row(2, gain_grad + kv_grad)
            open_pair(1)
        else:
            small_row(0, gain_grad)
            small_row(1, kv_grad)
            small_row(15, jnp.zeros_like(gain_grad))

            def tile(there, _):
                pair[:, there] = (
                    mm(picks_in[...], part_out[0, :, there])
                    + mm(picks_in[...], part_out[1, :, there])
                ).astype(BF)

            tiles(4, tile)
            small_copy(0).start()
            for which in range(3):
                point_copy(which).start()
            lat_start(1)

    def point_total():
        for which in range(3):
            point_copy(which).wait_recv()
        gathered = pair[
            pl.ds(pl.multiple_of(section_at * quarter_rows, 128), quarter_rows)
        ].astype(F32)
        for which in range(3):
            gathered += point_in[which].astype(F32)
        point_sum[...] = gathered.astype(BF)
        point_local().start(priority=LOCAL)
        for which in range(3):
            point_deal(which).start()

    def small_step(phase):
        small_copy(phase).wait_recv()
        small_sum[phase + 1] = small_sum[phase] + small_in[phase]
        if phase < 2:
            small_copy(phase + 1).start()
        else:
            for step in range(3):
                small_copy(3 + step).start()

    def small_end():
        for step in range(3):
            small_copy(3 + step).wait_recv()
        small_out[...] = (small_sum[3] + small_in[4]) + (small_in[3] + small_in[5])

    def rows_end():
        lat_onward(1)
        point_total()

    begin = pltpu.make_async_copy(top_in, grad, act_sems.at[4])
    begin.start()
    for index in range(2):
        slot_copy(index).start(priority=LOCAL)
    h_copy(0).start(priority=LOCAL)
    row_copy(0).start(priority=LOCAL)
    for copy in act_copies(0):
        copy.start(priority=LOCAL)
    begin.wait()
    open_pair(0)
    for part in range(2):
        kin_right(True, 0, part).start()
    pair_ready(0)
    for copy in kin_lefts(True, 1):
        copy.start()
    for job in range(4):
        for copy in kin_lefts(False, job):
            copy.start()
    for part in range(2):
        kin_right(True, 2, part).start()
    for copy in kin_lefts(True, 3):
        copy.start()
    for job in range(4, 8):
        for copy in kin_lefts(False, job):
            copy.start()
    raw_start(0)
    load(0)
    chain = {
        0: [functools.partial(feed_chunk, 0, 0)],
        1: [functools.partial(feed_chunk, 0, 1)],
        2: [functools.partial(lat_start, 0)],
        3: [functools.partial(feed_end, 0)],
        4: [functools.partial(attend_heads, 0)],
        5: [functools.partial(attend_end, 0), functools.partial(lat_onward, 0)],
        6: [functools.partial(pair_ready, 1)],
        7: [functools.partial(feed_chunk, 1, 0)],
        8: [functools.partial(feed_chunk, 1, 1)],
        10: [functools.partial(feed_end, 1)],
        11: [functools.partial(attend_heads, 1)],
        12: [functools.partial(attend_end, 1)],
        14: [functools.partial(small_step, 0), rows_end],
        16: [functools.partial(small_step, 1)],
        18: [functools.partial(small_step, 2)],
        20: [small_end],
    }

    def moment_body(moment, carry):
        @pl.when(moment < total)
        def _():
            by_kind(moment, offer)

        for lag, action in ((2, first), (3, second), (4, third), (5, close), (6, finish)):
            pl.when(jnp.logical_and(moment >= lag, moment < total + lag))(
                functools.partial(action, moment - lag)
            )
        for when, actions in chain.items():

            @pl.when(moment == when)
            def _():
                for action in actions:
                    action()

        for item in range(1, total):
            pl.when(moment == item - 1)(functools.partial(load, item))
        return carry

    lax.fori_loop(0, total + 6, moment_body, 0)

    for index in range(4):
        if index % 2 == 1:
            for copy in kin_lefts(True, index):
                copy.wait_send()
        if index != 1:
            for chunk in range(2):
                kin_right(True, index, chunk).wait_send()
    for index in range(8):
        for copy in kin_lefts(False, index):
            copy.wait_send()
        if index not in (1, 2, 3):
            kin_right(False, index, 0).wait_send()
    for phase in range(6):
        small_copy(phase).wait_send()
    for which in range(2):
        lat_local(which).wait()
        for way in range(2):
            lat_copy(which, way).wait_send()
            lat_far(which, way).wait()
    point_local().wait()
    for which in range(3):
        point_copy(which).wait_send()
        point_deal(which).wait()

    def drain(item, carry):
        @pl.when(item >= 4)
        def _():
            by_kind(item, drained)

        return carry

    for item in range(total - STAGES, total):
        xy_sent(item)
    lax.fori_loop(0, total, drain, 0)


def reduce_all(full, kept, latents, gains, mask, picks):
    total = ITEM_COUNT
    rows, width = kept[0].shape
    points = picks.shape[0]
    anywhere = pl.BlockSpec(memory_space=pl.ANY)
    vmem = pl.BlockSpec(memory_space=pltpu.VMEM)
    u1, u2, u3, u4, top = kept[:5]
    operands = [*full, u1, u2, u3, u4, top, *kept[5:16], *kept[17:], latents, kept[16]]
    operands += [gains, mask, picks]
    spaces = [anywhere] * (len(operands) - 4) + [vmem] * 4
    dma = pltpu.SemaphoreType.DMA
    flops = 2 * width * width * 24 * rows * 2
    return pl.pallas_call(
        reduce_kernel,
        out_shape=[
            jax.ShapeDtypeStruct((2, 128, 4 * width), BF),
            jax.ShapeDtypeStruct((2, 128, 4 * width), BF),
            jax.ShapeDtypeStruct((3, 128, width), BF),
            jax.ShapeDtypeStruct((3, 128, width), BF),
            jax.ShapeDtypeStruct((1, 128, width), BF),
            jax.ShapeDtypeStruct((1, 128, width), BF),
            jax.ShapeDtypeStruct((4 * rows, width), BF),
            jax.ShapeDtypeStruct((4 * rows, width), BF),
            jax.ShapeDtypeStruct((points, width), BF),
            jax.ShapeDtypeStruct((16, width), F32),
            jax.ShapeDtypeStruct((2, rows, width), BF),
            jax.ShapeDtypeStruct((4, 4, 2 * rows, 128), BF),
            jax.ShapeDtypeStruct((8, 4, rows, 128), BF),
            jax.ShapeDtypeStruct((4, 2 * rows, 2 * width), BF),
            jax.ShapeDtypeStruct((8, rows, width), BF),
        ],
        in_specs=spaces,
        out_specs=[anywhere] * 9 + [vmem] + [anywhere] * 5,
        scratch_shapes=[
            pltpu.VMEM((4, 4, 128, 1024), BF),
            pltpu.VMEM((8, 4, 128, 512), BF),
            pltpu.VMEM((4, 2, 512, 128), BF),
            pltpu.VMEM((WINDOWS, 1024, 1024), BF),
            pltpu.VMEM((STAGES, 4, 128, 512), BF),
            pltpu.VMEM((4, 4, 128, 1024), BF),
            pltpu.VMEM((8, 4, 128, 512), BF),
            pltpu.VMEM((8, 5, 128, 1024), BF),
            pltpu.VMEM((4, 128, 1024), BF),
            pltpu.VMEM((8, 128, 512), BF),
            pltpu.VMEM((4, 128, 1024), BF),
            pltpu.VMEM((8, 128, 512), BF),
            pltpu.VMEM((512, 1024), BF),
            pltpu.VMEM((512, 2048), BF),
            pltpu.VMEM((512, 1024), F32),
            pltpu.VMEM((512, 1024), F32),
            pltpu.VMEM((2, 1024, 1024), BF),
            pltpu.VMEM((256, 1024), BF),
            pltpu.VMEM((256, 1024), BF),
            pltpu.VMEM((256, 1024), BF),
            pltpu.VMEM((256, 1024), BF),
            pltpu.VMEM((3, 256, 1024), BF),
            pltpu.VMEM((2, 256, 1024), BF),
            pltpu.VMEM((2, 256, 1024), BF),
            pltpu.VMEM((256, 1024), BF),
            pltpu.VMEM((256, 1024), BF),
            pltpu.VMEM((3, points // 4, width), BF),
            pltpu.VMEM((points // 4, width), BF),
            pltpu.VMEM((6, 16, width), F32),
            pltpu.VMEM((4, 16, width), F32),
            dma((2, 12, 4)),
            dma((2, 16)),
            dma((4, 2)),
            dma((WINDOWS, 2)),
            dma((2, 8, 2)),
            dma((total, 4)),
            dma((total, 5)),
            dma((2, total, 2)),
            dma((2, total, 2)),
            dma((total, 2)),
            dma((2, 2, 2)),
            dma((2, 2, 2)),
            dma((2,)),
            dma((2, 3)),
            dma((2, 3)),
            dma((1,)),
            dma((2, 6)),
            dma((2, 2, 2)),
            dma((2,)),
            dma((1,)),
            dma((1,)),
            dma((5,)),
        ],
        compiler_params=pltpu.CompilerParams(
            collective_id=2, has_side_effects=True, vmem_limit_bytes=62 * 2**20
        ),
        cost_estimate=pl.CostEstimate(
            flops=flops, bytes_accessed=2**27, transcendentals=2**21
        ),
    )(*operands)[:10]


def plain_layers(full, spread, mine, source, valid, cot_own, picks, groups_all):
    proj_c, out_c, in_0, down_0, proj_s, out_s, in_1, down_1 = full
    width, hidden = in_0.shape

    def vector(first, count):
        return spread[:, first : first + count].reshape(-1)

    gains_cross = (vector(0, 1), vector(1, 1))
    gain_self = vector(2, 1)
    gains_mlp = (vector(3, 1), vector(4, 1))
    biases_out = (vector(5, 1), vector(6, 1))
    per_bias = hidden // width
    biases_in = (vector(7, per_bias), vector(7 + per_bias, per_bias))
    cot = cot_own.astype(F32)
    u1, kept_c = attend(mine, source, valid, gains_cross[0], gains_cross[1], proj_c, out_c)
    u2, kept_0 = feed(u1.astype(F32), gains_mlp[0], in_0, biases_in[0], down_0, biases_out[0])
    u2 = u2.astype(F32)
    u3, kept_s = attend(u2, u2, None, gain_self, gain_self, proj_s, out_s)
    u4, kept_1 = feed(u3.astype(F32), gains_mlp[1], in_1, biases_in[1], down_1, biases_out[1])
    final = u4.astype(F32)
    group_norm = jnp.sqrt(jnp.mean(final * final) + EPSILON)
    norm_mean = lax.psum(group_norm, ALL) / groups_all
    g4 = (cot + (norm_mean / group_norm) * final).astype(BF)

    dx, gain_1_grad, bias_1_grad, ob_1_grad, pairs_1 = feed_back(
        g4, kept_1, gains_mlp[1], in_1, down_1
    )
    g3 = (g4.astype(F32) + dx).astype(BF)
    dx, ds, gq, gkv, pairs_s = attend_back(g3, kept_s, gain_self, gain_self, proj_s, out_s)
    gain_s_grad = gq + gkv
    g2 = (g3.astype(F32) + dx + ds).astype(BF)
    dx, gain_0_grad, bias_0_grad, ob_0_grad, pairs_0 = feed_back(
        g2, kept_0, gains_mlp[0], in_0, down_0
    )
    g1 = (g2.astype(F32) + dx).astype(BF)
    dx, ds, cq_grad, ckv_grad, pairs_c = attend_back(
        g1, kept_c, gains_cross[0], gains_cross[1], proj_c, out_c
    )
    g0 = (g1.astype(F32) + dx).astype(BF)
    high = ds.astype(BF)
    low = (ds - high.astype(F32)).astype(BF)
    point_part = (mm_rows(picks, high) + mm_rows(picks, low)).astype(BF)
    small = jnp.concatenate(
        [
            cq_grad,
            ckv_grad,
            gain_s_grad,
            gain_0_grad,
            gain_1_grad,
            ob_0_grad,
            ob_1_grad,
            bias_0_grad,
            bias_1_grad,
            jnp.zeros_like(cq_grad),
        ]
    ).reshape(-1, width)
    pairs = pairs_1 + pairs_s + pairs_0 + pairs_c
    lefts, rights = [pair[0] for pair in pairs], [pair[1] for pair in pairs]
    def settled_grad(left, right):
        part = lax.psum_scatter(
            mm_rows(left, right).astype(BF), ALL, scatter_dimension=0, tiled=True
        )
        return lax.all_gather(part, "section", axis=0, tiled=True).astype(F32)

    done = [settled_grad(left, right) for left, right in pairs]
    mlp_in_grad = jnp.stack([done[6], done[0]])
    mlp_down_grad = jnp.stack([done[7], done[1]])
    proj_s_grad = jnp.concatenate(done[2:5], axis=1)
    proj_c_grad = jnp.concatenate(done[8:11], axis=1)
    out_s_grad, out_c_grad = done[5], done[11]
    points_sum = lax.psum(point_part, "section")
    latents_out = lax.all_gather(u4, "section", axis=0, tiled=True)
    g0_all = lax.all_gather(g0, "section", axis=0, tiled=True)
    small = lax.psum(small, ALL)
    return (
        norm_mean,
        latents_out,
        g0_all,
        points_sum,
        small,
        mlp_in_grad,
        mlp_down_grad,
        proj_c_grad,
        proj_s_grad,
        out_c_grad,
        out_s_grad,
    )


def per_device(
    latents,
    points,
    neighbours,
    lengths,
    cross_proj,
    cross_out,
    cross_gains,
    self_proj,
    self_out,
    self_gain,
    mlp_gain,
    mlp_in,
    mlp_in_bias,
    mlp_down,
    mlp_out_bias,
    cotangent,
):
    sections = lax.axis_size("section")
    section_at = lax.axis_index("section")
    width = latents.shape[1]
    hidden = mlp_in.shape[2]
    groups_dev = neighbours.shape[0]
    rows = latents.shape[0] // sections
    shard = cross_out.shape[0]
    piece = shard // sections
    groups_all = groups_dev * lax.axis_size("batch")

    def gathered(block):
        own = lax.dynamic_slice_in_dim(block, section_at * piece, piece, 0)
        return lax.all_gather(own, ALL, axis=0, tiled=True)

    projs = (cross_proj.reshape(shard, 3 * width), self_proj.reshape(shard, 3 * width))
    if lax.axis_size("batch") == 8:
        made = gather_forward(
            [projs[0], cross_out, mlp_in, mlp_down, projs[1], self_out],
            latents,
            cotangent,
            points,
            neighbours,
            lengths[:, None],
            [cross_gains, self_gain[None, :], mlp_gain, mlp_out_bias, mlp_in_bias],
        )
        full, gain_rows, norm_tile, mask, picks = made[:8], *made[8:12]
        norm_mean = norm_tile[0, 0]
        (
            mlp_in_grad,
            mlp_down_grad,
            proj_c_grad,
            proj_s_grad,
            out_c_grad,
            out_s_grad,
            latents_out,
            g0_all,
            points_sum,
            small,
        ) = reduce_all(full, made[12:], latents, gain_rows, mask, picks)
        mlp_in_grad = mlp_in_grad.astype(F32)
        mlp_down_grad = mlp_down_grad.astype(F32)
        proj_c_grad = jnp.swapaxes(proj_c_grad, 0, 1).astype(F32)
        proj_s_grad = jnp.swapaxes(proj_s_grad, 0, 1).astype(F32)
        out_c_grad, out_s_grad = out_c_grad[0].astype(F32), out_s_grad[0].astype(F32)
    else:
        vectors = jnp.concatenate(
            [
                cross_gains.reshape(-1),
                self_gain,
                mlp_gain.reshape(-1),
                mlp_out_bias.reshape(-1),
                mlp_in_bias.reshape(-1),
                jnp.zeros_like(self_gain),
            ]
        ).reshape(-1, shard)
        cot_own = lax.dynamic_slice_in_dim(cotangent, section_at * rows, rows, 0)
        mine = lax.dynamic_slice_in_dim(latents, section_at * rows, rows, 0).astype(F32)
        listed = lax.dynamic_index_in_dim(neighbours, section_at, 0, keepdims=False)
        length = lax.dynamic_index_in_dim(lengths, section_at, 0, keepdims=False)
        valid = jnp.arange(listed.shape[0], dtype=jnp.int32) < length
        picks = listed[:, None] == jnp.arange(points.shape[0], dtype=jnp.int32)[None, :]
        picks = picks.astype(BF)
        source = mm(picks, points)
        blocks = [projs[0], cross_out, mlp_in[0], mlp_down[0]]
        blocks += [projs[1], self_out, mlp_in[1], mlp_down[1]]
        full = [gathered(block) for block in blocks]
        spread = lax.all_gather(vectors, "batch", axis=0, tiled=False)
        (
            norm_mean,
            latents_out,
            g0_all,
            points_sum,
            small,
            mlp_in_grad,
            mlp_down_grad,
            proj_c_grad,
            proj_s_grad,
            out_c_grad,
            out_s_grad,
        ) = plain_layers(full, spread.astype(F32), mine, source, valid, cot_own, picks, groups_all)
    points_grad = points_sum.astype(F32)
    latents_grad = g0_all.astype(F32)
    per_bias = hidden // width
    batch_at = lax.axis_index("batch")

    def own(first, count):
        flat = small[first : first + count].reshape(-1)
        size = flat.shape[0] // lax.axis_size("batch")
        return lax.dynamic_slice_in_dim(flat, batch_at * size, size, 0)

    return (
        latents_out,
        latents_grad,
        points_grad,
        proj_c_grad.reshape(shard, 3, width),
        out_c_grad,
        jnp.stack([own(0, 1), own(1, 1)]),
        proj_s_grad.reshape(shard, 3, width),
        out_s_grad,
        own(2, 1),
        jnp.stack([own(3, 1), own(4, 1)]),
        mlp_in_grad,
        jnp.stack([own(7, per_bias), own(7 + per_bias, per_bias)]),
        mlp_down_grad,
        jnp.stack([own(5, 1), own(6, 1)]),
        norm_mean,
    )


def solution(mesh):
    rows = P("batch", None)
    cols = P(None, "batch")
    block = P("batch", None, None)
    pair = P(None, "batch", None)
    return jax.shard_map(
        per_device,
        mesh=mesh,
        in_specs=(
            rows,
            rows,
            rows,
            P("batch"),
            block,
            rows,
            cols,
            block,
            rows,
            P("batch"),
            cols,
            pair,
            cols,
            pair,
            cols,
            rows,
        ),
        out_specs=(
            rows,
            rows,
            rows,
            block,
            rows,
            cols,
            block,
            rows,
            P("batch"),
            cols,
            pair,
            cols,
            pair,
            cols,
            P(),
        ),
        check_vma=False,
    )
```

```python
import functools
import math

import jax
import jax.numpy as jnp
from jax import lax
from jax.experimental import pallas as pl
from jax.experimental.pallas import tpu as pltpu
from jax.sharding import PartitionSpec as P

HD = 128
EPSILON = 1e-05
MASKED = -1e30
BF = jnp.bfloat16
F32 = jnp.float32
ALL = ("batch", "section")
MESH = pl.DeviceIdType.MESH
GATHER_WIDTH = 1024
AHEAD = 4
LOCAL = 1
SLOTS = 3
GATHERED = tuple(
    (4 * layer + index, start)
    for layer in range(2)
    for index, start in (
        [(0, 0), (0, 1024), (0, 2048), (1, 0)]
        + [(2 + which, chunk) for chunk in range(0, 2048, 1024) for which in range(2)]
    )
)


def mm(a, b):
    return jnp.dot(a, b, preferred_element_type=F32)


def mm_rows(a, b):
    return lax.dot_general(a, b, (((0,), (0,)), ((), ())), preferred_element_type=F32)


def mm_cols(a, b):
    return lax.dot_general(a, b, (((1,), (1,)), ((), ())), preferred_element_type=F32)


def unit_rows(values):
    centred = values - jnp.mean(values, axis=-1, keepdims=True)
    inverse = lax.rsqrt(jnp.mean(centred * centred, axis=-1, keepdims=True) + EPSILON)
    return centred * inverse, inverse


def norm_back(gradient, unit, inverse, gain):
    scaled = gradient * gain
    inner = (
        scaled
        - jnp.mean(scaled, axis=-1, keepdims=True)
        - unit * jnp.mean(scaled * unit, axis=-1, keepdims=True)
    )
    return inverse * inner, jnp.sum(gradient * unit, axis=0)


def heads_of(rows):
    return rows.reshape(rows.shape[0], -1, HD)


def softmax(q, k, valid):
    scores = jnp.einsum(
        "lhc,nhc->hln", heads_of(q), heads_of(k), preferred_element_type=F32
    ) * (1.0 / math.sqrt(HD))
    if valid is not None:
        scores = jnp.where(valid[None, None, :], scores, MASKED)
    grown = jnp.exp(scores - jnp.max(scores, axis=-1, keepdims=True))
    return grown / jnp.sum(grown, axis=-1, keepdims=True)


def attend(inputs, source, valid, gain_q, gain_kv, proj, out):
    unit_x, inv_x = unit_rows(inputs)
    queries_in = (unit_x * gain_q).astype(BF)
    unit_s, inv_s = unit_rows(source)
    keys_in = (unit_s * gain_kv).astype(BF)
    width = inputs.shape[1]
    q = mm(queries_in, proj[:, :width]).astype(BF)
    kv = mm(keys_in, proj[:, width:]).astype(BF)
    k, v = kv[:, :width], kv[:, width:]
    soft = softmax(q, k, valid)
    mixture = jnp.einsum("hln,nhc->lhc", soft.astype(BF), heads_of(v), preferred_element_type=F32)
    mixture = mixture.reshape(inputs.shape).astype(BF)
    result = (inputs + mm(mixture, out)).astype(BF)
    return result, (unit_x, inv_x, queries_in, unit_s, inv_s, keys_in, q, k, v, soft, mixture)


def attend_back(gradient, kept, gain_q, gain_kv, proj, out):
    unit_x, inv_x, queries_in, unit_s, inv_s, keys_in, q, k, v, soft, mixture = kept
    width = gradient.shape[1]
    scale = 1.0 / math.sqrt(HD)
    grad_mix = mm_cols(gradient, out).astype(BF)
    grad_soft = jnp.einsum(
        "lhc,nhc->hln", heads_of(grad_mix), heads_of(v), preferred_element_type=F32
    )
    inner = jnp.sum(soft * grad_soft, axis=-1, keepdims=True)
    grad_scores = (soft * (grad_soft - inner)).astype(BF)
    dq = jnp.einsum("hln,nhc->lhc", grad_scores, heads_of(k), preferred_element_type=F32) * scale
    dk = jnp.einsum("hln,lhc->nhc", grad_scores, heads_of(q), preferred_element_type=F32) * scale
    dv = jnp.einsum(
        "hln,lhc->nhc", soft.astype(BF), heads_of(grad_mix), preferred_element_type=F32
    )
    dq = dq.reshape(gradient.shape).astype(BF)
    dk = dk.reshape(-1, width).astype(BF)
    dv = dv.reshape(-1, width).astype(BF)
    grad_x, gain_q_grad = norm_back(mm_cols(dq, proj[:, :width]), unit_x, inv_x, gain_q)
    back_s = mm_cols(dk, proj[:, width : 2 * width]) + mm_cols(dv, proj[:, 2 * width :])
    grad_s, gain_kv_grad = norm_back(back_s, unit_s, inv_s, gain_kv)
    pairs = ((queries_in, dq), (keys_in, dk), (keys_in, dv), (mixture, gradient))
    return grad_x, grad_s, gain_q_grad, gain_kv_grad, pairs


def feed(inputs, gain, w_in, b_in, w_down, b_out):
    unit, inverse = unit_rows(inputs)
    lowered = (unit * gain).astype(BF)
    pre_act = mm(lowered, w_in) + b_in
    active = jax.nn.gelu(pre_act).astype(BF)
    result = (inputs + mm_cols(active, w_down) + b_out).astype(BF)
    return result, (unit, inverse, lowered, pre_act, active)


def feed_back(gradient, kept, gain, w_in, w_down):
    unit, inverse, lowered, pre_act, active = kept
    grad_act = mm(gradient, w_down)
    grad_pre = jax.vjp(jax.nn.gelu, pre_act)[1](grad_act)[0].astype(BF)
    grad_x, gain_grad = norm_back(mm_cols(grad_pre, w_in), unit, inverse, gain)
    bias_grad = jnp.sum(grad_pre.astype(F32), axis=0)
    out_grad = jnp.sum(gradient.astype(F32), axis=0)
    return grad_x, gain_grad, bias_grad, out_grad, ((lowered, grad_pre), (gradient, active))


def gelu_both(value):
    factor = math.sqrt(2.0 / math.pi)
    square = value * value
    bent = jnp.tanh(factor * value * (1.0 + 0.044715 * square))
    inner = factor * (1.0 + 3.0 * 0.044715 * square)
    half = 0.5 * (1.0 + bent)
    return value * half, half + 0.5 * value * (1.0 - bent * bent) * inner


def tiles(count, body, size=256):
    def step(index, carry):
        body(pl.ds(pl.multiple_of(index * size, size), size), index)
        return carry

    lax.fori_loop(0, count, step, 0)


def norm_into(source, gain, target):
    def step(index, carry):
        here = pl.ds(pl.multiple_of(index * 32, 32), 32)
        unit, _ = unit_rows(source[here, :].astype(F32))
        target[here, :] = (unit * gain).astype(BF)
        return carry

    lax.fori_loop(0, source.shape[0] // 32, step, 0)


def gather_kernel(*refs):
    cross_proj, cross_out, mlp_in, mlp_down, self_proj, self_out = refs[:6]
    latents_in, cot_all, points_in, near_in, length_in = refs[6:11]
    vec_parts = refs[11:16]
    section_at = lax.axis_index("section")
    batch_at = lax.axis_index("batch")
    x_at = lax.rem(section_at, 2)
    y_at = section_at // 2
    ins = (
        cross_proj,
        cross_out,
        mlp_in.at[0],
        mlp_down.at[0],
        self_proj,
        self_out,
        mlp_in.at[1],
        mlp_down.at[1],
    )
    count = len(ins)
    outs = refs[16 : 16 + count]
    rest = refs[16 + count :]
    gains, norm_out, mask_in, picks_out = rest[:4]
    kept_outs = rest[4:24]
    (
        u1,
        u2,
        u3,
        u4,
        grad_top,
        xq_c,
        sn_c,
        q_c,
        k_c,
        v_c,
        o_c,
        xn_s,
        q_s,
        k_s,
        v_s,
        o_s,
        src_in,
        lowered,
        before,
        active,
        x_in,
        cot_in,
        vec_in,
        vec_rows,
        slots,
        total_rows,
        part_out,
        part_in,
        vec_out,
        biases,
        plane,
        line_in,
    ) = rest[24:56]
    (own_sem, send, recv, kin_send, kin_recv, vec_sems) = rest[56:62]
    (slot_sems, kept_sems, plane_sems, line_sems, pair_sems, row_sems) = rest[62:]
    line = 4
    core = lax.rem(batch_at, 2)
    spot = batch_at // 2
    beside = section_at + 1 - 2 * x_at
    above = lax.rem(section_at + 2, 4)
    sibling = batch_at + 1 - 2 * core
    shard = ins[0].shape[0]
    place = section_at * 2 + core
    rows = x_in.shape[0]

    def down_line(step):
        return lax.rem(spot + step, line) * 2 + core

    def up_line(step):
        return lax.rem(spot + line - step, line) * 2 + core

    near_peers = []
    for turn in range(1, 8):
        other = lax.rem(place + turn, 8)
        near_peers.append((other // 2, spot * 2 + lax.rem(other, 2)))
    line_peers = [(section_at, down_line(step)) for step in range(1, line)]
    far_peers = [(section_at, down_line(step) + 1 - 2 * core) for step in range(1, line)]
    vec_peers = [(section_at, sibling)] + line_peers + far_peers
    peers = near_peers + line_peers + far_peers
    barrier = pltpu.get_barrier_semaphore()
    for peer in peers:
        pl.semaphore_signal(barrier, inc=1, device_id=peer, device_id_type=MESH)
    pl.semaphore_wait(barrier, len(peers))

    def spread(ref, owner, first, size):
        return ref.at[pl.ds(pl.multiple_of(owner * shard, shard), shard), pl.ds(first, size)]

    def is_feed(item):
        return item % 8 >= 4

    def source_of(item, first, size):
        index, start = GATHERED[item]
        if is_feed(item):
            first = pl.multiple_of(first + y_at * outs[index].shape[1], 128)
        return ins[index].at[:, pl.ds(first, size)]

    def piece(item):
        start = GATHERED[item][1]
        if is_feed(item):
            return pl.multiple_of(start + x_at * 512, 128), 512
        return pl.multiple_of(start + section_at * 256, 128), 256

    def own_line(item, way):
        first, size = piece(item)
        return pltpu.make_async_remote_copy(
            source_of(item, first, size),
            spread(outs[GATHERED[item][0]], batch_at, first, size),
            send.at[5 * way, item, 0],
            recv.at[0, item, 3 if way else 1],
            device_id=(section_at, batch_at + (-2 if way else 2)),
            device_id_type=MESH,
        )

    def onward_line(item, step, way):
        first, size = piece(item)
        ref = spread(outs[GATHERED[item][0]], up_line(step), first, size)
        return pltpu.make_async_remote_copy(
            ref,
            ref,
            send.at[0, item, step],
            recv.at[0, item, step - 1 if way else step + 1],
            device_id=(section_at, batch_at + (-2 if way else 2)),
            device_id_type=MESH,
        )

    def came_line(item, step):
        first, size = piece(item)
        ref = spread(outs[GATHERED[item][0]], up_line(step), first, size)
        return pltpu.make_async_remote_copy(
            ref,
            ref,
            send.at[0, item, step],
            recv.at[0, item, step],
            device_id=(section_at, sibling),
            device_id_type=MESH,
        )

    def start_line(item):
        @pl.when(spot < 3)
        def _():
            own_line(item, 0).start()

        @pl.when(spot > 0)
        def _():
            own_line(item, 1).start()

    def arrive_line(item, apart):
        @pl.when(spot >= apart)
        def _():
            came_line(item, apart).wait_recv()

            @pl.when(spot < 3)
            def _():
                onward_line(item, apart, 0).start()

            for copy in near(item, apart):
                copy.start()

        @pl.when(spot + apart <= 3)
        def _():
            came_line(item, 4 - apart).wait_recv()

            @pl.when(spot > 0)
            def _():
                onward_line(item, 4 - apart, 1).start()

            for copy in near(item, 4 - apart):
                copy.start()

    def sent_line(item):
        @pl.when(spot < 3)
        def _():
            own_line(item, 0).wait_send()

        @pl.when(spot > 0)
        def _():
            own_line(item, 1).wait_send()

        for apart in (1, 2, 3):

            @pl.when(jnp.logical_and(spot >= apart, spot < 3))
            def _():
                onward_line(item, apart, 0).wait_send()

            @pl.when(jnp.logical_and(spot + apart <= 3, spot > 0))
            def _():
                onward_line(item, 4 - apart, 1).wait_send()

        for step in (1, 2, 3):
            for copy in near(item, step):
                copy.wait_send()

    def plane_copy(item, step, way, low, wide, peer):
        ref = spread(outs[GATHERED[item][0]], up_line(step), low, wide)
        return pltpu.make_async_remote_copy(
            ref,
            ref,
            send.at[way, item, step],
            recv.at[way, item, step],
            device_id=(peer, batch_at),
            device_id_type=MESH,
        )

    def near(item, step):
        first, size = piece(item)
        copies = [plane_copy(item, step, 1, first, size, beside)]
        if not is_feed(item):
            copies.append(plane_copy(item, step, 2, first, size, above))
        return copies

    def far(item, step):
        start = GATHERED[item][1]
        by_y = pl.multiple_of(start + beside * 256, 128)
        by_x = pl.multiple_of(start + above * 256 + 128, 128)
        return [
            plane_copy(item, step, 3, by_y, 128, above),
            plane_copy(item, step, 4, by_x, 128, beside),
        ]

    def kin(item, step):
        index, start = GATHERED[item]
        if step == 0:
            source = source_of(item, start, GATHER_WIDTH)
        else:
            source = spread(outs[index], up_line(step), start, GATHER_WIDTH)
        return pltpu.make_async_remote_copy(
            source,
            spread(outs[index], up_line(step), start, GATHER_WIDTH),
            kin_send.at[item, step],
            kin_recv.at[item, step],
            device_id=(section_at, sibling),
            device_id_type=MESH,
        )

    def own(item):
        index, start = GATHERED[item]
        return pltpu.make_async_copy(
            source_of(item, start, GATHER_WIDTH),
            spread(outs[index], batch_at, start, GATHER_WIDTH),
            own_sem.at[item],
        )

    def vec_copy(which):
        return pltpu.make_async_remote_copy(
            vec_in,
            vec_out.at[batch_at],
            vec_sems.at[0, which],
            vec_sems.at[1, which],
            device_id=vec_peers[which],
            device_id_type=MESH,
        )

    def slot_copy(item):
        index, start = GATHERED[item]
        return pltpu.make_async_copy(
            outs[index].at[:, pl.ds(start, GATHER_WIDTH)],
            slots.at[item % SLOTS],
            slot_sems.at[item % SLOTS],
        )

    def near_norm(turn):
        return pltpu.make_async_remote_copy(
            plane.at[8],
            plane.at[place],
            plane_sems.at[0, turn],
            plane_sems.at[1, turn],
            device_id=near_peers[turn],
            device_id_type=MESH,
        )

    def far_norm(step):
        return pltpu.make_async_remote_copy(
            line_in.at[4],
            line_in.at[spot],
            line_sems.at[0, step],
            line_sems.at[1, step],
            device_id=line_peers[step],
            device_id_type=MESH,
        )

    def rows_over(layer):
        return pltpu.make_async_remote_copy(
            lowered.at[layer, pl.ds(0, rows)],
            lowered.at[layer, pl.ds(rows, rows)],
            pair_sems.at[0, layer, 0],
            pair_sems.at[1, layer, 0],
            device_id=(above, batch_at),
            device_id_type=MESH,
        )

    def part_over(layer):
        return pltpu.make_async_remote_copy(
            part_out.at[layer],
            part_in.at[layer],
            pair_sems.at[0, layer, 1],
            pair_sems.at[1, layer, 1],
            device_id=(above, batch_at),
            device_id_type=MESH,
        )

    steps = range(1, line)
    total = len(GATHERED)
    started = []

    def launch(copies):
        for copy in copies:
            copy.start()
        started.extend(copies)

    kept = (
        (u1, u2, u3, u4, grad_top)
        + (xq_c, sn_c, q_c, k_c, v_c, o_c)
        + (xn_s, q_s, k_s, v_s, o_s)
        + (src_in, lowered, before, active)
    )
    names = {id(ref): place for place, ref in enumerate(kept)}

    def keep(*chosen):
        for ref in chosen:
            index = names[id(ref)]
            pltpu.make_async_copy(ref, kept_outs[index], kept_sems.at[index]).start(priority=LOCAL)

    def row(index):
        return gains[index : index + 1, :]

    def project(source, target, slot):
        def tile(columns, _):
            target[:, columns] = mm(source[...], slots[slot, :, columns]).astype(BF)

        tiles(2, tile, 512)

    def heads(q, k, v, o, masked):
        def head(index, carry):
            here = pl.ds(pl.multiple_of(index * HD, HD), HD)
            scores = mm_cols(q[:, here], k[:, here]) * (1.0 / math.sqrt(HD))
            if masked:
                scores = jnp.where(mask_in[...] > 0.0, scores, MASKED)
            grown = jnp.exp(scores - jnp.max(scores, axis=-1, keepdims=True))
            soft = grown / jnp.sum(grown, axis=-1, keepdims=True)
            o[:, here] = mm(soft.astype(BF), v[:, here]).astype(BF)
            return carry

        lax.fori_loop(0, q.shape[1] // HD, head, 0)

    def close_attention(inputs, o, target, slot):
        def tile(columns, _):
            target[:, columns] = (
                inputs[:, columns].astype(F32) + mm(o[...], slots[slot, :, columns])
            ).astype(BF)

        tiles(2, tile, 512)

    def feed_up(layer, chunk, slot):
        def tile(columns, index):
            first = chunk * GATHER_WIDTH + index * 512
            there = pl.ds(pl.multiple_of(first, 512), 512)
            lanes = pl.ds(pl.multiple_of(y_at * 2048 + first, 512), 512)
            value = mm(lowered[layer], slots[slot, :, columns]) + biases[layer : layer + 1, lanes]
            active_part, slope = gelu_both(value)
            before[layer, :, there] = slope
            active[layer, :, there] = active_part.astype(BF)

        tiles(2, tile, 512)

    def feed_down(layer, chunk, slot):
        chosen = pl.ds(chunk * GATHER_WIDTH, GATHER_WIDTH)

        def tile(columns, _):
            value = mm_cols(active[layer, :, chosen], slots[slot, columns, :])
            if chunk == 0:
                total_rows[:, columns] = value
            else:
                value = total_rows[:, columns] + value
                total_rows[:, columns] = value
                part_out[layer, :, columns] = value[rows:].astype(BF)

        tiles(2, tile, 512)

    def feed_close(layer):
        inputs, target = (u1, u3)[layer], (u2, u4)[layer]
        part_over(layer).wait_recv()

        def tile(columns, _):
            target[:, columns] = (
                inputs[:, columns].astype(F32)
                + (total_rows[0:rows, columns] + part_in[layer, :, columns].astype(F32))
                + gains[5 + layer : 6 + layer, columns]
            ).astype(BF)

        tiles(2, tile, 512)
        keep(target)

    def work(item):
        slot_copy(item).wait()
        slot = item % SLOTS
        layer, stage = item // 8, item % 8
        inputs = (x_in, u2)[layer]
        middle = (u1, u3)[layer]
        q, k, v, o = ((q_c, k_c, v_c, o_c), (q_s, k_s, v_s, o_s))[layer]
        if stage == 0:
            if layer == 0:
                norm_into(x_in, row(0), xq_c)
                norm_into(src_in, row(1), sn_c)
                keep(xq_c, sn_c)
            else:
                feed_close(0)
                norm_into(u2, row(2), xn_s)
                keep(xn_s)
            project((xq_c, xn_s)[layer], q, slot)
        elif stage == 1:
            project((sn_c, xn_s)[layer], k, slot)
        elif stage == 2:
            project((sn_c, xn_s)[layer], v, slot)
            heads(q, k, v, o, layer == 0)
            keep(q, k, v, o)
        elif stage == 3:
            close_attention(inputs, o, middle, slot)
            norm_into(middle, row(3 + layer), lowered.at[layer, pl.ds(0, rows)])
            launch([rows_over(layer)])
            keep(middle)
        elif stage % 2 == 0:
            if stage == 4:
                rows_over(layer).wait_recv()
            feed_up(layer, (stage - 4) // 2, slot)
        else:
            feed_down(layer, (stage - 4) // 2, slot)
            if stage == 7:
                launch([part_over(layer)])

    for item in range(AHEAD):
        start_line(item)
    here = pl.ds(pl.multiple_of(section_at * rows, rows), rows)
    row_copies = [
        pltpu.make_async_copy(latents_in.at[here], x_in, row_sems.at[0]),
        pltpu.make_async_copy(cot_all.at[here], cot_in, row_sems.at[1]),
    ]
    for copy in row_copies:
        copy.start()
    cross_gain, self_gain, feed_gain, out_bias, in_bias = vec_parts
    vec_rows[...] = jnp.zeros_like(vec_rows)
    vec_rows[0:2, :] = cross_gain[...].astype(F32)
    vec_rows[2:3, :] = self_gain[...].astype(F32)
    vec_rows[3:5, :] = feed_gain[...].astype(F32)
    vec_rows[5:7, :] = out_bias[...].astype(F32)
    bias_rows = in_bias[...].astype(F32)
    for layer in range(2):
        for part_at in range(4):
            index = 7 + 4 * layer + part_at
            vec_rows[index : index + 1, :] = bias_rows[
                layer : layer + 1, part_at * 128 : part_at * 128 + 128
            ]
    vec_in[...] = vec_rows[...].astype(BF)
    vec_out[batch_at] = vec_in[...]
    for which in range(7):
        vec_copy(which).start()
    lanes = lax.broadcasted_iota(jnp.int32, (1, rows), 1)
    length = length_in[pl.ds(section_at, 1), :]
    mask_in[...] = jnp.where(lanes < length, 1.0, 0.0)
    point_at = lax.broadcasted_iota(jnp.int32, (points_in.shape[0], rows), 0)
    wanted = near_in[pl.ds(section_at, 1), :]
    picks = jnp.where(point_at == wanted, 1.0, 0.0)
    picks_out[...] = picks.astype(BF)
    turned = picks.T.astype(BF)

    def source_tile(columns, _):
        src_in[:, columns] = mm(turned, points_in[:, columns]).astype(BF)

    tiles(2, source_tile, 512)
    keep(src_in)
    for copy in row_copies:
        copy.wait()
    for moment in range(-2, total + 4):
        if moment + 2 + AHEAD < total:
            start_line(moment + 2 + AHEAD)
        for apart in (1, 2, 3):
            if 0 <= moment + 3 - apart < total:
                arrive_line(moment + 3 - apart, apart)
        if 0 <= moment < total:
            own(moment).start(priority=LOCAL)
            launch([kin(moment, 0)])
        if 0 <= moment - 1 < total:
            for step in steps:
                if is_feed(moment - 1):
                    near(moment - 1, step)[0].wait_recv()
                    launch([kin(moment - 1, step)])
                else:
                    for copy, onward in zip(near(moment - 1, step), far(moment - 1, step)):
                        copy.wait_recv()
                        launch([onward])
        if 0 <= moment - 2 < total and not is_feed(moment - 2):
            for step in steps:
                for copy in far(moment - 2, step):
                    copy.wait_recv()
                launch([kin(moment - 2, step)])
        if moment == 2:
            for which in range(7):
                vec_copy(which).wait()
            for owner in range(8):
                values = vec_out[owner].astype(F32)
                gains[:, owner * 128 : owner * 128 + 128] = values
                for layer in range(2):
                    for part_at in range(4):
                        first = owner * 512 + part_at * 128
                        index = 7 + 4 * layer + part_at
                        biases[layer : layer + 1, first : first + 128] = values[index : index + 1]
        if 0 <= moment - 4 < total:
            work(moment - 4)
        if 0 <= moment - 3 < total:
            own(moment - 3).wait()
            for step in range(line):
                kin(moment - 3, step).wait_recv()
            slot_copy(moment - 3).start(priority=LOCAL)
    keep(lowered, before, active)
    feed_close(1)

    def square(index, carry):
        here = pl.ds(pl.multiple_of(index * 32, 32), 32)
        values = u4[here, :].astype(F32)
        return carry + jnp.sum(values * values, axis=0, keepdims=True)

    squares = lax.fori_loop(0, u4.shape[0] // 32, square, jnp.zeros((1, u4.shape[1]), F32))
    mean = jnp.sum(squares, axis=1, keepdims=True) / (u4.shape[0] * u4.shape[1])
    group_norm = jnp.sqrt(mean + EPSILON)
    plane[8] = jnp.broadcast_to(group_norm, plane.shape[1:])
    for turn in range(7):
        near_norm(turn).start()
    plane[place] = plane[8]
    for turn in range(7):
        near_norm(turn).wait()
    line_in[4] = jnp.sum(plane[0:8], axis=0)
    for step in range(3):
        far_norm(step).start()
    line_in[spot] = line_in[4]
    for step in range(3):
        far_norm(step).wait()
    norm_mean = jnp.sum(line_in[0:4], axis=0) / 32.0
    norm_out[...] = norm_mean
    ratio = norm_mean[0:1, 0:1] / group_norm

    def top(index, carry):
        here = pl.ds(pl.multiple_of(index * 32, 32), 32)
        grad_top[here, :] = (
            cot_in[here, :].astype(F32) + ratio * u4[here, :].astype(F32)
        ).astype(BF)
        return carry

    lax.fori_loop(0, u4.shape[0] // 32, top, 0)
    keep(grad_top)
    for index, ref in enumerate(kept):
        pltpu.make_async_copy(ref, kept_outs[index], kept_sems.at[index]).wait()
    for item in range(total):
        sent_line(item)
    for copy in started:
        copy.wait_send()


def gather_forward(blocks, latents, cotangent, points, near, lengths, vectors):
    width = latents.shape[1]
    rows = near.shape[1]
    half = blocks[2].shape[2] // 2
    widths = (3 * width, width, half, half) * 2
    total = len(GATHERED)
    anywhere = pl.BlockSpec(memory_space=pl.ANY)
    vmem = pl.BlockSpec(memory_space=pltpu.VMEM)
    plain = ((rows, width), BF)
    kept = [plain] * 17 + [
        ((2, 2 * rows, width), BF),
        ((2, 2 * rows, half), F32),
        ((2, 2 * rows, half), BF),
    ]
    dma = pltpu.SemaphoreType.DMA
    return pl.pallas_call(
        gather_kernel,
        out_shape=[jax.ShapeDtypeStruct((width, size), BF) for size in widths]
        + [
            jax.ShapeDtypeStruct((16, width), F32),
            jax.ShapeDtypeStruct((8, 128), F32),
            jax.ShapeDtypeStruct((1, rows), F32),
            jax.ShapeDtypeStruct((points.shape[0], rows), BF),
        ]
        + [jax.ShapeDtypeStruct(*one) for one in kept],
        in_specs=[anywhere] * (len(blocks) + 2) + [vmem] * 8,
        out_specs=[anywhere] * len(widths) + [vmem] * 4 + [anywhere] * len(kept),
        scratch_shapes=[pltpu.VMEM(*one) for one in kept]
        + [
            pltpu.VMEM((rows, width), BF),
            pltpu.VMEM((rows, width), BF),
            pltpu.VMEM((16, 128), BF),
            pltpu.VMEM((16, 128), F32),
            pltpu.VMEM((SLOTS, width, GATHER_WIDTH), BF),
            pltpu.VMEM((2 * rows, width), F32),
            pltpu.VMEM((2, rows, width), BF),
            pltpu.VMEM((2, rows, width), BF),
            pltpu.VMEM((8, 16, 128), BF),
            pltpu.VMEM((2, 2 * half), F32),
            pltpu.VMEM((9, 8, 128), F32),
            pltpu.VMEM((5, 8, 128), F32),
            dma((total,)),
            dma((6, total, 4)),
            dma((5, total, 4)),
            dma((total, 4)),
            dma((total, 4)),
            dma((2, 7)),
            dma((SLOTS,)),
            dma((len(kept),)),
            dma((2, 7)),
            dma((2, 3)),
            dma((2, 2, 2)),
            dma((2,)),
        ],
        compiler_params=pltpu.CompilerParams(
            collective_id=1, has_side_effects=True, vmem_limit_bytes=56 * 2**20
        ),
        cost_estimate=pl.CostEstimate(
            flops=2 * rows * width * sum(widths), bytes_accessed=2**27, transcendentals=2**21
        ),
    )(*blocks, latents, cotangent, points, near, lengths, *vectors)


ITEM_COUNT = 16
FEEDS = (0, 1, 2, 4, 6, 9, 10, 13)
ATTENDS = (3, 5, 7, 8, 11, 12, 14, 15)
WINDOWS = 4
STAGES = 3


def reduce_kernel(*refs):
    total = ITEM_COUNT
    (
        proj_c,
        out_c,
        in_0,
        down_0,
        proj_s,
        out_s,
        in_1,
        down_1,
        u1_in,
        u2_in,
        u3_in,
        last_ref,
        top_in,
        xq_c,
        sn_c,
        q_c,
        k_c,
        v_c,
        o_c,
        xn_s,
        q_s,
        k_s,
        v_s,
        o_s,
        lowered,
        before,
        active,
        latents_in,
        src_in,
        gains,
        mask_in,
        picks_in,
    ) = refs[:32]
    (up_out, down_out, proj_out_c, proj_out_s, end_out_c, end_out_s) = refs[32:38]
    (last_out, first_out, point_out, small_out) = refs[38:42]
    (grads_h, kin_lf, kin_la, kin_rf, kin_ra) = refs[42:47]
    (
        lwin_f,
        lwin_a,
        raw,
        rwin,
        stage,
        merged_f,
        merged_a,
        passing_f,
        passing_a,
        lined_f,
        lined_a,
        crossed_f,
        crossed_a,
        pair,
        slope,
        rows_sum,
        hbuf,
        slots,
        qb,
        kb,
        vb,
        dob,
        dqkv,
        part_out,
        part_in,
        grad,
        ub,
        point_in,
        point_sum,
        small_in,
        small_sum,
    ) = refs[47:78]
    (
        kin_l_sems,
        kin_r_sems,
        raw_sems,
        win_sems,
        xy_sems,
        line_send,
        line_recv,
        cross_sems,
        out_sems,
        own_sems,
        lat_sems,
        far_sems,
        lat_own,
        point_sems,
        deal_sems,
        point_own,
        small_sems,
        pair_sems,
        slot_sems,
        h_sem,
        save_sems,
        act_sems,
    ) = refs[78:]
    section_at = lax.axis_index("section")
    batch_at = lax.axis_index("batch")
    core = lax.rem(batch_at, 2)
    spot = batch_at // 2
    x_at = lax.rem(section_at, 2)
    y_at = section_at // 2
    beside = section_at + 1 - 2 * x_at
    above = lax.rem(section_at + 2, 4)
    across = lax.rem(beside + 2, 4)
    sibling = batch_at + 1 - 2 * core
    flat = (beside, above)
    bits = (x_at, y_at)
    rows, width = 256, 1024

    peers = [(beside, batch_at), (above, batch_at), (across, batch_at), (section_at, sibling)]
    peers += [(section_at, lax.rem(spot + step, 4) * 2 + core) for step in (1, 2, 3)]
    barrier = pltpu.get_barrier_semaphore()
    for peer in peers:
        pl.semaphore_signal(barrier, inc=1, device_id=peer, device_id_type=MESH)
    pl.semaphore_wait(barrier, len(peers))

    def remote(source, target, sems, where, peer):
        return pltpu.make_async_remote_copy(
            source,
            target,
            sems.at[(0, *where)],
            sems.at[(1, *where)],
            device_id=peer,
            device_id_type=MESH,
        )

    feed_left = (pair, lowered.at[1], pair, lowered.at[0])
    feed_right = (active.at[1], slope, active.at[0], slope)
    att_left = (o_s, xn_s, xn_s, xn_s, o_c, xq_c, sn_c, sn_c)
    att_right = tuple(
        ref
        for turn in range(2)
        for ref in (grads_h.at[turn], dqkv.at[0], dqkv.at[1], dqkv.at[2])
    )

    def columns(spot_of, parity):
        return pl.ds(pl.multiple_of((2 * spot_of + parity) * 128, 128), 128)

    def kin_lefts(feed, job):
        source, target = (feed_left, kin_lf) if feed else (att_left, kin_la)
        return [
            remote(
                source[job].at[:, columns(part, 1 - core)],
                target.at[job, part],
                kin_l_sems,
                (job if feed else 4 + job, part),
                (section_at, sibling),
            )
            for part in range(4)
        ]

    def kin_right(feed, job, chunk):
        if feed:
            here = pl.ds(chunk * 1024, 1024)
            source, target = feed_right[job].at[:, here], kin_rf.at[job, :, here]
        else:
            source, target = att_right[job], kin_ra.at[job]
        where = (2 * job + chunk if feed else 8 + job,)
        return remote(source, target, kin_r_sems, where, (section_at, sibling))

    def item_of(index):
        if index in FEEDS:
            order = FEEDS.index(index)
            return True, order // 2, order % 2
        return False, ATTENDS.index(index), 0

    def window_copies(index):
        feed, job, chunk = item_of(index)
        slot = index % WINDOWS
        size = 512 if feed else 256
        if feed:
            here = pl.ds(chunk * 1024, 1024)
            sources = (feed_right[job].at[:, here], kin_rf.at[job, :, here])
        else:
            sources = (att_right[job], kin_ra.at[job])
        return [
            pltpu.make_async_copy(
                sources[whose],
                rwin.at[slot, pl.ds(whose * size, size)],
                win_sems.at[slot, whose],
            )
            for whose in range(2)
        ]

    def raw_copies(index, part):
        feed, job, _ = item_of(index)
        size = 512 if feed else 256
        own_left = (feed_left if feed else att_left)[job]
        kin_left = (kin_lf if feed else kin_la).at[job]
        sources = (own_left.at[:, columns(part, core)], kin_left.at[part])
        return [
            pltpu.make_async_copy(
                source, raw.at[part, whose, pl.ds(0, size)], raw_sems.at[part, whose]
            )
            for whose, source in enumerate(sources)
        ]

    def raw_start(index):
        feed, job, chunk = item_of(index)
        if chunk == 0:
            for copy in kin_lefts(feed, job):
                copy.wait_recv()
            for part in range(4):
                for copy in raw_copies(index, part):
                    copy.start(priority=LOCAL)

    def load(index):
        feed, job, chunk = item_of(index)
        kin_right(feed, job, chunk).wait_recv()
        for copy in window_copies(index):
            copy.start(priority=LOCAL)
        if chunk == 0:
            if feed and job == 2:
                raw_start(index)
            size = 512 if feed else 256
            target = (lwin_f if feed else lwin_a).at[job]
            for part in range(4):
                for whose, copy in enumerate(raw_copies(index, part)):
                    copy.wait()
                    place = raw.at[part, whose, pl.ds(0, size)]
                    target[part, :, whose * size : whose * size + size] = place[...].T
        if index + 1 < total and item_of(index + 1)[:2] != (True, 2):
            raw_start(index + 1)

    def count_below(item, places):
        return sum((item > place).astype(jnp.int32) for place in places)

    def is_feed(item):
        return functools.reduce(jnp.logical_or, [item == place for place in FEEDS])

    def loaded(slot, feed):
        size = 512 if feed else 256
        for whose in range(2):
            source = kin_rf.at[0, :, pl.ds(0, 1024)] if feed else kin_ra.at[0]
            pltpu.make_async_copy(
                source, rwin.at[slot, pl.ds(whose * size, size)], win_sems.at[slot, whose]
            ).wait()

    def by_kind(item, action):
        @pl.when(is_feed(item))
        def _():
            action(count_below(item, FEEDS), True)

        @pl.when(jnp.logical_not(is_feed(item)))
        def _():
            action(count_below(item, ATTENDS), False)

    def mark(order, feed):
        return order if feed else 8 + order

    def merged_of(order, feed):
        return merged_f.at[lax.rem(order, 4)] if feed else merged_a.at[order]

    def passing_of(order, feed, slot):
        if feed:
            return passing_f.at[lax.rem(order, 6), slot]
        return passing_a.at[lax.rem(order, 4), slot]

    def lined_of(order, feed):
        return lined_f.at[lax.rem(order, 4)] if feed else lined_a.at[order]

    def crossed_of(order, feed):
        return crossed_f.at[lax.rem(order, 4)] if feed else crossed_a.at[order]

    def products(order, slot, choice, store):
        def quarter(index, carry):
            here = pl.ds(pl.multiple_of(index * 256, 256), 256)
            bit = choice[0] + index * (choice[1] - choice[0])
            first = pl.multiple_of(index * 512 + bit * 256, 256)
            left = lwin_a[order].reshape(512, 512)
            right = rwin[slot, 0:512, pl.ds(first, 256)]
            tile = jnp.dot(left, right, preferred_element_type=F32).reshape(4, 128, 256)
            store(pl.ds(0, 4), here, tile)
            return carry

        lax.fori_loop(0, 2, quarter, 0)

    def xy_copies(item):
        return [
            remote(
                stage.at[lax.rem(item, STAGES), :, :, pl.ds(side * 256, 256)],
                merged_a.at[item, :, :, pl.ds(side * 256, 256)],
                xy_sems,
                (item, side),
                (flat[side], batch_at),
            )
            for side in range(2)
        ]

    def xy_sent(item):
        for copy in xy_copies(item):
            copy.wait_send()

    def line_copy(item, feed, dest, place, rightward):
        step = 1 if rightward else -1
        slot = 4 if not rightward and place - 1 == dest else dest
        return pltpu.make_async_remote_copy(
            merged_of(item, feed).at[dest],
            passing_of(item, feed, slot),
            line_send.at[mark(item, feed), dest],
            line_recv.at[mark(item, feed), slot],
            device_id=(section_at, batch_at + 2 * step),
            device_id_type=MESH,
        )

    def line_wait(item, feed, slot):
        pltpu.make_async_remote_copy(
            merged_of(item, feed).at[0],
            passing_of(item, feed, slot),
            line_send.at[mark(item, feed), 0],
            line_recv.at[mark(item, feed), slot],
            device_id=(section_at, sibling),
            device_id_type=MESH,
        ).wait_recv()

    def line_sent(item, feed):
        for step in (1, 2, 3):
            dest = lax.rem(spot + step, 4)
            pltpu.make_async_remote_copy(
                merged_of(item, feed).at[dest],
                passing_of(item, feed, 0),
                line_send.at[mark(item, feed), dest],
                line_recv.at[mark(item, feed), 0],
                device_id=(section_at, sibling),
                device_id_type=MESH,
            ).wait_send()

    def outset(item, feed):
        @pl.when(spot == 0)
        def _():
            for dest in (3, 2, 1):
                line_copy(item, feed, dest, 0, True).start()

        @pl.when(spot == 3)
        def _():
            for dest in (0, 1, 2):
                line_copy(item, feed, dest, 3, False).start()

    def drained(item, feed):
        line_sent(item, feed)
        delivered(item, feed)

    def delivered(item, feed):
        if feed:
            feed_out(item, up_out).wait()
            feed_own(item, up_out).wait()
        else:
            for side in range(2):
                att_out(item, side, end_out_s, 0).wait()
                att_own(item, side, end_out_s, 0).wait()

    def offer(slot, item, feed):
        loaded(slot, feed)
        if feed:

            @pl.when(item >= 4)
            def _():
                line_sent(item - 4, True)

            target = merged_of(item, True)

            def tile(index, carry):
                here = pl.ds(pl.multiple_of(index * 256, 256), 256)
                left = lwin_f[item // 2].reshape(512, 1024)
                right = rwin[slot, :, here]
                value = jnp.dot(left, right, preferred_element_type=F32)
                target[:, :, here] = value.reshape(4, 128, 256).astype(BF)
                return carry

            lax.fori_loop(0, 4, tile, 0)
            outset(item, True)
        else:

            @pl.when(item >= STAGES)
            def _():
                xy_sent(item - STAGES)

            def store(blocks, here, tile):
                stage[lax.rem(item, STAGES), blocks, :, here] = tile.astype(BF)

            products(item, slot, (1 - x_at, 1 - y_at), store)
            for copy in xy_copies(item):
                copy.start()

    def take(slot, item, feed):
        for copy in xy_copies(item):
            copy.wait_recv()
        target = merged_a.at[item]

        def store(blocks, here, tile):
            target[blocks, :, here] = (tile + target[blocks, :, here].astype(F32)).astype(BF)

        products(item, slot, bits, store)
        outset(item, False)

    def relay(item, feed, dest, place, rightward):
        line_wait(item, feed, dest)
        target = merged_of(item, feed)
        arrived = passing_of(item, feed, dest)
        target[dest] = (target[dest].astype(F32) + arrived[...].astype(F32)).astype(BF)
        line_copy(item, feed, dest, place, rightward).start()

    def second_of(item, feed):
        @pl.when(spot == 1)
        def _():
            for dest in (3, 2):
                relay(item, feed, dest, 1, True)

        @pl.when(spot == 2)
        def _():
            for dest in (0, 1):
                relay(item, feed, dest, 2, False)

    def third_of(item, feed):
        @pl.when(spot == 1)
        def _():
            relay(item, feed, 0, 1, False)

        @pl.when(spot == 2)
        def _():
            relay(item, feed, 3, 2, True)

    def feed_cross(item):
        return remote(
            lined_of(item, True),
            crossed_of(item, True),
            cross_sems,
            (item, 0),
            (beside, batch_at),
        )

    def cross_copy(item, side):
        here = pl.ds(side * 256, 256)
        return remote(
            lined_of(item, False).at[:, here],
            crossed_of(item, False).at[:, here],
            cross_sems,
            (8 + item, side),
            (flat[1 - side], batch_at),
        )

    def feed_place(item, target):
        base = y_at * 2048 + lax.rem(item, 2) * 1024
        return target.at[1 - item // 4, :, pl.ds(pl.multiple_of(base, 1024), 1024)]

    def feed_out(item, target):
        return remote(
            lined_of(item, True),
            feed_place(item, target),
            out_sems,
            (item, 0),
            (above, batch_at),
        )

    def feed_own(item, target):
        return pltpu.make_async_copy(
            lined_of(item, True), feed_place(item, target), own_sems.at[item, 0]
        )

    def feed_write(item):
        @pl.when(lax.rem(item, 4) < 2)
        def _():
            feed_out(item, down_out).start()
            feed_own(item, down_out).start(priority=LOCAL)

        @pl.when(lax.rem(item, 4) >= 2)
        def _():
            feed_out(item, up_out).start()
            feed_own(item, up_out).start(priority=LOCAL)

    def att_place(item, side, target, inner):
        base = side * 512 + bits[side] * 256
        return target.at[inner, :, pl.ds(pl.multiple_of(base, 256), 256)]

    def att_out(item, side, target, inner):
        return remote(
            lined_of(item, False).at[:, pl.ds(side * 256, 256)],
            att_place(item, side, target, inner),
            out_sems,
            (8 + item, side),
            (flat[side], batch_at),
        )

    def att_own(item, side, target, inner):
        return pltpu.make_async_copy(
            lined_of(item, False).at[:, pl.ds(side * 256, 256)],
            att_place(item, side, target, inner),
            own_sems.at[8 + item, side],
        )

    def att_write(item):
        inner = lax.rem(item, 4) - 1
        for turn, proj, end in ((0, proj_out_s, end_out_s), (1, proj_out_c, end_out_c)):

            @pl.when(jnp.logical_and(item // 4 == turn, inner >= 0))
            def _():
                for side in range(2):
                    att_out(item, side, proj, inner).start()
                    att_own(item, side, proj, inner).start(priority=LOCAL)

            @pl.when(jnp.logical_and(item // 4 == turn, inner < 0))
            def _():
                for side in range(2):
                    att_out(item, side, end, 0).start()
                    att_own(item, side, end, 0).start(priority=LOCAL)

    def close_of(item, feed):
        if feed:

            @pl.when(item >= 4)
            def _():
                delivered(item - 4, True)

        for place in range(4):

            @pl.when(spot == place)
            def _():
                value = merged_of(item, feed)[place].astype(F32)
                if place > 0:
                    line_wait(item, feed, place)
                    value += passing_of(item, feed, place)[...].astype(F32)
                if place < 3:
                    line_wait(item, feed, 4)
                    value += passing_of(item, feed, 4)[...].astype(F32)
                lined_of(item, feed)[...] = value.astype(BF)

        if feed:
            feed_cross(item).start()
        else:
            for side in range(2):
                cross_copy(item, side).start()

    def finish_of(item, feed):
        if feed:
            feed_cross(item).wait()
        else:
            for side in range(2):
                cross_copy(item, side).wait()
        target = lined_of(item, feed)
        target[...] = (
            target[...].astype(F32) + crossed_of(item, feed)[...].astype(F32)
        ).astype(BF)
        if feed:
            feed_write(item)
        else:
            att_write(item)

    def small_copy(phase):
        if phase == 0:
            peer = (section_at, sibling)
        elif phase < 3:
            peer = (flat[phase - 1], batch_at)
        else:
            peer = (section_at, lax.rem(spot + phase - 2, 4) * 2 + core)
        return remote(
            small_sum.at[min(phase, 3)], small_in.at[phase], small_sems, (phase,), peer
        )

    quarter_rows = pair.shape[0] // 4

    def point_copy(which):
        peer = (beside, above, across)[which]
        return remote(
            pair.at[pl.ds(pl.multiple_of(peer * quarter_rows, 128), quarter_rows)],
            point_in.at[which],
            point_sems,
            (which,),
            (peer, batch_at),
        )

    def point_place():
        return point_out.at[pl.ds(pl.multiple_of(section_at * quarter_rows, 128), quarter_rows)]

    def point_deal(which):
        peer = (beside, above, across)[which]
        return remote(point_sum, point_place(), deal_sems, (which,), (peer, batch_at))

    def point_local():
        return pltpu.make_async_copy(point_sum, point_place(), point_own.at[0])

    pairs = ((last_ref, last_out), (grad, first_out))

    def lat_copy(which, way):
        source, target = pairs[which]
        return remote(
            source,
            target.at[pl.ds(pl.multiple_of(section_at * rows, rows), rows)],
            lat_sems,
            (which, way),
            (flat[way], batch_at),
        )

    def lat_far(which, way):
        target = pairs[which][1]
        low = flat[way] * rows + way * (rows // 2)
        part = target.at[pl.ds(pl.multiple_of(low, rows // 2), rows // 2)]
        return remote(part, part, far_sems, (which, way), (flat[1 - way], batch_at))

    def lat_local(which):
        source, target = pairs[which]
        return pltpu.make_async_copy(
            source,
            target.at[pl.ds(pl.multiple_of(section_at * rows, rows), rows)],
            lat_own.at[which],
        )

    def lat_start(which):
        lat_local(which).start(priority=LOCAL)
        for way in range(2):
            lat_copy(which, way).start()

    def lat_onward(which):
        for way in range(2):
            lat_copy(which, way).wait_recv()
            lat_far(which, way).start()

    loads = []
    for turn, (proj, out, up, down) in enumerate(
        ((proj_s, out_s, in_1, down_1), (proj_c, out_c, in_0, down_0))
    ):
        for chunk in range(2):
            loads += [down.at[:, pl.ds(chunk * 1024, 1024)], up.at[:, pl.ds(chunk * 1024, 1024)]]
        loads.append(out)
        loads += [proj.at[:, pl.ds(which * 1024, 1024)] for which in range(3)]

    def slot_copy(index):
        return pltpu.make_async_copy(loads[index], slots.at[index % 2], slot_sems.at[index % 2])

    def opened(index):
        slot_copy(index).wait()
        return index % 2

    def closed(index):
        if index + 2 < len(loads):
            slot_copy(index + 2).start(priority=LOCAL)

    def h_copy(index):
        layer, chunk = 1 - index // 2, index % 2
        return pltpu.make_async_copy(
            before.at[layer, :, pl.ds(chunk * 1024, 1024)], hbuf, h_sem.at[0]
        )

    def pair_over(turn):
        return remote(
            pair.at[pl.ds(0, rows)],
            pair.at[pl.ds(rows, rows)],
            pair_sems,
            (turn, 0),
            (above, batch_at),
        )

    def part_over(turn):
        return remote(
            part_out.at[turn], part_in.at[turn], pair_sems, (turn, 1), (above, batch_at)
        )

    def grad_saved(turn):
        return pltpu.make_async_copy(grad, grads_h.at[turn], save_sems.at[0])

    def act_copies(turn):
        chosen = ((q_s, k_s, v_s), (q_c, k_c, v_c))[turn]
        return [
            pltpu.make_async_copy(source, target, act_sems.at[index])
            for index, (source, target) in enumerate(zip(chosen, (qb, kb, vb)))
        ]

    def row_copy(index):
        if index == 3:
            source = latents_in.at[pl.ds(pl.multiple_of(section_at * rows, rows), rows)]
        else:
            source = (u3_in, u2_in, u1_in)[index]
        return pltpu.make_async_copy(source, ub, act_sems.at[3])

    def small_row(index, value):
        small_sum[0, index : index + 1, :] = value

    def open_pair(turn):
        pair[0:rows, :] = grad[...]
        pair_over(turn).start()

    def pair_ready(turn):
        pair_over(turn).wait()
        for copy in kin_lefts(True, 2 * turn):
            copy.start()

    def feed_chunk(turn, chunk):
        layer = 1 - turn
        base = 8 * turn + 2 * chunk
        h_copy(2 * turn + chunk).wait()
        if turn == 1:
            kin_right(True, 1, chunk).wait_send()
        slot = opened(base)

        def up_tile(here, index):
            there = pl.ds(pl.multiple_of(chunk * 1024 + index * 256, 256), 256)
            value = mm(pair[...], slots[slot, :, here]) * hbuf[:, here]
            short = value.astype(BF)
            slope[:, there] = short
            column = jnp.sum(short.astype(F32), axis=0, keepdims=True)
            for half in range(2):
                index_at = 7 + 4 * layer + 2 * half + chunk
                small_sum[0, index_at : index_at + 1, here] = jnp.where(
                    y_at == half, column, jnp.zeros_like(column)
                )

        tiles(4, up_tile)
        closed(base)
        if 2 * turn + chunk + 1 < 4:
            h_copy(2 * turn + chunk + 1).start(priority=LOCAL)
        kin_right(True, 2 * turn + 1, chunk).start()
        slot = opened(base + 1)

        def down_tile(there, _):
            value = mm_cols(slope[:, chunk * 1024 : chunk * 1024 + 1024], slots[slot, there, :])
            if chunk == 0:
                rows_sum[:, there] = value
            else:
                value = rows_sum[:, there] + value
                rows_sum[:, there] = value
                part_out[turn, :, there] = value[rows:].astype(BF)

        tiles(4, down_tile)
        closed(base + 1)
        if chunk == 1:
            if turn == 0:
                for copy in kin_lefts(True, 0):
                    copy.wait_send()
            part_over(turn).start()

    def row_steps(body, count):
        zero = jnp.zeros((1, width), F32)

        def step(index, carry):
            here = pl.ds(pl.multiple_of(index * 32, 32), 32)
            return tuple(a + b for a, b in zip(carry, body(here)))

        return lax.fori_loop(0, rows // 32, step, (zero,) * count)

    def lean(back, unit, inverse, gain):
        scaled = back * gain
        inner = (
            scaled
            - jnp.mean(scaled, axis=-1, keepdims=True)
            - unit * jnp.mean(scaled * unit, axis=-1, keepdims=True)
        )
        return inverse * inner, jnp.sum(back * unit, axis=0, keepdims=True)

    def feed_end(turn):
        layer = 1 - turn
        gain = gains[3 + layer : 4 + layer, :]
        part_over(turn).wait_recv()
        row_copy(2 * turn).wait()

        def body(here):
            unit, inverse = unit_rows(ub[here, :].astype(F32))
            back = rows_sum[here, :] + part_in[turn, here, :].astype(F32)
            dx, gain_part = lean(back, unit, inverse, gain)
            old = grad[here, :].astype(F32)
            grad[here, :] = (old + dx).astype(BF)
            return gain_part, jnp.sum(old, axis=0, keepdims=True)

        gain_grad, out_grad = row_steps(body, 2)
        row_copy(2 * turn + 1).start(priority=LOCAL)
        small_row(3 + layer, gain_grad)
        small_row(5 + layer, out_grad)
        grad_saved(turn).start(priority=LOCAL)
        slot = opened(8 * turn + 4)

        def tile(there, _):
            dob[:, there] = mm_cols(grad[...], slots[slot, there, :]).astype(BF)

        tiles(2, tile, 512)
        closed(8 * turn + 4)
        grad_saved(turn).wait()
        kin_right(False, 4 * turn, 0).start()

    def attend_heads(turn):
        scale = 1.0 / math.sqrt(HD)
        for copy in act_copies(turn):
            copy.wait()
        if turn == 1:
            for which in range(3):
                kin_right(False, 1 + which, 0).wait_send()

        def head(index, carry):
            here = pl.ds(pl.multiple_of(index * HD, HD), HD)
            q, k, v, do = qb[:, here], kb[:, here], vb[:, here], dob[:, here]
            scores = mm_cols(q, k) * scale
            if turn == 1:
                scores = jnp.where(mask_in[...] > 0.0, scores, MASKED)
            grown = jnp.exp(scores - jnp.max(scores, axis=-1, keepdims=True))
            soft = grown / jnp.sum(grown, axis=-1, keepdims=True)
            back = mm_cols(do, v)
            short = soft * (back - jnp.sum(soft * back, axis=-1, keepdims=True))
            dqkv[0, :, here] = (mm(short.astype(BF), k) * scale).astype(BF)
            dqkv[1, :, here] = (mm(short.T.astype(BF), q) * scale).astype(BF)
            dqkv[2, :, here] = mm(soft.T.astype(BF), do).astype(BF)
            return carry

        lax.fori_loop(0, width // HD, head, 0)
        if turn == 0:
            for copy in act_copies(1):
                copy.start(priority=LOCAL)
        for which in range(3):
            kin_right(False, 4 * turn + 1 + which, 0).start()

    def attend_end(turn):
        base = 8 * turn + 5
        for which in range(3):
            slot = opened(base + which)

            def tile(there, _):
                value = mm_cols(dqkv[which], slots[slot, there, :])
                if which == 0:
                    rows_sum[0:rows, there] = value
                elif which == 1:
                    rows_sum[rows : 2 * rows, there] = value
                else:
                    rows_sum[rows : 2 * rows, there] += value

            tiles(2, tile, 512)
            closed(base + which)
        row_copy(2 * turn + 1).wait()
        gain_q = gains[2:3, :] if turn == 0 else gains[0:1, :]
        gain_kv = gains[2:3, :] if turn == 0 else gains[1:2, :]

        def body(here):
            unit, inverse = unit_rows(ub[here, :].astype(F32))
            dx, gain_part = lean(rows_sum[here, :], unit, inverse, gain_q)
            if turn == 1:
                unit, inverse = unit_rows(src_in[here, :].astype(F32))
            there = pl.ds(pl.multiple_of(rows + here.start, 32), 32)
            ds, kv_part = lean(rows_sum[there, :], unit, inverse, gain_kv)
            fresh = grad[here, :].astype(F32) + dx
            if turn == 0:
                fresh += ds
            else:
                high = ds.astype(BF)
                part_out[0, here, :] = high
                part_out[1, here, :] = (ds - high.astype(F32)).astype(BF)
            grad[here, :] = fresh.astype(BF)
            return gain_part, kv_part

        if turn == 1:
            for which in range(2):
                part_over(which).wait_send()
            for copy in kin_lefts(True, 2):
                copy.wait_send()
        gain_grad, kv_grad = row_steps(body, 2)
        if turn == 0:
            row_copy(2).start(priority=LOCAL)
            small_row(2, gain_grad + kv_grad)
            open_pair(1)
        else:
            small_row(0, gain_grad)
            small_row(1, kv_grad)
            small_row(15, jnp.zeros_like(gain_grad))

            def tile(there, _):
                pair[:, there] = (
                    mm(picks_in[...], part_out[0, :, there])
                    + mm(picks_in[...], part_out[1, :, there])
                ).astype(BF)

            tiles(4, tile)
            small_copy(0).start()
            for which in range(3):
                point_copy(which).start()
            lat_start(1)

    def point_total():
        for which in range(3):
            point_copy(which).wait_recv()
        gathered = pair[
            pl.ds(pl.multiple_of(section_at * quarter_rows, 128), quarter_rows)
        ].astype(F32)
        for which in range(3):
            gathered += point_in[which].astype(F32)
        point_sum[...] = gathered.astype(BF)
        point_local().start(priority=LOCAL)
        for which in range(3):
            point_deal(which).start()

    def small_step(phase):
        small_copy(phase).wait_recv()
        small_sum[phase + 1] = small_sum[phase] + small_in[phase]
        if phase < 2:
            small_copy(phase + 1).start()
        else:
            for step in range(3):
                small_copy(3 + step).start()

    def small_end():
        for step in range(3):
            small_copy(3 + step).wait_recv()
        small_out[...] = (small_sum[3] + small_in[4]) + (small_in[3] + small_in[5])

    def rows_end():
        lat_onward(1)
        point_total()

    begin = pltpu.make_async_copy(top_in, grad, act_sems.at[4])
    begin.start()
    for index in range(2):
        slot_copy(index).start(priority=LOCAL)
    h_copy(0).start(priority=LOCAL)
    row_copy(0).start(priority=LOCAL)
    for copy in act_copies(0):
        copy.start(priority=LOCAL)
    begin.wait()
    open_pair(0)
    for part in range(2):
        kin_right(True, 0, part).start()
    pair_ready(0)
    for copy in kin_lefts(True, 1):
        copy.start()
    for job in range(4):
        for copy in kin_lefts(False, job):
            copy.start()
    for part in range(2):
        kin_right(True, 2, part).start()
    for copy in kin_lefts(True, 3):
        copy.start()
    for job in range(4, 8):
        for copy in kin_lefts(False, job):
            copy.start()
    raw_start(0)
    load(0)
    chain = {
        0: [functools.partial(feed_chunk, 0, 0), functools.partial(lat_start, 0)],
        1: [functools.partial(feed_chunk, 0, 1)],
        2: [functools.partial(feed_end, 0), functools.partial(lat_onward, 0)],
        3: [functools.partial(attend_heads, 0)],
        4: [functools.partial(attend_end, 0)],
        5: [functools.partial(pair_ready, 1), functools.partial(feed_chunk, 1, 0)],
        6: [functools.partial(feed_chunk, 1, 1)],
        7: [functools.partial(feed_end, 1)],
        8: [functools.partial(attend_heads, 1)],
        9: [functools.partial(attend_end, 1)],
        11: [functools.partial(small_step, 0), rows_end],
        13: [functools.partial(small_step, 1)],
        15: [functools.partial(small_step, 2)],
        17: [small_end],
    }

    def moment_body(moment, carry):
        @pl.when(moment < total)
        def _():
            by_kind(moment, functools.partial(offer, lax.rem(moment, WINDOWS)))

        ready = jnp.logical_and(moment >= 2, moment < total + 2)

        @pl.when(jnp.logical_and(ready, jnp.logical_not(is_feed(moment - 2))))
        def _():
            take(lax.rem(moment - 2, WINDOWS), count_below(moment - 2, ATTENDS), False)

        for lag, action in ((3, second_of), (4, third_of), (5, close_of), (6, finish_of)):

            @pl.when(jnp.logical_and(moment >= lag, moment < total + lag))
            def _():
                by_kind(moment - lag, action)
        for when, actions in chain.items():

            @pl.when(moment == when)
            def _():
                for action in actions:
                    action()

        for item in range(1, total):
            pl.when(moment == item - 1)(functools.partial(load, item))
        return carry

    lax.fori_loop(0, total + 6, moment_body, 0)

    for index in range(4):
        if index % 2 == 1:
            for copy in kin_lefts(True, index):
                copy.wait_send()
        if index != 1:
            for chunk in range(2):
                kin_right(True, index, chunk).wait_send()
    for index in range(8):
        for copy in kin_lefts(False, index):
            copy.wait_send()
        if index not in (1, 2, 3):
            kin_right(False, index, 0).wait_send()
    for phase in range(6):
        small_copy(phase).wait_send()
    for which in range(2):
        lat_local(which).wait()
        for way in range(2):
            lat_copy(which, way).wait_send()
            lat_far(which, way).wait()
    point_local().wait()
    for which in range(3):
        point_copy(which).wait_send()
        point_deal(which).wait()

    def drain(order, carry):
        @pl.when(order >= 4)
        def _():
            drained(order, True)

        drained(order, False)
        return carry

    for order in (5, 6, 7):
        xy_sent(order)
    lax.fori_loop(0, 8, drain, 0)


def reduce_all(full, kept, latents, gains, mask, picks):
    total = ITEM_COUNT
    rows, width = kept[0].shape
    points = picks.shape[0]
    anywhere = pl.BlockSpec(memory_space=pl.ANY)
    vmem = pl.BlockSpec(memory_space=pltpu.VMEM)
    u1, u2, u3, u4, top = kept[:5]
    operands = [*full, u1, u2, u3, u4, top, *kept[5:16], *kept[17:], latents, kept[16]]
    operands += [gains, mask, picks]
    spaces = [anywhere] * (len(operands) - 4) + [vmem] * 4
    dma = pltpu.SemaphoreType.DMA
    flops = 2 * width * width * 24 * rows * 2
    return pl.pallas_call(
        reduce_kernel,
        out_shape=[
            jax.ShapeDtypeStruct((2, 128, 4 * width), BF),
            jax.ShapeDtypeStruct((2, 128, 4 * width), BF),
            jax.ShapeDtypeStruct((3, 128, width), BF),
            jax.ShapeDtypeStruct((3, 128, width), BF),
            jax.ShapeDtypeStruct((1, 128, width), BF),
            jax.ShapeDtypeStruct((1, 128, width), BF),
            jax.ShapeDtypeStruct((4 * rows, width), BF),
            jax.ShapeDtypeStruct((4 * rows, width), BF),
            jax.ShapeDtypeStruct((points, width), BF),
            jax.ShapeDtypeStruct((16, width), F32),
            jax.ShapeDtypeStruct((2, rows, width), BF),
            jax.ShapeDtypeStruct((4, 4, 2 * rows, 128), BF),
            jax.ShapeDtypeStruct((8, 4, rows, 128), BF),
            jax.ShapeDtypeStruct((4, 2 * rows, 2 * width), BF),
            jax.ShapeDtypeStruct((8, rows, width), BF),
        ],
        in_specs=spaces,
        out_specs=[anywhere] * 9 + [vmem] + [anywhere] * 5,
        scratch_shapes=[
            pltpu.VMEM((4, 4, 128, 1024), BF),
            pltpu.VMEM((8, 4, 128, 512), BF),
            pltpu.VMEM((4, 2, 512, 128), BF),
            pltpu.VMEM((WINDOWS, 1024, 1024), BF),
            pltpu.VMEM((STAGES, 4, 128, 512), BF),
            pltpu.VMEM((4, 4, 128, 1024), BF),
            pltpu.VMEM((8, 4, 128, 512), BF),
            pltpu.VMEM((6, 5, 128, 1024), BF),
            pltpu.VMEM((4, 5, 128, 512), BF),
            pltpu.VMEM((4, 128, 1024), BF),
            pltpu.VMEM((8, 128, 512), BF),
            pltpu.VMEM((4, 128, 1024), BF),
            pltpu.VMEM((8, 128, 512), BF),
            pltpu.VMEM((512, 1024), BF),
            pltpu.VMEM((512, 2048), BF),
            pltpu.VMEM((512, 1024), F32),
            pltpu.VMEM((512, 1024), F32),
            pltpu.VMEM((2, 1024, 1024), BF),
            pltpu.VMEM((256, 1024), BF),
            pltpu.VMEM((256, 1024), BF),
            pltpu.VMEM((256, 1024), BF),
            pltpu.VMEM((256, 1024), BF),
            pltpu.VMEM((3, 256, 1024), BF),
            pltpu.VMEM((2, 256, 1024), BF),
            pltpu.VMEM((2, 256, 1024), BF),
            pltpu.VMEM((256, 1024), BF),
            pltpu.VMEM((256, 1024), BF),
            pltpu.VMEM((3, points // 4, width), BF),
            pltpu.VMEM((points // 4, width), BF),
            pltpu.VMEM((6, 16, width), F32),
            pltpu.VMEM((4, 16, width), F32),
            dma((2, 12, 4)),
            dma((2, 16)),
            dma((4, 2)),
            dma((WINDOWS, 2)),
            dma((2, 8, 2)),
            dma((total, 4)),
            dma((total, 5)),
            dma((2, total, 2)),
            dma((2, total, 2)),
            dma((total, 2)),
            dma((2, 2, 2)),
            dma((2, 2, 2)),
            dma((2,)),
            dma((2, 3)),
            dma((2, 3)),
            dma((1,)),
            dma((2, 6)),
            dma((2, 2, 2)),
            dma((2,)),
            dma((1,)),
            dma((1,)),
            dma((5,)),
        ],
        compiler_params=pltpu.CompilerParams(
            collective_id=2, has_side_effects=True, vmem_limit_bytes=62 * 2**20
        ),
        cost_estimate=pl.CostEstimate(
            flops=flops, bytes_accessed=2**27, transcendentals=2**21
        ),
    )(*operands)[:10]


def plain_layers(full, spread, mine, source, valid, cot_own, picks, groups_all):
    proj_c, out_c, in_0, down_0, proj_s, out_s, in_1, down_1 = full
    width, hidden = in_0.shape

    def vector(first, count):
        return spread[:, first : first + count].reshape(-1)

    gains_cross = (vector(0, 1), vector(1, 1))
    gain_self = vector(2, 1)
    gains_mlp = (vector(3, 1), vector(4, 1))
    biases_out = (vector(5, 1), vector(6, 1))
    per_bias = hidden // width
    biases_in = (vector(7, per_bias), vector(7 + per_bias, per_bias))
    cot = cot_own.astype(F32)
    u1, kept_c = attend(mine, source, valid, gains_cross[0], gains_cross[1], proj_c, out_c)
    u2, kept_0 = feed(u1.astype(F32), gains_mlp[0], in_0, biases_in[0], down_0, biases_out[0])
    u2 = u2.astype(F32)
    u3, kept_s = attend(u2, u2, None, gain_self, gain_self, proj_s, out_s)
    u4, kept_1 = feed(u3.astype(F32), gains_mlp[1], in_1, biases_in[1], down_1, biases_out[1])
    final = u4.astype(F32)
    group_norm = jnp.sqrt(jnp.mean(final * final) + EPSILON)
    norm_mean = lax.psum(group_norm, ALL) / groups_all
    g4 = (cot + (norm_mean / group_norm) * final).astype(BF)

    dx, gain_1_grad, bias_1_grad, ob_1_grad, pairs_1 = feed_back(
        g4, kept_1, gains_mlp[1], in_1, down_1
    )
    g3 = (g4.astype(F32) + dx).astype(BF)
    dx, ds, gq, gkv, pairs_s = attend_back(g3, kept_s, gain_self, gain_self, proj_s, out_s)
    gain_s_grad = gq + gkv
    g2 = (g3.astype(F32) + dx + ds).astype(BF)
    dx, gain_0_grad, bias_0_grad, ob_0_grad, pairs_0 = feed_back(
        g2, kept_0, gains_mlp[0], in_0, down_0
    )
    g1 = (g2.astype(F32) + dx).astype(BF)
    dx, ds, cq_grad, ckv_grad, pairs_c = attend_back(
        g1, kept_c, gains_cross[0], gains_cross[1], proj_c, out_c
    )
    g0 = (g1.astype(F32) + dx).astype(BF)
    high = ds.astype(BF)
    low = (ds - high.astype(F32)).astype(BF)
    point_part = (mm_rows(picks, high) + mm_rows(picks, low)).astype(BF)
    small = jnp.concatenate(
        [
            cq_grad,
            ckv_grad,
            gain_s_grad,
            gain_0_grad,
            gain_1_grad,
            ob_0_grad,
            ob_1_grad,
            bias_0_grad,
            bias_1_grad,
            jnp.zeros_like(cq_grad),
        ]
    ).reshape(-1, width)
    pairs = pairs_1 + pairs_s + pairs_0 + pairs_c
    lefts, rights = [pair[0] for pair in pairs], [pair[1] for pair in pairs]
    def settled_grad(left, right):
        part = lax.psum_scatter(
            mm_rows(left, right).astype(BF), ALL, scatter_dimension=0, tiled=True
        )
        return lax.all_gather(part, "section", axis=0, tiled=True).astype(F32)

    done = [settled_grad(left, right) for left, right in pairs]
    mlp_in_grad = jnp.stack([done[6], done[0]])
    mlp_down_grad = jnp.stack([done[7], done[1]])
    proj_s_grad = jnp.concatenate(done[2:5], axis=1)
    proj_c_grad = jnp.concatenate(done[8:11], axis=1)
    out_s_grad, out_c_grad = done[5], done[11]
    points_sum = lax.psum(point_part, "section")
    latents_out = lax.all_gather(u4, "section", axis=0, tiled=True)
    g0_all = lax.all_gather(g0, "section", axis=0, tiled=True)
    small = lax.psum(small, ALL)
    return (
        norm_mean,
        latents_out,
        g0_all,
        points_sum,
        small,
        mlp_in_grad,
        mlp_down_grad,
        proj_c_grad,
        proj_s_grad,
        out_c_grad,
        out_s_grad,
    )


def per_device(
    latents,
    points,
    neighbours,
    lengths,
    cross_proj,
    cross_out,
    cross_gains,
    self_proj,
    self_out,
    self_gain,
    mlp_gain,
    mlp_in,
    mlp_in_bias,
    mlp_down,
    mlp_out_bias,
    cotangent,
):
    sections = lax.axis_size("section")
    section_at = lax.axis_index("section")
    width = latents.shape[1]
    hidden = mlp_in.shape[2]
    groups_dev = neighbours.shape[0]
    rows = latents.shape[0] // sections
    shard = cross_out.shape[0]
    piece = shard // sections
    groups_all = groups_dev * lax.axis_size("batch")

    def gathered(block):
        own = lax.dynamic_slice_in_dim(block, section_at * piece, piece, 0)
        return lax.all_gather(own, ALL, axis=0, tiled=True)

    projs = (cross_proj.reshape(shard, 3 * width), self_proj.reshape(shard, 3 * width))
    if lax.axis_size("batch") == 8:
        made = gather_forward(
            [projs[0], cross_out, mlp_in, mlp_down, projs[1], self_out],
            latents,
            cotangent,
            points,
            neighbours,
            lengths[:, None],
            [cross_gains, self_gain[None, :], mlp_gain, mlp_out_bias, mlp_in_bias],
        )
        full, gain_rows, norm_tile, mask, picks = made[:8], *made[8:12]
        norm_mean = norm_tile[0, 0]
        (
            mlp_in_grad,
            mlp_down_grad,
            proj_c_grad,
            proj_s_grad,
            out_c_grad,
            out_s_grad,
            latents_out,
            g0_all,
            points_sum,
            small,
        ) = reduce_all(full, made[12:], latents, gain_rows, mask, picks)
        mlp_in_grad = mlp_in_grad.astype(F32)
        mlp_down_grad = mlp_down_grad.astype(F32)
        proj_c_grad = jnp.swapaxes(proj_c_grad, 0, 1).astype(F32)
        proj_s_grad = jnp.swapaxes(proj_s_grad, 0, 1).astype(F32)
        out_c_grad, out_s_grad = out_c_grad[0].astype(F32), out_s_grad[0].astype(F32)
    else:
        vectors = jnp.concatenate(
            [
                cross_gains.reshape(-1),
                self_gain,
                mlp_gain.reshape(-1),
                mlp_out_bias.reshape(-1),
                mlp_in_bias.reshape(-1),
                jnp.zeros_like(self_gain),
            ]
        ).reshape(-1, shard)
        cot_own = lax.dynamic_slice_in_dim(cotangent, section_at * rows, rows, 0)
        mine = lax.dynamic_slice_in_dim(latents, section_at * rows, rows, 0).astype(F32)
        listed = lax.dynamic_index_in_dim(neighbours, section_at, 0, keepdims=False)
        length = lax.dynamic_index_in_dim(lengths, section_at, 0, keepdims=False)
        valid = jnp.arange(listed.shape[0], dtype=jnp.int32) < length
        picks = listed[:, None] == jnp.arange(points.shape[0], dtype=jnp.int32)[None, :]
        picks = picks.astype(BF)
        source = mm(picks, points)
        blocks = [projs[0], cross_out, mlp_in[0], mlp_down[0]]
        blocks += [projs[1], self_out, mlp_in[1], mlp_down[1]]
        full = [gathered(block) for block in blocks]
        spread = lax.all_gather(vectors, "batch", axis=0, tiled=False)
        (
            norm_mean,
            latents_out,
            g0_all,
            points_sum,
            small,
            mlp_in_grad,
            mlp_down_grad,
            proj_c_grad,
            proj_s_grad,
            out_c_grad,
            out_s_grad,
        ) = plain_layers(full, spread.astype(F32), mine, source, valid, cot_own, picks, groups_all)
    points_grad = points_sum.astype(F32)
    latents_grad = g0_all.astype(F32)
    per_bias = hidden // width
    batch_at = lax.axis_index("batch")

    def own(first, count):
        flat = small[first : first + count].reshape(-1)
        size = flat.shape[0] // lax.axis_size("batch")
        return lax.dynamic_slice_in_dim(flat, batch_at * size, size, 0)

    return (
        latents_out,
        latents_grad,
        points_grad,
        proj_c_grad.reshape(shard, 3, width),
        out_c_grad,
        jnp.stack([own(0, 1), own(1, 1)]),
        proj_s_grad.reshape(shard, 3, width),
        out_s_grad,
        own(2, 1),
        jnp.stack([own(3, 1), own(4, 1)]),
        mlp_in_grad,
        jnp.stack([own(7, per_bias), own(7 + per_bias, per_bias)]),
        mlp_down_grad,
        jnp.stack([own(5, 1), own(6, 1)]),
        norm_mean,
    )


def solution(mesh):
    rows = P("batch", None)
    cols = P(None, "batch")
    block = P("batch", None, None)
    pair = P(None, "batch", None)
    return jax.shard_map(
        per_device,
        mesh=mesh,
        in_specs=(
            rows,
            rows,
            rows,
            P("batch"),
            block,
            rows,
            cols,
            block,
            rows,
            P("batch"),
            cols,
            pair,
            cols,
            pair,
            cols,
            rows,
        ),
        out_specs=(
            rows,
            rows,
            rows,
            block,
            rows,
            cols,
            block,
            rows,
            P("batch"),
            cols,
            pair,
            cols,
            pair,
            cols,
            P(),
        ),
        check_vma=False,
    )
```

```python
import functools
import math

import jax
import jax.numpy as jnp
from jax import lax
from jax.experimental import pallas as pl
from jax.experimental.pallas import tpu as pltpu
from jax.sharding import PartitionSpec as P

HD = 128
EPSILON = 1e-05
MASKED = -1e30
BF = jnp.bfloat16
F32 = jnp.float32
ALL = ("batch", "section")
MESH = pl.DeviceIdType.MESH
GATHER_WIDTH = 1024
AHEAD = 4
LOCAL = 1
SLOTS = 3
GATHERED = tuple(
    (4 * layer + index, start)
    for layer in range(2)
    for index, start in (
        [(0, 0), (0, 1024), (0, 2048), (1, 0)]
        + [(2 + which, chunk) for chunk in range(0, 2048, 1024) for which in range(2)]
    )
)


def mm(a, b):
    return jnp.dot(a, b, preferred_element_type=F32)


def mm_rows(a, b):
    return lax.dot_general(a, b, (((0,), (0,)), ((), ())), preferred_element_type=F32)


def mm_cols(a, b):
    return lax.dot_general(a, b, (((1,), (1,)), ((), ())), preferred_element_type=F32)


def unit_rows(values):
    centred = values - jnp.mean(values, axis=-1, keepdims=True)
    inverse = lax.rsqrt(jnp.mean(centred * centred, axis=-1, keepdims=True) + EPSILON)
    return centred * inverse, inverse


def norm_back(gradient, unit, inverse, gain):
    scaled = gradient * gain
    inner = (
        scaled
        - jnp.mean(scaled, axis=-1, keepdims=True)
        - unit * jnp.mean(scaled * unit, axis=-1, keepdims=True)
    )
    return inverse * inner, jnp.sum(gradient * unit, axis=0)


def heads_of(rows):
    return rows.reshape(rows.shape[0], -1, HD)


def softmax(q, k, valid):
    scores = jnp.einsum(
        "lhc,nhc->hln", heads_of(q), heads_of(k), preferred_element_type=F32
    ) * (1.0 / math.sqrt(HD))
    if valid is not None:
        scores = jnp.where(valid[None, None, :], scores, MASKED)
    grown = jnp.exp(scores - jnp.max(scores, axis=-1, keepdims=True))
    return grown / jnp.sum(grown, axis=-1, keepdims=True)


def attend(inputs, source, valid, gain_q, gain_kv, proj, out):
    unit_x, inv_x = unit_rows(inputs)
    queries_in = (unit_x * gain_q).astype(BF)
    unit_s, inv_s = unit_rows(source)
    keys_in = (unit_s * gain_kv).astype(BF)
    width = inputs.shape[1]
    q = mm(queries_in, proj[:, :width]).astype(BF)
    kv = mm(keys_in, proj[:, width:]).astype(BF)
    k, v = kv[:, :width], kv[:, width:]
    soft = softmax(q, k, valid)
    mixture = jnp.einsum("hln,nhc->lhc", soft.astype(BF), heads_of(v), preferred_element_type=F32)
    mixture = mixture.reshape(inputs.shape).astype(BF)
    result = (inputs + mm(mixture, out)).astype(BF)
    return result, (unit_x, inv_x, queries_in, unit_s, inv_s, keys_in, q, k, v, soft, mixture)


def attend_back(gradient, kept, gain_q, gain_kv, proj, out):
    unit_x, inv_x, queries_in, unit_s, inv_s, keys_in, q, k, v, soft, mixture = kept
    width = gradient.shape[1]
    scale = 1.0 / math.sqrt(HD)
    grad_mix = mm_cols(gradient, out).astype(BF)
    grad_soft = jnp.einsum(
        "lhc,nhc->hln", heads_of(grad_mix), heads_of(v), preferred_element_type=F32
    )
    inner = jnp.sum(soft * grad_soft, axis=-1, keepdims=True)
    grad_scores = (soft * (grad_soft - inner)).astype(BF)
    dq = jnp.einsum("hln,nhc->lhc", grad_scores, heads_of(k), preferred_element_type=F32) * scale
    dk = jnp.einsum("hln,lhc->nhc", grad_scores, heads_of(q), preferred_element_type=F32) * scale
    dv = jnp.einsum(
        "hln,lhc->nhc", soft.astype(BF), heads_of(grad_mix), preferred_element_type=F32
    )
    dq = dq.reshape(gradient.shape).astype(BF)
    dk = dk.reshape(-1, width).astype(BF)
    dv = dv.reshape(-1, width).astype(BF)
    grad_x, gain_q_grad = norm_back(mm_cols(dq, proj[:, :width]), unit_x, inv_x, gain_q)
    back_s = mm_cols(dk, proj[:, width : 2 * width]) + mm_cols(dv, proj[:, 2 * width :])
    grad_s, gain_kv_grad = norm_back(back_s, unit_s, inv_s, gain_kv)
    pairs = ((queries_in, dq), (keys_in, dk), (keys_in, dv), (mixture, gradient))
    return grad_x, grad_s, gain_q_grad, gain_kv_grad, pairs


def feed(inputs, gain, w_in, b_in, w_down, b_out):
    unit, inverse = unit_rows(inputs)
    lowered = (unit * gain).astype(BF)
    pre_act = mm(lowered, w_in) + b_in
    active = jax.nn.gelu(pre_act).astype(BF)
    result = (inputs + mm_cols(active, w_down) + b_out).astype(BF)
    return result, (unit, inverse, lowered, pre_act, active)


def feed_back(gradient, kept, gain, w_in, w_down):
    unit, inverse, lowered, pre_act, active = kept
    grad_act = mm(gradient, w_down)
    grad_pre = jax.vjp(jax.nn.gelu, pre_act)[1](grad_act)[0].astype(BF)
    grad_x, gain_grad = norm_back(mm_cols(grad_pre, w_in), unit, inverse, gain)
    bias_grad = jnp.sum(grad_pre.astype(F32), axis=0)
    out_grad = jnp.sum(gradient.astype(F32), axis=0)
    return grad_x, gain_grad, bias_grad, out_grad, ((lowered, grad_pre), (gradient, active))


def gelu_both(value):
    factor = math.sqrt(2.0 / math.pi)
    square = value * value
    bent = jnp.tanh(factor * value * (1.0 + 0.044715 * square))
    inner = factor * (1.0 + 3.0 * 0.044715 * square)
    half = 0.5 * (1.0 + bent)
    return value * half, half + 0.5 * value * (1.0 - bent * bent) * inner


def tiles(count, body, size=256):
    def step(index, carry):
        body(pl.ds(pl.multiple_of(index * size, size), size), index)
        return carry

    lax.fori_loop(0, count, step, 0)


def norm_into(source, gain, target):
    def step(index, carry):
        here = pl.ds(pl.multiple_of(index * 32, 32), 32)
        unit, _ = unit_rows(source[here, :].astype(F32))
        target[here, :] = (unit * gain).astype(BF)
        return carry

    lax.fori_loop(0, source.shape[0] // 32, step, 0)


def gather_kernel(*refs):
    cross_proj, cross_out, mlp_in, mlp_down, self_proj, self_out = refs[:6]
    latents_in, cot_all, points_in, near_in, length_in = refs[6:11]
    vec_parts = refs[11:16]
    section_at = lax.axis_index("section")
    batch_at = lax.axis_index("batch")
    x_at = lax.rem(section_at, 2)
    y_at = section_at // 2
    ins = (
        cross_proj,
        cross_out,
        mlp_in.at[0],
        mlp_down.at[0],
        self_proj,
        self_out,
        mlp_in.at[1],
        mlp_down.at[1],
    )
    count = len(ins)
    outs = refs[16 : 16 + count]
    rest = refs[16 + count :]
    gains, norm_out, mask_in, picks_out = rest[:4]
    kept_outs = rest[4:24]
    (
        u1,
        u2,
        u3,
        u4,
        grad_top,
        xq_c,
        sn_c,
        q_c,
        k_c,
        v_c,
        o_c,
        xn_s,
        q_s,
        k_s,
        v_s,
        o_s,
        src_in,
        lowered,
        before,
        active,
        x_in,
        cot_in,
        vec_in,
        vec_rows,
        slots,
        total_rows,
        part_out,
        part_in,
        vec_out,
        biases,
        plane,
        line_in,
    ) = rest[24:56]
    (own_sem, send, recv, kin_send, kin_recv, vec_sems) = rest[56:62]
    (slot_sems, kept_sems, plane_sems, line_sems, pair_sems, row_sems) = rest[62:]
    line = 4
    core = lax.rem(batch_at, 2)
    spot = batch_at // 2
    beside = section_at + 1 - 2 * x_at
    above = lax.rem(section_at + 2, 4)
    sibling = batch_at + 1 - 2 * core
    shard = ins[0].shape[0]
    place = section_at * 2 + core
    rows = x_in.shape[0]

    def down_line(step):
        return lax.rem(spot + step, line) * 2 + core

    def up_line(step):
        return lax.rem(spot + line - step, line) * 2 + core

    near_peers = []
    for turn in range(1, 8):
        other = lax.rem(place + turn, 8)
        near_peers.append((other // 2, spot * 2 + lax.rem(other, 2)))
    line_peers = [(section_at, down_line(step)) for step in range(1, line)]
    far_peers = [(section_at, down_line(step) + 1 - 2 * core) for step in range(1, line)]
    vec_peers = [(section_at, sibling)] + line_peers + far_peers
    peers = near_peers + line_peers + far_peers
    barrier = pltpu.get_barrier_semaphore()
    for peer in peers:
        pl.semaphore_signal(barrier, inc=1, device_id=peer, device_id_type=MESH)
    pl.semaphore_wait(barrier, len(peers))

    def spread(ref, owner, first, size):
        return ref.at[pl.ds(pl.multiple_of(owner * shard, shard), shard), pl.ds(first, size)]

    def is_feed(item):
        return item % 8 >= 4

    def source_of(item, first, size):
        index, start = GATHERED[item]
        if is_feed(item):
            half_at = (y_at, x_at)[item // 8]
            first = pl.multiple_of(first + half_at * outs[index].shape[1], 128)
        return ins[index].at[:, pl.ds(first, size)]

    def piece(item):
        start = GATHERED[item][1]
        if is_feed(item):
            return pl.multiple_of(start + (x_at, y_at)[item // 8] * 512, 128), 512
        return pl.multiple_of(start + section_at * 256, 128), 256

    def own_line(item, way):
        first, size = piece(item)
        return pltpu.make_async_remote_copy(
            source_of(item, first, size),
            spread(outs[GATHERED[item][0]], batch_at, first, size),
            send.at[5 * way, item, 0],
            recv.at[0, item, 3 if way else 1],
            device_id=(section_at, batch_at + (-2 if way else 2)),
            device_id_type=MESH,
        )

    def onward_line(item, step, way):
        first, size = piece(item)
        ref = spread(outs[GATHERED[item][0]], up_line(step), first, size)
        return pltpu.make_async_remote_copy(
            ref,
            ref,
            send.at[0, item, step],
            recv.at[0, item, step - 1 if way else step + 1],
            device_id=(section_at, batch_at + (-2 if way else 2)),
            device_id_type=MESH,
        )

    def came_line(item, step):
        first, size = piece(item)
        ref = spread(outs[GATHERED[item][0]], up_line(step), first, size)
        return pltpu.make_async_remote_copy(
            ref,
            ref,
            send.at[0, item, step],
            recv.at[0, item, step],
            device_id=(section_at, sibling),
            device_id_type=MESH,
        )

    def start_line(item):
        @pl.when(spot < 3)
        def _():
            own_line(item, 0).start()

        @pl.when(spot > 0)
        def _():
            own_line(item, 1).start()

    def arrive_line(item, apart):
        @pl.when(spot >= apart)
        def _():
            came_line(item, apart).wait_recv()

            @pl.when(spot < 3)
            def _():
                onward_line(item, apart, 0).start()

            for copy in near(item, apart):
                copy.start()

        @pl.when(spot + apart <= 3)
        def _():
            came_line(item, 4 - apart).wait_recv()

            @pl.when(spot > 0)
            def _():
                onward_line(item, 4 - apart, 1).start()

            for copy in near(item, 4 - apart):
                copy.start()

    def sent_line(item):
        @pl.when(spot < 3)
        def _():
            own_line(item, 0).wait_send()

        @pl.when(spot > 0)
        def _():
            own_line(item, 1).wait_send()

        for apart in (1, 2, 3):

            @pl.when(jnp.logical_and(spot >= apart, spot < 3))
            def _():
                onward_line(item, apart, 0).wait_send()

            @pl.when(jnp.logical_and(spot + apart <= 3, spot > 0))
            def _():
                onward_line(item, 4 - apart, 1).wait_send()

        for step in (1, 2, 3):
            for copy in near(item, step):
                copy.wait_send()

    def plane_copy(item, step, way, low, wide, peer):
        ref = spread(outs[GATHERED[item][0]], up_line(step), low, wide)
        return pltpu.make_async_remote_copy(
            ref,
            ref,
            send.at[way, item, step],
            recv.at[way, item, step],
            device_id=(peer, batch_at),
            device_id_type=MESH,
        )

    def near(item, step):
        first, size = piece(item)
        if is_feed(item):
            return [plane_copy(item, step, 1, first, size, (beside, above)[item // 8])]
        copies = [plane_copy(item, step, 1, first, size, beside)]
        if not is_feed(item):
            copies.append(plane_copy(item, step, 2, first, size, above))
        return copies

    def far(item, step):
        start = GATHERED[item][1]
        by_y = pl.multiple_of(start + beside * 256, 128)
        by_x = pl.multiple_of(start + above * 256 + 128, 128)
        return [
            plane_copy(item, step, 3, by_y, 128, above),
            plane_copy(item, step, 4, by_x, 128, beside),
        ]

    def kin(item, step):
        index, start = GATHERED[item]
        if step == 0:
            source = source_of(item, start, GATHER_WIDTH)
        else:
            source = spread(outs[index], up_line(step), start, GATHER_WIDTH)
        return pltpu.make_async_remote_copy(
            source,
            spread(outs[index], up_line(step), start, GATHER_WIDTH),
            kin_send.at[item, step],
            kin_recv.at[item, step],
            device_id=(section_at, sibling),
            device_id_type=MESH,
        )

    def own(item):
        index, start = GATHERED[item]
        return pltpu.make_async_copy(
            source_of(item, start, GATHER_WIDTH),
            spread(outs[index], batch_at, start, GATHER_WIDTH),
            own_sem.at[item],
        )

    def vec_copy(which):
        return pltpu.make_async_remote_copy(
            vec_in,
            vec_out.at[batch_at],
            vec_sems.at[0, which],
            vec_sems.at[1, which],
            device_id=vec_peers[which],
            device_id_type=MESH,
        )

    def slot_copy(item):
        index, start = GATHERED[item]
        return pltpu.make_async_copy(
            outs[index].at[:, pl.ds(start, GATHER_WIDTH)],
            slots.at[item % SLOTS],
            slot_sems.at[item % SLOTS],
        )

    def near_norm(turn):
        return pltpu.make_async_remote_copy(
            plane.at[8],
            plane.at[place],
            plane_sems.at[0, turn],
            plane_sems.at[1, turn],
            device_id=near_peers[turn],
            device_id_type=MESH,
        )

    def far_norm(step):
        return pltpu.make_async_remote_copy(
            line_in.at[4],
            line_in.at[spot],
            line_sems.at[0, step],
            line_sems.at[1, step],
            device_id=line_peers[step],
            device_id_type=MESH,
        )

    def rows_over(layer):
        return pltpu.make_async_remote_copy(
            lowered.at[layer, pl.ds(0, rows)],
            lowered.at[layer, pl.ds(rows, rows)],
            pair_sems.at[0, layer, 0],
            pair_sems.at[1, layer, 0],
            device_id=((above, beside)[layer], batch_at),
            device_id_type=MESH,
        )

    def part_over(layer):
        return pltpu.make_async_remote_copy(
            part_out.at[layer],
            part_in.at[layer],
            pair_sems.at[0, layer, 1],
            pair_sems.at[1, layer, 1],
            device_id=((above, beside)[layer], batch_at),
            device_id_type=MESH,
        )

    steps = range(1, line)
    total = len(GATHERED)
    started = []

    def launch(copies):
        for copy in copies:
            copy.start()
        started.extend(copies)

    kept = (
        (u1, u2, u3, u4, grad_top)
        + (xq_c, sn_c, q_c, k_c, v_c, o_c)
        + (xn_s, q_s, k_s, v_s, o_s)
        + (src_in, lowered, before, active)
    )
    names = {id(ref): place for place, ref in enumerate(kept)}

    def keep(*chosen):
        for ref in chosen:
            index = names[id(ref)]
            pltpu.make_async_copy(ref, kept_outs[index], kept_sems.at[index]).start(priority=LOCAL)

    def row(index):
        return gains[index : index + 1, :]

    def project(source, target, slot):
        def tile(columns, _):
            target[:, columns] = mm(source[...], slots[slot, :, columns]).astype(BF)

        tiles(2, tile, 512)

    def heads(q, k, v, o, masked):
        def head(index, carry):
            here = pl.ds(pl.multiple_of(index * HD, HD), HD)
            scores = mm_cols(q[:, here], k[:, here]) * (1.0 / math.sqrt(HD))
            if masked:
                scores = jnp.where(mask_in[...] > 0.0, scores, MASKED)
            grown = jnp.exp(scores - jnp.max(scores, axis=-1, keepdims=True))
            soft = grown / jnp.sum(grown, axis=-1, keepdims=True)
            o[:, here] = mm(soft.astype(BF), v[:, here]).astype(BF)
            return carry

        lax.fori_loop(0, q.shape[1] // HD, head, 0)

    def close_attention(inputs, o, target, slot):
        def tile(columns, _):
            target[:, columns] = (
                inputs[:, columns].astype(F32) + mm(o[...], slots[slot, :, columns])
            ).astype(BF)

        tiles(2, tile, 512)

    def feed_up(layer, chunk, slot):
        def tile(columns, index):
            first = chunk * GATHER_WIDTH + index * 512
            there = pl.ds(pl.multiple_of(first, 512), 512)
            lanes = pl.ds(pl.multiple_of((y_at, x_at)[layer] * 2048 + first, 512), 512)
            value = mm(lowered[layer], slots[slot, :, columns]) + biases[layer : layer + 1, lanes]
            active_part, slope = gelu_both(value)
            before[layer, :, there] = slope
            active[layer, :, there] = active_part.astype(BF)

        tiles(2, tile, 512)

    def feed_down(layer, chunk, slot):
        chosen = pl.ds(chunk * GATHER_WIDTH, GATHER_WIDTH)

        def tile(columns, _):
            value = mm_cols(active[layer, :, chosen], slots[slot, columns, :])
            if chunk == 0:
                total_rows[:, columns] = value
            else:
                value = total_rows[:, columns] + value
                total_rows[:, columns] = value
                part_out[layer, :, columns] = value[rows:].astype(BF)

        tiles(2, tile, 512)

    def feed_close(layer):
        inputs, target = (u1, u3)[layer], (u2, u4)[layer]
        part_over(layer).wait_recv()

        def tile(columns, _):
            target[:, columns] = (
                inputs[:, columns].astype(F32)
                + (total_rows[0:rows, columns] + part_in[layer, :, columns].astype(F32))
                + gains[5 + layer : 6 + layer, columns]
            ).astype(BF)

        tiles(2, tile, 512)
        keep(target)

    def work(item):
        slot_copy(item).wait()
        slot = item % SLOTS
        layer, stage = item // 8, item % 8
        inputs = (x_in, u2)[layer]
        middle = (u1, u3)[layer]
        q, k, v, o = ((q_c, k_c, v_c, o_c), (q_s, k_s, v_s, o_s))[layer]
        if stage == 0:
            if layer == 0:
                norm_into(x_in, row(0), xq_c)
                norm_into(src_in, row(1), sn_c)
                keep(xq_c, sn_c)
            else:
                feed_close(0)
                norm_into(u2, row(2), xn_s)
                keep(xn_s)
            project((xq_c, xn_s)[layer], q, slot)
        elif stage == 1:
            project((sn_c, xn_s)[layer], k, slot)
        elif stage == 2:
            project((sn_c, xn_s)[layer], v, slot)
            heads(q, k, v, o, layer == 0)
            keep(q, k, v, o)
        elif stage == 3:
            close_attention(inputs, o, middle, slot)
            norm_into(middle, row(3 + layer), lowered.at[layer, pl.ds(0, rows)])
            launch([rows_over(layer)])
            keep(middle)
        elif stage % 2 == 0:
            if stage == 4:
                rows_over(layer).wait_recv()
            feed_up(layer, (stage - 4) // 2, slot)
        else:
            feed_down(layer, (stage - 4) // 2, slot)
            if stage == 7:
                launch([part_over(layer)])

    for item in range(AHEAD):
        start_line(item)
    here = pl.ds(pl.multiple_of(section_at * rows, rows), rows)
    row_copies = [
        pltpu.make_async_copy(latents_in.at[here], x_in, row_sems.at[0]),
        pltpu.make_async_copy(cot_all.at[here], cot_in, row_sems.at[1]),
    ]
    for copy in row_copies:
        copy.start()
    cross_gain, self_gain, feed_gain, out_bias, in_bias = vec_parts
    vec_rows[...] = jnp.zeros_like(vec_rows)
    vec_rows[0:2, :] = cross_gain[...].astype(F32)
    vec_rows[2:3, :] = self_gain[...].astype(F32)
    vec_rows[3:5, :] = feed_gain[...].astype(F32)
    vec_rows[5:7, :] = out_bias[...].astype(F32)
    bias_rows = in_bias[...].astype(F32)
    for layer in range(2):
        for part_at in range(4):
            index = 7 + 4 * layer + part_at
            vec_rows[index : index + 1, :] = bias_rows[
                layer : layer + 1, part_at * 128 : part_at * 128 + 128
            ]
    vec_in[...] = vec_rows[...].astype(BF)
    vec_out[batch_at] = vec_in[...]
    for which in range(7):
        vec_copy(which).start()
    lanes = lax.broadcasted_iota(jnp.int32, (1, rows), 1)
    length = length_in[pl.ds(section_at, 1), :]
    mask_in[...] = jnp.where(lanes < length, 1.0, 0.0)
    point_at = lax.broadcasted_iota(jnp.int32, (points_in.shape[0], rows), 0)
    wanted = near_in[pl.ds(section_at, 1), :]
    picks = jnp.where(point_at == wanted, 1.0, 0.0)
    picks_out[...] = picks.astype(BF)
    turned = picks.T.astype(BF)

    def source_tile(columns, _):
        src_in[:, columns] = mm(turned, points_in[:, columns]).astype(BF)

    tiles(2, source_tile, 512)
    keep(src_in)
    for copy in row_copies:
        copy.wait()
    for moment in range(-2, total + 4):
        if moment + 2 + AHEAD < total:
            start_line(moment + 2 + AHEAD)
        for apart in (1, 2, 3):
            if 0 <= moment + 3 - apart < total:
                arrive_line(moment + 3 - apart, apart)
        if 0 <= moment < total:
            own(moment).start(priority=LOCAL)
            launch([kin(moment, 0)])
        if 0 <= moment - 1 < total:
            for step in steps:
                if is_feed(moment - 1):
                    near(moment - 1, step)[0].wait_recv()
                    launch([kin(moment - 1, step)])
                else:
                    for copy, onward in zip(near(moment - 1, step), far(moment - 1, step)):
                        copy.wait_recv()
                        launch([onward])
        if 0 <= moment - 2 < total and not is_feed(moment - 2):
            for step in steps:
                for copy in far(moment - 2, step):
                    copy.wait_recv()
                launch([kin(moment - 2, step)])
        if moment == 2:
            for which in range(7):
                vec_copy(which).wait()
            for owner in range(8):
                values = vec_out[owner].astype(F32)
                gains[:, owner * 128 : owner * 128 + 128] = values
                for layer in range(2):
                    for part_at in range(4):
                        first = owner * 512 + part_at * 128
                        index = 7 + 4 * layer + part_at
                        biases[layer : layer + 1, first : first + 128] = values[index : index + 1]
        if 0 <= moment - 4 < total:
            work(moment - 4)
        if 0 <= moment - 3 < total:
            own(moment - 3).wait()
            for step in range(line):
                kin(moment - 3, step).wait_recv()
            slot_copy(moment - 3).start(priority=LOCAL)
    keep(lowered, before, active)
    feed_close(1)

    def square(index, carry):
        here = pl.ds(pl.multiple_of(index * 32, 32), 32)
        values = u4[here, :].astype(F32)
        return carry + jnp.sum(values * values, axis=0, keepdims=True)

    squares = lax.fori_loop(0, u4.shape[0] // 32, square, jnp.zeros((1, u4.shape[1]), F32))
    mean = jnp.sum(squares, axis=1, keepdims=True) / (u4.shape[0] * u4.shape[1])
    group_norm = jnp.sqrt(mean + EPSILON)
    plane[8] = jnp.broadcast_to(group_norm, plane.shape[1:])
    for turn in range(7):
        near_norm(turn).start()
    plane[place] = plane[8]
    for turn in range(7):
        near_norm(turn).wait()
    line_in[4] = jnp.sum(plane[0:8], axis=0)
    for step in range(3):
        far_norm(step).start()
    line_in[spot] = line_in[4]
    for step in range(3):
        far_norm(step).wait()
    norm_mean = jnp.sum(line_in[0:4], axis=0) / 32.0
    norm_out[...] = norm_mean
    ratio = norm_mean[0:1, 0:1] / group_norm

    def top(index, carry):
        here = pl.ds(pl.multiple_of(index * 32, 32), 32)
        grad_top[here, :] = (
            cot_in[here, :].astype(F32) + ratio * u4[here, :].astype(F32)
        ).astype(BF)
        return carry

    lax.fori_loop(0, u4.shape[0] // 32, top, 0)
    keep(grad_top)
    for index, ref in enumerate(kept):
        pltpu.make_async_copy(ref, kept_outs[index], kept_sems.at[index]).wait()
    for item in range(total):
        sent_line(item)
    for copy in started:
        copy.wait_send()


def gather_forward(blocks, latents, cotangent, points, near, lengths, vectors):
    width = latents.shape[1]
    rows = near.shape[1]
    half = blocks[2].shape[2] // 2
    widths = (3 * width, width, half, half) * 2
    total = len(GATHERED)
    anywhere = pl.BlockSpec(memory_space=pl.ANY)
    vmem = pl.BlockSpec(memory_space=pltpu.VMEM)
    plain = ((rows, width), BF)
    kept = [plain] * 17 + [
        ((2, 2 * rows, width), BF),
        ((2, 2 * rows, half), F32),
        ((2, 2 * rows, half), BF),
    ]
    dma = pltpu.SemaphoreType.DMA
    return pl.pallas_call(
        gather_kernel,
        out_shape=[jax.ShapeDtypeStruct((width, size), BF) for size in widths]
        + [
            jax.ShapeDtypeStruct((16, width), F32),
            jax.ShapeDtypeStruct((8, 128), F32),
            jax.ShapeDtypeStruct((1, rows), F32),
            jax.ShapeDtypeStruct((points.shape[0], rows), BF),
        ]
        + [jax.ShapeDtypeStruct(*one) for one in kept],
        in_specs=[anywhere] * (len(blocks) + 2) + [vmem] * 8,
        out_specs=[anywhere] * len(widths) + [vmem] * 4 + [anywhere] * len(kept),
        scratch_shapes=[pltpu.VMEM(*one) for one in kept]
        + [
            pltpu.VMEM((rows, width), BF),
            pltpu.VMEM((rows, width), BF),
            pltpu.VMEM((16, 128), BF),
            pltpu.VMEM((16, 128), F32),
            pltpu.VMEM((SLOTS, width, GATHER_WIDTH), BF),
            pltpu.VMEM((2 * rows, width), F32),
            pltpu.VMEM((2, rows, width), BF),
            pltpu.VMEM((2, rows, width), BF),
            pltpu.VMEM((8, 16, 128), BF),
            pltpu.VMEM((2, 2 * half), F32),
            pltpu.VMEM((9, 8, 128), F32),
            pltpu.VMEM((5, 8, 128), F32),
            dma((total,)),
            dma((6, total, 4)),
            dma((5, total, 4)),
            dma((total, 4)),
            dma((total, 4)),
            dma((2, 7)),
            dma((SLOTS,)),
            dma((len(kept),)),
            dma((2, 7)),
            dma((2, 3)),
            dma((2, 2, 2)),
            dma((2,)),
        ],
        compiler_params=pltpu.CompilerParams(
            collective_id=1, has_side_effects=True, vmem_limit_bytes=56 * 2**20
        ),
        cost_estimate=pl.CostEstimate(
            flops=2 * rows * width * sum(widths), bytes_accessed=2**27, transcendentals=2**21
        ),
    )(*blocks, latents, cotangent, points, near, lengths, *vectors)


ITEM_COUNT = 16
FEEDS = (0, 1, 2, 4, 6, 9, 10, 13)
ATTENDS = (3, 5, 7, 8, 11, 12, 14, 15)
WINDOWS = 4
STAGES = 3


def reduce_kernel(*refs):
    total = ITEM_COUNT
    (
        proj_c,
        out_c,
        in_0,
        down_0,
        proj_s,
        out_s,
        in_1,
        down_1,
        u1_in,
        u2_in,
        u3_in,
        last_ref,
        top_in,
        xq_c,
        sn_c,
        q_c,
        k_c,
        v_c,
        o_c,
        xn_s,
        q_s,
        k_s,
        v_s,
        o_s,
        lowered,
        before,
        active,
        latents_in,
        src_in,
        gains,
        mask_in,
        picks_in,
    ) = refs[:32]
    (up_out, down_out, proj_out_c, proj_out_s, end_out_c, end_out_s) = refs[32:38]
    (last_out, first_out, point_out, small_out) = refs[38:42]
    (grads_h, kin_lf, kin_la, kin_rf, kin_ra) = refs[42:47]
    (
        lwin_f,
        lwin_a,
        raw,
        rwin,
        stage,
        merged_f,
        merged_a,
        passing_f,
        passing_a,
        lined_f,
        lined_a,
        crossed_f,
        crossed_a,
        pair,
        slope,
        rows_sum,
        hbuf,
        slots,
        qb,
        kb,
        vb,
        dob,
        dqkv,
        part_out,
        part_in,
        grad,
        ub,
        point_in,
        point_sum,
        small_in,
        small_sum,
    ) = refs[47:78]
    (
        kin_l_sems,
        kin_r_sems,
        raw_sems,
        win_sems,
        xy_sems,
        line_send,
        line_recv,
        cross_sems,
        out_sems,
        own_sems,
        lat_sems,
        far_sems,
        lat_own,
        point_sems,
        deal_sems,
        point_own,
        small_sems,
        pair_sems,
        slot_sems,
        h_sem,
        save_sems,
        act_sems,
        free_sem,
    ) = refs[78:]
    section_at = lax.axis_index("section")
    batch_at = lax.axis_index("batch")
    core = lax.rem(batch_at, 2)
    spot = batch_at // 2
    x_at = lax.rem(section_at, 2)
    y_at = section_at // 2
    beside = section_at + 1 - 2 * x_at
    above = lax.rem(section_at + 2, 4)
    across = lax.rem(beside + 2, 4)
    sibling = batch_at + 1 - 2 * core
    flat = (beside, above)
    bits = (x_at, y_at)
    rows, width = 256, 1024

    peers = [(beside, batch_at), (above, batch_at), (across, batch_at), (section_at, sibling)]
    peers += [(section_at, lax.rem(spot + step, 4) * 2 + core) for step in (1, 2, 3)]
    barrier = pltpu.get_barrier_semaphore()
    for peer in peers:
        pl.semaphore_signal(barrier, inc=1, device_id=peer, device_id_type=MESH)
    pl.semaphore_wait(barrier, len(peers))

    def remote(source, target, sems, where, peer):
        return pltpu.make_async_remote_copy(
            source,
            target,
            sems.at[(0, *where)],
            sems.at[(1, *where)],
            device_id=peer,
            device_id_type=MESH,
        )

    feed_left = (pair, lowered.at[1], pair, lowered.at[0])
    feed_right = (active.at[1], slope, active.at[0], slope)
    att_left = (o_s, xn_s, xn_s, xn_s, o_c, xq_c, sn_c, sn_c)
    att_right = tuple(
        ref
        for turn in range(2)
        for ref in (grads_h.at[turn], dqkv.at[0], dqkv.at[1], dqkv.at[2])
    )

    def columns(spot_of, parity):
        return pl.ds(pl.multiple_of((2 * spot_of + parity) * 128, 128), 128)

    def kin_lefts(feed, job):
        source, target = (feed_left, kin_lf) if feed else (att_left, kin_la)
        return [
            remote(
                source[job].at[:, columns(part, 1 - core)],
                target.at[job, part],
                kin_l_sems,
                (job if feed else 4 + job, part),
                (section_at, sibling),
            )
            for part in range(4)
        ]

    def kin_right(feed, job, chunk):
        if feed:
            here = pl.ds(chunk * 1024, 1024)
            source, target = feed_right[job].at[:, here], kin_rf.at[job, :, here]
        else:
            source, target = att_right[job], kin_ra.at[job]
        where = (2 * job + chunk if feed else 8 + job,)
        return remote(source, target, kin_r_sems, where, (section_at, sibling))

    def item_of(index):
        if index in FEEDS:
            order = FEEDS.index(index)
            return True, order // 2, order % 2
        return False, ATTENDS.index(index), 0

    def window_copies(index):
        feed, job, chunk = item_of(index)
        slot = index % WINDOWS
        size = 512 if feed else 256
        if feed:
            here = pl.ds(chunk * 1024, 1024)
            sources = (feed_right[job].at[:, here], kin_rf.at[job, :, here])
        else:
            sources = (att_right[job], kin_ra.at[job])
        return [
            pltpu.make_async_copy(
                sources[whose],
                rwin.at[slot, pl.ds(whose * size, size)],
                win_sems.at[slot, whose],
            )
            for whose in range(2)
        ]

    def raw_copies(index, part):
        feed, job, _ = item_of(index)
        size = 512 if feed else 256
        own_left = (feed_left if feed else att_left)[job]
        kin_left = (kin_lf if feed else kin_la).at[job]
        sources = (own_left.at[:, columns(part, core)], kin_left.at[part])
        return [
            pltpu.make_async_copy(
                source, raw.at[part, whose, pl.ds(0, size)], raw_sems.at[part, whose]
            )
            for whose, source in enumerate(sources)
        ]

    def raw_start(index):
        feed, job, chunk = item_of(index)
        if chunk == 0:
            for copy in kin_lefts(feed, job):
                copy.wait_recv()
            for part in range(4):
                for copy in raw_copies(index, part):
                    copy.start(priority=LOCAL)

    def load(index):
        feed, job, chunk = item_of(index)
        kin_right(feed, job, chunk).wait_recv()
        for copy in window_copies(index):
            copy.start(priority=LOCAL)
        if chunk == 0:
            if feed and job == 2:
                raw_start(index)
            size = 512 if feed else 256
            target = (lwin_f if feed else lwin_a).at[job]
            for part in range(4):
                for whose, copy in enumerate(raw_copies(index, part)):
                    copy.wait()
                    place = raw.at[part, whose, pl.ds(0, size)]
                    target[part, :, whose * size : whose * size + size] = place[...].T
        if index + 1 < total and item_of(index + 1)[:2] != (True, 2):
            raw_start(index + 1)

    def count_below(item, places):
        return sum((item > place).astype(jnp.int32) for place in places)

    def is_feed(item):
        return functools.reduce(jnp.logical_or, [item == place for place in FEEDS])

    def loaded(slot, feed):
        size = 512 if feed else 256
        for whose in range(2):
            source = kin_rf.at[0, :, pl.ds(0, 1024)] if feed else kin_ra.at[0]
            pltpu.make_async_copy(
                source, rwin.at[slot, pl.ds(whose * size, size)], win_sems.at[slot, whose]
            ).wait()

    def by_kind(item, action):
        @pl.when(is_feed(item))
        def _():
            action(count_below(item, FEEDS), True)

        @pl.when(jnp.logical_not(is_feed(item)))
        def _():
            action(count_below(item, ATTENDS), False)

    def mark(order, feed):
        return order if feed else 8 + order

    def merged_of(order, feed):
        return merged_f.at[lax.rem(order, 4)] if feed else merged_a.at[order]

    def passing_of(order, feed, slot):
        if feed:
            return passing_f.at[lax.rem(order, 6), slot]
        return passing_a.at[lax.rem(order, 4), slot]

    def lined_of(order, feed):
        return lined_f.at[lax.rem(order, 4)] if feed else lined_a.at[order]

    def crossed_of(order, feed):
        return crossed_f.at[lax.rem(order, 4)] if feed else crossed_a.at[order]

    def products(order, slot, choice, store):
        def quarter(index, carry):
            here = pl.ds(pl.multiple_of(index * 256, 256), 256)
            bit = choice[0] + index * (choice[1] - choice[0])
            first = pl.multiple_of(index * 512 + bit * 256, 256)
            left = lwin_a[order].reshape(512, 512)
            right = rwin[slot, 0:512, pl.ds(first, 256)]
            tile = jnp.dot(left, right, preferred_element_type=F32).reshape(4, 128, 256)
            store(pl.ds(0, 4), here, tile)
            return carry

        lax.fori_loop(0, 2, quarter, 0)

    def xy_copies(item):
        return [
            remote(
                stage.at[lax.rem(item, STAGES), :, :, pl.ds(side * 256, 256)],
                merged_a.at[item, :, :, pl.ds(side * 256, 256)],
                xy_sems,
                (item, side),
                (flat[side], batch_at),
            )
            for side in range(2)
        ]

    def xy_sent(item):
        for copy in xy_copies(item):
            copy.wait_send()

    def line_copy(item, feed, dest, place, rightward):
        step = 1 if rightward else -1
        slot = 4 if not rightward and place - 1 == dest else dest
        return pltpu.make_async_remote_copy(
            merged_of(item, feed).at[dest],
            passing_of(item, feed, slot),
            line_send.at[mark(item, feed), dest],
            line_recv.at[mark(item, feed), slot],
            device_id=(section_at, batch_at + 2 * step),
            device_id_type=MESH,
        )

    def line_wait(item, feed, slot):
        pltpu.make_async_remote_copy(
            merged_of(item, feed).at[0],
            passing_of(item, feed, slot),
            line_send.at[mark(item, feed), 0],
            line_recv.at[mark(item, feed), slot],
            device_id=(section_at, sibling),
            device_id_type=MESH,
        ).wait_recv()

    def line_sent(item, feed):
        for step in (1, 2, 3):
            dest = lax.rem(spot + step, 4)
            pltpu.make_async_remote_copy(
                merged_of(item, feed).at[dest],
                passing_of(item, feed, 0),
                line_send.at[mark(item, feed), dest],
                line_recv.at[mark(item, feed), 0],
                device_id=(section_at, sibling),
                device_id_type=MESH,
            ).wait_send()

    def outset(item, feed):
        @pl.when(spot == 0)
        def _():
            for dest in (3, 2, 1):
                line_copy(item, feed, dest, 0, True).start()

        @pl.when(spot == 3)
        def _():
            for dest in (0, 1, 2):
                line_copy(item, feed, dest, 3, False).start()

    def drained(item, feed):
        line_sent(item, feed)
        delivered(item, feed)

    def delivered(item, feed):
        if feed:
            feed_out(item, up_out).wait()
            feed_own(item, up_out).wait()
        else:
            for side in range(2):
                att_out(item, side, end_out_s, 0).wait()
                att_own(item, side, end_out_s, 0).wait()

    def offer(slot, item, feed):
        loaded(slot, feed)
        if feed:

            @pl.when(item >= 4)
            def _():
                line_sent(item - 4, True)

            target = merged_of(item, True)

            def tile(index, carry):
                here = pl.ds(pl.multiple_of(index * 256, 256), 256)
                left = lwin_f[item // 2].reshape(512, 1024)
                right = rwin[slot, :, here]
                value = jnp.dot(left, right, preferred_element_type=F32)
                target[:, :, here] = value.reshape(4, 128, 256).astype(BF)
                return carry

            lax.fori_loop(0, 4, tile, 0)
            outset(item, True)
        else:

            @pl.when(item >= STAGES)
            def _():
                xy_sent(item - STAGES)

            def store(blocks, here, tile):
                stage[lax.rem(item, STAGES), blocks, :, here] = tile.astype(BF)

            products(item, slot, (1 - x_at, 1 - y_at), store)
            for copy in xy_copies(item):
                copy.start()

    def take(slot, item, feed):
        for copy in xy_copies(item):
            copy.wait_recv()
        target = merged_a.at[item]

        def store(blocks, here, tile):
            target[blocks, :, here] = (tile + target[blocks, :, here].astype(F32)).astype(BF)

        products(item, slot, bits, store)
        outset(item, False)

    def relay(item, feed, dest, place, rightward):
        line_wait(item, feed, dest)
        target = merged_of(item, feed)
        arrived = passing_of(item, feed, dest)
        target[dest] = (target[dest].astype(F32) + arrived[...].astype(F32)).astype(BF)
        line_copy(item, feed, dest, place, rightward).start()

    def second_of(item, feed):
        @pl.when(spot == 1)
        def _():
            for dest in (3, 2):
                relay(item, feed, dest, 1, True)

        @pl.when(spot == 2)
        def _():
            for dest in (0, 1):
                relay(item, feed, dest, 2, False)

    def third_of(item, feed):
        @pl.when(spot == 1)
        def _():
            relay(item, feed, 0, 1, False)

        @pl.when(spot == 2)
        def _():
            relay(item, feed, 3, 2, True)

    def feed_cross(item):
        return remote(
            lined_of(item, True),
            crossed_of(item, True),
            cross_sems,
            (item, 0),
            (above + item // 4 * (beside - above), batch_at),
        )

    def cross_copy(item, side):
        here = pl.ds(side * 256, 256)
        return remote(
            lined_of(item, False).at[:, here],
            crossed_of(item, False).at[:, here],
            cross_sems,
            (8 + item, side),
            (flat[1 - side], batch_at),
        )

    def feed_place(item, target):
        base = (x_at + item // 4 * (y_at - x_at)) * 2048 + lax.rem(item, 2) * 1024
        return target.at[1 - item // 4, :, pl.ds(pl.multiple_of(base, 1024), 1024)]

    def feed_out(item, target):
        return remote(
            lined_of(item, True),
            feed_place(item, target),
            out_sems,
            (item, 0),
            (beside + item // 4 * (above - beside), batch_at),
        )

    def feed_own(item, target):
        return pltpu.make_async_copy(
            lined_of(item, True), feed_place(item, target), own_sems.at[item, 0]
        )

    def feed_write(item):
        @pl.when(lax.rem(item, 4) < 2)
        def _():
            feed_out(item, down_out).start()
            feed_own(item, down_out).start(priority=LOCAL)

        @pl.when(lax.rem(item, 4) >= 2)
        def _():
            feed_out(item, up_out).start()
            feed_own(item, up_out).start(priority=LOCAL)

    def att_place(item, side, target, inner):
        base = side * 512 + bits[side] * 256
        return target.at[inner, :, pl.ds(pl.multiple_of(base, 256), 256)]

    def att_out(item, side, target, inner):
        return remote(
            lined_of(item, False).at[:, pl.ds(side * 256, 256)],
            att_place(item, side, target, inner),
            out_sems,
            (8 + item, side),
            (flat[side], batch_at),
        )

    def att_own(item, side, target, inner):
        return pltpu.make_async_copy(
            lined_of(item, False).at[:, pl.ds(side * 256, 256)],
            att_place(item, side, target, inner),
            own_sems.at[8 + item, side],
        )

    def att_write(item):
        inner = lax.rem(item, 4) - 1
        for turn, proj, end in ((0, proj_out_s, end_out_s), (1, proj_out_c, end_out_c)):

            @pl.when(jnp.logical_and(item // 4 == turn, inner >= 0))
            def _():
                for side in range(2):
                    att_out(item, side, proj, inner).start()
                    att_own(item, side, proj, inner).start(priority=LOCAL)

            @pl.when(jnp.logical_and(item // 4 == turn, inner < 0))
            def _():
                for side in range(2):
                    att_out(item, side, end, 0).start()
                    att_own(item, side, end, 0).start(priority=LOCAL)

    def close_of(item, feed):
        if feed:

            @pl.when(item >= 4)
            def _():
                delivered(item - 4, True)

        for place in range(4):

            @pl.when(spot == place)
            def _():
                value = merged_of(item, feed)[place].astype(F32)
                if place > 0:
                    line_wait(item, feed, place)
                    value += passing_of(item, feed, place)[...].astype(F32)
                if place < 3:
                    line_wait(item, feed, 4)
                    value += passing_of(item, feed, 4)[...].astype(F32)
                lined_of(item, feed)[...] = value.astype(BF)

        if feed:
            feed_cross(item).start()
        else:
            for side in range(2):
                cross_copy(item, side).start()

    def finish_of(item, feed):
        if feed:
            feed_cross(item).wait()
        else:
            for side in range(2):
                cross_copy(item, side).wait()
        target = lined_of(item, feed)
        target[...] = (
            target[...].astype(F32) + crossed_of(item, feed)[...].astype(F32)
        ).astype(BF)
        if feed:
            feed_write(item)
        else:
            att_write(item)

    def small_copy(phase):
        if phase == 0:
            peer = (section_at, sibling)
        elif phase < 3:
            peer = (flat[phase - 1], batch_at)
        else:
            peer = (section_at, lax.rem(spot + phase - 2, 4) * 2 + core)
        return remote(
            small_sum.at[min(phase, 3)], small_in.at[phase], small_sems, (phase,), peer
        )

    quarter_rows = pair.shape[0] // 4

    def point_copy(which):
        peer = (beside, above, across)[which]
        return remote(
            pair.at[pl.ds(pl.multiple_of(peer * quarter_rows, 128), quarter_rows)],
            point_in.at[which],
            point_sems,
            (which,),
            (peer, batch_at),
        )

    def point_place():
        return point_out.at[pl.ds(pl.multiple_of(section_at * quarter_rows, 128), quarter_rows)]

    def point_deal(which):
        peer = (beside, above, across)[which]
        return remote(point_sum, point_place(), deal_sems, (which,), (peer, batch_at))

    def point_local():
        return pltpu.make_async_copy(point_sum, point_place(), point_own.at[0])

    pairs = ((last_ref, last_out), (grad, first_out))

    def lat_copy(which, way):
        source, target = pairs[which]
        return remote(
            source,
            target.at[pl.ds(pl.multiple_of(section_at * rows, rows), rows)],
            lat_sems,
            (which, way),
            (flat[way], batch_at),
        )

    def lat_far(which, way):
        target = pairs[which][1]
        low = flat[way] * rows + way * (rows // 2)
        part = target.at[pl.ds(pl.multiple_of(low, rows // 2), rows // 2)]
        return remote(part, part, far_sems, (which, way), (flat[1 - way], batch_at))

    def lat_local(which):
        source, target = pairs[which]
        return pltpu.make_async_copy(
            source,
            target.at[pl.ds(pl.multiple_of(section_at * rows, rows), rows)],
            lat_own.at[which],
        )

    def lat_start(which):
        lat_local(which).start(priority=LOCAL)
        for way in range(2):
            lat_copy(which, way).start()

    def lat_onward(which):
        for way in range(2):
            lat_copy(which, way).wait_recv()
            lat_far(which, way).start()

    loads = []
    for turn, (proj, out, up, down) in enumerate(
        ((proj_s, out_s, in_1, down_1), (proj_c, out_c, in_0, down_0))
    ):
        for chunk in range(2):
            loads += [down.at[:, pl.ds(chunk * 1024, 1024)], up.at[:, pl.ds(chunk * 1024, 1024)]]
        loads.append(out)
        loads += [proj.at[:, pl.ds(which * 1024, 1024)] for which in range(3)]

    def slot_copy(index):
        return pltpu.make_async_copy(loads[index], slots.at[index % 2], slot_sems.at[index % 2])

    def opened(index):
        slot_copy(index).wait()
        return index % 2

    def closed(index):
        if index + 2 < len(loads):
            slot_copy(index + 2).start(priority=LOCAL)

    def h_copy(index):
        layer, chunk = 1 - index // 2, index % 2
        return pltpu.make_async_copy(
            before.at[layer, :, pl.ds(chunk * 1024, 1024)], hbuf, h_sem.at[0]
        )

    def pair_over(turn):
        return remote(
            pair.at[pl.ds(0, rows)],
            pair.at[pl.ds(rows, rows)],
            pair_sems,
            (turn, 0),
            ((beside, above)[turn], batch_at),
        )

    def part_over(turn):
        return remote(
            part_out.at[turn], part_in.at[turn], pair_sems, (turn, 1), ((beside, above)[turn], batch_at)
        )

    def grad_saved(turn):
        return pltpu.make_async_copy(grad, grads_h.at[turn], save_sems.at[0])

    def act_copies(turn):
        chosen = ((q_s, k_s, v_s), (q_c, k_c, v_c))[turn]
        return [
            pltpu.make_async_copy(source, target, act_sems.at[index])
            for index, (source, target) in enumerate(zip(chosen, (qb, kb, vb)))
        ]

    def row_copy(index):
        if index == 3:
            source = latents_in.at[pl.ds(pl.multiple_of(section_at * rows, rows), rows)]
        else:
            source = (u3_in, u2_in, u1_in)[index]
        return pltpu.make_async_copy(source, ub, act_sems.at[3])

    def small_row(index, value):
        small_sum[0, index : index + 1, :] = value

    def open_pair(turn):
        pair[0:rows, :] = grad[...]
        if turn == 1:
            pl.semaphore_wait(free_sem, 1)
        pair_over(turn).start()

    def pair_ready(turn):
        pair_over(turn).wait()
        for copy in kin_lefts(True, 2 * turn):
            copy.start()

    def feed_chunk(turn, chunk):
        layer = 1 - turn
        base = 8 * turn + 2 * chunk
        h_copy(2 * turn + chunk).wait()
        if turn == 1:
            kin_right(True, 1, chunk).wait_send()
        slot = opened(base)

        def up_tile(here, index):
            there = pl.ds(pl.multiple_of(chunk * 1024 + index * 256, 256), 256)
            value = mm(pair[...], slots[slot, :, here]) * hbuf[:, here]
            short = value.astype(BF)
            slope[:, there] = short
            column = jnp.sum(short.astype(F32), axis=0, keepdims=True)
            for half in range(2):
                index_at = 7 + 4 * layer + 2 * half + chunk
                small_sum[0, index_at : index_at + 1, here] = jnp.where(
                    (x_at, y_at)[turn] == half, column, jnp.zeros_like(column)
                )

        tiles(4, up_tile)
        closed(base)
        if 2 * turn + chunk + 1 < 4:
            h_copy(2 * turn + chunk + 1).start(priority=LOCAL)
        kin_right(True, 2 * turn + 1, chunk).start()
        slot = opened(base + 1)

        def down_tile(there, _):
            value = mm_cols(slope[:, chunk * 1024 : chunk * 1024 + 1024], slots[slot, there, :])
            if chunk == 0:
                rows_sum[:, there] = value
            else:
                value = rows_sum[:, there] + value
                rows_sum[:, there] = value
                part_out[turn, :, there] = value[rows:].astype(BF)

        tiles(4, down_tile)
        closed(base + 1)
        if chunk == 1:
            if turn == 0:
                for copy in kin_lefts(True, 0):
                    copy.wait_send()
                pl.semaphore_signal(
                    free_sem, inc=1, device_id=(above, batch_at), device_id_type=MESH
                )
            part_over(turn).start()

    def row_steps(body, count):
        zero = jnp.zeros((1, width), F32)

        def step(index, carry):
            here = pl.ds(pl.multiple_of(index * 32, 32), 32)
            return tuple(a + b for a, b in zip(carry, body(here)))

        return lax.fori_loop(0, rows // 32, step, (zero,) * count)

    def lean(back, unit, inverse, gain):
        scaled = back * gain
        inner = (
            scaled
            - jnp.mean(scaled, axis=-1, keepdims=True)
            - unit * jnp.mean(scaled * unit, axis=-1, keepdims=True)
        )
        return inverse * inner, jnp.sum(back * unit, axis=0, keepdims=True)

    def feed_end(turn):
        layer = 1 - turn
        gain = gains[3 + layer : 4 + layer, :]
        part_over(turn).wait_recv()
        row_copy(2 * turn).wait()

        def body(here):
            unit, inverse = unit_rows(ub[here, :].astype(F32))
            back = rows_sum[here, :] + part_in[turn, here, :].astype(F32)
            dx, gain_part = lean(back, unit, inverse, gain)
            old = grad[here, :].astype(F32)
            grad[here, :] = (old + dx).astype(BF)
            return gain_part, jnp.sum(old, axis=0, keepdims=True)

        gain_grad, out_grad = row_steps(body, 2)
        row_copy(2 * turn + 1).start(priority=LOCAL)
        small_row(3 + layer, gain_grad)
        small_row(5 + layer, out_grad)
        grad_saved(turn).start(priority=LOCAL)
        slot = opened(8 * turn + 4)

        def tile(there, _):
            dob[:, there] = mm_cols(grad[...], slots[slot, there, :]).astype(BF)

        tiles(2, tile, 512)
        closed(8 * turn + 4)
        grad_saved(turn).wait()
        kin_right(False, 4 * turn, 0).start()

    def attend_heads(turn):
        scale = 1.0 / math.sqrt(HD)
        for copy in act_copies(turn):
            copy.wait()
        if turn == 1:
            for which in range(3):
                kin_right(False, 1 + which, 0).wait_send()

        def head(index, carry):
            here = pl.ds(pl.multiple_of(index * HD, HD), HD)
            q, k, v, do = qb[:, here], kb[:, here], vb[:, here], dob[:, here]
            scores = mm_cols(q, k) * scale
            if turn == 1:
                scores = jnp.where(mask_in[...] > 0.0, scores, MASKED)
            grown = jnp.exp(scores - jnp.max(scores, axis=-1, keepdims=True))
            soft = grown / jnp.sum(grown, axis=-1, keepdims=True)
            back = mm_cols(do, v)
            short = soft * (back - jnp.sum(soft * back, axis=-1, keepdims=True))
            dqkv[0, :, here] = (mm(short.astype(BF), k) * scale).astype(BF)
            dqkv[1, :, here] = (mm(short.T.astype(BF), q) * scale).astype(BF)
            dqkv[2, :, here] = mm(soft.T.astype(BF), do).astype(BF)
            return carry

        lax.fori_loop(0, width // HD, head, 0)
        if turn == 0:
            for copy in act_copies(1):
                copy.start(priority=LOCAL)
        for which in range(3):
            kin_right(False, 4 * turn + 1 + which, 0).start()

    def attend_end(turn):
        base = 8 * turn + 5
        for which in range(3):
            slot = opened(base + which)

            def tile(there, _):
                value = mm_cols(dqkv[which], slots[slot, there, :])
                if which == 0:
                    rows_sum[0:rows, there] = value
                elif which == 1:
                    rows_sum[rows : 2 * rows, there] = value
                else:
                    rows_sum[rows : 2 * rows, there] += value

            tiles(2, tile, 512)
            closed(base + which)
        row_copy(2 * turn + 1).wait()
        gain_q = gains[2:3, :] if turn == 0 else gains[0:1, :]
        gain_kv = gains[2:3, :] if turn == 0 else gains[1:2, :]

        def body(here):
            unit, inverse = unit_rows(ub[here, :].astype(F32))
            dx, gain_part = lean(rows_sum[here, :], unit, inverse, gain_q)
            if turn == 1:
                unit, inverse = unit_rows(src_in[here, :].astype(F32))
            there = pl.ds(pl.multiple_of(rows + here.start, 32), 32)
            ds, kv_part = lean(rows_sum[there, :], unit, inverse, gain_kv)
            fresh = grad[here, :].astype(F32) + dx
            if turn == 0:
                fresh += ds
            else:
                high = ds.astype(BF)
                part_out[0, here, :] = high
                part_out[1, here, :] = (ds - high.astype(F32)).astype(BF)
            grad[here, :] = fresh.astype(BF)
            return gain_part, kv_part

        if turn == 1:
            for which in range(2):
                part_over(which).wait_send()
            for copy in kin_lefts(True, 2):
                copy.wait_send()
        gain_grad, kv_grad = row_steps(body, 2)
        if turn == 0:
            row_copy(2).start(priority=LOCAL)
            small_row(2, gain_grad + kv_grad)
            open_pair(1)
        else:
            small_row(0, gain_grad)
            small_row(1, kv_grad)
            small_row(15, jnp.zeros_like(gain_grad))

            def tile(there, _):
                pair[:, there] = (
                    mm(picks_in[...], part_out[0, :, there])
                    + mm(picks_in[...], part_out[1, :, there])
                ).astype(BF)

            tiles(4, tile)
            small_copy(0).start()
            for which in range(3):
                point_copy(which).start()
            lat_start(1)

    def point_total():
        for which in range(3):
            point_copy(which).wait_recv()
        gathered = pair[
            pl.ds(pl.multiple_of(section_at * quarter_rows, 128), quarter_rows)
        ].astype(F32)
        for which in range(3):
            gathered += point_in[which].astype(F32)
        point_sum[...] = gathered.astype(BF)
        point_local().start(priority=LOCAL)
        for which in range(3):
            point_deal(which).start()

    def small_step(phase):
        small_copy(phase).wait_recv()
        small_sum[phase + 1] = small_sum[phase] + small_in[phase]
        if phase < 2:
            small_copy(phase + 1).start()
        else:
            for step in range(3):
                small_copy(3 + step).start()

    def small_end():
        for step in range(3):
            small_copy(3 + step).wait_recv()
        small_out[...] = (small_sum[3] + small_in[4]) + (small_in[3] + small_in[5])

    def rows_end():
        lat_onward(1)
        point_total()

    begin = pltpu.make_async_copy(top_in, grad, act_sems.at[4])
    begin.start()
    for index in range(2):
        slot_copy(index).start(priority=LOCAL)
    h_copy(0).start(priority=LOCAL)
    row_copy(0).start(priority=LOCAL)
    for copy in act_copies(0):
        copy.start(priority=LOCAL)
    begin.wait()
    open_pair(0)
    for part in range(2):
        kin_right(True, 0, part).start()
    pair_ready(0)
    for copy in kin_lefts(True, 1):
        copy.start()
    for job in range(4):
        for copy in kin_lefts(False, job):
            copy.start()
    for part in range(2):
        kin_right(True, 2, part).start()
    for copy in kin_lefts(True, 3):
        copy.start()
    for job in range(4, 8):
        for copy in kin_lefts(False, job):
            copy.start()
    raw_start(0)
    load(0)
    chain = {
        0: [functools.partial(feed_chunk, 0, 0), functools.partial(lat_start, 0)],
        1: [functools.partial(feed_chunk, 0, 1)],
        2: [functools.partial(feed_end, 0), functools.partial(lat_onward, 0)],
        3: [functools.partial(attend_heads, 0)],
        4: [functools.partial(attend_end, 0)],
        5: [functools.partial(pair_ready, 1), functools.partial(feed_chunk, 1, 0)],
        6: [functools.partial(feed_chunk, 1, 1)],
        7: [functools.partial(feed_end, 1)],
        8: [functools.partial(attend_heads, 1)],
        9: [functools.partial(attend_end, 1)],
        11: [functools.partial(small_step, 0), rows_end],
        13: [functools.partial(small_step, 1)],
        15: [functools.partial(small_step, 2)],
        17: [small_end],
    }

    def moment_body(moment, carry):
        @pl.when(moment < total)
        def _():
            by_kind(moment, functools.partial(offer, lax.rem(moment, WINDOWS)))

        ready = jnp.logical_and(moment >= 2, moment < total + 2)

        @pl.when(jnp.logical_and(ready, jnp.logical_not(is_feed(moment - 2))))
        def _():
            take(lax.rem(moment - 2, WINDOWS), count_below(moment - 2, ATTENDS), False)

        for lag, action in ((3, second_of), (4, third_of), (5, close_of), (6, finish_of)):

            @pl.when(jnp.logical_and(moment >= lag, moment < total + lag))
            def _():
                by_kind(moment - lag, action)
        for when, actions in chain.items():

            @pl.when(moment == when)
            def _():
                for action in actions:
                    action()

        for item in range(1, total):
            pl.when(moment == item - 1)(functools.partial(load, item))
        return carry

    lax.fori_loop(0, total + 6, moment_body, 0)

    for index in range(4):
        if index % 2 == 1:
            for copy in kin_lefts(True, index):
                copy.wait_send()
        if index != 1:
            for chunk in range(2):
                kin_right(True, index, chunk).wait_send()
    for index in range(8):
        for copy in kin_lefts(False, index):
            copy.wait_send()
        if index not in (1, 2, 3):
            kin_right(False, index, 0).wait_send()
    for phase in range(6):
        small_copy(phase).wait_send()
    for which in range(2):
        lat_local(which).wait()
        for way in range(2):
            lat_copy(which, way).wait_send()
            lat_far(which, way).wait()
    point_local().wait()
    for which in range(3):
        point_copy(which).wait_send()
        point_deal(which).wait()

    def drain(order, carry):
        @pl.when(order >= 4)
        def _():
            drained(order, True)

        drained(order, False)
        return carry

    for order in (5, 6, 7):
        xy_sent(order)
    lax.fori_loop(0, 8, drain, 0)


def reduce_all(full, kept, latents, gains, mask, picks):
    total = ITEM_COUNT
    rows, width = kept[0].shape
    points = picks.shape[0]
    anywhere = pl.BlockSpec(memory_space=pl.ANY)
    vmem = pl.BlockSpec(memory_space=pltpu.VMEM)
    u1, u2, u3, u4, top = kept[:5]
    operands = [*full, u1, u2, u3, u4, top, *kept[5:16], *kept[17:], latents, kept[16]]
    operands += [gains, mask, picks]
    spaces = [anywhere] * (len(operands) - 4) + [vmem] * 4
    dma = pltpu.SemaphoreType.DMA
    flops = 2 * width * width * 24 * rows * 2
    return pl.pallas_call(
        reduce_kernel,
        out_shape=[
            jax.ShapeDtypeStruct((2, 128, 4 * width), BF),
            jax.ShapeDtypeStruct((2, 128, 4 * width), BF),
            jax.ShapeDtypeStruct((3, 128, width), BF),
            jax.ShapeDtypeStruct((3, 128, width), BF),
            jax.ShapeDtypeStruct((1, 128, width), BF),
            jax.ShapeDtypeStruct((1, 128, width), BF),
            jax.ShapeDtypeStruct((4 * rows, width), BF),
            jax.ShapeDtypeStruct((4 * rows, width), BF),
            jax.ShapeDtypeStruct((points, width), BF),
            jax.ShapeDtypeStruct((16, width), F32),
            jax.ShapeDtypeStruct((2, rows, width), BF),
            jax.ShapeDtypeStruct((4, 4, 2 * rows, 128), BF),
            jax.ShapeDtypeStruct((8, 4, rows, 128), BF),
            jax.ShapeDtypeStruct((4, 2 * rows, 2 * width), BF),
            jax.ShapeDtypeStruct((8, rows, width), BF),
        ],
        in_specs=spaces,
        out_specs=[anywhere] * 9 + [vmem] + [anywhere] * 5,
        scratch_shapes=[
            pltpu.VMEM((4, 4, 128, 1024), BF),
            pltpu.VMEM((8, 4, 128, 512), BF),
            pltpu.VMEM((4, 2, 512, 128), BF),
            pltpu.VMEM((WINDOWS, 1024, 1024), BF),
            pltpu.VMEM((STAGES, 4, 128, 512), BF),
            pltpu.VMEM((4, 4, 128, 1024), BF),
            pltpu.VMEM((8, 4, 128, 512), BF),
            pltpu.VMEM((6, 5, 128, 1024), BF),
            pltpu.VMEM((4, 5, 128, 512), BF),
            pltpu.VMEM((4, 128, 1024), BF),
            pltpu.VMEM((8, 128, 512), BF),
            pltpu.VMEM((4, 128, 1024), BF),
            pltpu.VMEM((8, 128, 512), BF),
            pltpu.VMEM((512, 1024), BF),
            pltpu.VMEM((512, 2048), BF),
            pltpu.VMEM((512, 1024), F32),
            pltpu.VMEM((512, 1024), F32),
            pltpu.VMEM((2, 1024, 1024), BF),
            pltpu.VMEM((256, 1024), BF),
            pltpu.VMEM((256, 1024), BF),
            pltpu.VMEM((256, 1024), BF),
            pltpu.VMEM((256, 1024), BF),
            pltpu.VMEM((3, 256, 1024), BF),
            pltpu.VMEM((2, 256, 1024), BF),
            pltpu.VMEM((2, 256, 1024), BF),
            pltpu.VMEM((256, 1024), BF),
            pltpu.VMEM((256, 1024), BF),
            pltpu.VMEM((3, points // 4, width), BF),
            pltpu.VMEM((points // 4, width), BF),
            pltpu.VMEM((6, 16, width), F32),
            pltpu.VMEM((4, 16, width), F32),
            dma((2, 12, 4)),
            dma((2, 16)),
            dma((4, 2)),
            dma((WINDOWS, 2)),
            dma((2, 8, 2)),
            dma((total, 4)),
            dma((total, 5)),
            dma((2, total, 2)),
            dma((2, total, 2)),
            dma((total, 2)),
            dma((2, 2, 2)),
            dma((2, 2, 2)),
            dma((2,)),
            dma((2, 3)),
            dma((2, 3)),
            dma((1,)),
            dma((2, 6)),
            dma((2, 2, 2)),
            dma((2,)),
            dma((1,)),
            dma((1,)),
            dma((5,)),
            pltpu.SemaphoreType.REGULAR,
        ],
        compiler_params=pltpu.CompilerParams(
            collective_id=2, has_side_effects=True, vmem_limit_bytes=62 * 2**20
        ),
        cost_estimate=pl.CostEstimate(
            flops=flops, bytes_accessed=2**27, transcendentals=2**21
        ),
    )(*operands)[:10]


def plain_layers(full, spread, mine, source, valid, cot_own, picks, groups_all):
    proj_c, out_c, in_0, down_0, proj_s, out_s, in_1, down_1 = full
    width, hidden = in_0.shape

    def vector(first, count):
        return spread[:, first : first + count].reshape(-1)

    gains_cross = (vector(0, 1), vector(1, 1))
    gain_self = vector(2, 1)
    gains_mlp = (vector(3, 1), vector(4, 1))
    biases_out = (vector(5, 1), vector(6, 1))
    per_bias = hidden // width
    biases_in = (vector(7, per_bias), vector(7 + per_bias, per_bias))
    cot = cot_own.astype(F32)
    u1, kept_c = attend(mine, source, valid, gains_cross[0], gains_cross[1], proj_c, out_c)
    u2, kept_0 = feed(u1.astype(F32), gains_mlp[0], in_0, biases_in[0], down_0, biases_out[0])
    u2 = u2.astype(F32)
    u3, kept_s = attend(u2, u2, None, gain_self, gain_self, proj_s, out_s)
    u4, kept_1 = feed(u3.astype(F32), gains_mlp[1], in_1, biases_in[1], down_1, biases_out[1])
    final = u4.astype(F32)
    group_norm = jnp.sqrt(jnp.mean(final * final) + EPSILON)
    norm_mean = lax.psum(group_norm, ALL) / groups_all
    g4 = (cot + (norm_mean / group_norm) * final).astype(BF)

    dx, gain_1_grad, bias_1_grad, ob_1_grad, pairs_1 = feed_back(
        g4, kept_1, gains_mlp[1], in_1, down_1
    )
    g3 = (g4.astype(F32) + dx).astype(BF)
    dx, ds, gq, gkv, pairs_s = attend_back(g3, kept_s, gain_self, gain_self, proj_s, out_s)
    gain_s_grad = gq + gkv
    g2 = (g3.astype(F32) + dx + ds).astype(BF)
    dx, gain_0_grad, bias_0_grad, ob_0_grad, pairs_0 = feed_back(
        g2, kept_0, gains_mlp[0], in_0, down_0
    )
    g1 = (g2.astype(F32) + dx).astype(BF)
    dx, ds, cq_grad, ckv_grad, pairs_c = attend_back(
        g1, kept_c, gains_cross[0], gains_cross[1], proj_c, out_c
    )
    g0 = (g1.astype(F32) + dx).astype(BF)
    high = ds.astype(BF)
    low = (ds - high.astype(F32)).astype(BF)
    point_part = (mm_rows(picks, high) + mm_rows(picks, low)).astype(BF)
    small = jnp.concatenate(
        [
            cq_grad,
            ckv_grad,
            gain_s_grad,
            gain_0_grad,
            gain_1_grad,
            ob_0_grad,
            ob_1_grad,
            bias_0_grad,
            bias_1_grad,
            jnp.zeros_like(cq_grad),
        ]
    ).reshape(-1, width)
    pairs = pairs_1 + pairs_s + pairs_0 + pairs_c
    lefts, rights = [pair[0] for pair in pairs], [pair[1] for pair in pairs]
    def settled_grad(left, right):
        part = lax.psum_scatter(
            mm_rows(left, right).astype(BF), ALL, scatter_dimension=0, tiled=True
        )
        return lax.all_gather(part, "section", axis=0, tiled=True).astype(F32)

    done = [settled_grad(left, right) for left, right in pairs]
    mlp_in_grad = jnp.stack([done[6], done[0]])
    mlp_down_grad = jnp.stack([done[7], done[1]])
    proj_s_grad = jnp.concatenate(done[2:5], axis=1)
    proj_c_grad = jnp.concatenate(done[8:11], axis=1)
    out_s_grad, out_c_grad = done[5], done[11]
    points_sum = lax.psum(point_part, "section")
    latents_out = lax.all_gather(u4, "section", axis=0, tiled=True)
    g0_all = lax.all_gather(g0, "section", axis=0, tiled=True)
    small = lax.psum(small, ALL)
    return (
        norm_mean,
        latents_out,
        g0_all,
        points_sum,
        small,
        mlp_in_grad,
        mlp_down_grad,
        proj_c_grad,
        proj_s_grad,
        out_c_grad,
        out_s_grad,
    )


def per_device(
    latents,
    points,
    neighbours,
    lengths,
    cross_proj,
    cross_out,
    cross_gains,
    self_proj,
    self_out,
    self_gain,
    mlp_gain,
    mlp_in,
    mlp_in_bias,
    mlp_down,
    mlp_out_bias,
    cotangent,
):
    sections = lax.axis_size("section")
    section_at = lax.axis_index("section")
    width = latents.shape[1]
    hidden = mlp_in.shape[2]
    groups_dev = neighbours.shape[0]
    rows = latents.shape[0] // sections
    shard = cross_out.shape[0]
    piece = shard // sections
    groups_all = groups_dev * lax.axis_size("batch")

    def gathered(block):
        own = lax.dynamic_slice_in_dim(block, section_at * piece, piece, 0)
        return lax.all_gather(own, ALL, axis=0, tiled=True)

    projs = (cross_proj.reshape(shard, 3 * width), self_proj.reshape(shard, 3 * width))
    if lax.axis_size("batch") == 8:
        made = gather_forward(
            [projs[0], cross_out, mlp_in, mlp_down, projs[1], self_out],
            latents,
            cotangent,
            points,
            neighbours,
            lengths[:, None],
            [cross_gains, self_gain[None, :], mlp_gain, mlp_out_bias, mlp_in_bias],
        )
        full, gain_rows, norm_tile, mask, picks = made[:8], *made[8:12]
        norm_mean = norm_tile[0, 0]
        (
            mlp_in_grad,
            mlp_down_grad,
            proj_c_grad,
            proj_s_grad,
            out_c_grad,
            out_s_grad,
            latents_out,
            g0_all,
            points_sum,
            small,
        ) = reduce_all(full, made[12:], latents, gain_rows, mask, picks)
        mlp_in_grad = mlp_in_grad.astype(F32)
        mlp_down_grad = mlp_down_grad.astype(F32)
        proj_c_grad = jnp.swapaxes(proj_c_grad, 0, 1).astype(F32)
        proj_s_grad = jnp.swapaxes(proj_s_grad, 0, 1).astype(F32)
        out_c_grad, out_s_grad = out_c_grad[0].astype(F32), out_s_grad[0].astype(F32)
    else:
        vectors = jnp.concatenate(
            [
                cross_gains.reshape(-1),
                self_gain,
                mlp_gain.reshape(-1),
                mlp_out_bias.reshape(-1),
                mlp_in_bias.reshape(-1),
                jnp.zeros_like(self_gain),
            ]
        ).reshape(-1, shard)
        cot_own = lax.dynamic_slice_in_dim(cotangent, section_at * rows, rows, 0)
        mine = lax.dynamic_slice_in_dim(latents, section_at * rows, rows, 0).astype(F32)
        listed = lax.dynamic_index_in_dim(neighbours, section_at, 0, keepdims=False)
        length = lax.dynamic_index_in_dim(lengths, section_at, 0, keepdims=False)
        valid = jnp.arange(listed.shape[0], dtype=jnp.int32) < length
        picks = listed[:, None] == jnp.arange(points.shape[0], dtype=jnp.int32)[None, :]
        picks = picks.astype(BF)
        source = mm(picks, points)
        blocks = [projs[0], cross_out, mlp_in[0], mlp_down[0]]
        blocks += [projs[1], self_out, mlp_in[1], mlp_down[1]]
        full = [gathered(block) for block in blocks]
        spread = lax.all_gather(vectors, "batch", axis=0, tiled=False)
        (
            norm_mean,
            latents_out,
            g0_all,
            points_sum,
            small,
            mlp_in_grad,
            mlp_down_grad,
            proj_c_grad,
            proj_s_grad,
            out_c_grad,
            out_s_grad,
        ) = plain_layers(full, spread.astype(F32), mine, source, valid, cot_own, picks, groups_all)
    points_grad = points_sum.astype(F32)
    latents_grad = g0_all.astype(F32)
    per_bias = hidden // width
    batch_at = lax.axis_index("batch")

    def own(first, count):
        flat = small[first : first + count].reshape(-1)
        size = flat.shape[0] // lax.axis_size("batch")
        return lax.dynamic_slice_in_dim(flat, batch_at * size, size, 0)

    return (
        latents_out,
        latents_grad,
        points_grad,
        proj_c_grad.reshape(shard, 3, width),
        out_c_grad,
        jnp.stack([own(0, 1), own(1, 1)]),
        proj_s_grad.reshape(shard, 3, width),
        out_s_grad,
        own(2, 1),
        jnp.stack([own(3, 1), own(4, 1)]),
        mlp_in_grad,
        jnp.stack([own(7, per_bias), own(7 + per_bias, per_bias)]),
        mlp_down_grad,
        jnp.stack([own(5, 1), own(6, 1)]),
        norm_mean,
    )


def solution(mesh):
    rows = P("batch", None)
    cols = P(None, "batch")
    block = P("batch", None, None)
    pair = P(None, "batch", None)
    return jax.shard_map(
        per_device,
        mesh=mesh,
        in_specs=(
            rows,
            rows,
            rows,
            P("batch"),
            block,
            rows,
            cols,
            block,
            rows,
            P("batch"),
            cols,
            pair,
            cols,
            pair,
            cols,
            rows,
        ),
        out_specs=(
            rows,
            rows,
            rows,
            block,
            rows,
            cols,
            block,
            rows,
            P("batch"),
            cols,
            pair,
            cols,
            pair,
            cols,
            P(),
        ),
        check_vma=False,
    )
```

```python
import functools
import math

import jax
import jax.numpy as jnp
from jax import lax
from jax.experimental import pallas as pl
from jax.experimental.pallas import tpu as pltpu
from jax.sharding import PartitionSpec as P

HD = 128
EPSILON = 1e-05
MASKED = -1e30
BF = jnp.bfloat16
F32 = jnp.float32
ALL = ("batch", "section")
MESH = pl.DeviceIdType.MESH
GATHER_WIDTH = 1024
AHEAD = 4
LOCAL = 1
SLOTS = 3
GATHERED = tuple(
    (4 * layer + index, start)
    for layer in range(2)
    for index, start in (
        [(0, 0), (0, 1024), (0, 2048), (1, 0)]
        + [(2 + which, chunk) for chunk in range(0, 2048, 1024) for which in range(2)]
    )
)


def mm(a, b):
    return jnp.dot(a, b, preferred_element_type=F32)


def mm_rows(a, b):
    return lax.dot_general(a, b, (((0,), (0,)), ((), ())), preferred_element_type=F32)


def mm_cols(a, b):
    return lax.dot_general(a, b, (((1,), (1,)), ((), ())), preferred_element_type=F32)


def unit_rows(values):
    centred = values - jnp.mean(values, axis=-1, keepdims=True)
    inverse = lax.rsqrt(jnp.mean(centred * centred, axis=-1, keepdims=True) + EPSILON)
    return centred * inverse, inverse


def norm_back(gradient, unit, inverse, gain):
    scaled = gradient * gain
    inner = (
        scaled
        - jnp.mean(scaled, axis=-1, keepdims=True)
        - unit * jnp.mean(scaled * unit, axis=-1, keepdims=True)
    )
    return inverse * inner, jnp.sum(gradient * unit, axis=0)


def heads_of(rows):
    return rows.reshape(rows.shape[0], -1, HD)


def softmax(q, k, valid):
    scores = jnp.einsum(
        "lhc,nhc->hln", heads_of(q), heads_of(k), preferred_element_type=F32
    ) * (1.0 / math.sqrt(HD))
    if valid is not None:
        scores = jnp.where(valid[None, None, :], scores, MASKED)
    grown = jnp.exp(scores - jnp.max(scores, axis=-1, keepdims=True))
    return grown / jnp.sum(grown, axis=-1, keepdims=True)


def attend(inputs, source, valid, gain_q, gain_kv, proj, out):
    unit_x, inv_x = unit_rows(inputs)
    queries_in = (unit_x * gain_q).astype(BF)
    unit_s, inv_s = unit_rows(source)
    keys_in = (unit_s * gain_kv).astype(BF)
    width = inputs.shape[1]
    q = mm(queries_in, proj[:, :width]).astype(BF)
    kv = mm(keys_in, proj[:, width:]).astype(BF)
    k, v = kv[:, :width], kv[:, width:]
    soft = softmax(q, k, valid)
    mixture = jnp.einsum("hln,nhc->lhc", soft.astype(BF), heads_of(v), preferred_element_type=F32)
    mixture = mixture.reshape(inputs.shape).astype(BF)
    result = (inputs + mm(mixture, out)).astype(BF)
    return result, (unit_x, inv_x, queries_in, unit_s, inv_s, keys_in, q, k, v, soft, mixture)


def attend_back(gradient, kept, gain_q, gain_kv, proj, out):
    unit_x, inv_x, queries_in, unit_s, inv_s, keys_in, q, k, v, soft, mixture = kept
    width = gradient.shape[1]
    scale = 1.0 / math.sqrt(HD)
    grad_mix = mm_cols(gradient, out).astype(BF)
    grad_soft = jnp.einsum(
        "lhc,nhc->hln", heads_of(grad_mix), heads_of(v), preferred_element_type=F32
    )
    inner = jnp.sum(soft * grad_soft, axis=-1, keepdims=True)
    grad_scores = (soft * (grad_soft - inner)).astype(BF)
    dq = jnp.einsum("hln,nhc->lhc", grad_scores, heads_of(k), preferred_element_type=F32) * scale
    dk = jnp.einsum("hln,lhc->nhc", grad_scores, heads_of(q), preferred_element_type=F32) * scale
    dv = jnp.einsum(
        "hln,lhc->nhc", soft.astype(BF), heads_of(grad_mix), preferred_element_type=F32
    )
    dq = dq.reshape(gradient.shape).astype(BF)
    dk = dk.reshape(-1, width).astype(BF)
    dv = dv.reshape(-1, width).astype(BF)
    grad_x, gain_q_grad = norm_back(mm_cols(dq, proj[:, :width]), unit_x, inv_x, gain_q)
    back_s = mm_cols(dk, proj[:, width : 2 * width]) + mm_cols(dv, proj[:, 2 * width :])
    grad_s, gain_kv_grad = norm_back(back_s, unit_s, inv_s, gain_kv)
    pairs = ((queries_in, dq), (keys_in, dk), (keys_in, dv), (mixture, gradient))
    return grad_x, grad_s, gain_q_grad, gain_kv_grad, pairs


def feed(inputs, gain, w_in, b_in, w_down, b_out):
    unit, inverse = unit_rows(inputs)
    lowered = (unit * gain).astype(BF)
    pre_act = mm(lowered, w_in) + b_in
    active = jax.nn.gelu(pre_act).astype(BF)
    result = (inputs + mm_cols(active, w_down) + b_out).astype(BF)
    return result, (unit, inverse, lowered, pre_act, active)


def feed_back(gradient, kept, gain, w_in, w_down):
    unit, inverse, lowered, pre_act, active = kept
    grad_act = mm(gradient, w_down)
    grad_pre = jax.vjp(jax.nn.gelu, pre_act)[1](grad_act)[0].astype(BF)
    grad_x, gain_grad = norm_back(mm_cols(grad_pre, w_in), unit, inverse, gain)
    bias_grad = jnp.sum(grad_pre.astype(F32), axis=0)
    out_grad = jnp.sum(gradient.astype(F32), axis=0)
    return grad_x, gain_grad, bias_grad, out_grad, ((lowered, grad_pre), (gradient, active))


def gelu_both(value):
    factor = math.sqrt(2.0 / math.pi)
    square = value * value
    bent = jnp.tanh(factor * value * (1.0 + 0.044715 * square))
    inner = factor * (1.0 + 3.0 * 0.044715 * square)
    half = 0.5 * (1.0 + bent)
    return value * half, half + 0.5 * value * (1.0 - bent * bent) * inner


def tiles(count, body, size=256):
    def step(index, carry):
        body(pl.ds(pl.multiple_of(index * size, size), size), index)
        return carry

    lax.fori_loop(0, count, step, 0)


def norm_into(source, gain, target):
    def step(index, carry):
        here = pl.ds(pl.multiple_of(index * 32, 32), 32)
        unit, _ = unit_rows(source[here, :].astype(F32))
        target[here, :] = (unit * gain).astype(BF)
        return carry

    lax.fori_loop(0, source.shape[0] // 32, step, 0)


def gather_kernel(*refs):
    cross_proj, cross_out, mlp_in, mlp_down, self_proj, self_out = refs[:6]
    latents_in, cot_all, points_in, near_in, length_in = refs[6:11]
    vec_parts = refs[11:16]
    section_at = lax.axis_index("section")
    batch_at = lax.axis_index("batch")
    x_at = lax.rem(section_at, 2)
    y_at = section_at // 2
    ins = (
        cross_proj,
        cross_out,
        mlp_in.at[0],
        mlp_down.at[0],
        self_proj,
        self_out,
        mlp_in.at[1],
        mlp_down.at[1],
    )
    count = len(ins)
    outs = refs[16 : 16 + count]
    rest = refs[16 + count :]
    gains, norm_out, mask_in, picks_out = rest[:4]
    kept_outs = rest[4:24]
    (
        u1,
        u2,
        u3,
        u4,
        grad_top,
        xq_c,
        sn_c,
        q_c,
        k_c,
        v_c,
        o_c,
        xn_s,
        q_s,
        k_s,
        v_s,
        o_s,
        src_in,
        lowered,
        before,
        active,
        x_in,
        cot_in,
        vec_in,
        vec_rows,
        slots,
        total_rows,
        part_out,
        part_in,
        vec_out,
        biases,
        plane,
        line_in,
    ) = rest[24:56]
    (own_sem, send, recv, kin_send, kin_recv, vec_sems) = rest[56:62]
    (slot_sems, kept_sems, plane_sems, line_sems, pair_sems, row_sems) = rest[62:]
    line = 4
    core = lax.rem(batch_at, 2)
    spot = batch_at // 2
    beside = section_at + 1 - 2 * x_at
    above = lax.rem(section_at + 2, 4)
    sibling = batch_at + 1 - 2 * core
    shard = ins[0].shape[0]
    place = section_at * 2 + core
    rows = x_in.shape[0]

    def down_line(step):
        return lax.rem(spot + step, line) * 2 + core

    def up_line(step):
        return lax.rem(spot + line - step, line) * 2 + core

    near_peers = []
    for turn in range(1, 8):
        other = lax.rem(place + turn, 8)
        near_peers.append((other // 2, spot * 2 + lax.rem(other, 2)))
    line_peers = [(section_at, down_line(step)) for step in range(1, line)]
    far_peers = [(section_at, down_line(step) + 1 - 2 * core) for step in range(1, line)]
    vec_peers = [(section_at, sibling)] + line_peers + far_peers
    peers = near_peers + line_peers + far_peers
    barrier = pltpu.get_barrier_semaphore()
    for peer in peers:
        pl.semaphore_signal(barrier, inc=1, device_id=peer, device_id_type=MESH)
    pl.semaphore_wait(barrier, len(peers))

    def spread(ref, owner, first, size):
        return ref.at[pl.ds(pl.multiple_of(owner * shard, shard), shard), pl.ds(first, size)]

    def is_feed(item):
        return item % 8 >= 4

    def source_of(item, first, size):
        index, start = GATHERED[item]
        if is_feed(item):
            first = pl.multiple_of(first + y_at * outs[index].shape[1], 128)
        return ins[index].at[:, pl.ds(first, size)]

    def piece(item):
        start = GATHERED[item][1]
        if is_feed(item):
            return pl.multiple_of(start + x_at * 512, 128), 512
        return pl.multiple_of(start + section_at * 256, 128), 256

    def own_line(item, way):
        first, size = piece(item)
        return pltpu.make_async_remote_copy(
            source_of(item, first, size),
            spread(outs[GATHERED[item][0]], batch_at, first, size),
            send.at[5 * way, item, 0],
            recv.at[0, item, 3 if way else 1],
            device_id=(section_at, batch_at + (-2 if way else 2)),
            device_id_type=MESH,
        )

    def onward_line(item, step, way):
        first, size = piece(item)
        ref = spread(outs[GATHERED[item][0]], up_line(step), first, size)
        return pltpu.make_async_remote_copy(
            ref,
            ref,
            send.at[0, item, step],
            recv.at[0, item, step - 1 if way else step + 1],
            device_id=(section_at, batch_at + (-2 if way else 2)),
            device_id_type=MESH,
        )

    def came_line(item, step):
        first, size = piece(item)
        ref = spread(outs[GATHERED[item][0]], up_line(step), first, size)
        return pltpu.make_async_remote_copy(
            ref,
            ref,
            send.at[0, item, step],
            recv.at[0, item, step],
            device_id=(section_at, sibling),
            device_id_type=MESH,
        )

    def start_line(item):
        @pl.when(spot < 3)
        def _():
            own_line(item, 0).start()

        @pl.when(spot > 0)
        def _():
            own_line(item, 1).start()

    def arrive_line(item, apart):
        @pl.when(spot >= apart)
        def _():
            came_line(item, apart).wait_recv()

            @pl.when(spot < 3)
            def _():
                onward_line(item, apart, 0).start()

            for copy in near(item, apart):
                copy.start()

        @pl.when(spot + apart <= 3)
        def _():
            came_line(item, 4 - apart).wait_recv()

            @pl.when(spot > 0)
            def _():
                onward_line(item, 4 - apart, 1).start()

            for copy in near(item, 4 - apart):
                copy.start()

    def sent_line(item):
        @pl.when(spot < 3)
        def _():
            own_line(item, 0).wait_send()

        @pl.when(spot > 0)
        def _():
            own_line(item, 1).wait_send()

        for apart in (1, 2, 3):

            @pl.when(jnp.logical_and(spot >= apart, spot < 3))
            def _():
                onward_line(item, apart, 0).wait_send()

            @pl.when(jnp.logical_and(spot + apart <= 3, spot > 0))
            def _():
                onward_line(item, 4 - apart, 1).wait_send()

        for step in (1, 2, 3):
            for copy in near(item, step):
                copy.wait_send()

    def plane_copy(item, step, way, low, wide, peer):
        ref = spread(outs[GATHERED[item][0]], up_line(step), low, wide)
        return pltpu.make_async_remote_copy(
            ref,
            ref,
            send.at[way, item, step],
            recv.at[way, item, step],
            device_id=(peer, batch_at),
            device_id_type=MESH,
        )

    def near(item, step):
        first, size = piece(item)
        copies = [plane_copy(item, step, 1, first, size, beside)]
        if not is_feed(item):
            copies.append(plane_copy(item, step, 2, first, size, above))
        return copies

    def far(item, step):
        start = GATHERED[item][1]
        by_x = pl.multiple_of(start + above * 256, 128)
        return [plane_copy(item, step, 4, by_x, 256, beside)]

    def kin(item, step):
        index, start = GATHERED[item]
        if step == 0:
            source = source_of(item, start, GATHER_WIDTH)
        else:
            source = spread(outs[index], up_line(step), start, GATHER_WIDTH)
        return pltpu.make_async_remote_copy(
            source,
            spread(outs[index], up_line(step), start, GATHER_WIDTH),
            kin_send.at[item, step],
            kin_recv.at[item, step],
            device_id=(section_at, sibling),
            device_id_type=MESH,
        )

    def own(item):
        index, start = GATHERED[item]
        return pltpu.make_async_copy(
            source_of(item, start, GATHER_WIDTH),
            spread(outs[index], batch_at, start, GATHER_WIDTH),
            own_sem.at[item],
        )

    def vec_copy(which):
        return pltpu.make_async_remote_copy(
            vec_in,
            vec_out.at[batch_at],
            vec_sems.at[0, which],
            vec_sems.at[1, which],
            device_id=vec_peers[which],
            device_id_type=MESH,
        )

    def slot_copy(item):
        index, start = GATHERED[item]
        return pltpu.make_async_copy(
            outs[index].at[:, pl.ds(start, GATHER_WIDTH)],
            slots.at[item % SLOTS],
            slot_sems.at[item % SLOTS],
        )

    def near_norm(turn):
        return pltpu.make_async_remote_copy(
            plane.at[8],
            plane.at[place],
            plane_sems.at[0, turn],
            plane_sems.at[1, turn],
            device_id=near_peers[turn],
            device_id_type=MESH,
        )

    def far_norm(step):
        return pltpu.make_async_remote_copy(
            line_in.at[4],
            line_in.at[spot],
            line_sems.at[0, step],
            line_sems.at[1, step],
            device_id=line_peers[step],
            device_id_type=MESH,
        )

    def rows_over(layer):
        return pltpu.make_async_remote_copy(
            lowered.at[layer, pl.ds(0, rows)],
            lowered.at[layer, pl.ds(rows, rows)],
            pair_sems.at[0, layer, 0],
            pair_sems.at[1, layer, 0],
            device_id=(above, batch_at),
            device_id_type=MESH,
        )

    def part_over(layer):
        return pltpu.make_async_remote_copy(
            part_out.at[layer],
            part_in.at[layer],
            pair_sems.at[0, layer, 1],
            pair_sems.at[1, layer, 1],
            device_id=(above, batch_at),
            device_id_type=MESH,
        )

    steps = range(1, line)
    total = len(GATHERED)
    started = []

    def launch(copies):
        for copy in copies:
            copy.start()
        started.extend(copies)

    kept = (
        (u1, u2, u3, u4, grad_top)
        + (xq_c, sn_c, q_c, k_c, v_c, o_c)
        + (xn_s, q_s, k_s, v_s, o_s)
        + (src_in, lowered, before, active)
    )
    names = {id(ref): place for place, ref in enumerate(kept)}

    def keep(*chosen):
        for ref in chosen:
            index = names[id(ref)]
            pltpu.make_async_copy(ref, kept_outs[index], kept_sems.at[index]).start(priority=LOCAL)

    def row(index):
        return gains[index : index + 1, :]

    def project(source, target, slot):
        def tile(columns, _):
            target[:, columns] = mm(source[...], slots[slot, :, columns]).astype(BF)

        tiles(2, tile, 512)

    def heads(q, k, v, o, masked):
        def head(index, carry):
            here = pl.ds(pl.multiple_of(index * HD, HD), HD)
            scores = mm_cols(q[:, here], k[:, here]) * (1.0 / math.sqrt(HD))
            if masked:
                scores = jnp.where(mask_in[...] > 0.0, scores, MASKED)
            grown = jnp.exp(scores - jnp.max(scores, axis=-1, keepdims=True))
            soft = grown / jnp.sum(grown, axis=-1, keepdims=True)
            o[:, here] = mm(soft.astype(BF), v[:, here]).astype(BF)
            return carry

        lax.fori_loop(0, q.shape[1] // HD, head, 0)

    def close_attention(inputs, o, target, slot):
        def tile(columns, _):
            target[:, columns] = (
                inputs[:, columns].astype(F32) + mm(o[...], slots[slot, :, columns])
            ).astype(BF)

        tiles(2, tile, 512)

    def feed_up(layer, chunk, slot):
        def tile(columns, index):
            first = chunk * GATHER_WIDTH + index * 512
            there = pl.ds(pl.multiple_of(first, 512), 512)
            lanes = pl.ds(pl.multiple_of(y_at * 2048 + first, 512), 512)
            value = mm(lowered[layer], slots[slot, :, columns]) + biases[layer : layer + 1, lanes]
            active_part, slope = gelu_both(value)
            before[layer, :, there] = slope
            active[layer, :, there] = active_part.astype(BF)

        tiles(2, tile, 512)

    def feed_down(layer, chunk, slot):
        chosen = pl.ds(chunk * GATHER_WIDTH, GATHER_WIDTH)

        def tile(columns, _):
            value = mm_cols(active[layer, :, chosen], slots[slot, columns, :])
            if chunk == 0:
                total_rows[:, columns] = value
            else:
                value = total_rows[:, columns] + value
                total_rows[:, columns] = value
                part_out[layer, :, columns] = value[rows:].astype(BF)

        tiles(2, tile, 512)

    def feed_close(layer):
        inputs, target = (u1, u3)[layer], (u2, u4)[layer]
        part_over(layer).wait_recv()

        def tile(columns, _):
            target[:, columns] = (
                inputs[:, columns].astype(F32)
                + (total_rows[0:rows, columns] + part_in[layer, :, columns].astype(F32))
                + gains[5 + layer : 6 + layer, columns]
            ).astype(BF)

        tiles(2, tile, 512)
        keep(target)

    def work(item):
        slot_copy(item).wait()
        slot = item % SLOTS
        layer, stage = item // 8, item % 8
        inputs = (x_in, u2)[layer]
        middle = (u1, u3)[layer]
        q, k, v, o = ((q_c, k_c, v_c, o_c), (q_s, k_s, v_s, o_s))[layer]
        if stage == 0:
            if layer == 0:
                norm_into(x_in, row(0), xq_c)
                norm_into(src_in, row(1), sn_c)
                keep(xq_c, sn_c)
            else:
                feed_close(0)
                norm_into(u2, row(2), xn_s)
                keep(xn_s)
            project((xq_c, xn_s)[layer], q, slot)
        elif stage == 1:
            project((sn_c, xn_s)[layer], k, slot)
        elif stage == 2:
            project((sn_c, xn_s)[layer], v, slot)
            heads(q, k, v, o, layer == 0)
            keep(q, k, v, o)
        elif stage == 3:
            close_attention(inputs, o, middle, slot)
            norm_into(middle, row(3 + layer), lowered.at[layer, pl.ds(0, rows)])
            launch([rows_over(layer)])
            keep(middle)
        elif stage % 2 == 0:
            if stage == 4:
                rows_over(layer).wait_recv()
            feed_up(layer, (stage - 4) // 2, slot)
        else:
            feed_down(layer, (stage - 4) // 2, slot)
            if stage == 7:
                launch([part_over(layer)])

    for item in range(AHEAD):
        start_line(item)
    here = pl.ds(pl.multiple_of(section_at * rows, rows), rows)
    row_copies = [
        pltpu.make_async_copy(latents_in.at[here], x_in, row_sems.at[0]),
        pltpu.make_async_copy(cot_all.at[here], cot_in, row_sems.at[1]),
    ]
    for copy in row_copies:
        copy.start()
    cross_gain, self_gain, feed_gain, out_bias, in_bias = vec_parts
    vec_rows[...] = jnp.zeros_like(vec_rows)
    vec_rows[0:2, :] = cross_gain[...].astype(F32)
    vec_rows[2:3, :] = self_gain[...].astype(F32)
    vec_rows[3:5, :] = feed_gain[...].astype(F32)
    vec_rows[5:7, :] = out_bias[...].astype(F32)
    bias_rows = in_bias[...].astype(F32)
    for layer in range(2):
        for part_at in range(4):
            index = 7 + 4 * layer + part_at
            vec_rows[index : index + 1, :] = bias_rows[
                layer : layer + 1, part_at * 128 : part_at * 128 + 128
            ]
    vec_in[...] = vec_rows[...].astype(BF)
    vec_out[batch_at] = vec_in[...]
    for which in range(7):
        vec_copy(which).start()
    lanes = lax.broadcasted_iota(jnp.int32, (1, rows), 1)
    length = length_in[pl.ds(section_at, 1), :]
    mask_in[...] = jnp.where(lanes < length, 1.0, 0.0)
    point_at = lax.broadcasted_iota(jnp.int32, (points_in.shape[0], rows), 0)
    wanted = near_in[pl.ds(section_at, 1), :]
    picks = jnp.where(point_at == wanted, 1.0, 0.0)
    picks_out[...] = picks.astype(BF)
    turned = picks.T.astype(BF)

    def source_tile(columns, _):
        src_in[:, columns] = mm(turned, points_in[:, columns]).astype(BF)

    tiles(2, source_tile, 512)
    keep(src_in)
    for copy in row_copies:
        copy.wait()
    for moment in range(-2, total + 4):
        if moment + 2 + AHEAD < total:
            start_line(moment + 2 + AHEAD)
        for apart in (1, 2, 3):
            if 0 <= moment + 3 - apart < total:
                arrive_line(moment + 3 - apart, apart)
        if 0 <= moment < total:
            own(moment).start(priority=LOCAL)
            launch([kin(moment, 0)])
        if 0 <= moment - 1 < total:
            for step in steps:
                if is_feed(moment - 1):
                    near(moment - 1, step)[0].wait_recv()
                    launch([kin(moment - 1, step)])
                else:
                    by_beside, by_above = near(moment - 1, step)
                    by_above.wait_recv()
                    launch(far(moment - 1, step))
                    by_beside.wait_recv()
        if 0 <= moment - 2 < total and not is_feed(moment - 2):
            for step in steps:
                for copy in far(moment - 2, step):
                    copy.wait_recv()
                launch([kin(moment - 2, step)])
        if moment == 2:
            for which in range(7):
                vec_copy(which).wait()
            for owner in range(8):
                values = vec_out[owner].astype(F32)
                gains[:, owner * 128 : owner * 128 + 128] = values
                for layer in range(2):
                    for part_at in range(4):
                        first = owner * 512 + part_at * 128
                        index = 7 + 4 * layer + part_at
                        biases[layer : layer + 1, first : first + 128] = values[index : index + 1]
        if 0 <= moment - 4 < total:
            work(moment - 4)
        if 0 <= moment - 3 < total:
            own(moment - 3).wait()
            for step in range(line):
                kin(moment - 3, step).wait_recv()
            slot_copy(moment - 3).start(priority=LOCAL)
    keep(lowered, before, active)
    feed_close(1)

    def square(index, carry):
        here = pl.ds(pl.multiple_of(index * 32, 32), 32)
        values = u4[here, :].astype(F32)
        return carry + jnp.sum(values * values, axis=0, keepdims=True)

    squares = lax.fori_loop(0, u4.shape[0] // 32, square, jnp.zeros((1, u4.shape[1]), F32))
    mean = jnp.sum(squares, axis=1, keepdims=True) / (u4.shape[0] * u4.shape[1])
    group_norm = jnp.sqrt(mean + EPSILON)
    plane[8] = jnp.broadcast_to(group_norm, plane.shape[1:])
    for turn in range(7):
        near_norm(turn).start()
    plane[place] = plane[8]
    for turn in range(7):
        near_norm(turn).wait()
    line_in[4] = jnp.sum(plane[0:8], axis=0)
    for step in range(3):
        far_norm(step).start()
    line_in[spot] = line_in[4]
    for step in range(3):
        far_norm(step).wait()
    norm_mean = jnp.sum(line_in[0:4], axis=0) / 32.0
    norm_out[...] = norm_mean
    ratio = norm_mean[0:1, 0:1] / group_norm

    def top(index, carry):
        here = pl.ds(pl.multiple_of(index * 32, 32), 32)
        grad_top[here, :] = (
            cot_in[here, :].astype(F32) + ratio * u4[here, :].astype(F32)
        ).astype(BF)
        return carry

    lax.fori_loop(0, u4.shape[0] // 32, top, 0)
    keep(grad_top)
    for index, ref in enumerate(kept):
        pltpu.make_async_copy(ref, kept_outs[index], kept_sems.at[index]).wait()
    for item in range(total):
        sent_line(item)
    for copy in started:
        copy.wait_send()


def gather_forward(blocks, latents, cotangent, points, near, lengths, vectors):
    width = latents.shape[1]
    rows = near.shape[1]
    half = blocks[2].shape[2] // 2
    widths = (3 * width, width, half, half) * 2
    total = len(GATHERED)
    anywhere = pl.BlockSpec(memory_space=pl.ANY)
    vmem = pl.BlockSpec(memory_space=pltpu.VMEM)
    plain = ((rows, width), BF)
    kept = [plain] * 17 + [
        ((2, 2 * rows, width), BF),
        ((2, 2 * rows, half), F32),
        ((2, 2 * rows, half), BF),
    ]
    dma = pltpu.SemaphoreType.DMA
    return pl.pallas_call(
        gather_kernel,
        out_shape=[jax.ShapeDtypeStruct((width, size), BF) for size in widths]
        + [
            jax.ShapeDtypeStruct((16, width), F32),
            jax.ShapeDtypeStruct((8, 128), F32),
            jax.ShapeDtypeStruct((1, rows), F32),
            jax.ShapeDtypeStruct((points.shape[0], rows), BF),
        ]
        + [jax.ShapeDtypeStruct(*one) for one in kept],
        in_specs=[anywhere] * (len(blocks) + 2) + [vmem] * 8,
        out_specs=[anywhere] * len(widths) + [vmem] * 4 + [anywhere] * len(kept),
        scratch_shapes=[pltpu.VMEM(*one) for one in kept]
        + [
            pltpu.VMEM((rows, width), BF),
            pltpu.VMEM((rows, width), BF),
            pltpu.VMEM((16, 128), BF),
            pltpu.VMEM((16, 128), F32),
            pltpu.VMEM((SLOTS, width, GATHER_WIDTH), BF),
            pltpu.VMEM((2 * rows, width), F32),
            pltpu.VMEM((2, rows, width), BF),
            pltpu.VMEM((2, rows, width), BF),
            pltpu.VMEM((8, 16, 128), BF),
            pltpu.VMEM((2, 2 * half), F32),
            pltpu.VMEM((9, 8, 128), F32),
            pltpu.VMEM((5, 8, 128), F32),
            dma((total,)),
            dma((6, total, 4)),
            dma((5, total, 4)),
            dma((total, 4)),
            dma((total, 4)),
            dma((2, 7)),
            dma((SLOTS,)),
            dma((len(kept),)),
            dma((2, 7)),
            dma((2, 3)),
            dma((2, 2, 2)),
            dma((2,)),
        ],
        compiler_params=pltpu.CompilerParams(
            collective_id=1, has_side_effects=True, vmem_limit_bytes=56 * 2**20
        ),
        cost_estimate=pl.CostEstimate(
            flops=2 * rows * width * sum(widths), bytes_accessed=2**27, transcendentals=2**21
        ),
    )(*blocks, latents, cotangent, points, near, lengths, *vectors)


ITEM_COUNT = 16
FEEDS = (0, 1, 2, 4, 6, 9, 10, 13)
ATTENDS = (3, 5, 7, 8, 11, 12, 14, 15)
WINDOWS = 4
STAGES = 3


def reduce_kernel(*refs):
    total = ITEM_COUNT
    (
        proj_c,
        out_c,
        in_0,
        down_0,
        proj_s,
        out_s,
        in_1,
        down_1,
        u1_in,
        u2_in,
        u3_in,
        last_ref,
        top_in,
        xq_c,
        sn_c,
        q_c,
        k_c,
        v_c,
        o_c,
        xn_s,
        q_s,
        k_s,
        v_s,
        o_s,
        lowered,
        before,
        active,
        latents_in,
        src_in,
        gains,
        mask_in,
        picks_in,
    ) = refs[:32]
    (up_out, down_out, proj_out_c, proj_out_s, end_out_c, end_out_s) = refs[32:38]
    (last_out, first_out, point_out, small_out) = refs[38:42]
    (grads_h, kin_lf, kin_la, kin_rf, kin_ra) = refs[42:47]
    (
        lwin_f,
        lwin_a,
        raw,
        rwin,
        stage,
        merged_f,
        merged_a,
        passing_f,
        passing_a,
        lined_f,
        lined_a,
        crossed_f,
        crossed_a,
        pair,
        slope,
        rows_sum,
        hbuf,
        slots,
        qb,
        kb,
        vb,
        dob,
        dqkv,
        part_out,
        part_in,
        grad,
        ub,
        point_in,
        point_sum,
        small_in,
        small_sum,
    ) = refs[47:78]
    (
        kin_l_sems,
        kin_r_sems,
        raw_sems,
        win_sems,
        xy_sems,
        line_send,
        line_recv,
        cross_sems,
        out_sems,
        own_sems,
        lat_sems,
        far_sems,
        lat_own,
        point_sems,
        deal_sems,
        point_own,
        small_sems,
        pair_sems,
        slot_sems,
        h_sem,
        save_sems,
        act_sems,
    ) = refs[78:]
    section_at = lax.axis_index("section")
    batch_at = lax.axis_index("batch")
    core = lax.rem(batch_at, 2)
    spot = batch_at // 2
    x_at = lax.rem(section_at, 2)
    y_at = section_at // 2
    beside = section_at + 1 - 2 * x_at
    above = lax.rem(section_at + 2, 4)
    across = lax.rem(beside + 2, 4)
    sibling = batch_at + 1 - 2 * core
    flat = (beside, above)
    bits = (x_at, y_at)
    rows, width = 256, 1024

    peers = [(beside, batch_at), (above, batch_at), (across, batch_at), (section_at, sibling)]
    peers += [(section_at, lax.rem(spot + step, 4) * 2 + core) for step in (1, 2, 3)]
    barrier = pltpu.get_barrier_semaphore()
    for peer in peers:
        pl.semaphore_signal(barrier, inc=1, device_id=peer, device_id_type=MESH)
    pl.semaphore_wait(barrier, len(peers))

    def remote(source, target, sems, where, peer):
        return pltpu.make_async_remote_copy(
            source,
            target,
            sems.at[(0, *where)],
            sems.at[(1, *where)],
            device_id=peer,
            device_id_type=MESH,
        )

    feed_left = (pair, lowered.at[1], pair, lowered.at[0])
    feed_right = (active.at[1], slope, active.at[0], slope)
    att_left = (o_s, xn_s, xn_s, xn_s, o_c, xq_c, sn_c, sn_c)
    att_right = tuple(
        ref
        for turn in range(2)
        for ref in (grads_h.at[turn], dqkv.at[0], dqkv.at[1], dqkv.at[2])
    )

    def columns(spot_of, parity):
        return pl.ds(pl.multiple_of((2 * spot_of + parity) * 128, 128), 128)

    def kin_lefts(feed, job):
        source, target = (feed_left, kin_lf) if feed else (att_left, kin_la)
        return [
            remote(
                source[job].at[:, columns(part, 1 - core)],
                target.at[job, part],
                kin_l_sems,
                (job if feed else 4 + job, part),
                (section_at, sibling),
            )
            for part in range(4)
        ]

    def kin_right(feed, job, chunk):
        if feed:
            here = pl.ds(chunk * 1024, 1024)
            source, target = feed_right[job].at[:, here], kin_rf.at[job, :, here]
        else:
            source, target = att_right[job], kin_ra.at[job]
        where = (2 * job + chunk if feed else 8 + job,)
        return remote(source, target, kin_r_sems, where, (section_at, sibling))

    def item_of(index):
        if index in FEEDS:
            order = FEEDS.index(index)
            return True, order // 2, order % 2
        return False, ATTENDS.index(index), 0

    def window_copies(index):
        feed, job, chunk = item_of(index)
        slot = index % WINDOWS
        size = 512 if feed else 256
        if feed:
            here = pl.ds(chunk * 1024, 1024)
            sources = (feed_right[job].at[:, here], kin_rf.at[job, :, here])
        else:
            sources = (att_right[job], kin_ra.at[job])
        return [
            pltpu.make_async_copy(
                sources[whose],
                rwin.at[slot, pl.ds(whose * size, size)],
                win_sems.at[slot, whose],
            )
            for whose in range(2)
        ]

    def raw_copies(index, part):
        feed, job, _ = item_of(index)
        size = 512 if feed else 256
        own_left = (feed_left if feed else att_left)[job]
        kin_left = (kin_lf if feed else kin_la).at[job]
        sources = (own_left.at[:, columns(part, core)], kin_left.at[part])
        return [
            pltpu.make_async_copy(
                source, raw.at[part, whose, pl.ds(0, size)], raw_sems.at[part, whose]
            )
            for whose, source in enumerate(sources)
        ]

    def raw_start(index):
        feed, job, chunk = item_of(index)
        if chunk == 0:
            for copy in kin_lefts(feed, job):
                copy.wait_recv()
            for part in range(4):
                for copy in raw_copies(index, part):
                    copy.start(priority=LOCAL)

    def load(index):
        feed, job, chunk = item_of(index)
        kin_right(feed, job, chunk).wait_recv()
        for copy in window_copies(index):
            copy.start(priority=LOCAL)
        if chunk == 0:
            if feed and job == 2:
                raw_start(index)
            size = 512 if feed else 256
            target = (lwin_f if feed else lwin_a).at[job]
            for part in range(4):
                for whose, copy in enumerate(raw_copies(index, part)):
                    copy.wait()
                    place = raw.at[part, whose, pl.ds(0, size)]
                    target[part, :, whose * size : whose * size + size] = place[...].T
        if index + 1 < total and item_of(index + 1)[:2] != (True, 2):
            raw_start(index + 1)

    def count_below(item, places):
        return sum((item > place).astype(jnp.int32) for place in places)

    def is_feed(item):
        return functools.reduce(jnp.logical_or, [item == place for place in FEEDS])

    def loaded(slot, feed):
        size = 512 if feed else 256
        for whose in range(2):
            source = kin_rf.at[0, :, pl.ds(0, 1024)] if feed else kin_ra.at[0]
            pltpu.make_async_copy(
                source, rwin.at[slot, pl.ds(whose * size, size)], win_sems.at[slot, whose]
            ).wait()

    def by_kind(item, action):
        @pl.when(is_feed(item))
        def _():
            action(count_below(item, FEEDS), True)

        @pl.when(jnp.logical_not(is_feed(item)))
        def _():
            action(count_below(item, ATTENDS), False)

    def mark(order, feed):
        return order if feed else 8 + order

    def merged_of(order, feed):
        return merged_f.at[lax.rem(order, 4)] if feed else merged_a.at[order]

    def passing_of(order, feed, slot):
        if feed:
            return passing_f.at[lax.rem(order, 6), slot]
        return passing_a.at[lax.rem(order, 4), slot]

    def lined_of(order, feed):
        return lined_f.at[lax.rem(order, 4)] if feed else lined_a.at[order]

    def crossed_of(order, feed):
        return crossed_f.at[lax.rem(order, 4)] if feed else crossed_a.at[order]

    def products(order, slot, choice, store):
        def quarter(index, carry):
            here = pl.ds(pl.multiple_of(index * 256, 256), 256)
            bit = choice[0] + index * (choice[1] - choice[0])
            first = pl.multiple_of(index * 512 + bit * 256, 256)
            left = lwin_a[order].reshape(512, 512)
            right = rwin[slot, 0:512, pl.ds(first, 256)]
            tile = jnp.dot(left, right, preferred_element_type=F32).reshape(4, 128, 256)
            store(pl.ds(0, 4), here, tile)
            return carry

        lax.fori_loop(0, 2, quarter, 0)

    def xy_copies(item):
        return [
            remote(
                stage.at[lax.rem(item, STAGES), :, :, pl.ds(side * 256, 256)],
                merged_a.at[item, :, :, pl.ds(side * 256, 256)],
                xy_sems,
                (item, side),
                (flat[side], batch_at),
            )
            for side in range(2)
        ]

    def xy_sent(item):
        for copy in xy_copies(item):
            copy.wait_send()

    def line_copy(item, feed, dest, place, rightward):
        step = 1 if rightward else -1
        slot = 4 if not rightward and place - 1 == dest else dest
        return pltpu.make_async_remote_copy(
            merged_of(item, feed).at[dest],
            passing_of(item, feed, slot),
            line_send.at[mark(item, feed), dest],
            line_recv.at[mark(item, feed), slot],
            device_id=(section_at, batch_at + 2 * step),
            device_id_type=MESH,
        )

    def line_wait(item, feed, slot):
        pltpu.make_async_remote_copy(
            merged_of(item, feed).at[0],
            passing_of(item, feed, slot),
            line_send.at[mark(item, feed), 0],
            line_recv.at[mark(item, feed), slot],
            device_id=(section_at, sibling),
            device_id_type=MESH,
        ).wait_recv()

    def line_sent(item, feed):
        for step in (1, 2, 3):
            dest = lax.rem(spot + step, 4)
            pltpu.make_async_remote_copy(
                merged_of(item, feed).at[dest],
                passing_of(item, feed, 0),
                line_send.at[mark(item, feed), dest],
                line_recv.at[mark(item, feed), 0],
                device_id=(section_at, sibling),
                device_id_type=MESH,
            ).wait_send()

    def outset(item, feed):
        @pl.when(spot == 0)
        def _():
            for dest in (3, 2, 1):
                line_copy(item, feed, dest, 0, True).start()

        @pl.when(spot == 3)
        def _():
            for dest in (0, 1, 2):
                line_copy(item, feed, dest, 3, False).start()

    def drained(item, feed):
        line_sent(item, feed)
        delivered(item, feed)

    def delivered(item, feed):
        if feed:
            feed_out(item, up_out).wait()
            feed_own(item, up_out).wait()
        else:
            for side in range(2):
                att_out(item, side, end_out_s, 0).wait()
                att_own(item, side, end_out_s, 0).wait()

    def offer(slot, item, feed):
        loaded(slot, feed)
        if feed:

            @pl.when(item >= 4)
            def _():
                line_sent(item - 4, True)

            target = merged_of(item, True)

            def tile(index, carry):
                here = pl.ds(pl.multiple_of(index * 256, 256), 256)
                left = lwin_f[item // 2].reshape(512, 1024)
                right = rwin[slot, :, here]
                value = jnp.dot(left, right, preferred_element_type=F32)
                target[:, :, here] = value.reshape(4, 128, 256).astype(BF)
                return carry

            lax.fori_loop(0, 4, tile, 0)
            outset(item, True)
        else:

            @pl.when(item >= STAGES)
            def _():
                xy_sent(item - STAGES)

            def store(blocks, here, tile):
                stage[lax.rem(item, STAGES), blocks, :, here] = tile.astype(BF)

            products(item, slot, (1 - x_at, 1 - y_at), store)
            for copy in xy_copies(item):
                copy.start()

    def take(slot, item, feed):
        for copy in xy_copies(item):
            copy.wait_recv()
        target = merged_a.at[item]

        def store(blocks, here, tile):
            target[blocks, :, here] = (tile + target[blocks, :, here].astype(F32)).astype(BF)

        products(item, slot, bits, store)
        outset(item, False)

    def relay(item, feed, dest, place, rightward):
        line_wait(item, feed, dest)
        target = merged_of(item, feed)
        arrived = passing_of(item, feed, dest)
        target[dest] = (target[dest].astype(F32) + arrived[...].astype(F32)).astype(BF)
        line_copy(item, feed, dest, place, rightward).start()

    def second_of(item, feed):
        @pl.when(spot == 1)
        def _():
            for dest in (3, 2):
                relay(item, feed, dest, 1, True)

        @pl.when(spot == 2)
        def _():
            for dest in (0, 1):
                relay(item, feed, dest, 2, False)

    def third_of(item, feed):
        @pl.when(spot == 1)
        def _():
            relay(item, feed, 0, 1, False)

        @pl.when(spot == 2)
        def _():
            relay(item, feed, 3, 2, True)

    def feed_cross(item):
        return remote(
            lined_of(item, True),
            crossed_of(item, True),
            cross_sems,
            (item, 0),
            (beside, batch_at),
        )

    def cross_copy(item, side):
        here = pl.ds(side * 256, 256)
        return remote(
            lined_of(item, False).at[:, here],
            crossed_of(item, False).at[:, here],
            cross_sems,
            (8 + item, side),
            (flat[1 - side], batch_at),
        )

    def feed_place(item, target):
        base = y_at * 2048 + lax.rem(item, 2) * 1024
        return target.at[1 - item // 4, :, pl.ds(pl.multiple_of(base, 1024), 1024)]

    def feed_out(item, target):
        return remote(
            lined_of(item, True),
            feed_place(item, target),
            out_sems,
            (item, 0),
            (above, batch_at),
        )

    def feed_own(item, target):
        return pltpu.make_async_copy(
            lined_of(item, True), feed_place(item, target), own_sems.at[item, 0]
        )

    def feed_write(item):
        @pl.when(lax.rem(item, 4) < 2)
        def _():
            feed_out(item, down_out).start()
            feed_own(item, down_out).start(priority=LOCAL)

        @pl.when(lax.rem(item, 4) >= 2)
        def _():
            feed_out(item, up_out).start()
            feed_own(item, up_out).start(priority=LOCAL)

    def att_place(item, side, target, inner):
        base = side * 512 + bits[side] * 256
        return target.at[inner, :, pl.ds(pl.multiple_of(base, 256), 256)]

    def att_out(item, side, target, inner):
        return remote(
            lined_of(item, False).at[:, pl.ds(side * 256, 256)],
            att_place(item, side, target, inner),
            out_sems,
            (8 + item, side),
            (flat[side], batch_at),
        )

    def att_own(item, side, target, inner):
        return pltpu.make_async_copy(
            lined_of(item, False).at[:, pl.ds(side * 256, 256)],
            att_place(item, side, target, inner),
            own_sems.at[8 + item, side],
        )

    def att_write(item):
        inner = lax.rem(item, 4) - 1
        for turn, proj, end in ((0, proj_out_s, end_out_s), (1, proj_out_c, end_out_c)):

            @pl.when(jnp.logical_and(item // 4 == turn, inner >= 0))
            def _():
                for side in range(2):
                    att_out(item, side, proj, inner).start()
                    att_own(item, side, proj, inner).start(priority=LOCAL)

            @pl.when(jnp.logical_and(item // 4 == turn, inner < 0))
            def _():
                for side in range(2):
                    att_out(item, side, end, 0).start()
                    att_own(item, side, end, 0).start(priority=LOCAL)

    def close_of(item, feed):
        if feed:

            @pl.when(item >= 4)
            def _():
                delivered(item - 4, True)

        for place in range(4):

            @pl.when(spot == place)
            def _():
                value = merged_of(item, feed)[place].astype(F32)
                if place > 0:
                    line_wait(item, feed, place)
                    value += passing_of(item, feed, place)[...].astype(F32)
                if place < 3:
                    line_wait(item, feed, 4)
                    value += passing_of(item, feed, 4)[...].astype(F32)
                lined_of(item, feed)[...] = value.astype(BF)

        if feed:
            feed_cross(item).start()
        else:
            for side in range(2):
                cross_copy(item, side).start()

    def finish_of(item, feed):
        if feed:
            feed_cross(item).wait()
        else:
            for side in range(2):
                cross_copy(item, side).wait()
        target = lined_of(item, feed)
        target[...] = (
            target[...].astype(F32) + crossed_of(item, feed)[...].astype(F32)
        ).astype(BF)
        if feed:
            feed_write(item)
        else:
            att_write(item)

    def small_copy(phase):
        if phase == 0:
            peer = (section_at, sibling)
        elif phase < 3:
            peer = (flat[phase - 1], batch_at)
        else:
            peer = (section_at, lax.rem(spot + phase - 2, 4) * 2 + core)
        return remote(
            small_sum.at[min(phase, 3)], small_in.at[phase], small_sems, (phase,), peer
        )

    quarter_rows = pair.shape[0] // 4

    def point_copy(which):
        peer = (beside, above, across)[which]
        return remote(
            pair.at[pl.ds(pl.multiple_of(peer * quarter_rows, 128), quarter_rows)],
            point_in.at[which],
            point_sems,
            (which,),
            (peer, batch_at),
        )

    def point_place():
        return point_out.at[pl.ds(pl.multiple_of(section_at * quarter_rows, 128), quarter_rows)]

    def point_deal(which):
        peer = (beside, above, across)[which]
        return remote(point_sum, point_place(), deal_sems, (which,), (peer, batch_at))

    def point_local():
        return pltpu.make_async_copy(point_sum, point_place(), point_own.at[0])

    pairs = ((last_ref, last_out), (grad, first_out))

    def lat_copy(which, way):
        source, target = pairs[which]
        return remote(
            source,
            target.at[pl.ds(pl.multiple_of(section_at * rows, rows), rows)],
            lat_sems,
            (which, way),
            (flat[way], batch_at),
        )

    def lat_far(which):
        target = pairs[which][1]
        part = target.at[pl.ds(pl.multiple_of(above * rows, rows), rows)]
        return remote(part, part, far_sems, (which, 0), (beside, batch_at))

    def lat_local(which):
        source, target = pairs[which]
        return pltpu.make_async_copy(
            source,
            target.at[pl.ds(pl.multiple_of(section_at * rows, rows), rows)],
            lat_own.at[which],
        )

    def lat_start(which):
        lat_local(which).start(priority=LOCAL)
        for way in range(2):
            lat_copy(which, way).start()

    def lat_onward(which):
        lat_copy(which, 1).wait_recv()
        lat_far(which).start()
        lat_copy(which, 0).wait_recv()

    loads = []
    for turn, (proj, out, up, down) in enumerate(
        ((proj_s, out_s, in_1, down_1), (proj_c, out_c, in_0, down_0))
    ):
        for chunk in range(2):
            loads += [down.at[:, pl.ds(chunk * 1024, 1024)], up.at[:, pl.ds(chunk * 1024, 1024)]]
        loads.append(out)
        loads += [proj.at[:, pl.ds(which * 1024, 1024)] for which in range(3)]

    def slot_copy(index):
        return pltpu.make_async_copy(loads[index], slots.at[index % 2], slot_sems.at[index % 2])

    def opened(index):
        slot_copy(index).wait()
        return index % 2

    def closed(index):
        if index + 2 < len(loads):
            slot_copy(index + 2).start(priority=LOCAL)

    def h_copy(index):
        layer, chunk = 1 - index // 2, index % 2
        return pltpu.make_async_copy(
            before.at[layer, :, pl.ds(chunk * 1024, 1024)], hbuf, h_sem.at[0]
        )

    def pair_over(turn):
        return remote(
            pair.at[pl.ds(0, rows)],
            pair.at[pl.ds(rows, rows)],
            pair_sems,
            (turn, 0),
            (above, batch_at),
        )

    def part_over(turn):
        return remote(
            part_out.at[turn], part_in.at[turn], pair_sems, (turn, 1), (above, batch_at)
        )

    def grad_saved(turn):
        return pltpu.make_async_copy(grad, grads_h.at[turn], save_sems.at[0])

    def act_copies(turn):
        chosen = ((q_s, k_s, v_s), (q_c, k_c, v_c))[turn]
        return [
            pltpu.make_async_copy(source, target, act_sems.at[index])
            for index, (source, target) in enumerate(zip(chosen, (qb, kb, vb)))
        ]

    def row_copy(index):
        if index == 3:
            source = latents_in.at[pl.ds(pl.multiple_of(section_at * rows, rows), rows)]
        else:
            source = (u3_in, u2_in, u1_in)[index]
        return pltpu.make_async_copy(source, ub, act_sems.at[3])

    def small_row(index, value):
        small_sum[0, index : index + 1, :] = value

    def open_pair(turn):
        pair[0:rows, :] = grad[...]
        pair_over(turn).start()

    def pair_ready(turn):
        pair_over(turn).wait()
        for copy in kin_lefts(True, 2 * turn):
            copy.start()

    def feed_chunk(turn, chunk):
        layer = 1 - turn
        base = 8 * turn + 2 * chunk
        h_copy(2 * turn + chunk).wait()
        if turn == 1:
            kin_right(True, 1, chunk).wait_send()
        slot = opened(base)

        def up_tile(here, index):
            there = pl.ds(pl.multiple_of(chunk * 1024 + index * 256, 256), 256)
            value = mm(pair[...], slots[slot, :, here]) * hbuf[:, here]
            short = value.astype(BF)
            slope[:, there] = short
            column = jnp.sum(short.astype(F32), axis=0, keepdims=True)
            for half in range(2):
                index_at = 7 + 4 * layer + 2 * half + chunk
                small_sum[0, index_at : index_at + 1, here] = jnp.where(
                    y_at == half, column, jnp.zeros_like(column)
                )

        tiles(4, up_tile)
        closed(base)
        if 2 * turn + chunk + 1 < 4:
            h_copy(2 * turn + chunk + 1).start(priority=LOCAL)
        kin_right(True, 2 * turn + 1, chunk).start()
        slot = opened(base + 1)

        def down_tile(there, _):
            value = mm_cols(slope[:, chunk * 1024 : chunk * 1024 + 1024], slots[slot, there, :])
            if chunk == 0:
                rows_sum[:, there] = value
            else:
                value = rows_sum[:, there] + value
                rows_sum[:, there] = value
                part_out[turn, :, there] = value[rows:].astype(BF)

        tiles(4, down_tile)
        closed(base + 1)
        if chunk == 1:
            if turn == 0:
                for copy in kin_lefts(True, 0):
                    copy.wait_send()
            part_over(turn).start()

    def row_steps(body, count):
        zero = jnp.zeros((1, width), F32)

        def step(index, carry):
            here = pl.ds(pl.multiple_of(index * 32, 32), 32)
            return tuple(a + b for a, b in zip(carry, body(here)))

        return lax.fori_loop(0, rows // 32, step, (zero,) * count)

    def lean(back, unit, inverse, gain):
        scaled = back * gain
        inner = (
            scaled
            - jnp.mean(scaled, axis=-1, keepdims=True)
            - unit * jnp.mean(scaled * unit, axis=-1, keepdims=True)
        )
        return inverse * inner, jnp.sum(back * unit, axis=0, keepdims=True)

    def feed_end(turn):
        layer = 1 - turn
        gain = gains[3 + layer : 4 + layer, :]
        part_over(turn).wait_recv()
        row_copy(2 * turn).wait()

        def body(here):
            unit, inverse = unit_rows(ub[here, :].astype(F32))
            back = rows_sum[here, :] + part_in[turn, here, :].astype(F32)
            dx, gain_part = lean(back, unit, inverse, gain)
            old = grad[here, :].astype(F32)
            grad[here, :] = (old + dx).astype(BF)
            return gain_part, jnp.sum(old, axis=0, keepdims=True)

        gain_grad, out_grad = row_steps(body, 2)
        row_copy(2 * turn + 1).start(priority=LOCAL)
        small_row(3 + layer, gain_grad)
        small_row(5 + layer, out_grad)
        grad_saved(turn).start(priority=LOCAL)
        slot = opened(8 * turn + 4)

        def tile(there, _):
            dob[:, there] = mm_cols(grad[...], slots[slot, there, :]).astype(BF)

        tiles(2, tile, 512)
        closed(8 * turn + 4)
        grad_saved(turn).wait()
        kin_right(False, 4 * turn, 0).start()

    def attend_heads(turn):
        scale = 1.0 / math.sqrt(HD)
        for copy in act_copies(turn):
            copy.wait()
        if turn == 1:
            for which in range(3):
                kin_right(False, 1 + which, 0).wait_send()

        def head(index, carry):
            here = pl.ds(pl.multiple_of(index * HD, HD), HD)
            q, k, v, do = qb[:, here], kb[:, here], vb[:, here], dob[:, here]
            scores = mm_cols(q, k) * scale
            if turn == 1:
                scores = jnp.where(mask_in[...] > 0.0, scores, MASKED)
            grown = jnp.exp(scores - jnp.max(scores, axis=-1, keepdims=True))
            soft = grown / jnp.sum(grown, axis=-1, keepdims=True)
            back = mm_cols(do, v)
            short = soft * (back - jnp.sum(soft * back, axis=-1, keepdims=True))
            dqkv[0, :, here] = (mm(short.astype(BF), k) * scale).astype(BF)
            dqkv[1, :, here] = (mm(short.T.astype(BF), q) * scale).astype(BF)
            dqkv[2, :, here] = mm(soft.T.astype(BF), do).astype(BF)
            return carry

        lax.fori_loop(0, width // HD, head, 0)
        if turn == 0:
            for copy in act_copies(1):
                copy.start(priority=LOCAL)
        for which in range(3):
            kin_right(False, 4 * turn + 1 + which, 0).start()

    def attend_end(turn):
        base = 8 * turn + 5
        for which in range(3):
            slot = opened(base + which)

            def tile(there, _):
                value = mm_cols(dqkv[which], slots[slot, there, :])
                if which == 0:
                    rows_sum[0:rows, there] = value
                elif which == 1:
                    rows_sum[rows : 2 * rows, there] = value
                else:
                    rows_sum[rows : 2 * rows, there] += value

            tiles(2, tile, 512)
            closed(base + which)
        row_copy(2 * turn + 1).wait()
        gain_q = gains[2:3, :] if turn == 0 else gains[0:1, :]
        gain_kv = gains[2:3, :] if turn == 0 else gains[1:2, :]

        def body(here):
            unit, inverse = unit_rows(ub[here, :].astype(F32))
            dx, gain_part = lean(rows_sum[here, :], unit, inverse, gain_q)
            if turn == 1:
                unit, inverse = unit_rows(src_in[here, :].astype(F32))
            there = pl.ds(pl.multiple_of(rows + here.start, 32), 32)
            ds, kv_part = lean(rows_sum[there, :], unit, inverse, gain_kv)
            fresh = grad[here, :].astype(F32) + dx
            if turn == 0:
                fresh += ds
            else:
                high = ds.astype(BF)
                part_out[0, here, :] = high
                part_out[1, here, :] = (ds - high.astype(F32)).astype(BF)
            grad[here, :] = fresh.astype(BF)
            return gain_part, kv_part

        if turn == 1:
            for which in range(2):
                part_over(which).wait_send()
            for copy in kin_lefts(True, 2):
                copy.wait_send()
        gain_grad, kv_grad = row_steps(body, 2)
        if turn == 0:
            row_copy(2).start(priority=LOCAL)
            small_row(2, gain_grad + kv_grad)
            open_pair(1)
        else:
            small_row(0, gain_grad)
            small_row(1, kv_grad)
            small_row(15, jnp.zeros_like(gain_grad))

            def tile(there, _):
                pair[:, there] = (
                    mm(picks_in[...], part_out[0, :, there])
                    + mm(picks_in[...], part_out[1, :, there])
                ).astype(BF)

            tiles(4, tile)
            small_copy(0).start()
            for which in range(3):
                point_copy(which).start()
            lat_start(1)

    def point_total():
        for which in range(3):
            point_copy(which).wait_recv()
        gathered = pair[
            pl.ds(pl.multiple_of(section_at * quarter_rows, 128), quarter_rows)
        ].astype(F32)
        for which in range(3):
            gathered += point_in[which].astype(F32)
        point_sum[...] = gathered.astype(BF)
        point_local().start(priority=LOCAL)
        for which in range(3):
            point_deal(which).start()

    def small_step(phase):
        small_copy(phase).wait_recv()
        small_sum[phase + 1] = small_sum[phase] + small_in[phase]
        if phase < 2:
            small_copy(phase + 1).start()
        else:
            for step in range(3):
                small_copy(3 + step).start()

    def small_end():
        for step in range(3):
            small_copy(3 + step).wait_recv()
        small_out[...] = (small_sum[3] + small_in[4]) + (small_in[3] + small_in[5])

    def rows_end():
        lat_onward(1)
        point_total()

    begin = pltpu.make_async_copy(top_in, grad, act_sems.at[4])
    begin.start()
    for index in range(2):
        slot_copy(index).start(priority=LOCAL)
    h_copy(0).start(priority=LOCAL)
    row_copy(0).start(priority=LOCAL)
    for copy in act_copies(0):
        copy.start(priority=LOCAL)
    begin.wait()
    open_pair(0)
    for part in range(2):
        kin_right(True, 0, part).start()
    pair_ready(0)
    for copy in kin_lefts(True, 1):
        copy.start()
    for job in range(4):
        for copy in kin_lefts(False, job):
            copy.start()
    for part in range(2):
        kin_right(True, 2, part).start()
    for copy in kin_lefts(True, 3):
        copy.start()
    for job in range(4, 8):
        for copy in kin_lefts(False, job):
            copy.start()
    raw_start(0)
    load(0)
    chain = {
        0: [functools.partial(feed_chunk, 0, 0), functools.partial(lat_start, 0)],
        1: [functools.partial(feed_chunk, 0, 1)],
        2: [functools.partial(feed_end, 0), functools.partial(lat_onward, 0)],
        3: [functools.partial(attend_heads, 0)],
        4: [functools.partial(attend_end, 0)],
        5: [functools.partial(pair_ready, 1), functools.partial(feed_chunk, 1, 0)],
        6: [functools.partial(feed_chunk, 1, 1)],
        7: [functools.partial(feed_end, 1)],
        8: [functools.partial(attend_heads, 1)],
        9: [functools.partial(attend_end, 1)],
        11: [functools.partial(small_step, 0), rows_end],
        13: [functools.partial(small_step, 1)],
        15: [functools.partial(small_step, 2)],
        17: [small_end],
    }

    def moment_body(moment, carry):
        @pl.when(moment < total)
        def _():
            by_kind(moment, functools.partial(offer, lax.rem(moment, WINDOWS)))

        ready = jnp.logical_and(moment >= 2, moment < total + 2)

        @pl.when(jnp.logical_and(ready, jnp.logical_not(is_feed(moment - 2))))
        def _():
            take(lax.rem(moment - 2, WINDOWS), count_below(moment - 2, ATTENDS), False)

        for lag, action in ((3, second_of), (4, third_of), (5, close_of), (6, finish_of)):

            @pl.when(jnp.logical_and(moment >= lag, moment < total + lag))
            def _():
                by_kind(moment - lag, action)
        for when, actions in chain.items():

            @pl.when(moment == when)
            def _():
                for action in actions:
                    action()

        for item in range(1, total):
            pl.when(moment == item - 1)(functools.partial(load, item))
        return carry

    lax.fori_loop(0, total + 6, moment_body, 0)

    for index in range(4):
        if index % 2 == 1:
            for copy in kin_lefts(True, index):
                copy.wait_send()
        if index != 1:
            for chunk in range(2):
                kin_right(True, index, chunk).wait_send()
    for index in range(8):
        for copy in kin_lefts(False, index):
            copy.wait_send()
        if index not in (1, 2, 3):
            kin_right(False, index, 0).wait_send()
    for phase in range(6):
        small_copy(phase).wait_send()
    for which in range(2):
        lat_local(which).wait()
        for way in range(2):
            lat_copy(which, way).wait_send()
        lat_far(which).wait()
    point_local().wait()
    for which in range(3):
        point_copy(which).wait_send()
        point_deal(which).wait()

    def drain(order, carry):
        @pl.when(order >= 4)
        def _():
            drained(order, True)

        drained(order, False)
        return carry

    for order in (5, 6, 7):
        xy_sent(order)
    lax.fori_loop(0, 8, drain, 0)


def reduce_all(full, kept, latents, gains, mask, picks):
    total = ITEM_COUNT
    rows, width = kept[0].shape
    points = picks.shape[0]
    anywhere = pl.BlockSpec(memory_space=pl.ANY)
    vmem = pl.BlockSpec(memory_space=pltpu.VMEM)
    u1, u2, u3, u4, top = kept[:5]
    operands = [*full, u1, u2, u3, u4, top, *kept[5:16], *kept[17:], latents, kept[16]]
    operands += [gains, mask, picks]
    spaces = [anywhere] * (len(operands) - 4) + [vmem] * 4
    dma = pltpu.SemaphoreType.DMA
    flops = 2 * width * width * 24 * rows * 2
    return pl.pallas_call(
        reduce_kernel,
        out_shape=[
            jax.ShapeDtypeStruct((2, 128, 4 * width), BF),
            jax.ShapeDtypeStruct((2, 128, 4 * width), BF),
            jax.ShapeDtypeStruct((3, 128, width), BF),
            jax.ShapeDtypeStruct((3, 128, width), BF),
            jax.ShapeDtypeStruct((1, 128, width), BF),
            jax.ShapeDtypeStruct((1, 128, width), BF),
            jax.ShapeDtypeStruct((4 * rows, width), BF),
            jax.ShapeDtypeStruct((4 * rows, width), BF),
            jax.ShapeDtypeStruct((points, width), BF),
            jax.ShapeDtypeStruct((16, width), F32),
            jax.ShapeDtypeStruct((2, rows, width), BF),
            jax.ShapeDtypeStruct((4, 4, 2 * rows, 128), BF),
            jax.ShapeDtypeStruct((8, 4, rows, 128), BF),
            jax.ShapeDtypeStruct((4, 2 * rows, 2 * width), BF),
            jax.ShapeDtypeStruct((8, rows, width), BF),
        ],
        in_specs=spaces,
        out_specs=[anywhere] * 9 + [vmem] + [anywhere] * 5,
        scratch_shapes=[
            pltpu.VMEM((4, 4, 128, 1024), BF),
            pltpu.VMEM((8, 4, 128, 512), BF),
            pltpu.VMEM((4, 2, 512, 128), BF),
            pltpu.VMEM((WINDOWS, 1024, 1024), BF),
            pltpu.VMEM((STAGES, 4, 128, 512), BF),
            pltpu.VMEM((4, 4, 128, 1024), BF),
            pltpu.VMEM((8, 4, 128, 512), BF),
            pltpu.VMEM((6, 5, 128, 1024), BF),
            pltpu.VMEM((4, 5, 128, 512), BF),
            pltpu.VMEM((4, 128, 1024), BF),
            pltpu.VMEM((8, 128, 512), BF),
            pltpu.VMEM((4, 128, 1024), BF),
            pltpu.VMEM((8, 128, 512), BF),
            pltpu.VMEM((512, 1024), BF),
            pltpu.VMEM((512, 2048), BF),
            pltpu.VMEM((512, 1024), F32),
            pltpu.VMEM((512, 1024), F32),
            pltpu.VMEM((2, 1024, 1024), BF),
            pltpu.VMEM((256, 1024), BF),
            pltpu.VMEM((256, 1024), BF),
            pltpu.VMEM((256, 1024), BF),
            pltpu.VMEM((256, 1024), BF),
            pltpu.VMEM((3, 256, 1024), BF),
            pltpu.VMEM((2, 256, 1024), BF),
            pltpu.VMEM((2, 256, 1024), BF),
            pltpu.VMEM((256, 1024), BF),
            pltpu.VMEM((256, 1024), BF),
            pltpu.VMEM((3, points // 4, width), BF),
            pltpu.VMEM((points // 4, width), BF),
            pltpu.VMEM((6, 16, width), F32),
            pltpu.VMEM((4, 16, width), F32),
            dma((2, 12, 4)),
            dma((2, 16)),
            dma((4, 2)),
            dma((WINDOWS, 2)),
            dma((2, 8, 2)),
            dma((total, 4)),
            dma((total, 5)),
            dma((2, total, 2)),
            dma((2, total, 2)),
            dma((total, 2)),
            dma((2, 2, 2)),
            dma((2, 2, 2)),
            dma((2,)),
            dma((2, 3)),
            dma((2, 3)),
            dma((1,)),
            dma((2, 6)),
            dma((2, 2, 2)),
            dma((2,)),
            dma((1,)),
            dma((1,)),
            dma((5,)),
        ],
        compiler_params=pltpu.CompilerParams(
            collective_id=2, has_side_effects=True, vmem_limit_bytes=62 * 2**20
        ),
        cost_estimate=pl.CostEstimate(
            flops=flops, bytes_accessed=2**27, transcendentals=2**21
        ),
    )(*operands)[:10]


def plain_layers(full, spread, mine, source, valid, cot_own, picks, groups_all):
    proj_c, out_c, in_0, down_0, proj_s, out_s, in_1, down_1 = full
    width, hidden = in_0.shape

    def vector(first, count):
        return spread[:, first : first + count].reshape(-1)

    gains_cross = (vector(0, 1), vector(1, 1))
    gain_self = vector(2, 1)
    gains_mlp = (vector(3, 1), vector(4, 1))
    biases_out = (vector(5, 1), vector(6, 1))
    per_bias = hidden // width
    biases_in = (vector(7, per_bias), vector(7 + per_bias, per_bias))
    cot = cot_own.astype(F32)
    u1, kept_c = attend(mine, source, valid, gains_cross[0], gains_cross[1], proj_c, out_c)
    u2, kept_0 = feed(u1.astype(F32), gains_mlp[0], in_0, biases_in[0], down_0, biases_out[0])
    u2 = u2.astype(F32)
    u3, kept_s = attend(u2, u2, None, gain_self, gain_self, proj_s, out_s)
    u4, kept_1 = feed(u3.astype(F32), gains_mlp[1], in_1, biases_in[1], down_1, biases_out[1])
    final = u4.astype(F32)
    group_norm = jnp.sqrt(jnp.mean(final * final) + EPSILON)
    norm_mean = lax.psum(group_norm, ALL) / groups_all
    g4 = (cot + (norm_mean / group_norm) * final).astype(BF)

    dx, gain_1_grad, bias_1_grad, ob_1_grad, pairs_1 = feed_back(
        g4, kept_1, gains_mlp[1], in_1, down_1
    )
    g3 = (g4.astype(F32) + dx).astype(BF)
    dx, ds, gq, gkv, pairs_s = attend_back(g3, kept_s, gain_self, gain_self, proj_s, out_s)
    gain_s_grad = gq + gkv
    g2 = (g3.astype(F32) + dx + ds).astype(BF)
    dx, gain_0_grad, bias_0_grad, ob_0_grad, pairs_0 = feed_back(
        g2, kept_0, gains_mlp[0], in_0, down_0
    )
    g1 = (g2.astype(F32) + dx).astype(BF)
    dx, ds, cq_grad, ckv_grad, pairs_c = attend_back(
        g1, kept_c, gains_cross[0], gains_cross[1], proj_c, out_c
    )
    g0 = (g1.astype(F32) + dx).astype(BF)
    high = ds.astype(BF)
    low = (ds - high.astype(F32)).astype(BF)
    point_part = (mm_rows(picks, high) + mm_rows(picks, low)).astype(BF)
    small = jnp.concatenate(
        [
            cq_grad,
            ckv_grad,
            gain_s_grad,
            gain_0_grad,
            gain_1_grad,
            ob_0_grad,
            ob_1_grad,
            bias_0_grad,
            bias_1_grad,
            jnp.zeros_like(cq_grad),
        ]
    ).reshape(-1, width)
    pairs = pairs_1 + pairs_s + pairs_0 + pairs_c
    lefts, rights = [pair[0] for pair in pairs], [pair[1] for pair in pairs]
    def settled_grad(left, right):
        part = lax.psum_scatter(
            mm_rows(left, right).astype(BF), ALL, scatter_dimension=0, tiled=True
        )
        return lax.all_gather(part, "section", axis=0, tiled=True).astype(F32)

    done = [settled_grad(left, right) for left, right in pairs]
    mlp_in_grad = jnp.stack([done[6], done[0]])
    mlp_down_grad = jnp.stack([done[7], done[1]])
    proj_s_grad = jnp.concatenate(done[2:5], axis=1)
    proj_c_grad = jnp.concatenate(done[8:11], axis=1)
    out_s_grad, out_c_grad = done[5], done[11]
    points_sum = lax.psum(point_part, "section")
    latents_out = lax.all_gather(u4, "section", axis=0, tiled=True)
    g0_all = lax.all_gather(g0, "section", axis=0, tiled=True)
    small = lax.psum(small, ALL)
    return (
        norm_mean,
        latents_out,
        g0_all,
        points_sum,
        small,
        mlp_in_grad,
        mlp_down_grad,
        proj_c_grad,
        proj_s_grad,
        out_c_grad,
        out_s_grad,
    )


def per_device(
    latents,
    points,
    neighbours,
    lengths,
    cross_proj,
    cross_out,
    cross_gains,
    self_proj,
    self_out,
    self_gain,
    mlp_gain,
    mlp_in,
    mlp_in_bias,
    mlp_down,
    mlp_out_bias,
    cotangent,
):
    sections = lax.axis_size("section")
    section_at = lax.axis_index("section")
    width = latents.shape[1]
    hidden = mlp_in.shape[2]
    groups_dev = neighbours.shape[0]
    rows = latents.shape[0] // sections
    shard = cross_out.shape[0]
    piece = shard // sections
    groups_all = groups_dev * lax.axis_size("batch")

    def gathered(block):
        own = lax.dynamic_slice_in_dim(block, section_at * piece, piece, 0)
        return lax.all_gather(own, ALL, axis=0, tiled=True)

    projs = (cross_proj.reshape(shard, 3 * width), self_proj.reshape(shard, 3 * width))
    if lax.axis_size("batch") == 8:
        made = gather_forward(
            [projs[0], cross_out, mlp_in, mlp_down, projs[1], self_out],
            latents,
            cotangent,
            points,
            neighbours,
            lengths[:, None],
            [cross_gains, self_gain[None, :], mlp_gain, mlp_out_bias, mlp_in_bias],
        )
        full, gain_rows, norm_tile, mask, picks = made[:8], *made[8:12]
        norm_mean = norm_tile[0, 0]
        (
            mlp_in_grad,
            mlp_down_grad,
            proj_c_grad,
            proj_s_grad,
            out_c_grad,
            out_s_grad,
            latents_out,
            g0_all,
            points_sum,
            small,
        ) = reduce_all(full, made[12:], latents, gain_rows, mask, picks)
        mlp_in_grad = mlp_in_grad.astype(F32)
        mlp_down_grad = mlp_down_grad.astype(F32)
        proj_c_grad = jnp.swapaxes(proj_c_grad, 0, 1).astype(F32)
        proj_s_grad = jnp.swapaxes(proj_s_grad, 0, 1).astype(F32)
        out_c_grad, out_s_grad = out_c_grad[0].astype(F32), out_s_grad[0].astype(F32)
    else:
        vectors = jnp.concatenate(
            [
                cross_gains.reshape(-1),
                self_gain,
                mlp_gain.reshape(-1),
                mlp_out_bias.reshape(-1),
                mlp_in_bias.reshape(-1),
                jnp.zeros_like(self_gain),
            ]
        ).reshape(-1, shard)
        cot_own = lax.dynamic_slice_in_dim(cotangent, section_at * rows, rows, 0)
        mine = lax.dynamic_slice_in_dim(latents, section_at * rows, rows, 0).astype(F32)
        listed = lax.dynamic_index_in_dim(neighbours, section_at, 0, keepdims=False)
        length = lax.dynamic_index_in_dim(lengths, section_at, 0, keepdims=False)
        valid = jnp.arange(listed.shape[0], dtype=jnp.int32) < length
        picks = listed[:, None] == jnp.arange(points.shape[0], dtype=jnp.int32)[None, :]
        picks = picks.astype(BF)
        source = mm(picks, points)
        blocks = [projs[0], cross_out, mlp_in[0], mlp_down[0]]
        blocks += [projs[1], self_out, mlp_in[1], mlp_down[1]]
        full = [gathered(block) for block in blocks]
        spread = lax.all_gather(vectors, "batch", axis=0, tiled=False)
        (
            norm_mean,
            latents_out,
            g0_all,
            points_sum,
            small,
            mlp_in_grad,
            mlp_down_grad,
            proj_c_grad,
            proj_s_grad,
            out_c_grad,
            out_s_grad,
        ) = plain_layers(full, spread.astype(F32), mine, source, valid, cot_own, picks, groups_all)
    points_grad = points_sum.astype(F32)
    latents_grad = g0_all.astype(F32)
    per_bias = hidden // width
    batch_at = lax.axis_index("batch")

    def own(first, count):
        flat = small[first : first + count].reshape(-1)
        size = flat.shape[0] // lax.axis_size("batch")
        return lax.dynamic_slice_in_dim(flat, batch_at * size, size, 0)

    return (
        latents_out,
        latents_grad,
        points_grad,
        proj_c_grad.reshape(shard, 3, width),
        out_c_grad,
        jnp.stack([own(0, 1), own(1, 1)]),
        proj_s_grad.reshape(shard, 3, width),
        out_s_grad,
        own(2, 1),
        jnp.stack([own(3, 1), own(4, 1)]),
        mlp_in_grad,
        jnp.stack([own(7, per_bias), own(7 + per_bias, per_bias)]),
        mlp_down_grad,
        jnp.stack([own(5, 1), own(6, 1)]),
        norm_mean,
    )


def solution(mesh):
    rows = P("batch", None)
    cols = P(None, "batch")
    block = P("batch", None, None)
    pair = P(None, "batch", None)
    return jax.shard_map(
        per_device,
        mesh=mesh,
        in_specs=(
            rows,
            rows,
            rows,
            P("batch"),
            block,
            rows,
            cols,
            block,
            rows,
            P("batch"),
            cols,
            pair,
            cols,
            pair,
            cols,
            rows,
        ),
        out_specs=(
            rows,
            rows,
            rows,
            block,
            rows,
            cols,
            block,
            rows,
            P("batch"),
            cols,
            pair,
            cols,
            pair,
            cols,
            P(),
        ),
        check_vma=False,
    )
```

```python
import functools
import math

import jax
import jax.numpy as jnp
from jax import lax
from jax.experimental import pallas as pl
from jax.experimental.pallas import tpu as pltpu
from jax.sharding import PartitionSpec as P

HD = 128
EPSILON = 1e-05
MASKED = -1e30
BF = jnp.bfloat16
F32 = jnp.float32
ALL = ("batch", "section")
MESH = pl.DeviceIdType.MESH
GATHER_WIDTH = 1024
AHEAD = 6
LOCAL = 1
SLOTS = 3
GATHERED = tuple(
    (4 * layer + index, start)
    for layer in range(2)
    for index, start in (
        [(0, 0), (0, 1024), (0, 2048), (1, 0)]
        + [(2 + which, chunk) for chunk in range(0, 2048, 1024) for which in range(2)]
    )
)


def mm(a, b):
    return jnp.dot(a, b, preferred_element_type=F32)


def mm_rows(a, b):
    return lax.dot_general(a, b, (((0,), (0,)), ((), ())), preferred_element_type=F32)


def mm_cols(a, b):
    return lax.dot_general(a, b, (((1,), (1,)), ((), ())), preferred_element_type=F32)


def unit_rows(values):
    centred = values - jnp.mean(values, axis=-1, keepdims=True)
    inverse = lax.rsqrt(jnp.mean(centred * centred, axis=-1, keepdims=True) + EPSILON)
    return centred * inverse, inverse


def norm_back(gradient, unit, inverse, gain):
    scaled = gradient * gain
    inner = (
        scaled
        - jnp.mean(scaled, axis=-1, keepdims=True)
        - unit * jnp.mean(scaled * unit, axis=-1, keepdims=True)
    )
    return inverse * inner, jnp.sum(gradient * unit, axis=0)


def heads_of(rows):
    return rows.reshape(rows.shape[0], -1, HD)


def softmax(q, k, valid):
    scores = jnp.einsum(
        "lhc,nhc->hln", heads_of(q), heads_of(k), preferred_element_type=F32
    ) * (1.0 / math.sqrt(HD))
    if valid is not None:
        scores = jnp.where(valid[None, None, :], scores, MASKED)
    grown = jnp.exp(scores - jnp.max(scores, axis=-1, keepdims=True))
    return grown / jnp.sum(grown, axis=-1, keepdims=True)


def attend(inputs, source, valid, gain_q, gain_kv, proj, out):
    unit_x, inv_x = unit_rows(inputs)
    queries_in = (unit_x * gain_q).astype(BF)
    unit_s, inv_s = unit_rows(source)
    keys_in = (unit_s * gain_kv).astype(BF)
    width = inputs.shape[1]
    q = mm(queries_in, proj[:, :width]).astype(BF)
    kv = mm(keys_in, proj[:, width:]).astype(BF)
    k, v = kv[:, :width], kv[:, width:]
    soft = softmax(q, k, valid)
    mixture = jnp.einsum("hln,nhc->lhc", soft.astype(BF), heads_of(v), preferred_element_type=F32)
    mixture = mixture.reshape(inputs.shape).astype(BF)
    result = (inputs + mm(mixture, out)).astype(BF)
    return result, (unit_x, inv_x, queries_in, unit_s, inv_s, keys_in, q, k, v, soft, mixture)


def attend_back(gradient, kept, gain_q, gain_kv, proj, out):
    unit_x, inv_x, queries_in, unit_s, inv_s, keys_in, q, k, v, soft, mixture = kept
    width = gradient.shape[1]
    scale = 1.0 / math.sqrt(HD)
    grad_mix = mm_cols(gradient, out).astype(BF)
    grad_soft = jnp.einsum(
        "lhc,nhc->hln", heads_of(grad_mix), heads_of(v), preferred_element_type=F32
    )
    inner = jnp.sum(soft * grad_soft, axis=-1, keepdims=True)
    grad_scores = (soft * (grad_soft - inner)).astype(BF)
    dq = jnp.einsum("hln,nhc->lhc", grad_scores, heads_of(k), preferred_element_type=F32) * scale
    dk = jnp.einsum("hln,lhc->nhc", grad_scores, heads_of(q), preferred_element_type=F32) * scale
    dv = jnp.einsum(
        "hln,lhc->nhc", soft.astype(BF), heads_of(grad_mix), preferred_element_type=F32
    )
    dq = dq.reshape(gradient.shape).astype(BF)
    dk = dk.reshape(-1, width).astype(BF)
    dv = dv.reshape(-1, width).astype(BF)
    grad_x, gain_q_grad = norm_back(mm_cols(dq, proj[:, :width]), unit_x, inv_x, gain_q)
    back_s = mm_cols(dk, proj[:, width : 2 * width]) + mm_cols(dv, proj[:, 2 * width :])
    grad_s, gain_kv_grad = norm_back(back_s, unit_s, inv_s, gain_kv)
    pairs = ((queries_in, dq), (keys_in, dk), (keys_in, dv), (mixture, gradient))
    return grad_x, grad_s, gain_q_grad, gain_kv_grad, pairs


def feed(inputs, gain, w_in, b_in, w_down, b_out):
    unit, inverse = unit_rows(inputs)
    lowered = (unit * gain).astype(BF)
    pre_act = mm(lowered, w_in) + b_in
    active = jax.nn.gelu(pre_act).astype(BF)
    result = (inputs + mm_cols(active, w_down) + b_out).astype(BF)
    return result, (unit, inverse, lowered, pre_act, active)


def feed_back(gradient, kept, gain, w_in, w_down):
    unit, inverse, lowered, pre_act, active = kept
    grad_act = mm(gradient, w_down)
    grad_pre = jax.vjp(jax.nn.gelu, pre_act)[1](grad_act)[0].astype(BF)
    grad_x, gain_grad = norm_back(mm_cols(grad_pre, w_in), unit, inverse, gain)
    bias_grad = jnp.sum(grad_pre.astype(F32), axis=0)
    out_grad = jnp.sum(gradient.astype(F32), axis=0)
    return grad_x, gain_grad, bias_grad, out_grad, ((lowered, grad_pre), (gradient, active))


def gelu_both(value):
    factor = math.sqrt(2.0 / math.pi)
    square = value * value
    bent = jnp.tanh(factor * value * (1.0 + 0.044715 * square))
    inner = factor * (1.0 + 3.0 * 0.044715 * square)
    half = 0.5 * (1.0 + bent)
    return value * half, half + 0.5 * value * (1.0 - bent * bent) * inner


def tiles(count, body, size=256):
    def step(index, carry):
        body(pl.ds(pl.multiple_of(index * size, size), size), index)
        return carry

    lax.fori_loop(0, count, step, 0)


def norm_into(source, gain, target):
    def step(index, carry):
        here = pl.ds(pl.multiple_of(index * 32, 32), 32)
        unit, _ = unit_rows(source[here, :].astype(F32))
        target[here, :] = (unit * gain).astype(BF)
        return carry

    lax.fori_loop(0, source.shape[0] // 32, step, 0)


def gather_kernel(*refs):
    cross_proj, cross_out, mlp_in, mlp_down, self_proj, self_out = refs[:6]
    latents_in, cot_all, points_in, near_in, length_in = refs[6:11]
    vec_parts = refs[11:16]
    section_at = lax.axis_index("section")
    batch_at = lax.axis_index("batch")
    x_at = lax.rem(section_at, 2)
    y_at = section_at // 2
    ins = (
        cross_proj,
        cross_out,
        mlp_in.at[0],
        mlp_down.at[0],
        self_proj,
        self_out,
        mlp_in.at[1],
        mlp_down.at[1],
    )
    count = len(ins)
    outs = refs[16 : 16 + count]
    rest = refs[16 + count :]
    gains, norm_out, mask_in, picks_out = rest[:4]
    kept_outs = rest[4:24]
    (
        u1,
        u2,
        u3,
        u4,
        grad_top,
        xq_c,
        sn_c,
        q_c,
        k_c,
        v_c,
        o_c,
        xn_s,
        q_s,
        k_s,
        v_s,
        o_s,
        src_in,
        lowered,
        before,
        active,
        x_in,
        cot_in,
        vec_in,
        vec_rows,
        slots,
        total_rows,
        part_out,
        part_in,
        vec_out,
        biases,
        plane,
        line_in,
    ) = rest[24:56]
    (own_sem, send, recv, kin_send, kin_recv, vec_sems) = rest[56:62]
    (slot_sems, kept_sems, plane_sems, line_sems, pair_sems, row_sems) = rest[62:]
    line = 4
    core = lax.rem(batch_at, 2)
    spot = batch_at // 2
    beside = section_at + 1 - 2 * x_at
    above = lax.rem(section_at + 2, 4)
    sibling = batch_at + 1 - 2 * core
    shard = ins[0].shape[0]
    place = section_at * 2 + core
    rows = x_in.shape[0]

    def down_line(step):
        return lax.rem(spot + step, line) * 2 + core

    def up_line(step):
        return lax.rem(spot + line - step, line) * 2 + core

    near_peers = []
    for turn in range(1, 8):
        other = lax.rem(place + turn, 8)
        near_peers.append((other // 2, spot * 2 + lax.rem(other, 2)))
    line_peers = [(section_at, down_line(step)) for step in range(1, line)]
    far_peers = [(section_at, down_line(step) + 1 - 2 * core) for step in range(1, line)]
    vec_peers = [(section_at, sibling)] + line_peers + far_peers
    peers = near_peers + line_peers + far_peers
    barrier = pltpu.get_barrier_semaphore()
    for peer in peers:
        pl.semaphore_signal(barrier, inc=1, device_id=peer, device_id_type=MESH)
    pl.semaphore_wait(barrier, len(peers))

    def spread(ref, owner, first, size):
        return ref.at[pl.ds(pl.multiple_of(owner * shard, shard), shard), pl.ds(first, size)]

    def is_feed(item):
        return item % 8 >= 4

    def source_of(item, first, size):
        index, start = GATHERED[item]
        if is_feed(item):
            first = pl.multiple_of(first + y_at * outs[index].shape[1], 128)
        return ins[index].at[:, pl.ds(first, size)]

    def piece(item):
        start = GATHERED[item][1]
        if is_feed(item):
            return pl.multiple_of(start + x_at * 512, 128), 512
        return pl.multiple_of(start + section_at * 256, 128), 256

    def own_line(item, way):
        first, size = piece(item)
        return pltpu.make_async_remote_copy(
            source_of(item, first, size),
            spread(outs[GATHERED[item][0]], batch_at, first, size),
            send.at[5 * way, item, 0],
            recv.at[0, item, 3 if way else 1],
            device_id=(section_at, batch_at + (-2 if way else 2)),
            device_id_type=MESH,
        )

    def onward_line(item, step, way):
        first, size = piece(item)
        ref = spread(outs[GATHERED[item][0]], up_line(step), first, size)
        return pltpu.make_async_remote_copy(
            ref,
            ref,
            send.at[0, item, step],
            recv.at[0, item, step - 1 if way else step + 1],
            device_id=(section_at, batch_at + (-2 if way else 2)),
            device_id_type=MESH,
        )

    def came_line(item, step):
        first, size = piece(item)
        ref = spread(outs[GATHERED[item][0]], up_line(step), first, size)
        return pltpu.make_async_remote_copy(
            ref,
            ref,
            send.at[0, item, step],
            recv.at[0, item, step],
            device_id=(section_at, sibling),
            device_id_type=MESH,
        )

    def start_line(item):
        @pl.when(spot < 3)
        def _():
            own_line(item, 0).start()

        @pl.when(spot > 0)
        def _():
            own_line(item, 1).start()

    def arrive_line(item, apart):
        @pl.when(spot >= apart)
        def _():
            came_line(item, apart).wait_recv()

            @pl.when(spot < 3)
            def _():
                onward_line(item, apart, 0).start()

            for copy in near(item, apart):
                copy.start()

        @pl.when(spot + apart <= 3)
        def _():
            came_line(item, 4 - apart).wait_recv()

            @pl.when(spot > 0)
            def _():
                onward_line(item, 4 - apart, 1).start()

            for copy in near(item, 4 - apart):
                copy.start()

    def sent_line(item):
        @pl.when(spot < 3)
        def _():
            own_line(item, 0).wait_send()

        @pl.when(spot > 0)
        def _():
            own_line(item, 1).wait_send()

        for apart in (1, 2, 3):

            @pl.when(jnp.logical_and(spot >= apart, spot < 3))
            def _():
                onward_line(item, apart, 0).wait_send()

            @pl.when(jnp.logical_and(spot + apart <= 3, spot > 0))
            def _():
                onward_line(item, 4 - apart, 1).wait_send()

        for step in (1, 2, 3):
            for copy in near(item, step):
                copy.wait_send()

    def plane_copy(item, step, way, low, wide, peer):
        ref = spread(outs[GATHERED[item][0]], up_line(step), low, wide)
        return pltpu.make_async_remote_copy(
            ref,
            ref,
            send.at[way, item, step],
            recv.at[way, item, step],
            device_id=(peer, batch_at),
            device_id_type=MESH,
        )

    def near(item, step):
        first, size = piece(item)
        copies = [plane_copy(item, step, 1, first, size, beside)]
        if not is_feed(item):
            copies.append(plane_copy(item, step, 2, first, size, above))
        return copies

    def far(item, step):
        start = GATHERED[item][1]
        by_y = pl.multiple_of(start + beside * 256, 128)
        by_x = pl.multiple_of(start + above * 256 + 128, 128)
        return [
            plane_copy(item, step, 3, by_y, 128, above),
            plane_copy(item, step, 4, by_x, 128, beside),
        ]

    def kin(item, step):
        index, start = GATHERED[item]
        if step == 0:
            source = source_of(item, start, GATHER_WIDTH)
        else:
            source = spread(outs[index], up_line(step), start, GATHER_WIDTH)
        return pltpu.make_async_remote_copy(
            source,
            spread(outs[index], up_line(step), start, GATHER_WIDTH),
            kin_send.at[item, step],
            kin_recv.at[item, step],
            device_id=(section_at, sibling),
            device_id_type=MESH,
        )

    def own(item):
        index, start = GATHERED[item]
        return pltpu.make_async_copy(
            source_of(item, start, GATHER_WIDTH),
            spread(outs[index], batch_at, start, GATHER_WIDTH),
            own_sem.at[item],
        )

    def vec_copy(which):
        return pltpu.make_async_remote_copy(
            vec_in,
            vec_out.at[batch_at],
            vec_sems.at[0, which],
            vec_sems.at[1, which],
            device_id=vec_peers[which],
            device_id_type=MESH,
        )

    def slot_copy(item):
        index, start = GATHERED[item]
        return pltpu.make_async_copy(
            outs[index].at[:, pl.ds(start, GATHER_WIDTH)],
            slots.at[item % SLOTS],
            slot_sems.at[item % SLOTS],
        )

    def near_norm(turn):
        return pltpu.make_async_remote_copy(
            plane.at[8],
            plane.at[place],
            plane_sems.at[0, turn],
            plane_sems.at[1, turn],
            device_id=near_peers[turn],
            device_id_type=MESH,
        )

    def far_norm(step):
        return pltpu.make_async_remote_copy(
            line_in.at[4],
            line_in.at[spot],
            line_sems.at[0, step],
            line_sems.at[1, step],
            device_id=line_peers[step],
            device_id_type=MESH,
        )

    def rows_over(layer):
        return pltpu.make_async_remote_copy(
            lowered.at[layer, pl.ds(0, rows)],
            lowered.at[layer, pl.ds(rows, rows)],
            pair_sems.at[0, layer, 0],
            pair_sems.at[1, layer, 0],
            device_id=(above, batch_at),
            device_id_type=MESH,
        )

    def part_over(layer):
        return pltpu.make_async_remote_copy(
            part_out.at[layer],
            part_in.at[layer],
            pair_sems.at[0, layer, 1],
            pair_sems.at[1, layer, 1],
            device_id=(above, batch_at),
            device_id_type=MESH,
        )

    steps = range(1, line)
    total = len(GATHERED)
    started = []

    def launch(copies):
        for copy in copies:
            copy.start()
        started.extend(copies)

    kept = (
        (u1, u2, u3, u4, grad_top)
        + (xq_c, sn_c, q_c, k_c, v_c, o_c)
        + (xn_s, q_s, k_s, v_s, o_s)
        + (src_in, lowered, before, active)
    )
    names = {id(ref): place for place, ref in enumerate(kept)}

    def keep(*chosen):
        for ref in chosen:
            index = names[id(ref)]
            pltpu.make_async_copy(ref, kept_outs[index], kept_sems.at[index]).start(priority=LOCAL)

    def row(index):
        return gains[index : index + 1, :]

    def project(source, target, slot):
        def tile(columns, _):
            target[:, columns] = mm(source[...], slots[slot, :, columns]).astype(BF)

        tiles(2, tile, 512)

    def heads(q, k, v, o, masked):
        def head(index, carry):
            here = pl.ds(pl.multiple_of(index * HD, HD), HD)
            scores = mm_cols(q[:, here], k[:, here]) * (1.0 / math.sqrt(HD))
            if masked:
                scores = jnp.where(mask_in[...] > 0.0, scores, MASKED)
            grown = jnp.exp(scores - jnp.max(scores, axis=-1, keepdims=True))
            soft = grown / jnp.sum(grown, axis=-1, keepdims=True)
            o[:, here] = mm(soft.astype(BF), v[:, here]).astype(BF)
            return carry

        lax.fori_loop(0, q.shape[1] // HD, head, 0)

    def close_attention(inputs, o, target, slot):
        def tile(columns, _):
            target[:, columns] = (
                inputs[:, columns].astype(F32) + mm(o[...], slots[slot, :, columns])
            ).astype(BF)

        tiles(2, tile, 512)

    def feed_up(layer, chunk, slot):
        def tile(columns, index):
            first = chunk * GATHER_WIDTH + index * 512
            there = pl.ds(pl.multiple_of(first, 512), 512)
            lanes = pl.ds(pl.multiple_of(y_at * 2048 + first, 512), 512)
            value = mm(lowered[layer], slots[slot, :, columns]) + biases[layer : layer + 1, lanes]
            active_part, slope = gelu_both(value)
            before[layer, :, there] = slope
            active[layer, :, there] = active_part.astype(BF)

        tiles(2, tile, 512)

    def feed_down(layer, chunk, slot):
        chosen = pl.ds(chunk * GATHER_WIDTH, GATHER_WIDTH)

        def tile(columns, _):
            value = mm_cols(active[layer, :, chosen], slots[slot, columns, :])
            if chunk == 0:
                total_rows[:, columns] = value
            else:
                value = total_rows[:, columns] + value
                total_rows[:, columns] = value
                part_out[layer, :, columns] = value[rows:].astype(BF)

        tiles(2, tile, 512)

    def feed_close(layer):
        inputs, target = (u1, u3)[layer], (u2, u4)[layer]
        part_over(layer).wait_recv()

        def tile(columns, _):
            target[:, columns] = (
                inputs[:, columns].astype(F32)
                + (total_rows[0:rows, columns] + part_in[layer, :, columns].astype(F32))
                + gains[5 + layer : 6 + layer, columns]
            ).astype(BF)

        tiles(2, tile, 512)
        keep(target)

    def work(item):
        slot_copy(item).wait()
        slot = item % SLOTS
        layer, stage = item // 8, item % 8
        inputs = (x_in, u2)[layer]
        middle = (u1, u3)[layer]
        q, k, v, o = ((q_c, k_c, v_c, o_c), (q_s, k_s, v_s, o_s))[layer]
        if stage == 0:
            if layer == 0:
                norm_into(x_in, row(0), xq_c)
                norm_into(src_in, row(1), sn_c)
                keep(xq_c, sn_c)
            else:
                feed_close(0)
                norm_into(u2, row(2), xn_s)
                keep(xn_s)
            project((xq_c, xn_s)[layer], q, slot)
        elif stage == 1:
            project((sn_c, xn_s)[layer], k, slot)
        elif stage == 2:
            project((sn_c, xn_s)[layer], v, slot)
            heads(q, k, v, o, layer == 0)
            keep(q, k, v, o)
        elif stage == 3:
            close_attention(inputs, o, middle, slot)
            norm_into(middle, row(3 + layer), lowered.at[layer, pl.ds(0, rows)])
            launch([rows_over(layer)])
            keep(middle)
        elif stage % 2 == 0:
            if stage == 4:
                rows_over(layer).wait_recv()
            feed_up(layer, (stage - 4) // 2, slot)
        else:
            feed_down(layer, (stage - 4) // 2, slot)
            if stage == 7:
                launch([part_over(layer)])

    for item in range(AHEAD):
        start_line(item)
    here = pl.ds(pl.multiple_of(section_at * rows, rows), rows)
    row_copies = [
        pltpu.make_async_copy(latents_in.at[here], x_in, row_sems.at[0]),
        pltpu.make_async_copy(cot_all.at[here], cot_in, row_sems.at[1]),
    ]
    for copy in row_copies:
        copy.start()
    cross_gain, self_gain, feed_gain, out_bias, in_bias = vec_parts
    vec_rows[...] = jnp.zeros_like(vec_rows)
    vec_rows[0:2, :] = cross_gain[...].astype(F32)
    vec_rows[2:3, :] = self_gain[...].astype(F32)
    vec_rows[3:5, :] = feed_gain[...].astype(F32)
    vec_rows[5:7, :] = out_bias[...].astype(F32)
    bias_rows = in_bias[...].astype(F32)
    for layer in range(2):
        for part_at in range(4):
            index = 7 + 4 * layer + part_at
            vec_rows[index : index + 1, :] = bias_rows[
                layer : layer + 1, part_at * 128 : part_at * 128 + 128
            ]
    vec_in[...] = vec_rows[...].astype(BF)
    vec_out[batch_at] = vec_in[...]
    for which in range(7):
        vec_copy(which).start()
    lanes = lax.broadcasted_iota(jnp.int32, (1, rows), 1)
    length = length_in[pl.ds(section_at, 1), :]
    mask_in[...] = jnp.where(lanes < length, 1.0, 0.0)
    point_at = lax.broadcasted_iota(jnp.int32, (points_in.shape[0], rows), 0)
    wanted = near_in[pl.ds(section_at, 1), :]
    picks = jnp.where(point_at == wanted, 1.0, 0.0)
    picks_out[...] = picks.astype(BF)
    turned = picks.T.astype(BF)

    def source_tile(columns, _):
        src_in[:, columns] = mm(turned, points_in[:, columns]).astype(BF)

    tiles(2, source_tile, 512)
    keep(src_in)
    for copy in row_copies:
        copy.wait()
    for moment in range(-2, total + 4):
        if moment + 2 + AHEAD < total:
            start_line(moment + 2 + AHEAD)
        for apart in (1, 2, 3):
            if 0 <= moment + 3 - apart < total:
                arrive_line(moment + 3 - apart, apart)
        if 0 <= moment < total:
            own(moment).start(priority=LOCAL)
            launch([kin(moment, 0)])
        if 0 <= moment - 1 < total:
            for step in steps:
                if is_feed(moment - 1):
                    near(moment - 1, step)[0].wait_recv()
                    launch([kin(moment - 1, step)])
                else:
                    for copy, onward in zip(near(moment - 1, step), far(moment - 1, step)):
                        copy.wait_recv()
                        launch([onward])
        if 0 <= moment - 2 < total and not is_feed(moment - 2):
            for step in steps:
                for copy in far(moment - 2, step):
                    copy.wait_recv()
                launch([kin(moment - 2, step)])
        if moment == 2:
            for which in range(7):
                vec_copy(which).wait()
            for owner in range(8):
                values = vec_out[owner].astype(F32)
                gains[:, owner * 128 : owner * 128 + 128] = values
                for layer in range(2):
                    for part_at in range(4):
                        first = owner * 512 + part_at * 128
                        index = 7 + 4 * layer + part_at
                        biases[layer : layer + 1, first : first + 128] = values[index : index + 1]
        if 0 <= moment - 4 < total:
            work(moment - 4)
        if 0 <= moment - 3 < total:
            own(moment - 3).wait()
            for step in range(line):
                kin(moment - 3, step).wait_recv()
            slot_copy(moment - 3).start(priority=LOCAL)
    keep(lowered, before, active)
    feed_close(1)

    def square(index, carry):
        here = pl.ds(pl.multiple_of(index * 32, 32), 32)
        values = u4[here, :].astype(F32)
        return carry + jnp.sum(values * values, axis=0, keepdims=True)

    squares = lax.fori_loop(0, u4.shape[0] // 32, square, jnp.zeros((1, u4.shape[1]), F32))
    mean = jnp.sum(squares, axis=1, keepdims=True) / (u4.shape[0] * u4.shape[1])
    group_norm = jnp.sqrt(mean + EPSILON)
    plane[8] = jnp.broadcast_to(group_norm, plane.shape[1:])
    for turn in range(7):
        near_norm(turn).start()
    plane[place] = plane[8]
    for turn in range(7):
        near_norm(turn).wait()
    line_in[4] = jnp.sum(plane[0:8], axis=0)
    for step in range(3):
        far_norm(step).start()
    line_in[spot] = line_in[4]
    for step in range(3):
        far_norm(step).wait()
    norm_mean = jnp.sum(line_in[0:4], axis=0) / 32.0
    norm_out[...] = norm_mean
    ratio = norm_mean[0:1, 0:1] / group_norm

    def top(index, carry):
        here = pl.ds(pl.multiple_of(index * 32, 32), 32)
        grad_top[here, :] = (
            cot_in[here, :].astype(F32) + ratio * u4[here, :].astype(F32)
        ).astype(BF)
        return carry

    lax.fori_loop(0, u4.shape[0] // 32, top, 0)
    keep(grad_top)
    for index, ref in enumerate(kept):
        pltpu.make_async_copy(ref, kept_outs[index], kept_sems.at[index]).wait()
    for item in range(total):
        sent_line(item)
    for copy in started:
        copy.wait_send()


def gather_forward(blocks, latents, cotangent, points, near, lengths, vectors):
    width = latents.shape[1]
    rows = near.shape[1]
    half = blocks[2].shape[2] // 2
    widths = (3 * width, width, half, half) * 2
    total = len(GATHERED)
    anywhere = pl.BlockSpec(memory_space=pl.ANY)
    vmem = pl.BlockSpec(memory_space=pltpu.VMEM)
    plain = ((rows, width), BF)
    kept = [plain] * 17 + [
        ((2, 2 * rows, width), BF),
        ((2, 2 * rows, half), F32),
        ((2, 2 * rows, half), BF),
    ]
    dma = pltpu.SemaphoreType.DMA
    return pl.pallas_call(
        gather_kernel,
        out_shape=[jax.ShapeDtypeStruct((width, size), BF) for size in widths]
        + [
            jax.ShapeDtypeStruct((16, width), F32),
            jax.ShapeDtypeStruct((8, 128), F32),
            jax.ShapeDtypeStruct((1, rows), F32),
            jax.ShapeDtypeStruct((points.shape[0], rows), BF),
        ]
        + [jax.ShapeDtypeStruct(*one) for one in kept],
        in_specs=[anywhere] * (len(blocks) + 2) + [vmem] * 8,
        out_specs=[anywhere] * len(widths) + [vmem] * 4 + [anywhere] * len(kept),
        scratch_shapes=[pltpu.VMEM(*one) for one in kept]
        + [
            pltpu.VMEM((rows, width), BF),
            pltpu.VMEM((rows, width), BF),
            pltpu.VMEM((16, 128), BF),
            pltpu.VMEM((16, 128), F32),
            pltpu.VMEM((SLOTS, width, GATHER_WIDTH), BF),
            pltpu.VMEM((2 * rows, width), F32),
            pltpu.VMEM((2, rows, width), BF),
            pltpu.VMEM((2, rows, width), BF),
            pltpu.VMEM((8, 16, 128), BF),
            pltpu.VMEM((2, 2 * half), F32),
            pltpu.VMEM((9, 8, 128), F32),
            pltpu.VMEM((5, 8, 128), F32),
            dma((total,)),
            dma((6, total, 4)),
            dma((5, total, 4)),
            dma((total, 4)),
            dma((total, 4)),
            dma((2, 7)),
            dma((SLOTS,)),
            dma((len(kept),)),
            dma((2, 7)),
            dma((2, 3)),
            dma((2, 2, 2)),
            dma((2,)),
        ],
        compiler_params=pltpu.CompilerParams(
            collective_id=1, has_side_effects=True, vmem_limit_bytes=56 * 2**20
        ),
        cost_estimate=pl.CostEstimate(
            flops=2 * rows * width * sum(widths), bytes_accessed=2**27, transcendentals=2**21
        ),
    )(*blocks, latents, cotangent, points, near, lengths, *vectors)


ITEM_COUNT = 16
FEEDS = (0, 1, 2, 4, 6, 9, 10, 13)
ATTENDS = (3, 5, 7, 8, 11, 12, 14, 15)
WINDOWS = 4
STAGES = 3


def reduce_kernel(*refs):
    total = ITEM_COUNT
    (
        proj_c,
        out_c,
        in_0,
        down_0,
        proj_s,
        out_s,
        in_1,
        down_1,
        u1_in,
        u2_in,
        u3_in,
        last_ref,
        top_in,
        xq_c,
        sn_c,
        q_c,
        k_c,
        v_c,
        o_c,
        xn_s,
        q_s,
        k_s,
        v_s,
        o_s,
        lowered,
        before,
        active,
        latents_in,
        src_in,
        gains,
        mask_in,
        picks_in,
    ) = refs[:32]
    (up_out, down_out, proj_out_c, proj_out_s, end_out_c, end_out_s) = refs[32:38]
    (last_out, first_out, point_out, small_out) = refs[38:42]
    (grads_h, kin_lf, kin_la, kin_rf, kin_ra) = refs[42:47]
    (
        lwin_f,
        lwin_a,
        raw,
        rwin,
        stage,
        merged_f,
        merged_a,
        passing_f,
        passing_a,
        lined_f,
        lined_a,
        crossed_f,
        crossed_a,
        pair,
        slope,
        rows_sum,
        hbuf,
        slots,
        qb,
        kb,
        vb,
        dob,
        dqkv,
        part_out,
        part_in,
        grad,
        ub,
        point_in,
        point_sum,
        small_in,
        small_sum,
    ) = refs[47:78]
    (
        kin_l_sems,
        kin_r_sems,
        raw_sems,
        win_sems,
        xy_sems,
        line_send,
        line_recv,
        cross_sems,
        out_sems,
        own_sems,
        lat_sems,
        far_sems,
        lat_own,
        point_sems,
        deal_sems,
        point_own,
        small_sems,
        pair_sems,
        slot_sems,
        h_sem,
        save_sems,
        act_sems,
    ) = refs[78:]
    section_at = lax.axis_index("section")
    batch_at = lax.axis_index("batch")
    core = lax.rem(batch_at, 2)
    spot = batch_at // 2
    x_at = lax.rem(section_at, 2)
    y_at = section_at // 2
    beside = section_at + 1 - 2 * x_at
    above = lax.rem(section_at + 2, 4)
    across = lax.rem(beside + 2, 4)
    sibling = batch_at + 1 - 2 * core
    flat = (beside, above)
    bits = (x_at, y_at)
    rows, width = 256, 1024

    peers = [(beside, batch_at), (above, batch_at), (across, batch_at), (section_at, sibling)]
    peers += [(section_at, lax.rem(spot + step, 4) * 2 + core) for step in (1, 2, 3)]
    barrier = pltpu.get_barrier_semaphore()
    for peer in peers:
        pl.semaphore_signal(barrier, inc=1, device_id=peer, device_id_type=MESH)
    pl.semaphore_wait(barrier, len(peers))

    def remote(source, target, sems, where, peer):
        return pltpu.make_async_remote_copy(
            source,
            target,
            sems.at[(0, *where)],
            sems.at[(1, *where)],
            device_id=peer,
            device_id_type=MESH,
        )

    feed_left = (pair, lowered.at[1], pair, lowered.at[0])
    feed_right = (active.at[1], slope, active.at[0], slope)
    att_left = (o_s, xn_s, xn_s, xn_s, o_c, xq_c, sn_c, sn_c)
    att_right = tuple(
        ref
        for turn in range(2)
        for ref in (grads_h.at[turn], dqkv.at[0], dqkv.at[1], dqkv.at[2])
    )

    def columns(spot_of, parity):
        return pl.ds(pl.multiple_of((2 * spot_of + parity) * 128, 128), 128)

    def kin_lefts(feed, job):
        source, target = (feed_left, kin_lf) if feed else (att_left, kin_la)
        return [
            remote(
                source[job].at[:, columns(part, 1 - core)],
                target.at[job, part],
                kin_l_sems,
                (job if feed else 4 + job, part),
                (section_at, sibling),
            )
            for part in range(4)
        ]

    def kin_right(feed, job, chunk):
        if feed:
            here = pl.ds(chunk * 1024, 1024)
            source, target = feed_right[job].at[:, here], kin_rf.at[job, :, here]
        else:
            source, target = att_right[job], kin_ra.at[job]
        where = (2 * job + chunk if feed else 8 + job,)
        return remote(source, target, kin_r_sems, where, (section_at, sibling))

    def item_of(index):
        if index in FEEDS:
            order = FEEDS.index(index)
            return True, order // 2, order % 2
        return False, ATTENDS.index(index), 0

    def window_copies(index):
        feed, job, chunk = item_of(index)
        slot = index % WINDOWS
        size = 512 if feed else 256
        if feed:
            here = pl.ds(chunk * 1024, 1024)
            sources = (feed_right[job].at[:, here], kin_rf.at[job, :, here])
        else:
            sources = (att_right[job], kin_ra.at[job])
        return [
            pltpu.make_async_copy(
                sources[whose],
                rwin.at[slot, pl.ds(whose * size, size)],
                win_sems.at[slot, whose],
            )
            for whose in range(2)
        ]

    def raw_copies(index, part):
        feed, job, _ = item_of(index)
        size = 512 if feed else 256
        own_left = (feed_left if feed else att_left)[job]
        kin_left = (kin_lf if feed else kin_la).at[job]
        sources = (own_left.at[:, columns(part, core)], kin_left.at[part])
        return [
            pltpu.make_async_copy(
                source, raw.at[part, whose, pl.ds(0, size)], raw_sems.at[part, whose]
            )
            for whose, source in enumerate(sources)
        ]

    def raw_start(index):
        feed, job, chunk = item_of(index)
        if chunk == 0:
            for copy in kin_lefts(feed, job):
                copy.wait_recv()
            for part in range(4):
                for copy in raw_copies(index, part):
                    copy.start(priority=LOCAL)

    def load(index):
        feed, job, chunk = item_of(index)
        kin_right(feed, job, chunk).wait_recv()
        for copy in window_copies(index):
            copy.start(priority=LOCAL)
        if chunk == 0:
            if feed and job == 2:
                raw_start(index)
            size = 512 if feed else 256
            target = (lwin_f if feed else lwin_a).at[job]
            for part in range(4):
                for whose, copy in enumerate(raw_copies(index, part)):
                    copy.wait()
                    place = raw.at[part, whose, pl.ds(0, size)]
                    target[part, :, whose * size : whose * size + size] = place[...].T
        if index + 1 < total and item_of(index + 1)[:2] != (True, 2):
            raw_start(index + 1)

    def count_below(item, places):
        return sum((item > place).astype(jnp.int32) for place in places)

    def is_feed(item):
        return functools.reduce(jnp.logical_or, [item == place for place in FEEDS])

    def loaded(slot, feed):
        size = 512 if feed else 256
        for whose in range(2):
            source = kin_rf.at[0, :, pl.ds(0, 1024)] if feed else kin_ra.at[0]
            pltpu.make_async_copy(
                source, rwin.at[slot, pl.ds(whose * size, size)], win_sems.at[slot, whose]
            ).wait()

    def by_kind(item, action):
        @pl.when(is_feed(item))
        def _():
            action(count_below(item, FEEDS), True)

        @pl.when(jnp.logical_not(is_feed(item)))
        def _():
            action(count_below(item, ATTENDS), False)

    def mark(order, feed):
        return order if feed else 8 + order

    def merged_of(order, feed):
        return merged_f.at[lax.rem(order, 4)] if feed else merged_a.at[order]

    def passing_of(order, feed, slot):
        if feed:
            return passing_f.at[lax.rem(order, 6), slot]
        return passing_a.at[lax.rem(order, 4), slot]

    def lined_of(order, feed):
        return lined_f.at[lax.rem(order, 4)] if feed else lined_a.at[order]

    def crossed_of(order, feed):
        return crossed_f.at[lax.rem(order, 4)] if feed else crossed_a.at[order]

    def products(order, slot, choice, store):
        def quarter(index, carry):
            here = pl.ds(pl.multiple_of(index * 256, 256), 256)
            bit = choice[0] + index * (choice[1] - choice[0])
            first = pl.multiple_of(index * 512 + bit * 256, 256)
            left = lwin_a[order].reshape(512, 512)
            right = rwin[slot, 0:512, pl.ds(first, 256)]
            tile = jnp.dot(left, right, preferred_element_type=F32).reshape(4, 128, 256)
            store(pl.ds(0, 4), here, tile)
            return carry

        lax.fori_loop(0, 2, quarter, 0)

    def xy_copies(item):
        return [
            remote(
                stage.at[lax.rem(item, STAGES), :, :, pl.ds(side * 256, 256)],
                merged_a.at[item, :, :, pl.ds(side * 256, 256)],
                xy_sems,
                (item, side),
                (flat[side], batch_at),
            )
            for side in range(2)
        ]

    def xy_sent(item):
        for copy in xy_copies(item):
            copy.wait_send()

    def line_copy(item, feed, dest, place, rightward):
        step = 1 if rightward else -1
        slot = 4 if not rightward and place - 1 == dest else dest
        return pltpu.make_async_remote_copy(
            merged_of(item, feed).at[dest],
            passing_of(item, feed, slot),
            line_send.at[mark(item, feed), dest],
            line_recv.at[mark(item, feed), slot],
            device_id=(section_at, batch_at + 2 * step),
            device_id_type=MESH,
        )

    def line_wait(item, feed, slot):
        pltpu.make_async_remote_copy(
            merged_of(item, feed).at[0],
            passing_of(item, feed, slot),
            line_send.at[mark(item, feed), 0],
            line_recv.at[mark(item, feed), slot],
            device_id=(section_at, sibling),
            device_id_type=MESH,
        ).wait_recv()

    def line_sent(item, feed):
        for step in (1, 2, 3):
            dest = lax.rem(spot + step, 4)
            pltpu.make_async_remote_copy(
                merged_of(item, feed).at[dest],
                passing_of(item, feed, 0),
                line_send.at[mark(item, feed), dest],
                line_recv.at[mark(item, feed), 0],
                device_id=(section_at, sibling),
                device_id_type=MESH,
            ).wait_send()

    def outset(item, feed):
        @pl.when(spot == 0)
        def _():
            for dest in (3, 2, 1):
                line_copy(item, feed, dest, 0, True).start()

        @pl.when(spot == 3)
        def _():
            for dest in (0, 1, 2):
                line_copy(item, feed, dest, 3, False).start()

    def drained(item, feed):
        line_sent(item, feed)
        delivered(item, feed)

    def delivered(item, feed):
        if feed:
            feed_out(item, up_out).wait()
            feed_own(item, up_out).wait()
        else:
            for side in range(2):
                att_out(item, side, end_out_s, 0).wait()
                att_own(item, side, end_out_s, 0).wait()

    def offer(slot, item, feed):
        loaded(slot, feed)
        if feed:

            @pl.when(item >= 4)
            def _():
                line_sent(item - 4, True)

            target = merged_of(item, True)

            def tile(index, carry):
                here = pl.ds(pl.multiple_of(index * 256, 256), 256)
                left = lwin_f[item // 2].reshape(512, 1024)
                right = rwin[slot, :, here]
                value = jnp.dot(left, right, preferred_element_type=F32)
                target[:, :, here] = value.reshape(4, 128, 256).astype(BF)
                return carry

            lax.fori_loop(0, 4, tile, 0)
            outset(item, True)
        else:

            @pl.when(item >= STAGES)
            def _():
                xy_sent(item - STAGES)

            def store(blocks, here, tile):
                stage[lax.rem(item, STAGES), blocks, :, here] = tile.astype(BF)

            products(item, slot, (1 - x_at, 1 - y_at), store)
            for copy in xy_copies(item):
                copy.start()

    def take(slot, item, feed):
        for copy in xy_copies(item):
            copy.wait_recv()
        target = merged_a.at[item]

        def store(blocks, here, tile):
            target[blocks, :, here] = (tile + target[blocks, :, here].astype(F32)).astype(BF)

        products(item, slot, bits, store)
        outset(item, False)

    def relay(item, feed, dest, place, rightward):
        line_wait(item, feed, dest)
        target = merged_of(item, feed)
        arrived = passing_of(item, feed, dest)
        target[dest] = (target[dest].astype(F32) + arrived[...].astype(F32)).astype(BF)
        line_copy(item, feed, dest, place, rightward).start()

    def second_of(item, feed):
        @pl.when(spot == 1)
        def _():
            for dest in (3, 2):
                relay(item, feed, dest, 1, True)

        @pl.when(spot == 2)
        def _():
            for dest in (0, 1):
                relay(item, feed, dest, 2, False)

    def third_of(item, feed):
        @pl.when(spot == 1)
        def _():
            relay(item, feed, 0, 1, False)

        @pl.when(spot == 2)
        def _():
            relay(item, feed, 3, 2, True)

    def feed_cross(item):
        return remote(
            lined_of(item, True),
            crossed_of(item, True),
            cross_sems,
            (item, 0),
            (beside, batch_at),
        )

    def cross_copy(item, side):
        here = pl.ds(side * 256, 256)
        return remote(
            lined_of(item, False).at[:, here],
            crossed_of(item, False).at[:, here],
            cross_sems,
            (8 + item, side),
            (flat[1 - side], batch_at),
        )

    def feed_place(item, target):
        base = y_at * 2048 + lax.rem(item, 2) * 1024
        return target.at[1 - item // 4, :, pl.ds(pl.multiple_of(base, 1024), 1024)]

    def feed_out(item, target):
        return remote(
            lined_of(item, True),
            feed_place(item, target),
            out_sems,
            (item, 0),
            (above, batch_at),
        )

    def feed_own(item, target):
        return pltpu.make_async_copy(
            lined_of(item, True), feed_place(item, target), own_sems.at[item, 0]
        )

    def feed_write(item):
        @pl.when(lax.rem(item, 4) < 2)
        def _():
            feed_out(item, down_out).start()
            feed_own(item, down_out).start(priority=LOCAL)

        @pl.when(lax.rem(item, 4) >= 2)
        def _():
            feed_out(item, up_out).start()
            feed_own(item, up_out).start(priority=LOCAL)

    def att_place(item, side, target, inner):
        base = side * 512 + bits[side] * 256
        return target.at[inner, :, pl.ds(pl.multiple_of(base, 256), 256)]

    def att_out(item, side, target, inner):
        return remote(
            lined_of(item, False).at[:, pl.ds(side * 256, 256)],
            att_place(item, side, target, inner),
            out_sems,
            (8 + item, side),
            (flat[side], batch_at),
        )

    def att_own(item, side, target, inner):
        return pltpu.make_async_copy(
            lined_of(item, False).at[:, pl.ds(side * 256, 256)],
            att_place(item, side, target, inner),
            own_sems.at[8 + item, side],
        )

    def att_write(item):
        inner = lax.rem(item, 4) - 1
        for turn, proj, end in ((0, proj_out_s, end_out_s), (1, proj_out_c, end_out_c)):

            @pl.when(jnp.logical_and(item // 4 == turn, inner >= 0))
            def _():
                for side in range(2):
                    att_out(item, side, proj, inner).start()
                    att_own(item, side, proj, inner).start(priority=LOCAL)

            @pl.when(jnp.logical_and(item // 4 == turn, inner < 0))
            def _():
                for side in range(2):
                    att_out(item, side, end, 0).start()
                    att_own(item, side, end, 0).start(priority=LOCAL)

    def close_of(item, feed):
        if feed:

            @pl.when(item >= 4)
            def _():
                delivered(item - 4, True)

        for place in range(4):

            @pl.when(spot == place)
            def _():
                value = merged_of(item, feed)[place].astype(F32)
                if place > 0:
                    line_wait(item, feed, place)
                    value += passing_of(item, feed, place)[...].astype(F32)
                if place < 3:
                    line_wait(item, feed, 4)
                    value += passing_of(item, feed, 4)[...].astype(F32)
                lined_of(item, feed)[...] = value.astype(BF)

        if feed:
            feed_cross(item).start()
        else:
            for side in range(2):
                cross_copy(item, side).start()

    def finish_of(item, feed):
        if feed:
            feed_cross(item).wait()
        else:
            for side in range(2):
                cross_copy(item, side).wait()
        target = lined_of(item, feed)
        target[...] = (
            target[...].astype(F32) + crossed_of(item, feed)[...].astype(F32)
        ).astype(BF)
        if feed:
            feed_write(item)
        else:
            att_write(item)

    def small_copy(phase):
        if phase == 0:
            peer = (section_at, sibling)
        elif phase < 3:
            peer = (flat[phase - 1], batch_at)
        else:
            peer = (section_at, lax.rem(spot + phase - 2, 4) * 2 + core)
        return remote(
            small_sum.at[min(phase, 3)], small_in.at[phase], small_sems, (phase,), peer
        )

    quarter_rows = pair.shape[0] // 4

    def point_copy(which):
        peer = (beside, above, across)[which]
        return remote(
            pair.at[pl.ds(pl.multiple_of(peer * quarter_rows, 128), quarter_rows)],
            point_in.at[which],
            point_sems,
            (which,),
            (peer, batch_at),
        )

    def point_place():
        return point_out.at[pl.ds(pl.multiple_of(section_at * quarter_rows, 128), quarter_rows)]

    def point_deal(which):
        peer = (beside, above, across)[which]
        return remote(point_sum, point_place(), deal_sems, (which,), (peer, batch_at))

    def point_local():
        return pltpu.make_async_copy(point_sum, point_place(), point_own.at[0])

    pairs = ((last_ref, last_out), (grad, first_out))

    def lat_copy(which, way):
        source, target = pairs[which]
        return remote(
            source,
            target.at[pl.ds(pl.multiple_of(section_at * rows, rows), rows)],
            lat_sems,
            (which, way),
            (flat[way], batch_at),
        )

    def lat_far(which, way):
        target = pairs[which][1]
        low = flat[way] * rows + way * (rows // 2)
        part = target.at[pl.ds(pl.multiple_of(low, rows // 2), rows // 2)]
        return remote(part, part, far_sems, (which, way), (flat[1 - way], batch_at))

    def lat_local(which):
        source, target = pairs[which]
        return pltpu.make_async_copy(
            source,
            target.at[pl.ds(pl.multiple_of(section_at * rows, rows), rows)],
            lat_own.at[which],
        )

    def lat_start(which):
        lat_local(which).start(priority=LOCAL)
        for way in range(2):
            lat_copy(which, way).start()

    def lat_onward(which):
        for way in range(2):
            lat_copy(which, way).wait_recv()
            lat_far(which, way).start()

    loads = []
    for turn, (proj, out, up, down) in enumerate(
        ((proj_s, out_s, in_1, down_1), (proj_c, out_c, in_0, down_0))
    ):
        for chunk in range(2):
            loads += [down.at[:, pl.ds(chunk * 1024, 1024)], up.at[:, pl.ds(chunk * 1024, 1024)]]
        loads.append(out)
        loads += [proj.at[:, pl.ds(which * 1024, 1024)] for which in range(3)]

    def slot_copy(index):
        return pltpu.make_async_copy(loads[index], slots.at[index % 2], slot_sems.at[index % 2])

    def opened(index):
        slot_copy(index).wait()
        return index % 2

    def closed(index):
        if index + 2 < len(loads):
            slot_copy(index + 2).start(priority=LOCAL)

    def h_copy(index):
        layer, chunk = 1 - index // 2, index % 2
        return pltpu.make_async_copy(
            before.at[layer, :, pl.ds(chunk * 1024, 1024)], hbuf, h_sem.at[0]
        )

    def pair_over(turn):
        return remote(
            pair.at[pl.ds(0, rows)],
            pair.at[pl.ds(rows, rows)],
            pair_sems,
            (turn, 0),
            (above, batch_at),
        )

    def part_over(turn):
        return remote(
            part_out.at[turn], part_in.at[turn], pair_sems, (turn, 1), (above, batch_at)
        )

    def grad_saved(turn):
        return pltpu.make_async_copy(grad, grads_h.at[turn], save_sems.at[0])

    def act_copies(turn):
        chosen = ((q_s, k_s, v_s), (q_c, k_c, v_c))[turn]
        return [
            pltpu.make_async_copy(source, target, act_sems.at[index])
            for index, (source, target) in enumerate(zip(chosen, (qb, kb, vb)))
        ]

    def row_copy(index):
        if index == 3:
            source = latents_in.at[pl.ds(pl.multiple_of(section_at * rows, rows), rows)]
        else:
            source = (u3_in, u2_in, u1_in)[index]
        return pltpu.make_async_copy(source, ub, act_sems.at[3])

    def small_row(index, value):
        small_sum[0, index : index + 1, :] = value

    def open_pair(turn):
        pair[0:rows, :] = grad[...]
        pair_over(turn).start()

    def pair_ready(turn):
        pair_over(turn).wait()
        for copy in kin_lefts(True, 2 * turn):
            copy.start()

    def feed_chunk(turn, chunk):
        layer = 1 - turn
        base = 8 * turn + 2 * chunk
        h_copy(2 * turn + chunk).wait()
        if turn == 1:
            kin_right(True, 1, chunk).wait_send()
        slot = opened(base)

        def up_tile(here, index):
            there = pl.ds(pl.multiple_of(chunk * 1024 + index * 256, 256), 256)
            value = mm(pair[...], slots[slot, :, here]) * hbuf[:, here]
            short = value.astype(BF)
            slope[:, there] = short
            column = jnp.sum(short.astype(F32), axis=0, keepdims=True)
            for half in range(2):
                index_at = 7 + 4 * layer + 2 * half + chunk
                small_sum[0, index_at : index_at + 1, here] = jnp.where(
                    y_at == half, column, jnp.zeros_like(column)
                )

        tiles(4, up_tile)
        closed(base)
        if 2 * turn + chunk + 1 < 4:
            h_copy(2 * turn + chunk + 1).start(priority=LOCAL)
        kin_right(True, 2 * turn + 1, chunk).start()
        slot = opened(base + 1)

        def down_tile(there, _):
            value = mm_cols(slope[:, chunk * 1024 : chunk * 1024 + 1024], slots[slot, there, :])
            if chunk == 0:
                rows_sum[:, there] = value
            else:
                value = rows_sum[:, there] + value
                rows_sum[:, there] = value
                part_out[turn, :, there] = value[rows:].astype(BF)

        tiles(4, down_tile)
        closed(base + 1)
        if chunk == 1:
            if turn == 0:
                for copy in kin_lefts(True, 0):
                    copy.wait_send()
            part_over(turn).start()

    def row_steps(body, count):
        zero = jnp.zeros((1, width), F32)

        def step(index, carry):
            here = pl.ds(pl.multiple_of(index * 32, 32), 32)
            return tuple(a + b for a, b in zip(carry, body(here)))

        return lax.fori_loop(0, rows // 32, step, (zero,) * count)

    def lean(back, unit, inverse, gain):
        scaled = back * gain
        inner = (
            scaled
            - jnp.mean(scaled, axis=-1, keepdims=True)
            - unit * jnp.mean(scaled * unit, axis=-1, keepdims=True)
        )
        return inverse * inner, jnp.sum(back * unit, axis=0, keepdims=True)

    def feed_end(turn):
        layer = 1 - turn
        gain = gains[3 + layer : 4 + layer, :]
        part_over(turn).wait_recv()
        row_copy(2 * turn).wait()

        def body(here):
            unit, inverse = unit_rows(ub[here, :].astype(F32))
            back = rows_sum[here, :] + part_in[turn, here, :].astype(F32)
            dx, gain_part = lean(back, unit, inverse, gain)
            old = grad[here, :].astype(F32)
            grad[here, :] = (old + dx).astype(BF)
            return gain_part, jnp.sum(old, axis=0, keepdims=True)

        gain_grad, out_grad = row_steps(body, 2)
        row_copy(2 * turn + 1).start(priority=LOCAL)
        small_row(3 + layer, gain_grad)
        small_row(5 + layer, out_grad)
        grad_saved(turn).start(priority=LOCAL)
        slot = opened(8 * turn + 4)

        def tile(there, _):
            dob[:, there] = mm_cols(grad[...], slots[slot, there, :]).astype(BF)

        tiles(2, tile, 512)
        closed(8 * turn + 4)
        grad_saved(turn).wait()
        kin_right(False, 4 * turn, 0).start()

    def attend_heads(turn):
        scale = 1.0 / math.sqrt(HD)
        for copy in act_copies(turn):
            copy.wait()
        if turn == 1:
            for which in range(3):
                kin_right(False, 1 + which, 0).wait_send()

        def head(index, carry):
            here = pl.ds(pl.multiple_of(index * HD, HD), HD)
            q, k, v, do = qb[:, here], kb[:, here], vb[:, here], dob[:, here]
            scores = mm_cols(q, k) * scale
            if turn == 1:
                scores = jnp.where(mask_in[...] > 0.0, scores, MASKED)
            grown = jnp.exp(scores - jnp.max(scores, axis=-1, keepdims=True))
            soft = grown / jnp.sum(grown, axis=-1, keepdims=True)
            back = mm_cols(do, v)
            short = soft * (back - jnp.sum(soft * back, axis=-1, keepdims=True))
            dqkv[0, :, here] = (mm(short.astype(BF), k) * scale).astype(BF)
            dqkv[1, :, here] = (mm(short.T.astype(BF), q) * scale).astype(BF)
            dqkv[2, :, here] = mm(soft.T.astype(BF), do).astype(BF)
            return carry

        lax.fori_loop(0, width // HD, head, 0)
        if turn == 0:
            for copy in act_copies(1):
                copy.start(priority=LOCAL)
        for which in range(3):
            kin_right(False, 4 * turn + 1 + which, 0).start()

    def attend_end(turn):
        base = 8 * turn + 5
        for which in range(3):
            slot = opened(base + which)

            def tile(there, _):
                value = mm_cols(dqkv[which], slots[slot, there, :])
                if which == 0:
                    rows_sum[0:rows, there] = value
                elif which == 1:
                    rows_sum[rows : 2 * rows, there] = value
                else:
                    rows_sum[rows : 2 * rows, there] += value

            tiles(2, tile, 512)
            closed(base + which)
        row_copy(2 * turn + 1).wait()
        gain_q = gains[2:3, :] if turn == 0 else gains[0:1, :]
        gain_kv = gains[2:3, :] if turn == 0 else gains[1:2, :]

        def body(here):
            unit, inverse = unit_rows(ub[here, :].astype(F32))
            dx, gain_part = lean(rows_sum[here, :], unit, inverse, gain_q)
            if turn == 1:
                unit, inverse = unit_rows(src_in[here, :].astype(F32))
            there = pl.ds(pl.multiple_of(rows + here.start, 32), 32)
            ds, kv_part = lean(rows_sum[there, :], unit, inverse, gain_kv)
            fresh = grad[here, :].astype(F32) + dx
            if turn == 0:
                fresh += ds
            else:
                high = ds.astype(BF)
                part_out[0, here, :] = high
                part_out[1, here, :] = (ds - high.astype(F32)).astype(BF)
            grad[here, :] = fresh.astype(BF)
            return gain_part, kv_part

        if turn == 1:
            for which in range(2):
                part_over(which).wait_send()
            for copy in kin_lefts(True, 2):
                copy.wait_send()
        gain_grad, kv_grad = row_steps(body, 2)
        if turn == 0:
            row_copy(2).start(priority=LOCAL)
            small_row(2, gain_grad + kv_grad)
            open_pair(1)
        else:
            small_row(0, gain_grad)
            small_row(1, kv_grad)
            small_row(15, jnp.zeros_like(gain_grad))

            def tile(there, _):
                pair[:, there] = (
                    mm(picks_in[...], part_out[0, :, there])
                    + mm(picks_in[...], part_out[1, :, there])
                ).astype(BF)

            tiles(4, tile)
            small_copy(0).start()
            for which in range(3):
                point_copy(which).start()
            lat_start(1)

    def point_total():
        for which in range(3):
            point_copy(which).wait_recv()
        gathered = pair[
            pl.ds(pl.multiple_of(section_at * quarter_rows, 128), quarter_rows)
        ].astype(F32)
        for which in range(3):
            gathered += point_in[which].astype(F32)
        point_sum[...] = gathered.astype(BF)
        point_local().start(priority=LOCAL)
        for which in range(3):
            point_deal(which).start()

    def small_step(phase):
        small_copy(phase).wait_recv()
        small_sum[phase + 1] = small_sum[phase] + small_in[phase]
        if phase < 2:
            small_copy(phase + 1).start()
        else:
            for step in range(3):
                small_copy(3 + step).start()

    def small_end():
        for step in range(3):
            small_copy(3 + step).wait_recv()
        small_out[...] = (small_sum[3] + small_in[4]) + (small_in[3] + small_in[5])

    def rows_end():
        lat_onward(1)
        point_total()

    begin = pltpu.make_async_copy(top_in, grad, act_sems.at[4])
    begin.start()
    for index in range(2):
        slot_copy(index).start(priority=LOCAL)
    h_copy(0).start(priority=LOCAL)
    row_copy(0).start(priority=LOCAL)
    for copy in act_copies(0):
        copy.start(priority=LOCAL)
    begin.wait()
    open_pair(0)
    for part in range(2):
        kin_right(True, 0, part).start()
    pair_ready(0)
    for copy in kin_lefts(True, 1):
        copy.start()
    for job in range(4):
        for copy in kin_lefts(False, job):
            copy.start()
    for part in range(2):
        kin_right(True, 2, part).start()
    for copy in kin_lefts(True, 3):
        copy.start()
    for job in range(4, 8):
        for copy in kin_lefts(False, job):
            copy.start()
    raw_start(0)
    load(0)
    chain = {
        0: [functools.partial(feed_chunk, 0, 0)],
        1: [functools.partial(feed_chunk, 0, 1), functools.partial(lat_start, 0)],
        2: [functools.partial(feed_end, 0)],
        3: [functools.partial(attend_heads, 0), functools.partial(lat_onward, 0)],
        4: [functools.partial(attend_end, 0)],
        5: [functools.partial(pair_ready, 1), functools.partial(feed_chunk, 1, 0)],
        6: [functools.partial(feed_chunk, 1, 1)],
        7: [functools.partial(feed_end, 1)],
        8: [functools.partial(attend_heads, 1)],
        9: [functools.partial(attend_end, 1)],
        11: [functools.partial(small_step, 0), rows_end],
        13: [functools.partial(small_step, 1)],
        15: [functools.partial(small_step, 2)],
        17: [small_end],
    }

    def moment_body(moment, carry):
        @pl.when(moment < total)
        def _():
            by_kind(moment, functools.partial(offer, lax.rem(moment, WINDOWS)))

        ready = jnp.logical_and(moment >= 2, moment < total + 2)

        @pl.when(jnp.logical_and(ready, jnp.logical_not(is_feed(moment - 2))))
        def _():
            take(lax.rem(moment - 2, WINDOWS), count_below(moment - 2, ATTENDS), False)

        for lag, action in ((3, second_of), (4, third_of), (5, close_of), (6, finish_of)):

            @pl.when(jnp.logical_and(moment >= lag, moment < total + lag))
            def _():
                by_kind(moment - lag, action)
        for when, actions in chain.items():

            @pl.when(moment == when)
            def _():
                for action in actions:
                    action()

        for item in range(1, total):
            pl.when(moment == item - 1)(functools.partial(load, item))
        return carry

    lax.fori_loop(0, total + 6, moment_body, 0)

    for index in range(4):
        if index % 2 == 1:
            for copy in kin_lefts(True, index):
                copy.wait_send()
        if index != 1:
            for chunk in range(2):
                kin_right(True, index, chunk).wait_send()
    for index in range(8):
        for copy in kin_lefts(False, index):
            copy.wait_send()
        if index not in (1, 2, 3):
            kin_right(False, index, 0).wait_send()
    for phase in range(6):
        small_copy(phase).wait_send()
    for which in range(2):
        lat_local(which).wait()
        for way in range(2):
            lat_copy(which, way).wait_send()
            lat_far(which, way).wait()
    point_local().wait()
    for which in range(3):
        point_copy(which).wait_send()
        point_deal(which).wait()

    def drain(order, carry):
        @pl.when(order >= 4)
        def _():
            drained(order, True)

        drained(order, False)
        return carry

    for order in (5, 6, 7):
        xy_sent(order)
    lax.fori_loop(0, 8, drain, 0)


def reduce_all(full, kept, latents, gains, mask, picks):
    total = ITEM_COUNT
    rows, width = kept[0].shape
    points = picks.shape[0]
    anywhere = pl.BlockSpec(memory_space=pl.ANY)
    vmem = pl.BlockSpec(memory_space=pltpu.VMEM)
    u1, u2, u3, u4, top = kept[:5]
    operands = [*full, u1, u2, u3, u4, top, *kept[5:16], *kept[17:], latents, kept[16]]
    operands += [gains, mask, picks]
    spaces = [anywhere] * (len(operands) - 4) + [vmem] * 4
    dma = pltpu.SemaphoreType.DMA
    flops = 2 * width * width * 24 * rows * 2
    return pl.pallas_call(
        reduce_kernel,
        out_shape=[
            jax.ShapeDtypeStruct((2, 128, 4 * width), BF),
            jax.ShapeDtypeStruct((2, 128, 4 * width), BF),
            jax.ShapeDtypeStruct((3, 128, width), BF),
            jax.ShapeDtypeStruct((3, 128, width), BF),
            jax.ShapeDtypeStruct((1, 128, width), BF),
            jax.ShapeDtypeStruct((1, 128, width), BF),
            jax.ShapeDtypeStruct((4 * rows, width), BF),
            jax.ShapeDtypeStruct((4 * rows, width), BF),
            jax.ShapeDtypeStruct((points, width), BF),
            jax.ShapeDtypeStruct((16, width), F32),
            jax.ShapeDtypeStruct((2, rows, width), BF),
            jax.ShapeDtypeStruct((4, 4, 2 * rows, 128), BF),
            jax.ShapeDtypeStruct((8, 4, rows, 128), BF),
            jax.ShapeDtypeStruct((4, 2 * rows, 2 * width), BF),
            jax.ShapeDtypeStruct((8, rows, width), BF),
        ],
        in_specs=spaces,
        out_specs=[anywhere] * 9 + [vmem] + [anywhere] * 5,
        scratch_shapes=[
            pltpu.VMEM((4, 4, 128, 1024), BF),
            pltpu.VMEM((8, 4, 128, 512), BF),
            pltpu.VMEM((4, 2, 512, 128), BF),
            pltpu.VMEM((WINDOWS, 1024, 1024), BF),
            pltpu.VMEM((STAGES, 4, 128, 512), BF),
            pltpu.VMEM((4, 4, 128, 1024), BF),
            pltpu.VMEM((8, 4, 128, 512), BF),
            pltpu.VMEM((6, 5, 128, 1024), BF),
            pltpu.VMEM((4, 5, 128, 512), BF),
            pltpu.VMEM((4, 128, 1024), BF),
            pltpu.VMEM((8, 128, 512), BF),
            pltpu.VMEM((4, 128, 1024), BF),
            pltpu.VMEM((8, 128, 512), BF),
            pltpu.VMEM((512, 1024), BF),
            pltpu.VMEM((512, 2048), BF),
            pltpu.VMEM((512, 1024), F32),
            pltpu.VMEM((512, 1024), F32),
            pltpu.VMEM((2, 1024, 1024), BF),
            pltpu.VMEM((256, 1024), BF),
            pltpu.VMEM((256, 1024), BF),
            pltpu.VMEM((256, 1024), BF),
            pltpu.VMEM((256, 1024), BF),
            pltpu.VMEM((3, 256, 1024), BF),
            pltpu.VMEM((2, 256, 1024), BF),
            pltpu.VMEM((2, 256, 1024), BF),
            pltpu.VMEM((256, 1024), BF),
            pltpu.VMEM((256, 1024), BF),
            pltpu.VMEM((3, points // 4, width), BF),
            pltpu.VMEM((points // 4, width), BF),
            pltpu.VMEM((6, 16, width), F32),
            pltpu.VMEM((4, 16, width), F32),
            dma((2, 12, 4)),
            dma((2, 16)),
            dma((4, 2)),
            dma((WINDOWS, 2)),
            dma((2, 8, 2)),
            dma((total, 4)),
            dma((total, 5)),
            dma((2, total, 2)),
            dma((2, total, 2)),
            dma((total, 2)),
            dma((2, 2, 2)),
            dma((2, 2, 2)),
            dma((2,)),
            dma((2, 3)),
            dma((2, 3)),
            dma((1,)),
            dma((2, 6)),
            dma((2, 2, 2)),
            dma((2,)),
            dma((1,)),
            dma((1,)),
            dma((5,)),
        ],
        compiler_params=pltpu.CompilerParams(
            collective_id=2, has_side_effects=True, vmem_limit_bytes=62 * 2**20
        ),
        cost_estimate=pl.CostEstimate(
            flops=flops, bytes_accessed=2**27, transcendentals=2**21
        ),
    )(*operands)[:10]


def plain_layers(full, spread, mine, source, valid, cot_own, picks, groups_all):
    proj_c, out_c, in_0, down_0, proj_s, out_s, in_1, down_1 = full
    width, hidden = in_0.shape

    def vector(first, count):
        return spread[:, first : first + count].reshape(-1)

    gains_cross = (vector(0, 1), vector(1, 1))
    gain_self = vector(2, 1)
    gains_mlp = (vector(3, 1), vector(4, 1))
    biases_out = (vector(5, 1), vector(6, 1))
    per_bias = hidden // width
    biases_in = (vector(7, per_bias), vector(7 + per_bias, per_bias))
    cot = cot_own.astype(F32)
    u1, kept_c = attend(mine, source, valid, gains_cross[0], gains_cross[1], proj_c, out_c)
    u2, kept_0 = feed(u1.astype(F32), gains_mlp[0], in_0, biases_in[0], down_0, biases_out[0])
    u2 = u2.astype(F32)
    u3, kept_s = attend(u2, u2, None, gain_self, gain_self, proj_s, out_s)
    u4, kept_1 = feed(u3.astype(F32), gains_mlp[1], in_1, biases_in[1], down_1, biases_out[1])
    final = u4.astype(F32)
    group_norm = jnp.sqrt(jnp.mean(final * final) + EPSILON)
    norm_mean = lax.psum(group_norm, ALL) / groups_all
    g4 = (cot + (norm_mean / group_norm) * final).astype(BF)

    dx, gain_1_grad, bias_1_grad, ob_1_grad, pairs_1 = feed_back(
        g4, kept_1, gains_mlp[1], in_1, down_1
    )
    g3 = (g4.astype(F32) + dx).astype(BF)
    dx, ds, gq, gkv, pairs_s = attend_back(g3, kept_s, gain_self, gain_self, proj_s, out_s)
    gain_s_grad = gq + gkv
    g2 = (g3.astype(F32) + dx + ds).astype(BF)
    dx, gain_0_grad, bias_0_grad, ob_0_grad, pairs_0 = feed_back(
        g2, kept_0, gains_mlp[0], in_0, down_0
    )
    g1 = (g2.astype(F32) + dx).astype(BF)
    dx, ds, cq_grad, ckv_grad, pairs_c = attend_back(
        g1, kept_c, gains_cross[0], gains_cross[1], proj_c, out_c
    )
    g0 = (g1.astype(F32) + dx).astype(BF)
    high = ds.astype(BF)
    low = (ds - high.astype(F32)).astype(BF)
    point_part = (mm_rows(picks, high) + mm_rows(picks, low)).astype(BF)
    small = jnp.concatenate(
        [
            cq_grad,
            ckv_grad,
            gain_s_grad,
            gain_0_grad,
            gain_1_grad,
            ob_0_grad,
            ob_1_grad,
            bias_0_grad,
            bias_1_grad,
            jnp.zeros_like(cq_grad),
        ]
    ).reshape(-1, width)
    pairs = pairs_1 + pairs_s + pairs_0 + pairs_c
    lefts, rights = [pair[0] for pair in pairs], [pair[1] for pair in pairs]
    def settled_grad(left, right):
        part = lax.psum_scatter(
            mm_rows(left, right).astype(BF), ALL, scatter_dimension=0, tiled=True
        )
        return lax.all_gather(part, "section", axis=0, tiled=True).astype(F32)

    done = [settled_grad(left, right) for left, right in pairs]
    mlp_in_grad = jnp.stack([done[6], done[0]])
    mlp_down_grad = jnp.stack([done[7], done[1]])
    proj_s_grad = jnp.concatenate(done[2:5], axis=1)
    proj_c_grad = jnp.concatenate(done[8:11], axis=1)
    out_s_grad, out_c_grad = done[5], done[11]
    points_sum = lax.psum(point_part, "section")
    latents_out = lax.all_gather(u4, "section", axis=0, tiled=True)
    g0_all = lax.all_gather(g0, "section", axis=0, tiled=True)
    small = lax.psum(small, ALL)
    return (
        norm_mean,
        latents_out,
        g0_all,
        points_sum,
        small,
        mlp_in_grad,
        mlp_down_grad,
        proj_c_grad,
        proj_s_grad,
        out_c_grad,
        out_s_grad,
    )


def per_device(
    latents,
    points,
    neighbours,
    lengths,
    cross_proj,
    cross_out,
    cross_gains,
    self_proj,
    self_out,
    self_gain,
    mlp_gain,
    mlp_in,
    mlp_in_bias,
    mlp_down,
    mlp_out_bias,
    cotangent,
):
    sections = lax.axis_size("section")
    section_at = lax.axis_index("section")
    width = latents.shape[1]
    hidden = mlp_in.shape[2]
    groups_dev = neighbours.shape[0]
    rows = latents.shape[0] // sections
    shard = cross_out.shape[0]
    piece = shard // sections
    groups_all = groups_dev * lax.axis_size("batch")

    def gathered(block):
        own = lax.dynamic_slice_in_dim(block, section_at * piece, piece, 0)
        return lax.all_gather(own, ALL, axis=0, tiled=True)

    projs = (cross_proj.reshape(shard, 3 * width), self_proj.reshape(shard, 3 * width))
    if lax.axis_size("batch") == 8:
        made = gather_forward(
            [projs[0], cross_out, mlp_in, mlp_down, projs[1], self_out],
            latents,
            cotangent,
            points,
            neighbours,
            lengths[:, None],
            [cross_gains, self_gain[None, :], mlp_gain, mlp_out_bias, mlp_in_bias],
        )
        full, gain_rows, norm_tile, mask, picks = made[:8], *made[8:12]
        norm_mean = norm_tile[0, 0]
        (
            mlp_in_grad,
            mlp_down_grad,
            proj_c_grad,
            proj_s_grad,
            out_c_grad,
            out_s_grad,
            latents_out,
            g0_all,
            points_sum,
            small,
        ) = reduce_all(full, made[12:], latents, gain_rows, mask, picks)
        mlp_in_grad = mlp_in_grad.astype(F32)
        mlp_down_grad = mlp_down_grad.astype(F32)
        proj_c_grad = jnp.swapaxes(proj_c_grad, 0, 1).astype(F32)
        proj_s_grad = jnp.swapaxes(proj_s_grad, 0, 1).astype(F32)
        out_c_grad, out_s_grad = out_c_grad[0].astype(F32), out_s_grad[0].astype(F32)
    else:
        vectors = jnp.concatenate(
            [
                cross_gains.reshape(-1),
                self_gain,
                mlp_gain.reshape(-1),
                mlp_out_bias.reshape(-1),
                mlp_in_bias.reshape(-1),
                jnp.zeros_like(self_gain),
            ]
        ).reshape(-1, shard)
        cot_own = lax.dynamic_slice_in_dim(cotangent, section_at * rows, rows, 0)
        mine = lax.dynamic_slice_in_dim(latents, section_at * rows, rows, 0).astype(F32)
        listed = lax.dynamic_index_in_dim(neighbours, section_at, 0, keepdims=False)
        length = lax.dynamic_index_in_dim(lengths, section_at, 0, keepdims=False)
        valid = jnp.arange(listed.shape[0], dtype=jnp.int32) < length
        picks = listed[:, None] == jnp.arange(points.shape[0], dtype=jnp.int32)[None, :]
        picks = picks.astype(BF)
        source = mm(picks, points)
        blocks = [projs[0], cross_out, mlp_in[0], mlp_down[0]]
        blocks += [projs[1], self_out, mlp_in[1], mlp_down[1]]
        full = [gathered(block) for block in blocks]
        spread = lax.all_gather(vectors, "batch", axis=0, tiled=False)
        (
            norm_mean,
            latents_out,
            g0_all,
            points_sum,
            small,
            mlp_in_grad,
            mlp_down_grad,
            proj_c_grad,
            proj_s_grad,
            out_c_grad,
            out_s_grad,
        ) = plain_layers(full, spread.astype(F32), mine, source, valid, cot_own, picks, groups_all)
    points_grad = points_sum.astype(F32)
    latents_grad = g0_all.astype(F32)
    per_bias = hidden // width
    batch_at = lax.axis_index("batch")

    def own(first, count):
        flat = small[first : first + count].reshape(-1)
        size = flat.shape[0] // lax.axis_size("batch")
        return lax.dynamic_slice_in_dim(flat, batch_at * size, size, 0)

    return (
        latents_out,
        latents_grad,
        points_grad,
        proj_c_grad.reshape(shard, 3, width),
        out_c_grad,
        jnp.stack([own(0, 1), own(1, 1)]),
        proj_s_grad.reshape(shard, 3, width),
        out_s_grad,
        own(2, 1),
        jnp.stack([own(3, 1), own(4, 1)]),
        mlp_in_grad,
        jnp.stack([own(7, per_bias), own(7 + per_bias, per_bias)]),
        mlp_down_grad,
        jnp.stack([own(5, 1), own(6, 1)]),
        norm_mean,
    )


def solution(mesh):
    rows = P("batch", None)
    cols = P(None, "batch")
    block = P("batch", None, None)
    pair = P(None, "batch", None)
    return jax.shard_map(
        per_device,
        mesh=mesh,
        in_specs=(
            rows,
            rows,
            rows,
            P("batch"),
            block,
            rows,
            cols,
            block,
            rows,
            P("batch"),
            cols,
            pair,
            cols,
            pair,
            cols,
            rows,
        ),
        out_specs=(
            rows,
            rows,
            rows,
            block,
            rows,
            cols,
            block,
            rows,
            P("batch"),
            cols,
            pair,
            cols,
            pair,
            cols,
            P(),
        ),
        check_vma=False,
    )
```
